32 devices in a mesh: dp: 8 (over z, core), tensor: 4 (over y, x).
Axes of the slice: x: 2, y: 2, z: 4, core: 2. Of those that a mesh axis runs over, the one named last changes fastest.
Arguments:
- tokens: bfloat16 [16384, 2048], P(('dp', 'tensor')), may hold values from -6 to 6
- cotangent: bfloat16 [16384, 2048], P(('dp', 'tensor')), may hold values from -6 to 6
- segment: int32 [16384], P('dp'), may hold values from -1 to 2, as said below
- first_gain: float32 [2048], replicated, may hold values from 0.1 to 1.9
- first_bias: float32 [2048], replicated, may hold values from -2 to 2
- query_weight: bfloat16 [2048, 2048], P('dp', 'tensor'), may hold values from -0.125 to 0.125
- key_weight: bfloat16 [2048, 2048], P('dp', 'tensor'), may hold values from -0.125 to 0.125
- value_weight: bfloat16 [2048, 4096], P('dp', 'tensor'), may hold values from -0.125 to 0.125
- gate_weight: bfloat16 [2048, 4096], P('dp', 'tensor'), may hold values from -0.125 to 0.125
- out_weight: bfloat16 [4096, 2048], P('tensor', 'dp'), may hold values from -0.09375 to 0.09375
- second_gain: float32 [2048], replicated, may hold values from 0.1 to 1.9
- second_bias: float32 [2048], replicated, may hold values from -2 to 2
- up_weight: bfloat16 [2048, 4096], P('dp', 'tensor'), may hold values from -0.125 to 0.125
- down_weight: bfloat16 [4096, 2048], P('tensor', 'dp'), may hold values from -0.09375 to 0.09375
Outputs:
- block_output: bfloat16 [16384, 2048], P(('dp', 'tensor'))
- tokens_grad: bfloat16 [16384, 2048], P(('dp', 'tensor'))
- first_gain_grad: float32 [2048], P(('dp', 'tensor'))
- first_bias_grad: float32 [2048], P(('dp', 'tensor'))
- query_weight_grad: float32 [2048, 2048], P('dp', 'tensor')
- key_weight_grad: float32 [2048, 2048], P('dp', 'tensor')
- value_weight_grad: float32 [2048, 4096], P('dp', 'tensor')
- gate_weight_grad: float32 [2048, 4096], P('dp', 'tensor')
- out_weight_grad: float32 [4096, 2048], P('tensor', 'dp')
- second_gain_grad: float32 [2048], P(('dp', 'tensor'))
- second_bias_grad: float32 [2048], P(('dp', 'tensor'))
- up_weight_grad: float32 [2048, 4096], P('dp', 'tensor')
- down_weight_grad: float32 [4096, 2048], P('tensor', 'dp')
The draws below stay inside these ranges and needn't reach their ends.
Inputs may be any that keep to these rules, and one draw needn't show every extreme that they name: `segment`: in each aligned block of 2048 rows, sequence ids 0, 1 and 2 in this order, each on a run of 128 rows or more, then -1 (padding, one row or more) to the block's end; sequence 1 starts within the block's first 512 rows and ends within its last 512 rows.
All inputs are finite; a program needn't handle non-finite values.
Results may differ from the reference program's by a relative error of at most 0.02.
Values may be sent and summed in bfloat16 or wider, within the bound.
A program may use at most 320 MiB of HBM per device.

```python
import jax
import jax.numpy as jnp
from jax import lax

D = 2048
KEY = 256
VAL = 512
FF = 4096
BUF = 2048
MIN_LEN = 128
BLOCK = 512
QK = 2048
VD = 4096
TOKENS = 16384
N_DP = 8
N_TENSOR = 4


def draw_segment(key, part):
    key = jax.random.fold_in(key, 11)
    subkeys = jax.random.split(key, 3)
    per_device = BUF // N_TENSOR
    head_length = jax.random.randint(subkeys[0], (N_DP, 1), MIN_LEN, per_device)
    tail_length = jax.random.randint(subkeys[1], (N_DP, 1), MIN_LEN + 1, per_device + 1)
    padding = jax.random.randint(subkeys[2], (N_DP, 1), 1, tail_length - MIN_LEN + 1)
    row_index = jnp.arange(BUF, dtype=jnp.int32)[None, :]
    long_end = BUF - tail_length
    pad_start = BUF - padding
    labels = jnp.where(row_index < head_length, 0, jnp.where(row_index < long_end, 1, jnp.where(row_index < pad_start, 2, -1)))
    return labels.reshape(TOKENS).astype(jnp.int32)


def level_of(stream_key, dims, shards, low, high):
    def one(position, blocks):
        heights = jax.random.uniform(jax.random.fold_in(jax.random.fold_in(stream_key, 6), position), (blocks,), jnp.float32, low / len(shards), high / len(shards))
        return jnp.repeat(jnp.exp(heights), dims[position] // blocks).reshape((-1,) + (1,) * (len(dims) - position - 1))

    level = one(*shards[0])
    for cut in shards[1:]:
        level = level * one(*cut)
    return level


def noise(stream_key, extent, deviation, most, cuts=(), kind=jnp.bfloat16):
    drawn = jax.random.normal(stream_key, extent, jnp.float32) * deviation
    if len(cuts) > 0:
        drawn = level_of(stream_key, extent, cuts, -0.22, 0.18) * drawn
    return jnp.clip(drawn, min=-most, max=most).astype(kind)


def setup_inputs(seed: int = 0) -> dict:
    key_list = jax.random.split(jax.random.key(seed), 15)
    tokens = noise(key_list[0], (TOKENS, D), 1.0, 6.0, ((0, 32),))
    cotangent = noise(key_list[1], (TOKENS, D), 1.0, 6.0, ((0, 32),))
    segment = draw_segment(jax.random.fold_in(key_list[14], 71), 0)
    first_gain = jnp.clip(1.0 + 0.18 * jax.random.normal(key_list[3], (D,), jnp.float32), 0.1, 1.9)
    first_bias = noise(key_list[4], (D,), 0.3, 2.0, (), jnp.float32)
    query_weight = noise(key_list[5], (D, QK), D ** -0.5, 0.125, ((0, 8), (1, 4)))
    key_weight = noise(key_list[6], (D, QK), D ** -0.5, 0.125, ((0, 8), (1, 4)))
    value_weight = noise(key_list[7], (D, VD), D ** -0.5, 0.125, ((0, 8), (1, 4)))
    gate_weight = noise(key_list[8], (D, VD), D ** -0.5, 0.125, ((0, 8), (1, 4)))
    out_weight = noise(key_list[9], (VD, D), VD ** -0.5, 0.09375, ((0, 4), (1, 8)))
    second_gain = jnp.clip(1.0 + 0.18 * jax.random.normal(key_list[10], (D,), jnp.float32), 0.1, 1.9)
    second_bias = noise(key_list[11], (D,), 0.3, 2.0, (), jnp.float32)
    up_weight = noise(key_list[12], (D, FF), D ** -0.5, 0.125, ((0, 8), (1, 4)))
    down_weight = noise(key_list[13], (FF, D), FF ** -0.5, 0.09375, ((0, 4), (1, 8)))
    return {"tokens": tokens, "cotangent": cotangent, "segment": segment, "first_gain": first_gain, "first_bias": first_bias, "query_weight": query_weight, "key_weight": key_weight, "value_weight": value_weight, "gate_weight": gate_weight, "out_weight": out_weight, "second_gain": second_gain, "second_bias": second_bias, "up_weight": up_weight, "down_weight": down_weight}


highest_precision = lax.Precision.HIGHEST
norm_epsilon = 1e-05
group_floor = 0.5

@jax.custom_vjp
def low(v):
    return lax.optimization_barrier(v.astype(jnp.bfloat16)).astype(jnp.float32)

@jax.custom_vjp
def low_back(v):
    return v

def low_keep(v):
    return (low(v), None)

def low_pass(kept, grad):
    return (grad,)

def back_keep(v):
    return (v, None)

def back_low(kept, grad):
    return (low(grad),)
low.defvjp(low_keep, low_pass)
low_back.defvjp(back_keep, back_low)

def matmul(left, right):
    return jnp.dot(left, right, precision=highest_precision)

def layer_norm(values, norm_gain, norm_bias):
    average = lax.optimization_barrier(jnp.mean(values, axis=-1, keepdims=True))
    centred = values - average
    variance = lax.optimization_barrier(jnp.mean(centred * centred, axis=-1, keepdims=True))
    return centred * lax.rsqrt(variance + norm_epsilon) * norm_gain + norm_bias

def gelu_tanh(values):
    return jax.nn.gelu(values, approximate=True)

def positions_of(segments):
    length_all = segments.shape[0]
    row_index = jnp.arange(length_all, dtype=jnp.int32)
    boundary = jnp.concatenate([jnp.ones((1,), jnp.int32), (segments[1:] != segments[:-1]).astype(jnp.int32)])
    run_start = lax.cummax(jnp.where(boundary > 0, row_index, 0).astype(jnp.int32), axis=0)
    return row_index - run_start

def rotate(stacked, positions):
    half_width = stacked.shape[-1] // 2
    frequency = jnp.exp(-jnp.log(10000.0) * jnp.arange(half_width, dtype=jnp.float32) / half_width)
    angles = positions.astype(jnp.float32)[:, None] * frequency[None, :]
    cosine = jnp.cos(angles)[:, None, :]
    sine_part = jnp.sin(angles)[:, None, :]
    first_half = stacked[..., :half_width]
    second_half = stacked[..., half_width:]
    return jnp.concatenate([first_half * cosine - second_half * sine_part, second_half * cosine + first_half * sine_part], axis=-1)

def decay_mask(row_ids, segment_rows, segment_all, log_decay):
    col_ids = jnp.arange(segment_all.shape[0], dtype=jnp.int32)
    distance = row_ids[:, None] - col_ids[None, :]
    linked = (distance >= 0) & (segment_rows[:, None] == segment_all[None, :]) & (segment_rows[:, None] >= 0)
    exponent = jnp.where(linked, distance, 0).astype(jnp.float32)
    weight = jnp.exp(log_decay[:, None, None] * exponent[None])
    return jnp.where(linked[None], weight, 0.0)

def forward(tok_rows, segments, first_gain, first_bias, query_weight, key_weight, value_weight, gate_weight, out_weight, second_gain, second_bias, up_weight, down_weight):
    length_all = tok_rows.shape[0]
    head_count = query_weight.shape[1] // KEY
    normed1 = low(layer_norm(tok_rows, first_gain, first_bias))
    positions = positions_of(segments)
    query_field = low_back(matmul(normed1, query_weight)).reshape(length_all, head_count, KEY)
    key_field = low_back(matmul(normed1, key_weight)).reshape(length_all, head_count, KEY)
    value_field = low(low_back(matmul(normed1, value_weight))).reshape(length_all, head_count, VAL)
    gate_raw = low_back(matmul(normed1, gate_weight))
    query_field = low(rotate(query_field, positions))
    key_field = low(rotate(key_field, positions) * KEY ** (-0.5))
    log_decay = jnp.log1p(-jnp.exp2(-5.0 - jnp.arange(head_count, dtype=jnp.float32)))

    def one_block(offset):
        row_ids = offset + jnp.arange(BLOCK, dtype=jnp.int32)
        query_block = lax.dynamic_slice_in_dim(query_field, offset, BLOCK, 0)
        segment_block = lax.dynamic_slice_in_dim(segments, offset, BLOCK, 0)
        scores = jnp.einsum('qhk,nhk->hqn', query_block, key_field, precision=highest_precision)
        weights = low(decay_mask(row_ids, segment_block, segments, log_decay) * low_back(scores))
        return low_back(jnp.einsum('hqn,nhv->qhv', weights, value_field, precision=highest_precision))
    starts = jnp.arange(length_all // BLOCK, dtype=jnp.int32) * BLOCK
    retained = lax.map(jax.checkpoint(one_block), starts).reshape(length_all, head_count, VAL)
    centred = retained - lax.optimization_barrier(jnp.mean(retained, axis=-1, keepdims=True))
    grouped = centred * lax.rsqrt(lax.optimization_barrier(jnp.mean(centred * centred, axis=-1, keepdims=True)) + group_floor)
    gated = low(jax.nn.silu(gate_raw) * grouped.reshape(length_all, head_count * VAL))
    mixed = tok_rows + low_back(matmul(gated, out_weight))
    normed2 = low(layer_norm(mixed, second_gain, second_bias))
    hidden = low(gelu_tanh(low_back(matmul(normed2, up_weight))))
    return mixed + matmul(hidden, down_weight)

def reference(tokens, cotangent, segment, first_gain, first_bias, query_weight, key_weight, value_weight, gate_weight, out_weight, second_gain, second_bias, up_weight, down_weight):
    float_params = tuple((weight_item.astype(jnp.float32) for weight_item in (first_gain, first_bias, query_weight, key_weight, value_weight, gate_weight, out_weight, second_gain, second_bias, up_weight, down_weight)))
    all_rows = tokens.astype(jnp.float32).reshape(N_DP, BUF, D)
    all_cot = cotangent.astype(jnp.float32).reshape(N_DP, BUF, D)
    all_segments = segment.reshape(N_DP, BUF)

    def buffer_step(totals, buffer_item):
        buffer_rows, buffer_cot, buffer_seg = buffer_item

        def layer_fn(rows_in, *weights_in):
            return forward(rows_in, buffer_seg, *weights_in)
        buffer_out, pullback = jax.vjp(layer_fn, buffer_rows, *float_params)
        gradients = pullback(buffer_cot)
        totals = tuple((total + gradient for total, gradient in zip(totals, gradients[1:])))
        return (totals, (buffer_out, gradients[0]))
    zero_totals = tuple((jnp.zeros_like(weight_item) for weight_item in float_params))
    totals, (outputs, input_grads) = lax.scan(buffer_step, zero_totals, (all_rows, all_cot, all_segments))
    return (outputs.reshape(TOKENS, D).astype(jnp.bfloat16), input_grads.reshape(TOKENS, D).astype(jnp.bfloat16), totals[0], totals[1], totals[2], totals[3], totals[4], totals[5], totals[6], totals[7], totals[8], totals[9], totals[10])
```

```python
import functools

import jax
import jax.numpy as jnp
from jax import lax
from jax.experimental import pallas as pl
from jax.experimental.pallas import tpu as pltpu
from jax.sharding import PartitionSpec as P

KEY = 256
VAL = 512
CHUNK = 256
HEAD = 2 * KEY + 2 * VAL

norm_epsilon = 1e-05
group_floor = 0.5
key_scale = KEY ** (-0.5)

f32 = jnp.float32
bf16 = jnp.bfloat16


def dot_nn(left, right):
    return lax.dot_general(left, right, (((1,), (0,)), ((), ())), preferred_element_type=f32)


def dot_nt(left, right):
    return lax.dot_general(left, right, (((1,), (1,)), ((), ())), preferred_element_type=f32)


def dot_tn(left, right):
    return lax.dot_general(left, right, (((0,), (0,)), ((), ())), preferred_element_type=f32)


def tensor_permute(values, bit):
    pairs = [(i, i ^ bit) for i in range(4)]
    return lax.ppermute(values, "tensor", pairs)


def gather_pieces(own, devices):
    if devices != 4:
        whole = lax.all_gather(own, "tensor", axis=0, tiled=True)
        return list(jnp.split(whole, devices, axis=0))
    half = own.shape[0] // 2
    from_x = tensor_permute(own, 1)
    from_y = tensor_permute(own, 2)
    lower = tensor_permute(from_y[:half], 1)
    upper = tensor_permute(from_x[half:], 2)
    return [own, from_x, from_y, jnp.concatenate([lower, upper], axis=0)]


def scatter_sum(terms):
    if len(terms) != 4:
        stacked = jnp.concatenate([term.astype(bf16) for term in terms], axis=0)
        return lax.psum_scatter(stacked, "tensor", scatter_dimension=0, tiled=True).astype(f32)
    own, over_x, over_y, across = terms
    half = own.shape[0] // 2
    across = across.astype(bf16)
    first = tensor_permute(across[:half], 1)
    second = tensor_permute(across[half:], 2)
    over_y = jnp.concatenate([over_y[:half] + first.astype(f32), over_y[half:]], axis=0)
    over_x = jnp.concatenate([over_x[:half], over_x[half:] + second.astype(f32)], axis=0)
    by_x = tensor_permute(over_x.astype(bf16), 1)
    by_y = tensor_permute(over_y.astype(bf16), 2)
    return own + by_x.astype(f32) + by_y.astype(f32)


def normalize(values):
    average = jnp.mean(values, axis=-1, keepdims=True)
    centred = values - average
    variance = jnp.mean(centred * centred, axis=-1, keepdims=True)
    scale = lax.rsqrt(variance + norm_epsilon)
    return centred * scale, scale


def normalize_back(normed_grad, unit, scale, gain):
    g = normed_grad * gain
    mean_g = jnp.mean(g, axis=-1, keepdims=True)
    mean_gx = jnp.mean(g * unit, axis=-1, keepdims=True)
    return scale * (g - mean_g - unit * mean_gx)


def gelu_both(values):
    inner = 0.7978845608 * (values + 0.044715 * values * values * values)
    t = jnp.tanh(inner)
    slope = 0.7978845608 * (1.0 + 3.0 * 0.044715 * values * values)
    return 0.5 * values * (1.0 + t), 0.5 * (1.0 + t) + 0.5 * values * (1.0 - t * t) * slope


def turn(block, cosine, sine):
    a = block[:, : KEY // 2]
    b = block[:, KEY // 2 :]
    return jnp.concatenate([a * cosine - b * sine, b * cosine + a * sine], axis=1)


def turn_back(block, cosine, sine):
    a = block[:, : KEY // 2]
    b = block[:, KEY // 2 :]
    return jnp.concatenate([a * cosine + b * sine, b * cosine - a * sine], axis=1)


def head_parts(field, angles, head):
    base = head * HEAD
    cosine = angles[:, : KEY // 2]
    sine = angles[:, KEY // 2 :]
    query = turn(field[:, base : base + KEY].astype(f32), cosine, sine).astype(bf16)
    key = turn(field[:, base + KEY : base + 2 * KEY].astype(f32), cosine, sine)
    key = (key * key_scale).astype(bf16)
    value = field[:, base + 2 * KEY : base + 2 * KEY + VAL]
    gate = field[:, base + 2 * KEY + VAL : base + HEAD].astype(f32)
    return query, key, value, gate


def retention_forward(heads, which, field_ref, angle_ref, info_ref, row_ref, decay_ref, gated_ref, grouped_ref, scale_ref, past_ref, state_ref):
    @pl.when(pl.program_id(0) == 0)
    def _():
        state_ref[...] = jnp.zeros_like(state_ref)

    angles = angle_ref[...]
    info = info_ref[...]
    same = info[:, 0:1] == row_ref[0]
    for head in range(heads):
        query, key, value, gate = head_parts(field_ref[...], angles, head)
        into = info[:, 1 + 2 * head : 2 + 2 * head]
        onward = info[:, 2 + 2 * head : 3 + 2 * head]
        state = state_ref[head]
        past_ref[0, head] = state.astype(bf16)
        scores = dot_nt(query, key)
        weights = (jnp.where(same, decay_ref[head], 0.0) * scores).astype(bf16)
        retained = dot_nn(weights, value) + into * dot_nn(query, state.astype(bf16))
        moved = (key.astype(f32) * onward).astype(bf16)
        state_ref[head] = into[CHUNK - 1 :, :] * state + dot_tn(moved, value)
        centred = retained - jnp.mean(retained, axis=-1, keepdims=True)
        scale = lax.rsqrt(jnp.mean(centred * centred, axis=-1, keepdims=True) + group_floor)
        grouped = centred * scale
        gated = gate / (1.0 + jnp.exp(-gate)) * grouped
        columns = slice(head * VAL, (head + 1) * VAL)
        gated_ref[:, columns] = gated.astype(bf16)
        grouped_ref[:, columns] = grouped.astype(bf16)
        scale_ref[:, head * 128 : (head + 1) * 128] = jnp.broadcast_to(scale, (CHUNK, 128))


def retention_backward(heads, which, field_ref, angle_ref, info_ref, row_ref, decay_ref, grad_ref, grouped_ref, scale_ref, past_ref, back_ref, state_ref):
    @pl.when(pl.program_id(0) == 0)
    def _():
        state_ref[...] = jnp.zeros_like(state_ref)

    angles = angle_ref[...]
    cosine = angles[:, : KEY // 2]
    sine = angles[:, KEY // 2 :]
    info = info_ref[...]
    same = info[:, 0:1] == row_ref[0]
    for head in range(heads):
        query, key, value, gate = head_parts(field_ref[...], angles, head)
        into = info[:, 1 + 2 * head : 2 + 2 * head]
        onward = info[:, 2 + 2 * head : 3 + 2 * head]
        columns = slice(head * VAL, (head + 1) * VAL)
        gated_grad = grad_ref[:, columns].astype(f32)
        grouped = grouped_ref[:, columns].astype(f32)
        scale = scale_ref[:, head * 128 : head * 128 + 1]
        sigmoid = 1.0 / (1.0 + jnp.exp(-gate))
        gate_grad = gated_grad * grouped * (sigmoid * (1.0 + gate * (1.0 - sigmoid)))
        c = gated_grad * (gate * sigmoid)
        mean_c = jnp.mean(c, axis=-1, keepdims=True)
        mean_cx = jnp.mean(c * grouped, axis=-1, keepdims=True)
        out_grad = (scale * (c - mean_c - grouped * mean_cx)).astype(bf16)
        state = state_ref[head]
        state_low = state.astype(bf16)
        past = past_ref[0, head]
        masked = jnp.where(same, decay_ref[head], 0.0)
        weights = (masked * dot_nt(query, key)).astype(bf16)
        score_grad = (masked * dot_nt(out_grad, value)).astype(bf16)
        value_grad = dot_tn(weights, out_grad) + onward * dot_nn(key, state_low)
        query_grad = dot_nn(score_grad, key) + into * dot_nt(out_grad, past)
        key_grad = dot_tn(score_grad, query) + onward * dot_nt(value, state_low)
        moved = (query.astype(f32) * into).astype(bf16)
        state_ref[head] = into[CHUNK - 1 :, :] * state + dot_tn(moved, out_grad)
        base = head * HEAD
        back_ref[:, base : base + KEY] = turn_back(query_grad, cosine, sine).astype(bf16)
        back_ref[:, base + KEY : base + 2 * KEY] = (turn_back(key_grad, cosine, sine) * key_scale).astype(bf16)
        back_ref[:, base + 2 * KEY : base + 2 * KEY + VAL] = value_grad.astype(bf16)
        back_ref[:, base + 2 * KEY + VAL : base + HEAD] = gate_grad.astype(bf16)


def retention_tables(segment, heads, first_head):
    rows = segment.shape[0]
    chunks = rows // CHUNK
    index = jnp.arange(rows, dtype=jnp.int32)
    boundary = jnp.concatenate([jnp.ones((1,), jnp.int32), (segment[1:] != segment[:-1]).astype(jnp.int32)])
    position = index - lax.cummax(jnp.where(boundary > 0, index, 0), axis=0)
    half = KEY // 2
    frequency = jnp.exp(-jnp.log(10000.0) * jnp.arange(half, dtype=f32) / half)
    angles = position.astype(f32)[:, None] * frequency[None, :]
    angles = jnp.concatenate([jnp.cos(angles), jnp.sin(angles)], axis=1)
    head_ids = (first_head + jnp.arange(heads, dtype=jnp.int32)).astype(f32)
    log_decay = jnp.log1p(-jnp.exp2(-5.0 - head_ids))
    last = segment.reshape(chunks, CHUNK)[:, -1]
    before = jnp.concatenate([jnp.full((1,), -2, jnp.int32), last[:-1]])
    offset = (index % CHUNK).astype(f32)
    linked_in = (segment == jnp.repeat(before, CHUNK)) & (segment >= 0)
    linked_on = (segment == jnp.repeat(last, CHUNK)) & (segment >= 0)
    columns = [segment.astype(f32)]
    for head in range(heads):
        columns.append(jnp.where(linked_in, jnp.exp(log_decay[head] * (offset + 1.0)), 0.0))
        columns.append(jnp.where(linked_on, jnp.exp(log_decay[head] * (CHUNK - 1.0 - offset)), 0.0))
    info = jnp.stack(columns, axis=1)
    info = jnp.pad(info, ((0, 0), (0, 128 - info.shape[1])))
    keys = jnp.where(segment >= 0, segment, -7).astype(f32).reshape(chunks, 1, CHUNK)
    distance = (jnp.arange(CHUNK)[:, None] - jnp.arange(CHUNK)[None, :]).astype(f32)
    decay = jnp.where(distance >= 0, jnp.exp(log_decay[:, None, None] * jnp.maximum(distance, 0.0)), 0.0)
    return angles, info, keys, decay


def retention_call(backward, which, piece_rows, heads, field, tables, extra):
    rows = field.shape[0]
    chunks = rows // CHUNK
    angles, info, keys, decay = tables
    per_piece = piece_rows // CHUNK

    def step(i):
        return chunks - 1 - i if backward else i

    def place(i, which_ref):
        c = step(i)
        return ((c // per_piece) ^ which_ref[0]) * per_piece + c % per_piece

    def placed(width):
        return pl.BlockSpec((CHUNK, width), lambda i, w: (place(i, w), 0))

    in_specs = [
        placed(heads * HEAD),
        pl.BlockSpec((CHUNK, KEY), lambda i, w: (step(i), 0)),
        pl.BlockSpec((CHUNK, 128), lambda i, w: (step(i), 0)),
        pl.BlockSpec((1, 1, CHUNK), lambda i, w: (step(i), 0, 0)),
        pl.BlockSpec((heads, CHUNK, CHUNK), lambda i, w: (0, 0, 0)),
    ]
    past_spec = pl.BlockSpec((1, heads, KEY, VAL), lambda i, w: (step(i), 0, 0, 0))
    if backward:
        in_specs += [placed(heads * VAL), placed(heads * VAL), placed(heads * 128), past_spec]
        out_specs = placed(heads * HEAD)
        out_shape = jax.ShapeDtypeStruct((rows, heads * HEAD), bf16)
    else:
        out_specs = [placed(heads * VAL), placed(heads * VAL), placed(heads * 128), past_spec]
        out_shape = [
            jax.ShapeDtypeStruct((rows, heads * VAL), bf16),
            jax.ShapeDtypeStruct((rows, heads * VAL), bf16),
            jax.ShapeDtypeStruct((rows, heads * 128), f32),
            jax.ShapeDtypeStruct((chunks, heads, KEY, VAL), bf16),
        ]
    products = 15 if backward else 7
    return pl.pallas_call(
        functools.partial(retention_backward if backward else retention_forward, heads),
        grid_spec=pltpu.PrefetchScalarGridSpec(
            num_scalar_prefetch=1,
            grid=(chunks,),
            in_specs=in_specs,
            out_specs=out_specs,
            scratch_shapes=[pltpu.VMEM((heads, KEY, VAL), f32)],
        ),
        out_shape=out_shape,
        compiler_params=pltpu.CompilerParams(
            dimension_semantics=("arbitrary",), vmem_limit_bytes=48 * 1024 * 1024
        ),
        cost_estimate=pl.CostEstimate(
            flops=products * chunks * heads * 2 * CHUNK * CHUNK * CHUNK,
            bytes_accessed=(5 if backward else 4) * rows * heads * HEAD,
            transcendentals=rows * heads * VAL,
        ),
        name="retention_backward" if backward else "retention_forward",
    )(which, field, angles, info, keys, decay, *extra)


def body(tokens, cotangent, segment, first_gain, first_bias, query_weight, key_weight, value_weight, gate_weight, out_weight, second_gain, second_bias, up_weight, down_weight):
    devices = lax.axis_size("tensor")
    rows = tokens.shape[0]
    heads = query_weight.shape[1] // KEY
    here = lax.axis_index("tensor")
    which = (here if devices == 4 else jnp.zeros_like(here)).astype(jnp.int32).reshape(1)

    def per_piece(values):
        return [values[i * rows : (i + 1) * rows] for i in range(devices)]

    shards = []
    for h in range(heads):
        shards += [
            query_weight[:, h * KEY : (h + 1) * KEY],
            key_weight[:, h * KEY : (h + 1) * KEY],
            value_weight[:, h * VAL : (h + 1) * VAL],
            gate_weight[:, h * VAL : (h + 1) * VAL],
        ]
    w_in = lax.all_gather(jnp.concatenate(shards, axis=1), "dp", axis=0, tiled=True)
    w_out = lax.all_gather(out_weight, "dp", axis=1, tiled=True)
    w_down = lax.all_gather(down_weight, "dp", axis=1, tiled=True)
    w_up = lax.all_gather(up_weight, "dp", axis=0, tiled=True)

    token_rows = tokens.astype(f32)
    unit1, scale1 = normalize(token_rows)
    normed1 = (unit1 * first_gain + first_bias).astype(bf16)
    normed1_all = jnp.concatenate(gather_pieces(normed1, devices), axis=0)
    cot_pieces = gather_pieces(cotangent, devices)
    tables = retention_tables(segment, heads, here * heads)
    field = dot_nn(normed1_all, w_in).astype(bf16)
    gated, grouped, group_scale, past = retention_call(False, which, rows, heads, field, tables, ())
    branch = scatter_sum([dot_nn(piece, w_out) for piece in per_piece(gated)])

    mixed = token_rows + branch
    unit2, scale2 = normalize(mixed)
    normed2 = (unit2 * second_gain + second_bias).astype(bf16)
    normed2_pieces = gather_pieces(normed2, devices)
    hidden_grads = [dot_nt(piece, w_down) for piece in cot_pieces]
    hidden, up_grad = [], []
    for piece, hidden_grad in zip(normed2_pieces, hidden_grads):
        value, slope = gelu_both(dot_nn(piece, w_up))
        hidden.append(value.astype(bf16))
        up_grad.append((hidden_grad * slope).astype(bf16))
    normed2_grad = scatter_sum([dot_nt(piece, w_up) for piece in up_grad])
    mixed_grad = cotangent.astype(f32) + normalize_back(normed2_grad, unit2, scale2, second_gain)
    gain2_grad = jnp.sum(normed2_grad * unit2, axis=0)
    bias2_grad = jnp.sum(normed2_grad, axis=0)
    mixed_pieces = gather_pieces(mixed_grad.astype(bf16), devices)
    ffn = scatter_sum([dot_nn(piece, w_down) for piece in hidden])
    result = (mixed + ffn).astype(bf16)
    normed2_all = jnp.concatenate(normed2_pieces, axis=0)
    up_grad_all = jnp.concatenate(up_grad, axis=0)
    cot_all = jnp.concatenate(cot_pieces, axis=0)
    hidden_all = jnp.concatenate(hidden, axis=0)
    up_weight_grad = dot_tn(normed2_all, up_grad_all).astype(bf16)
    down_weight_grad = dot_tn(hidden_all, cot_all).astype(bf16)

    gated_grad = jnp.concatenate([dot_nt(piece, w_out).astype(bf16) for piece in mixed_pieces], axis=0)
    mixed_all = jnp.concatenate(mixed_pieces, axis=0)
    back = retention_call(True, which, rows, heads, field, tables, (gated_grad, grouped, group_scale, past))
    out_weight_grad = dot_tn(gated, mixed_all).astype(bf16)
    normed1_grad = scatter_sum([dot_nt(piece, w_in) for piece in per_piece(back)])
    in_weight_grad = dot_tn(normed1_all, back).astype(bf16)
    input_grad = mixed_grad + normalize_back(normed1_grad, unit1, scale1, first_gain)
    gain1_grad = jnp.sum(normed1_grad * unit1, axis=0)
    bias1_grad = jnp.sum(normed1_grad, axis=0)

    up_sum = lax.psum_scatter(up_weight_grad, "dp", scatter_dimension=0, tiled=True).astype(f32)
    down_sum = lax.psum_scatter(down_weight_grad, "dp", scatter_dimension=1, tiled=True).astype(f32)
    out_sum = lax.psum_scatter(out_weight_grad, "dp", scatter_dimension=1, tiled=True).astype(f32)
    in_sum = lax.psum_scatter(in_weight_grad, "dp", scatter_dimension=0, tiled=True).astype(f32)

    def columns_of(start, width):
        return jnp.concatenate(
            [in_sum[:, h * HEAD + start : h * HEAD + start + width] for h in range(heads)], axis=1
        )

    norm_sums = [
        lax.psum_scatter(v, ("dp", "tensor"), scatter_dimension=0, tiled=True)
        for v in (gain1_grad, bias1_grad, gain2_grad, bias2_grad)
    ]
    return (
        result,
        input_grad.astype(bf16),
        norm_sums[0],
        norm_sums[1],
        columns_of(0, KEY),
        columns_of(KEY, KEY),
        columns_of(2 * KEY, VAL),
        columns_of(2 * KEY + VAL, VAL),
        out_sum,
        norm_sums[2],
        norm_sums[3],
        up_sum,
        down_sum,
    )


def solution(mesh):
    rows = P(("dp", "tensor"), None)
    vector = P(("dp", "tensor"))
    into = P("dp", "tensor")
    back = P("tensor", "dp")
    return jax.shard_map(
        body,
        mesh=mesh,
        in_specs=(rows, rows, P("dp"), P(), P(), into, into, into, into, back, P(), P(), into, back),
        out_specs=(rows, rows, vector, vector, into, into, into, into, back, vector, vector, into, back),
        check_vma=False,
    )
```

```python
import functools

import jax
import jax.numpy as jnp
from jax import lax
from jax.experimental import pallas as pl
from jax.experimental.pallas import tpu as pltpu
from jax.sharding import PartitionSpec as P

KEY = 256
VAL = 512
CHUNK = 256
QKV = 2 * KEY + VAL

norm_epsilon = 1e-05
group_floor = 0.5
key_scale = KEY ** (-0.5)

f32 = jnp.float32
bf16 = jnp.bfloat16


def dot_nn(left, right):
    return lax.dot_general(left, right, (((1,), (0,)), ((), ())), preferred_element_type=f32)


def dot_nt(left, right):
    return lax.dot_general(left, right, (((1,), (1,)), ((), ())), preferred_element_type=f32)


def dot_tn(left, right):
    return lax.dot_general(left, right, (((0,), (0,)), ((), ())), preferred_element_type=f32)


def tensor_permute(values, bit):
    pairs = [(i, i ^ bit) for i in range(4)]
    return lax.ppermute(values, "tensor", pairs)


def after(values, *tokens):
    return lax.optimization_barrier((values, tokens))[0]


def gather_pieces(own, devices, between=()):
    if devices != 4:
        whole = lax.all_gather(own, "tensor", axis=0, tiled=True)
        return list(jnp.split(whole, devices, axis=0))
    half = own.shape[0] // 2
    from_x = tensor_permute(own, 1)
    from_y = tensor_permute(own, 2)
    lower, upper = after((from_y[:half], from_x[half:]), *between)
    lower = tensor_permute(lower, 1)
    upper = tensor_permute(upper, 2)
    return [own, from_x, from_y, jnp.concatenate([lower, upper], axis=0)]


def scatter_sum(terms):
    if len(terms) != 4:
        stacked = jnp.concatenate([term.astype(bf16) for term in terms], axis=0)
        return lax.psum_scatter(stacked, "tensor", scatter_dimension=0, tiled=True).astype(f32), (stacked,), (stacked,)
    own, over_x, over_y, across = terms
    half = own.shape[0] // 2
    across = across.astype(bf16)
    first = tensor_permute(across[:half], 1)
    second = tensor_permute(across[half:], 2)
    over_y = jnp.concatenate([over_y[:half] + first.astype(f32), over_y[half:]], axis=0)
    over_x = jnp.concatenate([over_x[:half], over_x[half:] + second.astype(f32)], axis=0)
    by_x = tensor_permute(over_x.astype(bf16), 1)
    by_y = tensor_permute(over_y.astype(bf16), 2)
    return own + by_x.astype(f32) + by_y.astype(f32), (first, second), (by_x, by_y)


def spread_sum_kernel(tensor_devices, devices, given_ref, sum_ref, landed_ref, send_sem, recv_sem):
    here = lax.axis_index("dp") * tensor_devices + lax.axis_index("tensor")

    def partner(k):
        other = lax.rem(here + k, devices)
        return other, (lax.div(other, tensor_devices), lax.rem(other, tensor_devices))

    def copy(k):
        other, device = partner(k)
        return pltpu.make_async_remote_copy(
            src_ref=given_ref.at[other],
            dst_ref=landed_ref.at[k],
            send_sem=send_sem.at[k],
            recv_sem=recv_sem.at[k],
            device_id=device,
            device_id_type=pl.DeviceIdType.MESH,
        )

    barrier = pltpu.get_barrier_semaphore()

    @pl.loop(1, devices)
    def _(k):
        pl.semaphore_signal(barrier, inc=1, device_id=partner(k)[1], device_id_type=pl.DeviceIdType.MESH)

    pl.semaphore_wait(barrier, devices - 1)

    @pl.loop(1, devices)
    def _(k):
        copy(k).start()

    sum_ref[...] = given_ref[here]

    @pl.loop(1, devices)
    def _(k):
        copy(k).wait()
        sum_ref[...] += landed_ref[k]


def spread_sum(vectors):
    dp, tensor = lax.axis_size("dp"), lax.axis_size("tensor")
    devices = dp * tensor
    part = vectors[0].shape[0] // devices
    given = jnp.stack([v.reshape(devices, part) for v in vectors], axis=1)
    given = jnp.pad(given, ((0, 0), (0, 8 - len(vectors)), (0, 128 - part)))
    total = pl.pallas_call(
        functools.partial(spread_sum_kernel, tensor, devices),
        out_shape=jax.ShapeDtypeStruct((8, 128), f32),
        in_specs=[pl.BlockSpec(memory_space=pltpu.VMEM)],
        out_specs=pl.BlockSpec(memory_space=pltpu.VMEM),
        scratch_shapes=[
            pltpu.VMEM((devices, 8, 128), f32),
            pltpu.SemaphoreType.DMA((devices,)),
            pltpu.SemaphoreType.DMA((devices,)),
        ],
        compiler_params=pltpu.CompilerParams(collective_id=1, has_side_effects=True),
        name="spread_sum",
    )(given)
    return [total[i, :part] for i in range(len(vectors))]


def normalize(values):
    average = jnp.mean(values, axis=-1, keepdims=True)
    centred = values - average
    variance = jnp.mean(centred * centred, axis=-1, keepdims=True)
    scale = lax.rsqrt(variance + norm_epsilon)
    return centred * scale, scale


def normalize_back(normed_grad, unit, scale, gain):
    g = normed_grad * gain
    mean_g = jnp.mean(g, axis=-1, keepdims=True)
    mean_gx = jnp.mean(g * unit, axis=-1, keepdims=True)
    return scale * (g - mean_g - unit * mean_gx)


def gelu_both(values):
    inner = 0.7978845608 * (values + 0.044715 * values * values * values)
    t = jnp.tanh(inner)
    slope = 0.7978845608 * (1.0 + 3.0 * 0.044715 * values * values)
    return 0.5 * values * (1.0 + t), 0.5 * (1.0 + t) + 0.5 * values * (1.0 - t * t) * slope


def turn(block, cosine, sine):
    a = block[:, : KEY // 2]
    b = block[:, KEY // 2 :]
    return jnp.concatenate([a * cosine - b * sine, b * cosine + a * sine], axis=1)


def turn_back(block, cosine, sine):
    a = block[:, : KEY // 2]
    b = block[:, KEY // 2 :]
    return jnp.concatenate([a * cosine + b * sine, b * cosine - a * sine], axis=1)


def head_parts(field_ref, angles, heads, head):
    cosine = angles[:, : KEY // 2]
    sine = angles[:, KEY // 2 :]
    query_at = head * KEY
    key_at = (heads + head) * KEY
    value_at = 2 * heads * KEY + head * VAL
    query = turn(field_ref[:, query_at : query_at + KEY].astype(f32), cosine, sine).astype(bf16)
    key = turn(field_ref[:, key_at : key_at + KEY].astype(f32), cosine, sine)
    key = (key * key_scale).astype(bf16)
    return query, key, field_ref[:, value_at : value_at + VAL]


def retention_forward(heads, which, field_ref, gate_ref, angle_ref, info_ref, row_ref, decay_ref, gated_ref, grouped_ref, scale_ref, past_ref, state_ref):
    @pl.when(pl.program_id(0) == 0)
    def _():
        state_ref[...] = jnp.zeros_like(state_ref)

    angles = angle_ref[...]
    info = info_ref[...]
    same = info[:, 0:1] == row_ref[0]
    for head in range(heads):
        query, key, value = head_parts(field_ref, angles, heads, head)
        columns = slice(head * VAL, (head + 1) * VAL)
        gate = gate_ref[:, columns].astype(f32)
        into = info[:, 1 + 2 * head : 2 + 2 * head]
        onward = info[:, 2 + 2 * head : 3 + 2 * head]
        state = state_ref[head]
        past_ref[0, head] = state.astype(bf16)
        scores = dot_nt(query, key)
        weights = (jnp.where(same, decay_ref[head], 0.0) * scores).astype(bf16)
        retained = dot_nn(weights, value) + into * dot_nn(query, state.astype(bf16))
        moved = (key.astype(f32) * onward).astype(bf16)
        state_ref[head] = into[CHUNK - 1 :, :] * state + dot_tn(moved, value)
        centred = retained - jnp.mean(retained, axis=-1, keepdims=True)
        scale = lax.rsqrt(jnp.mean(centred * centred, axis=-1, keepdims=True) + group_floor)
        grouped = centred * scale
        gated = gate / (1.0 + jnp.exp(-gate)) * grouped
        gated_ref[:, columns] = gated.astype(bf16)
        grouped_ref[:, columns] = grouped.astype(bf16)
        scale_ref[:, head * 128 : (head + 1) * 128] = jnp.broadcast_to(scale, (CHUNK, 128))


def retention_backward(heads, which, field_ref, gate_ref, angle_ref, info_ref, row_ref, decay_ref, grad_ref, grouped_ref, scale_ref, past_ref, back_ref, state_ref):
    @pl.when(pl.program_id(0) == 0)
    def _():
        state_ref[...] = jnp.zeros_like(state_ref)

    angles = angle_ref[...]
    cosine = angles[:, : KEY // 2]
    sine = angles[:, KEY // 2 :]
    info = info_ref[...]
    same = info[:, 0:1] == row_ref[0]
    for head in range(heads):
        query, key, value = head_parts(field_ref, angles, heads, head)
        columns = slice(head * VAL, (head + 1) * VAL)
        gate = gate_ref[:, columns].astype(f32)
        into = info[:, 1 + 2 * head : 2 + 2 * head]
        onward = info[:, 2 + 2 * head : 3 + 2 * head]
        grouped = grouped_ref[:, columns].astype(f32)
        scale = scale_ref[:, head * 128 : head * 128 + 1]
        c = grad_ref[:, columns].astype(f32) * (gate / (1.0 + jnp.exp(-gate)))
        mean_c = jnp.mean(c, axis=-1, keepdims=True)
        mean_cx = jnp.mean(c * grouped, axis=-1, keepdims=True)
        out_grad = (scale * (c - mean_c - grouped * mean_cx)).astype(bf16)
        state = state_ref[head]
        state_low = state.astype(bf16)
        past = past_ref[0, head]
        masked = jnp.where(same, decay_ref[head], 0.0)
        weights = (masked * dot_nt(query, key)).astype(bf16)
        score_grad = (masked * dot_nt(out_grad, value)).astype(bf16)
        value_grad = dot_tn(weights, out_grad) + onward * dot_nn(key, state_low)
        query_grad = dot_nn(score_grad, key) + into * dot_nt(out_grad, past)
        key_grad = dot_tn(score_grad, query) + onward * dot_nt(value, state_low)
        moved = (query.astype(f32) * into).astype(bf16)
        state_ref[head] = into[CHUNK - 1 :, :] * state + dot_tn(moved, out_grad)
        query_at = head * KEY
        key_at = (heads + head) * KEY
        value_at = 2 * heads * KEY + head * VAL
        back_ref[:, query_at : query_at + KEY] = turn_back(query_grad, cosine, sine).astype(bf16)
        back_ref[:, key_at : key_at + KEY] = (turn_back(key_grad, cosine, sine) * key_scale).astype(bf16)
        back_ref[:, value_at : value_at + VAL] = value_grad.astype(bf16)


def retention_tables(segment, heads, first_head):
    rows = segment.shape[0]
    chunks = rows // CHUNK
    index = jnp.arange(rows, dtype=jnp.int32)
    boundary = jnp.concatenate([jnp.ones((1,), jnp.int32), (segment[1:] != segment[:-1]).astype(jnp.int32)])
    position = index - lax.cummax(jnp.where(boundary > 0, index, 0), axis=0)
    half = KEY // 2
    frequency = jnp.exp(-jnp.log(10000.0) * jnp.arange(half, dtype=f32) / half)
    angles = position.astype(f32)[:, None] * frequency[None, :]
    angles = jnp.concatenate([jnp.cos(angles), jnp.sin(angles)], axis=1)
    head_ids = (first_head + jnp.arange(heads, dtype=jnp.int32)).astype(f32)
    log_decay = jnp.log1p(-jnp.exp2(-5.0 - head_ids))
    last = segment.reshape(chunks, CHUNK)[:, -1]
    before = jnp.concatenate([jnp.full((1,), -2, jnp.int32), last[:-1]])
    offset = (index % CHUNK).astype(f32)
    linked_in = (segment == jnp.repeat(before, CHUNK)) & (segment >= 0)
    linked_on = (segment == jnp.repeat(last, CHUNK)) & (segment >= 0)
    columns = [segment.astype(f32)]
    for head in range(heads):
        columns.append(jnp.where(linked_in, jnp.exp(log_decay[head] * (offset + 1.0)), 0.0))
        columns.append(jnp.where(linked_on, jnp.exp(log_decay[head] * (CHUNK - 1.0 - offset)), 0.0))
    info = jnp.stack(columns, axis=1)
    info = jnp.pad(info, ((0, 0), (0, 128 - info.shape[1])))
    keys = jnp.where(segment >= 0, segment, -7).astype(f32).reshape(chunks, 1, CHUNK)
    distance = (jnp.arange(CHUNK)[:, None] - jnp.arange(CHUNK)[None, :]).astype(f32)
    decay = jnp.where(distance >= 0, jnp.exp(log_decay[:, None, None] * jnp.maximum(distance, 0.0)), 0.0)
    return angles, info, keys, decay


def retention_call(backward, which, piece_rows, heads, field, gate, tables, extra):
    rows = field.shape[0]
    chunks = rows // CHUNK
    angles, info, keys, decay = tables
    per_piece = piece_rows // CHUNK

    def step(i):
        return chunks - 1 - i if backward else i

    def place(i, which_ref):
        c = step(i)
        return ((c // per_piece) ^ which_ref[0]) * per_piece + c % per_piece

    def placed(width):
        return pl.BlockSpec((CHUNK, width), lambda i, w: (place(i, w), 0))

    in_specs = [
        placed(heads * QKV),
        placed(heads * VAL),
        pl.BlockSpec((CHUNK, KEY), lambda i, w: (step(i), 0)),
        pl.BlockSpec((CHUNK, 128), lambda i, w: (step(i), 0)),
        pl.BlockSpec((1, 1, CHUNK), lambda i, w: (step(i), 0, 0)),
        pl.BlockSpec((heads, CHUNK, CHUNK), lambda i, w: (0, 0, 0)),
    ]
    past_spec = pl.BlockSpec((1, heads, KEY, VAL), lambda i, w: (step(i), 0, 0, 0))
    if backward:
        in_specs += [placed(heads * VAL), placed(heads * VAL), placed(heads * 128), past_spec]
        out_specs = placed(heads * QKV)
        out_shape = jax.ShapeDtypeStruct((rows, heads * QKV), bf16)
    else:
        out_specs = [placed(heads * VAL), placed(heads * VAL), placed(heads * 128), past_spec]
        out_shape = [
            jax.ShapeDtypeStruct((rows, heads * VAL), bf16),
            jax.ShapeDtypeStruct((rows, heads * VAL), bf16),
            jax.ShapeDtypeStruct((rows, heads * 128), f32),
            jax.ShapeDtypeStruct((chunks, heads, KEY, VAL), bf16),
        ]
    products = 15 if backward else 7
    return pl.pallas_call(
        functools.partial(retention_backward if backward else retention_forward, heads),
        grid_spec=pltpu.PrefetchScalarGridSpec(
            num_scalar_prefetch=1,
            grid=(chunks,),
            in_specs=in_specs,
            out_specs=out_specs,
            scratch_shapes=[pltpu.VMEM((heads, KEY, VAL), f32)],
        ),
        out_shape=out_shape,
        compiler_params=pltpu.CompilerParams(
            dimension_semantics=("arbitrary",), vmem_limit_bytes=48 * 1024 * 1024
        ),
        cost_estimate=pl.CostEstimate(
            flops=products * chunks * heads * 2 * CHUNK * CHUNK * CHUNK,
            bytes_accessed=(5 if backward else 4) * rows * heads * (QKV + VAL),
            transcendentals=rows * heads * VAL,
        ),
        name="retention_backward" if backward else "retention_forward",
    )(which, field, gate, angles, info, keys, decay, *extra)


MESH = pl.DeviceIdType.MESH


def opening_kernel(
    query_ref, key_ref, value_ref, gate_ref, token_ref, gain_ref, bias_ref, cot_ref,
    w_qkv_ref, w_gate_ref, normed_ref, cot_all_ref,
    w_qkv, w_gate, normed, token_own, cot_own, cot_got,
    local_sem, out_sem, up_send, up_recv, down_send, down_recv, core_send, core_recv, row_send, row_recv,
):
    dp = lax.axis_index("dp")
    tensor = lax.axis_index("tensor")
    z = lax.div(dp, 2)
    layers = lax.div(lax.axis_size("dp"), 2)
    shard_rows = query_ref.shape[0]
    rows = token_ref.shape[0]
    half = rows // 2
    above = (dp + 2, tensor)
    below = (dp - 2, tensor)
    twin = (dp + 1 - 2 * lax.rem(dp, 2), tensor)
    over_x = (dp, tensor + 1 - 2 * lax.rem(tensor, 2))
    over_y = (dp, lax.rem(tensor + 2, 4))

    keys = query_ref.shape[1]
    values = value_ref.shape[1]
    mine = pl.ds(pl.multiple_of(dp * shard_rows, shard_rows), shard_rows)
    places = [
        (query_ref, w_qkv.at[mine, pl.ds(0, keys)]),
        (key_ref, w_qkv.at[mine, pl.ds(keys, keys)]),
        (value_ref, w_qkv.at[mine, pl.ds(2 * keys, values)]),
        (gate_ref, w_gate.at[mine]),
        (token_ref, token_own),
        (cot_ref.at[pl.ds(0, half)], cot_own),
    ]
    local = [pltpu.make_async_copy(a, b, local_sem.at[i]) for i, (a, b) in enumerate(places)]
    for copy in local:
        copy.start()

    barrier = pltpu.get_barrier_semaphore()

    def greet(device):
        pl.semaphore_signal(barrier, inc=1, device_id=device, device_id_type=MESH)

    for device in (twin, over_x, over_y):
        greet(device)
    pl.when(z < layers - 1)(lambda: greet(above))
    pl.when(z > 0)(lambda: greet(below))
    pl.semaphore_wait(barrier, 3 + (z < layers - 1).astype(jnp.int32) + (z > 0).astype(jnp.int32))
    for copy in local[:4]:
        copy.wait()

    def weight_copies(shard, send_sem, recv_sem, step, device):
        place = pl.ds(pl.multiple_of(shard * shard_rows, shard_rows), shard_rows)
        return [
            pltpu.make_async_remote_copy(
                src_ref=ref.at[place], dst_ref=ref.at[place],
                send_sem=send_sem.at[step, i], recv_sem=recv_sem.at[step, i],
                device_id=device, device_id_type=MESH,
            )
            for i, ref in enumerate((w_qkv, w_gate))
        ]

    def shard_out(shard, slot):
        place = pl.ds(pl.multiple_of(shard * shard_rows, shard_rows), shard_rows)
        return [
            pltpu.make_async_copy(w_qkv.at[place], w_qkv_ref.at[place], out_sem.at[slot, 0]),
            pltpu.make_async_copy(w_gate.at[place], w_gate_ref.at[place], out_sem.at[slot, 1]),
        ]

    def start(copies):
        for copy in copies:
            copy.start()

    def wait_send(copies):
        for copy in copies:
            copy.wait_send()

    def wait_recv(copies):
        for copy in copies:
            copy.wait_recv()

    def up(j):
        return weight_copies(dp - 2 * j, up_send, up_recv, j, above)

    def down(j):
        return weight_copies(dp + 2 * j, down_send, down_recv, j, below)

    def to_twin(j):
        return weight_copies(dp + 2 * j, core_send, core_recv, j + 3, twin)

    def from_twin(j):
        return weight_copies(twin[0] + 2 * j, core_send, core_recv, j + 3, twin)

    def step(j):
        @pl.when(z - j >= 0)
        def _():
            wait_recv(weight_copies(dp - 2 * j, up_send, up_recv, j - 1, twin))
            if j < 3:
                pl.when(z < layers - 1)(lambda: start(up(j)))
            start(to_twin(-j))
            start(shard_out(dp - 2 * j, 3 - j))

        @pl.when(z + j < layers)
        def _():
            wait_recv(weight_copies(dp + 2 * j, down_send, down_recv, j - 1, twin))
            if j < 3:
                pl.when(z > 0)(lambda: start(down(j)))
            start(to_twin(j))
            start(shard_out(dp + 2 * j, 3 + j))

    pl.when(z < layers - 1)(lambda: start(up(0)))
    pl.when(z > 0)(lambda: start(down(0)))
    start(to_twin(0))
    start(shard_out(dp, 3))

    local[4].wait()

    @pl.loop(0, rows // 64)
    def _(i):
        block = pl.ds(pl.multiple_of(i * 64, 64), 64)
        unit, _ = normalize(token_own[block, :].astype(f32))
        normed[block, :] = (unit * gain_ref[...] + bias_ref[...]).astype(bf16)

    def row_copy(index, src, dst, device):
        return pltpu.make_async_remote_copy(
            src_ref=src, dst_ref=dst, send_sem=row_send.at[index], recv_sem=row_recv.at[index],
            device_id=device, device_id_type=MESH,
        )

    local[5].wait()
    over = [
        row_copy(0, normed.at[pl.ds(0, rows)], normed.at[pl.ds(rows, rows)], over_x),
        row_copy(1, normed.at[pl.ds(0, rows)], normed.at[pl.ds(2 * rows, rows)], over_y),
    ]
    start(over)
    step(1)
    wait_recv(over)
    onward = [
        row_copy(2, normed.at[pl.ds(2 * rows, half)], normed.at[pl.ds(3 * rows, half)], over_x),
        row_copy(3, normed.at[pl.ds(rows + half, half)], normed.at[pl.ds(3 * rows + half, half)], over_y),
    ]
    start(onward)
    cots = [
        row_copy(4, cot_own, cot_got.at[0], over_x),
        row_copy(5, cot_own, cot_got.at[1], over_y),
    ]
    start(cots)
    step(2)
    wait_recv(onward)
    normed_out = pltpu.make_async_copy(normed, normed_ref, local_sem.at[6])
    normed_out.start()
    wait_recv(cots)
    cot_out = pltpu.make_async_copy(cot_got, cot_all_ref, local_sem.at[7])
    cot_out.start()
    step(3)

    for j in range(-3, 4):
        @pl.when((z + j >= 0) & (z + j < layers))
        def _():
            wait_recv(from_twin(j))
            start(shard_out(twin[0] + 2 * j, 10 + j))
    wait_send(over + onward + cots)
    for j in range(3):
        pl.when((z < layers - 1) & (z - j >= 0))(lambda: wait_send(up(j)))
        pl.when((z > 0) & (z + j < layers))(lambda: wait_send(down(j)))
    normed_out.wait()
    cot_out.wait()
    for j in range(-3, 4):
        @pl.when((z + j >= 0) & (z + j < layers))
        def _():
            wait_send(to_twin(j))
            for copy in shard_out(dp + 2 * j, 3 + j) + shard_out(twin[0] + 2 * j, 10 + j):
                copy.wait()


def opening_exchange(query_weight, key_weight, value_weight, gate_weight, tokens, gain, bias, cotangent):
    dp = lax.axis_size("dp")
    depth, keys = query_weight.shape
    values = value_weight.shape[1]
    rows, width = tokens.shape
    anywhere = pl.BlockSpec(memory_space=pl.ANY)
    in_vmem = pl.BlockSpec(memory_space=pltpu.VMEM)
    return pl.pallas_call(
        opening_kernel,
        out_shape=[
            jax.ShapeDtypeStruct((dp * depth, 2 * keys + values), bf16),
            jax.ShapeDtypeStruct((dp * depth, values), bf16),
            jax.ShapeDtypeStruct((4 * rows, width), bf16),
            jax.ShapeDtypeStruct((2, rows // 2, width), bf16),
        ],
        in_specs=[anywhere] * 5 + [in_vmem] * 2 + [anywhere],
        out_specs=[anywhere] * 4,
        scratch_shapes=[
            pltpu.VMEM((dp * depth, 2 * keys + values), bf16),
            pltpu.VMEM((dp * depth, values), bf16),
            pltpu.VMEM((4 * rows, width), bf16),
            pltpu.VMEM((rows, width), bf16),
            pltpu.VMEM((rows // 2, width), bf16),
            pltpu.VMEM((2, rows // 2, width), bf16),
            pltpu.SemaphoreType.DMA((8,)),
            pltpu.SemaphoreType.DMA((14, 2)),
            pltpu.SemaphoreType.DMA((3, 2)),
            pltpu.SemaphoreType.DMA((3, 2)),
            pltpu.SemaphoreType.DMA((3, 2)),
            pltpu.SemaphoreType.DMA((3, 2)),
            pltpu.SemaphoreType.DMA((7, 2)),
            pltpu.SemaphoreType.DMA((7, 2)),
            pltpu.SemaphoreType.DMA((6,)),
            pltpu.SemaphoreType.DMA((6,)),
        ],
        compiler_params=pltpu.CompilerParams(
            collective_id=2, has_side_effects=True, vmem_limit_bytes=60 * 1024 * 1024
        ),
        name="opening_exchange",
    )(query_weight, key_weight, value_weight, gate_weight, tokens, gain.reshape(1, width), bias.reshape(1, width), cotangent)


def opening(query_weight, key_weight, value_weight, gate_weight, tokens, gain, bias, cotangent, devices):
    if devices == 4 and lax.axis_size("dp") == 8:
        w_qkv, w_gate, normed1_all, cot_half = opening_exchange(
            query_weight, key_weight, value_weight, gate_weight, tokens, gain, bias, cotangent
        )
        half = tokens.shape[0] // 2
        rest = after(cotangent, cot_half)[half:]
        rest_x = tensor_permute(rest, 1)
        rest_y = tensor_permute(rest, 2)
        lower = tensor_permute(cot_half[1], 1)
        upper = tensor_permute(rest_x, 2)
        cots = [cotangent, cot_half[0], rest_x, cot_half[1], rest_y, lower, upper]
        return w_qkv, w_gate, normed1_all, cots, (rest_x, rest_y)
    w_qkv = lax.all_gather(jnp.concatenate([query_weight, key_weight, value_weight], axis=1), "dp", axis=0, tiled=True)
    w_gate = lax.all_gather(gate_weight, "dp", axis=0, tiled=True)
    unit, _ = normalize(tokens.astype(f32))
    normed1_all = jnp.concatenate(gather_pieces((unit * gain + bias).astype(bf16), devices), axis=0)
    cots = gather_pieces(cotangent, devices)
    return w_qkv, w_gate, normed1_all, cots, (cots[0],)


def body(tokens, cotangent, segment, first_gain, first_bias, query_weight, key_weight, value_weight, gate_weight, out_weight, second_gain, second_bias, up_weight, down_weight):
    devices = lax.axis_size("tensor")
    rows = tokens.shape[0]
    heads = query_weight.shape[1] // KEY
    here = lax.axis_index("tensor")
    which = (here if devices == 4 else jnp.zeros_like(here)).astype(jnp.int32).reshape(1)

    def per_piece(values):
        return [values[i * rows : (i + 1) * rows] for i in range(devices)]

    w_qkv, w_gate, normed1_all, cots, cot_begun = opening(
        query_weight, key_weight, value_weight, gate_weight, tokens, first_gain, first_bias, cotangent, devices
    )
    w_out = lax.all_gather(after(out_weight, w_gate), "dp", axis=1, tiled=True)
    w_down = lax.all_gather(after(down_weight, w_out), "dp", axis=1, tiled=True)
    w_up = lax.all_gather(after(up_weight, w_down), "dp", axis=0, tiled=True)

    token_rows = tokens.astype(f32)
    unit1, scale1 = normalize(token_rows)
    tables = retention_tables(segment, heads, here * heads)
    field = dot_nn(normed1_all, w_qkv).astype(bf16)
    gate = dot_nn(normed1_all, w_gate).astype(bf16)
    gated, grouped, group_scale, past = retention_call(
        False, which, rows, heads, field, after(gate, *cot_begun), tables, ()
    )
    branch, begun, _ = scatter_sum([dot_nn(piece, w_out) for piece in per_piece(after(gated, *cots))])

    mixed = token_rows + branch
    unit2, scale2 = normalize(mixed)
    normed2 = (unit2 * second_gain + second_bias).astype(bf16)
    cot_all = jnp.concatenate(after(cots, *begun), axis=0)
    hidden_grads = per_piece(dot_nt(cot_all, after(w_down, normed2)).astype(bf16))

    def feed(piece, hidden_grad):
        value, slope = gelu_both(dot_nn(piece, w_up))
        return after((value.astype(bf16), (hidden_grad.astype(f32) * slope).astype(bf16)))

    fed_own = feed(normed2, hidden_grads[0])
    normed2_pieces = gather_pieces(normed2, devices, fed_own)
    fed = [fed_own] + [feed(piece, grad) for piece, grad in zip(normed2_pieces[1:-1], hidden_grads[1:-1])]
    fed.append(feed(after(normed2_pieces[-1], *fed), hidden_grads[-1]))
    hidden = [f[0] for f in fed]
    up_grad = [f[1] for f in fed]
    terms = [dot_nt(piece, w_up) for piece in up_grad]
    normed2_grad, _, _ = scatter_sum(terms)
    mixed_grad = cotangent.astype(f32) + normalize_back(normed2_grad, unit2, scale2, second_gain)
    gain2_grad = jnp.sum(normed2_grad * unit2, axis=0)
    bias2_grad = jnp.sum(normed2_grad, axis=0)
    mixed_low = mixed_grad.astype(bf16)
    mixed_pieces = gather_pieces(mixed_low, devices)

    hidden_all = jnp.concatenate(after(hidden, *terms), axis=0)
    down_weight_grad = dot_tn(hidden_all, cot_all).astype(bf16)
    down_sum = lax.psum_scatter(down_weight_grad, "dp", scatter_dimension=1, tiled=True).astype(f32)
    normed2_all = jnp.concatenate(after(normed2_pieces, mixed_low), axis=0)
    up_weight_grad = dot_tn(normed2_all, jnp.concatenate(up_grad, axis=0)).astype(bf16)
    up_sum = lax.psum_scatter(up_weight_grad, "dp", scatter_dimension=0, tiled=True).astype(f32)
    ffn_terms = per_piece(dot_nn(after(hidden_all, mixed_low), w_down).astype(bf16))

    gated_grad, gate_grad = [], []
    for piece, unit, raw in zip(mixed_pieces, per_piece(grouped), per_piece(gate)):
        grad = dot_nt(after(piece, *ffn_terms), w_out)
        raw = raw.astype(f32)
        sigmoid = 1.0 / (1.0 + jnp.exp(-raw))
        both = after((
            grad.astype(bf16),
            (grad * unit.astype(f32) * (sigmoid * (1.0 + raw * (1.0 - sigmoid)))).astype(bf16),
        ))
        gated_grad.append(both[0])
        gate_grad.append(both[1])
    gate_weight_grad = dot_tn(normed1_all, jnp.concatenate(gate_grad, axis=0)).astype(bf16)
    gate_sum = lax.psum_scatter(gate_weight_grad, "dp", scatter_dimension=0, tiled=True).astype(f32)
    ffn, ffn_begun, ffn_done = scatter_sum([term.astype(f32) for term in after(ffn_terms, mixed_pieces[3])])
    result = (mixed + ffn).astype(bf16)
    out_weight_grad = dot_tn(gated, jnp.concatenate(after(mixed_pieces, gate_weight_grad), axis=0)).astype(bf16)
    out_sum = lax.psum_scatter(out_weight_grad, "dp", scatter_dimension=1, tiled=True).astype(f32)
    back = retention_call(
        True, which, rows, heads, field, gate, tables,
        (jnp.concatenate(after(gated_grad, out_weight_grad, *ffn_begun), axis=0), grouped, group_scale, past),
    )
    terms = [dot_nt(first, w_qkv) + dot_nt(second, w_gate) for first, second in zip(per_piece(back), gate_grad)]
    normed1_grad, begun, _ = scatter_sum(terms)
    qkv_weight_grad = dot_tn(normed1_all, after(back, terms[-1], *ffn_done, up_sum, down_sum)).astype(bf16)
    qkv_sum = lax.psum_scatter(qkv_weight_grad, "dp", scatter_dimension=0, tiled=True)
    input_grad = mixed_grad + normalize_back(normed1_grad, unit1, scale1, first_gain)
    gain1_grad = jnp.sum(normed1_grad * unit1, axis=0)
    bias1_grad = jnp.sum(normed1_grad, axis=0)
    norm_sums = spread_sum([gain1_grad, bias1_grad, gain2_grad, bias2_grad])
    keys_end = heads * KEY
    return (
        result,
        input_grad.astype(bf16),
        norm_sums[0],
        norm_sums[1],
        qkv_sum[:, :keys_end].astype(f32),
        qkv_sum[:, keys_end : 2 * keys_end].astype(f32),
        qkv_sum[:, 2 * keys_end :].astype(f32),
        gate_sum,
        out_sum,
        norm_sums[2],
        norm_sums[3],
        up_sum,
        down_sum,
    )


def solution(mesh):
    rows = P(("dp", "tensor"), None)
    vector = P(("dp", "tensor"))
    into = P("dp", "tensor")
    back = P("tensor", "dp")
    return jax.shard_map(
        body,
        mesh=mesh,
        in_specs=(rows, rows, P("dp"), P(), P(), into, into, into, into, back, P(), P(), into, back),
        out_specs=(rows, rows, vector, vector, into, into, into, into, back, vector, vector, into, back),
        check_vma=False,
    )
```

```python
import functools

import jax
import jax.numpy as jnp
from jax import lax
from jax.experimental import pallas as pl
from jax.experimental.pallas import tpu as pltpu
from jax.sharding import PartitionSpec as P

KEY = 256
VAL = 512
CHUNK = 256
QKV = 2 * KEY + VAL

norm_epsilon = 1e-05
group_floor = 0.5
key_scale = KEY ** (-0.5)

f32 = jnp.float32
bf16 = jnp.bfloat16


def dot_nn(left, right):
    return lax.dot_general(left, right, (((1,), (0,)), ((), ())), preferred_element_type=f32)


def dot_nt(left, right):
    return lax.dot_general(left, right, (((1,), (1,)), ((), ())), preferred_element_type=f32)


def dot_tn(left, right):
    return lax.dot_general(left, right, (((0,), (0,)), ((), ())), preferred_element_type=f32)


def tensor_permute(values, bit):
    pairs = [(i, i ^ bit) for i in range(4)]
    return lax.ppermute(values, "tensor", pairs)


def after(values, *tokens):
    return lax.optimization_barrier((values, tokens))[0]


def gather_pieces(own, devices, between=()):
    if devices != 4:
        whole = lax.all_gather(own, "tensor", axis=0, tiled=True)
        return list(jnp.split(whole, devices, axis=0))
    half = own.shape[0] // 2
    from_x = tensor_permute(own, 1)
    from_y = tensor_permute(own, 2)
    lower, upper = after((from_y[:half], from_x[half:]), *between)
    lower = tensor_permute(lower, 1)
    upper = tensor_permute(upper, 2)
    return [own, from_x, from_y, jnp.concatenate([lower, upper], axis=0)]


def scatter_sum(terms):
    if len(terms) != 4:
        stacked = jnp.concatenate([term.astype(bf16) for term in terms], axis=0)
        return lax.psum_scatter(stacked, "tensor", scatter_dimension=0, tiled=True).astype(f32), (stacked,), (stacked,)
    own, over_x, over_y, across = terms
    half = own.shape[0] // 2
    across = across.astype(bf16)
    first = tensor_permute(across[:half], 1)
    second = tensor_permute(across[half:], 2)
    over_y = jnp.concatenate([over_y[:half] + first.astype(f32), over_y[half:]], axis=0)
    over_x = jnp.concatenate([over_x[:half], over_x[half:] + second.astype(f32)], axis=0)
    by_x = tensor_permute(over_x.astype(bf16), 1)
    by_y = tensor_permute(over_y.astype(bf16), 2)
    return own + by_x.astype(f32) + by_y.astype(f32), (first, second), (by_x, by_y)


def spread_sum_kernel(tensor_devices, devices, given_ref, sum_ref, landed_ref, send_sem, recv_sem):
    here = lax.axis_index("dp") * tensor_devices + lax.axis_index("tensor")

    def partner(k):
        other = lax.rem(here + k, devices)
        return other, (lax.div(other, tensor_devices), lax.rem(other, tensor_devices))

    def copy(k):
        other, device = partner(k)
        return pltpu.make_async_remote_copy(
            src_ref=given_ref.at[other],
            dst_ref=landed_ref.at[k],
            send_sem=send_sem.at[k],
            recv_sem=recv_sem.at[k],
            device_id=device,
            device_id_type=pl.DeviceIdType.MESH,
        )

    barrier = pltpu.get_barrier_semaphore()

    @pl.loop(1, devices)
    def _(k):
        pl.semaphore_signal(barrier, inc=1, device_id=partner(k)[1], device_id_type=pl.DeviceIdType.MESH)

    pl.semaphore_wait(barrier, devices - 1)

    @pl.loop(1, devices)
    def _(k):
        copy(k).start()

    sum_ref[...] = given_ref[here]

    @pl.loop(1, devices)
    def _(k):
        copy(k).wait()
        sum_ref[...] += landed_ref[k]


def spread_sum(vectors):
    dp, tensor = lax.axis_size("dp"), lax.axis_size("tensor")
    devices = dp * tensor
    part = vectors[0].shape[0] // devices
    given = jnp.stack([v.reshape(devices, part) for v in vectors], axis=1)
    given = jnp.pad(given, ((0, 0), (0, 8 - len(vectors)), (0, 128 - part)))
    total = pl.pallas_call(
        functools.partial(spread_sum_kernel, tensor, devices),
        out_shape=jax.ShapeDtypeStruct((8, 128), f32),
        in_specs=[pl.BlockSpec(memory_space=pltpu.VMEM)],
        out_specs=pl.BlockSpec(memory_space=pltpu.VMEM),
        scratch_shapes=[
            pltpu.VMEM((devices, 8, 128), f32),
            pltpu.SemaphoreType.DMA((devices,)),
            pltpu.SemaphoreType.DMA((devices,)),
        ],
        compiler_params=pltpu.CompilerParams(collective_id=1, has_side_effects=True),
        name="spread_sum",
    )(given)
    return [total[i, :part] for i in range(len(vectors))]


def normalize(values):
    average = jnp.mean(values, axis=-1, keepdims=True)
    centred = values - average
    variance = jnp.mean(centred * centred, axis=-1, keepdims=True)
    scale = lax.rsqrt(variance + norm_epsilon)
    return centred * scale, scale


def normalize_back(normed_grad, unit, scale, gain):
    g = normed_grad * gain
    mean_g = jnp.mean(g, axis=-1, keepdims=True)
    mean_gx = jnp.mean(g * unit, axis=-1, keepdims=True)
    return scale * (g - mean_g - unit * mean_gx)


def gelu_both(values):
    inner = 0.7978845608 * (values + 0.044715 * values * values * values)
    t = jnp.tanh(inner)
    slope = 0.7978845608 * (1.0 + 3.0 * 0.044715 * values * values)
    return 0.5 * values * (1.0 + t), 0.5 * (1.0 + t) + 0.5 * values * (1.0 - t * t) * slope


def turn(block, cosine, sine):
    a = block[:, : KEY // 2]
    b = block[:, KEY // 2 :]
    return jnp.concatenate([a * cosine - b * sine, b * cosine + a * sine], axis=1)


def turn_back(block, cosine, sine):
    a = block[:, : KEY // 2]
    b = block[:, KEY // 2 :]
    return jnp.concatenate([a * cosine + b * sine, b * cosine - a * sine], axis=1)


def head_parts(field_ref, angles, heads, head):
    cosine = angles[:, : KEY // 2]
    sine = angles[:, KEY // 2 :]
    query_at = head * KEY
    key_at = (heads + head) * KEY
    value_at = 2 * heads * KEY + head * VAL
    query = turn(field_ref[:, query_at : query_at + KEY].astype(f32), cosine, sine).astype(bf16)
    key = turn(field_ref[:, key_at : key_at + KEY].astype(f32), cosine, sine)
    key = (key * key_scale).astype(bf16)
    return query, key, field_ref[:, value_at : value_at + VAL]


def retention_forward(heads, which, field_ref, gate_ref, angle_ref, info_ref, row_ref, decay_ref, gated_ref, grouped_ref, scale_ref, past_ref, state_ref):
    @pl.when(pl.program_id(0) == 0)
    def _():
        state_ref[...] = jnp.zeros_like(state_ref)

    angles = angle_ref[...]
    info = info_ref[...]
    same = info[:, 0:1] == row_ref[0]
    for head in range(heads):
        query, key, value = head_parts(field_ref, angles, heads, head)
        columns = slice(head * VAL, (head + 1) * VAL)
        gate = gate_ref[:, columns].astype(f32)
        into = info[:, 1 + 2 * head : 2 + 2 * head]
        onward = info[:, 2 + 2 * head : 3 + 2 * head]
        state = state_ref[head]
        past_ref[0, head] = state.astype(bf16)
        scores = dot_nt(query, key)
        weights = (jnp.where(same, decay_ref[head], 0.0) * scores).astype(bf16)
        retained = dot_nn(weights, value) + into * dot_nn(query, state.astype(bf16))
        moved = (key.astype(f32) * onward).astype(bf16)
        state_ref[head] = into[CHUNK - 1 :, :] * state + dot_tn(moved, value)
        centred = retained - jnp.mean(retained, axis=-1, keepdims=True)
        scale = lax.rsqrt(jnp.mean(centred * centred, axis=-1, keepdims=True) + group_floor)
        grouped = centred * scale
        gated = gate / (1.0 + jnp.exp(-gate)) * grouped
        gated_ref[:, columns] = gated.astype(bf16)
        grouped_ref[:, columns] = grouped.astype(bf16)
        scale_ref[:, head * 128 : (head + 1) * 128] = jnp.broadcast_to(scale, (CHUNK, 128))


def retention_backward(heads, which, field_ref, gate_ref, angle_ref, info_ref, row_ref, decay_ref, grad_ref, grouped_ref, scale_ref, past_ref, back_ref, state_ref):
    @pl.when(pl.program_id(0) == 0)
    def _():
        state_ref[...] = jnp.zeros_like(state_ref)

    angles = angle_ref[...]
    cosine = angles[:, : KEY // 2]
    sine = angles[:, KEY // 2 :]
    info = info_ref[...]
    same = info[:, 0:1] == row_ref[0]
    for head in range(heads):
        query, key, value = head_parts(field_ref, angles, heads, head)
        columns = slice(head * VAL, (head + 1) * VAL)
        gate = gate_ref[:, columns].astype(f32)
        into = info[:, 1 + 2 * head : 2 + 2 * head]
        onward = info[:, 2 + 2 * head : 3 + 2 * head]
        grouped = grouped_ref[:, columns].astype(f32)
        scale = scale_ref[:, head * 128 : head * 128 + 1]
        c = grad_ref[:, columns].astype(f32) * (gate / (1.0 + jnp.exp(-gate)))
        mean_c = jnp.mean(c, axis=-1, keepdims=True)
        mean_cx = jnp.mean(c * grouped, axis=-1, keepdims=True)
        out_grad = (scale * (c - mean_c - grouped * mean_cx)).astype(bf16)
        state = state_ref[head]
        state_low = state.astype(bf16)
        past = past_ref[0, head]
        masked = jnp.where(same, decay_ref[head], 0.0)
        weights = (masked * dot_nt(query, key)).astype(bf16)
        score_grad = (masked * dot_nt(out_grad, value)).astype(bf16)
        value_grad = dot_tn(weights, out_grad) + onward * dot_nn(key, state_low)
        query_grad = dot_nn(score_grad, key) + into * dot_nt(out_grad, past)
        key_grad = dot_tn(score_grad, query) + onward * dot_nt(value, state_low)
        moved = (query.astype(f32) * into).astype(bf16)
        state_ref[head] = into[CHUNK - 1 :, :] * state + dot_tn(moved, out_grad)
        query_at = head * KEY
        key_at = (heads + head) * KEY
        value_at = 2 * heads * KEY + head * VAL
        back_ref[:, query_at : query_at + KEY] = turn_back(query_grad, cosine, sine).astype(bf16)
        back_ref[:, key_at : key_at + KEY] = (turn_back(key_grad, cosine, sine) * key_scale).astype(bf16)
        back_ref[:, value_at : value_at + VAL] = value_grad.astype(bf16)


def retention_tables(segment, heads, first_head):
    rows = segment.shape[0]
    chunks = rows // CHUNK
    index = jnp.arange(rows, dtype=jnp.int32)
    boundary = jnp.concatenate([jnp.ones((1,), jnp.int32), (segment[1:] != segment[:-1]).astype(jnp.int32)])
    position = index - lax.cummax(jnp.where(boundary > 0, index, 0), axis=0)
    half = KEY // 2
    frequency = jnp.exp(-jnp.log(10000.0) * jnp.arange(half, dtype=f32) / half)
    angles = position.astype(f32)[:, None] * frequency[None, :]
    angles = jnp.concatenate([jnp.cos(angles), jnp.sin(angles)], axis=1)
    head_ids = (first_head + jnp.arange(heads, dtype=jnp.int32)).astype(f32)
    log_decay = jnp.log1p(-jnp.exp2(-5.0 - head_ids))
    last = segment.reshape(chunks, CHUNK)[:, -1]
    before = jnp.concatenate([jnp.full((1,), -2, jnp.int32), last[:-1]])
    offset = (index % CHUNK).astype(f32)
    linked_in = (segment == jnp.repeat(before, CHUNK)) & (segment >= 0)
    linked_on = (segment == jnp.repeat(last, CHUNK)) & (segment >= 0)
    columns = [segment.astype(f32)]
    for head in range(heads):
        columns.append(jnp.where(linked_in, jnp.exp(log_decay[head] * (offset + 1.0)), 0.0))
        columns.append(jnp.where(linked_on, jnp.exp(log_decay[head] * (CHUNK - 1.0 - offset)), 0.0))
    info = jnp.stack(columns, axis=1)
    info = jnp.pad(info, ((0, 0), (0, 128 - info.shape[1])))
    keys = jnp.where(segment >= 0, segment, -7).astype(f32).reshape(chunks, 1, CHUNK)
    distance = (jnp.arange(CHUNK)[:, None] - jnp.arange(CHUNK)[None, :]).astype(f32)
    decay = jnp.where(distance >= 0, jnp.exp(log_decay[:, None, None] * jnp.maximum(distance, 0.0)), 0.0)
    return angles, info, keys, decay


def retention_call(backward, which, piece_rows, heads, field, gate, tables, extra):
    rows = field.shape[0]
    chunks = rows // CHUNK
    angles, info, keys, decay = tables
    per_piece = piece_rows // CHUNK

    def step(i):
        return chunks - 1 - i if backward else i

    def place(i, which_ref):
        c = step(i)
        return ((c // per_piece) ^ which_ref[0]) * per_piece + c % per_piece

    def placed(width):
        return pl.BlockSpec((CHUNK, width), lambda i, w: (place(i, w), 0))

    in_specs = [
        placed(heads * QKV),
        placed(heads * VAL),
        pl.BlockSpec((CHUNK, KEY), lambda i, w: (step(i), 0)),
        pl.BlockSpec((CHUNK, 128), lambda i, w: (step(i), 0)),
        pl.BlockSpec((1, 1, CHUNK), lambda i, w: (step(i), 0, 0)),
        pl.BlockSpec((heads, CHUNK, CHUNK), lambda i, w: (0, 0, 0)),
    ]
    past_spec = pl.BlockSpec((1, heads, KEY, VAL), lambda i, w: (step(i), 0, 0, 0))
    if backward:
        in_specs += [placed(heads * VAL), placed(heads * VAL), placed(heads * 128), past_spec]
        out_specs = placed(heads * QKV)
        out_shape = jax.ShapeDtypeStruct((rows, heads * QKV), bf16)
    else:
        out_specs = [placed(heads * VAL), placed(heads * VAL), placed(heads * 128), past_spec]
        out_shape = [
            jax.ShapeDtypeStruct((rows, heads * VAL), bf16),
            jax.ShapeDtypeStruct((rows, heads * VAL), bf16),
            jax.ShapeDtypeStruct((rows, heads * 128), f32),
            jax.ShapeDtypeStruct((chunks, heads, KEY, VAL), bf16),
        ]
    products = 15 if backward else 7
    return pl.pallas_call(
        functools.partial(retention_backward if backward else retention_forward, heads),
        grid_spec=pltpu.PrefetchScalarGridSpec(
            num_scalar_prefetch=1,
            grid=(chunks,),
            in_specs=in_specs,
            out_specs=out_specs,
            scratch_shapes=[pltpu.VMEM((heads, KEY, VAL), f32)],
        ),
        out_shape=out_shape,
        compiler_params=pltpu.CompilerParams(
            dimension_semantics=("arbitrary",), vmem_limit_bytes=48 * 1024 * 1024
        ),
        cost_estimate=pl.CostEstimate(
            flops=products * chunks * heads * 2 * CHUNK * CHUNK * CHUNK,
            bytes_accessed=(5 if backward else 4) * rows * heads * (QKV + VAL),
            transcendentals=rows * heads * VAL,
        ),
        name="retention_backward" if backward else "retention_forward",
    )(which, field, gate, angles, info, keys, decay, *extra)


MESH = pl.DeviceIdType.MESH


def opening_kernel(
    query_ref, key_ref, value_ref, gate_ref, token_ref, gain_ref, bias_ref, cot_ref,
    w_qkv_ref, w_gate_ref, normed_ref, cot_all_ref,
    w_qkv, w_gate, normed, token_own, cot_own, cot_got,
    local_sem, out_sem, up_send, up_recv, down_send, down_recv, core_send, core_recv, row_send, row_recv,
):
    dp = lax.axis_index("dp")
    tensor = lax.axis_index("tensor")
    z = lax.div(dp, 2)
    layers = lax.div(lax.axis_size("dp"), 2)
    shard_rows = query_ref.shape[0]
    rows = token_ref.shape[0]
    half = rows // 2
    above = (dp + 2, tensor)
    below = (dp - 2, tensor)
    twin = (dp + 1 - 2 * lax.rem(dp, 2), tensor)
    over_x = (dp, tensor + 1 - 2 * lax.rem(tensor, 2))
    over_y = (dp, lax.rem(tensor + 2, 4))

    keys = query_ref.shape[1]
    values = value_ref.shape[1]
    mine = pl.ds(pl.multiple_of(dp * shard_rows, shard_rows), shard_rows)
    places = [
        (query_ref, w_qkv.at[mine, pl.ds(0, keys)]),
        (key_ref, w_qkv.at[mine, pl.ds(keys, keys)]),
        (value_ref, w_qkv.at[mine, pl.ds(2 * keys, values)]),
        (gate_ref, w_gate.at[mine]),
        (token_ref, token_own),
        (cot_ref.at[pl.ds(0, half)], cot_own),
    ]
    local = [pltpu.make_async_copy(a, b, local_sem.at[i]) for i, (a, b) in enumerate(places)]
    for copy in local:
        copy.start()

    barrier = pltpu.get_barrier_semaphore()

    def greet(device):
        pl.semaphore_signal(barrier, inc=1, device_id=device, device_id_type=MESH)

    for device in (twin, over_x, over_y):
        greet(device)
    pl.when(z < layers - 1)(lambda: greet(above))
    pl.when(z > 0)(lambda: greet(below))
    pl.semaphore_wait(barrier, 3 + (z < layers - 1).astype(jnp.int32) + (z > 0).astype(jnp.int32))
    for copy in local[:4]:
        copy.wait()

    def weight_copies(shard, send_sem, recv_sem, step, device):
        place = pl.ds(pl.multiple_of(shard * shard_rows, shard_rows), shard_rows)
        return [
            pltpu.make_async_remote_copy(
                src_ref=ref.at[place], dst_ref=ref.at[place],
                send_sem=send_sem.at[step, i], recv_sem=recv_sem.at[step, i],
                device_id=device, device_id_type=MESH,
            )
            for i, ref in enumerate((w_qkv, w_gate))
        ]

    def shard_out(shard, slot):
        place = pl.ds(pl.multiple_of(shard * shard_rows, shard_rows), shard_rows)
        return [
            pltpu.make_async_copy(w_qkv.at[place], w_qkv_ref.at[place], out_sem.at[slot, 0]),
            pltpu.make_async_copy(w_gate.at[place], w_gate_ref.at[place], out_sem.at[slot, 1]),
        ]

    def start(copies):
        for copy in copies:
            copy.start()

    def wait_send(copies):
        for copy in copies:
            copy.wait_send()

    def wait_recv(copies):
        for copy in copies:
            copy.wait_recv()

    def up(j):
        return weight_copies(dp - 2 * j, up_send, up_recv, j, above)

    def down(j):
        return weight_copies(dp + 2 * j, down_send, down_recv, j, below)

    def to_twin(j):
        return weight_copies(dp + 2 * j, core_send, core_recv, j + 3, twin)

    def from_twin(j):
        return weight_copies(twin[0] + 2 * j, core_send, core_recv, j + 3, twin)

    def step(j):
        @pl.when(z - j >= 0)
        def _():
            wait_recv(weight_copies(dp - 2 * j, up_send, up_recv, j - 1, twin))
            if j < 3:
                pl.when(z < layers - 1)(lambda: start(up(j)))
            start(to_twin(-j))
            start(shard_out(dp - 2 * j, 3 - j))

        @pl.when(z + j < layers)
        def _():
            wait_recv(weight_copies(dp + 2 * j, down_send, down_recv, j - 1, twin))
            if j < 3:
                pl.when(z > 0)(lambda: start(down(j)))
            start(to_twin(j))
            start(shard_out(dp + 2 * j, 3 + j))

    pl.when(z < layers - 1)(lambda: start(up(0)))
    pl.when(z > 0)(lambda: start(down(0)))
    start(to_twin(0))
    start(shard_out(dp, 3))

    local[4].wait()

    @pl.loop(0, rows // 64)
    def _(i):
        block = pl.ds(pl.multiple_of(i * 64, 64), 64)
        unit, _ = normalize(token_own[block, :].astype(f32))
        normed[block, :] = (unit * gain_ref[...] + bias_ref[...]).astype(bf16)

    def row_copy(index, src, dst, device):
        return pltpu.make_async_remote_copy(
            src_ref=src, dst_ref=dst, send_sem=row_send.at[index], recv_sem=row_recv.at[index],
            device_id=device, device_id_type=MESH,
        )

    local[5].wait()
    over = [
        row_copy(0, normed.at[pl.ds(0, rows)], normed.at[pl.ds(rows, rows)], over_x),
        row_copy(1, normed.at[pl.ds(0, rows)], normed.at[pl.ds(2 * rows, rows)], over_y),
    ]
    start(over)
    step(1)
    wait_recv(over)
    onward = [
        row_copy(2, normed.at[pl.ds(2 * rows, half)], normed.at[pl.ds(3 * rows, half)], over_x),
        row_copy(3, normed.at[pl.ds(rows + half, half)], normed.at[pl.ds(3 * rows + half, half)], over_y),
    ]
    start(onward)
    cots = [
        row_copy(4, cot_own, cot_got.at[0], over_x),
        row_copy(5, cot_own, cot_got.at[1], over_y),
    ]
    start(cots)
    step(2)
    wait_recv(onward)
    normed_out = pltpu.make_async_copy(normed, normed_ref, local_sem.at[6])
    normed_out.start()
    wait_recv(cots)
    cot_out = pltpu.make_async_copy(cot_got, cot_all_ref, local_sem.at[7])
    cot_out.start()
    step(3)

    for j in range(-3, 4):
        @pl.when((z + j >= 0) & (z + j < layers))
        def _():
            wait_recv(from_twin(j))
            start(shard_out(twin[0] + 2 * j, 10 + j))
    wait_send(over + onward + cots)
    for j in range(3):
        pl.when((z < layers - 1) & (z - j >= 0))(lambda: wait_send(up(j)))
        pl.when((z > 0) & (z + j < layers))(lambda: wait_send(down(j)))
    normed_out.wait()
    cot_out.wait()
    for j in range(-3, 4):
        @pl.when((z + j >= 0) & (z + j < layers))
        def _():
            wait_send(to_twin(j))
            for copy in shard_out(dp + 2 * j, 3 + j) + shard_out(twin[0] + 2 * j, 10 + j):
                copy.wait()


def opening_exchange(query_weight, key_weight, value_weight, gate_weight, tokens, gain, bias, cotangent):
    dp = lax.axis_size("dp")
    depth, keys = query_weight.shape
    values = value_weight.shape[1]
    rows, width = tokens.shape
    anywhere = pl.BlockSpec(memory_space=pl.ANY)
    in_vmem = pl.BlockSpec(memory_space=pltpu.VMEM)
    return pl.pallas_call(
        opening_kernel,
        out_shape=[
            jax.ShapeDtypeStruct((dp * depth, 2 * keys + values), bf16),
            jax.ShapeDtypeStruct((dp * depth, values), bf16),
            jax.ShapeDtypeStruct((4 * rows, width), bf16),
            jax.ShapeDtypeStruct((2, rows // 2, width), bf16),
        ],
        in_specs=[anywhere] * 5 + [in_vmem] * 2 + [anywhere],
        out_specs=[anywhere] * 4,
        scratch_shapes=[
            pltpu.VMEM((dp * depth, 2 * keys + values), bf16),
            pltpu.VMEM((dp * depth, values), bf16),
            pltpu.VMEM((4 * rows, width), bf16),
            pltpu.VMEM((rows, width), bf16),
            pltpu.VMEM((rows // 2, width), bf16),
            pltpu.VMEM((2, rows // 2, width), bf16),
            pltpu.SemaphoreType.DMA((8,)),
            pltpu.SemaphoreType.DMA((14, 2)),
            pltpu.SemaphoreType.DMA((3, 2)),
            pltpu.SemaphoreType.DMA((3, 2)),
            pltpu.SemaphoreType.DMA((3, 2)),
            pltpu.SemaphoreType.DMA((3, 2)),
            pltpu.SemaphoreType.DMA((7, 2)),
            pltpu.SemaphoreType.DMA((7, 2)),
            pltpu.SemaphoreType.DMA((6,)),
            pltpu.SemaphoreType.DMA((6,)),
        ],
        compiler_params=pltpu.CompilerParams(
            collective_id=2, has_side_effects=True, vmem_limit_bytes=60 * 1024 * 1024
        ),
        name="opening_exchange",
    )(query_weight, key_weight, value_weight, gate_weight, tokens, gain.reshape(1, width), bias.reshape(1, width), cotangent)


def opening(query_weight, key_weight, value_weight, gate_weight, tokens, gain, bias, cotangent, devices):
    if devices == 4 and lax.axis_size("dp") == 8:
        w_qkv, w_gate, normed1_all, cot_half = opening_exchange(
            query_weight, key_weight, value_weight, gate_weight, tokens, gain, bias, cotangent
        )
        half = tokens.shape[0] // 2
        rest = after(cotangent, cot_half)[half:]
        rest_x = tensor_permute(rest, 1)
        rest_y = tensor_permute(rest, 2)
        lower = tensor_permute(cot_half[1], 1)
        upper = tensor_permute(rest_x, 2)
        cots = [cotangent, cot_half[0], rest_x, cot_half[1], rest_y, lower, upper]
        return w_qkv, w_gate, normed1_all, cots, (rest_x, rest_y)
    w_qkv = lax.all_gather(jnp.concatenate([query_weight, key_weight, value_weight], axis=1), "dp", axis=0, tiled=True)
    w_gate = lax.all_gather(gate_weight, "dp", axis=0, tiled=True)
    unit, _ = normalize(tokens.astype(f32))
    normed1_all = jnp.concatenate(gather_pieces((unit * gain + bias).astype(bf16), devices), axis=0)
    cots = gather_pieces(cotangent, devices)
    return w_qkv, w_gate, normed1_all, cots, (cots[0],)


def closing_kernel(
    heads, normed_ref, back_ref, weight_ref, gate_terms_ref, token_ref, mixed_ref, gain_ref, late_ref,
    grad_ref, query_out, key_out, value_out, sums_ref,
    back, weight, terms, columns, half_in, full_in, products, twin_in, line_in, token_own, mixed_own,
    given, landed, total,
    load_sem, column_sem, out_sem, half_send, half_recv, full_send, full_recv, twin_send, twin_recv,
    line_send, line_recv, sum_send, sum_recv,
):
    dp = lax.axis_index("dp")
    tensor = lax.axis_index("tensor")
    z = lax.div(dp, 2)
    core = lax.rem(dp, 2)
    rows = token_ref.shape[0]
    half = rows // 2
    depth = columns.shape[2] // 2
    width = terms.shape[1]
    at_end = (z == 0) | (z == 3)
    upper = z >= 2
    twin = (dp + 1 - 2 * core, tensor)
    over_x = (dp, tensor + 1 - 2 * lax.rem(tensor, 2))
    over_y = (dp, lax.rem(tensor + 2, 4))
    here = dp * 4 + tensor
    peers = 32

    def layer(index):
        return (2 * index + core, tensor)

    def seen(index):
        return jnp.where(upper, 3 - index, index)

    end = layer(seen(0))
    near = layer(seen(1))
    opposite = layer(seen(2))
    targets = [seen(3), seen(2), jnp.where(at_end, seen(1), seen(0)), z]

    def column_copy(k):
        place = pl.ds(pl.multiple_of(targets[k] * 2 * depth, 2 * depth), 2 * depth)
        return pltpu.make_async_copy(normed_ref.at[:, place], columns.at[k % 2], column_sem.at[k])

    loads = [
        pltpu.make_async_copy(src, dst, load_sem.at[i])
        for i, (src, dst) in enumerate(
            ((back_ref, back), (weight_ref, weight), (gate_terms_ref, terms), (token_ref, token_own), (mixed_ref, mixed_own))
        )
    ]
    column_copy(0).start()
    loads[0].start()
    column_copy(1).start()
    for copy in loads[1:]:
        copy.start()

    barrier = pltpu.get_barrier_semaphore()

    def partner(k):
        other = lax.rem(here + k, peers)
        return other, (lax.div(other, 4), lax.rem(other, 4))

    @pl.loop(1, peers)
    def _(k):
        pl.semaphore_signal(barrier, inc=1, device_id=partner(k)[1], device_id_type=MESH)

    pl.semaphore_wait(barrier, peers - 1)

    def remote(src, dst, send, recv, device):
        return pltpu.make_async_remote_copy(
            src_ref=src, dst_ref=dst, send_sem=send, recv_sem=recv, device_id=device, device_id_type=MESH
        )

    mine = pl.ds(pl.multiple_of(core * depth, depth), depth)
    theirs = pl.ds(pl.multiple_of((1 - core) * depth, depth), depth)

    def to_twin(k):
        return remote(products.at[k, theirs], twin_in.at[k], twin_send.at[k], twin_recv.at[k], twin)

    def multiply(k):
        column_copy(k).wait()

        @pl.loop(0, width // 512)
        def _(j):
            tile = pl.ds(pl.multiple_of(j * 512, 512), 512)
            products[k, :, tile] = dot_tn(columns[k % 2], back[:, tile]).astype(bf16)

        if k + 2 < 4:
            column_copy(k + 2).start()
        to_twin(k).start()

    def merge(k, *arrived):
        @pl.loop(0, depth // 64)
        def _(i):
            block = pl.ds(pl.multiple_of(i * 64, 64), 64)
            inner = pl.ds(pl.multiple_of(core * depth + i * 64, 64), 64)
            value = products[k, inner].astype(f32) + twin_in[k, block].astype(f32)
            for slot in arrived:
                value = value + line_in[slot, block].astype(f32)
            products[k, inner] = value.astype(bf16)

    def along(k, slot, device):
        return remote(products.at[k, mine], line_in.at[slot], line_send.at[k], line_recv.at[slot], device)

    def line_wait(slot):
        along(0, slot, end).wait_recv()

    def rows_of(r, start=0, count=rows):
        return pl.ds(r * rows + start, count)

    def project(r):
        @pl.loop(0, width // 256)
        def _(j):
            tile = pl.ds(pl.multiple_of(j * 256, 256), 256)
            grown = terms[rows_of(r), tile].astype(f32) + dot_nt(back[rows_of(r), :], weight[tile, :])
            terms[rows_of(r), tile] = grown.astype(bf16)

    halves = [
        remote(terms.at[rows_of(3, 0, half)], half_in.at[0], half_send.at[0], half_recv.at[0], over_x),
        remote(terms.at[rows_of(3, half, half)], half_in.at[1], half_send.at[1], half_recv.at[1], over_y),
    ]
    fulls = [
        remote(terms.at[rows_of(1)], full_in.at[0], full_send.at[0], full_recv.at[0], over_x),
        remote(terms.at[rows_of(2)], full_in.at[1], full_send.at[1], full_recv.at[1], over_y),
    ]

    def add_half(r, start, slot):
        @pl.loop(0, half // 64)
        def _(i):
            block = pl.ds(pl.multiple_of(i * 64, 64), 64)
            place = pl.ds(pl.multiple_of(r * rows + start + i * 64, 64), 64)
            terms[place, :] = (terms[place, :].astype(f32) + half_in[slot, block].astype(f32)).astype(bf16)

    loads[0].wait()
    multiply(0)
    loads[1].wait()
    loads[2].wait()
    project(3)
    for copy in halves:
        copy.start()
    multiply(1)
    to_twin(0).wait_recv()

    @pl.when(at_end)
    def _():
        merge(0)
        along(0, 0, near).start()

    project(1)
    project(2)
    to_twin(1).wait_recv()

    @pl.when(at_end)
    def _():
        merge(1)
        along(1, 1, near).start()

    for copy in halves:
        copy.wait_recv()
    add_half(2, 0, 0)
    add_half(1, half, 1)
    for copy in fulls:
        copy.start()
    multiply(2)
    to_twin(2).wait_recv()

    @pl.when(at_end)
    def _():
        merge(2)
        along(2, 2, near).start()

    @pl.when(jnp.logical_not(at_end))
    def _():
        line_wait(0)
        merge(0, 0)
        along(0, 3, opposite).start()

    multiply(3)
    project(0)
    to_twin(3).wait_recv()

    @pl.when(jnp.logical_not(at_end))
    def _():
        line_wait(1)
        merge(1, 1)
        along(1, 4, opposite).start()
        line_wait(3)
        merge(2, 3)
        along(2, 0, end).start()

    loads[3].wait()
    loads[4].wait()
    for copy in fulls:
        copy.wait_recv()
    total[...] = jnp.zeros_like(total)

    @pl.loop(0, rows // 64)
    def _(i):
        block = pl.ds(pl.multiple_of(i * 64, 64), 64)
        normed_grad = terms[block, :].astype(f32) + full_in[0, block].astype(f32) + full_in[1, block].astype(f32)
        unit, scale = normalize(token_own[block, :].astype(f32))
        grad = mixed_own[block, :] + normalize_back(normed_grad, unit, scale, gain_ref[...])
        full_in[0, block] = grad.astype(bf16)
        total[0:1, :] += jnp.sum(normed_grad * unit, axis=0, keepdims=True)
        total[1:2, :] += jnp.sum(normed_grad, axis=0, keepdims=True)

    grad_out = pltpu.make_async_copy(full_in.at[0], grad_ref, out_sem.at[0])
    grad_out.start()

    total[2:4, :] = late_ref[...]
    for k in range(peers // 2):
        given[k] = total[:, k * 128 : (k + 1) * 128]

    def sum_copy(k):
        other, device = partner(k)
        return remote(given.at[lax.div(other, 2)], landed.at[k], sum_send.at[k], sum_recv.at[k], device)

    @pl.loop(1, peers)
    def _(k):
        sum_copy(k).start()

    @pl.when(at_end)
    def _():
        line_wait(0)
        merge(3, 0)

    @pl.when(jnp.logical_not(at_end))
    def _():
        line_wait(2)
        line_wait(4)
        merge(3, 2, 4)

    @pl.loop(0, depth // 64)
    def _(i):
        block = pl.ds(pl.multiple_of(i * 64, 64), 64)
        inner = pl.ds(pl.multiple_of(core * depth + i * 64, 64), 64)
        mixed_own[block, :] = products[3, inner].astype(f32)

    keys = heads * KEY
    values = heads * VAL
    outs = [
        pltpu.make_async_copy(mixed_own.at[pl.ds(0, depth), pl.ds(0, keys)], query_out, out_sem.at[1]),
        pltpu.make_async_copy(mixed_own.at[pl.ds(0, depth), pl.ds(keys, keys)], key_out, out_sem.at[2]),
        pltpu.make_async_copy(mixed_own.at[pl.ds(0, depth), pl.ds(2 * keys, values)], value_out, out_sem.at[3]),
    ]
    for copy in outs:
        copy.start()
    sums_ref[...] = given[lax.div(here, 2)]

    @pl.loop(1, peers)
    def _(k):
        sum_copy(k).wait()
        sums_ref[...] += landed[k]

    for copy in halves + fulls:
        copy.wait_send()
    for k in range(4):
        to_twin(k).wait_send()
    for k in range(3):
        along(k, k, near).wait_send()
    grad_out.wait()
    for copy in outs:
        copy.wait()


def closing_exchange(heads, normed, back, weight, gate_terms, tokens, mixed_grad, gain, late):
    rows, width = tokens.shape
    depth = width // 8
    keys, values = heads * KEY, heads * VAL
    anywhere = pl.BlockSpec(memory_space=pl.ANY)
    in_vmem = pl.BlockSpec(memory_space=pltpu.VMEM)
    sem = pltpu.SemaphoreType.DMA
    grad, query, key, value, sums = pl.pallas_call(
        functools.partial(closing_kernel, heads),
        out_shape=[
            jax.ShapeDtypeStruct((rows, width), bf16),
            jax.ShapeDtypeStruct((depth, keys), f32),
            jax.ShapeDtypeStruct((depth, keys), f32),
            jax.ShapeDtypeStruct((depth, values), f32),
            jax.ShapeDtypeStruct((8, 128), f32),
        ],
        in_specs=[anywhere] * 6 + [in_vmem] * 2,
        out_specs=[anywhere] * 4 + [in_vmem],
        scratch_shapes=[
            pltpu.VMEM((4 * rows, width), bf16),
            pltpu.VMEM((width, width), bf16),
            pltpu.VMEM((4 * rows, width), bf16),
            pltpu.VMEM((2, 4 * rows, 2 * depth), bf16),
            pltpu.VMEM((2, rows // 2, width), bf16),
            pltpu.VMEM((2, rows, width), bf16),
            pltpu.VMEM((4, 2 * depth, width), bf16),
            pltpu.VMEM((4, depth, width), bf16),
            pltpu.VMEM((5, depth, width), bf16),
            pltpu.VMEM((rows, width), bf16),
            pltpu.VMEM((rows, width), f32),
            pltpu.VMEM((16, 8, 128), f32),
            pltpu.VMEM((32, 8, 128), f32),
            pltpu.VMEM((8, width), f32),
            sem((5,)), sem((4,)), sem((4,)),
            sem((2,)), sem((2,)), sem((2,)), sem((2,)),
            sem((4,)), sem((4,)), sem((3,)), sem((5,)),
            sem((32,)), sem((32,)),
        ],
        compiler_params=pltpu.CompilerParams(
            collective_id=3, has_side_effects=True, vmem_limit_bytes=60 * 1024 * 1024
        ),
        name="closing_exchange",
    )(normed, back, weight, gate_terms, tokens, mixed_grad, gain.reshape(1, width), late)
    return grad, query, key, value, sums


def body(tokens, cotangent, segment, first_gain, first_bias, query_weight, key_weight, value_weight, gate_weight, out_weight, second_gain, second_bias, up_weight, down_weight):
    devices = lax.axis_size("tensor")
    rows = tokens.shape[0]
    heads = query_weight.shape[1] // KEY
    here = lax.axis_index("tensor")
    which = (here if devices == 4 else jnp.zeros_like(here)).astype(jnp.int32).reshape(1)

    def per_piece(values):
        return [values[i * rows : (i + 1) * rows] for i in range(devices)]

    w_qkv, w_gate, normed1_all, cots, cot_begun = opening(
        query_weight, key_weight, value_weight, gate_weight, tokens, first_gain, first_bias, cotangent, devices
    )
    w_out = lax.all_gather(after(out_weight, w_gate), "dp", axis=1, tiled=True)
    w_down = lax.all_gather(after(down_weight, w_out), "dp", axis=1, tiled=True)
    w_up = lax.all_gather(after(up_weight, w_down), "dp", axis=0, tiled=True)

    token_rows = tokens.astype(f32)
    tables = retention_tables(segment, heads, here * heads)
    field = dot_nn(normed1_all, w_qkv).astype(bf16)
    gate = dot_nn(normed1_all, w_gate).astype(bf16)
    gated, grouped, group_scale, past = retention_call(
        False, which, rows, heads, field, after(gate, *cot_begun), tables, ()
    )
    branch, begun, _ = scatter_sum([dot_nn(piece, w_out) for piece in per_piece(after(gated, *cots))])

    mixed = token_rows + branch
    unit2, scale2 = normalize(mixed)
    normed2 = (unit2 * second_gain + second_bias).astype(bf16)
    cot_all = jnp.concatenate(after(cots, *begun), axis=0)
    hidden_grads = per_piece(dot_nt(cot_all, after(w_down, normed2)).astype(bf16))

    def feed(piece, hidden_grad):
        value, slope = gelu_both(dot_nn(piece, w_up))
        return after((value.astype(bf16), (hidden_grad.astype(f32) * slope).astype(bf16)))

    fed_own = feed(normed2, hidden_grads[0])
    normed2_pieces = gather_pieces(normed2, devices, fed_own)
    fed = [fed_own] + [feed(piece, grad) for piece, grad in zip(normed2_pieces[1:-1], hidden_grads[1:-1])]
    fed.append(feed(after(normed2_pieces[-1], *fed), hidden_grads[-1]))
    hidden = [f[0] for f in fed]
    up_grad = [f[1] for f in fed]
    terms = [dot_nt(piece, w_up) for piece in up_grad]
    normed2_grad, _, _ = scatter_sum(terms)
    mixed_grad = cotangent.astype(f32) + normalize_back(normed2_grad, unit2, scale2, second_gain)
    gain2_grad = jnp.sum(normed2_grad * unit2, axis=0)
    bias2_grad = jnp.sum(normed2_grad, axis=0)
    mixed_low = mixed_grad.astype(bf16)
    mixed_pieces = gather_pieces(mixed_low, devices)

    hidden_all = jnp.concatenate(after(hidden, *terms), axis=0)
    down_weight_grad = dot_tn(hidden_all, cot_all).astype(bf16)
    down_sum = lax.psum_scatter(down_weight_grad, "dp", scatter_dimension=1, tiled=True).astype(f32)
    normed2_all = jnp.concatenate(after(normed2_pieces, mixed_low), axis=0)
    up_weight_grad = dot_tn(normed2_all, jnp.concatenate(up_grad, axis=0)).astype(bf16)
    up_sum = lax.psum_scatter(up_weight_grad, "dp", scatter_dimension=0, tiled=True).astype(f32)
    ffn_terms = per_piece(dot_nn(after(hidden_all, mixed_low), w_down).astype(bf16))

    gated_grad, gate_grad = [], []
    for piece, unit, raw in zip(mixed_pieces, per_piece(grouped), per_piece(gate)):
        grad = dot_nt(after(piece, *ffn_terms), w_out)
        raw = raw.astype(f32)
        sigmoid = 1.0 / (1.0 + jnp.exp(-raw))
        both = after((
            grad.astype(bf16),
            (grad * unit.astype(f32) * (sigmoid * (1.0 + raw * (1.0 - sigmoid)))).astype(bf16),
        ))
        gated_grad.append(both[0])
        gate_grad.append(both[1])
    gate_grad_all = jnp.concatenate(gate_grad, axis=0)
    gate_weight_grad = dot_tn(normed1_all, gate_grad_all).astype(bf16)
    gate_sum = lax.psum_scatter(gate_weight_grad, "dp", scatter_dimension=0, tiled=True).astype(f32)
    ffn, ffn_begun, ffn_done = scatter_sum([term.astype(f32) for term in after(ffn_terms, mixed_pieces[3])])
    result = (mixed + ffn).astype(bf16)
    out_weight_grad = dot_tn(gated, jnp.concatenate(after(mixed_pieces, gate_weight_grad), axis=0)).astype(bf16)
    out_sum = lax.psum_scatter(out_weight_grad, "dp", scatter_dimension=1, tiled=True).astype(f32)
    back = retention_call(
        True, which, rows, heads, field, gate, tables,
        (jnp.concatenate(after(gated_grad, out_weight_grad, *ffn_begun), axis=0), grouped, group_scale, past),
    )
    keys_end = heads * KEY
    if devices == 4 and lax.axis_size("dp") == 8:
        gate_terms = dot_nt(gate_grad_all, w_gate).astype(bf16)
        input_grad, query_sum, key_sum, value_sum, sums = closing_exchange(
            heads, normed1_all, back, w_qkv, after(gate_terms, *ffn_done, up_sum, down_sum), tokens, mixed_grad, first_gain,
            jnp.stack([gain2_grad, bias2_grad]),
        )
        part = first_gain.shape[0] // 32
        sums = lax.dynamic_slice_in_dim(sums, (here % 2) * part, part, 1)
        norm_sums = [sums[0], sums[1], sums[2], sums[3]]
    else:
        terms = [dot_nt(first, w_qkv) + dot_nt(second, w_gate) for first, second in zip(per_piece(back), gate_grad)]
        normed1_grad, _, _ = scatter_sum(terms)
        qkv_weight_grad = dot_tn(normed1_all, back).astype(bf16)
        qkv_sum = lax.psum_scatter(qkv_weight_grad, "dp", scatter_dimension=0, tiled=True).astype(f32)
        query_sum = qkv_sum[:, :keys_end]
        key_sum = qkv_sum[:, keys_end : 2 * keys_end]
        value_sum = qkv_sum[:, 2 * keys_end :]
        unit1, scale1 = normalize(token_rows)
        input_grad = (mixed_grad + normalize_back(normed1_grad, unit1, scale1, first_gain)).astype(bf16)
        gain1_grad = jnp.sum(normed1_grad * unit1, axis=0)
        bias1_grad = jnp.sum(normed1_grad, axis=0)
        norm_sums = spread_sum([gain1_grad, bias1_grad, gain2_grad, bias2_grad])
    return (
        result,
        input_grad,
        norm_sums[0],
        norm_sums[1],
        query_sum,
        key_sum,
        value_sum,
        gate_sum,
        out_sum,
        norm_sums[2],
        norm_sums[3],
        up_sum,
        down_sum,
    )


def solution(mesh):
    rows = P(("dp", "tensor"), None)
    vector = P(("dp", "tensor"))
    into = P("dp", "tensor")
    back = P("tensor", "dp")
    return jax.shard_map(
        body,
        mesh=mesh,
        in_specs=(rows, rows, P("dp"), P(), P(), into, into, into, into, back, P(), P(), into, back),
        out_specs=(rows, rows, vector, vector, into, into, into, into, back, vector, vector, into, back),
        check_vma=False,
    )
```

```python
import functools

import jax
import jax.numpy as jnp
from jax import lax
from jax.experimental import pallas as pl
from jax.experimental.pallas import tpu as pltpu
from jax.sharding import PartitionSpec as P

KEY = 256
VAL = 512
CHUNK = 256
QKV = 2 * KEY + VAL

norm_epsilon = 1e-05
group_floor = 0.5
key_scale = KEY ** (-0.5)

f32 = jnp.float32
bf16 = jnp.bfloat16


def dot_nn(left, right):
    return lax.dot_general(left, right, (((1,), (0,)), ((), ())), preferred_element_type=f32)


def dot_nt(left, right):
    return lax.dot_general(left, right, (((1,), (1,)), ((), ())), preferred_element_type=f32)


def dot_tn(left, right):
    return lax.dot_general(left, right, (((0,), (0,)), ((), ())), preferred_element_type=f32)


def tensor_permute(values, bit):
    pairs = [(i, i ^ bit) for i in range(4)]
    return lax.ppermute(values, "tensor", pairs)


def after(values, *tokens):
    return lax.optimization_barrier((values, tokens))[0]


def gather_pieces(own, devices, between=()):
    if devices != 4:
        whole = lax.all_gather(own, "tensor", axis=0, tiled=True)
        return list(jnp.split(whole, devices, axis=0))
    half = own.shape[0] // 2
    from_x = tensor_permute(own, 1)
    from_y = tensor_permute(own, 2)
    lower, upper = after((from_y[:half], from_x[half:]), *between)
    lower = tensor_permute(lower, 1)
    upper = tensor_permute(upper, 2)
    return [own, from_x, from_y, jnp.concatenate([lower, upper], axis=0)]


def scatter_sum(terms):
    if len(terms) != 4:
        stacked = jnp.concatenate([term.astype(bf16) for term in terms], axis=0)
        return lax.psum_scatter(stacked, "tensor", scatter_dimension=0, tiled=True).astype(f32), (stacked,), (stacked,)
    own, over_x, over_y, across = terms
    half = own.shape[0] // 2
    across = across.astype(bf16)
    first = tensor_permute(across[:half], 1)
    second = tensor_permute(across[half:], 2)
    over_y = jnp.concatenate([over_y[:half] + first.astype(f32), over_y[half:]], axis=0)
    over_x = jnp.concatenate([over_x[:half], over_x[half:] + second.astype(f32)], axis=0)
    by_x = tensor_permute(over_x.astype(bf16), 1)
    by_y = tensor_permute(over_y.astype(bf16), 2)
    return own + by_x.astype(f32) + by_y.astype(f32), (first, second), (by_x, by_y)


def spread_sum_kernel(tensor_devices, devices, given_ref, sum_ref, landed_ref, send_sem, recv_sem):
    here = lax.axis_index("dp") * tensor_devices + lax.axis_index("tensor")

    def partner(k):
        other = lax.rem(here + k, devices)
        return other, (lax.div(other, tensor_devices), lax.rem(other, tensor_devices))

    def copy(k):
        other, device = partner(k)
        return pltpu.make_async_remote_copy(
            src_ref=given_ref.at[other],
            dst_ref=landed_ref.at[k],
            send_sem=send_sem.at[k],
            recv_sem=recv_sem.at[k],
            device_id=device,
            device_id_type=pl.DeviceIdType.MESH,
        )

    barrier = pltpu.get_barrier_semaphore()

    @pl.loop(1, devices)
    def _(k):
        pl.semaphore_signal(barrier, inc=1, device_id=partner(k)[1], device_id_type=pl.DeviceIdType.MESH)

    pl.semaphore_wait(barrier, devices - 1)

    @pl.loop(1, devices)
    def _(k):
        copy(k).start()

    sum_ref[...] = given_ref[here]

    @pl.loop(1, devices)
    def _(k):
        copy(k).wait()
        sum_ref[...] += landed_ref[k]


def spread_sum(vectors):
    dp, tensor = lax.axis_size("dp"), lax.axis_size("tensor")
    devices = dp * tensor
    part = vectors[0].shape[0] // devices
    given = jnp.stack([v.reshape(devices, part) for v in vectors], axis=1)
    given = jnp.pad(given, ((0, 0), (0, 8 - len(vectors)), (0, 128 - part)))
    total = pl.pallas_call(
        functools.partial(spread_sum_kernel, tensor, devices),
        out_shape=jax.ShapeDtypeStruct((8, 128), f32),
        in_specs=[pl.BlockSpec(memory_space=pltpu.VMEM)],
        out_specs=pl.BlockSpec(memory_space=pltpu.VMEM),
        scratch_shapes=[
            pltpu.VMEM((devices, 8, 128), f32),
            pltpu.SemaphoreType.DMA((devices,)),
            pltpu.SemaphoreType.DMA((devices,)),
        ],
        compiler_params=pltpu.CompilerParams(collective_id=1, has_side_effects=True),
        name="spread_sum",
    )(given)
    return [total[i, :part] for i in range(len(vectors))]


def normalize(values):
    average = jnp.mean(values, axis=-1, keepdims=True)
    centred = values - average
    variance = jnp.mean(centred * centred, axis=-1, keepdims=True)
    scale = lax.rsqrt(variance + norm_epsilon)
    return centred * scale, scale


def normalize_back(normed_grad, unit, scale, gain):
    g = normed_grad * gain
    mean_g = jnp.mean(g, axis=-1, keepdims=True)
    mean_gx = jnp.mean(g * unit, axis=-1, keepdims=True)
    return scale * (g - mean_g - unit * mean_gx)


def gelu_both(values):
    inner = 0.7978845608 * (values + 0.044715 * values * values * values)
    t = jnp.tanh(inner)
    slope = 0.7978845608 * (1.0 + 3.0 * 0.044715 * values * values)
    return 0.5 * values * (1.0 + t), 0.5 * (1.0 + t) + 0.5 * values * (1.0 - t * t) * slope


def turn(block, cosine, sine):
    a = block[:, : KEY // 2]
    b = block[:, KEY // 2 :]
    return jnp.concatenate([a * cosine - b * sine, b * cosine + a * sine], axis=1)


def turn_back(block, cosine, sine):
    a = block[:, : KEY // 2]
    b = block[:, KEY // 2 :]
    return jnp.concatenate([a * cosine + b * sine, b * cosine - a * sine], axis=1)


def head_parts(field_ref, angles, heads, head):
    cosine = angles[:, : KEY // 2]
    sine = angles[:, KEY // 2 :]
    query_at = head * KEY
    key_at = (heads + head) * KEY
    value_at = 2 * heads * KEY + head * VAL
    query = turn(field_ref[:, query_at : query_at + KEY].astype(f32), cosine, sine).astype(bf16)
    key = turn(field_ref[:, key_at : key_at + KEY].astype(f32), cosine, sine)
    key = (key * key_scale).astype(bf16)
    return query, key, field_ref[:, value_at : value_at + VAL]


def retention_forward(heads, which, field_ref, gate_ref, angle_ref, info_ref, row_ref, decay_ref, gated_ref, grouped_ref, scale_ref, past_ref, state_ref):
    @pl.when(pl.program_id(0) == 0)
    def _():
        state_ref[...] = jnp.zeros_like(state_ref)

    angles = angle_ref[...]
    info = info_ref[...]
    same = info[:, 0:1] == row_ref[0]
    scales = []
    for head in range(heads):
        query, key, value = head_parts(field_ref, angles, heads, head)
        columns = slice(head * VAL, (head + 1) * VAL)
        gate = gate_ref[:, columns].astype(f32)
        into = info[:, 1 + 2 * head : 2 + 2 * head]
        onward = info[:, 2 + 2 * head : 3 + 2 * head]
        state = state_ref[head]
        past_ref[0, head] = state.astype(bf16)
        scores = dot_nt(query, key)
        weights = (jnp.where(same, decay_ref[head], 0.0) * scores).astype(bf16)
        retained = dot_nn(weights, value) + into * dot_nn(query, state.astype(bf16))
        moved = (key.astype(f32) * onward).astype(bf16)
        state_ref[head] = into[CHUNK - 1 :, :] * state + dot_tn(moved, value)
        centred = retained - jnp.mean(retained, axis=-1, keepdims=True)
        scale = lax.rsqrt(jnp.mean(centred * centred, axis=-1, keepdims=True) + group_floor)
        grouped = centred * scale
        gated = gate / (1.0 + jnp.exp(-gate)) * grouped
        gated_ref[:, columns] = gated.astype(bf16)
        grouped_ref[:, columns] = grouped.astype(bf16)
        scales.append(scale)
    lane = lax.broadcasted_iota(jnp.int32, (CHUNK, 128), 1)
    spread = jnp.zeros((CHUNK, 128), f32)
    for head in range(heads):
        spread = jnp.where(lane == head, scales[head], spread)
    scale_ref[...] = spread


def retention_backward(heads, which, field_ref, gate_ref, angle_ref, info_ref, row_ref, decay_ref, grad_ref, grouped_ref, scale_ref, past_ref, back_ref, state_ref):
    @pl.when(pl.program_id(0) == 0)
    def _():
        state_ref[...] = jnp.zeros_like(state_ref)

    angles = angle_ref[...]
    cosine = angles[:, : KEY // 2]
    sine = angles[:, KEY // 2 :]
    info = info_ref[...]
    same = info[:, 0:1] == row_ref[0]
    for head in range(heads):
        query, key, value = head_parts(field_ref, angles, heads, head)
        columns = slice(head * VAL, (head + 1) * VAL)
        gate = gate_ref[:, columns].astype(f32)
        into = info[:, 1 + 2 * head : 2 + 2 * head]
        onward = info[:, 2 + 2 * head : 3 + 2 * head]
        grouped = grouped_ref[:, columns].astype(f32)
        scale = scale_ref[:, head : head + 1]
        c = grad_ref[:, columns].astype(f32) * (gate / (1.0 + jnp.exp(-gate)))
        mean_c = jnp.mean(c, axis=-1, keepdims=True)
        mean_cx = jnp.mean(c * grouped, axis=-1, keepdims=True)
        out_grad = (scale * (c - mean_c - grouped * mean_cx)).astype(bf16)
        state = state_ref[head]
        state_low = state.astype(bf16)
        past = past_ref[0, head]
        masked = jnp.where(same, decay_ref[head], 0.0)
        weights = (masked * dot_nt(query, key)).astype(bf16)
        score_grad = (masked * dot_nt(out_grad, value)).astype(bf16)
        value_grad = dot_tn(weights, out_grad) + onward * dot_nn(key, state_low)
        query_grad = dot_nn(score_grad, key) + into * dot_nt(out_grad, past)
        key_grad = dot_tn(score_grad, query) + onward * dot_nt(value, state_low)
        moved = (query.astype(f32) * into).astype(bf16)
        state_ref[head] = into[CHUNK - 1 :, :] * state + dot_tn(moved, out_grad)
        query_at = head * KEY
        key_at = (heads + head) * KEY
        value_at = 2 * heads * KEY + head * VAL
        back_ref[:, query_at : query_at + KEY] = turn_back(query_grad, cosine, sine).astype(bf16)
        back_ref[:, key_at : key_at + KEY] = (turn_back(key_grad, cosine, sine) * key_scale).astype(bf16)
        back_ref[:, value_at : value_at + VAL] = value_grad.astype(bf16)


def retention_tables(segment, heads, first_head):
    rows = segment.shape[0]
    chunks = rows // CHUNK
    index = jnp.arange(rows, dtype=jnp.int32)
    boundary = jnp.concatenate([jnp.ones((1,), jnp.int32), (segment[1:] != segment[:-1]).astype(jnp.int32)])
    position = index - lax.cummax(jnp.where(boundary > 0, index, 0), axis=0)
    half = KEY // 2
    frequency = jnp.exp(-jnp.log(10000.0) * jnp.arange(half, dtype=f32) / half)
    angles = position.astype(f32)[:, None] * frequency[None, :]
    angles = jnp.concatenate([jnp.cos(angles), jnp.sin(angles)], axis=1)
    head_ids = (first_head + jnp.arange(heads, dtype=jnp.int32)).astype(f32)
    log_decay = jnp.log1p(-jnp.exp2(-5.0 - head_ids))
    last = segment.reshape(chunks, CHUNK)[:, -1]
    before = jnp.concatenate([jnp.full((1,), -2, jnp.int32), last[:-1]])
    offset = (index % CHUNK).astype(f32)
    linked_in = (segment == jnp.repeat(before, CHUNK)) & (segment >= 0)
    linked_on = (segment == jnp.repeat(last, CHUNK)) & (segment >= 0)
    columns = [segment.astype(f32)]
    for head in range(heads):
        columns.append(jnp.where(linked_in, jnp.exp(log_decay[head] * (offset + 1.0)), 0.0))
        columns.append(jnp.where(linked_on, jnp.exp(log_decay[head] * (CHUNK - 1.0 - offset)), 0.0))
    info = jnp.stack(columns, axis=1)
    info = jnp.pad(info, ((0, 0), (0, 128 - info.shape[1])))
    keys = jnp.where(segment >= 0, segment, -7).astype(f32).reshape(chunks, 1, CHUNK)
    distance = (jnp.arange(CHUNK)[:, None] - jnp.arange(CHUNK)[None, :]).astype(f32)
    decay = jnp.where(distance >= 0, jnp.exp(log_decay[:, None, None] * jnp.maximum(distance, 0.0)), 0.0)
    return angles, info, keys, decay


def retention_call(backward, which, piece_rows, heads, field, gate, tables, extra):
    rows = field.shape[0]
    chunks = rows // CHUNK
    angles, info, keys, decay = tables
    per_piece = piece_rows // CHUNK

    def step(i):
        return chunks - 1 - i if backward else i

    def place(i, which_ref):
        c = step(i)
        return ((c // per_piece) ^ which_ref[0]) * per_piece + c % per_piece

    def placed(width):
        return pl.BlockSpec((CHUNK, width), lambda i, w: (place(i, w), 0))

    in_specs = [
        placed(heads * QKV),
        placed(heads * VAL),
        pl.BlockSpec((CHUNK, KEY), lambda i, w: (step(i), 0)),
        pl.BlockSpec((CHUNK, 128), lambda i, w: (step(i), 0)),
        pl.BlockSpec((1, 1, CHUNK), lambda i, w: (step(i), 0, 0)),
        pl.BlockSpec((heads, CHUNK, CHUNK), lambda i, w: (0, 0, 0)),
    ]
    past_spec = pl.BlockSpec((1, heads, KEY, VAL), lambda i, w: (step(i), 0, 0, 0))
    if backward:
        in_specs += [placed(heads * VAL), placed(heads * VAL), placed(128), past_spec]
        out_specs = placed(heads * QKV)
        out_shape = jax.ShapeDtypeStruct((rows, heads * QKV), bf16)
    else:
        out_specs = [placed(heads * VAL), placed(heads * VAL), placed(128), past_spec]
        out_shape = [
            jax.ShapeDtypeStruct((rows, heads * VAL), bf16),
            jax.ShapeDtypeStruct((rows, heads * VAL), bf16),
            jax.ShapeDtypeStruct((rows, 128), f32),
            jax.ShapeDtypeStruct((chunks, heads, KEY, VAL), bf16),
        ]
    products = 15 if backward else 7
    return pl.pallas_call(
        functools.partial(retention_backward if backward else retention_forward, heads),
        grid_spec=pltpu.PrefetchScalarGridSpec(
            num_scalar_prefetch=1,
            grid=(chunks,),
            in_specs=in_specs,
            out_specs=out_specs,
            scratch_shapes=[pltpu.VMEM((heads, KEY, VAL), f32)],
        ),
        out_shape=out_shape,
        compiler_params=pltpu.CompilerParams(
            dimension_semantics=("arbitrary",), vmem_limit_bytes=48 * 1024 * 1024
        ),
        cost_estimate=pl.CostEstimate(
            flops=products * chunks * heads * 2 * CHUNK * CHUNK * CHUNK,
            bytes_accessed=(5 if backward else 4) * rows * heads * (QKV + VAL),
            transcendentals=rows * heads * VAL,
        ),
        name="retention_backward" if backward else "retention_forward",
    )(which, field, gate, angles, info, keys, decay, *extra)


MESH = pl.DeviceIdType.MESH


def opening_kernel(
    query_ref, key_ref, value_ref, gate_ref, token_ref, gain_ref, bias_ref, cot_ref,
    w_qkv_ref, w_gate_ref, normed_ref, cot_all_ref,
    w_qkv, w_gate, normed, token_own, cot_own, cot_got,
    local_sem, out_sem, up_send, up_recv, down_send, down_recv, core_send, core_recv, row_send, row_recv,
):
    dp = lax.axis_index("dp")
    tensor = lax.axis_index("tensor")
    z = lax.div(dp, 2)
    layers = lax.div(lax.axis_size("dp"), 2)
    shard_rows = query_ref.shape[0]
    rows = token_ref.shape[0]
    half = rows // 2
    above = (dp + 2, tensor)
    below = (dp - 2, tensor)
    twin = (dp + 1 - 2 * lax.rem(dp, 2), tensor)
    over_x = (dp, tensor + 1 - 2 * lax.rem(tensor, 2))
    over_y = (dp, lax.rem(tensor + 2, 4))

    keys = query_ref.shape[1]
    values = value_ref.shape[1]
    mine = pl.ds(pl.multiple_of(dp * shard_rows, shard_rows), shard_rows)
    places = [
        (query_ref, w_qkv.at[mine, pl.ds(0, keys)]),
        (key_ref, w_qkv.at[mine, pl.ds(keys, keys)]),
        (value_ref, w_qkv.at[mine, pl.ds(2 * keys, values)]),
        (gate_ref, w_gate.at[mine]),
        (token_ref, token_own),
        (cot_ref.at[pl.ds(0, half)], cot_own),
    ]
    local = [pltpu.make_async_copy(a, b, local_sem.at[i]) for i, (a, b) in enumerate(places)]
    for copy in local:
        copy.start()

    barrier = pltpu.get_barrier_semaphore()

    def greet(device):
        pl.semaphore_signal(barrier, inc=1, device_id=device, device_id_type=MESH)

    for device in (twin, over_x, over_y):
        greet(device)
    pl.when(z < layers - 1)(lambda: greet(above))
    pl.when(z > 0)(lambda: greet(below))
    pl.semaphore_wait(barrier, 3 + (z < layers - 1).astype(jnp.int32) + (z > 0).astype(jnp.int32))
    for copy in local[:4]:
        copy.wait()

    def weight_copies(shard, send_sem, recv_sem, step, device):
        place = pl.ds(pl.multiple_of(shard * shard_rows, shard_rows), shard_rows)
        return [
            pltpu.make_async_remote_copy(
                src_ref=ref.at[place], dst_ref=ref.at[place],
                send_sem=send_sem.at[step, i], recv_sem=recv_sem.at[step, i],
                device_id=device, device_id_type=MESH,
            )
            for i, ref in enumerate((w_qkv, w_gate))
        ]

    def shard_out(shard, slot):
        place = pl.ds(pl.multiple_of(shard * shard_rows, shard_rows), shard_rows)
        return [
            pltpu.make_async_copy(w_qkv.at[place], w_qkv_ref.at[place], out_sem.at[slot, 0]),
            pltpu.make_async_copy(w_gate.at[place], w_gate_ref.at[place], out_sem.at[slot, 1]),
        ]

    def start(copies):
        for copy in copies:
            copy.start()

    def wait_send(copies):
        for copy in copies:
            copy.wait_send()

    def wait_recv(copies):
        for copy in copies:
            copy.wait_recv()

    def up(j):
        return weight_copies(dp - 2 * j, up_send, up_recv, j, above)

    def down(j):
        return weight_copies(dp + 2 * j, down_send, down_recv, j, below)

    def to_twin(j):
        return weight_copies(dp + 2 * j, core_send, core_recv, j + 3, twin)

    def from_twin(j):
        return weight_copies(twin[0] + 2 * j, core_send, core_recv, j + 3, twin)

    def step(j):
        @pl.when(z - j >= 0)
        def _():
            wait_recv(weight_copies(dp - 2 * j, up_send, up_recv, j - 1, twin))
            if j < 3:
                pl.when(z < layers - 1)(lambda: start(up(j)))
            start(to_twin(-j))
            start(shard_out(dp - 2 * j, 3 - j))

        @pl.when(z + j < layers)
        def _():
            wait_recv(weight_copies(dp + 2 * j, down_send, down_recv, j - 1, twin))
            if j < 3:
                pl.when(z > 0)(lambda: start(down(j)))
            start(to_twin(j))
            start(shard_out(dp + 2 * j, 3 + j))

    pl.when(z < layers - 1)(lambda: start(up(0)))
    pl.when(z > 0)(lambda: start(down(0)))
    start(to_twin(0))
    start(shard_out(dp, 3))

    local[4].wait()

    @pl.loop(0, rows // 64)
    def _(i):
        block = pl.ds(pl.multiple_of(i * 64, 64), 64)
        unit, _ = normalize(token_own[block, :].astype(f32))
        normed[block, :] = (unit * gain_ref[...] + bias_ref[...]).astype(bf16)

    def row_copy(index, src, dst, device):
        return pltpu.make_async_remote_copy(
            src_ref=src, dst_ref=dst, send_sem=row_send.at[index], recv_sem=row_recv.at[index],
            device_id=device, device_id_type=MESH,
        )

    local[5].wait()
    over = [
        row_copy(0, normed.at[pl.ds(0, rows)], normed.at[pl.ds(rows, rows)], over_x),
        row_copy(1, normed.at[pl.ds(0, rows)], normed.at[pl.ds(2 * rows, rows)], over_y),
    ]
    start(over)
    step(1)
    wait_recv(over)
    onward = [
        row_copy(2, normed.at[pl.ds(2 * rows, half)], normed.at[pl.ds(3 * rows, half)], over_x),
        row_copy(3, normed.at[pl.ds(rows + half, half)], normed.at[pl.ds(3 * rows + half, half)], over_y),
    ]
    start(onward)
    cots = [
        row_copy(4, cot_own, cot_got.at[0], over_x),
        row_copy(5, cot_own, cot_got.at[1], over_y),
    ]
    start(cots)
    step(2)
    wait_recv(onward)
    normed_out = pltpu.make_async_copy(normed, normed_ref, local_sem.at[6])
    normed_out.start()
    wait_recv(cots)
    cot_out = pltpu.make_async_copy(cot_got, cot_all_ref, local_sem.at[7])
    cot_out.start()
    step(3)

    for j in range(-3, 4):
        @pl.when((z + j >= 0) & (z + j < layers))
        def _():
            wait_recv(from_twin(j))
            start(shard_out(twin[0] + 2 * j, 10 + j))
    wait_send(over + onward + cots)
    for j in range(3):
        pl.when((z < layers - 1) & (z - j >= 0))(lambda: wait_send(up(j)))
        pl.when((z > 0) & (z + j < layers))(lambda: wait_send(down(j)))
    normed_out.wait()
    cot_out.wait()
    for j in range(-3, 4):
        @pl.when((z + j >= 0) & (z + j < layers))
        def _():
            wait_send(to_twin(j))
            for copy in shard_out(dp + 2 * j, 3 + j) + shard_out(twin[0] + 2 * j, 10 + j):
                copy.wait()


def opening_exchange(query_weight, key_weight, value_weight, gate_weight, tokens, gain, bias, cotangent):
    dp = lax.axis_size("dp")
    depth, keys = query_weight.shape
    values = value_weight.shape[1]
    rows, width = tokens.shape
    anywhere = pl.BlockSpec(memory_space=pl.ANY)
    in_vmem = pl.BlockSpec(memory_space=pltpu.VMEM)
    return pl.pallas_call(
        opening_kernel,
        out_shape=[
            jax.ShapeDtypeStruct((dp * depth, 2 * keys + values), bf16),
            jax.ShapeDtypeStruct((dp * depth, values), bf16),
            jax.ShapeDtypeStruct((4 * rows, width), bf16),
            jax.ShapeDtypeStruct((2, rows // 2, width), bf16),
        ],
        in_specs=[anywhere] * 5 + [in_vmem] * 2 + [anywhere],
        out_specs=[anywhere] * 4,
        scratch_shapes=[
            pltpu.VMEM((dp * depth, 2 * keys + values), bf16),
            pltpu.VMEM((dp * depth, values), bf16),
            pltpu.VMEM((4 * rows, width), bf16),
            pltpu.VMEM((rows, width), bf16),
            pltpu.VMEM((rows // 2, width), bf16),
            pltpu.VMEM((2, rows // 2, width), bf16),
            pltpu.SemaphoreType.DMA((8,)),
            pltpu.SemaphoreType.DMA((14, 2)),
            pltpu.SemaphoreType.DMA((3, 2)),
            pltpu.SemaphoreType.DMA((3, 2)),
            pltpu.SemaphoreType.DMA((3, 2)),
            pltpu.SemaphoreType.DMA((3, 2)),
            pltpu.SemaphoreType.DMA((7, 2)),
            pltpu.SemaphoreType.DMA((7, 2)),
            pltpu.SemaphoreType.DMA((6,)),
            pltpu.SemaphoreType.DMA((6,)),
        ],
        compiler_params=pltpu.CompilerParams(
            collective_id=2, has_side_effects=True, vmem_limit_bytes=60 * 1024 * 1024
        ),
        name="opening_exchange",
    )(query_weight, key_weight, value_weight, gate_weight, tokens, gain.reshape(1, width), bias.reshape(1, width), cotangent)


def opening(query_weight, key_weight, value_weight, gate_weight, tokens, gain, bias, cotangent, devices):
    if devices == 4 and lax.axis_size("dp") == 8:
        w_qkv, w_gate, normed1_all, cot_half = opening_exchange(
            query_weight, key_weight, value_weight, gate_weight, tokens, gain, bias, cotangent
        )
        half = tokens.shape[0] // 2
        rest = after(cotangent, cot_half)[half:]
        rest_x = tensor_permute(rest, 1)
        rest_y = tensor_permute(rest, 2)
        lower = tensor_permute(cot_half[1], 1)
        upper = tensor_permute(rest_x, 2)
        cots = [cotangent, cot_half[0], rest_x, cot_half[1], rest_y, lower, upper]
        return w_qkv, w_gate, normed1_all, cots, (rest_x, rest_y)
    w_qkv = lax.all_gather(jnp.concatenate([query_weight, key_weight, value_weight], axis=1), "dp", axis=0, tiled=True)
    w_gate = lax.all_gather(gate_weight, "dp", axis=0, tiled=True)
    unit, _ = normalize(tokens.astype(f32))
    normed1_all = jnp.concatenate(gather_pieces((unit * gain + bias).astype(bf16), devices), axis=0)
    cots = gather_pieces(cotangent, devices)
    return w_qkv, w_gate, normed1_all, cots, (cots[0],)


def closing_kernel(
    heads,
    normed1_ref, up_ref, down_ref, feed_ref, w_out_ref, w_qkv_ref, w_gate_ref,
    gate_ref, grouped_ref, gated_ref, scale_ref, field_ref, past_ref, angle_ref, info_ref,
    low_ref, plus_ref, token_ref, row_ref, decay_ref, gain_ref, late_ref,
    result_ref, grad_ref, query_out, key_out, value_out, gate_out, out_out, up_out, down_out, sums_ref,
    big, units, columns, terms, half_in, full_in, products, twin_in, line_in,
    state_ref, past_in, scale_in, angle_in, info_in, blocks, given, landed, total,
    unit_sem, column_sem, chunk_sem, block_sem, out_sem, mixed_sem, over_send, over_recv, onward_send, onward_recv,
    half_send, half_recv, full_send, full_recv, twin_send, twin_recv, line_send, line_recv, sum_send, sum_recv,
    twin_free, line_free, half_free, full_free,
):
    dp = lax.axis_index("dp")
    tensor = lax.axis_index("tensor")
    z = lax.div(dp, 2)
    core = lax.rem(dp, 2)
    rows = token_ref.shape[0]
    half = rows // 2
    width = token_ref.shape[1]
    unit = units.shape[2]
    depth = columns.shape[2] // 2
    at_end = (z == 0) | (z == 3)
    upper = z >= 2
    twin = (dp + 1 - 2 * core, tensor)
    over_x = (dp, tensor + 1 - 2 * lax.rem(tensor, 2))
    over_y = (dp, lax.rem(tensor + 2, 4))
    here = dp * 4 + tensor
    peers = 32
    last = 5

    def layer(index):
        return (2 * index + core, tensor)

    def seen(index):
        return jnp.where(upper, 3 - index, index)

    end = layer(seen(0))
    near = layer(seen(1))
    opposite = layer(seen(2))
    targets = [seen(3), seen(2), jnp.where(at_end, seen(1), seen(0)), z]

    def remote(src, dst, send, recv, device):
        return pltpu.make_async_remote_copy(
            src_ref=src, dst_ref=dst, send_sem=send, recv_sem=recv, device_id=device, device_id_type=MESH
        )

    def block_of(start, count):
        return pl.ds(pl.multiple_of(start, count), count)


    def whole(index, ref, sem):
        return [pltpu.make_async_copy(ref, units.at[index], unit_sem.at[sem])]

    def folded(index, ref, sem):
        return [
            pltpu.make_async_copy(ref.at[:, pl.ds(0, unit)], units.at[index, pl.ds(0, unit)], unit_sem.at[sem]),
            pltpu.make_async_copy(ref.at[:, pl.ds(unit, unit)], units.at[index, pl.ds(unit, unit)], unit_sem.at[sem + 1]),
        ]

    def part(index, ref, start, sem):
        return [pltpu.make_async_copy(ref.at[:, pl.ds(start, unit)], units.at[index], unit_sem.at[sem])]

    def start(copies):
        for copy in copies:
            copy.start()

    def wait(copies):
        for copy in copies:
            copy.wait()

    out_load = folded(3, w_out_ref, 4)
    feed_load = [
        pltpu.make_async_copy(feed_ref.at[pl.ds((i + 1) * rows, rows)], terms.at[i], unit_sem.at[i]) for i in range(3)
    ]
    gated_load = whole(2, gated_ref, 6)
    w_gate_load = whole(3, w_gate_ref, 7)
    w_value_load = part(2, w_qkv_ref, unit, 8)
    w_key_load = part(1, w_qkv_ref, 0, 9)


    sources = [up_ref, down_ref, normed1_ref, None, normed1_ref, normed1_ref]

    def given_copy(r, k):
        place = block_of(targets[k] * 2 * depth, 2 * depth)
        return pltpu.make_async_copy(sources[r].at[place], products.at[r, k], column_sem.at[4 * r + k])

    def column_copy(r, k):
        place = block_of(targets[k] * 2 * depth, 2 * depth)
        return pltpu.make_async_copy(sources[r].at[:, place], columns.at[k % 2], column_sem.at[k])

    def prefetch(r):
        column_copy(r, 0).start()
        column_copy(r, 1).start()

    mine = block_of(core * depth, depth)
    theirs = block_of((1 - core) * depth, depth)

    def to_twin(r, k):
        return remote(
            products.at[r % 2, k, theirs], twin_in.at[k % 2], twin_send.at[r % 2, k], twin_recv.at[k % 2], twin
        )

    def along(r, k, slot, device):
        return remote(
            products.at[r % 2, k, mine], line_in.at[slot], line_send.at[r % 2, k], line_recv.at[slot], device
        )

    def send_to_twin(r, k):
        if r >= 1 or k >= 2:
            pl.semaphore_wait(twin_free.at[k % 2], 1)
        to_twin(r, k).start()

    def multiply(r, k):
        to_twin(r - 2, k).wait_send()
        if k < 3:
            along(r - 2, k, 0, end).wait_send()
        else:
            wait(outputs(r - 2))
        if sources[r] is not None:
            column_copy(r, k).wait()

        @pl.loop(0, unit // 256)
        def _(j):
            tile = block_of(j * 256, 256)
            product = None
            for place in (pl.ds(0, 2 * rows), pl.ds(2 * rows, 2 * rows)):
                if r < 4:
                    right = units[(None, None, 0, 2)[r], place, tile]
                else:
                    right = big[place, block_of((r - 4) * unit + j * 256, 256)]
                if sources[r] is None:
                    left = big[place, block_of(targets[k] * 2 * depth, 2 * depth)]
                else:
                    left = columns[k % 2, place]
                more = dot_tn(left, right)
                product = more if product is None else product + more
            products[r % 2, k, :, tile] = product.astype(bf16)

        if sources[r] is not None and k + 2 < 4:
            column_copy(r, k + 2).start()
        send_to_twin(r, k)

    def add_to_mine(r, k, others):
        @pl.loop(0, depth // 64)
        def _(i):
            inner = block_of(core * depth + i * 64, 64)
            value = products[r % 2, k, inner].astype(f32)
            for ref, index in others:
                value = value + ref[index, block_of(i * 64, 64)].astype(f32)
            products[r % 2, k, inner] = value.astype(bf16)

    def settle(r, k):
        to_twin(r, k).wait_recv()
        add_to_mine(r, k, [(twin_in, k % 2)])
        if r < last or k < 2:
            pl.semaphore_signal(twin_free.at[k % 2], inc=1, device_id=twin, device_id_type=MESH)

    def push(r, k):
        @pl.when(at_end)
        def _():
            if r >= 1:
                pl.semaphore_wait(line_free.at[k], 1)
            along(r, k, k, near).start()

    def line_wait(slot):
        along(0, 0, slot, end).wait_recv()

    def used(device, index):
        pl.semaphore_signal(line_free.at[index], inc=1, device_id=device, device_id_type=MESH)

    def pass_on(r, which):
        arrived, sender, slot, device = ((0, end, 3, opposite), (1, end, 4, opposite), (3, opposite, 0, end))[which]

        @pl.when(jnp.logical_not(at_end))
        def _():
            line_wait(arrived)
            add_to_mine(r, which, [(line_in, arrived)])
            if r < last:
                used(sender, (0, 1, 0)[which])
            if r >= 1:
                pl.semaphore_wait(line_free.at[which], 1)
            along(r, which, slot, device).start()

    def outputs(r):
        keys = heads * KEY
        slot = products.at[r % 2, 3]
        if r == 4:
            return [
                pltpu.make_async_copy(slot.at[mine, pl.ds(0, keys)], query_out, out_sem.at[0, 0]),
                pltpu.make_async_copy(slot.at[mine, pl.ds(keys, keys)], key_out, out_sem.at[0, 1]),
            ]
        out = (up_out, down_out, gate_out, out_out, None, value_out)[r]
        return [pltpu.make_async_copy(slot.at[mine], out, out_sem.at[r % 2, 0])]

    def finish(r):
        @pl.when(at_end)
        def _():
            line_wait(0)
            add_to_mine(r, 3, [(line_in, 0)])
            if r < last:
                used(near, 2)

        @pl.when(jnp.logical_not(at_end))
        def _():
            line_wait(2)
            line_wait(4)
            add_to_mine(r, 3, [(line_in, 2), (line_in, 4)])
            if r < last:
                used(end, 2)
                used(opposite, 1)

        start(outputs(r))


    def rows_of(r, first=0, count=rows):
        return pl.ds(r * rows + first, count)

    over = [
        remote(big.at[rows_of(0)], big.at[rows_of(1)], over_send.at[0], over_recv.at[0], over_x),
        remote(big.at[rows_of(0)], big.at[rows_of(2)], over_send.at[1], over_recv.at[1], over_y),
    ]
    onward = [
        remote(big.at[rows_of(2, 0, half)], big.at[rows_of(3, 0, half)], onward_send.at[0], onward_recv.at[0], over_x),
        remote(big.at[rows_of(1, half, half)], big.at[rows_of(3, half, half)], onward_send.at[1], onward_recv.at[1], over_y),
    ]
    halves = [
        remote(terms.at[2, pl.ds(0, half)], half_in.at[0], half_send.at[0], half_recv.at[0], over_x),
        remote(terms.at[2, pl.ds(half, half)], half_in.at[1], half_send.at[1], half_recv.at[1], over_y),
    ]
    fulls = [
        remote(terms.at[0], full_in.at[0], full_send.at[0], full_recv.at[0], over_x),
        remote(terms.at[1], full_in.at[1], full_send.at[1], full_recv.at[1], over_y),
    ]
    sides = (over_x, over_y)

    def send_halves(stage):
        for i, copy in enumerate(halves):
            if stage == 1:
                pl.semaphore_wait(half_free.at[i], 1)
            copy.start()

    def take_halves(stage):
        for copy in halves:
            copy.wait_recv()
        for term, first, slot in ((1, 0, 0), (0, half, 1)):
            @pl.loop(0, half // 64)
            def _(i):
                place = block_of(first + i * 64, 64)
                grown = terms[term, place].astype(f32) + half_in[slot, block_of(i * 64, 64)].astype(f32)
                terms[term, place] = grown.astype(bf16)

        for i, copy in enumerate(fulls):
            if stage == 0:
                pl.semaphore_signal(half_free.at[i], inc=1, device_id=sides[i], device_id_type=MESH)
            else:
                pl.semaphore_wait(full_free.at[i], 1)
            copy.start()

    def project(r):
        slot = (2, 0, 1, 2)[r]

        @pl.loop(0, width // 256)
        def _(j):
            tile = block_of(j * 256, 256)
            term = dot_nt(big[rows_of(r), pl.ds(0, unit)], units[1, tile])
            term = term + dot_nt(big[rows_of(r), pl.ds(unit, unit)], units[2, tile])
            term = term + dot_nt(units[0, rows_of(r)], units[3, tile])
            terms[slot, :, tile] = term.astype(bf16)


    def gate_copies(r):
        return [
            pltpu.make_async_copy(
                ref.at[rows_of(r), pl.ds(h * VAL, VAL)],
                columns.at[r % 2, pl.ds((2 * i + h) * rows, rows)],
                chunk_sem.at[r % 2, 2 * i + h],
            )
            for i, ref in enumerate((gate_ref, grouped_ref))
            for h in range(heads)
        ]

    def gate_back(r):
        wait(gate_copies(r))

        @pl.loop(0, unit // 256)
        def _(j):
            grad = dot_nt(big[rows_of(r), pl.ds(0, unit)], units[3, block_of(j * 256, 256)])
            grad = grad + dot_nt(big[rows_of(r), pl.ds(unit, unit)], units[3, block_of(unit + j * 256, 256)])
            head = lax.div(j, VAL // 256)
            inner = block_of(lax.rem(j, VAL // 256) * 256, 256)
            raw = columns[r % 2, block_of(head * rows, rows), inner].astype(f32)
            grouped = columns[r % 2, block_of((heads + head) * rows, rows), inner].astype(f32)
            sigmoid = 1.0 / (1.0 + jnp.exp(-raw))
            tile = block_of(j * 256, 256)
            units[0, rows_of(r), tile] = (grad * grouped * (sigmoid * (1.0 + raw * (1.0 - sigmoid)))).astype(bf16)
            units[1, rows_of(r), tile] = grad.astype(bf16)

    chunks = 4 * rows // CHUNK
    per_piece = rows // CHUNK

    def chunk_place(c):
        piece = lax.div(c, per_piece)
        low = lax.rem(lax.rem(piece, 2) + lax.rem(tensor, 2), 2)
        high = lax.rem(lax.div(piece, 2) + lax.div(tensor, 2), 2)
        return (2 * high + low) * per_piece + lax.rem(c, per_piece)

    def chunk_copies(c, slot):
        place = block_of(chunk_place(c) * CHUNK, CHUNK)
        seat = block_of(c * CHUNK, CHUNK)
        keys = heads * KEY
        pieces = [
            (field_ref.at[place, pl.ds(0, keys)], columns.at[slot, pl.ds(0, CHUNK)]),
            (field_ref.at[place, pl.ds(keys, keys)], columns.at[slot, pl.ds(CHUNK, CHUNK)]),
        ]
        for h in range(heads):
            pieces.append((field_ref.at[place, pl.ds(2 * keys + h * VAL, VAL)], columns.at[slot, pl.ds((2 + h) * CHUNK, CHUNK)]))
            pieces.append((gate_ref.at[place, pl.ds(h * VAL, VAL)], columns.at[slot, pl.ds((4 + h) * CHUNK, CHUNK)]))
            pieces.append((grouped_ref.at[place, pl.ds(h * VAL, VAL)], columns.at[slot, pl.ds((6 + h) * CHUNK, CHUNK)]))
        pieces += [
            (past_ref.at[c], past_in.at[slot]),
            (scale_ref.at[place], scale_in.at[slot]),
            (angle_ref.at[seat], angle_in.at[slot]),
            (info_ref.at[seat], info_in.at[slot]),
        ]
        return [pltpu.make_async_copy(src, dst, chunk_sem.at[slot, i]) for i, (src, dst) in enumerate(pieces)]

    def retention_steps(between):
        @pl.loop(0, chunks)
        def _(step):
            c = chunks - 1 - step
            slot = lax.rem(step, 2)
            wait(chunk_copies(c, slot))

            @pl.when(step + 1 < chunks)
            def _():
                start(chunk_copies(c - 1, 1 - slot))

            place = block_of(chunk_place(c) * CHUNK, CHUNK)
            angles = angle_in[slot]
            cosine = angles[:, : KEY // 2]
            sine = angles[:, KEY // 2 :]
            info = info_in[slot]
            same = info[:, 0:1] == row_ref[c]

            for head in range(heads):
                at = pl.ds(head * KEY, KEY)
                query = turn(columns[slot, pl.ds(0, CHUNK), at].astype(f32), cosine, sine).astype(bf16)
                key = turn(columns[slot, pl.ds(CHUNK, CHUNK), at].astype(f32), cosine, sine)
                key = (key * key_scale).astype(bf16)
                value = columns[slot, pl.ds((2 + head) * CHUNK, CHUNK)]
                gate = columns[slot, pl.ds((4 + head) * CHUNK, CHUNK)].astype(f32)
                grouped = columns[slot, pl.ds((6 + head) * CHUNK, CHUNK)].astype(f32)
                into = info[:, 1 + 2 * head : 2 + 2 * head]
                onto = info[:, 2 + 2 * head : 3 + 2 * head]
                scale = scale_in[slot, :, head : head + 1]
                past = past_in[slot, head]
                out_grad_in = units[1, place, pl.ds(head * VAL, VAL)].astype(f32)
                c_in = out_grad_in * (gate / (1.0 + jnp.exp(-gate)))
                mean_c = jnp.mean(c_in, axis=-1, keepdims=True)
                mean_cx = jnp.mean(c_in * grouped, axis=-1, keepdims=True)
                out_grad = (scale * (c_in - mean_c - grouped * mean_cx)).astype(bf16)
                state = state_ref[head]
                state_low = state.astype(bf16)
                masked = jnp.where(same, decay_ref[head], 0.0)
                weights = (masked * dot_nt(query, key)).astype(bf16)
                score_grad = (masked * dot_nt(out_grad, value)).astype(bf16)
                value_grad = dot_tn(weights, out_grad) + onto * dot_nn(key, state_low)
                query_grad = dot_nn(score_grad, key) + into * dot_nt(out_grad, past)
                key_grad = dot_tn(score_grad, query) + onto * dot_nt(value, state_low)
                moved = (query.astype(f32) * into).astype(bf16)
                state_ref[head] = into[CHUNK - 1 :, :] * state + dot_tn(moved, out_grad)
                big[place, pl.ds(head * KEY, KEY)] = turn_back(query_grad, cosine, sine).astype(bf16)
                big[place, pl.ds((heads + head) * KEY, KEY)] = (turn_back(key_grad, cosine, sine) * key_scale).astype(bf16)
                big[place, pl.ds(2 * heads * KEY + head * VAL, VAL)] = value_grad.astype(bf16)

            between(step)


    def block_copy(ref, i, slot):
        return pltpu.make_async_copy(ref.at[block_of(i * 64, 64)], blocks.at[slot], block_sem.at[slot])

    def stream(ref, use):
        @pl.loop(0, rows // 64)
        def _(i):
            slot = lax.rem(i, 4)
            block_copy(ref, i, slot).wait()
            use(block_of(i * 64, 64), blocks[slot])

            @pl.when(i + 4 < rows // 64)
            def _():
                block_copy(ref, i + 4, slot).start()


    own_load = pltpu.make_async_copy(low_ref, big.at[rows_of(0)], mixed_sem.at[0])
    own_load.start()
    for r in range(2):
        for k in range(4):
            given_copy(r, k).start()
    start(out_load)
    start(gate_copies(0))
    start(gate_copies(1))
    start(feed_load)

    barrier = pltpu.get_barrier_semaphore()

    def partner(k):
        other = lax.rem(here + k, peers)
        return other, (lax.div(other, 4), lax.rem(other, 4))

    @pl.loop(1, peers)
    def _(k):
        pl.semaphore_signal(barrier, inc=1, device_id=partner(k)[1], device_id_type=MESH)

    pl.semaphore_wait(barrier, peers - 1)

    own_load.wait()
    start(over)
    for k in range(4):
        given_copy(0, k).wait()
        send_to_twin(0, k)
        if k > 0:
            settle(0, k - 1)
            push(0, k - 1)
    settle(0, 3)
    for k in range(4):
        given_copy(1, k).wait()
        send_to_twin(1, k)
        if k > 0:
            settle(1, k - 1)
    settle(1, 3)
    wait(out_load)
    gate_back(0)
    start(gate_copies(2))
    pass_on(0, 0)
    push(1, 0)
    pass_on(0, 1)
    push(1, 1)
    pass_on(0, 2)
    for copy in over:
        copy.wait_recv()
    start(onward)
    gate_back(1)
    start(gate_copies(3))
    finish(0)
    push(1, 2)
    gate_back(2)
    pass_on(1, 0)
    pass_on(1, 1)
    wait(feed_load)
    start(gated_load)
    for copy in onward:
        copy.wait_recv()
    send_halves(0)
    gate_back(3)
    prefetch(2)
    start(w_gate_load)
    pass_on(1, 2)
    state_ref[...] = jnp.zeros_like(state_ref)

    def produce(r, k, pushed=True):
        multiply(r, k)
        if k > 0:
            settle(r, k - 1)
            if pushed:
                push(r, k - 1)

    produce(2, 0)
    produce(2, 1)
    finish(1)
    produce(2, 2)
    produce(2, 3)
    settle(2, 3)
    start(chunk_copies(chunks - 1, 0))
    wait(gated_load)
    produce(3, 0)
    produce(3, 1, False)
    take_halves(0)
    pass_on(2, 0)
    push(3, 0)
    produce(3, 2, False)
    produce(3, 3, False)
    settle(3, 3)
    start(w_value_load)
    for copy in over + onward:
        copy.wait_send()

    def between(step):
        @pl.when(step == 1)
        def _():
            pass_on(2, 1)
            push(3, 1)

        @pl.when(step == 2)
        def _():
            pass_on(2, 2)

        @pl.when(step == 5)
        def _():
            finish(2)
            push(3, 2)

    retention_steps(between)
    start(w_key_load)
    prefetch(4)
    pass_on(3, 0)
    for copy in halves:
        copy.wait_send()
    wait(w_gate_load)
    wait(w_value_load)
    wait(w_key_load)
    project(3)
    send_halves(1)
    for i in range(4):
        block_copy(plus_ref, i, i).start()
    produce(4, 0)
    produce(4, 1)
    pass_on(3, 1)
    for copy in fulls:
        copy.wait_recv()

    def add_result(place, value):
        full_in[0, place] = (value.astype(f32) + full_in[0, place].astype(f32) + full_in[1, place].astype(f32)).astype(bf16)

    stream(plus_ref, add_result)
    result_copy = pltpu.make_async_copy(full_in.at[0], result_ref, mixed_sem.at[1])
    result_copy.start()
    for copy in fulls:
        copy.wait_send()
    pass_on(3, 2)
    project(1)
    result_copy.wait()
    for i, side in enumerate(sides):
        pl.semaphore_signal(full_free.at[i], inc=1, device_id=side, device_id_type=MESH)
    project(2)
    take_halves(1)
    finish(3)
    produce(4, 2)
    produce(4, 3, False)
    push(4, 2)
    settle(4, 3)
    prefetch(5)
    pass_on(4, 0)
    produce(5, 0)
    produce(5, 1)
    pass_on(4, 1)
    produce(5, 2)
    pass_on(4, 2)
    produce(5, 3, False)
    settle(5, 3)
    for copy in halves:
        copy.wait_send()
    project(0)
    finish(4)
    push(5, 2)
    pass_on(5, 0)
    pass_on(5, 1)
    for copy in fulls:
        copy.wait_recv()
        copy.wait_send()
    last_loads = [
        pltpu.make_async_copy(token_ref, terms.at[0], mixed_sem.at[2]),
        pltpu.make_async_copy(low_ref, terms.at[1], mixed_sem.at[0]),
    ]
    start(last_loads)
    total[...] = jnp.zeros_like(total)
    wait(last_loads)

    @pl.loop(0, rows // 64)
    def _(i):
        place = block_of(i * 64, 64)
        normed_grad = terms[2, place].astype(f32) + full_in[0, place].astype(f32) + full_in[1, place].astype(f32)
        plain, scale = normalize(terms[0, place].astype(f32))
        grad = terms[1, place].astype(f32) + normalize_back(normed_grad, plain, scale, gain_ref[...])
        full_in[0, place] = grad.astype(bf16)
        total[0:1, :] += jnp.sum(normed_grad * plain, axis=0, keepdims=True)
        total[1:2, :] += jnp.sum(normed_grad, axis=0, keepdims=True)

    grad_copy = pltpu.make_async_copy(full_in.at[0], grad_ref, mixed_sem.at[3])
    grad_copy.start()

    total[2:4, :] = late_ref[...]
    for k in range(peers // 2):
        given[k] = total[:, k * 128 : (k + 1) * 128]

    def sum_copy(k):
        other, device = partner(k)
        return remote(given.at[lax.div(other, 2)], landed.at[k], sum_send.at[k], sum_recv.at[k], device)

    @pl.loop(1, peers)
    def _(k):
        sum_copy(k).start()

    pass_on(5, 2)
    sums_ref[...] = given[lax.div(here, 2)]

    @pl.loop(1, peers)
    def _(k):
        sum_copy(k).wait()
        sums_ref[...] += landed[k]

    finish(5)

    for r in (4, 5):
        for k in range(4):
            to_twin(r, k).wait_send()
            if k < 3:
                along(r, k, 0, end).wait_send()
    wait(outputs(4) + outputs(5))
    grad_copy.wait()


def closing_exchange(heads, operands, small):
    token_rows, width = operands[-1].shape
    rows = 4 * token_rows
    depth = width // 8
    keys, values = heads * KEY, heads * VAL
    unit = operands[1].shape[1]
    anywhere = pl.BlockSpec(memory_space=pl.ANY)
    in_vmem = pl.BlockSpec(memory_space=pltpu.VMEM)
    sem = pltpu.SemaphoreType.DMA
    regular = pltpu.SemaphoreType.REGULAR
    vmem = pltpu.VMEM
    return pl.pallas_call(
        functools.partial(closing_kernel, heads),
        out_shape=[
            jax.ShapeDtypeStruct((token_rows, width), bf16),
            jax.ShapeDtypeStruct((token_rows, width), bf16),
            jax.ShapeDtypeStruct((depth, keys), bf16),
            jax.ShapeDtypeStruct((depth, keys), bf16),
            jax.ShapeDtypeStruct((depth, values), bf16),
            jax.ShapeDtypeStruct((depth, values), bf16),
            jax.ShapeDtypeStruct((depth, unit), bf16),
            jax.ShapeDtypeStruct((depth, unit), bf16),
            jax.ShapeDtypeStruct((depth, unit), bf16),
            jax.ShapeDtypeStruct((8, 128), f32),
        ],
        in_specs=[anywhere] * len(operands) + [in_vmem] * len(small),
        out_specs=[anywhere] * 9 + [in_vmem],
        scratch_shapes=[
            vmem((rows, width), bf16),
            vmem((4, rows, unit), bf16),
            vmem((2, rows, 2 * depth), bf16),
            vmem((3, token_rows, width), bf16),
            vmem((2, token_rows // 2, width), bf16),
            vmem((2, token_rows, width), bf16),
            vmem((2, 4, 2 * depth, unit), bf16),
            vmem((2, depth, unit), bf16),
            vmem((5, depth, unit), bf16),
            vmem((heads, KEY, VAL), f32),
            vmem((2, heads, KEY, VAL), bf16),
            vmem((2, CHUNK, 128), f32),
            vmem((2, CHUNK, KEY), f32),
            vmem((2, CHUNK, 128), f32),
            vmem((4, 64, width), bf16),
            vmem((16, 8, 128), f32),
            vmem((32, 8, 128), f32),
            vmem((8, width), f32),
            sem((10,)), sem((8,)), sem((2, 12)), sem((4,)), sem((2, 2)), sem((4,)),
            sem((2,)), sem((2,)), sem((2,)), sem((2,)),
            sem((2,)), sem((2,)), sem((2,)), sem((2,)),
            sem((2, 4)), sem((2,)), sem((2, 3)), sem((5,)), sem((32,)), sem((32,)),
            regular((2,)), regular((3,)), regular((2,)), regular((2,)),
        ],
        compiler_params=pltpu.CompilerParams(
            collective_id=3, has_side_effects=True, vmem_limit_bytes=63_400_000
        ),
        name="closing_exchange",
    )(*operands, *small)


def body(tokens, cotangent, segment, first_gain, first_bias, query_weight, key_weight, value_weight, gate_weight, out_weight, second_gain, second_bias, up_weight, down_weight):
    devices = lax.axis_size("tensor")
    rows = tokens.shape[0]
    heads = query_weight.shape[1] // KEY
    here = lax.axis_index("tensor")
    which = (here if devices == 4 else jnp.zeros_like(here)).astype(jnp.int32).reshape(1)

    def per_piece(values):
        return [values[i * rows : (i + 1) * rows] for i in range(devices)]

    w_qkv, w_gate, normed1_all, cots, cot_begun = opening(
        query_weight, key_weight, value_weight, gate_weight, tokens, first_gain, first_bias, cotangent, devices
    )
    w_out = lax.all_gather(after(out_weight, w_gate), "dp", axis=1, tiled=True)
    w_down = lax.all_gather(after(down_weight, w_out), "dp", axis=1, tiled=True)
    w_up = lax.all_gather(after(up_weight, w_down), "dp", axis=0, tiled=True)

    token_rows = tokens.astype(f32)
    tables = retention_tables(segment, heads, here * heads)
    field = dot_nn(normed1_all, w_qkv).astype(bf16)
    gate = dot_nn(normed1_all, w_gate).astype(bf16)
    gated, grouped, group_scale, past = retention_call(
        False, which, rows, heads, field, after(gate, *cot_begun), tables, ()
    )
    branch, begun, _ = scatter_sum([dot_nn(piece, w_out) for piece in per_piece(after(gated, *cots))])

    mixed = token_rows + branch
    unit2, scale2 = normalize(mixed)
    normed2 = (unit2 * second_gain + second_bias).astype(bf16)
    cot_all = jnp.concatenate(after(cots, *begun), axis=0)
    hidden_grads = per_piece(dot_nt(cot_all, after(w_down, normed2)).astype(bf16))

    def feed(piece, hidden_grad):
        value, slope = gelu_both(dot_nn(piece, w_up))
        return after((value.astype(bf16), (hidden_grad.astype(f32) * slope).astype(bf16)))

    fed_own = feed(normed2, hidden_grads[0])
    normed2_pieces = gather_pieces(normed2, devices, fed_own)
    fed = [fed_own] + [feed(piece, grad) for piece, grad in zip(normed2_pieces[1:-1], hidden_grads[1:-1])]
    fed.append(feed(after(normed2_pieces[-1], *fed), hidden_grads[-1]))
    hidden = [f[0] for f in fed]
    up_grad = [f[1] for f in fed]
    terms = [dot_nt(piece, w_up) for piece in up_grad]
    normed2_grad, _, _ = scatter_sum(terms)
    mixed_grad = cotangent.astype(f32) + normalize_back(normed2_grad, unit2, scale2, second_gain)
    gain2_grad = jnp.sum(normed2_grad * unit2, axis=0)
    bias2_grad = jnp.sum(normed2_grad, axis=0)
    mixed_low = mixed_grad.astype(bf16)
    hidden_all = jnp.concatenate(after(hidden, *terms), axis=0)
    normed2_all = jnp.concatenate(after(normed2_pieces, *terms), axis=0)
    up_grad_all = jnp.concatenate(after(up_grad, *terms), axis=0)
    feed_terms = dot_nn(hidden_all, w_down).astype(bf16)
    own_term = feed_terms[:rows].astype(f32)
    up_weight_grad = dot_tn(normed2_all, up_grad_all).astype(bf16)
    down_weight_grad = dot_tn(cot_all, hidden_all).astype(bf16)
    angles, info, keys, decay = tables

    if devices == 4 and lax.axis_size("dp") == 8:
        result, input_grad, query_sum, key_sum, value_sum, gate_sum, out_sum, up_sum, down_sum, sums = closing_exchange(
            heads,
            (
                normed1_all, up_weight_grad, down_weight_grad, feed_terms, w_out, w_qkv, w_gate,
                gate, grouped, gated, group_scale, field, past, angles, info,
                mixed_low, (mixed + own_term).astype(bf16), tokens,
            ),
            (keys, decay, first_gain.reshape(1, -1), jnp.stack([gain2_grad, bias2_grad])),
        )
        part = first_gain.shape[0] // 32
        sums = lax.dynamic_slice_in_dim(sums, (here % 2) * part, part, 1)
        norm_sums = [sums[0], sums[1], sums[2], sums[3]]
        query_sum, key_sum, value_sum, gate_sum, up_sum = (
            v.astype(f32) for v in (query_sum, key_sum, value_sum, gate_sum, up_sum)
        )
        out_sum, down_sum = out_sum.astype(f32).T, down_sum.astype(f32).T
    else:
        def summed(gradient, dimension):
            return lax.psum_scatter(
                gradient.astype(bf16), "dp", scatter_dimension=dimension, tiled=True
            ).astype(f32)

        up_sum = summed(up_weight_grad, 0)
        down_sum = summed(down_weight_grad, 0).T
        mixed_all = jnp.concatenate(gather_pieces(mixed_low, devices), axis=0)
        ffn, _, _ = scatter_sum([term.astype(f32) for term in per_piece(feed_terms)])
        result = (mixed + ffn).astype(bf16)
        gated_grad = dot_nt(mixed_all, w_out)
        raw = gate.astype(f32)
        sigmoid = 1.0 / (1.0 + jnp.exp(-raw))
        gate_grad = (gated_grad * grouped.astype(f32) * (sigmoid * (1.0 + raw * (1.0 - sigmoid)))).astype(bf16)
        back = retention_call(
            True, which, rows, heads, field, gate, tables, (gated_grad.astype(bf16), grouped, group_scale, past)
        )
        gate_sum = summed(dot_tn(normed1_all, gate_grad), 0)
        out_sum = summed(dot_tn(gated, mixed_all), 1)
        qkv_sum = summed(dot_tn(normed1_all, back), 0)
        keys_end = heads * KEY
        query_sum = qkv_sum[:, :keys_end]
        key_sum = qkv_sum[:, keys_end : 2 * keys_end]
        value_sum = qkv_sum[:, 2 * keys_end :]
        terms = [
            dot_nt(first, w_qkv) + dot_nt(second, w_gate) for first, second in zip(per_piece(back), per_piece(gate_grad))
        ]
        normed1_grad, _, _ = scatter_sum(terms)
        unit1, scale1 = normalize(token_rows)
        input_grad = (mixed_grad + normalize_back(normed1_grad, unit1, scale1, first_gain)).astype(bf16)
        gain1_grad = jnp.sum(normed1_grad * unit1, axis=0)
        bias1_grad = jnp.sum(normed1_grad, axis=0)
        norm_sums = spread_sum([gain1_grad, bias1_grad, gain2_grad, bias2_grad])
    return (
        result,
        input_grad,
        norm_sums[0],
        norm_sums[1],
        query_sum,
        key_sum,
        value_sum,
        gate_sum,
        out_sum,
        norm_sums[2],
        norm_sums[3],
        up_sum,
        down_sum,
    )


def solution(mesh):
    rows = P(("dp", "tensor"), None)
    vector = P(("dp", "tensor"))
    into = P("dp", "tensor")
    back = P("tensor", "dp")
    return jax.shard_map(
        body,
        mesh=mesh,
        in_specs=(rows, rows, P("dp"), P(), P(), into, into, into, into, back, P(), P(), into, back),
        out_specs=(rows, rows, vector, vector, into, into, into, into, back, vector, vector, into, back),
        check_vma=False,
    )
```

```python
import functools

import jax
import jax.numpy as jnp
from jax import lax
from jax.experimental import pallas as pl
from jax.experimental.pallas import tpu as pltpu
from jax.sharding import PartitionSpec as P

KEY = 256
VAL = 512
CHUNK = 256
QKV = 2 * KEY + VAL

norm_epsilon = 1e-05
group_floor = 0.5
key_scale = KEY ** (-0.5)

f32 = jnp.float32
bf16 = jnp.bfloat16


def dot_nn(left, right):
    return lax.dot_general(left, right, (((1,), (0,)), ((), ())), preferred_element_type=f32)


def dot_nt(left, right):
    return lax.dot_general(left, right, (((1,), (1,)), ((), ())), preferred_element_type=f32)


def dot_tn(left, right):
    return lax.dot_general(left, right, (((0,), (0,)), ((), ())), preferred_element_type=f32)


def tensor_permute(values, bit):
    pairs = [(i, i ^ bit) for i in range(4)]
    return lax.ppermute(values, "tensor", pairs)


def after(values, *tokens):
    return lax.optimization_barrier((values, tokens))[0]


def gather_pieces(own, devices, between=()):
    if devices != 4:
        whole = lax.all_gather(own, "tensor", axis=0, tiled=True)
        return list(jnp.split(whole, devices, axis=0))
    half = own.shape[0] // 2
    from_x = tensor_permute(own, 1)
    from_y = tensor_permute(own, 2)
    lower, upper = after((from_y[:half], from_x[half:]), *between)
    lower = tensor_permute(lower, 1)
    upper = tensor_permute(upper, 2)
    return [own, from_x, from_y, jnp.concatenate([lower, upper], axis=0)]


def scatter_sum(terms):
    if len(terms) != 4:
        stacked = jnp.concatenate([term.astype(bf16) for term in terms], axis=0)
        return lax.psum_scatter(stacked, "tensor", scatter_dimension=0, tiled=True).astype(f32), (stacked,), (stacked,)
    own, over_x, over_y, across = terms
    half = own.shape[0] // 2
    across = across.astype(bf16)
    first = tensor_permute(across[:half], 1)
    second = tensor_permute(across[half:], 2)
    over_y = jnp.concatenate([over_y[:half] + first.astype(f32), over_y[half:]], axis=0)
    over_x = jnp.concatenate([over_x[:half], over_x[half:] + second.astype(f32)], axis=0)
    by_x = tensor_permute(over_x.astype(bf16), 1)
    by_y = tensor_permute(over_y.astype(bf16), 2)
    return own + by_x.astype(f32) + by_y.astype(f32), (first, second), (by_x, by_y)


def spread_sum_kernel(tensor_devices, devices, given_ref, sum_ref, landed_ref, send_sem, recv_sem):
    here = lax.axis_index("dp") * tensor_devices + lax.axis_index("tensor")

    def partner(k):
        other = lax.rem(here + k, devices)
        return other, (lax.div(other, tensor_devices), lax.rem(other, tensor_devices))

    def copy(k):
        other, device = partner(k)
        return pltpu.make_async_remote_copy(
            src_ref=given_ref.at[other],
            dst_ref=landed_ref.at[k],
            send_sem=send_sem.at[k],
            recv_sem=recv_sem.at[k],
            device_id=device,
            device_id_type=pl.DeviceIdType.MESH,
        )

    barrier = pltpu.get_barrier_semaphore()

    @pl.loop(1, devices)
    def _(k):
        pl.semaphore_signal(barrier, inc=1, device_id=partner(k)[1], device_id_type=pl.DeviceIdType.MESH)

    pl.semaphore_wait(barrier, devices - 1)

    @pl.loop(1, devices)
    def _(k):
        copy(k).start()

    sum_ref[...] = given_ref[here]

    @pl.loop(1, devices)
    def _(k):
        copy(k).wait()
        sum_ref[...] += landed_ref[k]


def spread_sum(vectors):
    dp, tensor = lax.axis_size("dp"), lax.axis_size("tensor")
    devices = dp * tensor
    part = vectors[0].shape[0] // devices
    given = jnp.stack([v.reshape(devices, part) for v in vectors], axis=1)
    given = jnp.pad(given, ((0, 0), (0, 8 - len(vectors)), (0, 128 - part)))
    total = pl.pallas_call(
        functools.partial(spread_sum_kernel, tensor, devices),
        out_shape=jax.ShapeDtypeStruct((8, 128), f32),
        in_specs=[pl.BlockSpec(memory_space=pltpu.VMEM)],
        out_specs=pl.BlockSpec(memory_space=pltpu.VMEM),
        scratch_shapes=[
            pltpu.VMEM((devices, 8, 128), f32),
            pltpu.SemaphoreType.DMA((devices,)),
            pltpu.SemaphoreType.DMA((devices,)),
        ],
        compiler_params=pltpu.CompilerParams(collective_id=1, has_side_effects=True),
        name="spread_sum",
    )(given)
    return [total[i, :part] for i in range(len(vectors))]


def normalize(values):
    average = jnp.mean(values, axis=-1, keepdims=True)
    centred = values - average
    variance = jnp.mean(centred * centred, axis=-1, keepdims=True)
    scale = lax.rsqrt(variance + norm_epsilon)
    return centred * scale, scale


def normalize_back(normed_grad, unit, scale, gain):
    g = normed_grad * gain
    mean_g = jnp.mean(g, axis=-1, keepdims=True)
    mean_gx = jnp.mean(g * unit, axis=-1, keepdims=True)
    return scale * (g - mean_g - unit * mean_gx)


def gelu_both(values):
    inner = 0.7978845608 * (values + 0.044715 * values * values * values)
    t = jnp.tanh(inner)
    slope = 0.7978845608 * (1.0 + 3.0 * 0.044715 * values * values)
    return 0.5 * values * (1.0 + t), 0.5 * (1.0 + t) + 0.5 * values * (1.0 - t * t) * slope


def turn(block, cosine, sine):
    a = block[:, : KEY // 2]
    b = block[:, KEY // 2 :]
    return jnp.concatenate([a * cosine - b * sine, b * cosine + a * sine], axis=1)


def turn_back(block, cosine, sine):
    a = block[:, : KEY // 2]
    b = block[:, KEY // 2 :]
    return jnp.concatenate([a * cosine + b * sine, b * cosine - a * sine], axis=1)


def head_parts(field_ref, angles, heads, head):
    cosine = angles[:, : KEY // 2]
    sine = angles[:, KEY // 2 :]
    query_at = head * KEY
    key_at = (heads + head) * KEY
    value_at = 2 * heads * KEY + head * VAL
    query = turn(field_ref[:, query_at : query_at + KEY].astype(f32), cosine, sine).astype(bf16)
    key = turn(field_ref[:, key_at : key_at + KEY].astype(f32), cosine, sine)
    key = (key * key_scale).astype(bf16)
    return query, key, field_ref[:, value_at : value_at + VAL]


def retention_forward(heads, which, field_ref, gate_ref, angle_ref, info_ref, row_ref, decay_ref, gated_ref, grouped_ref, scale_ref, past_ref, state_ref):
    @pl.when(pl.program_id(0) == 0)
    def _():
        state_ref[...] = jnp.zeros_like(state_ref)

    angles = angle_ref[...]
    info = info_ref[...]
    same = info[:, 0:1] == row_ref[0]
    scales = []
    for head in range(heads):
        query, key, value = head_parts(field_ref, angles, heads, head)
        columns = slice(head * VAL, (head + 1) * VAL)
        gate = gate_ref[:, columns].astype(f32)
        into = info[:, 1 + 2 * head : 2 + 2 * head]
        onward = info[:, 2 + 2 * head : 3 + 2 * head]
        state = state_ref[head]
        past_ref[0, head] = state.astype(bf16)
        scores = dot_nt(query, key)
        weights = (jnp.where(same, decay_ref[head], 0.0) * scores).astype(bf16)
        retained = dot_nn(weights, value) + into * dot_nn(query, state.astype(bf16))
        moved = (key.astype(f32) * onward).astype(bf16)
        state_ref[head] = into[CHUNK - 1 :, :] * state + dot_tn(moved, value)
        centred = retained - jnp.mean(retained, axis=-1, keepdims=True)
        scale = lax.rsqrt(jnp.mean(centred * centred, axis=-1, keepdims=True) + group_floor)
        grouped = centred * scale
        gated = gate / (1.0 + jnp.exp(-gate)) * grouped
        gated_ref[:, columns] = gated.astype(bf16)
        grouped_ref[:, columns] = grouped.astype(bf16)
        scales.append(scale)
    lane = lax.broadcasted_iota(jnp.int32, (CHUNK, 128), 1)
    spread = jnp.zeros((CHUNK, 128), f32)
    for head in range(heads):
        spread = jnp.where(lane == head, scales[head], spread)
    scale_ref[...] = spread


def retention_backward(heads, which, field_ref, gate_ref, angle_ref, info_ref, row_ref, decay_ref, grad_ref, grouped_ref, scale_ref, past_ref, back_ref, state_ref):
    @pl.when(pl.program_id(0) == 0)
    def _():
        state_ref[...] = jnp.zeros_like(state_ref)

    angles = angle_ref[...]
    cosine = angles[:, : KEY // 2]
    sine = angles[:, KEY // 2 :]
    info = info_ref[...]
    same = info[:, 0:1] == row_ref[0]
    for head in range(heads):
        query, key, value = head_parts(field_ref, angles, heads, head)
        columns = slice(head * VAL, (head + 1) * VAL)
        gate = gate_ref[:, columns].astype(f32)
        into = info[:, 1 + 2 * head : 2 + 2 * head]
        onward = info[:, 2 + 2 * head : 3 + 2 * head]
        grouped = grouped_ref[:, columns].astype(f32)
        scale = scale_ref[:, head : head + 1]
        c = grad_ref[:, columns].astype(f32) * (gate / (1.0 + jnp.exp(-gate)))
        mean_c = jnp.mean(c, axis=-1, keepdims=True)
        mean_cx = jnp.mean(c * grouped, axis=-1, keepdims=True)
        out_grad = (scale * (c - mean_c - grouped * mean_cx)).astype(bf16)
        state = state_ref[head]
        state_low = state.astype(bf16)
        past = past_ref[0, head]
        masked = jnp.where(same, decay_ref[head], 0.0)
        weights = (masked * dot_nt(query, key)).astype(bf16)
        score_grad = (masked * dot_nt(out_grad, value)).astype(bf16)
        value_grad = dot_tn(weights, out_grad) + onward * dot_nn(key, state_low)
        query_grad = dot_nn(score_grad, key) + into * dot_nt(out_grad, past)
        key_grad = dot_tn(score_grad, query) + onward * dot_nt(value, state_low)
        moved = (query.astype(f32) * into).astype(bf16)
        state_ref[head] = into[CHUNK - 1 :, :] * state + dot_tn(moved, out_grad)
        query_at = head * KEY
        key_at = (heads + head) * KEY
        value_at = 2 * heads * KEY + head * VAL
        back_ref[:, query_at : query_at + KEY] = turn_back(query_grad, cosine, sine).astype(bf16)
        back_ref[:, key_at : key_at + KEY] = (turn_back(key_grad, cosine, sine) * key_scale).astype(bf16)
        back_ref[:, value_at : value_at + VAL] = value_grad.astype(bf16)


def retention_tables(segment, heads, first_head):
    rows = segment.shape[0]
    chunks = rows // CHUNK
    index = jnp.arange(rows, dtype=jnp.int32)
    boundary = jnp.concatenate([jnp.ones((1,), jnp.int32), (segment[1:] != segment[:-1]).astype(jnp.int32)])
    position = index - lax.cummax(jnp.where(boundary > 0, index, 0), axis=0)
    half = KEY // 2
    frequency = jnp.exp(-jnp.log(10000.0) * jnp.arange(half, dtype=f32) / half)
    angles = position.astype(f32)[:, None] * frequency[None, :]
    angles = jnp.concatenate([jnp.cos(angles), jnp.sin(angles)], axis=1)
    head_ids = (first_head + jnp.arange(heads, dtype=jnp.int32)).astype(f32)
    log_decay = jnp.log1p(-jnp.exp2(-5.0 - head_ids))
    last = segment.reshape(chunks, CHUNK)[:, -1]
    before = jnp.concatenate([jnp.full((1,), -2, jnp.int32), last[:-1]])
    offset = (index % CHUNK).astype(f32)
    linked_in = (segment == jnp.repeat(before, CHUNK)) & (segment >= 0)
    linked_on = (segment == jnp.repeat(last, CHUNK)) & (segment >= 0)
    columns = [segment.astype(f32)]
    for head in range(heads):
        columns.append(jnp.where(linked_in, jnp.exp(log_decay[head] * (offset + 1.0)), 0.0))
        columns.append(jnp.where(linked_on, jnp.exp(log_decay[head] * (CHUNK - 1.0 - offset)), 0.0))
    info = jnp.stack(columns, axis=1)
    info = jnp.pad(info, ((0, 0), (0, 128 - info.shape[1])))
    keys = jnp.where(segment >= 0, segment, -7).astype(f32).reshape(chunks, 1, CHUNK)
    distance = (jnp.arange(CHUNK)[:, None] - jnp.arange(CHUNK)[None, :]).astype(f32)
    decay = jnp.where(distance >= 0, jnp.exp(log_decay[:, None, None] * jnp.maximum(distance, 0.0)), 0.0)
    return angles, info, keys, decay


def retention_call(backward, which, piece_rows, heads, field, gate, tables, extra):
    rows = field.shape[0]
    chunks = rows // CHUNK
    angles, info, keys, decay = tables
    per_piece = piece_rows // CHUNK

    def step(i):
        return chunks - 1 - i if backward else i

    def place(i, which_ref):
        c = step(i)
        return ((c // per_piece) ^ which_ref[0]) * per_piece + c % per_piece

    def placed(width):
        return pl.BlockSpec((CHUNK, width), lambda i, w: (place(i, w), 0))

    in_specs = [
        placed(heads * QKV),
        placed(heads * VAL),
        pl.BlockSpec((CHUNK, KEY), lambda i, w: (step(i), 0)),
        pl.BlockSpec((CHUNK, 128), lambda i, w: (step(i), 0)),
        pl.BlockSpec((1, 1, CHUNK), lambda i, w: (step(i), 0, 0)),
        pl.BlockSpec((heads, CHUNK, CHUNK), lambda i, w: (0, 0, 0)),
    ]
    past_spec = pl.BlockSpec((1, heads, KEY, VAL), lambda i, w: (step(i), 0, 0, 0))
    if backward:
        in_specs += [placed(heads * VAL), placed(heads * VAL), placed(128), past_spec]
        out_specs = placed(heads * QKV)
        out_shape = jax.ShapeDtypeStruct((rows, heads * QKV), bf16)
    else:
        out_specs = [placed(heads * VAL), placed(heads * VAL), placed(128), past_spec]
        out_shape = [
            jax.ShapeDtypeStruct((rows, heads * VAL), bf16),
            jax.ShapeDtypeStruct((rows, heads * VAL), bf16),
            jax.ShapeDtypeStruct((rows, 128), f32),
            jax.ShapeDtypeStruct((chunks, heads, KEY, VAL), bf16),
        ]
    products = 15 if backward else 7
    return pl.pallas_call(
        functools.partial(retention_backward if backward else retention_forward, heads),
        grid_spec=pltpu.PrefetchScalarGridSpec(
            num_scalar_prefetch=1,
            grid=(chunks,),
            in_specs=in_specs,
            out_specs=out_specs,
            scratch_shapes=[pltpu.VMEM((heads, KEY, VAL), f32)],
        ),
        out_shape=out_shape,
        compiler_params=pltpu.CompilerParams(
            dimension_semantics=("arbitrary",), vmem_limit_bytes=48 * 1024 * 1024
        ),
        cost_estimate=pl.CostEstimate(
            flops=products * chunks * heads * 2 * CHUNK * CHUNK * CHUNK,
            bytes_accessed=(5 if backward else 4) * rows * heads * (QKV + VAL),
            transcendentals=rows * heads * VAL,
        ),
        name="retention_backward" if backward else "retention_forward",
    )(which, field, gate, angles, info, keys, decay, *extra)


MESH = pl.DeviceIdType.MESH


def opening_kernel(
    query_ref, key_ref, value_ref, gate_ref, token_ref, gain_ref, bias_ref, cot_ref,
    w_qkv_ref, w_gate_ref, normed_ref, cot_all_ref,
    w_qkv, w_gate, normed, token_own, cot_own, cot_got,
    local_sem, out_sem, up_send, up_recv, down_send, down_recv, core_send, core_recv, row_send, row_recv,
):
    dp = lax.axis_index("dp")
    tensor = lax.axis_index("tensor")
    z = lax.div(dp, 2)
    layers = lax.div(lax.axis_size("dp"), 2)
    shard_rows = query_ref.shape[0]
    rows = token_ref.shape[0]
    half = rows // 2
    above = (dp + 2, tensor)
    below = (dp - 2, tensor)
    twin = (dp + 1 - 2 * lax.rem(dp, 2), tensor)
    over_x = (dp, tensor + 1 - 2 * lax.rem(tensor, 2))
    over_y = (dp, lax.rem(tensor + 2, 4))

    keys = query_ref.shape[1]
    values = value_ref.shape[1]
    mine = pl.ds(pl.multiple_of(dp * shard_rows, shard_rows), shard_rows)
    places = [
        (query_ref, w_qkv.at[mine, pl.ds(0, keys)]),
        (key_ref, w_qkv.at[mine, pl.ds(keys, keys)]),
        (value_ref, w_qkv.at[mine, pl.ds(2 * keys, values)]),
        (gate_ref, w_gate.at[mine]),
        (token_ref, token_own),
        (cot_ref.at[pl.ds(0, half)], cot_own),
    ]
    local = [pltpu.make_async_copy(a, b, local_sem.at[i]) for i, (a, b) in enumerate(places)]
    for copy in local:
        copy.start()

    barrier = pltpu.get_barrier_semaphore()

    def greet(device):
        pl.semaphore_signal(barrier, inc=1, device_id=device, device_id_type=MESH)

    for device in (twin, over_x, over_y):
        greet(device)
    pl.when(z < layers - 1)(lambda: greet(above))
    pl.when(z > 0)(lambda: greet(below))
    pl.semaphore_wait(barrier, 3 + (z < layers - 1).astype(jnp.int32) + (z > 0).astype(jnp.int32))
    for copy in local[:4]:
        copy.wait()

    def weight_copies(shard, send_sem, recv_sem, step, device):
        place = pl.ds(pl.multiple_of(shard * shard_rows, shard_rows), shard_rows)
        return [
            pltpu.make_async_remote_copy(
                src_ref=ref.at[place], dst_ref=ref.at[place],
                send_sem=send_sem.at[step, i], recv_sem=recv_sem.at[step, i],
                device_id=device, device_id_type=MESH,
            )
            for i, ref in enumerate((w_qkv, w_gate))
        ]

    def shard_out(shard, slot):
        place = pl.ds(pl.multiple_of(shard * shard_rows, shard_rows), shard_rows)
        return [
            pltpu.make_async_copy(w_qkv.at[place], w_qkv_ref.at[place], out_sem.at[slot, 0]),
            pltpu.make_async_copy(w_gate.at[place], w_gate_ref.at[place], out_sem.at[slot, 1]),
        ]

    def start(copies):
        for copy in copies:
            copy.start()

    def wait_send(copies):
        for copy in copies:
            copy.wait_send()

    def wait_recv(copies):
        for copy in copies:
            copy.wait_recv()

    def up(j):
        return weight_copies(dp - 2 * j, up_send, up_recv, j, above)

    def down(j):
        return weight_copies(dp + 2 * j, down_send, down_recv, j, below)

    def to_twin(j):
        return weight_copies(dp + 2 * j, core_send, core_recv, j + 3, twin)

    def from_twin(j):
        return weight_copies(twin[0] + 2 * j, core_send, core_recv, j + 3, twin)

    def step(j):
        @pl.when(z - j >= 0)
        def _():
            wait_recv(weight_copies(dp - 2 * j, up_send, up_recv, j - 1, twin))
            if j < 3:
                pl.when(z < layers - 1)(lambda: start(up(j)))
            start(to_twin(-j))
            start(shard_out(dp - 2 * j, 3 - j))

        @pl.when(z + j < layers)
        def _():
            wait_recv(weight_copies(dp + 2 * j, down_send, down_recv, j - 1, twin))
            if j < 3:
                pl.when(z > 0)(lambda: start(down(j)))
            start(to_twin(j))
            start(shard_out(dp + 2 * j, 3 + j))

    pl.when(z < layers - 1)(lambda: start(up(0)))
    pl.when(z > 0)(lambda: start(down(0)))
    start(to_twin(0))
    start(shard_out(dp, 3))

    local[4].wait()

    @pl.loop(0, rows // 64)
    def _(i):
        block = pl.ds(pl.multiple_of(i * 64, 64), 64)
        unit, _ = normalize(token_own[block, :].astype(f32))
        normed[block, :] = (unit * gain_ref[...] + bias_ref[...]).astype(bf16)

    def row_copy(index, src, dst, device):
        return pltpu.make_async_remote_copy(
            src_ref=src, dst_ref=dst, send_sem=row_send.at[index], recv_sem=row_recv.at[index],
            device_id=device, device_id_type=MESH,
        )

    local[5].wait()
    over = [
        row_copy(0, normed.at[pl.ds(0, rows)], normed.at[pl.ds(rows, rows)], over_x),
        row_copy(1, normed.at[pl.ds(0, rows)], normed.at[pl.ds(2 * rows, rows)], over_y),
    ]
    start(over)
    step(1)
    wait_recv(over)
    onward = [
        row_copy(2, normed.at[pl.ds(2 * rows, half)], normed.at[pl.ds(3 * rows, half)], over_x),
        row_copy(3, normed.at[pl.ds(rows + half, half)], normed.at[pl.ds(3 * rows + half, half)], over_y),
    ]
    start(onward)
    cots = [
        row_copy(4, cot_own, cot_got.at[0], over_x),
        row_copy(5, cot_own, cot_got.at[1], over_y),
    ]
    start(cots)
    step(2)
    wait_recv(onward)
    normed_out = pltpu.make_async_copy(normed, normed_ref, local_sem.at[6])
    normed_out.start()
    wait_recv(cots)
    cot_out = pltpu.make_async_copy(cot_got, cot_all_ref, local_sem.at[7])
    cot_out.start()
    step(3)

    for j in range(-3, 4):
        @pl.when((z + j >= 0) & (z + j < layers))
        def _():
            wait_recv(from_twin(j))
            start(shard_out(twin[0] + 2 * j, 10 + j))
    wait_send(over + onward + cots)
    for j in range(3):
        pl.when((z < layers - 1) & (z - j >= 0))(lambda: wait_send(up(j)))
        pl.when((z > 0) & (z + j < layers))(lambda: wait_send(down(j)))
    normed_out.wait()
    cot_out.wait()
    for j in range(-3, 4):
        @pl.when((z + j >= 0) & (z + j < layers))
        def _():
            wait_send(to_twin(j))
            for copy in shard_out(dp + 2 * j, 3 + j) + shard_out(twin[0] + 2 * j, 10 + j):
                copy.wait()


def opening_exchange(query_weight, key_weight, value_weight, gate_weight, tokens, gain, bias, cotangent):
    dp = lax.axis_size("dp")
    depth, keys = query_weight.shape
    values = value_weight.shape[1]
    rows, width = tokens.shape
    anywhere = pl.BlockSpec(memory_space=pl.ANY)
    in_vmem = pl.BlockSpec(memory_space=pltpu.VMEM)
    return pl.pallas_call(
        opening_kernel,
        out_shape=[
            jax.ShapeDtypeStruct((dp * depth, 2 * keys + values), bf16),
            jax.ShapeDtypeStruct((dp * depth, values), bf16),
            jax.ShapeDtypeStruct((4 * rows, width), bf16),
            jax.ShapeDtypeStruct((2, rows // 2, width), bf16),
        ],
        in_specs=[anywhere] * 5 + [in_vmem] * 2 + [anywhere],
        out_specs=[anywhere] * 4,
        scratch_shapes=[
            pltpu.VMEM((dp * depth, 2 * keys + values), bf16),
            pltpu.VMEM((dp * depth, values), bf16),
            pltpu.VMEM((4 * rows, width), bf16),
            pltpu.VMEM((rows, width), bf16),
            pltpu.VMEM((rows // 2, width), bf16),
            pltpu.VMEM((2, rows // 2, width), bf16),
            pltpu.SemaphoreType.DMA((8,)),
            pltpu.SemaphoreType.DMA((14, 2)),
            pltpu.SemaphoreType.DMA((3, 2)),
            pltpu.SemaphoreType.DMA((3, 2)),
            pltpu.SemaphoreType.DMA((3, 2)),
            pltpu.SemaphoreType.DMA((3, 2)),
            pltpu.SemaphoreType.DMA((7, 2)),
            pltpu.SemaphoreType.DMA((7, 2)),
            pltpu.SemaphoreType.DMA((6,)),
            pltpu.SemaphoreType.DMA((6,)),
        ],
        compiler_params=pltpu.CompilerParams(
            collective_id=2, has_side_effects=True, vmem_limit_bytes=60 * 1024 * 1024
        ),
        name="opening_exchange",
    )(query_weight, key_weight, value_weight, gate_weight, tokens, gain.reshape(1, width), bias.reshape(1, width), cotangent)


def opening(query_weight, key_weight, value_weight, gate_weight, tokens, gain, bias, cotangent, devices):
    if devices == 4 and lax.axis_size("dp") == 8:
        w_qkv, w_gate, normed1_all, cot_half = opening_exchange(
            query_weight, key_weight, value_weight, gate_weight, tokens, gain, bias, cotangent
        )
        half = tokens.shape[0] // 2
        rest = after(cotangent, cot_half)[half:]
        rest_x = tensor_permute(rest, 1)
        rest_y = tensor_permute(rest, 2)
        lower = tensor_permute(cot_half[1], 1)
        upper = tensor_permute(rest_x, 2)
        cots = [cotangent, cot_half[0], rest_x, cot_half[1], rest_y, lower, upper]
        return w_qkv, w_gate, normed1_all, cots, (rest_x, rest_y)
    w_qkv = lax.all_gather(jnp.concatenate([query_weight, key_weight, value_weight], axis=1), "dp", axis=0, tiled=True)
    w_gate = lax.all_gather(gate_weight, "dp", axis=0, tiled=True)
    unit, _ = normalize(tokens.astype(f32))
    normed1_all = jnp.concatenate(gather_pieces((unit * gain + bias).astype(bf16), devices), axis=0)
    cots = gather_pieces(cotangent, devices)
    return w_qkv, w_gate, normed1_all, cots, (cots[0],)


def middle_kernel(
    gated_ref, w_out_ref, up_ref, down_ref, cot_ref, token_ref, gain_ref, bias_ref,
    low_ref, plus_ref, feed_ref, up_grad_out, down_grad_out, late_ref,
    big, units, columns, staged, terms, half_in, full_in, mixed, plus, total,
    load_sem, column_sem, staged_sem, feed_sem, out_sem, up_send, up_recv, below_send, below_recv, core_send, core_recv,
    row_send, row_recv, half_send, half_recv, full_send, full_recv, half_free, full_free, big_free,
):
    dp = lax.axis_index("dp")
    tensor = lax.axis_index("tensor")
    z = lax.div(dp, 2)
    layers = 4
    rows = token_ref.shape[0]
    half = rows // 2
    width = token_ref.shape[1]
    unit = units.shape[2]
    depth = up_ref.shape[0]
    above = (dp + 2, tensor)
    below = (dp - 2, tensor)
    twin = (dp + 1 - 2 * lax.rem(dp, 2), tensor)
    over_x = (dp, tensor + 1 - 2 * lax.rem(tensor, 2))
    over_y = (dp, lax.rem(tensor + 2, 4))
    sides = (over_x, over_y)

    def block_of(start, count):
        return pl.ds(pl.multiple_of(start, count), count)

    def start(copies):
        for copy in copies:
            copy.start()

    def wait(copies):
        for copy in copies:
            copy.wait()

    def remote(src, dst, send, recv, device):
        return pltpu.make_async_remote_copy(
            src_ref=src, dst_ref=dst, send_sem=send, recv_sem=recv, device_id=device, device_id_type=MESH
        )

    mine = block_of(dp * depth, depth)
    shard_loads = [
        pltpu.make_async_copy(down_ref, units.at[3, mine], load_sem.at[0]),
        pltpu.make_async_copy(up_ref, units.at[2, mine], load_sem.at[1]),
    ]
    first_loads = [
        pltpu.make_async_copy(gated_ref, units.at[0], load_sem.at[2]),
        pltpu.make_async_copy(w_out_ref.at[:, pl.ds(0, unit)], units.at[1, pl.ds(0, unit)], load_sem.at[3]),
        pltpu.make_async_copy(w_out_ref.at[:, pl.ds(unit, unit)], units.at[1, pl.ds(unit, unit)], load_sem.at[4]),
    ]
    token_load = pltpu.make_async_copy(token_ref, plus, load_sem.at[5])
    cot_load = pltpu.make_async_copy(cot_ref, big, load_sem.at[6])
    start(shard_loads)
    start(first_loads)
    token_load.start()
    cot_load.start()

    barrier = pltpu.get_barrier_semaphore()

    def greet(device):
        pl.semaphore_signal(barrier, inc=1, device_id=device, device_id_type=MESH)

    for device in (twin, over_x, over_y):
        greet(device)
    pl.when(z < layers - 1)(lambda: greet(above))
    pl.when(z > 0)(lambda: greet(below))
    pl.semaphore_wait(barrier, 3 + (z < layers - 1).astype(jnp.int32) + (z > 0).astype(jnp.int32))


    def shard_copy(a, shard, send_sem, recv_sem, index, device):
        place = block_of(shard * depth, depth)
        ref = units.at[3 - a, place]
        return remote(ref, ref, send_sem.at[a, index], recv_sem.at[a, index], device)

    def rise(a, j):
        return shard_copy(a, dp - 2 * j, up_send, up_recv, j, above)

    def sink(a, j):
        return shard_copy(a, dp + 2 * j, below_send, below_recv, j, below)

    def to_twin(a, j):
        return shard_copy(a, dp + 2 * j, core_send, core_recv, j + 3, twin)

    def from_twin(a, j):
        return shard_copy(a, twin[0] + 2 * j, core_send, core_recv, j + 3, twin)

    def first_step(a):
        shard_loads[a].wait()
        pl.when(z < layers - 1)(lambda: rise(a, 0).start())
        pl.when(z > 0)(lambda: sink(a, 0).start())
        to_twin(a, 0).start()

    def step(a, j):
        @pl.when(z - j >= 0)
        def _():
            shard_copy(a, dp - 2 * j, up_send, up_recv, j - 1, twin).wait_recv()
            if j < 3:
                pl.when(z < layers - 1)(lambda: rise(a, j).start())
            to_twin(a, -j).start()

        @pl.when(z + j < layers)
        def _():
            shard_copy(a, dp + 2 * j, below_send, below_recv, j - 1, twin).wait_recv()
            if j < 3:
                pl.when(z > 0)(lambda: sink(a, j).start())
            to_twin(a, j).start()

    def gathered(a):
        for j in range(-3, 4):
            @pl.when((z + j >= 0) & (z + j < layers))
            def _():
                from_twin(a, j).wait_recv()


    def rows_of(r, first=0, count=rows):
        return pl.ds(r * rows + first, count)

    halves = [
        remote(terms.at[2, pl.ds(0, half)], half_in.at[0], half_send.at[0], half_recv.at[0], over_x),
        remote(terms.at[2, pl.ds(half, half)], half_in.at[1], half_send.at[1], half_recv.at[1], over_y),
    ]
    fulls = [
        remote(terms.at[0], full_in.at[0], full_send.at[0], full_recv.at[0], over_x),
        remote(terms.at[1], full_in.at[1], full_send.at[1], full_recv.at[1], over_y),
    ]
    lower, upper = (0, half), (half, half)

    def row_copy(index, source, first, target, device):
        return remote(
            big.at[rows_of(source, *first)], big.at[rows_of(target, *first)],
            row_send.at[index], row_recv.at[index], device,
        )

    early = [row_copy(0, 0, lower, 1, over_x), row_copy(1, 0, upper, 2, over_y)]
    across = [row_copy(2, 2, upper, 3, over_x), row_copy(3, 1, lower, 3, over_y)]
    late = [row_copy(4, 0, upper, 1, over_x), row_copy(5, 0, lower, 2, over_y)]

    def send_halves(stage):
        for i, copy in enumerate(halves):
            if stage == 1:
                pl.semaphore_wait(half_free.at[i], 1)
            copy.start()

    def take_halves(stage):
        for copy in halves:
            copy.wait_recv()
        for term, first, slot in ((1, 0, 0), (0, half, 1)):
            @pl.loop(0, half // 64)
            def _(i):
                place = block_of(first + i * 64, 64)
                grown = terms[term, place].astype(f32) + half_in[slot, block_of(i * 64, 64)].astype(f32)
                terms[term, place] = grown.astype(bf16)

        for i, copy in enumerate(fulls):
            if stage == 0:
                pl.semaphore_signal(half_free.at[i], inc=1, device_id=sides[i], device_id_type=MESH)
            else:
                pl.semaphore_wait(full_free.at[i], 1)
            copy.start()

    def slot_of(r):
        return (3, 0, 1, 2)[r]

    def branch_term(r):
        @pl.loop(0, width // 256)
        def _(j):
            top = lax.div(j, unit // 256) * unit
            inner = block_of(lax.rem(j, unit // 256) * 256, 256)
            term = dot_nn(units[0, rows_of(r)], units[1, pl.ds(pl.multiple_of(top, unit), unit), inner])
            terms[slot_of(r), :, block_of(j * 256, 256)] = term.astype(bf16)

    def feed_grads():
        @pl.loop(0, unit // 256)
        def _(j):
            tile = block_of(j * 256, 256)
            for r in range(4):
                units[4, rows_of(r), tile] = dot_nn(big[rows_of(r)], units[3, :, tile]).astype(bf16)

    def feed(r):
        @pl.loop(0, unit // 256)
        def _(j):
            tile = block_of(j * 256, 256)
            value, slope = gelu_both(dot_nn(big[rows_of(r)], units[2, :, tile]))
            units[0, rows_of(r), tile] = value.astype(bf16)
            units[1, rows_of(r), tile] = (units[4, rows_of(r), tile].astype(f32) * slope).astype(bf16)

    def back_term(r):
        @pl.loop(0, width // 256)
        def _(j):
            tile = block_of(j * 256, 256)
            terms[slot_of(r), :, tile] = dot_nt(units[1, rows_of(r)], units[2, tile]).astype(bf16)


    first_step(0)
    wait(first_loads)
    branch_term(3)
    send_halves(0)
    step(0, 1)
    branch_term(1)
    branch_term(2)
    step(0, 2)
    first_step(1)
    take_halves(0)
    branch_term(0)
    step(0, 3)
    cot_load.wait()
    gathered(0)
    feed_grads()
    for side in sides:
        pl.semaphore_signal(big_free, inc=1, device_id=side, device_id_type=MESH)
    step(1, 1)
    step(1, 2)
    step(1, 3)
    gathered(1)
    token_load.wait()
    for copy in fulls:
        copy.wait_recv()

    @pl.loop(0, rows // 64)
    def _(i):
        place = block_of(i * 64, 64)
        value = plus[place].astype(f32) + terms[3, place].astype(f32)
        value = value + full_in[0, place].astype(f32) + full_in[1, place].astype(f32)
        mixed[place] = value
        plain, _ = normalize(value)
        big[place] = (plain * gain_ref[...] + bias_ref[...]).astype(bf16)

    for i, side in enumerate(sides):
        pl.semaphore_signal(full_free.at[i], inc=1, device_id=side, device_id_type=MESH)
    pl.semaphore_wait(big_free, 2)
    start(early)
    feed(0)
    for copy in halves + fulls:
        copy.wait_send()
    back_term(0)
    for copy in early:
        copy.wait_recv()
    start(across)
    start(late)

    def cot_columns(t):
        return pltpu.make_async_copy(cot_ref.at[:, pl.ds(t * 512, 512)], columns.at[t % 2], column_sem.at[t])

    cot_columns(0).start()
    cot_columns(1).start()
    for copy in across:
        copy.wait_recv()
    feed(3)
    back_term(3)
    send_halves(1)
    for copy in late:
        copy.wait_recv()
    feed(1)
    feed(2)
    back_term(1)
    back_term(2)
    take_halves(1)

    def staged_out(out, t, slot):
        return pltpu.make_async_copy(staged.at[slot], out.at[pl.ds(t * 512, 512)], staged_sem.at[slot])

    def weight_grad(out, t, left_of, right):
        for j in range(unit // 256):
            tile = pl.ds(j * 256, 256)
            product = None
            for place in (pl.ds(0, 2 * rows), pl.ds(2 * rows, 2 * rows)):
                more = dot_tn(left_of(place), units[right, place, tile])
                product = more if product is None else product + more
            staged[t % 2, :, tile] = product.astype(bf16)
        staged_out(out, t, t % 2).start()

    for t in range(4):
        cot_columns(t).wait()
        if t >= 2:
            staged_out(down_grad_out, t - 2, t % 2).wait()
        weight_grad(down_grad_out, t, lambda place: columns[t % 2, place], 0)
        if t < 2:
            cot_columns(t + 2).start()
    for t in range(4):
        if t < 2:
            staged_out(down_grad_out, t + 2, t % 2).wait()
        else:
            staged_out(up_grad_out, t - 2, t % 2).wait()
        weight_grad(up_grad_out, t, lambda place: big[place, pl.ds(t * 512, 512)], 1)

    def feed_out(t):
        return pltpu.make_async_copy(columns.at[t % 2], feed_ref.at[:, pl.ds(t * 512, 512)], feed_sem.at[t % 2])

    for t in range(4):
        if t >= 2:
            feed_out(t - 2).wait()

        @pl.loop(0, 4)
        def _(r):
            place = block_of(r * rows, rows)
            columns[t % 2, place] = dot_nt(units[0, place], units[3, pl.ds(t * 512, 512)]).astype(bf16)

        feed_out(t).start()

        @pl.loop(0, rows // 64)
        def _(i):
            place = block_of(i * 64, 64)
            tile = pl.ds(t * 512, 512)
            plus[place, tile] = (mixed[place, tile] + columns[t % 2, place].astype(f32)).astype(bf16)

    plus_out = pltpu.make_async_copy(plus, plus_ref, out_sem.at[0])
    plus_out.start()
    for copy in halves:
        copy.wait_send()
    cot_own = pltpu.make_async_copy(cot_ref.at[pl.ds(0, rows)], terms.at[2], load_sem.at[7])
    cot_own.start()
    total[...] = jnp.zeros_like(total)
    cot_own.wait()
    for copy in fulls:
        copy.wait_recv()

    @pl.loop(0, rows // 64)
    def _(i):
        place = block_of(i * 64, 64)
        grad = terms[3, place].astype(f32) + full_in[0, place].astype(f32) + full_in[1, place].astype(f32)
        plain, scale = normalize(mixed[place])
        back = terms[2, place].astype(f32) + normalize_back(grad, plain, scale, gain_ref[...])
        full_in[0, place] = back.astype(bf16)
        total[0:1, :] += jnp.sum(grad * plain, axis=0, keepdims=True)
        total[1:2, :] += jnp.sum(grad, axis=0, keepdims=True)

    low_out = pltpu.make_async_copy(full_in.at[0], low_ref, out_sem.at[1])
    low_out.start()
    late_ref[...] = total[...]

    for t in (2, 3):
        staged_out(up_grad_out, t, t % 2).wait()
        feed_out(t).wait()
    for copy in fulls + early + across + late:
        copy.wait_send()
    for a in range(2):
        for j in range(3):
            pl.when((z < layers - 1) & (z - j >= 0))(lambda: rise(a, j).wait_send())
            pl.when((z > 0) & (z + j < layers))(lambda: sink(a, j).wait_send())
        for j in range(-3, 4):
            pl.when((z + j >= 0) & (z + j < layers))(lambda: to_twin(a, j).wait_send())
    plus_out.wait()
    low_out.wait()


def middle_exchange(gated, w_out, up_shard, down_shard, cot_all, tokens, gain, bias):
    token_rows, width = tokens.shape
    rows = 4 * token_rows
    unit = gated.shape[1]
    anywhere = pl.BlockSpec(memory_space=pl.ANY)
    in_vmem = pl.BlockSpec(memory_space=pltpu.VMEM)
    sem = pltpu.SemaphoreType.DMA
    regular = pltpu.SemaphoreType.REGULAR
    vmem = pltpu.VMEM
    return pl.pallas_call(
        middle_kernel,
        out_shape=[
            jax.ShapeDtypeStruct((token_rows, width), bf16),
            jax.ShapeDtypeStruct((token_rows, width), bf16),
            jax.ShapeDtypeStruct((rows, width), bf16),
            jax.ShapeDtypeStruct((width, unit), bf16),
            jax.ShapeDtypeStruct((width, unit), bf16),
            jax.ShapeDtypeStruct((2, width), f32),
        ],
        in_specs=[anywhere] * 6 + [in_vmem] * 2,
        out_specs=[anywhere] * 5 + [in_vmem],
        scratch_shapes=[
            vmem((rows, width), bf16),
            vmem((5, rows, unit), bf16),
            vmem((2, rows, 512), bf16),
            vmem((2, 512, unit), bf16),
            vmem((4, token_rows, width), bf16),
            vmem((2, token_rows // 2, width), bf16),
            vmem((2, token_rows, width), bf16),
            vmem((token_rows, width), f32),
            vmem((token_rows, width), bf16),
            vmem((2, width), f32),
            sem((8,)), sem((4,)), sem((2,)), sem((2,)), sem((2,)),
            sem((2, 3)), sem((2, 3)), sem((2, 3)), sem((2, 3)), sem((2, 7)), sem((2, 7)),
            sem((6,)), sem((6,)), sem((2,)), sem((2,)), sem((2,)), sem((2,)),
            regular((2,)), regular((2,)), regular,
        ],
        compiler_params=pltpu.CompilerParams(
            collective_id=4, has_side_effects=True, vmem_limit_bytes=63_400_000
        ),
        name="middle_exchange",
    )(gated, w_out, up_shard, down_shard, cot_all, tokens, gain.reshape(1, width), bias.reshape(1, width))


def closing_kernel(
    heads,
    normed1_ref, up_ref, down_ref, feed_ref, w_out_ref, w_qkv_ref, w_gate_ref,
    gate_ref, grouped_ref, gated_ref, scale_ref, field_ref, past_ref, angle_ref, info_ref,
    low_ref, plus_ref, token_ref, row_ref, decay_ref, gain_ref, late_ref,
    result_ref, grad_ref, query_out, key_out, value_out, gate_out, out_out, up_out, down_out, sums_ref,
    big, units, columns, terms, half_in, full_in, products, twin_in, line_in,
    state_ref, past_in, scale_in, angle_in, info_in, blocks, given, landed, total,
    unit_sem, column_sem, chunk_sem, block_sem, out_sem, mixed_sem, over_send, over_recv, onward_send, onward_recv,
    half_send, half_recv, full_send, full_recv, twin_send, twin_recv, line_send, line_recv, sum_send, sum_recv,
    twin_free, line_free, half_free, full_free,
):
    dp = lax.axis_index("dp")
    tensor = lax.axis_index("tensor")
    z = lax.div(dp, 2)
    core = lax.rem(dp, 2)
    rows = token_ref.shape[0]
    half = rows // 2
    width = token_ref.shape[1]
    unit = units.shape[2]
    depth = columns.shape[2] // 2
    at_end = (z == 0) | (z == 3)
    upper = z >= 2
    twin = (dp + 1 - 2 * core, tensor)
    over_x = (dp, tensor + 1 - 2 * lax.rem(tensor, 2))
    over_y = (dp, lax.rem(tensor + 2, 4))
    here = dp * 4 + tensor
    peers = 32
    last = 5

    def layer(index):
        return (2 * index + core, tensor)

    def seen(index):
        return jnp.where(upper, 3 - index, index)

    end = layer(seen(0))
    near = layer(seen(1))
    opposite = layer(seen(2))
    targets = [seen(3), seen(2), jnp.where(at_end, seen(1), seen(0)), z]

    def remote(src, dst, send, recv, device):
        return pltpu.make_async_remote_copy(
            src_ref=src, dst_ref=dst, send_sem=send, recv_sem=recv, device_id=device, device_id_type=MESH
        )

    def block_of(start, count):
        return pl.ds(pl.multiple_of(start, count), count)


    def whole(index, ref, sem):
        return [pltpu.make_async_copy(ref, units.at[index], unit_sem.at[sem])]

    def folded(index, ref, sem):
        return [
            pltpu.make_async_copy(ref.at[:, pl.ds(0, unit)], units.at[index, pl.ds(0, unit)], unit_sem.at[sem]),
            pltpu.make_async_copy(ref.at[:, pl.ds(unit, unit)], units.at[index, pl.ds(unit, unit)], unit_sem.at[sem + 1]),
        ]

    def part(index, ref, start, sem):
        return [pltpu.make_async_copy(ref.at[:, pl.ds(start, unit)], units.at[index], unit_sem.at[sem])]

    def start(copies):
        for copy in copies:
            copy.start()

    def wait(copies):
        for copy in copies:
            copy.wait()

    out_load = folded(3, w_out_ref, 4)
    feed_load = [
        pltpu.make_async_copy(feed_ref.at[pl.ds((i + 1) * rows, rows)], terms.at[i], unit_sem.at[i]) for i in range(3)
    ]
    gated_load = whole(2, gated_ref, 6)
    w_gate_load = whole(3, w_gate_ref, 7)
    w_value_load = part(2, w_qkv_ref, unit, 8)
    w_key_load = part(1, w_qkv_ref, 0, 9)


    sources = [up_ref, down_ref, normed1_ref, None, normed1_ref, normed1_ref]

    def given_copy(r, k):
        place = block_of(targets[k] * 2 * depth, 2 * depth)
        return pltpu.make_async_copy(sources[r].at[place], products.at[r, k], column_sem.at[4 * r + k])

    def column_copy(r, k):
        place = block_of(targets[k] * 2 * depth, 2 * depth)
        return pltpu.make_async_copy(sources[r].at[:, place], columns.at[k % 2], column_sem.at[k])

    def prefetch(r):
        column_copy(r, 0).start()
        column_copy(r, 1).start()

    mine = block_of(core * depth, depth)
    theirs = block_of((1 - core) * depth, depth)

    def to_twin(r, k):
        return remote(
            products.at[r % 2, k, theirs], twin_in.at[k % 2], twin_send.at[r % 2, k], twin_recv.at[k % 2], twin
        )

    def along(r, k, slot, device):
        return remote(
            products.at[r % 2, k, mine], line_in.at[slot], line_send.at[r % 2, k], line_recv.at[slot], device
        )

    def send_to_twin(r, k):
        if r >= 1 or k >= 2:
            pl.semaphore_wait(twin_free.at[k % 2], 1)
        to_twin(r, k).start()

    def multiply(r, k):
        to_twin(r - 2, k).wait_send()
        if k < 3:
            along(r - 2, k, 0, end).wait_send()
        else:
            wait(outputs(r - 2))
        if sources[r] is not None:
            column_copy(r, k).wait()

        @pl.loop(0, unit // 256)
        def _(j):
            tile = block_of(j * 256, 256)
            product = None
            for place in (pl.ds(0, 2 * rows), pl.ds(2 * rows, 2 * rows)):
                if r < 4:
                    right = units[(None, None, 0, 2)[r], place, tile]
                else:
                    right = big[place, block_of((r - 4) * unit + j * 256, 256)]
                if sources[r] is None:
                    left = big[place, block_of(targets[k] * 2 * depth, 2 * depth)]
                else:
                    left = columns[k % 2, place]
                more = dot_tn(left, right)
                product = more if product is None else product + more
            products[r % 2, k, :, tile] = product.astype(bf16)

        if sources[r] is not None and k + 2 < 4:
            column_copy(r, k + 2).start()
        send_to_twin(r, k)

    def add_to_mine(r, k, others):
        @pl.loop(0, depth // 64)
        def _(i):
            inner = block_of(core * depth + i * 64, 64)
            value = products[r % 2, k, inner].astype(f32)
            for ref, index in others:
                value = value + ref[index, block_of(i * 64, 64)].astype(f32)
            products[r % 2, k, inner] = value.astype(bf16)

    def settle(r, k):
        to_twin(r, k).wait_recv()
        add_to_mine(r, k, [(twin_in, k % 2)])
        if r < last or k < 2:
            pl.semaphore_signal(twin_free.at[k % 2], inc=1, device_id=twin, device_id_type=MESH)

    def push(r, k):
        @pl.when(at_end)
        def _():
            if r >= 1:
                pl.semaphore_wait(line_free.at[k], 1)
            along(r, k, k, near).start()

    def line_wait(slot):
        along(0, 0, slot, end).wait_recv()

    def used(device, index):
        pl.semaphore_signal(line_free.at[index], inc=1, device_id=device, device_id_type=MESH)

    def pass_on(r, which):
        arrived, sender, slot, device = ((0, end, 3, opposite), (1, end, 4, opposite), (3, opposite, 0, end))[which]

        @pl.when(jnp.logical_not(at_end))
        def _():
            line_wait(arrived)
            add_to_mine(r, which, [(line_in, arrived)])
            if r < last:
                used(sender, (0, 1, 0)[which])
            if r >= 1:
                pl.semaphore_wait(line_free.at[which], 1)
            along(r, which, slot, device).start()

    def outputs(r):
        keys = heads * KEY
        slot = products.at[r % 2, 3]
        if r == 4:
            return [
                pltpu.make_async_copy(slot.at[mine, pl.ds(0, keys)], query_out, out_sem.at[0, 0]),
                pltpu.make_async_copy(slot.at[mine, pl.ds(keys, keys)], key_out, out_sem.at[0, 1]),
            ]
        out = (up_out, down_out, gate_out, out_out, None, value_out)[r]
        return [pltpu.make_async_copy(slot.at[mine], out, out_sem.at[r % 2, 0])]

    def finish(r):
        @pl.when(at_end)
        def _():
            line_wait(0)
            add_to_mine(r, 3, [(line_in, 0)])
            if r < last:
                used(near, 2)

        @pl.when(jnp.logical_not(at_end))
        def _():
            line_wait(2)
            line_wait(4)
            add_to_mine(r, 3, [(line_in, 2), (line_in, 4)])
            if r < last:
                used(end, 2)
                used(opposite, 1)

        start(outputs(r))


    def rows_of(r, first=0, count=rows):
        return pl.ds(r * rows + first, count)

    over = [
        remote(big.at[rows_of(0)], big.at[rows_of(1)], over_send.at[0], over_recv.at[0], over_x),
        remote(big.at[rows_of(0)], big.at[rows_of(2)], over_send.at[1], over_recv.at[1], over_y),
    ]
    onward = [
        remote(big.at[rows_of(2, 0, half)], big.at[rows_of(3, 0, half)], onward_send.at[0], onward_recv.at[0], over_x),
        remote(big.at[rows_of(1, half, half)], big.at[rows_of(3, half, half)], onward_send.at[1], onward_recv.at[1], over_y),
    ]
    halves = [
        remote(terms.at[2, pl.ds(0, half)], half_in.at[0], half_send.at[0], half_recv.at[0], over_x),
        remote(terms.at[2, pl.ds(half, half)], half_in.at[1], half_send.at[1], half_recv.at[1], over_y),
    ]
    fulls = [
        remote(terms.at[0], full_in.at[0], full_send.at[0], full_recv.at[0], over_x),
        remote(terms.at[1], full_in.at[1], full_send.at[1], full_recv.at[1], over_y),
    ]
    sides = (over_x, over_y)

    def send_halves(stage):
        for i, copy in enumerate(halves):
            if stage == 1:
                pl.semaphore_wait(half_free.at[i], 1)
            copy.start()

    def take_halves(stage):
        for copy in halves:
            copy.wait_recv()
        for term, first, slot in ((1, 0, 0), (0, half, 1)):
            @pl.loop(0, half // 64)
            def _(i):
                place = block_of(first + i * 64, 64)
                grown = terms[term, place].astype(f32) + half_in[slot, block_of(i * 64, 64)].astype(f32)
                terms[term, place] = grown.astype(bf16)

        for i, copy in enumerate(fulls):
            if stage == 0:
                pl.semaphore_signal(half_free.at[i], inc=1, device_id=sides[i], device_id_type=MESH)
            else:
                pl.semaphore_wait(full_free.at[i], 1)
            copy.start()

    def project(r):
        slot = (2, 0, 1, 2)[r]

        @pl.loop(0, width // 256)
        def _(j):
            tile = block_of(j * 256, 256)
            term = dot_nt(big[rows_of(r), pl.ds(0, unit)], units[1, tile])
            term = term + dot_nt(big[rows_of(r), pl.ds(unit, unit)], units[2, tile])
            term = term + dot_nt(units[0, rows_of(r)], units[3, tile])
            terms[slot, :, tile] = term.astype(bf16)


    def gate_copies(r):
        return [
            pltpu.make_async_copy(
                ref.at[rows_of(r), pl.ds(h * VAL, VAL)],
                columns.at[r % 2, pl.ds((2 * i + h) * rows, rows)],
                chunk_sem.at[r % 2, 2 * i + h],
            )
            for i, ref in enumerate((gate_ref, grouped_ref))
            for h in range(heads)
        ]

    def gate_back(r):
        wait(gate_copies(r))

        @pl.loop(0, unit // 256)
        def _(j):
            grad = dot_nt(big[rows_of(r), pl.ds(0, unit)], units[3, block_of(j * 256, 256)])
            grad = grad + dot_nt(big[rows_of(r), pl.ds(unit, unit)], units[3, block_of(unit + j * 256, 256)])
            head = lax.div(j, VAL // 256)
            inner = block_of(lax.rem(j, VAL // 256) * 256, 256)
            raw = columns[r % 2, block_of(head * rows, rows), inner].astype(f32)
            grouped = columns[r % 2, block_of((heads + head) * rows, rows), inner].astype(f32)
            sigmoid = 1.0 / (1.0 + jnp.exp(-raw))
            tile = block_of(j * 256, 256)
            units[0, rows_of(r), tile] = (grad * grouped * (sigmoid * (1.0 + raw * (1.0 - sigmoid)))).astype(bf16)
            units[1, rows_of(r), tile] = grad.astype(bf16)

    chunks = 4 * rows // CHUNK
    per_piece = rows // CHUNK

    def chunk_place(c):
        piece = lax.div(c, per_piece)
        low = lax.rem(lax.rem(piece, 2) + lax.rem(tensor, 2), 2)
        high = lax.rem(lax.div(piece, 2) + lax.div(tensor, 2), 2)
        return (2 * high + low) * per_piece + lax.rem(c, per_piece)

    def chunk_copies(c, slot):
        place = block_of(chunk_place(c) * CHUNK, CHUNK)
        seat = block_of(c * CHUNK, CHUNK)
        keys = heads * KEY
        pieces = [
            (field_ref.at[place, pl.ds(0, keys)], columns.at[slot, pl.ds(0, CHUNK)]),
            (field_ref.at[place, pl.ds(keys, keys)], columns.at[slot, pl.ds(CHUNK, CHUNK)]),
        ]
        for h in range(heads):
            pieces.append((field_ref.at[place, pl.ds(2 * keys + h * VAL, VAL)], columns.at[slot, pl.ds((2 + h) * CHUNK, CHUNK)]))
            pieces.append((gate_ref.at[place, pl.ds(h * VAL, VAL)], columns.at[slot, pl.ds((4 + h) * CHUNK, CHUNK)]))
            pieces.append((grouped_ref.at[place, pl.ds(h * VAL, VAL)], columns.at[slot, pl.ds((6 + h) * CHUNK, CHUNK)]))
        pieces += [
            (past_ref.at[c], past_in.at[slot]),
            (scale_ref.at[place], scale_in.at[slot]),
            (angle_ref.at[seat], angle_in.at[slot]),
            (info_ref.at[seat], info_in.at[slot]),
        ]
        return [pltpu.make_async_copy(src, dst, chunk_sem.at[slot, i]) for i, (src, dst) in enumerate(pieces)]

    def retention_steps(between):
        @pl.loop(0, chunks)
        def _(step):
            c = chunks - 1 - step
            slot = lax.rem(step, 2)
            wait(chunk_copies(c, slot))

            @pl.when(step + 1 < chunks)
            def _():
                start(chunk_copies(c - 1, 1 - slot))

            place = block_of(chunk_place(c) * CHUNK, CHUNK)
            angles = angle_in[slot]
            cosine = angles[:, : KEY // 2]
            sine = angles[:, KEY // 2 :]
            info = info_in[slot]
            same = info[:, 0:1] == row_ref[c]

            for head in range(heads):
                at = pl.ds(head * KEY, KEY)
                query = turn(columns[slot, pl.ds(0, CHUNK), at].astype(f32), cosine, sine).astype(bf16)
                key = turn(columns[slot, pl.ds(CHUNK, CHUNK), at].astype(f32), cosine, sine)
                key = (key * key_scale).astype(bf16)
                value = columns[slot, pl.ds((2 + head) * CHUNK, CHUNK)]
                gate = columns[slot, pl.ds((4 + head) * CHUNK, CHUNK)].astype(f32)
                grouped = columns[slot, pl.ds((6 + head) * CHUNK, CHUNK)].astype(f32)
                into = info[:, 1 + 2 * head : 2 + 2 * head]
                onto = info[:, 2 + 2 * head : 3 + 2 * head]
                scale = scale_in[slot, :, head : head + 1]
                past = past_in[slot, head]
                out_grad_in = units[1, place, pl.ds(head * VAL, VAL)].astype(f32)
                c_in = out_grad_in * (gate / (1.0 + jnp.exp(-gate)))
                mean_c = jnp.mean(c_in, axis=-1, keepdims=True)
                mean_cx = jnp.mean(c_in * grouped, axis=-1, keepdims=True)
                out_grad = (scale * (c_in - mean_c - grouped * mean_cx)).astype(bf16)
                state = state_ref[head]
                state_low = state.astype(bf16)
                masked = jnp.where(same, decay_ref[head], 0.0)
                weights = (masked * dot_nt(query, key)).astype(bf16)
                score_grad = (masked * dot_nt(out_grad, value)).astype(bf16)
                value_grad = dot_tn(weights, out_grad) + onto * dot_nn(key, state_low)
                query_grad = dot_nn(score_grad, key) + into * dot_nt(out_grad, past)
                key_grad = dot_tn(score_grad, query) + onto * dot_nt(value, state_low)
                moved = (query.astype(f32) * into).astype(bf16)
                state_ref[head] = into[CHUNK - 1 :, :] * state + dot_tn(moved, out_grad)
                big[place, pl.ds(head * KEY, KEY)] = turn_back(query_grad, cosine, sine).astype(bf16)
                big[place, pl.ds((heads + head) * KEY, KEY)] = (turn_back(key_grad, cosine, sine) * key_scale).astype(bf16)
                big[place, pl.ds(2 * heads * KEY + head * VAL, VAL)] = value_grad.astype(bf16)

            between(step)


    def block_copy(ref, i, slot):
        return pltpu.make_async_copy(ref.at[block_of(i * 64, 64)], blocks.at[slot], block_sem.at[slot])

    def stream(ref, use):
        @pl.loop(0, rows // 64)
        def _(i):
            slot = lax.rem(i, 4)
            block_copy(ref, i, slot).wait()
            use(block_of(i * 64, 64), blocks[slot])

            @pl.when(i + 4 < rows // 64)
            def _():
                block_copy(ref, i + 4, slot).start()


    own_load = pltpu.make_async_copy(low_ref, big.at[rows_of(0)], mixed_sem.at[0])
    own_load.start()
    for r in range(2):
        for k in range(4):
            given_copy(r, k).start()
    start(out_load)
    start(gate_copies(0))
    start(gate_copies(1))
    start(feed_load)

    barrier = pltpu.get_barrier_semaphore()

    def partner(k):
        other = lax.rem(here + k, peers)
        return other, (lax.div(other, 4), lax.rem(other, 4))

    @pl.loop(1, peers)
    def _(k):
        pl.semaphore_signal(barrier, inc=1, device_id=partner(k)[1], device_id_type=MESH)

    pl.semaphore_wait(barrier, peers - 1)

    own_load.wait()
    start(over)
    for k in range(4):
        given_copy(0, k).wait()
        send_to_twin(0, k)
        if k > 0:
            settle(0, k - 1)
            push(0, k - 1)
    settle(0, 3)
    for k in range(4):
        given_copy(1, k).wait()
        send_to_twin(1, k)
        if k > 0:
            settle(1, k - 1)
    settle(1, 3)
    wait(out_load)
    gate_back(0)
    start(gate_copies(2))
    pass_on(0, 0)
    push(1, 0)
    pass_on(0, 1)
    push(1, 1)
    pass_on(0, 2)
    for copy in over:
        copy.wait_recv()
    start(onward)
    gate_back(1)
    start(gate_copies(3))
    finish(0)
    push(1, 2)
    gate_back(2)
    pass_on(1, 0)
    pass_on(1, 1)
    wait(feed_load)
    start(gated_load)
    for copy in onward:
        copy.wait_recv()
    send_halves(0)
    gate_back(3)
    prefetch(2)
    start(w_gate_load)
    pass_on(1, 2)
    state_ref[...] = jnp.zeros_like(state_ref)

    def produce(r, k, pushed=True):
        multiply(r, k)
        if k > 0:
            settle(r, k - 1)
            if pushed:
                push(r, k - 1)

    produce(2, 0)
    produce(2, 1)
    finish(1)
    produce(2, 2)
    produce(2, 3)
    settle(2, 3)
    start(chunk_copies(chunks - 1, 0))
    wait(gated_load)
    produce(3, 0)
    produce(3, 1, False)
    take_halves(0)
    pass_on(2, 0)
    push(3, 0)
    produce(3, 2, False)
    produce(3, 3, False)
    settle(3, 3)
    start(w_value_load)
    for copy in over + onward:
        copy.wait_send()

    def between(step):
        @pl.when(step == 1)
        def _():
            pass_on(2, 1)
            push(3, 1)

        @pl.when(step == 2)
        def _():
            pass_on(2, 2)

        @pl.when(step == 5)
        def _():
            finish(2)
            push(3, 2)

    retention_steps(between)
    start(w_key_load)
    prefetch(4)
    pass_on(3, 0)
    for copy in halves:
        copy.wait_send()
    wait(w_gate_load)
    wait(w_value_load)
    wait(w_key_load)
    project(3)
    send_halves(1)
    for i in range(4):
        block_copy(plus_ref, i, i).start()
    produce(4, 0)
    produce(4, 1)
    pass_on(3, 1)
    for copy in fulls:
        copy.wait_recv()

    def add_result(place, value):
        full_in[0, place] = (value.astype(f32) + full_in[0, place].astype(f32) + full_in[1, place].astype(f32)).astype(bf16)

    stream(plus_ref, add_result)
    result_copy = pltpu.make_async_copy(full_in.at[0], result_ref, mixed_sem.at[1])
    result_copy.start()
    for copy in fulls:
        copy.wait_send()
    pass_on(3, 2)
    project(1)
    result_copy.wait()
    for i, side in enumerate(sides):
        pl.semaphore_signal(full_free.at[i], inc=1, device_id=side, device_id_type=MESH)
    project(2)
    take_halves(1)
    finish(3)
    produce(4, 2)
    produce(4, 3, False)
    push(4, 2)
    settle(4, 3)
    prefetch(5)
    pass_on(4, 0)
    produce(5, 0)
    produce(5, 1)
    pass_on(4, 1)
    produce(5, 2)
    pass_on(4, 2)
    produce(5, 3, False)
    settle(5, 3)
    for copy in halves:
        copy.wait_send()
    project(0)
    finish(4)
    push(5, 2)
    pass_on(5, 0)
    pass_on(5, 1)
    for copy in fulls:
        copy.wait_recv()
        copy.wait_send()
    last_loads = [
        pltpu.make_async_copy(token_ref, terms.at[0], mixed_sem.at[2]),
        pltpu.make_async_copy(low_ref, terms.at[1], mixed_sem.at[0]),
    ]
    start(last_loads)
    total[...] = jnp.zeros_like(total)
    wait(last_loads)

    @pl.loop(0, rows // 64)
    def _(i):
        place = block_of(i * 64, 64)
        normed_grad = terms[2, place].astype(f32) + full_in[0, place].astype(f32) + full_in[1, place].astype(f32)
        plain, scale = normalize(terms[0, place].astype(f32))
        grad = terms[1, place].astype(f32) + normalize_back(normed_grad, plain, scale, gain_ref[...])
        full_in[0, place] = grad.astype(bf16)
        total[0:1, :] += jnp.sum(normed_grad * plain, axis=0, keepdims=True)
        total[1:2, :] += jnp.sum(normed_grad, axis=0, keepdims=True)

    grad_copy = pltpu.make_async_copy(full_in.at[0], grad_ref, mixed_sem.at[3])
    grad_copy.start()

    total[2:4, :] = late_ref[...]
    for k in range(peers // 2):
        given[k] = total[:, k * 128 : (k + 1) * 128]

    def sum_copy(k):
        other, device = partner(k)
        return remote(given.at[lax.div(other, 2)], landed.at[k], sum_send.at[k], sum_recv.at[k], device)

    @pl.loop(1, peers)
    def _(k):
        sum_copy(k).start()

    pass_on(5, 2)
    sums_ref[...] = given[lax.div(here, 2)]

    @pl.loop(1, peers)
    def _(k):
        sum_copy(k).wait()
        sums_ref[...] += landed[k]

    finish(5)

    for r in (4, 5):
        for k in range(4):
            to_twin(r, k).wait_send()
            if k < 3:
                along(r, k, 0, end).wait_send()
    wait(outputs(4) + outputs(5))
    grad_copy.wait()


def closing_exchange(heads, operands, small):
    token_rows, width = operands[-1].shape
    rows = 4 * token_rows
    depth = width // 8
    keys, values = heads * KEY, heads * VAL
    unit = operands[1].shape[1]
    anywhere = pl.BlockSpec(memory_space=pl.ANY)
    in_vmem = pl.BlockSpec(memory_space=pltpu.VMEM)
    sem = pltpu.SemaphoreType.DMA
    regular = pltpu.SemaphoreType.REGULAR
    vmem = pltpu.VMEM
    return pl.pallas_call(
        functools.partial(closing_kernel, heads),
        out_shape=[
            jax.ShapeDtypeStruct((token_rows, width), bf16),
            jax.ShapeDtypeStruct((token_rows, width), bf16),
            jax.ShapeDtypeStruct((depth, keys), bf16),
            jax.ShapeDtypeStruct((depth, keys), bf16),
            jax.ShapeDtypeStruct((depth, values), bf16),
            jax.ShapeDtypeStruct((depth, values), bf16),
            jax.ShapeDtypeStruct((depth, unit), bf16),
            jax.ShapeDtypeStruct((depth, unit), bf16),
            jax.ShapeDtypeStruct((depth, unit), bf16),
            jax.ShapeDtypeStruct((8, 128), f32),
        ],
        in_specs=[anywhere] * len(operands) + [in_vmem] * len(small),
        out_specs=[anywhere] * 9 + [in_vmem],
        scratch_shapes=[
            vmem((rows, width), bf16),
            vmem((4, rows, unit), bf16),
            vmem((2, rows, 2 * depth), bf16),
            vmem((3, token_rows, width), bf16),
            vmem((2, token_rows // 2, width), bf16),
            vmem((2, token_rows, width), bf16),
            vmem((2, 4, 2 * depth, unit), bf16),
            vmem((2, depth, unit), bf16),
            vmem((5, depth, unit), bf16),
            vmem((heads, KEY, VAL), f32),
            vmem((2, heads, KEY, VAL), bf16),
            vmem((2, CHUNK, 128), f32),
            vmem((2, CHUNK, KEY), f32),
            vmem((2, CHUNK, 128), f32),
            vmem((4, 64, width), bf16),
            vmem((16, 8, 128), f32),
            vmem((32, 8, 128), f32),
            vmem((8, width), f32),
            sem((10,)), sem((8,)), sem((2, 12)), sem((4,)), sem((2, 2)), sem((4,)),
            sem((2,)), sem((2,)), sem((2,)), sem((2,)),
            sem((2,)), sem((2,)), sem((2,)), sem((2,)),
            sem((2, 4)), sem((2,)), sem((2, 3)), sem((5,)), sem((32,)), sem((32,)),
            regular((2,)), regular((3,)), regular((2,)), regular((2,)),
        ],
        compiler_params=pltpu.CompilerParams(
            collective_id=3, has_side_effects=True, vmem_limit_bytes=63_400_000
        ),
        name="closing_exchange",
    )(*operands, *small)


def body(tokens, cotangent, segment, first_gain, first_bias, query_weight, key_weight, value_weight, gate_weight, out_weight, second_gain, second_bias, up_weight, down_weight):
    devices = lax.axis_size("tensor")
    rows = tokens.shape[0]
    heads = query_weight.shape[1] // KEY
    here = lax.axis_index("tensor")
    which = (here if devices == 4 else jnp.zeros_like(here)).astype(jnp.int32).reshape(1)

    def per_piece(values):
        return [values[i * rows : (i + 1) * rows] for i in range(devices)]

    w_qkv, w_gate, normed1_all, cots, cot_begun = opening(
        query_weight, key_weight, value_weight, gate_weight, tokens, first_gain, first_bias, cotangent, devices
    )
    w_out = lax.all_gather(after(out_weight, w_gate), "dp", axis=1, tiled=True)
    token_rows = tokens.astype(f32)
    down_shard = down_weight.T
    tables = retention_tables(segment, heads, here * heads)
    field = dot_nn(normed1_all, w_qkv).astype(bf16)
    gate = dot_nn(normed1_all, w_gate).astype(bf16)
    gated, grouped, group_scale, past = retention_call(
        False, which, rows, heads, field, after(gate, *cot_begun), tables, ()
    )
    cot_all = jnp.concatenate(cots, axis=0)
    angles, info, keys, decay = tables

    if devices == 4 and lax.axis_size("dp") == 8:
        mixed_low, plus, feed_terms, up_weight_grad, down_weight_grad, late = middle_exchange(
            gated, w_out, up_weight, down_shard, cot_all, tokens, second_gain, second_bias
        )
        result, input_grad, query_sum, key_sum, value_sum, gate_sum, out_sum, up_sum, down_sum, sums = closing_exchange(
            heads,
            (
                normed1_all, up_weight_grad, down_weight_grad, feed_terms, w_out, w_qkv, w_gate,
                gate, grouped, gated, group_scale, field, past, angles, info,
                mixed_low, plus, tokens,
            ),
            (keys, decay, first_gain.reshape(1, -1), late),
        )
        part = first_gain.shape[0] // 32
        sums = lax.dynamic_slice_in_dim(sums, (here % 2) * part, part, 1)
        norm_sums = [sums[0], sums[1], sums[2], sums[3]]
        query_sum, key_sum, value_sum, gate_sum, up_sum = (
            v.astype(f32) for v in (query_sum, key_sum, value_sum, gate_sum, up_sum)
        )
        out_sum, down_sum = out_sum.astype(f32).T, down_sum.astype(f32).T
    else:
        w_down = lax.all_gather(after(down_weight, w_out), "dp", axis=1, tiled=True)
        w_up = lax.all_gather(after(up_weight, w_down), "dp", axis=0, tiled=True)
        branch, begun, _ = scatter_sum([dot_nn(piece, w_out) for piece in per_piece(after(gated, *cots))])

        mixed = token_rows + branch
        unit2, scale2 = normalize(mixed)
        normed2 = (unit2 * second_gain + second_bias).astype(bf16)
        hidden_grads = per_piece(dot_nt(cot_all, after(w_down, normed2)).astype(bf16))

        def feed(piece, hidden_grad):
            value, slope = gelu_both(dot_nn(piece, w_up))
            return after((value.astype(bf16), (hidden_grad.astype(f32) * slope).astype(bf16)))

        fed_own = feed(normed2, hidden_grads[0])
        normed2_pieces = gather_pieces(normed2, devices, fed_own)
        fed = [fed_own] + [feed(piece, grad) for piece, grad in zip(normed2_pieces[1:-1], hidden_grads[1:-1])]
        fed.append(feed(after(normed2_pieces[-1], *fed), hidden_grads[-1]))
        hidden = [f[0] for f in fed]
        up_grad = [f[1] for f in fed]
        terms = [dot_nt(piece, w_up) for piece in up_grad]
        normed2_grad, _, _ = scatter_sum(terms)
        mixed_grad = cotangent.astype(f32) + normalize_back(normed2_grad, unit2, scale2, second_gain)
        gain2_grad = jnp.sum(normed2_grad * unit2, axis=0)
        bias2_grad = jnp.sum(normed2_grad, axis=0)
        mixed_low = mixed_grad.astype(bf16)
        hidden_all = jnp.concatenate(after(hidden, *terms), axis=0)
        normed2_all = jnp.concatenate(after(normed2_pieces, *terms), axis=0)
        up_grad_all = jnp.concatenate(after(up_grad, *terms), axis=0)
        feed_terms = dot_nn(hidden_all, w_down).astype(bf16)
        own_term = feed_terms[:rows].astype(f32)
        up_weight_grad = dot_tn(normed2_all, up_grad_all).astype(bf16)
        down_weight_grad = dot_tn(cot_all, hidden_all).astype(bf16)

        def summed(gradient, dimension):
            return lax.psum_scatter(
                gradient.astype(bf16), "dp", scatter_dimension=dimension, tiled=True
            ).astype(f32)

        up_sum = summed(up_weight_grad, 0)
        down_sum = summed(down_weight_grad, 0).T
        mixed_all = jnp.concatenate(gather_pieces(mixed_low, devices), axis=0)
        ffn, _, _ = scatter_sum([term.astype(f32) for term in per_piece(feed_terms)])
        result = (mixed + ffn).astype(bf16)
        gated_grad = dot_nt(mixed_all, w_out)
        raw = gate.astype(f32)
        sigmoid = 1.0 / (1.0 + jnp.exp(-raw))
        gate_grad = (gated_grad * grouped.astype(f32) * (sigmoid * (1.0 + raw * (1.0 - sigmoid)))).astype(bf16)
        back = retention_call(
            True, which, rows, heads, field, gate, tables, (gated_grad.astype(bf16), grouped, group_scale, past)
        )
        gate_sum = summed(dot_tn(normed1_all, gate_grad), 0)
        out_sum = summed(dot_tn(gated, mixed_all), 1)
        qkv_sum = summed(dot_tn(normed1_all, back), 0)
        keys_end = heads * KEY
        query_sum = qkv_sum[:, :keys_end]
        key_sum = qkv_sum[:, keys_end : 2 * keys_end]
        value_sum = qkv_sum[:, 2 * keys_end :]
        terms = [
            dot_nt(first, w_qkv) + dot_nt(second, w_gate) for first, second in zip(per_piece(back), per_piece(gate_grad))
        ]
        normed1_grad, _, _ = scatter_sum(terms)
        unit1, scale1 = normalize(token_rows)
        input_grad = (mixed_grad + normalize_back(normed1_grad, unit1, scale1, first_gain)).astype(bf16)
        gain1_grad = jnp.sum(normed1_grad * unit1, axis=0)
        bias1_grad = jnp.sum(normed1_grad, axis=0)
        norm_sums = spread_sum([gain1_grad, bias1_grad, gain2_grad, bias2_grad])
    return (
        result,
        input_grad,
        norm_sums[0],
        norm_sums[1],
        query_sum,
        key_sum,
        value_sum,
        gate_sum,
        out_sum,
        norm_sums[2],
        norm_sums[3],
        up_sum,
        down_sum,
    )


def solution(mesh):
    rows = P(("dp", "tensor"), None)
    vector = P(("dp", "tensor"))
    into = P("dp", "tensor")
    back = P("tensor", "dp")
    return jax.shard_map(
        body,
        mesh=mesh,
        in_specs=(rows, rows, P("dp"), P(), P(), into, into, into, into, back, P(), P(), into, back),
        out_specs=(rows, rows, vector, vector, into, into, into, into, back, vector, vector, into, back),
        check_vma=False,
    )
```

```python
import functools

import jax
import jax.numpy as jnp
from jax import lax
from jax.experimental import pallas as pl
from jax.experimental.pallas import tpu as pltpu
from jax.sharding import PartitionSpec as P

KEY = 256
VAL = 512
CHUNK = 256
QKV = 2 * KEY + VAL

norm_epsilon = 1e-05
group_floor = 0.5
key_scale = KEY ** (-0.5)

f32 = jnp.float32
bf16 = jnp.bfloat16


def dot_nn(left, right):
    return lax.dot_general(left, right, (((1,), (0,)), ((), ())), preferred_element_type=f32)


def dot_nt(left, right):
    return lax.dot_general(left, right, (((1,), (1,)), ((), ())), preferred_element_type=f32)


def dot_tn(left, right):
    return lax.dot_general(left, right, (((0,), (0,)), ((), ())), preferred_element_type=f32)


def tensor_permute(values, bit):
    pairs = [(i, i ^ bit) for i in range(4)]
    return lax.ppermute(values, "tensor", pairs)


def after(values, *tokens):
    return lax.optimization_barrier((values, tokens))[0]


def gather_pieces(own, devices, between=()):
    if devices != 4:
        whole = lax.all_gather(own, "tensor", axis=0, tiled=True)
        return list(jnp.split(whole, devices, axis=0))
    half = own.shape[0] // 2
    from_x = tensor_permute(own, 1)
    from_y = tensor_permute(own, 2)
    lower, upper = after((from_y[:half], from_x[half:]), *between)
    lower = tensor_permute(lower, 1)
    upper = tensor_permute(upper, 2)
    return [own, from_x, from_y, jnp.concatenate([lower, upper], axis=0)]


def scatter_sum(terms):
    if len(terms) != 4:
        stacked = jnp.concatenate([term.astype(bf16) for term in terms], axis=0)
        return lax.psum_scatter(stacked, "tensor", scatter_dimension=0, tiled=True).astype(f32), (stacked,), (stacked,)
    own, over_x, over_y, across = terms
    half = own.shape[0] // 2
    across = across.astype(bf16)
    first = tensor_permute(across[:half], 1)
    second = tensor_permute(across[half:], 2)
    over_y = jnp.concatenate([over_y[:half] + first.astype(f32), over_y[half:]], axis=0)
    over_x = jnp.concatenate([over_x[:half], over_x[half:] + second.astype(f32)], axis=0)
    by_x = tensor_permute(over_x.astype(bf16), 1)
    by_y = tensor_permute(over_y.astype(bf16), 2)
    return own + by_x.astype(f32) + by_y.astype(f32), (first, second), (by_x, by_y)


def spread_sum_kernel(tensor_devices, devices, given_ref, sum_ref, landed_ref, send_sem, recv_sem):
    here = lax.axis_index("dp") * tensor_devices + lax.axis_index("tensor")

    def partner(k):
        other = lax.rem(here + k, devices)
        return other, (lax.div(other, tensor_devices), lax.rem(other, tensor_devices))

    def copy(k):
        other, device = partner(k)
        return pltpu.make_async_remote_copy(
            src_ref=given_ref.at[other],
            dst_ref=landed_ref.at[k],
            send_sem=send_sem.at[k],
            recv_sem=recv_sem.at[k],
            device_id=device,
            device_id_type=pl.DeviceIdType.MESH,
        )

    barrier = pltpu.get_barrier_semaphore()

    @pl.loop(1, devices)
    def _(k):
        pl.semaphore_signal(barrier, inc=1, device_id=partner(k)[1], device_id_type=pl.DeviceIdType.MESH)

    pl.semaphore_wait(barrier, devices - 1)

    @pl.loop(1, devices)
    def _(k):
        copy(k).start()

    sum_ref[...] = given_ref[here]

    @pl.loop(1, devices)
    def _(k):
        copy(k).wait()
        sum_ref[...] += landed_ref[k]


def spread_sum(vectors):
    dp, tensor = lax.axis_size("dp"), lax.axis_size("tensor")
    devices = dp * tensor
    part = vectors[0].shape[0] // devices
    given = jnp.stack([v.reshape(devices, part) for v in vectors], axis=1)
    given = jnp.pad(given, ((0, 0), (0, 8 - len(vectors)), (0, 128 - part)))
    total = pl.pallas_call(
        functools.partial(spread_sum_kernel, tensor, devices),
        out_shape=jax.ShapeDtypeStruct((8, 128), f32),
        in_specs=[pl.BlockSpec(memory_space=pltpu.VMEM)],
        out_specs=pl.BlockSpec(memory_space=pltpu.VMEM),
        scratch_shapes=[
            pltpu.VMEM((devices, 8, 128), f32),
            pltpu.SemaphoreType.DMA((devices,)),
            pltpu.SemaphoreType.DMA((devices,)),
        ],
        compiler_params=pltpu.CompilerParams(collective_id=1, has_side_effects=True),
        name="spread_sum",
    )(given)
    return [total[i, :part] for i in range(len(vectors))]


def normalize(values):
    average = jnp.mean(values, axis=-1, keepdims=True)
    centred = values - average
    variance = jnp.mean(centred * centred, axis=-1, keepdims=True)
    scale = lax.rsqrt(variance + norm_epsilon)
    return centred * scale, scale


def normalize_back(normed_grad, unit, scale, gain):
    g = normed_grad * gain
    mean_g = jnp.mean(g, axis=-1, keepdims=True)
    mean_gx = jnp.mean(g * unit, axis=-1, keepdims=True)
    return scale * (g - mean_g - unit * mean_gx)


def gelu_both(values):
    inner = 0.7978845608 * (values + 0.044715 * values * values * values)
    t = jnp.tanh(inner)
    slope = 0.7978845608 * (1.0 + 3.0 * 0.044715 * values * values)
    return 0.5 * values * (1.0 + t), 0.5 * (1.0 + t) + 0.5 * values * (1.0 - t * t) * slope


def turn(block, cosine, sine):
    a = block[:, : KEY // 2]
    b = block[:, KEY // 2 :]
    return jnp.concatenate([a * cosine - b * sine, b * cosine + a * sine], axis=1)


def turn_back(block, cosine, sine):
    a = block[:, : KEY // 2]
    b = block[:, KEY // 2 :]
    return jnp.concatenate([a * cosine + b * sine, b * cosine - a * sine], axis=1)


def head_parts(field_ref, angles, heads, head):
    cosine = angles[:, : KEY // 2]
    sine = angles[:, KEY // 2 :]
    query_at = head * KEY
    key_at = (heads + head) * KEY
    value_at = 2 * heads * KEY + head * VAL
    query = turn(field_ref[:, query_at : query_at + KEY].astype(f32), cosine, sine).astype(bf16)
    key = turn(field_ref[:, key_at : key_at + KEY].astype(f32), cosine, sine)
    key = (key * key_scale).astype(bf16)
    return query, key, field_ref[:, value_at : value_at + VAL]


def retention_forward(heads, which, field_ref, gate_ref, angle_ref, info_ref, row_ref, decay_ref, gated_ref, grouped_ref, scale_ref, past_ref, state_ref):
    @pl.when(pl.program_id(0) == 0)
    def _():
        state_ref[...] = jnp.zeros_like(state_ref)

    angles = angle_ref[...]
    info = info_ref[...]
    same = info[:, 0:1] == row_ref[0]
    scales = []
    for head in range(heads):
        query, key, value = head_parts(field_ref, angles, heads, head)
        columns = slice(head * VAL, (head + 1) * VAL)
        gate = gate_ref[:, columns].astype(f32)
        into = info[:, 1 + 2 * head : 2 + 2 * head]
        onward = info[:, 2 + 2 * head : 3 + 2 * head]
        state = state_ref[head]
        past_ref[0, head] = state.astype(bf16)
        scores = dot_nt(query, key)
        weights = (jnp.where(same, decay_ref[head], 0.0) * scores).astype(bf16)
        retained = dot_nn(weights, value) + into * dot_nn(query, state.astype(bf16))
        moved = (key.astype(f32) * onward).astype(bf16)
        state_ref[head] = into[CHUNK - 1 :, :] * state + dot_tn(moved, value)
        centred = retained - jnp.mean(retained, axis=-1, keepdims=True)
        scale = lax.rsqrt(jnp.mean(centred * centred, axis=-1, keepdims=True) + group_floor)
        grouped = centred * scale
        gated = gate / (1.0 + jnp.exp(-gate)) * grouped
        gated_ref[:, columns] = gated.astype(bf16)
        grouped_ref[:, columns] = grouped.astype(bf16)
        scales.append(scale)
    lane = lax.broadcasted_iota(jnp.int32, (CHUNK, 128), 1)
    spread = jnp.zeros((CHUNK, 128), f32)
    for head in range(heads):
        spread = jnp.where(lane == head, scales[head], spread)
    scale_ref[...] = spread


def retention_backward(heads, which, field_ref, gate_ref, angle_ref, info_ref, row_ref, decay_ref, grad_ref, grouped_ref, scale_ref, past_ref, back_ref, state_ref):
    @pl.when(pl.program_id(0) == 0)
    def _():
        state_ref[...] = jnp.zeros_like(state_ref)

    angles = angle_ref[...]
    cosine = angles[:, : KEY // 2]
    sine = angles[:, KEY // 2 :]
    info = info_ref[...]
    same = info[:, 0:1] == row_ref[0]
    for head in range(heads):
        query, key, value = head_parts(field_ref, angles, heads, head)
        columns = slice(head * VAL, (head + 1) * VAL)
        gate = gate_ref[:, columns].astype(f32)
        into = info[:, 1 + 2 * head : 2 + 2 * head]
        onward = info[:, 2 + 2 * head : 3 + 2 * head]
        grouped = grouped_ref[:, columns].astype(f32)
        scale = scale_ref[:, head : head + 1]
        c = grad_ref[:, columns].astype(f32) * (gate / (1.0 + jnp.exp(-gate)))
        mean_c = jnp.mean(c, axis=-1, keepdims=True)
        mean_cx = jnp.mean(c * grouped, axis=-1, keepdims=True)
        out_grad = (scale * (c - mean_c - grouped * mean_cx)).astype(bf16)
        state = state_ref[head]
        state_low = state.astype(bf16)
        past = past_ref[0, head]
        masked = jnp.where(same, decay_ref[head], 0.0)
        weights = (masked * dot_nt(query, key)).astype(bf16)
        score_grad = (masked * dot_nt(out_grad, value)).astype(bf16)
        value_grad = dot_tn(weights, out_grad) + onward * dot_nn(key, state_low)
        query_grad = dot_nn(score_grad, key) + into * dot_nt(out_grad, past)
        key_grad = dot_tn(score_grad, query) + onward * dot_nt(value, state_low)
        moved = (query.astype(f32) * into).astype(bf16)
        state_ref[head] = into[CHUNK - 1 :, :] * state + dot_tn(moved, out_grad)
        query_at = head * KEY
        key_at = (heads + head) * KEY
        value_at = 2 * heads * KEY + head * VAL
        back_ref[:, query_at : query_at + KEY] = turn_back(query_grad, cosine, sine).astype(bf16)
        back_ref[:, key_at : key_at + KEY] = (turn_back(key_grad, cosine, sine) * key_scale).astype(bf16)
        back_ref[:, value_at : value_at + VAL] = value_grad.astype(bf16)


def retention_tables(segment, heads, first_head):
    rows = segment.shape[0]
    chunks = rows // CHUNK
    index = jnp.arange(rows, dtype=jnp.int32)
    boundary = jnp.concatenate([jnp.ones((1,), jnp.int32), (segment[1:] != segment[:-1]).astype(jnp.int32)])
    position = index - lax.cummax(jnp.where(boundary > 0, index, 0), axis=0)
    half = KEY // 2
    frequency = jnp.exp(-jnp.log(10000.0) * jnp.arange(half, dtype=f32) / half)
    angles = position.astype(f32)[:, None] * frequency[None, :]
    angles = jnp.concatenate([jnp.cos(angles), jnp.sin(angles)], axis=1)
    head_ids = (first_head + jnp.arange(heads, dtype=jnp.int32)).astype(f32)
    log_decay = jnp.log1p(-jnp.exp2(-5.0 - head_ids))
    last = segment.reshape(chunks, CHUNK)[:, -1]
    before = jnp.concatenate([jnp.full((1,), -2, jnp.int32), last[:-1]])
    offset = (index % CHUNK).astype(f32)
    linked_in = (segment == jnp.repeat(before, CHUNK)) & (segment >= 0)
    linked_on = (segment == jnp.repeat(last, CHUNK)) & (segment >= 0)
    columns = [segment.astype(f32)]
    for head in range(heads):
        columns.append(jnp.where(linked_in, jnp.exp(log_decay[head] * (offset + 1.0)), 0.0))
        columns.append(jnp.where(linked_on, jnp.exp(log_decay[head] * (CHUNK - 1.0 - offset)), 0.0))
    info = jnp.stack(columns, axis=1)
    info = jnp.pad(info, ((0, 0), (0, 128 - info.shape[1])))
    keys = jnp.where(segment >= 0, segment, -7).astype(f32).reshape(chunks, 1, CHUNK)
    distance = (jnp.arange(CHUNK)[:, None] - jnp.arange(CHUNK)[None, :]).astype(f32)
    decay = jnp.where(distance >= 0, jnp.exp(log_decay[:, None, None] * jnp.maximum(distance, 0.0)), 0.0)
    return angles, info, keys, decay


def retention_call(backward, which, piece_rows, heads, field, gate, tables, extra):
    rows = field.shape[0]
    chunks = rows // CHUNK
    angles, info, keys, decay = tables
    per_piece = piece_rows // CHUNK

    def step(i):
        return chunks - 1 - i if backward else i

    def place(i, which_ref):
        c = step(i)
        return ((c // per_piece) ^ which_ref[0]) * per_piece + c % per_piece

    def placed(width):
        return pl.BlockSpec((CHUNK, width), lambda i, w: (place(i, w), 0))

    in_specs = [
        placed(heads * QKV),
        placed(heads * VAL),
        pl.BlockSpec((CHUNK, KEY), lambda i, w: (step(i), 0)),
        pl.BlockSpec((CHUNK, 128), lambda i, w: (step(i), 0)),
        pl.BlockSpec((1, 1, CHUNK), lambda i, w: (step(i), 0, 0)),
        pl.BlockSpec((heads, CHUNK, CHUNK), lambda i, w: (0, 0, 0)),
    ]
    past_spec = pl.BlockSpec((1, heads, KEY, VAL), lambda i, w: (step(i), 0, 0, 0))
    if backward:
        in_specs += [placed(heads * VAL), placed(heads * VAL), placed(128), past_spec]
        out_specs = placed(heads * QKV)
        out_shape = jax.ShapeDtypeStruct((rows, heads * QKV), bf16)
    else:
        out_specs = [placed(heads * VAL), placed(heads * VAL), placed(128), past_spec]
        out_shape = [
            jax.ShapeDtypeStruct((rows, heads * VAL), bf16),
            jax.ShapeDtypeStruct((rows, heads * VAL), bf16),
            jax.ShapeDtypeStruct((rows, 128), f32),
            jax.ShapeDtypeStruct((chunks, heads, KEY, VAL), bf16),
        ]
    products = 15 if backward else 7
    return pl.pallas_call(
        functools.partial(retention_backward if backward else retention_forward, heads),
        grid_spec=pltpu.PrefetchScalarGridSpec(
            num_scalar_prefetch=1,
            grid=(chunks,),
            in_specs=in_specs,
            out_specs=out_specs,
            scratch_shapes=[pltpu.VMEM((heads, KEY, VAL), f32)],
        ),
        out_shape=out_shape,
        compiler_params=pltpu.CompilerParams(
            dimension_semantics=("arbitrary",), vmem_limit_bytes=48 * 1024 * 1024
        ),
        cost_estimate=pl.CostEstimate(
            flops=products * chunks * heads * 2 * CHUNK * CHUNK * CHUNK,
            bytes_accessed=(5 if backward else 4) * rows * heads * (QKV + VAL),
            transcendentals=rows * heads * VAL,
        ),
        name="retention_backward" if backward else "retention_forward",
    )(which, field, gate, angles, info, keys, decay, *extra)


MESH = pl.DeviceIdType.MESH


def opening_kernel(
    heads, query_ref, key_ref, value_ref, gate_ref, out_ref, token_ref, cot_ref, segment_ref, row_ref, rate_ref, gain_ref, bias_ref,
    w_qkv_ref, w_gate_ref, w_out_ref, normed_ref, cot_all_ref, field_ref, gate_raw_ref, gated_ref, grouped_ref, scale_ref, past_ref,
    angle_ref, info_ref, decay_ref,
    w_qkv, w_gate, w_out, normed, product, blocks, angles, info, decay, state, field_out, gate_out, gated_out, grouped_out,
    scale_out, past_out,
    local_sem, block_sem, out_sem, stage_sem, table_sem, up_send, up_recv, down_send, down_recv, core_send, core_recv,
    row_send, row_recv,
):
    dp = lax.axis_index("dp")
    tensor = lax.axis_index("tensor")
    z = lax.div(dp, 2)
    layers = 4
    depth = query_ref.shape[0]
    rows = token_ref.shape[0]
    half = rows // 2
    above = (dp + 2, tensor)
    below = (dp - 2, tensor)
    twin = (dp + 1 - 2 * lax.rem(dp, 2), tensor)
    over_x = (dp, tensor + 1 - 2 * lax.rem(tensor, 2))
    over_y = (dp, lax.rem(tensor + 2, 4))
    keys = heads * KEY
    values = heads * VAL

    def block_of(start, count):
        return pl.ds(pl.multiple_of(start, count), count)

    def start(copies):
        for copy in copies:
            copy.start()

    def wait(copies):
        for copy in copies:
            copy.wait()

    def remote(src, dst, send, recv, device):
        return pltpu.make_async_remote_copy(
            src_ref=src, dst_ref=dst, send_sem=send, recv_sem=recv, device_id=device, device_id_type=MESH
        )

    mine = block_of(dp * depth, depth)
    local = [
        pltpu.make_async_copy(src, dst, local_sem.at[i])
        for i, (src, dst) in enumerate((
            (query_ref, w_qkv.at[mine, pl.ds(0, keys)]),
            (key_ref, w_qkv.at[mine, pl.ds(keys, keys)]),
            (value_ref, w_qkv.at[mine, pl.ds(2 * keys, values)]),
            (gate_ref, w_gate.at[mine]),
            (out_ref, w_out.at[mine]),
            (segment_ref, info),
        ))
    ]
    start(local)

    def token_block(i, slot):
        return pltpu.make_async_copy(token_ref.at[block_of(i * 64, 64)], blocks.at[slot], block_sem.at[slot])

    for i in range(4):
        token_block(i, i).start()
    own_cot = pltpu.make_async_copy(cot_ref, cot_all_ref.at[pl.ds(0, rows)], local_sem.at[6])
    own_cot.start()

    barrier = pltpu.get_barrier_semaphore()

    def greet(device):
        pl.semaphore_signal(barrier, inc=1, device_id=device, device_id_type=MESH)

    for device in (twin, over_x, over_y):
        greet(device)
    pl.when(z < layers - 1)(lambda: greet(above))
    pl.when(z > 0)(lambda: greet(below))
    pl.semaphore_wait(barrier, 3 + (z < layers - 1).astype(jnp.int32) + (z > 0).astype(jnp.int32))
    wait(local[:5])


    groups = ((w_qkv, w_gate), (w_out,))

    def shard_copies(g, shard, send_sem, recv_sem, index, device):
        place = block_of(shard * depth, depth)
        return [
            remote(ref.at[place], ref.at[place], send_sem.at[index, i + 2 * g], recv_sem.at[index, i + 2 * g], device)
            for i, ref in enumerate(groups[g])
        ]

    def rise(g, j):
        return shard_copies(g, dp - 2 * j, up_send, up_recv, j, above)

    def sink(g, j):
        return shard_copies(g, dp + 2 * j, down_send, down_recv, j, below)

    def to_twin(g, j):
        return shard_copies(g, dp + 2 * j, core_send, core_recv, j + 3, twin)

    def from_twin(g, j):
        return shard_copies(g, twin[0] + 2 * j, core_send, core_recv, j + 3, twin)

    def wait_recv(copies):
        for copy in copies:
            copy.wait_recv()

    def wait_send(copies):
        for copy in copies:
            copy.wait_send()

    def first_step(g):
        pl.when(z < layers - 1)(lambda: start(rise(g, 0)))
        pl.when(z > 0)(lambda: start(sink(g, 0)))
        start(to_twin(g, 0))

    def step(g, j):
        @pl.when(z - j >= 0)
        def _():
            wait_recv(shard_copies(g, dp - 2 * j, up_send, up_recv, j - 1, twin))
            if j < 3:
                pl.when(z < layers - 1)(lambda: start(rise(g, j)))
            start(to_twin(g, -j))

        @pl.when(z + j < layers)
        def _():
            wait_recv(shard_copies(g, dp + 2 * j, down_send, down_recv, j - 1, twin))
            if j < 3:
                pl.when(z > 0)(lambda: start(sink(g, j)))
            start(to_twin(g, j))

    def twin_step(g, j):
        for signed in sorted({-j, j}):
            @pl.when((z + signed >= 0) & (z + signed < layers))
            def _():
                wait_recv(from_twin(g, signed))

    first_step(0)

    @pl.loop(0, rows // 64)
    def _(i):
        slot = lax.rem(i, 4)
        token_block(i, slot).wait()
        plain, _ = normalize(blocks[slot].astype(f32))
        normed[block_of(i * 64, 64), :] = (plain * gain_ref[...] + bias_ref[...]).astype(bf16)

        @pl.when(i + 4 < rows // 64)
        def _():
            token_block(i + 4, slot).start()

    def rows_of(r, first=0, count=rows):
        return pl.ds(r * rows + first, count)

    def row_copy(index, src, dst, device):
        return remote(src, dst, row_send.at[index], row_recv.at[index], device)

    over = [
        row_copy(0, normed.at[rows_of(0)], normed.at[rows_of(1)], over_x),
        row_copy(1, normed.at[rows_of(0)], normed.at[rows_of(2)], over_y),
    ]
    onward = [
        row_copy(2, normed.at[rows_of(2, 0, half)], normed.at[rows_of(3, 0, half)], over_x),
        row_copy(3, normed.at[rows_of(1, half, half)], normed.at[rows_of(3, half, half)], over_y),
    ]
    cot_over = [
        row_copy(4, cot_ref, cot_all_ref.at[rows_of(1)], over_x),
        row_copy(5, cot_ref, cot_all_ref.at[rows_of(2)], over_y),
    ]
    cot_onward = [
        row_copy(6, cot_all_ref.at[rows_of(2, 0, half)], cot_all_ref.at[rows_of(3, 0, half)], over_x),
        row_copy(7, cot_all_ref.at[rows_of(1, half, half)], cot_all_ref.at[rows_of(3, half, half)], over_y),
    ]
    start(over)

    local[5].wait()
    half_key = KEY // 2
    lanes = lax.broadcasted_iota(jnp.int32, (CHUNK, half_key), 1).astype(f32)
    frequency = jnp.exp(lanes * (-9.210340371976184 / half_key))
    chunks = 4 * rows // CHUNK

    @pl.loop(0, chunks)
    def _(c):
        seat = block_of(c * CHUNK, CHUNK)
        own = info[seat, 0:1]
        ranked = jnp.where(own < 0, 3.0, own)
        before = jnp.zeros((CHUNK, 1), f32)
        for other in range(chunks):
            seen = row_ref[other]
            seen = jnp.where(seen < 0, 3.0, seen)
            before = before + jnp.sum((seen < ranked).astype(f32), axis=1, keepdims=True)
        index = lax.broadcasted_iota(jnp.int32, (CHUNK, 1), 0) + c * CHUNK
        turned = (index.astype(f32) - before) * frequency
        angles[seat, 0:half_key] = jnp.cos(turned)
        angles[seat, half_key:KEY] = jnp.sin(turned)

    distance = lax.broadcasted_iota(jnp.int32, (CHUNK, CHUNK), 0) - lax.broadcasted_iota(jnp.int32, (CHUNK, CHUNK), 1)
    span = jnp.maximum(distance, 0).astype(f32)
    for head in range(heads):
        decay[head] = jnp.where(distance >= 0, jnp.exp(rate_ref[head : head + 1, 0:1] * span), 0.0)
    table_outs = [
        pltpu.make_async_copy(angles, angle_ref, table_sem.at[0]),
        pltpu.make_async_copy(decay, decay_ref, table_sem.at[1]),
    ]
    start(table_outs)


    at_end = (z == 0) | (z == 3)

    def seen_from_end(index):
        return jnp.where(z >= 2, 3 - index, index)

    order = [z, jnp.where(at_end, seen_from_end(1), seen_from_end(0)), seen_from_end(2), seen_from_end(3)]

    def project(r, s):
        deep = block_of(order[s] * 2 * depth, 2 * depth)

        @pl.loop(0, (2 * keys + values) // 512)
        def _(j):
            tile = block_of(j * 512, 512)
            more = dot_nn(normed[rows_of(r), deep], w_qkv[deep, tile])
            product[rows_of(r), tile] = more if s == 0 else product[rows_of(r), tile] + more

        @pl.loop(0, values // 512)
        def _(j):
            tile = block_of(j * 512, 512)
            more = dot_nn(normed[rows_of(r), deep], w_gate[deep, tile])
            place = block_of(2 * keys + values + j * 512, 512)
            product[rows_of(r), place] = more if s == 0 else product[rows_of(r), place] + more


    per_piece = rows // CHUNK

    def chunk_place(c):
        piece = lax.div(c, per_piece)
        low = lax.rem(lax.rem(piece, 2) + lax.rem(tensor, 2), 2)
        high = lax.rem(lax.div(piece, 2) + lax.div(tensor, 2), 2)
        return (2 * high + low) * per_piece + lax.rem(c, per_piece)

    def chunk_outs(c):
        place = block_of(chunk_place(c) * CHUNK, CHUNK)
        pairs = (
            (field_out, field_ref.at[place]),
            (gate_out, gate_raw_ref.at[place]),
            (gated_out, gated_ref.at[place]),
            (grouped_out, grouped_ref.at[place]),
            (scale_out, scale_ref.at[place]),
            (past_out, past_ref.at[c]),
        )
        return [pltpu.make_async_copy(src, dst, stage_sem.at[i]) for i, (src, dst) in enumerate(pairs)]

    def retention(between):
        state[...] = jnp.zeros_like(state)

        @pl.loop(0, chunks)
        def _(c):
            place = block_of(chunk_place(c) * CHUNK, CHUNK)
            seat = block_of(c * CHUNK, CHUNK)
            cosine = angles[seat, 0:half_key]
            sine = angles[seat, half_key:KEY]
            own = info[seat, 0:1]
            same = own == row_ref[c]
            entering = (own == row_ref[jnp.maximum(c - 1, 0)][:, CHUNK - 1 :]) & (c > 0)
            leaving = own == row_ref[c][:, CHUNK - 1 :]
            offset = lax.broadcasted_iota(jnp.int32, (CHUNK, 1), 0).astype(f32)
            lane = lax.broadcasted_iota(jnp.int32, (CHUNK, 128), 1)
            facts = jnp.where(lane == 0, own, 0.0)
            scales = jnp.zeros((CHUNK, 128), f32)

            @pl.when(c > 0)
            def _():
                wait(chunk_outs(c - 1))

            for head in range(heads):
                rate = rate_ref[head : head + 1, 0:1]
                into = jnp.where(entering, jnp.exp(rate * (offset + 1.0)), 0.0)
                onto = jnp.where(leaving, jnp.exp(rate * (CHUNK - 1.0 - offset)), 0.0)
                facts = jnp.where(lane == 1 + 2 * head, into, facts)
                facts = jnp.where(lane == 2 + 2 * head, onto, facts)
                query_raw = product[place, pl.ds(head * KEY, KEY)]
                key_raw = product[place, pl.ds(keys + head * KEY, KEY)]
                value = product[place, pl.ds(2 * keys + head * VAL, VAL)].astype(bf16)
                gate = product[place, pl.ds(2 * keys + values + head * VAL, VAL)]
                query_raw = query_raw.astype(bf16)
                key_raw = key_raw.astype(bf16)
                gate_low = gate.astype(bf16)
                field_out[:, pl.ds(head * KEY, KEY)] = query_raw
                field_out[:, pl.ds(keys + head * KEY, KEY)] = key_raw
                field_out[:, pl.ds(2 * keys + head * VAL, VAL)] = value
                gate_out[:, pl.ds(head * VAL, VAL)] = gate_low
                query = turn(query_raw.astype(f32), cosine, sine).astype(bf16)
                key = (turn(key_raw.astype(f32), cosine, sine) * key_scale).astype(bf16)
                memory = state[head]
                memory_low = memory.astype(bf16)
                past_out[head] = memory_low
                scores = dot_nt(query, key)
                weights = (jnp.where(same, decay[head], 0.0) * scores).astype(bf16)
                retained = dot_nn(weights, value) + into * dot_nn(query, memory_low)
                moved = (key.astype(f32) * onto).astype(bf16)
                state[head] = into[CHUNK - 1 :, :] * memory + dot_tn(moved, value)
                centred = retained - jnp.mean(retained, axis=-1, keepdims=True)
                scale = lax.rsqrt(jnp.mean(centred * centred, axis=-1, keepdims=True) + group_floor)
                grouped = centred * scale
                columns = pl.ds(head * VAL, VAL)
                gated_out[:, columns] = (gate / (1.0 + jnp.exp(-gate)) * grouped).astype(bf16)
                grouped_out[:, columns] = grouped.astype(bf16)
                scales = jnp.where(lane == head, scale, scales)
            info[seat, :] = facts
            scale_out[...] = scales
            start(chunk_outs(c))
            between(c)

        wait(chunk_outs(chunks - 1))


    twin_step(0, 0)
    project(0, 0)
    step(0, 1)
    twin_step(0, 1)
    project(0, 1)
    wait_recv(over)
    start(onward)
    start(cot_over)
    for r in (1, 2):
        for s in (0, 1):
            project(r, s)
    step(0, 2)
    first_step(1)
    twin_step(0, 2)
    for r in (0, 1, 2):
        project(r, 2)
    wait_recv(onward)
    normed_out = pltpu.make_async_copy(normed, normed_ref, local_sem.at[7])
    normed_out.start()
    for s in (0, 1, 2):
        project(3, s)
    step(0, 3)
    twin_step(0, 3)
    for r in range(4):
        project(r, 3)
    step(1, 1)
    w_outs = [
        pltpu.make_async_copy(w_qkv, w_qkv_ref, out_sem.at[0]),
        pltpu.make_async_copy(w_gate, w_gate_ref, out_sem.at[1]),
    ]
    start(w_outs)

    def between(c):
        @pl.when(c == 3)
        def _():
            wait_recv(cot_over)
            start(cot_onward)

        @pl.when(c == 4)
        def _():
            step(1, 2)

    retention(between)
    info_out = pltpu.make_async_copy(info, info_ref, table_sem.at[2])
    info_out.start()
    step(1, 3)
    for j in range(4):
        twin_step(1, j)
    w_out_out = pltpu.make_async_copy(w_out, w_out_ref, out_sem.at[2])
    w_out_out.start()
    wait_recv(cot_onward)

    wait_send(over + onward + cot_over + cot_onward)
    for g in range(2):
        for j in range(3):
            pl.when((z < layers - 1) & (z - j >= 0))(lambda: wait_send(rise(g, j)))
            pl.when((z > 0) & (z + j < layers))(lambda: wait_send(sink(g, j)))
        for j in range(-3, 4):
            pl.when((z + j >= 0) & (z + j < layers))(lambda: wait_send(to_twin(g, j)))
    wait(table_outs + w_outs + [normed_out, own_cot, info_out, w_out_out])


def opening_exchange(heads, shards, tokens, cotangent, segment, gain, bias):
    dp = lax.axis_size("dp")
    depth, keys = shards[0].shape
    values = shards[2].shape[1]
    unit = shards[4].shape[1]
    token_rows, width = tokens.shape
    rows = 4 * token_rows
    chunks = rows // CHUNK
    anywhere = pl.BlockSpec(memory_space=pl.ANY)
    in_vmem = pl.BlockSpec(memory_space=pltpu.VMEM)
    sem = pltpu.SemaphoreType.DMA
    vmem = pltpu.VMEM
    here = lax.axis_index("tensor") * heads
    head_ids = (here + jnp.arange(8, dtype=jnp.int32)).astype(f32)
    rates = jnp.broadcast_to(jnp.log1p(-jnp.exp2(-5.0 - head_ids))[:, None], (8, 128))
    wide_segment = jnp.broadcast_to(segment.astype(f32)[:, None], (rows, 128))
    row_segment = jnp.where(segment >= 0, segment, -7).astype(f32).reshape(chunks, 1, CHUNK)
    results = pl.pallas_call(
        functools.partial(opening_kernel, heads),
        out_shape=[
            jax.ShapeDtypeStruct((dp * depth, 2 * keys + values), bf16),
            jax.ShapeDtypeStruct((dp * depth, values), bf16),
            jax.ShapeDtypeStruct((dp * depth, unit), bf16),
            jax.ShapeDtypeStruct((rows, width), bf16),
            jax.ShapeDtypeStruct((rows, width), bf16),
            jax.ShapeDtypeStruct((rows, 2 * keys + values), bf16),
            jax.ShapeDtypeStruct((rows, values), bf16),
            jax.ShapeDtypeStruct((rows, values), bf16),
            jax.ShapeDtypeStruct((rows, values), bf16),
            jax.ShapeDtypeStruct((rows, 128), f32),
            jax.ShapeDtypeStruct((chunks, heads, KEY, VAL), bf16),
            jax.ShapeDtypeStruct((rows, KEY), f32),
            jax.ShapeDtypeStruct((rows, 128), f32),
            jax.ShapeDtypeStruct((heads, CHUNK, CHUNK), f32),
        ],
        in_specs=[anywhere] * 8 + [in_vmem] * 4,
        out_specs=[anywhere] * 14,
        scratch_shapes=[
            vmem((dp * depth, 2 * keys + values), bf16),
            vmem((dp * depth, values), bf16),
            vmem((dp * depth, unit), bf16),
            vmem((rows, width), bf16),
            vmem((rows, 2 * keys + 2 * values), f32),
            vmem((4, 64, width), bf16),
            vmem((rows, KEY), f32),
            vmem((rows, 128), f32),
            vmem((heads, CHUNK, CHUNK), f32),
            vmem((heads, KEY, VAL), f32),
            vmem((CHUNK, 2 * keys + values), bf16),
            vmem((CHUNK, values), bf16),
            vmem((CHUNK, values), bf16),
            vmem((CHUNK, values), bf16),
            vmem((CHUNK, 128), f32),
            vmem((heads, KEY, VAL), bf16),
            sem((8,)), sem((4,)), sem((3,)), sem((6,)), sem((3,)),
            sem((3, 3)), sem((3, 3)), sem((3, 3)), sem((3, 3)), sem((7, 3)), sem((7, 3)), sem((8,)), sem((8,)),
        ],
        compiler_params=pltpu.CompilerParams(
            collective_id=2, has_side_effects=True, vmem_limit_bytes=63_400_000
        ),
        name="opening_exchange",
    )(*shards, tokens, cotangent, wide_segment, row_segment, rates, gain.reshape(1, width), bias.reshape(1, width))
    return results, row_segment


def middle_kernel(
    gated_ref, w_out_ref, up_ref, down_ref, cot_ref, token_ref, gain_ref, bias_ref,
    low_ref, plus_ref, feed_ref, up_grad_out, down_grad_out, late_ref,
    big, units, columns, staged, terms, half_in, full_in, mixed, plus, total,
    load_sem, column_sem, staged_sem, feed_sem, out_sem, up_send, up_recv, below_send, below_recv, core_send, core_recv,
    row_send, row_recv, half_send, half_recv, full_send, full_recv, half_free, full_free, big_free,
):
    dp = lax.axis_index("dp")
    tensor = lax.axis_index("tensor")
    z = lax.div(dp, 2)
    layers = 4
    rows = token_ref.shape[0]
    half = rows // 2
    width = token_ref.shape[1]
    unit = units.shape[2]
    depth = up_ref.shape[0]
    above = (dp + 2, tensor)
    below = (dp - 2, tensor)
    twin = (dp + 1 - 2 * lax.rem(dp, 2), tensor)
    over_x = (dp, tensor + 1 - 2 * lax.rem(tensor, 2))
    over_y = (dp, lax.rem(tensor + 2, 4))
    sides = (over_x, over_y)

    def block_of(start, count):
        return pl.ds(pl.multiple_of(start, count), count)

    def start(copies):
        for copy in copies:
            copy.start()

    def wait(copies):
        for copy in copies:
            copy.wait()

    def remote(src, dst, send, recv, device):
        return pltpu.make_async_remote_copy(
            src_ref=src, dst_ref=dst, send_sem=send, recv_sem=recv, device_id=device, device_id_type=MESH
        )

    mine = block_of(dp * depth, depth)
    shard_loads = [
        pltpu.make_async_copy(down_ref, units.at[3, mine], load_sem.at[0]),
        pltpu.make_async_copy(up_ref, units.at[2, mine], load_sem.at[1]),
    ]
    first_loads = [
        pltpu.make_async_copy(gated_ref, units.at[0], load_sem.at[2]),
        pltpu.make_async_copy(w_out_ref, units.at[1], load_sem.at[3]),
    ]
    token_load = pltpu.make_async_copy(token_ref, plus, load_sem.at[5])
    cot_load = pltpu.make_async_copy(cot_ref, big, load_sem.at[6])
    start(shard_loads)
    start(first_loads)
    token_load.start()
    cot_load.start()

    barrier = pltpu.get_barrier_semaphore()

    def greet(device):
        pl.semaphore_signal(barrier, inc=1, device_id=device, device_id_type=MESH)

    for device in (twin, over_x, over_y):
        greet(device)
    pl.when(z < layers - 1)(lambda: greet(above))
    pl.when(z > 0)(lambda: greet(below))
    pl.semaphore_wait(barrier, 3 + (z < layers - 1).astype(jnp.int32) + (z > 0).astype(jnp.int32))


    def shard_copy(a, shard, send_sem, recv_sem, index, device):
        place = block_of(shard * depth, depth)
        ref = units.at[3 - a, place]
        return remote(ref, ref, send_sem.at[a, index], recv_sem.at[a, index], device)

    def rise(a, j):
        return shard_copy(a, dp - 2 * j, up_send, up_recv, j, above)

    def sink(a, j):
        return shard_copy(a, dp + 2 * j, below_send, below_recv, j, below)

    def to_twin(a, j):
        return shard_copy(a, dp + 2 * j, core_send, core_recv, j + 3, twin)

    def from_twin(a, j):
        return shard_copy(a, twin[0] + 2 * j, core_send, core_recv, j + 3, twin)

    def first_step(a):
        shard_loads[a].wait()
        pl.when(z < layers - 1)(lambda: rise(a, 0).start())
        pl.when(z > 0)(lambda: sink(a, 0).start())
        to_twin(a, 0).start()

    def step(a, j):
        @pl.when(z - j >= 0)
        def _():
            shard_copy(a, dp - 2 * j, up_send, up_recv, j - 1, twin).wait_recv()
            if j < 3:
                pl.when(z < layers - 1)(lambda: rise(a, j).start())
            to_twin(a, -j).start()

        @pl.when(z + j < layers)
        def _():
            shard_copy(a, dp + 2 * j, below_send, below_recv, j - 1, twin).wait_recv()
            if j < 3:
                pl.when(z > 0)(lambda: sink(a, j).start())
            to_twin(a, j).start()

    def gathered(a):
        for j in range(-3, 4):
            @pl.when((z + j >= 0) & (z + j < layers))
            def _():
                from_twin(a, j).wait_recv()


    def rows_of(r, first=0, count=rows):
        return pl.ds(r * rows + first, count)

    halves = [
        remote(terms.at[2, pl.ds(0, half)], half_in.at[0], half_send.at[0], half_recv.at[0], over_x),
        remote(terms.at[2, pl.ds(half, half)], half_in.at[1], half_send.at[1], half_recv.at[1], over_y),
    ]
    fulls = [
        remote(terms.at[0], full_in.at[0], full_send.at[0], full_recv.at[0], over_x),
        remote(terms.at[1], full_in.at[1], full_send.at[1], full_recv.at[1], over_y),
    ]
    lower, upper = (0, half), (half, half)

    def row_copy(index, source, first, target, device):
        return remote(
            big.at[rows_of(source, *first)], big.at[rows_of(target, *first)],
            row_send.at[index], row_recv.at[index], device,
        )

    early = [row_copy(0, 0, lower, 1, over_x), row_copy(1, 0, upper, 2, over_y)]
    across = [row_copy(2, 2, upper, 3, over_x), row_copy(3, 1, lower, 3, over_y)]
    late = [row_copy(4, 0, upper, 1, over_x), row_copy(5, 0, lower, 2, over_y)]

    def send_halves(stage):
        for i, copy in enumerate(halves):
            if stage == 1:
                pl.semaphore_wait(half_free.at[i], 1)
            copy.start()

    def take_halves(stage):
        for copy in halves:
            copy.wait_recv()
        for term, first, slot in ((1, 0, 0), (0, half, 1)):
            @pl.loop(0, half // 64)
            def _(i):
                place = block_of(first + i * 64, 64)
                grown = terms[term, place].astype(f32) + half_in[slot, block_of(i * 64, 64)].astype(f32)
                terms[term, place] = grown.astype(bf16)

        for i, copy in enumerate(fulls):
            if stage == 0:
                pl.semaphore_signal(half_free.at[i], inc=1, device_id=sides[i], device_id_type=MESH)
            else:
                pl.semaphore_wait(full_free.at[i], 1)
            copy.start()

    def slot_of(r):
        return (3, 0, 1, 2)[r]

    def branch_term(r):
        @pl.loop(0, width // 256)
        def _(j):
            tile = block_of(j * 256, 256)
            terms[slot_of(r), :, tile] = dot_nt(units[0, rows_of(r)], units[1, tile]).astype(bf16)

    def feed_grads():
        @pl.loop(0, unit // 256)
        def _(j):
            tile = block_of(j * 256, 256)
            for r in range(4):
                units[4, rows_of(r), tile] = dot_nn(big[rows_of(r)], units[3, :, tile]).astype(bf16)

    def feed(r):
        @pl.loop(0, unit // 256)
        def _(j):
            tile = block_of(j * 256, 256)
            value, slope = gelu_both(dot_nn(big[rows_of(r)], units[2, :, tile]))
            units[0, rows_of(r), tile] = value.astype(bf16)
            units[1, rows_of(r), tile] = (units[4, rows_of(r), tile].astype(f32) * slope).astype(bf16)

    def back_term(r):
        @pl.loop(0, width // 256)
        def _(j):
            tile = block_of(j * 256, 256)
            terms[slot_of(r), :, tile] = dot_nt(units[1, rows_of(r)], units[2, tile]).astype(bf16)


    first_step(0)
    wait(first_loads)
    branch_term(3)
    send_halves(0)
    step(0, 1)
    branch_term(1)
    branch_term(2)
    step(0, 2)
    first_step(1)
    take_halves(0)
    branch_term(0)
    step(0, 3)
    cot_load.wait()
    gathered(0)
    feed_grads()
    for side in sides:
        pl.semaphore_signal(big_free, inc=1, device_id=side, device_id_type=MESH)
    step(1, 1)
    step(1, 2)
    step(1, 3)
    gathered(1)
    token_load.wait()
    for copy in fulls:
        copy.wait_recv()

    @pl.loop(0, rows // 64)
    def _(i):
        place = block_of(i * 64, 64)
        value = plus[place].astype(f32) + terms[3, place].astype(f32)
        value = value + full_in[0, place].astype(f32) + full_in[1, place].astype(f32)
        mixed[place] = value
        plain, _ = normalize(value)
        big[place] = (plain * gain_ref[...] + bias_ref[...]).astype(bf16)

    for i, side in enumerate(sides):
        pl.semaphore_signal(full_free.at[i], inc=1, device_id=side, device_id_type=MESH)
    pl.semaphore_wait(big_free, 2)
    start(early)
    feed(0)
    for copy in halves + fulls:
        copy.wait_send()
    back_term(0)
    for copy in early:
        copy.wait_recv()
    start(across)
    start(late)

    def cot_columns(t):
        return pltpu.make_async_copy(cot_ref.at[:, pl.ds(t * 512, 512)], columns.at[t % 2], column_sem.at[t])

    cot_columns(0).start()
    cot_columns(1).start()
    for copy in across:
        copy.wait_recv()
    feed(3)
    back_term(3)
    send_halves(1)
    for copy in late:
        copy.wait_recv()
    feed(1)
    feed(2)
    back_term(1)
    back_term(2)
    take_halves(1)

    def staged_out(out, t, slot):
        return pltpu.make_async_copy(staged.at[slot], out.at[pl.ds(t * 512, 512)], staged_sem.at[slot])

    def weight_grad(out, t, left_of, right):
        for j in range(unit // 256):
            tile = pl.ds(j * 256, 256)
            product = None
            for place in (pl.ds(0, 2 * rows), pl.ds(2 * rows, 2 * rows)):
                more = dot_tn(left_of(place), units[right, place, tile])
                product = more if product is None else product + more
            staged[t % 2, :, tile] = product.astype(bf16)
        staged_out(out, t, t % 2).start()

    for t in range(4):
        cot_columns(t).wait()
        if t >= 2:
            staged_out(down_grad_out, t - 2, t % 2).wait()
        weight_grad(down_grad_out, t, lambda place: columns[t % 2, place], 0)
        if t < 2:
            cot_columns(t + 2).start()
    for t in range(4):
        if t < 2:
            staged_out(down_grad_out, t + 2, t % 2).wait()
        else:
            staged_out(up_grad_out, t - 2, t % 2).wait()
        weight_grad(up_grad_out, t, lambda place: big[place, pl.ds(t * 512, 512)], 1)

    def feed_out(t):
        return pltpu.make_async_copy(columns.at[t % 2], feed_ref.at[:, pl.ds(t * 512, 512)], feed_sem.at[t % 2])

    for t in range(4):
        if t >= 2:
            feed_out(t - 2).wait()

        @pl.loop(0, 4)
        def _(r):
            place = block_of(r * rows, rows)
            columns[t % 2, place] = dot_nt(units[0, place], units[3, pl.ds(t * 512, 512)]).astype(bf16)

        feed_out(t).start()

        @pl.loop(0, rows // 64)
        def _(i):
            place = block_of(i * 64, 64)
            tile = pl.ds(t * 512, 512)
            plus[place, tile] = (mixed[place, tile] + columns[t % 2, place].astype(f32)).astype(bf16)

    plus_out = pltpu.make_async_copy(plus, plus_ref, out_sem.at[0])
    plus_out.start()
    for copy in halves:
        copy.wait_send()
    cot_own = pltpu.make_async_copy(cot_ref.at[pl.ds(0, rows)], terms.at[2], load_sem.at[7])
    cot_own.start()
    total[...] = jnp.zeros_like(total)
    cot_own.wait()
    for copy in fulls:
        copy.wait_recv()

    @pl.loop(0, rows // 64)
    def _(i):
        place = block_of(i * 64, 64)
        grad = terms[3, place].astype(f32) + full_in[0, place].astype(f32) + full_in[1, place].astype(f32)
        plain, scale = normalize(mixed[place])
        back = terms[2, place].astype(f32) + normalize_back(grad, plain, scale, gain_ref[...])
        full_in[0, place] = back.astype(bf16)
        total[0:1, :] += jnp.sum(grad * plain, axis=0, keepdims=True)
        total[1:2, :] += jnp.sum(grad, axis=0, keepdims=True)

    low_out = pltpu.make_async_copy(full_in.at[0], low_ref, out_sem.at[1])
    low_out.start()
    late_ref[...] = total[...]

    for t in (2, 3):
        staged_out(up_grad_out, t, t % 2).wait()
        feed_out(t).wait()
    for copy in fulls + early + across + late:
        copy.wait_send()
    for a in range(2):
        for j in range(3):
            pl.when((z < layers - 1) & (z - j >= 0))(lambda: rise(a, j).wait_send())
            pl.when((z > 0) & (z + j < layers))(lambda: sink(a, j).wait_send())
        for j in range(-3, 4):
            pl.when((z + j >= 0) & (z + j < layers))(lambda: to_twin(a, j).wait_send())
    plus_out.wait()
    low_out.wait()


def middle_exchange(gated, w_out, up_shard, down_shard, cot_all, tokens, gain, bias):
    token_rows, width = tokens.shape
    rows = 4 * token_rows
    unit = gated.shape[1]
    anywhere = pl.BlockSpec(memory_space=pl.ANY)
    in_vmem = pl.BlockSpec(memory_space=pltpu.VMEM)
    sem = pltpu.SemaphoreType.DMA
    regular = pltpu.SemaphoreType.REGULAR
    vmem = pltpu.VMEM
    return pl.pallas_call(
        middle_kernel,
        out_shape=[
            jax.ShapeDtypeStruct((token_rows, width), bf16),
            jax.ShapeDtypeStruct((token_rows, width), bf16),
            jax.ShapeDtypeStruct((rows, width), bf16),
            jax.ShapeDtypeStruct((width, unit), bf16),
            jax.ShapeDtypeStruct((width, unit), bf16),
            jax.ShapeDtypeStruct((2, width), f32),
        ],
        in_specs=[anywhere] * 6 + [in_vmem] * 2,
        out_specs=[anywhere] * 5 + [in_vmem],
        scratch_shapes=[
            vmem((rows, width), bf16),
            vmem((5, rows, unit), bf16),
            vmem((2, rows, 512), bf16),
            vmem((2, 512, unit), bf16),
            vmem((4, token_rows, width), bf16),
            vmem((2, token_rows // 2, width), bf16),
            vmem((2, token_rows, width), bf16),
            vmem((token_rows, width), f32),
            vmem((token_rows, width), bf16),
            vmem((2, width), f32),
            sem((8,)), sem((4,)), sem((2,)), sem((2,)), sem((2,)),
            sem((2, 3)), sem((2, 3)), sem((2, 3)), sem((2, 3)), sem((2, 7)), sem((2, 7)),
            sem((6,)), sem((6,)), sem((2,)), sem((2,)), sem((2,)), sem((2,)),
            regular((2,)), regular((2,)), regular,
        ],
        compiler_params=pltpu.CompilerParams(
            collective_id=4, has_side_effects=True, vmem_limit_bytes=63_400_000
        ),
        name="middle_exchange",
    )(gated, w_out, up_shard, down_shard, cot_all, tokens, gain.reshape(1, width), bias.reshape(1, width))


def closing_kernel(
    heads,
    normed1_ref, up_ref, down_ref, feed_ref, w_out_ref, w_qkv_ref, w_gate_ref,
    gate_ref, grouped_ref, gated_ref, scale_ref, field_ref, past_ref, angle_ref, info_ref,
    low_ref, plus_ref, token_ref, row_ref, decay_ref, gain_ref, late_ref,
    result_ref, grad_ref, query_out, key_out, value_out, gate_out, out_out, up_out, down_out, sums_ref,
    big, units, columns, terms, half_in, full_in, products, twin_in, line_in,
    state_ref, past_in, scale_in, angle_in, info_in, blocks, given, landed, total,
    unit_sem, column_sem, chunk_sem, block_sem, out_sem, mixed_sem, over_send, over_recv, onward_send, onward_recv,
    half_send, half_recv, full_send, full_recv, twin_send, twin_recv, line_send, line_recv, sum_send, sum_recv,
    twin_free, line_free, half_free, full_free,
):
    dp = lax.axis_index("dp")
    tensor = lax.axis_index("tensor")
    z = lax.div(dp, 2)
    core = lax.rem(dp, 2)
    rows = token_ref.shape[0]
    half = rows // 2
    width = token_ref.shape[1]
    unit = units.shape[2]
    depth = columns.shape[2] // 2
    at_end = (z == 0) | (z == 3)
    upper = z >= 2
    twin = (dp + 1 - 2 * core, tensor)
    over_x = (dp, tensor + 1 - 2 * lax.rem(tensor, 2))
    over_y = (dp, lax.rem(tensor + 2, 4))
    here = dp * 4 + tensor
    peers = 32
    last = 5

    def layer(index):
        return (2 * index + core, tensor)

    def seen(index):
        return jnp.where(upper, 3 - index, index)

    end = layer(seen(0))
    near = layer(seen(1))
    opposite = layer(seen(2))
    targets = [seen(3), seen(2), jnp.where(at_end, seen(1), seen(0)), z]

    def remote(src, dst, send, recv, device):
        return pltpu.make_async_remote_copy(
            src_ref=src, dst_ref=dst, send_sem=send, recv_sem=recv, device_id=device, device_id_type=MESH
        )

    def block_of(start, count):
        return pl.ds(pl.multiple_of(start, count), count)


    def whole(index, ref, sem):
        return [pltpu.make_async_copy(ref, units.at[index], unit_sem.at[sem])]

    def part(index, ref, start, sem):
        return [pltpu.make_async_copy(ref.at[:, pl.ds(start, unit)], units.at[index], unit_sem.at[sem])]

    def start(copies):
        for copy in copies:
            copy.start()

    def wait(copies):
        for copy in copies:
            copy.wait()

    out_load = whole(3, w_out_ref, 4)
    feed_load = [
        pltpu.make_async_copy(feed_ref.at[pl.ds((i + 1) * rows, rows)], terms.at[i], unit_sem.at[i]) for i in range(3)
    ]
    gated_load = whole(2, gated_ref, 6)
    w_gate_load = whole(3, w_gate_ref, 7)
    w_value_load = part(2, w_qkv_ref, unit, 8)
    w_key_load = part(1, w_qkv_ref, 0, 9)


    sources = [up_ref, down_ref, normed1_ref, None, normed1_ref, normed1_ref]

    def given_copy(r, k):
        place = block_of(targets[k] * 2 * depth, 2 * depth)
        return pltpu.make_async_copy(sources[r].at[place], products.at[r, k], column_sem.at[4 * r + k])

    def column_copy(r, k):
        place = block_of(targets[k] * 2 * depth, 2 * depth)
        return pltpu.make_async_copy(sources[r].at[:, place], columns.at[k % 2], column_sem.at[k])

    def prefetch(r):
        column_copy(r, 0).start()
        column_copy(r, 1).start()

    mine = block_of(core * depth, depth)
    theirs = block_of((1 - core) * depth, depth)

    def to_twin(r, k):
        return remote(
            products.at[r % 2, k, theirs], twin_in.at[k % 2], twin_send.at[r % 2, k], twin_recv.at[k % 2], twin
        )

    def along(r, k, slot, device):
        return remote(
            products.at[r % 2, k, mine], line_in.at[slot], line_send.at[r % 2, k], line_recv.at[slot], device
        )

    def send_to_twin(r, k):
        if r >= 1 or k >= 2:
            pl.semaphore_wait(twin_free.at[k % 2], 1)
        to_twin(r, k).start()

    def multiply(r, k):
        to_twin(r - 2, k).wait_send()
        if k < 3:
            along(r - 2, k, 0, end).wait_send()
        else:
            wait(outputs(r - 2))
        if sources[r] is not None:
            column_copy(r, k).wait()

        @pl.loop(0, unit // 256)
        def _(j):
            tile = block_of(j * 256, 256)
            product = None
            for place in (pl.ds(0, 2 * rows), pl.ds(2 * rows, 2 * rows)):
                if r < 4:
                    right = units[(None, None, 0, 2)[r], place, tile]
                else:
                    right = big[place, block_of((r - 4) * unit + j * 256, 256)]
                if sources[r] is None:
                    left = big[place, block_of(targets[k] * 2 * depth, 2 * depth)]
                else:
                    left = columns[k % 2, place]
                more = dot_tn(left, right)
                product = more if product is None else product + more
            products[r % 2, k, :, tile] = product.astype(bf16)

        if sources[r] is not None and k + 2 < 4:
            column_copy(r, k + 2).start()
        send_to_twin(r, k)

    def add_to_mine(r, k, others):
        @pl.loop(0, depth // 64)
        def _(i):
            inner = block_of(core * depth + i * 64, 64)
            value = products[r % 2, k, inner].astype(f32)
            for ref, index in others:
                value = value + ref[index, block_of(i * 64, 64)].astype(f32)
            products[r % 2, k, inner] = value.astype(bf16)

    def settle(r, k):
        to_twin(r, k).wait_recv()
        add_to_mine(r, k, [(twin_in, k % 2)])
        if r < last or k < 2:
            pl.semaphore_signal(twin_free.at[k % 2], inc=1, device_id=twin, device_id_type=MESH)

    def push(r, k):
        @pl.when(at_end)
        def _():
            if r >= 1:
                pl.semaphore_wait(line_free.at[k], 1)
            along(r, k, k, near).start()

    def line_wait(slot):
        along(0, 0, slot, end).wait_recv()

    def used(device, index):
        pl.semaphore_signal(line_free.at[index], inc=1, device_id=device, device_id_type=MESH)

    def pass_on(r, which):
        arrived, sender, slot, device = ((0, end, 3, opposite), (1, end, 4, opposite), (3, opposite, 0, end))[which]

        @pl.when(jnp.logical_not(at_end))
        def _():
            line_wait(arrived)
            add_to_mine(r, which, [(line_in, arrived)])
            if r < last:
                used(sender, (0, 1, 0)[which])
            if r >= 1:
                pl.semaphore_wait(line_free.at[which], 1)
            along(r, which, slot, device).start()

    def outputs(r):
        keys = heads * KEY
        slot = products.at[r % 2, 3]
        if r == 4:
            return [
                pltpu.make_async_copy(slot.at[mine, pl.ds(0, keys)], query_out, out_sem.at[0, 0]),
                pltpu.make_async_copy(slot.at[mine, pl.ds(keys, keys)], key_out, out_sem.at[0, 1]),
            ]
        out = (up_out, down_out, gate_out, out_out, None, value_out)[r]
        return [pltpu.make_async_copy(slot.at[mine], out, out_sem.at[r % 2, 0])]

    def finish(r):
        @pl.when(at_end)
        def _():
            line_wait(0)
            add_to_mine(r, 3, [(line_in, 0)])
            if r < last:
                used(near, 2)

        @pl.when(jnp.logical_not(at_end))
        def _():
            line_wait(2)
            line_wait(4)
            add_to_mine(r, 3, [(line_in, 2), (line_in, 4)])
            if r < last:
                used(end, 2)
                used(opposite, 1)

        start(outputs(r))


    def rows_of(r, first=0, count=rows):
        return pl.ds(r * rows + first, count)

    over = [
        remote(big.at[rows_of(0)], big.at[rows_of(1)], over_send.at[0], over_recv.at[0], over_x),
        remote(big.at[rows_of(0)], big.at[rows_of(2)], over_send.at[1], over_recv.at[1], over_y),
    ]
    onward = [
        remote(big.at[rows_of(2, 0, half)], big.at[rows_of(3, 0, half)], onward_send.at[0], onward_recv.at[0], over_x),
        remote(big.at[rows_of(1, half, half)], big.at[rows_of(3, half, half)], onward_send.at[1], onward_recv.at[1], over_y),
    ]
    halves = [
        remote(terms.at[2, pl.ds(0, half)], half_in.at[0], half_send.at[0], half_recv.at[0], over_x),
        remote(terms.at[2, pl.ds(half, half)], half_in.at[1], half_send.at[1], half_recv.at[1], over_y),
    ]
    fulls = [
        remote(terms.at[0], full_in.at[0], full_send.at[0], full_recv.at[0], over_x),
        remote(terms.at[1], full_in.at[1], full_send.at[1], full_recv.at[1], over_y),
    ]
    sides = (over_x, over_y)

    def send_halves(stage):
        for i, copy in enumerate(halves):
            if stage == 1:
                pl.semaphore_wait(half_free.at[i], 1)
            copy.start()

    def take_halves(stage):
        for copy in halves:
            copy.wait_recv()
        for term, first, slot in ((1, 0, 0), (0, half, 1)):
            @pl.loop(0, half // 64)
            def _(i):
                place = block_of(first + i * 64, 64)
                grown = terms[term, place].astype(f32) + half_in[slot, block_of(i * 64, 64)].astype(f32)
                terms[term, place] = grown.astype(bf16)

        for i, copy in enumerate(fulls):
            if stage == 0:
                pl.semaphore_signal(half_free.at[i], inc=1, device_id=sides[i], device_id_type=MESH)
            else:
                pl.semaphore_wait(full_free.at[i], 1)
            copy.start()

    def project(r):
        slot = (2, 0, 1, 2)[r]

        @pl.loop(0, width // 256)
        def _(j):
            tile = block_of(j * 256, 256)
            term = dot_nt(big[rows_of(r), pl.ds(0, unit)], units[1, tile])
            term = term + dot_nt(big[rows_of(r), pl.ds(unit, unit)], units[2, tile])
            term = term + dot_nt(units[0, rows_of(r)], units[3, tile])
            terms[slot, :, tile] = term.astype(bf16)


    def gate_copies(r):
        return [
            pltpu.make_async_copy(
                ref.at[rows_of(r), pl.ds(h * VAL, VAL)],
                columns.at[r % 2, pl.ds((2 * i + h) * rows, rows)],
                chunk_sem.at[r % 2, 2 * i + h],
            )
            for i, ref in enumerate((gate_ref, grouped_ref))
            for h in range(heads)
        ]

    def gate_back(r):
        wait(gate_copies(r))

        @pl.loop(0, unit // 256)
        def _(j):
            grad = dot_nn(big[rows_of(r)], units[3, :, block_of(j * 256, 256)])
            head = lax.div(j, VAL // 256)
            inner = block_of(lax.rem(j, VAL // 256) * 256, 256)
            raw = columns[r % 2, block_of(head * rows, rows), inner].astype(f32)
            grouped = columns[r % 2, block_of((heads + head) * rows, rows), inner].astype(f32)
            sigmoid = 1.0 / (1.0 + jnp.exp(-raw))
            tile = block_of(j * 256, 256)
            units[0, rows_of(r), tile] = (grad * grouped * (sigmoid * (1.0 + raw * (1.0 - sigmoid)))).astype(bf16)
            units[1, rows_of(r), tile] = grad.astype(bf16)

    chunks = 4 * rows // CHUNK
    per_piece = rows // CHUNK

    def chunk_place(c):
        piece = lax.div(c, per_piece)
        low = lax.rem(lax.rem(piece, 2) + lax.rem(tensor, 2), 2)
        high = lax.rem(lax.div(piece, 2) + lax.div(tensor, 2), 2)
        return (2 * high + low) * per_piece + lax.rem(c, per_piece)

    def chunk_copies(c, slot):
        place = block_of(chunk_place(c) * CHUNK, CHUNK)
        seat = block_of(c * CHUNK, CHUNK)
        keys = heads * KEY
        pieces = [
            (field_ref.at[place, pl.ds(0, keys)], columns.at[slot, pl.ds(0, CHUNK)]),
            (field_ref.at[place, pl.ds(keys, keys)], columns.at[slot, pl.ds(CHUNK, CHUNK)]),
        ]
        for h in range(heads):
            pieces.append((field_ref.at[place, pl.ds(2 * keys + h * VAL, VAL)], columns.at[slot, pl.ds((2 + h) * CHUNK, CHUNK)]))
            pieces.append((gate_ref.at[place, pl.ds(h * VAL, VAL)], columns.at[slot, pl.ds((4 + h) * CHUNK, CHUNK)]))
            pieces.append((grouped_ref.at[place, pl.ds(h * VAL, VAL)], columns.at[slot, pl.ds((6 + h) * CHUNK, CHUNK)]))
        pieces += [
            (past_ref.at[c], past_in.at[slot]),
            (scale_ref.at[place], scale_in.at[slot]),
            (angle_ref.at[seat], angle_in.at[slot]),
            (info_ref.at[seat], info_in.at[slot]),
        ]
        return [pltpu.make_async_copy(src, dst, chunk_sem.at[slot, i]) for i, (src, dst) in enumerate(pieces)]

    def retention_steps(between):
        @pl.loop(0, chunks)
        def _(step):
            c = chunks - 1 - step
            slot = lax.rem(step, 2)
            wait(chunk_copies(c, slot))

            @pl.when(step + 1 < chunks)
            def _():
                start(chunk_copies(c - 1, 1 - slot))

            place = block_of(chunk_place(c) * CHUNK, CHUNK)
            angles = angle_in[slot]
            cosine = angles[:, : KEY // 2]
            sine = angles[:, KEY // 2 :]
            info = info_in[slot]
            same = info[:, 0:1] == row_ref[c]

            for head in range(heads):
                at = pl.ds(head * KEY, KEY)
                query = turn(columns[slot, pl.ds(0, CHUNK), at].astype(f32), cosine, sine).astype(bf16)
                key = turn(columns[slot, pl.ds(CHUNK, CHUNK), at].astype(f32), cosine, sine)
                key = (key * key_scale).astype(bf16)
                value = columns[slot, pl.ds((2 + head) * CHUNK, CHUNK)]
                gate = columns[slot, pl.ds((4 + head) * CHUNK, CHUNK)].astype(f32)
                grouped = columns[slot, pl.ds((6 + head) * CHUNK, CHUNK)].astype(f32)
                into = info[:, 1 + 2 * head : 2 + 2 * head]
                onto = info[:, 2 + 2 * head : 3 + 2 * head]
                scale = scale_in[slot, :, head : head + 1]
                past = past_in[slot, head]
                out_grad_in = units[1, place, pl.ds(head * VAL, VAL)].astype(f32)
                c_in = out_grad_in * (gate / (1.0 + jnp.exp(-gate)))
                mean_c = jnp.mean(c_in, axis=-1, keepdims=True)
                mean_cx = jnp.mean(c_in * grouped, axis=-1, keepdims=True)
                out_grad = (scale * (c_in - mean_c - grouped * mean_cx)).astype(bf16)
                state = state_ref[head]
                state_low = state.astype(bf16)
                masked = jnp.where(same, decay_ref[head], 0.0)
                weights = (masked * dot_nt(query, key)).astype(bf16)
                score_grad = (masked * dot_nt(out_grad, value)).astype(bf16)
                value_grad = dot_tn(weights, out_grad) + onto * dot_nn(key, state_low)
                query_grad = dot_nn(score_grad, key) + into * dot_nt(out_grad, past)
                key_grad = dot_tn(score_grad, query) + onto * dot_nt(value, state_low)
                moved = (query.astype(f32) * into).astype(bf16)
                state_ref[head] = into[CHUNK - 1 :, :] * state + dot_tn(moved, out_grad)
                big[place, pl.ds(head * KEY, KEY)] = turn_back(query_grad, cosine, sine).astype(bf16)
                big[place, pl.ds((heads + head) * KEY, KEY)] = (turn_back(key_grad, cosine, sine) * key_scale).astype(bf16)
                big[place, pl.ds(2 * heads * KEY + head * VAL, VAL)] = value_grad.astype(bf16)

            between(step)


    def block_copy(ref, i, slot):
        return pltpu.make_async_copy(ref.at[block_of(i * 64, 64)], blocks.at[slot], block_sem.at[slot])

    def stream(ref, use):
        @pl.loop(0, rows // 64)
        def _(i):
            slot = lax.rem(i, 4)
            block_copy(ref, i, slot).wait()
            use(block_of(i * 64, 64), blocks[slot])

            @pl.when(i + 4 < rows // 64)
            def _():
                block_copy(ref, i + 4, slot).start()


    own_load = pltpu.make_async_copy(low_ref, big.at[rows_of(0)], mixed_sem.at[0])
    own_load.start()
    for r in range(2):
        for k in range(4):
            given_copy(r, k).start()
    start(out_load)
    start(gate_copies(0))
    start(gate_copies(1))
    start(feed_load)

    barrier = pltpu.get_barrier_semaphore()

    def partner(k):
        other = lax.rem(here + k, peers)
        return other, (lax.div(other, 4), lax.rem(other, 4))

    @pl.loop(1, peers)
    def _(k):
        pl.semaphore_signal(barrier, inc=1, device_id=partner(k)[1], device_id_type=MESH)

    pl.semaphore_wait(barrier, peers - 1)

    own_load.wait()
    start(over)
    for k in range(4):
        given_copy(0, k).wait()
        send_to_twin(0, k)
        if k > 0:
            settle(0, k - 1)
            push(0, k - 1)
    settle(0, 3)
    for k in range(4):
        given_copy(1, k).wait()
        send_to_twin(1, k)
        if k > 0:
            settle(1, k - 1)
    settle(1, 3)
    wait(out_load)
    gate_back(0)
    start(gate_copies(2))
    pass_on(0, 0)
    push(1, 0)
    pass_on(0, 1)
    push(1, 1)
    pass_on(0, 2)
    for copy in over:
        copy.wait_recv()
    start(onward)
    gate_back(1)
    start(gate_copies(3))
    finish(0)
    push(1, 2)
    gate_back(2)
    pass_on(1, 0)
    pass_on(1, 1)
    wait(feed_load)
    start(gated_load)
    for copy in onward:
        copy.wait_recv()
    send_halves(0)
    gate_back(3)
    prefetch(2)
    start(w_gate_load)
    pass_on(1, 2)
    state_ref[...] = jnp.zeros_like(state_ref)

    def produce(r, k, pushed=True):
        multiply(r, k)
        if k > 0:
            settle(r, k - 1)
            if pushed:
                push(r, k - 1)

    produce(2, 0)
    produce(2, 1)
    finish(1)
    produce(2, 2)
    produce(2, 3)
    settle(2, 3)
    start(chunk_copies(chunks - 1, 0))
    wait(gated_load)
    produce(3, 0)
    produce(3, 1, False)
    take_halves(0)
    pass_on(2, 0)
    push(3, 0)
    produce(3, 2, False)
    produce(3, 3, False)
    settle(3, 3)
    start(w_value_load)
    for copy in over + onward:
        copy.wait_send()

    def between(step):
        @pl.when(step == 1)
        def _():
            pass_on(2, 1)
            push(3, 1)

        @pl.when(step == 2)
        def _():
            pass_on(2, 2)

        @pl.when(step == 5)
        def _():
            finish(2)
            push(3, 2)

    retention_steps(between)
    start(w_key_load)
    prefetch(4)
    pass_on(3, 0)
    for copy in halves:
        copy.wait_send()
    wait(w_gate_load)
    wait(w_value_load)
    wait(w_key_load)
    project(3)
    send_halves(1)
    for i in range(4):
        block_copy(plus_ref, i, i).start()
    produce(4, 0)
    produce(4, 1)
    pass_on(3, 1)
    for copy in fulls:
        copy.wait_recv()

    def add_result(place, value):
        full_in[0, place] = (value.astype(f32) + full_in[0, place].astype(f32) + full_in[1, place].astype(f32)).astype(bf16)

    stream(plus_ref, add_result)
    result_copy = pltpu.make_async_copy(full_in.at[0], result_ref, mixed_sem.at[1])
    result_copy.start()
    for copy in fulls:
        copy.wait_send()
    pass_on(3, 2)
    project(1)
    result_copy.wait()
    for i, side in enumerate(sides):
        pl.semaphore_signal(full_free.at[i], inc=1, device_id=side, device_id_type=MESH)
    project(2)
    take_halves(1)
    finish(3)
    produce(4, 2)
    produce(4, 3, False)
    push(4, 2)
    settle(4, 3)
    prefetch(5)
    pass_on(4, 0)
    produce(5, 0)
    produce(5, 1)
    pass_on(4, 1)
    produce(5, 2)
    pass_on(4, 2)
    produce(5, 3, False)
    settle(5, 3)
    for copy in halves:
        copy.wait_send()
    project(0)
    finish(4)
    push(5, 2)
    pass_on(5, 0)
    pass_on(5, 1)
    for copy in fulls:
        copy.wait_recv()
        copy.wait_send()
    last_loads = [
        pltpu.make_async_copy(token_ref, terms.at[0], mixed_sem.at[2]),
        pltpu.make_async_copy(low_ref, terms.at[1], mixed_sem.at[0]),
    ]
    start(last_loads)
    total[...] = jnp.zeros_like(total)
    wait(last_loads)

    @pl.loop(0, rows // 64)
    def _(i):
        place = block_of(i * 64, 64)
        normed_grad = terms[2, place].astype(f32) + full_in[0, place].astype(f32) + full_in[1, place].astype(f32)
        plain, scale = normalize(terms[0, place].astype(f32))
        grad = terms[1, place].astype(f32) + normalize_back(normed_grad, plain, scale, gain_ref[...])
        full_in[0, place] = grad.astype(bf16)
        total[0:1, :] += jnp.sum(normed_grad * plain, axis=0, keepdims=True)
        total[1:2, :] += jnp.sum(normed_grad, axis=0, keepdims=True)

    grad_copy = pltpu.make_async_copy(full_in.at[0], grad_ref, mixed_sem.at[3])
    grad_copy.start()

    total[2:4, :] = late_ref[...]
    for k in range(peers // 2):
        given[k] = total[:, k * 128 : (k + 1) * 128]

    def sum_copy(k):
        other, device = partner(k)
        return remote(given.at[lax.div(other, 2)], landed.at[k], sum_send.at[k], sum_recv.at[k], device)

    @pl.loop(1, peers)
    def _(k):
        sum_copy(k).start()

    pass_on(5, 2)
    sums_ref[...] = given[lax.div(here, 2)]

    @pl.loop(1, peers)
    def _(k):
        sum_copy(k).wait()
        sums_ref[...] += landed[k]

    finish(5)

    for r in (4, 5):
        for k in range(4):
            to_twin(r, k).wait_send()
            if k < 3:
                along(r, k, 0, end).wait_send()
    wait(outputs(4) + outputs(5))
    grad_copy.wait()


def closing_exchange(heads, operands, small):
    token_rows, width = operands[-1].shape
    rows = 4 * token_rows
    depth = width // 8
    keys, values = heads * KEY, heads * VAL
    unit = operands[1].shape[1]
    anywhere = pl.BlockSpec(memory_space=pl.ANY)
    in_vmem = pl.BlockSpec(memory_space=pltpu.VMEM)
    sem = pltpu.SemaphoreType.DMA
    regular = pltpu.SemaphoreType.REGULAR
    vmem = pltpu.VMEM
    return pl.pallas_call(
        functools.partial(closing_kernel, heads),
        out_shape=[
            jax.ShapeDtypeStruct((token_rows, width), bf16),
            jax.ShapeDtypeStruct((token_rows, width), bf16),
            jax.ShapeDtypeStruct((depth, keys), bf16),
            jax.ShapeDtypeStruct((depth, keys), bf16),
            jax.ShapeDtypeStruct((depth, values), bf16),
            jax.ShapeDtypeStruct((depth, values), bf16),
            jax.ShapeDtypeStruct((depth, unit), bf16),
            jax.ShapeDtypeStruct((depth, unit), bf16),
            jax.ShapeDtypeStruct((depth, unit), bf16),
            jax.ShapeDtypeStruct((8, 128), f32),
        ],
        in_specs=[anywhere] * len(operands) + [in_vmem] * len(small),
        out_specs=[anywhere] * 9 + [in_vmem],
        scratch_shapes=[
            vmem((rows, width), bf16),
            vmem((4, rows, unit), bf16),
            vmem((2, rows, 2 * depth), bf16),
            vmem((3, token_rows, width), bf16),
            vmem((2, token_rows // 2, width), bf16),
            vmem((2, token_rows, width), bf16),
            vmem((2, 4, 2 * depth, unit), bf16),
            vmem((2, depth, unit), bf16),
            vmem((5, depth, unit), bf16),
            vmem((heads, KEY, VAL), f32),
            vmem((2, heads, KEY, VAL), bf16),
            vmem((2, CHUNK, 128), f32),
            vmem((2, CHUNK, KEY), f32),
            vmem((2, CHUNK, 128), f32),
            vmem((4, 64, width), bf16),
            vmem((16, 8, 128), f32),
            vmem((32, 8, 128), f32),
            vmem((8, width), f32),
            sem((10,)), sem((8,)), sem((2, 12)), sem((4,)), sem((2, 2)), sem((4,)),
            sem((2,)), sem((2,)), sem((2,)), sem((2,)),
            sem((2,)), sem((2,)), sem((2,)), sem((2,)),
            sem((2, 4)), sem((2,)), sem((2, 3)), sem((5,)), sem((32,)), sem((32,)),
            regular((2,)), regular((3,)), regular((2,)), regular((2,)),
        ],
        compiler_params=pltpu.CompilerParams(
            collective_id=3, has_side_effects=True, vmem_limit_bytes=63_400_000
        ),
        name="closing_exchange",
    )(*operands, *small)


def body(tokens, cotangent, segment, first_gain, first_bias, query_weight, key_weight, value_weight, gate_weight, out_weight, second_gain, second_bias, up_weight, down_weight):
    devices = lax.axis_size("tensor")
    rows = tokens.shape[0]
    heads = query_weight.shape[1] // KEY
    here = lax.axis_index("tensor")
    which = (here if devices == 4 else jnp.zeros_like(here)).astype(jnp.int32).reshape(1)

    def per_piece(values):
        return [values[i * rows : (i + 1) * rows] for i in range(devices)]

    if devices == 4 and lax.axis_size("dp") == 8:
        shards = (query_weight, key_weight, value_weight, gate_weight, out_weight.T)
        opened, keys = opening_exchange(heads, shards, tokens, cotangent, segment, first_gain, first_bias)
        w_qkv, w_gate, w_out, normed1_all, cot_all, field, gate, gated, grouped, group_scale, past, angles, info, decay = opened
        mixed_low, plus, feed_terms, up_weight_grad, down_weight_grad, late = middle_exchange(
            gated, w_out, up_weight, down_weight.T, cot_all, tokens, second_gain, second_bias
        )
        result, input_grad, query_sum, key_sum, value_sum, gate_sum, out_sum, up_sum, down_sum, sums = closing_exchange(
            heads,
            (
                normed1_all, up_weight_grad, down_weight_grad, feed_terms, w_out, w_qkv, w_gate,
                gate, grouped, gated, group_scale, field, past, angles, info,
                mixed_low, plus, tokens,
            ),
            (keys, decay, first_gain.reshape(1, -1), late),
        )
        part = first_gain.shape[0] // 32
        sums = lax.dynamic_slice_in_dim(sums, (here % 2) * part, part, 1)
        norm_sums = [sums[0], sums[1], sums[2], sums[3]]
        query_sum, key_sum, value_sum, gate_sum, up_sum = (
            v.astype(f32) for v in (query_sum, key_sum, value_sum, gate_sum, up_sum)
        )
        out_sum, down_sum = out_sum.astype(f32).T, down_sum.astype(f32).T
    else:
        w_qkv = lax.all_gather(
            jnp.concatenate([query_weight, key_weight, value_weight], axis=1), "dp", axis=0, tiled=True
        )
        w_gate = lax.all_gather(gate_weight, "dp", axis=0, tiled=True)
        w_out = lax.all_gather(out_weight, "dp", axis=1, tiled=True)
        token_rows = tokens.astype(f32)
        unit1, scale1 = normalize(token_rows)
        normed1_all = jnp.concatenate(
            gather_pieces((unit1 * first_gain + first_bias).astype(bf16), devices), axis=0
        )
        cot_all = jnp.concatenate(gather_pieces(cotangent, devices), axis=0)
        tables = retention_tables(segment, heads, here * heads)
        field = dot_nn(normed1_all, w_qkv).astype(bf16)
        gate = dot_nn(normed1_all, w_gate).astype(bf16)
        gated, grouped, group_scale, past = retention_call(False, which, rows, heads, field, gate, tables, ())
        w_down = lax.all_gather(after(down_weight, w_out), "dp", axis=1, tiled=True)
        w_up = lax.all_gather(after(up_weight, w_down), "dp", axis=0, tiled=True)
        branch, begun, _ = scatter_sum([dot_nn(piece, w_out) for piece in per_piece(gated)])

        mixed = token_rows + branch
        unit2, scale2 = normalize(mixed)
        normed2 = (unit2 * second_gain + second_bias).astype(bf16)
        hidden_grads = per_piece(dot_nt(cot_all, after(w_down, normed2)).astype(bf16))

        def feed(piece, hidden_grad):
            value, slope = gelu_both(dot_nn(piece, w_up))
            return after((value.astype(bf16), (hidden_grad.astype(f32) * slope).astype(bf16)))

        fed_own = feed(normed2, hidden_grads[0])
        normed2_pieces = gather_pieces(normed2, devices, fed_own)
        fed = [fed_own] + [feed(piece, grad) for piece, grad in zip(normed2_pieces[1:-1], hidden_grads[1:-1])]
        fed.append(feed(after(normed2_pieces[-1], *fed), hidden_grads[-1]))
        hidden = [f[0] for f in fed]
        up_grad = [f[1] for f in fed]
        terms = [dot_nt(piece, w_up) for piece in up_grad]
        normed2_grad, _, _ = scatter_sum(terms)
        mixed_grad = cotangent.astype(f32) + normalize_back(normed2_grad, unit2, scale2, second_gain)
        gain2_grad = jnp.sum(normed2_grad * unit2, axis=0)
        bias2_grad = jnp.sum(normed2_grad, axis=0)
        mixed_low = mixed_grad.astype(bf16)
        hidden_all = jnp.concatenate(after(hidden, *terms), axis=0)
        normed2_all = jnp.concatenate(after(normed2_pieces, *terms), axis=0)
        up_grad_all = jnp.concatenate(after(up_grad, *terms), axis=0)
        feed_terms = dot_nn(hidden_all, w_down).astype(bf16)
        own_term = feed_terms[:rows].astype(f32)
        up_weight_grad = dot_tn(normed2_all, up_grad_all).astype(bf16)
        down_weight_grad = dot_tn(cot_all, hidden_all).astype(bf16)

        def summed(gradient, dimension):
            return lax.psum_scatter(
                gradient.astype(bf16), "dp", scatter_dimension=dimension, tiled=True
            ).astype(f32)

        up_sum = summed(up_weight_grad, 0)
        down_sum = summed(down_weight_grad, 0).T
        mixed_all = jnp.concatenate(gather_pieces(mixed_low, devices), axis=0)
        ffn, _, _ = scatter_sum([term.astype(f32) for term in per_piece(feed_terms)])
        result = (mixed + ffn).astype(bf16)
        gated_grad = dot_nt(mixed_all, w_out)
        raw = gate.astype(f32)
        sigmoid = 1.0 / (1.0 + jnp.exp(-raw))
        gate_grad = (gated_grad * grouped.astype(f32) * (sigmoid * (1.0 + raw * (1.0 - sigmoid)))).astype(bf16)
        back = retention_call(
            True, which, rows, heads, field, gate, tables, (gated_grad.astype(bf16), grouped, group_scale, past)
        )
        gate_sum = summed(dot_tn(normed1_all, gate_grad), 0)
        out_sum = summed(dot_tn(gated, mixed_all), 1)
        qkv_sum = summed(dot_tn(normed1_all, back), 0)
        keys_end = heads * KEY
        query_sum = qkv_sum[:, :keys_end]
        key_sum = qkv_sum[:, keys_end : 2 * keys_end]
        value_sum = qkv_sum[:, 2 * keys_end :]
        terms = [
            dot_nt(first, w_qkv) + dot_nt(second, w_gate) for first, second in zip(per_piece(back), per_piece(gate_grad))
        ]
        normed1_grad, _, _ = scatter_sum(terms)
        input_grad = (mixed_grad + normalize_back(normed1_grad, unit1, scale1, first_gain)).astype(bf16)
        gain1_grad = jnp.sum(normed1_grad * unit1, axis=0)
        bias1_grad = jnp.sum(normed1_grad, axis=0)
        norm_sums = spread_sum([gain1_grad, bias1_grad, gain2_grad, bias2_grad])
    return (
        result,
        input_grad,
        norm_sums[0],
        norm_sums[1],
        query_sum,
        key_sum,
        value_sum,
        gate_sum,
        out_sum,
        norm_sums[2],
        norm_sums[3],
        up_sum,
        down_sum,
    )


def solution(mesh):
    rows = P(("dp", "tensor"), None)
    vector = P(("dp", "tensor"))
    into = P("dp", "tensor")
    back = P("tensor", "dp")
    return jax.shard_map(
        body,
        mesh=mesh,
        in_specs=(rows, rows, P("dp"), P(), P(), into, into, into, into, back, P(), P(), into, back),
        out_specs=(rows, rows, vector, vector, into, into, into, into, back, vector, vector, into, back),
        check_vma=False,
    )
```

```python
import functools

import jax
import jax.numpy as jnp
from jax import lax
from jax.experimental import pallas as pl
from jax.experimental.pallas import tpu as pltpu
from jax.sharding import PartitionSpec as P

KEY = 256
VAL = 512
CHUNK = 256
QKV = 2 * KEY + VAL

norm_epsilon = 1e-05
group_floor = 0.5
key_scale = KEY ** (-0.5)

f32 = jnp.float32
bf16 = jnp.bfloat16


def dot_nn(left, right):
    return lax.dot_general(left, right, (((1,), (0,)), ((), ())), preferred_element_type=f32)


def dot_nt(left, right):
    return lax.dot_general(left, right, (((1,), (1,)), ((), ())), preferred_element_type=f32)


def dot_tn(left, right):
    return lax.dot_general(left, right, (((0,), (0,)), ((), ())), preferred_element_type=f32)


def tensor_permute(values, bit):
    pairs = [(i, i ^ bit) for i in range(4)]
    return lax.ppermute(values, "tensor", pairs)


def after(values, *tokens):
    return lax.optimization_barrier((values, tokens))[0]


def gather_pieces(own, devices, between=()):
    if devices != 4:
        whole = lax.all_gather(own, "tensor", axis=0, tiled=True)
        return list(jnp.split(whole, devices, axis=0))
    half = own.shape[0] // 2
    from_x = tensor_permute(own, 1)
    from_y = tensor_permute(own, 2)
    lower, upper = after((from_y[:half], from_x[half:]), *between)
    lower = tensor_permute(lower, 1)
    upper = tensor_permute(upper, 2)
    return [own, from_x, from_y, jnp.concatenate([lower, upper], axis=0)]


def scatter_sum(terms):
    if len(terms) != 4:
        stacked = jnp.concatenate([term.astype(bf16) for term in terms], axis=0)
        return lax.psum_scatter(stacked, "tensor", scatter_dimension=0, tiled=True).astype(f32), (stacked,), (stacked,)
    own, over_x, over_y, across = terms
    half = own.shape[0] // 2
    across = across.astype(bf16)
    first = tensor_permute(across[:half], 1)
    second = tensor_permute(across[half:], 2)
    over_y = jnp.concatenate([over_y[:half] + first.astype(f32), over_y[half:]], axis=0)
    over_x = jnp.concatenate([over_x[:half], over_x[half:] + second.astype(f32)], axis=0)
    by_x = tensor_permute(over_x.astype(bf16), 1)
    by_y = tensor_permute(over_y.astype(bf16), 2)
    return own + by_x.astype(f32) + by_y.astype(f32), (first, second), (by_x, by_y)


def spread_sum_kernel(tensor_devices, devices, given_ref, sum_ref, landed_ref, send_sem, recv_sem):
    here = lax.axis_index("dp") * tensor_devices + lax.axis_index("tensor")

    def partner(k):
        other = lax.rem(here + k, devices)
        return other, (lax.div(other, tensor_devices), lax.rem(other, tensor_devices))

    def copy(k):
        other, device = partner(k)
        return pltpu.make_async_remote_copy(
            src_ref=given_ref.at[other],
            dst_ref=landed_ref.at[k],
            send_sem=send_sem.at[k],
            recv_sem=recv_sem.at[k],
            device_id=device,
            device_id_type=pl.DeviceIdType.MESH,
        )

    barrier = pltpu.get_barrier_semaphore()

    @pl.loop(1, devices)
    def _(k):
        pl.semaphore_signal(barrier, inc=1, device_id=partner(k)[1], device_id_type=pl.DeviceIdType.MESH)

    pl.semaphore_wait(barrier, devices - 1)

    @pl.loop(1, devices)
    def _(k):
        copy(k).start()

    sum_ref[...] = given_ref[here]

    @pl.loop(1, devices)
    def _(k):
        copy(k).wait()
        sum_ref[...] += landed_ref[k]


def spread_sum(vectors):
    dp, tensor = lax.axis_size("dp"), lax.axis_size("tensor")
    devices = dp * tensor
    part = vectors[0].shape[0] // devices
    given = jnp.stack([v.reshape(devices, part) for v in vectors], axis=1)
    given = jnp.pad(given, ((0, 0), (0, 8 - len(vectors)), (0, 128 - part)))
    total = pl.pallas_call(
        functools.partial(spread_sum_kernel, tensor, devices),
        out_shape=jax.ShapeDtypeStruct((8, 128), f32),
        in_specs=[pl.BlockSpec(memory_space=pltpu.VMEM)],
        out_specs=pl.BlockSpec(memory_space=pltpu.VMEM),
        scratch_shapes=[
            pltpu.VMEM((devices, 8, 128), f32),
            pltpu.SemaphoreType.DMA((devices,)),
            pltpu.SemaphoreType.DMA((devices,)),
        ],
        compiler_params=pltpu.CompilerParams(collective_id=1, has_side_effects=True),
        name="spread_sum",
    )(given)
    return [total[i, :part] for i in range(len(vectors))]


def normalize(values):
    average = jnp.mean(values, axis=-1, keepdims=True)
    centred = values - average
    variance = jnp.mean(centred * centred, axis=-1, keepdims=True)
    scale = lax.rsqrt(variance + norm_epsilon)
    return centred * scale, scale


def normalize_back(normed_grad, unit, scale, gain):
    g = normed_grad * gain
    mean_g = jnp.mean(g, axis=-1, keepdims=True)
    mean_gx = jnp.mean(g * unit, axis=-1, keepdims=True)
    return scale * (g - mean_g - unit * mean_gx)


def gelu_both(values):
    inner = 0.7978845608 * (values + 0.044715 * values * values * values)
    t = jnp.tanh(inner)
    slope = 0.7978845608 * (1.0 + 3.0 * 0.044715 * values * values)
    return 0.5 * values * (1.0 + t), 0.5 * (1.0 + t) + 0.5 * values * (1.0 - t * t) * slope


def turn(block, cosine, sine):
    a = block[:, : KEY // 2]
    b = block[:, KEY // 2 :]
    return jnp.concatenate([a * cosine - b * sine, b * cosine + a * sine], axis=1)


def turn_back(block, cosine, sine):
    a = block[:, : KEY // 2]
    b = block[:, KEY // 2 :]
    return jnp.concatenate([a * cosine + b * sine, b * cosine - a * sine], axis=1)


def head_parts(field_ref, angles, heads, head):
    cosine = angles[:, : KEY // 2]
    sine = angles[:, KEY // 2 :]
    query_at = head * KEY
    key_at = (heads + head) * KEY
    value_at = 2 * heads * KEY + head * VAL
    query = turn(field_ref[:, query_at : query_at + KEY].astype(f32), cosine, sine).astype(bf16)
    key = turn(field_ref[:, key_at : key_at + KEY].astype(f32), cosine, sine)
    key = (key * key_scale).astype(bf16)
    return query, key, field_ref[:, value_at : value_at + VAL]


def retention_forward(heads, which, field_ref, gate_ref, angle_ref, info_ref, row_ref, decay_ref, gated_ref, grouped_ref, scale_ref, past_ref, state_ref):
    @pl.when(pl.program_id(0) == 0)
    def _():
        state_ref[...] = jnp.zeros_like(state_ref)

    angles = angle_ref[...]
    info = info_ref[...]
    same = info[:, 0:1] == row_ref[0]
    scales = []
    for head in range(heads):
        query, key, value = head_parts(field_ref, angles, heads, head)
        columns = slice(head * VAL, (head + 1) * VAL)
        gate = gate_ref[:, columns].astype(f32)
        into = info[:, 1 + 2 * head : 2 + 2 * head]
        onward = info[:, 2 + 2 * head : 3 + 2 * head]
        state = state_ref[head]
        past_ref[0, head] = state.astype(bf16)
        scores = dot_nt(query, key)
        weights = (jnp.where(same, decay_ref[head], 0.0) * scores).astype(bf16)
        retained = dot_nn(weights, value) + into * dot_nn(query, state.astype(bf16))
        moved = (key.astype(f32) * onward).astype(bf16)
        state_ref[head] = into[CHUNK - 1 :, :] * state + dot_tn(moved, value)
        centred = retained - jnp.mean(retained, axis=-1, keepdims=True)
        scale = lax.rsqrt(jnp.mean(centred * centred, axis=-1, keepdims=True) + group_floor)
        grouped = centred * scale
        gated = gate / (1.0 + jnp.exp(-gate)) * grouped
        gated_ref[:, columns] = gated.astype(bf16)
        grouped_ref[:, columns] = grouped.astype(bf16)
        scales.append(scale)
    lane = lax.broadcasted_iota(jnp.int32, (CHUNK, 128), 1)
    spread = jnp.zeros((CHUNK, 128), f32)
    for head in range(heads):
        spread = jnp.where(lane == head, scales[head], spread)
    scale_ref[...] = spread


def retention_backward(heads, which, field_ref, gate_ref, angle_ref, info_ref, row_ref, decay_ref, grad_ref, grouped_ref, scale_ref, past_ref, back_ref, state_ref):
    @pl.when(pl.program_id(0) == 0)
    def _():
        state_ref[...] = jnp.zeros_like(state_ref)

    angles = angle_ref[...]
    cosine = angles[:, : KEY // 2]
    sine = angles[:, KEY // 2 :]
    info = info_ref[...]
    same = info[:, 0:1] == row_ref[0]
    for head in range(heads):
        query, key, value = head_parts(field_ref, angles, heads, head)
        columns = slice(head * VAL, (head + 1) * VAL)
        gate = gate_ref[:, columns].astype(f32)
        into = info[:, 1 + 2 * head : 2 + 2 * head]
        onward = info[:, 2 + 2 * head : 3 + 2 * head]
        grouped = grouped_ref[:, columns].astype(f32)
        scale = scale_ref[:, head : head + 1]
        c = grad_ref[:, columns].astype(f32) * (gate / (1.0 + jnp.exp(-gate)))
        mean_c = jnp.mean(c, axis=-1, keepdims=True)
        mean_cx = jnp.mean(c * grouped, axis=-1, keepdims=True)
        out_grad = (scale * (c - mean_c - grouped * mean_cx)).astype(bf16)
        state = state_ref[head]
        state_low = state.astype(bf16)
        past = past_ref[0, head]
        masked = jnp.where(same, decay_ref[head], 0.0)
        weights = (masked * dot_nt(query, key)).astype(bf16)
        score_grad = (masked * dot_nt(out_grad, value)).astype(bf16)
        value_grad = dot_tn(weights, out_grad) + onward * dot_nn(key, state_low)
        query_grad = dot_nn(score_grad, key) + into * dot_nt(out_grad, past)
        key_grad = dot_tn(score_grad, query) + onward * dot_nt(value, state_low)
        moved = (query.astype(f32) * into).astype(bf16)
        state_ref[head] = into[CHUNK - 1 :, :] * state + dot_tn(moved, out_grad)
        query_at = head * KEY
        key_at = (heads + head) * KEY
        value_at = 2 * heads * KEY + head * VAL
        back_ref[:, query_at : query_at + KEY] = turn_back(query_grad, cosine, sine).astype(bf16)
        back_ref[:, key_at : key_at + KEY] = (turn_back(key_grad, cosine, sine) * key_scale).astype(bf16)
        back_ref[:, value_at : value_at + VAL] = value_grad.astype(bf16)


def retention_tables(segment, heads, first_head):
    rows = segment.shape[0]
    chunks = rows // CHUNK
    index = jnp.arange(rows, dtype=jnp.int32)
    boundary = jnp.concatenate([jnp.ones((1,), jnp.int32), (segment[1:] != segment[:-1]).astype(jnp.int32)])
    position = index - lax.cummax(jnp.where(boundary > 0, index, 0), axis=0)
    half = KEY // 2
    frequency = jnp.exp(-jnp.log(10000.0) * jnp.arange(half, dtype=f32) / half)
    angles = position.astype(f32)[:, None] * frequency[None, :]
    angles = jnp.concatenate([jnp.cos(angles), jnp.sin(angles)], axis=1)
    head_ids = (first_head + jnp.arange(heads, dtype=jnp.int32)).astype(f32)
    log_decay = jnp.log1p(-jnp.exp2(-5.0 - head_ids))
    last = segment.reshape(chunks, CHUNK)[:, -1]
    before = jnp.concatenate([jnp.full((1,), -2, jnp.int32), last[:-1]])
    offset = (index % CHUNK).astype(f32)
    linked_in = (segment == jnp.repeat(before, CHUNK)) & (segment >= 0)
    linked_on = (segment == jnp.repeat(last, CHUNK)) & (segment >= 0)
    columns = [segment.astype(f32)]
    for head in range(heads):
        columns.append(jnp.where(linked_in, jnp.exp(log_decay[head] * (offset + 1.0)), 0.0))
        columns.append(jnp.where(linked_on, jnp.exp(log_decay[head] * (CHUNK - 1.0 - offset)), 0.0))
    info = jnp.stack(columns, axis=1)
    info = jnp.pad(info, ((0, 0), (0, 128 - info.shape[1])))
    keys = jnp.where(segment >= 0, segment, -7).astype(f32).reshape(chunks, 1, CHUNK)
    distance = (jnp.arange(CHUNK)[:, None] - jnp.arange(CHUNK)[None, :]).astype(f32)
    decay = jnp.where(distance >= 0, jnp.exp(log_decay[:, None, None] * jnp.maximum(distance, 0.0)), 0.0)
    return angles, info, keys, decay


def retention_call(backward, which, piece_rows, heads, field, gate, tables, extra):
    rows = field.shape[0]
    chunks = rows // CHUNK
    angles, info, keys, decay = tables
    per_piece = piece_rows // CHUNK

    def step(i):
        return chunks - 1 - i if backward else i

    def place(i, which_ref):
        c = step(i)
        return ((c // per_piece) ^ which_ref[0]) * per_piece + c % per_piece

    def placed(width):
        return pl.BlockSpec((CHUNK, width), lambda i, w: (place(i, w), 0))

    in_specs = [
        placed(heads * QKV),
        placed(heads * VAL),
        pl.BlockSpec((CHUNK, KEY), lambda i, w: (step(i), 0)),
        pl.BlockSpec((CHUNK, 128), lambda i, w: (step(i), 0)),
        pl.BlockSpec((1, 1, CHUNK), lambda i, w: (step(i), 0, 0)),
        pl.BlockSpec((heads, CHUNK, CHUNK), lambda i, w: (0, 0, 0)),
    ]
    past_spec = pl.BlockSpec((1, heads, KEY, VAL), lambda i, w: (step(i), 0, 0, 0))
    if backward:
        in_specs += [placed(heads * VAL), placed(heads * VAL), placed(128), past_spec]
        out_specs = placed(heads * QKV)
        out_shape = jax.ShapeDtypeStruct((rows, heads * QKV), bf16)
    else:
        out_specs = [placed(heads * VAL), placed(heads * VAL), placed(128), past_spec]
        out_shape = [
            jax.ShapeDtypeStruct((rows, heads * VAL), bf16),
            jax.ShapeDtypeStruct((rows, heads * VAL), bf16),
            jax.ShapeDtypeStruct((rows, 128), f32),
            jax.ShapeDtypeStruct((chunks, heads, KEY, VAL), bf16),
        ]
    products = 15 if backward else 7
    return pl.pallas_call(
        functools.partial(retention_backward if backward else retention_forward, heads),
        grid_spec=pltpu.PrefetchScalarGridSpec(
            num_scalar_prefetch=1,
            grid=(chunks,),
            in_specs=in_specs,
            out_specs=out_specs,
            scratch_shapes=[pltpu.VMEM((heads, KEY, VAL), f32)],
        ),
        out_shape=out_shape,
        compiler_params=pltpu.CompilerParams(
            dimension_semantics=("arbitrary",), vmem_limit_bytes=48 * 1024 * 1024
        ),
        cost_estimate=pl.CostEstimate(
            flops=products * chunks * heads * 2 * CHUNK * CHUNK * CHUNK,
            bytes_accessed=(5 if backward else 4) * rows * heads * (QKV + VAL),
            transcendentals=rows * heads * VAL,
        ),
        name="retention_backward" if backward else "retention_forward",
    )(which, field, gate, angles, info, keys, decay, *extra)


MESH = pl.DeviceIdType.MESH


def opening_kernel(
    heads, query_ref, key_ref, value_ref, gate_ref, out_ref, down_ref, token_ref, cot_ref, segment_ref, row_ref, rate_ref, gain_ref, bias_ref,
    w_qkv_ref, w_gate_ref, w_out_ref, normed_ref, cot_all_ref, field_ref, gate_raw_ref, gated_ref, grouped_ref, scale_ref, past_ref,
    angle_ref, info_ref, decay_ref, down_turned_ref,
    w_qkv, w_gate, w_out, tall, down_turned, normed, product, blocks, angles, info, decay, state, field_out, gate_out, gated_out, grouped_out,
    scale_out, past_out,
    local_sem, block_sem, out_sem, stage_sem, table_sem, up_send, up_recv, down_send, down_recv, core_send, core_recv,
    row_send, row_recv,
):
    dp = lax.axis_index("dp")
    tensor = lax.axis_index("tensor")
    z = lax.div(dp, 2)
    layers = 4
    depth = query_ref.shape[0]
    rows = token_ref.shape[0]
    half = rows // 2
    above = (dp + 2, tensor)
    below = (dp - 2, tensor)
    twin = (dp + 1 - 2 * lax.rem(dp, 2), tensor)
    over_x = (dp, tensor + 1 - 2 * lax.rem(tensor, 2))
    over_y = (dp, lax.rem(tensor + 2, 4))
    keys = heads * KEY
    values = heads * VAL

    def block_of(start, count):
        return pl.ds(pl.multiple_of(start, count), count)

    def start(copies):
        for copy in copies:
            copy.start()

    def wait(copies):
        for copy in copies:
            copy.wait()

    def remote(src, dst, send, recv, device):
        return pltpu.make_async_remote_copy(
            src_ref=src, dst_ref=dst, send_sem=send, recv_sem=recv, device_id=device, device_id_type=MESH
        )

    mine = block_of(dp * depth, depth)
    local = [
        pltpu.make_async_copy(src, dst, local_sem.at[i])
        for i, (src, dst) in enumerate((
            (query_ref, w_qkv.at[mine, pl.ds(0, keys)]),
            (key_ref, w_qkv.at[mine, pl.ds(keys, keys)]),
            (value_ref, w_qkv.at[mine, pl.ds(2 * keys, values)]),
            (gate_ref, w_gate.at[mine]),
            (out_ref, tall),
            (segment_ref, info),
        ))
    ]
    start(local)

    def token_block(i, slot):
        return pltpu.make_async_copy(token_ref.at[block_of(i * 64, 64)], blocks.at[slot], block_sem.at[slot])

    for i in range(4):
        token_block(i, i).start()
    own_cot = pltpu.make_async_copy(cot_ref, cot_all_ref.at[pl.ds(0, rows)], local_sem.at[6])
    own_cot.start()

    barrier = pltpu.get_barrier_semaphore()

    def greet(device):
        pl.semaphore_signal(barrier, inc=1, device_id=device, device_id_type=MESH)

    for device in (twin, over_x, over_y):
        greet(device)
    pl.when(z < layers - 1)(lambda: greet(above))
    pl.when(z > 0)(lambda: greet(below))
    pl.semaphore_wait(barrier, 3 + (z < layers - 1).astype(jnp.int32) + (z > 0).astype(jnp.int32))
    wait(local[:4])


    groups = ((w_qkv, w_gate), (w_out,))

    def shard_copies(g, shard, send_sem, recv_sem, index, device):
        place = block_of(shard * depth, depth)
        return [
            remote(ref.at[place], ref.at[place], send_sem.at[index, i + 2 * g], recv_sem.at[index, i + 2 * g], device)
            for i, ref in enumerate(groups[g])
        ]

    def rise(g, j):
        return shard_copies(g, dp - 2 * j, up_send, up_recv, j, above)

    def sink(g, j):
        return shard_copies(g, dp + 2 * j, down_send, down_recv, j, below)

    def to_twin(g, j):
        return shard_copies(g, dp + 2 * j, core_send, core_recv, j + 3, twin)

    def from_twin(g, j):
        return shard_copies(g, twin[0] + 2 * j, core_send, core_recv, j + 3, twin)

    def wait_recv(copies):
        for copy in copies:
            copy.wait_recv()

    def wait_send(copies):
        for copy in copies:
            copy.wait_send()

    def first_step(g):
        pl.when(z < layers - 1)(lambda: start(rise(g, 0)))
        pl.when(z > 0)(lambda: start(sink(g, 0)))
        start(to_twin(g, 0))

    def step(g, j):
        @pl.when(z - j >= 0)
        def _():
            wait_recv(shard_copies(g, dp - 2 * j, up_send, up_recv, j - 1, twin))
            if j < 3:
                pl.when(z < layers - 1)(lambda: start(rise(g, j)))
            start(to_twin(g, -j))

        @pl.when(z + j < layers)
        def _():
            wait_recv(shard_copies(g, dp + 2 * j, down_send, down_recv, j - 1, twin))
            if j < 3:
                pl.when(z > 0)(lambda: start(sink(g, j)))
            start(to_twin(g, j))

    def twin_step(g, j):
        for signed in sorted({-j, j}):
            @pl.when((z + signed >= 0) & (z + signed < layers))
            def _():
                wait_recv(from_twin(g, signed))

    def rows_of(r, first=0, count=rows):
        return pl.ds(r * rows + first, count)

    def row_copy(index, src, dst, device):
        return remote(src, dst, row_send.at[index], row_recv.at[index], device)

    piece = 64
    cot_early = [
        row_copy(8, cot_ref.at[pl.ds(0, piece)], cot_all_ref.at[rows_of(1, 0, piece)], over_x),
        row_copy(9, cot_ref.at[pl.ds(0, piece)], cot_all_ref.at[rows_of(2, 0, piece)], over_y),
    ]
    cot_over = [
        row_copy(4, cot_ref.at[pl.ds(piece, rows - piece)], cot_all_ref.at[rows_of(1, piece, rows - piece)], over_x),
        row_copy(5, cot_ref.at[pl.ds(piece, rows - piece)], cot_all_ref.at[rows_of(2, piece, rows - piece)], over_y),
    ]

    first_step(0)
    start(cot_early)

    @pl.loop(0, rows // 64)
    def _(i):
        slot = lax.rem(i, 4)
        token_block(i, slot).wait()
        plain, _ = normalize(blocks[slot].astype(f32))
        normed[block_of(i * 64, 64), :] = (plain * gain_ref[...] + bias_ref[...]).astype(bf16)

        @pl.when(i + 4 < rows // 64)
        def _():
            token_block(i + 4, slot).start()

    over = [
        row_copy(0, normed.at[rows_of(0)], normed.at[rows_of(1)], over_x),
        row_copy(1, normed.at[rows_of(0)], normed.at[rows_of(2)], over_y),
    ]
    onward = [
        row_copy(2, normed.at[rows_of(2, 0, half)], normed.at[rows_of(3, 0, half)], over_x),
        row_copy(3, normed.at[rows_of(1, half, half)], normed.at[rows_of(3, half, half)], over_y),
    ]
    cot_onward = [
        row_copy(6, cot_all_ref.at[rows_of(2, 0, half)], cot_all_ref.at[rows_of(3, 0, half)], over_x),
        row_copy(7, cot_all_ref.at[rows_of(1, half, half)], cot_all_ref.at[rows_of(3, half, half)], over_y),
    ]
    start(over)

    local[4].wait()
    w_out[mine, :] = tall[...].T
    down_load = pltpu.make_async_copy(down_ref, tall, local_sem.at[4])
    down_load.start()

    local[5].wait()
    half_key = KEY // 2
    lanes = lax.broadcasted_iota(jnp.int32, (CHUNK, half_key), 1).astype(f32)
    frequency = jnp.exp(lanes * (-9.210340371976184 / half_key))
    chunks = 4 * rows // CHUNK

    @pl.loop(0, chunks)
    def _(c):
        seat = block_of(c * CHUNK, CHUNK)
        own = info[seat, 0:1]
        ranked = jnp.where(own < 0, 3.0, own)
        before = jnp.zeros((CHUNK, 1), f32)
        for other in range(chunks):
            seen = row_ref[other]
            seen = jnp.where(seen < 0, 3.0, seen)
            before = before + jnp.sum((seen < ranked).astype(f32), axis=1, keepdims=True)
        index = lax.broadcasted_iota(jnp.int32, (CHUNK, 1), 0) + c * CHUNK
        turned = (index.astype(f32) - before) * frequency
        angles[seat, 0:half_key] = jnp.cos(turned)
        angles[seat, half_key:KEY] = jnp.sin(turned)

    distance = lax.broadcasted_iota(jnp.int32, (CHUNK, CHUNK), 0) - lax.broadcasted_iota(jnp.int32, (CHUNK, CHUNK), 1)
    span = jnp.maximum(distance, 0).astype(f32)
    for head in range(heads):
        decay[head] = jnp.where(distance >= 0, jnp.exp(rate_ref[head : head + 1, 0:1] * span), 0.0)
    down_load.wait()
    down_turned[...] = tall[...].T
    table_outs = [
        pltpu.make_async_copy(down_turned, down_turned_ref, table_sem.at[3]),
        pltpu.make_async_copy(angles, angle_ref, table_sem.at[0]),
        pltpu.make_async_copy(decay, decay_ref, table_sem.at[1]),
    ]
    start(table_outs)


    at_end = (z == 0) | (z == 3)

    def seen_from_end(index):
        return jnp.where(z >= 2, 3 - index, index)

    order = [z, jnp.where(at_end, seen_from_end(1), seen_from_end(0)), seen_from_end(2), seen_from_end(3)]

    def project(r, s):
        deep = block_of(order[s] * 2 * depth, 2 * depth)

        @pl.loop(0, (2 * keys + values) // 512)
        def _(j):
            tile = block_of(j * 512, 512)
            more = dot_nn(normed[rows_of(r), deep], w_qkv[deep, tile])
            product[rows_of(r), tile] = more if s == 0 else product[rows_of(r), tile] + more

        @pl.loop(0, values // 512)
        def _(j):
            tile = block_of(j * 512, 512)
            more = dot_nn(normed[rows_of(r), deep], w_gate[deep, tile])
            place = block_of(2 * keys + values + j * 512, 512)
            product[rows_of(r), place] = more if s == 0 else product[rows_of(r), place] + more


    per_piece = rows // CHUNK

    def chunk_place(c):
        piece = lax.div(c, per_piece)
        low = lax.rem(lax.rem(piece, 2) + lax.rem(tensor, 2), 2)
        high = lax.rem(lax.div(piece, 2) + lax.div(tensor, 2), 2)
        return (2 * high + low) * per_piece + lax.rem(c, per_piece)

    def chunk_outs(c):
        place = block_of(chunk_place(c) * CHUNK, CHUNK)
        pairs = (
            (field_out, field_ref.at[place]),
            (gate_out, gate_raw_ref.at[place]),
            (gated_out, gated_ref.at[place]),
            (grouped_out, grouped_ref.at[place]),
            (scale_out, scale_ref.at[place]),
            (past_out, past_ref.at[c]),
        )
        return [pltpu.make_async_copy(src, dst, stage_sem.at[i]) for i, (src, dst) in enumerate(pairs)]

    def retention(between):
        state[...] = jnp.zeros_like(state)

        @pl.loop(0, chunks)
        def _(c):
            place = block_of(chunk_place(c) * CHUNK, CHUNK)
            seat = block_of(c * CHUNK, CHUNK)
            cosine = angles[seat, 0:half_key]
            sine = angles[seat, half_key:KEY]
            own = info[seat, 0:1]
            same = own == row_ref[c]
            entering = (own == row_ref[jnp.maximum(c - 1, 0)][:, CHUNK - 1 :]) & (c > 0)
            leaving = own == row_ref[c][:, CHUNK - 1 :]
            offset = lax.broadcasted_iota(jnp.int32, (CHUNK, 1), 0).astype(f32)
            lane = lax.broadcasted_iota(jnp.int32, (CHUNK, 128), 1)
            facts = jnp.where(lane == 0, own, 0.0)
            scales = jnp.zeros((CHUNK, 128), f32)

            @pl.when(c > 0)
            def _():
                wait(chunk_outs(c - 1))

            for head in range(heads):
                rate = rate_ref[head : head + 1, 0:1]
                into = jnp.where(entering, jnp.exp(rate * (offset + 1.0)), 0.0)
                onto = jnp.where(leaving, jnp.exp(rate * (CHUNK - 1.0 - offset)), 0.0)
                facts = jnp.where(lane == 1 + 2 * head, into, facts)
                facts = jnp.where(lane == 2 + 2 * head, onto, facts)
                query_raw = product[place, pl.ds(head * KEY, KEY)]
                key_raw = product[place, pl.ds(keys + head * KEY, KEY)]
                value = product[place, pl.ds(2 * keys + head * VAL, VAL)].astype(bf16)
                gate = product[place, pl.ds(2 * keys + values + head * VAL, VAL)]
                query_raw = query_raw.astype(bf16)
                key_raw = key_raw.astype(bf16)
                gate_low = gate.astype(bf16)
                field_out[:, pl.ds(head * KEY, KEY)] = query_raw
                field_out[:, pl.ds(keys + head * KEY, KEY)] = key_raw
                field_out[:, pl.ds(2 * keys + head * VAL, VAL)] = value
                gate_out[:, pl.ds(head * VAL, VAL)] = gate_low
                query = turn(query_raw.astype(f32), cosine, sine).astype(bf16)
                key = (turn(key_raw.astype(f32), cosine, sine) * key_scale).astype(bf16)
                memory = state[head]
                memory_low = memory.astype(bf16)
                past_out[head] = memory_low
                scores = dot_nt(query, key)
                weights = (jnp.where(same, decay[head], 0.0) * scores).astype(bf16)
                retained = dot_nn(weights, value) + into * dot_nn(query, memory_low)
                moved = (key.astype(f32) * onto).astype(bf16)
                state[head] = into[CHUNK - 1 :, :] * memory + dot_tn(moved, value)
                centred = retained - jnp.mean(retained, axis=-1, keepdims=True)
                scale = lax.rsqrt(jnp.mean(centred * centred, axis=-1, keepdims=True) + group_floor)
                grouped = centred * scale
                columns = pl.ds(head * VAL, VAL)
                gated_out[:, columns] = (gate / (1.0 + jnp.exp(-gate)) * grouped).astype(bf16)
                grouped_out[:, columns] = grouped.astype(bf16)
                scales = jnp.where(lane == head, scale, scales)
            info[seat, :] = facts
            scale_out[...] = scales
            start(chunk_outs(c))
            between(c)

        wait(chunk_outs(chunks - 1))


    twin_step(0, 0)
    project(0, 0)
    step(0, 1)
    twin_step(0, 1)
    project(0, 1)
    wait_recv(over)
    start(onward)
    start(cot_over)
    for r in (1, 2):
        for s in (0, 1):
            project(r, s)
    step(0, 2)
    first_step(1)
    twin_step(0, 2)
    for r in (0, 1, 2):
        project(r, 2)
    wait_recv(onward)
    normed_out = pltpu.make_async_copy(normed, normed_ref, local_sem.at[7])
    normed_out.start()
    for s in (0, 1, 2):
        project(3, s)
    step(0, 3)
    twin_step(0, 3)
    for r in range(4):
        project(r, 3)
    step(1, 1)
    w_outs = [
        pltpu.make_async_copy(w_qkv, w_qkv_ref, out_sem.at[0]),
        pltpu.make_async_copy(w_gate, w_gate_ref, out_sem.at[1]),
    ]
    start(w_outs)

    def between(c):
        @pl.when(c == 2)
        def _():
            wait_recv(cot_early + cot_over)
            start(cot_onward)

        @pl.when(c == 4)
        def _():
            step(1, 2)

    retention(between)
    info_out = pltpu.make_async_copy(info, info_ref, table_sem.at[2])
    info_out.start()
    step(1, 3)
    for j in range(4):
        twin_step(1, j)
    w_out_out = pltpu.make_async_copy(w_out, w_out_ref, out_sem.at[2])
    w_out_out.start()
    wait_recv(cot_onward)

    wait_send(over + onward + cot_early + cot_over + cot_onward)
    for g in range(2):
        for j in range(3):
            pl.when((z < layers - 1) & (z - j >= 0))(lambda: wait_send(rise(g, j)))
            pl.when((z > 0) & (z + j < layers))(lambda: wait_send(sink(g, j)))
        for j in range(-3, 4):
            pl.when((z + j >= 0) & (z + j < layers))(lambda: wait_send(to_twin(g, j)))
    wait(table_outs + w_outs + [normed_out, own_cot, info_out, w_out_out])


def opening_exchange(heads, shards, tokens, cotangent, segment, gain, bias):
    dp = lax.axis_size("dp")
    depth, keys = shards[0].shape
    values = shards[2].shape[1]
    unit = shards[4].shape[0]
    token_rows, width = tokens.shape
    rows = 4 * token_rows
    chunks = rows // CHUNK
    anywhere = pl.BlockSpec(memory_space=pl.ANY)
    in_vmem = pl.BlockSpec(memory_space=pltpu.VMEM)
    sem = pltpu.SemaphoreType.DMA
    vmem = pltpu.VMEM
    here = lax.axis_index("tensor") * heads
    head_ids = (here + jnp.arange(8, dtype=jnp.int32)).astype(f32)
    rates = jnp.broadcast_to(jnp.log1p(-jnp.exp2(-5.0 - head_ids))[:, None], (8, 128))
    wide_segment = jnp.broadcast_to(segment.astype(f32)[:, None], (rows, 128))
    row_segment = jnp.where(segment >= 0, segment, -7).astype(f32).reshape(chunks, 1, CHUNK)
    results = pl.pallas_call(
        functools.partial(opening_kernel, heads),
        out_shape=[
            jax.ShapeDtypeStruct((dp * depth, 2 * keys + values), bf16),
            jax.ShapeDtypeStruct((dp * depth, values), bf16),
            jax.ShapeDtypeStruct((dp * depth, unit), bf16),
            jax.ShapeDtypeStruct((rows, width), bf16),
            jax.ShapeDtypeStruct((rows, width), bf16),
            jax.ShapeDtypeStruct((rows, 2 * keys + values), bf16),
            jax.ShapeDtypeStruct((rows, values), bf16),
            jax.ShapeDtypeStruct((rows, values), bf16),
            jax.ShapeDtypeStruct((rows, values), bf16),
            jax.ShapeDtypeStruct((rows, 128), f32),
            jax.ShapeDtypeStruct((chunks, heads, KEY, VAL), bf16),
            jax.ShapeDtypeStruct((rows, KEY), f32),
            jax.ShapeDtypeStruct((rows, 128), f32),
            jax.ShapeDtypeStruct((heads, CHUNK, CHUNK), f32),
            jax.ShapeDtypeStruct((depth, unit), bf16),
        ],
        in_specs=[anywhere] * 9 + [in_vmem] * 4,
        out_specs=[anywhere] * 15,
        scratch_shapes=[
            vmem((dp * depth, 2 * keys + values), bf16),
            vmem((dp * depth, values), bf16),
            vmem((dp * depth, unit), bf16),
            vmem((unit, depth), bf16),
            vmem((depth, unit), bf16),
            vmem((rows, width), bf16),
            vmem((rows, 2 * keys + 2 * values), f32),
            vmem((4, 64, width), bf16),
            vmem((rows, KEY), f32),
            vmem((rows, 128), f32),
            vmem((heads, CHUNK, CHUNK), f32),
            vmem((heads, KEY, VAL), f32),
            vmem((CHUNK, 2 * keys + values), bf16),
            vmem((CHUNK, values), bf16),
            vmem((CHUNK, values), bf16),
            vmem((CHUNK, values), bf16),
            vmem((CHUNK, 128), f32),
            vmem((heads, KEY, VAL), bf16),
            sem((8,)), sem((4,)), sem((3,)), sem((6,)), sem((4,)),
            sem((3, 3)), sem((3, 3)), sem((3, 3)), sem((3, 3)), sem((7, 3)), sem((7, 3)), sem((10,)), sem((10,)),
        ],
        compiler_params=pltpu.CompilerParams(
            collective_id=2, has_side_effects=True, vmem_limit_bytes=63_400_000
        ),
        name="opening_exchange",
    )(*shards, tokens, cotangent, wide_segment, row_segment, rates, gain.reshape(1, width), bias.reshape(1, width))
    return results, row_segment


def middle_kernel(
    gated_ref, w_out_ref, up_ref, down_ref, cot_ref, token_ref, gain_ref, bias_ref,
    low_ref, plus_ref, feed_ref, up_grad_out, down_grad_out, late_ref,
    big, units, columns, staged, terms, half_in, full_in, mixed, plus, total,
    load_sem, column_sem, staged_sem, feed_sem, out_sem, up_send, up_recv, below_send, below_recv, core_send, core_recv,
    row_send, row_recv, half_send, half_recv, full_send, full_recv, half_free, full_free, big_free,
):
    dp = lax.axis_index("dp")
    tensor = lax.axis_index("tensor")
    z = lax.div(dp, 2)
    layers = 4
    rows = token_ref.shape[0]
    half = rows // 2
    width = token_ref.shape[1]
    unit = units.shape[2]
    depth = up_ref.shape[0]
    above = (dp + 2, tensor)
    below = (dp - 2, tensor)
    twin = (dp + 1 - 2 * lax.rem(dp, 2), tensor)
    over_x = (dp, tensor + 1 - 2 * lax.rem(tensor, 2))
    over_y = (dp, lax.rem(tensor + 2, 4))
    sides = (over_x, over_y)

    def block_of(start, count):
        return pl.ds(pl.multiple_of(start, count), count)

    def start(copies):
        for copy in copies:
            copy.start()

    def wait(copies):
        for copy in copies:
            copy.wait()

    def remote(src, dst, send, recv, device):
        return pltpu.make_async_remote_copy(
            src_ref=src, dst_ref=dst, send_sem=send, recv_sem=recv, device_id=device, device_id_type=MESH
        )

    mine = block_of(dp * depth, depth)
    shard_loads = [
        pltpu.make_async_copy(down_ref, units.at[3, mine], load_sem.at[0]),
        pltpu.make_async_copy(up_ref, units.at[2, mine], load_sem.at[1]),
    ]
    first_loads = [
        pltpu.make_async_copy(gated_ref, units.at[0], load_sem.at[2]),
        pltpu.make_async_copy(w_out_ref, units.at[1], load_sem.at[3]),
    ]
    token_load = pltpu.make_async_copy(token_ref, plus, load_sem.at[5])
    cot_load = pltpu.make_async_copy(cot_ref, big, load_sem.at[6])
    start(shard_loads)
    start(first_loads)
    token_load.start()
    cot_load.start()

    barrier = pltpu.get_barrier_semaphore()

    def greet(device):
        pl.semaphore_signal(barrier, inc=1, device_id=device, device_id_type=MESH)

    for device in (twin, over_x, over_y):
        greet(device)
    pl.when(z < layers - 1)(lambda: greet(above))
    pl.when(z > 0)(lambda: greet(below))
    pl.semaphore_wait(barrier, 3 + (z < layers - 1).astype(jnp.int32) + (z > 0).astype(jnp.int32))


    def shard_copy(a, shard, send_sem, recv_sem, index, device):
        place = block_of(shard * depth, depth)
        ref = units.at[3 - a, place]
        return remote(ref, ref, send_sem.at[a, index], recv_sem.at[a, index], device)

    def rise(a, j):
        return shard_copy(a, dp - 2 * j, up_send, up_recv, j, above)

    def sink(a, j):
        return shard_copy(a, dp + 2 * j, below_send, below_recv, j, below)

    def to_twin(a, j):
        return shard_copy(a, dp + 2 * j, core_send, core_recv, j + 3, twin)

    def from_twin(a, j):
        return shard_copy(a, twin[0] + 2 * j, core_send, core_recv, j + 3, twin)

    def first_step(a):
        shard_loads[a].wait()
        pl.when(z < layers - 1)(lambda: rise(a, 0).start())
        pl.when(z > 0)(lambda: sink(a, 0).start())
        to_twin(a, 0).start()

    def step(a, j):
        @pl.when(z - j >= 0)
        def _():
            shard_copy(a, dp - 2 * j, up_send, up_recv, j - 1, twin).wait_recv()
            if j < 3:
                pl.when(z < layers - 1)(lambda: rise(a, j).start())
            to_twin(a, -j).start()

        @pl.when(z + j < layers)
        def _():
            shard_copy(a, dp + 2 * j, below_send, below_recv, j - 1, twin).wait_recv()
            if j < 3:
                pl.when(z > 0)(lambda: sink(a, j).start())
            to_twin(a, j).start()

    def gathered(a):
        for j in range(-3, 4):
            @pl.when((z + j >= 0) & (z + j < layers))
            def _():
                from_twin(a, j).wait_recv()


    def rows_of(r, first=0, count=rows):
        return pl.ds(r * rows + first, count)

    halves = [
        remote(terms.at[2, pl.ds(0, half)], half_in.at[0], half_send.at[0], half_recv.at[0], over_x),
        remote(terms.at[2, pl.ds(half, half)], half_in.at[1], half_send.at[1], half_recv.at[1], over_y),
    ]
    fulls = [
        remote(terms.at[0], full_in.at[0], full_send.at[0], full_recv.at[0], over_x),
        remote(terms.at[1], full_in.at[1], full_send.at[1], full_recv.at[1], over_y),
    ]
    lower, upper = (0, half), (half, half)

    def row_copy(index, source, first, target, device):
        return remote(
            big.at[rows_of(source, *first)], big.at[rows_of(target, *first)],
            row_send.at[index], row_recv.at[index], device,
        )

    early = [row_copy(0, 0, lower, 1, over_x), row_copy(1, 0, upper, 2, over_y)]
    across = [row_copy(2, 2, upper, 3, over_x), row_copy(3, 1, lower, 3, over_y)]
    late = [row_copy(4, 0, upper, 1, over_x), row_copy(5, 0, lower, 2, over_y)]

    def send_halves(stage):
        for i, copy in enumerate(halves):
            if stage == 1:
                pl.semaphore_wait(half_free.at[i], 1)
            copy.start()

    def take_halves(stage):
        for copy in halves:
            copy.wait_recv()
        for term, first, slot in ((1, 0, 0), (0, half, 1)):
            @pl.loop(0, half // 64)
            def _(i):
                place = block_of(first + i * 64, 64)
                grown = terms[term, place].astype(f32) + half_in[slot, block_of(i * 64, 64)].astype(f32)
                terms[term, place] = grown.astype(bf16)

        for i, copy in enumerate(fulls):
            if stage == 0:
                pl.semaphore_signal(half_free.at[i], inc=1, device_id=sides[i], device_id_type=MESH)
            else:
                pl.semaphore_wait(full_free.at[i], 1)
            copy.start()

    def slot_of(r):
        return (3, 0, 1, 2)[r]

    def branch_term(r):
        @pl.loop(0, width // 256)
        def _(j):
            tile = block_of(j * 256, 256)
            terms[slot_of(r), :, tile] = dot_nt(units[0, rows_of(r)], units[1, tile]).astype(bf16)

    def feed_grads(r):
        @pl.loop(0, unit // 256)
        def _(j):
            tile = block_of(j * 256, 256)
            units[4, rows_of(r), tile] = dot_nn(big[rows_of(r)], units[3, :, tile]).astype(bf16)

    def feed(r):
        @pl.loop(0, unit // 256)
        def _(j):
            tile = block_of(j * 256, 256)
            value, slope = gelu_both(dot_nn(big[rows_of(r)], units[2, :, tile]))
            units[0, rows_of(r), tile] = value.astype(bf16)
            units[1, rows_of(r), tile] = (units[4, rows_of(r), tile].astype(f32) * slope).astype(bf16)

    def back_term(r):
        @pl.loop(0, width // 256)
        def _(j):
            tile = block_of(j * 256, 256)
            terms[slot_of(r), :, tile] = dot_nt(units[1, rows_of(r)], units[2, tile]).astype(bf16)


    first_step(0)
    wait(first_loads)
    branch_term(3)
    send_halves(0)
    step(0, 1)
    branch_term(1)
    branch_term(2)
    step(0, 2)
    first_step(1)
    take_halves(0)
    branch_term(0)
    step(0, 3)
    cot_load.wait()
    gathered(0)
    step(1, 1)
    feed_grads(0)
    feed_grads(1)
    step(1, 2)
    feed_grads(2)
    feed_grads(3)
    for side in sides:
        pl.semaphore_signal(big_free, inc=1, device_id=side, device_id_type=MESH)
    step(1, 3)
    gathered(1)
    token_load.wait()
    pl.semaphore_wait(big_free, 2)
    for copy in fulls:
        copy.wait_recv()

    def second_norm(i):
        place = block_of(i * 64, 64)
        value = plus[place].astype(f32) + terms[3, place].astype(f32)
        value = value + full_in[0, place].astype(f32) + full_in[1, place].astype(f32)
        mixed[place] = value
        plain, _ = normalize(value)
        big[place] = (plain * gain_ref[...] + bias_ref[...]).astype(bf16)

    pl.loop(0, half // 64)(second_norm)
    early[0].start()
    pl.loop(half // 64, rows // 64)(second_norm)
    early[1].start()
    for i, side in enumerate(sides):
        pl.semaphore_signal(full_free.at[i], inc=1, device_id=side, device_id_type=MESH)
    feed(0)
    for copy in halves + fulls:
        copy.wait_send()
    back_term(0)
    for copy in early:
        copy.wait_recv()
    start(across)
    start(late)

    def cot_columns(t):
        return pltpu.make_async_copy(cot_ref.at[:, pl.ds(t * 512, 512)], columns.at[t % 2], column_sem.at[t])

    cot_columns(0).start()
    cot_columns(1).start()
    for copy in across:
        copy.wait_recv()
    feed(3)
    back_term(3)
    send_halves(1)
    for copy in late:
        copy.wait_recv()
    feed(1)
    feed(2)
    back_term(1)
    back_term(2)
    take_halves(1)

    def staged_out(out, t, slot):
        return pltpu.make_async_copy(staged.at[slot], out.at[pl.ds(t * 512, 512)], staged_sem.at[slot])

    def weight_grad(out, t, left_of, right):
        for j in range(unit // 256):
            tile = pl.ds(j * 256, 256)
            product = None
            for place in (pl.ds(0, 2 * rows), pl.ds(2 * rows, 2 * rows)):
                more = dot_tn(left_of(place), units[right, place, tile])
                product = more if product is None else product + more
            staged[t % 2, :, tile] = product.astype(bf16)
        staged_out(out, t, t % 2).start()

    for t in range(4):
        cot_columns(t).wait()
        if t >= 2:
            staged_out(down_grad_out, t - 2, t % 2).wait()
        weight_grad(down_grad_out, t, lambda place: columns[t % 2, place], 0)
        if t < 2:
            cot_columns(t + 2).start()
    for t in range(4):
        if t < 2:
            staged_out(down_grad_out, t + 2, t % 2).wait()
        else:
            staged_out(up_grad_out, t - 2, t % 2).wait()
        weight_grad(up_grad_out, t, lambda place: big[place, pl.ds(t * 512, 512)], 1)

    def feed_out(t):
        return pltpu.make_async_copy(columns.at[t % 2], feed_ref.at[:, pl.ds(t * 512, 512)], feed_sem.at[t % 2])

    for t in range(4):
        if t >= 2:
            feed_out(t - 2).wait()

        @pl.loop(0, 4)
        def _(r):
            place = block_of(r * rows, rows)
            columns[t % 2, place] = dot_nt(units[0, place], units[3, pl.ds(t * 512, 512)]).astype(bf16)

        feed_out(t).start()

        @pl.loop(0, rows // 64)
        def _(i):
            place = block_of(i * 64, 64)
            tile = pl.ds(t * 512, 512)
            plus[place, tile] = (mixed[place, tile] + columns[t % 2, place].astype(f32)).astype(bf16)

    plus_out = pltpu.make_async_copy(plus, plus_ref, out_sem.at[0])
    plus_out.start()
    for copy in halves:
        copy.wait_send()
    cot_own = pltpu.make_async_copy(cot_ref.at[pl.ds(0, rows)], terms.at[2], load_sem.at[7])
    cot_own.start()
    total[...] = jnp.zeros_like(total)
    cot_own.wait()
    for copy in fulls:
        copy.wait_recv()

    @pl.loop(0, rows // 64)
    def _(i):
        place = block_of(i * 64, 64)
        grad = terms[3, place].astype(f32) + full_in[0, place].astype(f32) + full_in[1, place].astype(f32)
        plain, scale = normalize(mixed[place])
        back = terms[2, place].astype(f32) + normalize_back(grad, plain, scale, gain_ref[...])
        full_in[0, place] = back.astype(bf16)
        total[0:1, :] += jnp.sum(grad * plain, axis=0, keepdims=True)
        total[1:2, :] += jnp.sum(grad, axis=0, keepdims=True)

    low_out = pltpu.make_async_copy(full_in.at[0], low_ref, out_sem.at[1])
    low_out.start()
    late_ref[...] = total[...]

    for t in (2, 3):
        staged_out(up_grad_out, t, t % 2).wait()
        feed_out(t).wait()
    for copy in fulls + early + across + late:
        copy.wait_send()
    for a in range(2):
        for j in range(3):
            pl.when((z < layers - 1) & (z - j >= 0))(lambda: rise(a, j).wait_send())
            pl.when((z > 0) & (z + j < layers))(lambda: sink(a, j).wait_send())
        for j in range(-3, 4):
            pl.when((z + j >= 0) & (z + j < layers))(lambda: to_twin(a, j).wait_send())
    plus_out.wait()
    low_out.wait()


def middle_exchange(gated, w_out, up_shard, down_shard, cot_all, tokens, gain, bias):
    token_rows, width = tokens.shape
    rows = 4 * token_rows
    unit = gated.shape[1]
    anywhere = pl.BlockSpec(memory_space=pl.ANY)
    in_vmem = pl.BlockSpec(memory_space=pltpu.VMEM)
    sem = pltpu.SemaphoreType.DMA
    regular = pltpu.SemaphoreType.REGULAR
    vmem = pltpu.VMEM
    return pl.pallas_call(
        middle_kernel,
        out_shape=[
            jax.ShapeDtypeStruct((token_rows, width), bf16),
            jax.ShapeDtypeStruct((token_rows, width), bf16),
            jax.ShapeDtypeStruct((rows, width), bf16),
            jax.ShapeDtypeStruct((width, unit), bf16),
            jax.ShapeDtypeStruct((width, unit), bf16),
            jax.ShapeDtypeStruct((2, width), f32),
        ],
        in_specs=[anywhere] * 6 + [in_vmem] * 2,
        out_specs=[anywhere] * 5 + [in_vmem],
        scratch_shapes=[
            vmem((rows, width), bf16),
            vmem((5, rows, unit), bf16),
            vmem((2, rows, 512), bf16),
            vmem((2, 512, unit), bf16),
            vmem((4, token_rows, width), bf16),
            vmem((2, token_rows // 2, width), bf16),
            vmem((2, token_rows, width), bf16),
            vmem((token_rows, width), f32),
            vmem((token_rows, width), bf16),
            vmem((2, width), f32),
            sem((8,)), sem((4,)), sem((2,)), sem((2,)), sem((2,)),
            sem((2, 3)), sem((2, 3)), sem((2, 3)), sem((2, 3)), sem((2, 7)), sem((2, 7)),
            sem((6,)), sem((6,)), sem((2,)), sem((2,)), sem((2,)), sem((2,)),
            regular((2,)), regular((2,)), regular,
        ],
        compiler_params=pltpu.CompilerParams(
            collective_id=4, has_side_effects=True, vmem_limit_bytes=63_400_000
        ),
        name="middle_exchange",
    )(gated, w_out, up_shard, down_shard, cot_all, tokens, gain.reshape(1, width), bias.reshape(1, width))


def closing_kernel(
    heads,
    normed1_ref, up_ref, down_ref, feed_ref, w_out_ref, w_qkv_ref, w_gate_ref,
    gate_ref, grouped_ref, gated_ref, scale_ref, field_ref, past_ref, angle_ref, info_ref,
    low_ref, token_ref, row_ref, decay_ref, gain_ref, late_ref,
    result_ref, grad_ref, query_out, key_out, value_out, gate_out, out_out, up_out, down_out, sums_ref,
    big, units, columns, terms, half_in, full_in, products, twin_in, line_in,
    state_ref, past_in, scale_in, angle_in, info_in, given, landed, total,
    unit_sem, column_sem, chunk_sem, out_sem, mixed_sem, over_send, over_recv, onward_send, onward_recv,
    half_send, half_recv, full_send, full_recv, twin_send, twin_recv, line_send, line_recv, sum_send, sum_recv,
    twin_free, line_free, half_free, full_free,
):
    dp = lax.axis_index("dp")
    tensor = lax.axis_index("tensor")
    z = lax.div(dp, 2)
    core = lax.rem(dp, 2)
    rows = token_ref.shape[0]
    half = rows // 2
    width = token_ref.shape[1]
    unit = units.shape[2]
    depth = columns.shape[2] // 2
    at_end = (z == 0) | (z == 3)
    upper = z >= 2
    twin = (dp + 1 - 2 * core, tensor)
    over_x = (dp, tensor + 1 - 2 * lax.rem(tensor, 2))
    over_y = (dp, lax.rem(tensor + 2, 4))
    here = dp * 4 + tensor
    peers = 32
    last = 5

    def layer(index):
        return (2 * index + core, tensor)

    def seen(index):
        return jnp.where(upper, 3 - index, index)

    end = layer(seen(0))
    near = layer(seen(1))
    opposite = layer(seen(2))
    targets = [seen(3), seen(2), jnp.where(at_end, seen(1), seen(0)), z]

    def remote(src, dst, send, recv, device):
        return pltpu.make_async_remote_copy(
            src_ref=src, dst_ref=dst, send_sem=send, recv_sem=recv, device_id=device, device_id_type=MESH
        )

    def block_of(start, count):
        return pl.ds(pl.multiple_of(start, count), count)


    def whole(index, ref, sem):
        return [pltpu.make_async_copy(ref, units.at[index], unit_sem.at[sem])]

    def part(index, ref, start, sem):
        return [pltpu.make_async_copy(ref.at[:, pl.ds(start, unit)], units.at[index], unit_sem.at[sem])]

    def start(copies):
        for copy in copies:
            copy.start()

    def wait(copies):
        for copy in copies:
            copy.wait()

    out_load = whole(3, w_out_ref, 4)
    feed_load = [
        pltpu.make_async_copy(feed_ref.at[pl.ds((i + 1) * rows, rows)], terms.at[i], unit_sem.at[i]) for i in range(3)
    ]
    gated_load = whole(2, gated_ref, 6)
    w_gate_load = whole(3, w_gate_ref, 7)
    w_value_load = part(2, w_qkv_ref, unit, 8)
    w_key_load = part(1, w_qkv_ref, 0, 9)


    sources = [up_ref, down_ref, normed1_ref, None, normed1_ref, normed1_ref]

    def given_copy(r, k):
        place = block_of(targets[k] * 2 * depth, 2 * depth)
        return pltpu.make_async_copy(sources[r].at[place], products.at[r, k], column_sem.at[4 * r + k])

    def column_copy(r, k):
        place = block_of(targets[k] * 2 * depth, 2 * depth)
        return pltpu.make_async_copy(sources[r].at[:, place], columns.at[k % 2], column_sem.at[k])

    def prefetch(r):
        column_copy(r, 0).start()
        column_copy(r, 1).start()

    mine = block_of(core * depth, depth)
    theirs = block_of((1 - core) * depth, depth)

    def to_twin(r, k):
        return remote(
            products.at[r % 2, k, theirs], twin_in.at[k % 2], twin_send.at[r % 2, k], twin_recv.at[k % 2], twin
        )

    def along(r, k, slot, device):
        return remote(
            products.at[r % 2, k, mine], line_in.at[slot], line_send.at[r % 2, k], line_recv.at[slot], device
        )

    def send_to_twin(r, k):
        if r >= 1 or k >= 2:
            pl.semaphore_wait(twin_free.at[k % 2], 1)
        to_twin(r, k).start()

    def multiply(r, k):
        to_twin(r - 2, k).wait_send()
        if k < 3:
            along(r - 2, k, 0, end).wait_send()
        else:
            wait(outputs(r - 2))
        if sources[r] is not None:
            column_copy(r, k).wait()

        @pl.loop(0, unit // 512)
        def _(j):
            tile = block_of(j * 512, 512)
            product = None
            for place in (pl.ds(0, 2 * rows), pl.ds(2 * rows, 2 * rows)):
                if r < 4:
                    right = units[(None, None, 0, 2)[r], place, tile]
                else:
                    right = big[place, block_of((r - 4) * unit + j * 512, 512)]
                if sources[r] is None:
                    left = big[place, block_of(targets[k] * 2 * depth, 2 * depth)]
                else:
                    left = columns[k % 2, place]
                more = dot_tn(left, right)
                product = more if product is None else product + more
            products[r % 2, k, :, tile] = product.astype(bf16)

        if sources[r] is not None and k + 2 < 4:
            column_copy(r, k + 2).start()
        send_to_twin(r, k)

    def add_to_mine(r, k, others):
        @pl.loop(0, depth // 64)
        def _(i):
            inner = block_of(core * depth + i * 64, 64)
            value = products[r % 2, k, inner].astype(f32)
            for ref, index in others:
                value = value + ref[index, block_of(i * 64, 64)].astype(f32)
            products[r % 2, k, inner] = value.astype(bf16)

    def settle(r, k):
        to_twin(r, k).wait_recv()
        add_to_mine(r, k, [(twin_in, k % 2)])
        if r < last or k < 2:
            pl.semaphore_signal(twin_free.at[k % 2], inc=1, device_id=twin, device_id_type=MESH)

    def push(r, k):
        @pl.when(at_end)
        def _():
            if r >= 1:
                pl.semaphore_wait(line_free.at[k], 1)
            along(r, k, k, near).start()

    def line_wait(slot):
        along(0, 0, slot, end).wait_recv()

    def used(device, index):
        pl.semaphore_signal(line_free.at[index], inc=1, device_id=device, device_id_type=MESH)

    def pass_on(r, which):
        arrived, sender, slot, device = ((0, end, 3, opposite), (1, end, 4, opposite), (3, opposite, 0, end))[which]

        @pl.when(jnp.logical_not(at_end))
        def _():
            line_wait(arrived)
            add_to_mine(r, which, [(line_in, arrived)])
            if r < last:
                used(sender, (0, 1, 0)[which])
            if r >= 1:
                pl.semaphore_wait(line_free.at[which], 1)
            along(r, which, slot, device).start()

    def outputs(r):
        keys = heads * KEY
        slot = products.at[r % 2, 3]
        if r == 4:
            return [
                pltpu.make_async_copy(slot.at[mine, pl.ds(0, keys)], query_out, out_sem.at[0, 0]),
                pltpu.make_async_copy(slot.at[mine, pl.ds(keys, keys)], key_out, out_sem.at[0, 1]),
            ]
        out = (up_out, down_out, gate_out, out_out, None, value_out)[r]
        return [pltpu.make_async_copy(slot.at[mine], out, out_sem.at[r % 2, 0])]

    def finish(r):
        @pl.when(at_end)
        def _():
            line_wait(0)
            add_to_mine(r, 3, [(line_in, 0)])
            if r < last:
                used(near, 2)

        @pl.when(jnp.logical_not(at_end))
        def _():
            line_wait(2)
            line_wait(4)
            add_to_mine(r, 3, [(line_in, 2), (line_in, 4)])
            if r < last:
                used(end, 2)
                used(opposite, 1)

        start(outputs(r))


    def rows_of(r, first=0, count=rows):
        return pl.ds(r * rows + first, count)

    over = [
        remote(big.at[rows_of(0)], big.at[rows_of(1)], over_send.at[0], over_recv.at[0], over_x),
        remote(big.at[rows_of(0)], big.at[rows_of(2)], over_send.at[1], over_recv.at[1], over_y),
    ]
    onward = [
        remote(big.at[rows_of(2, 0, half)], big.at[rows_of(3, 0, half)], onward_send.at[0], onward_recv.at[0], over_x),
        remote(big.at[rows_of(1, half, half)], big.at[rows_of(3, half, half)], onward_send.at[1], onward_recv.at[1], over_y),
    ]
    halves = [
        remote(terms.at[2, pl.ds(0, half)], half_in.at[0], half_send.at[0], half_recv.at[0], over_x),
        remote(terms.at[2, pl.ds(half, half)], half_in.at[1], half_send.at[1], half_recv.at[1], over_y),
    ]
    fulls = [
        remote(terms.at[0], full_in.at[0], full_send.at[0], full_recv.at[0], over_x),
        remote(terms.at[1], full_in.at[1], full_send.at[1], full_recv.at[1], over_y),
    ]
    sides = (over_x, over_y)

    def send_halves(stage):
        for i, copy in enumerate(halves):
            if stage == 1:
                pl.semaphore_wait(half_free.at[i], 1)
            copy.start()

    def take_halves(stage):
        for copy in halves:
            copy.wait_recv()
        for term, first, slot in ((1, 0, 0), (0, half, 1)):
            @pl.loop(0, half // 64)
            def _(i):
                place = block_of(first + i * 64, 64)
                grown = terms[term, place].astype(f32) + half_in[slot, block_of(i * 64, 64)].astype(f32)
                terms[term, place] = grown.astype(bf16)

        for i, copy in enumerate(fulls):
            if stage == 0:
                pl.semaphore_signal(half_free.at[i], inc=1, device_id=sides[i], device_id_type=MESH)
            else:
                pl.semaphore_wait(full_free.at[i], 1)
            copy.start()

    def project(r):
        slot = (2, 0, 1, 2)[r]

        @pl.loop(0, width // 512)
        def _(j):
            tile = block_of(j * 512, 512)
            term = dot_nt(big[rows_of(r), pl.ds(0, unit)], units[1, tile])
            term = term + dot_nt(big[rows_of(r), pl.ds(unit, unit)], units[2, tile])
            term = term + dot_nt(units[0, rows_of(r)], units[3, tile])
            terms[slot, :, tile] = term.astype(bf16)


    def gate_copies(r):
        return [
            pltpu.make_async_copy(
                ref.at[rows_of(r), pl.ds(h * VAL, VAL)],
                columns.at[r % 2, pl.ds((2 * i + h) * rows, rows)],
                chunk_sem.at[r % 2, 2 * i + h],
            )
            for i, ref in enumerate((gate_ref, grouped_ref))
            for h in range(heads)
        ]

    def gate_back(r):
        wait(gate_copies(r))

        @pl.loop(0, unit // 256)
        def _(j):
            grad = dot_nn(big[rows_of(r)], units[3, :, block_of(j * 256, 256)])
            head = lax.div(j, VAL // 256)
            inner = block_of(lax.rem(j, VAL // 256) * 256, 256)
            raw = columns[r % 2, block_of(head * rows, rows), inner].astype(f32)
            grouped = columns[r % 2, block_of((heads + head) * rows, rows), inner].astype(f32)
            sigmoid = 1.0 / (1.0 + jnp.exp(-raw))
            tile = block_of(j * 256, 256)
            units[0, rows_of(r), tile] = (grad * grouped * (sigmoid * (1.0 + raw * (1.0 - sigmoid)))).astype(bf16)
            units[1, rows_of(r), tile] = grad.astype(bf16)

    chunks = 4 * rows // CHUNK
    per_piece = rows // CHUNK

    def chunk_place(c):
        piece = lax.div(c, per_piece)
        low = lax.rem(lax.rem(piece, 2) + lax.rem(tensor, 2), 2)
        high = lax.rem(lax.div(piece, 2) + lax.div(tensor, 2), 2)
        return (2 * high + low) * per_piece + lax.rem(c, per_piece)

    def chunk_copies(c, slot):
        place = block_of(chunk_place(c) * CHUNK, CHUNK)
        seat = block_of(c * CHUNK, CHUNK)
        keys = heads * KEY
        pieces = [
            (field_ref.at[place, pl.ds(0, keys)], columns.at[slot, pl.ds(0, CHUNK)]),
            (field_ref.at[place, pl.ds(keys, keys)], columns.at[slot, pl.ds(CHUNK, CHUNK)]),
        ]
        for h in range(heads):
            pieces.append((field_ref.at[place, pl.ds(2 * keys + h * VAL, VAL)], columns.at[slot, pl.ds((2 + h) * CHUNK, CHUNK)]))
            pieces.append((gate_ref.at[place, pl.ds(h * VAL, VAL)], columns.at[slot, pl.ds((4 + h) * CHUNK, CHUNK)]))
            pieces.append((grouped_ref.at[place, pl.ds(h * VAL, VAL)], columns.at[slot, pl.ds((6 + h) * CHUNK, CHUNK)]))
        pieces += [
            (past_ref.at[c], past_in.at[slot]),
            (scale_ref.at[place], scale_in.at[slot]),
            (angle_ref.at[seat], angle_in.at[slot]),
            (info_ref.at[seat], info_in.at[slot]),
        ]
        return [pltpu.make_async_copy(src, dst, chunk_sem.at[slot, i]) for i, (src, dst) in enumerate(pieces)]

    def retention_steps(between):
        @pl.loop(0, chunks)
        def _(step):
            c = chunks - 1 - step
            slot = lax.rem(step, 2)
            wait(chunk_copies(c, slot))

            @pl.when(step + 1 < chunks)
            def _():
                start(chunk_copies(c - 1, 1 - slot))

            place = block_of(chunk_place(c) * CHUNK, CHUNK)
            angles = angle_in[slot]
            cosine = angles[:, : KEY // 2]
            sine = angles[:, KEY // 2 :]
            info = info_in[slot]
            same = info[:, 0:1] == row_ref[c]

            for head in range(heads):
                at = pl.ds(head * KEY, KEY)
                query = turn(columns[slot, pl.ds(0, CHUNK), at].astype(f32), cosine, sine).astype(bf16)
                key = turn(columns[slot, pl.ds(CHUNK, CHUNK), at].astype(f32), cosine, sine)
                key = (key * key_scale).astype(bf16)
                value = columns[slot, pl.ds((2 + head) * CHUNK, CHUNK)]
                gate = columns[slot, pl.ds((4 + head) * CHUNK, CHUNK)].astype(f32)
                grouped = columns[slot, pl.ds((6 + head) * CHUNK, CHUNK)].astype(f32)
                into = info[:, 1 + 2 * head : 2 + 2 * head]
                onto = info[:, 2 + 2 * head : 3 + 2 * head]
                scale = scale_in[slot, :, head : head + 1]
                past = past_in[slot, head]
                out_grad_in = units[1, place, pl.ds(head * VAL, VAL)].astype(f32)
                c_in = out_grad_in * (gate / (1.0 + jnp.exp(-gate)))
                mean_c = jnp.mean(c_in, axis=-1, keepdims=True)
                mean_cx = jnp.mean(c_in * grouped, axis=-1, keepdims=True)
                out_grad = (scale * (c_in - mean_c - grouped * mean_cx)).astype(bf16)
                state = state_ref[head]
                state_low = state.astype(bf16)
                masked = jnp.where(same, decay_ref[head], 0.0)
                weights = (masked * dot_nt(query, key)).astype(bf16)
                score_grad = (masked * dot_nt(out_grad, value)).astype(bf16)
                value_grad = dot_tn(weights, out_grad) + onto * dot_nn(key, state_low)
                query_grad = dot_nn(score_grad, key) + into * dot_nt(out_grad, past)
                key_grad = dot_tn(score_grad, query) + onto * dot_nt(value, state_low)
                moved = (query.astype(f32) * into).astype(bf16)
                state_ref[head] = into[CHUNK - 1 :, :] * state + dot_tn(moved, out_grad)
                big[place, pl.ds(head * KEY, KEY)] = turn_back(query_grad, cosine, sine).astype(bf16)
                big[place, pl.ds((heads + head) * KEY, KEY)] = (turn_back(key_grad, cosine, sine) * key_scale).astype(bf16)
                big[place, pl.ds(2 * heads * KEY + head * VAL, VAL)] = value_grad.astype(bf16)

            between(step)


    own_load = pltpu.make_async_copy(low_ref, big.at[rows_of(0)], mixed_sem.at[0])
    own_load.start()
    for r in range(2):
        for k in range(4):
            given_copy(r, k).start()
    start(out_load)
    start(gate_copies(0))
    start(gate_copies(1))
    start(feed_load)

    barrier = pltpu.get_barrier_semaphore()

    def partner(k):
        other = lax.rem(here + k, peers)
        return other, (lax.div(other, 4), lax.rem(other, 4))

    @pl.loop(1, peers)
    def _(k):
        pl.semaphore_signal(barrier, inc=1, device_id=partner(k)[1], device_id_type=MESH)

    pl.semaphore_wait(barrier, peers - 1)

    own_load.wait()
    start(over)
    for k in range(4):
        given_copy(0, k).wait()
        send_to_twin(0, k)
        if k > 0:
            settle(0, k - 1)
            push(0, k - 1)
    settle(0, 3)
    for k in range(4):
        given_copy(1, k).wait()
        send_to_twin(1, k)
        if k > 0:
            settle(1, k - 1)
    settle(1, 3)
    wait(out_load)
    gate_back(0)
    start(gate_copies(2))
    pass_on(0, 0)
    push(1, 0)
    pass_on(0, 1)
    push(1, 1)
    pass_on(0, 2)
    for copy in over:
        copy.wait_recv()
    start(onward)
    gate_back(1)
    start(gate_copies(3))
    finish(0)
    push(1, 2)
    gate_back(2)
    pass_on(1, 0)
    pass_on(1, 1)
    wait(feed_load)
    start(gated_load)
    for copy in onward:
        copy.wait_recv()
    send_halves(0)
    gate_back(3)
    prefetch(2)
    start(w_gate_load)
    pass_on(1, 2)
    state_ref[...] = jnp.zeros_like(state_ref)

    def produce(r, k, pushed=True):
        multiply(r, k)
        if k > 0:
            settle(r, k - 1)
            if pushed:
                push(r, k - 1)

    produce(2, 0)
    produce(2, 1)
    finish(1)
    produce(2, 2)
    produce(2, 3)
    settle(2, 3)
    start(chunk_copies(chunks - 1, 0))
    take_halves(0)
    wait(gated_load)
    produce(3, 0)
    produce(3, 1, False)
    pass_on(2, 0)
    push(3, 0)
    produce(3, 2, False)
    produce(3, 3, False)
    settle(3, 3)
    start(w_value_load)
    for copy in over + onward:
        copy.wait_send()

    def between(step):
        @pl.when(step == 1)
        def _():
            pass_on(2, 1)
            push(3, 1)

        @pl.when(step == 2)
        def _():
            pass_on(2, 2)

        @pl.when(step == 5)
        def _():
            finish(2)
            push(3, 2)

    retention_steps(between)
    start(w_key_load)
    prefetch(4)
    pass_on(3, 0)
    for copy in halves:
        copy.wait_send()
    wait(w_gate_load)
    wait(w_value_load)
    wait(w_key_load)
    project(3)
    send_halves(1)
    for copy in fulls:
        copy.wait_recv()
    result_copy = pltpu.make_async_copy(full_in, result_ref, mixed_sem.at[1])
    result_copy.start()
    produce(4, 0)
    produce(4, 1)
    pass_on(3, 1)
    result_copy.wait()
    for i, side in enumerate(sides):
        pl.semaphore_signal(full_free.at[i], inc=1, device_id=side, device_id_type=MESH)
    for copy in fulls:
        copy.wait_send()
    project(1)
    pass_on(3, 2)
    project(2)
    take_halves(1)
    finish(3)
    produce(4, 2)
    produce(4, 3, False)
    push(4, 2)
    settle(4, 3)
    prefetch(5)
    pass_on(4, 0)
    produce(5, 0)
    produce(5, 1)
    pass_on(4, 1)
    produce(5, 2)
    pass_on(4, 2)
    produce(5, 3, False)
    settle(5, 3)
    finish(4)
    push(5, 2)
    pass_on(5, 0)
    for copy in halves:
        copy.wait_send()
    project(0)
    pass_on(5, 1)
    pass_on(5, 2)
    for copy in fulls:
        copy.wait_recv()
        copy.wait_send()
    last_loads = [
        pltpu.make_async_copy(token_ref, terms.at[0], mixed_sem.at[2]),
        pltpu.make_async_copy(low_ref, terms.at[1], mixed_sem.at[0]),
    ]
    start(last_loads)
    total[...] = jnp.zeros_like(total)
    wait(last_loads)

    @pl.loop(0, rows // 64)
    def _(i):
        place = block_of(i * 64, 64)
        normed_grad = terms[2, place].astype(f32) + full_in[0, place].astype(f32) + full_in[1, place].astype(f32)
        plain, scale = normalize(terms[0, place].astype(f32))
        grad = terms[1, place].astype(f32) + normalize_back(normed_grad, plain, scale, gain_ref[...])
        full_in[0, place] = grad.astype(bf16)
        total[0:1, :] += jnp.sum(normed_grad * plain, axis=0, keepdims=True)
        total[1:2, :] += jnp.sum(normed_grad, axis=0, keepdims=True)

    grad_copy = pltpu.make_async_copy(full_in.at[0], grad_ref, mixed_sem.at[3])
    grad_copy.start()

    total[2:4, :] = late_ref[...]
    for k in range(peers // 2):
        given[k] = total[:, k * 128 : (k + 1) * 128]

    def sum_copy(k):
        other, device = partner(k)
        return remote(given.at[lax.div(other, 2)], landed.at[k], sum_send.at[k], sum_recv.at[k], device)

    @pl.loop(1, peers)
    def _(k):
        sum_copy(k).start()

    sums_ref[...] = given[lax.div(here, 2)]

    @pl.loop(1, peers)
    def _(k):
        sum_copy(k).wait()
        sums_ref[...] += landed[k]

    finish(5)

    for r in (4, 5):
        for k in range(4):
            to_twin(r, k).wait_send()
            if k < 3:
                along(r, k, 0, end).wait_send()
    wait(outputs(4) + outputs(5))
    grad_copy.wait()


def cast_kernel(plus_ref, parts_ref, *refs):
    count = len(refs) // 2
    total = plus_ref[...].astype(f32) + parts_ref[0].astype(f32) + parts_ref[1].astype(f32)
    refs[count][...] = total.astype(bf16)
    for i, (source, target) in enumerate(zip(refs[:count], refs[count + 1 :])):
        value = source[...].astype(target.dtype)
        target[...] = value.T if i >= count - 2 else value


def cast_all(plus, parts, arrays):
    steps = 2

    def slab(rows, width):
        return pl.BlockSpec((rows // steps, width), lambda j: (j, 0))

    rows, width = plus.shape
    in_specs = [slab(rows, width), pl.BlockSpec((2, rows // steps, width), lambda j: (0, j, 0))]
    out_specs, shapes = [slab(rows, width)], [jax.ShapeDtypeStruct(plus.shape, bf16)]
    for i, v in enumerate(arrays):
        rows, width = v.shape
        in_specs.append(slab(rows, width))
        if i >= len(arrays) - 2:
            out_specs.append(pl.BlockSpec((width, rows // steps), lambda j: (0, j)))
            shapes.append(jax.ShapeDtypeStruct((width, rows), f32))
        else:
            out_specs.append(slab(rows, width))
            shapes.append(jax.ShapeDtypeStruct((rows, width), bf16 if i == 0 else f32))
    return pl.pallas_call(
        cast_kernel,
        grid=(steps,),
        in_specs=in_specs,
        out_specs=out_specs,
        out_shape=shapes,
        compiler_params=pltpu.CompilerParams(vmem_limit_bytes=60 * 1024 * 1024),
        name="last_casts",
    )(plus, parts, *arrays)


def closing_exchange(heads, operands, small):
    token_rows, width = operands[-1].shape
    rows = 4 * token_rows
    depth = width // 8
    keys, values = heads * KEY, heads * VAL
    unit = operands[1].shape[1]
    anywhere = pl.BlockSpec(memory_space=pl.ANY)
    in_vmem = pl.BlockSpec(memory_space=pltpu.VMEM)
    sem = pltpu.SemaphoreType.DMA
    regular = pltpu.SemaphoreType.REGULAR
    vmem = pltpu.VMEM
    return pl.pallas_call(
        functools.partial(closing_kernel, heads),
        out_shape=[
            jax.ShapeDtypeStruct((2, token_rows, width), bf16),
            jax.ShapeDtypeStruct((token_rows, width), bf16),
            jax.ShapeDtypeStruct((depth, keys), bf16),
            jax.ShapeDtypeStruct((depth, keys), bf16),
            jax.ShapeDtypeStruct((depth, values), bf16),
            jax.ShapeDtypeStruct((depth, values), bf16),
            jax.ShapeDtypeStruct((depth, unit), bf16),
            jax.ShapeDtypeStruct((depth, unit), bf16),
            jax.ShapeDtypeStruct((depth, unit), bf16),
            jax.ShapeDtypeStruct((8, 128), f32),
        ],
        in_specs=[anywhere] * len(operands) + [in_vmem] * len(small),
        out_specs=[anywhere] * 9 + [in_vmem],
        scratch_shapes=[
            vmem((rows, width), bf16),
            vmem((4, rows, unit), bf16),
            vmem((2, rows, 2 * depth), bf16),
            vmem((3, token_rows, width), bf16),
            vmem((2, token_rows // 2, width), bf16),
            vmem((2, token_rows, width), bf16),
            vmem((2, 4, 2 * depth, unit), bf16),
            vmem((2, depth, unit), bf16),
            vmem((5, depth, unit), bf16),
            vmem((heads, KEY, VAL), f32),
            vmem((2, heads, KEY, VAL), bf16),
            vmem((2, CHUNK, 128), f32),
            vmem((2, CHUNK, KEY), f32),
            vmem((2, CHUNK, 128), f32),
            vmem((16, 8, 128), f32),
            vmem((32, 8, 128), f32),
            vmem((8, width), f32),
            sem((10,)), sem((8,)), sem((2, 12)), sem((2, 2)), sem((4,)),
            sem((2,)), sem((2,)), sem((2,)), sem((2,)),
            sem((2,)), sem((2,)), sem((2,)), sem((2,)),
            sem((2, 4)), sem((2,)), sem((2, 3)), sem((5,)), sem((32,)), sem((32,)),
            regular((2,)), regular((3,)), regular((2,)), regular((2,)),
        ],
        compiler_params=pltpu.CompilerParams(
            collective_id=3, has_side_effects=True, vmem_limit_bytes=63_400_000
        ),
        name="closing_exchange",
    )(*operands, *small)


def body(tokens, cotangent, segment, first_gain, first_bias, query_weight, key_weight, value_weight, gate_weight, out_weight, second_gain, second_bias, up_weight, down_weight):
    devices = lax.axis_size("tensor")
    rows = tokens.shape[0]
    heads = query_weight.shape[1] // KEY
    here = lax.axis_index("tensor")
    which = (here if devices == 4 else jnp.zeros_like(here)).astype(jnp.int32).reshape(1)

    def per_piece(values):
        return [values[i * rows : (i + 1) * rows] for i in range(devices)]

    if devices == 4 and lax.axis_size("dp") == 8:
        shards = (query_weight, key_weight, value_weight, gate_weight, out_weight, down_weight)
        opened, keys = opening_exchange(heads, shards, tokens, cotangent, segment, first_gain, first_bias)
        w_qkv, w_gate, w_out, normed1_all, cot_all, field, gate, gated, grouped, group_scale, past = opened[:11]
        angles, info, decay, down_shard = opened[11:]
        mixed_low, plus, feed_terms, up_weight_grad, down_weight_grad, late = middle_exchange(
            gated, w_out, up_weight, down_shard, cot_all, tokens, second_gain, second_bias
        )
        parts, input_grad, query_sum, key_sum, value_sum, gate_sum, out_sum, up_sum, down_sum, sums = closing_exchange(
            heads,
            (
                normed1_all, up_weight_grad, down_weight_grad, feed_terms, w_out, w_qkv, w_gate,
                gate, grouped, gated, group_scale, field, past, angles, info,
                mixed_low, tokens,
            ),
            (keys, decay, first_gain.reshape(1, -1), late),
        )
        part = first_gain.shape[0] // 32
        sums = lax.dynamic_slice_in_dim(sums, (here % 2) * part, part, 1)
        norm_sums = [sums[0], sums[1], sums[2], sums[3]]
        result, input_grad, query_sum, key_sum, value_sum, gate_sum, up_sum, out_sum, down_sum = cast_all(
            plus, parts, (input_grad, query_sum, key_sum, value_sum, gate_sum, up_sum, out_sum, down_sum)
        )
    else:
        w_qkv = lax.all_gather(
            jnp.concatenate([query_weight, key_weight, value_weight], axis=1), "dp", axis=0, tiled=True
        )
        w_gate = lax.all_gather(gate_weight, "dp", axis=0, tiled=True)
        w_out = lax.all_gather(out_weight, "dp", axis=1, tiled=True)
        token_rows = tokens.astype(f32)
        unit1, scale1 = normalize(token_rows)
        normed1_all = jnp.concatenate(
            gather_pieces((unit1 * first_gain + first_bias).astype(bf16), devices), axis=0
        )
        cot_all = jnp.concatenate(gather_pieces(cotangent, devices), axis=0)
        tables = retention_tables(segment, heads, here * heads)
        field = dot_nn(normed1_all, w_qkv).astype(bf16)
        gate = dot_nn(normed1_all, w_gate).astype(bf16)
        gated, grouped, group_scale, past = retention_call(False, which, rows, heads, field, gate, tables, ())
        w_down = lax.all_gather(after(down_weight, w_out), "dp", axis=1, tiled=True)
        w_up = lax.all_gather(after(up_weight, w_down), "dp", axis=0, tiled=True)
        branch, begun, _ = scatter_sum([dot_nn(piece, w_out) for piece in per_piece(gated)])

        mixed = token_rows + branch
        unit2, scale2 = normalize(mixed)
        normed2 = (unit2 * second_gain + second_bias).astype(bf16)
        hidden_grads = per_piece(dot_nt(cot_all, after(w_down, normed2)).astype(bf16))

        def feed(piece, hidden_grad):
            value, slope = gelu_both(dot_nn(piece, w_up))
            return after((value.astype(bf16), (hidden_grad.astype(f32) * slope).astype(bf16)))

        fed_own = feed(normed2, hidden_grads[0])
        normed2_pieces = gather_pieces(normed2, devices, fed_own)
        fed = [fed_own] + [feed(piece, grad) for piece, grad in zip(normed2_pieces[1:-1], hidden_grads[1:-1])]
        fed.append(feed(after(normed2_pieces[-1], *fed), hidden_grads[-1]))
        hidden = [f[0] for f in fed]
        up_grad = [f[1] for f in fed]
        terms = [dot_nt(piece, w_up) for piece in up_grad]
        normed2_grad, _, _ = scatter_sum(terms)
        mixed_grad = cotangent.astype(f32) + normalize_back(normed2_grad, unit2, scale2, second_gain)
        gain2_grad = jnp.sum(normed2_grad * unit2, axis=0)
        bias2_grad = jnp.sum(normed2_grad, axis=0)
        mixed_low = mixed_grad.astype(bf16)
        hidden_all = jnp.concatenate(after(hidden, *terms), axis=0)
        normed2_all = jnp.concatenate(after(normed2_pieces, *terms), axis=0)
        up_grad_all = jnp.concatenate(after(up_grad, *terms), axis=0)
        feed_terms = dot_nn(hidden_all, w_down).astype(bf16)
        own_term = feed_terms[:rows].astype(f32)
        up_weight_grad = dot_tn(normed2_all, up_grad_all).astype(bf16)
        down_weight_grad = dot_tn(cot_all, hidden_all).astype(bf16)

        def summed(gradient, dimension):
            return lax.psum_scatter(
                gradient.astype(bf16), "dp", scatter_dimension=dimension, tiled=True
            ).astype(f32)

        up_sum = summed(up_weight_grad, 0)
        down_sum = summed(down_weight_grad, 0).T
        mixed_all = jnp.concatenate(gather_pieces(mixed_low, devices), axis=0)
        ffn, _, _ = scatter_sum([term.astype(f32) for term in per_piece(feed_terms)])
        result = (mixed + ffn).astype(bf16)
        gated_grad = dot_nt(mixed_all, w_out)
        raw = gate.astype(f32)
        sigmoid = 1.0 / (1.0 + jnp.exp(-raw))
        gate_grad = (gated_grad * grouped.astype(f32) * (sigmoid * (1.0 + raw * (1.0 - sigmoid)))).astype(bf16)
        back = retention_call(
            True, which, rows, heads, field, gate, tables, (gated_grad.astype(bf16), grouped, group_scale, past)
        )
        gate_sum = summed(dot_tn(normed1_all, gate_grad), 0)
        out_sum = summed(dot_tn(gated, mixed_all), 1)
        qkv_sum = summed(dot_tn(normed1_all, back), 0)
        keys_end = heads * KEY
        query_sum = qkv_sum[:, :keys_end]
        key_sum = qkv_sum[:, keys_end : 2 * keys_end]
        value_sum = qkv_sum[:, 2 * keys_end :]
        terms = [
            dot_nt(first, w_qkv) + dot_nt(second, w_gate) for first, second in zip(per_piece(back), per_piece(gate_grad))
        ]
        normed1_grad, _, _ = scatter_sum(terms)
        input_grad = (mixed_grad + normalize_back(normed1_grad, unit1, scale1, first_gain)).astype(bf16)
        gain1_grad = jnp.sum(normed1_grad * unit1, axis=0)
        bias1_grad = jnp.sum(normed1_grad, axis=0)
        norm_sums = spread_sum([gain1_grad, bias1_grad, gain2_grad, bias2_grad])
    return (
        result,
        input_grad,
        norm_sums[0],
        norm_sums[1],
        query_sum,
        key_sum,
        value_sum,
        gate_sum,
        out_sum,
        norm_sums[2],
        norm_sums[3],
        up_sum,
        down_sum,
    )


def solution(mesh):
    rows = P(("dp", "tensor"), None)
    vector = P(("dp", "tensor"))
    into = P("dp", "tensor")
    back = P("tensor", "dp")
    return jax.shard_map(
        body,
        mesh=mesh,
        in_specs=(rows, rows, P("dp"), P(), P(), into, into, into, into, back, P(), P(), into, back),
        out_specs=(rows, rows, vector, vector, into, into, into, into, back, vector, vector, into, back),
        check_vma=False,
    )
```

```python
import functools

import jax
import jax.numpy as jnp
from jax import lax
from jax.experimental import pallas as pl
from jax.experimental.pallas import tpu as pltpu
from jax.sharding import PartitionSpec as P

KEY = 256
VAL = 512
CHUNK = 256
QKV = 2 * KEY + VAL

norm_epsilon = 1e-05
group_floor = 0.5
key_scale = KEY ** (-0.5)

f32 = jnp.float32
bf16 = jnp.bfloat16


def dot_nn(left, right):
    return lax.dot_general(left, right, (((1,), (0,)), ((), ())), preferred_element_type=f32)


def dot_nt(left, right):
    return lax.dot_general(left, right, (((1,), (1,)), ((), ())), preferred_element_type=f32)


def dot_tn(left, right):
    return lax.dot_general(left, right, (((0,), (0,)), ((), ())), preferred_element_type=f32)


def tensor_permute(values, bit):
    pairs = [(i, i ^ bit) for i in range(4)]
    return lax.ppermute(values, "tensor", pairs)


def after(values, *tokens):
    return lax.optimization_barrier((values, tokens))[0]


def gather_pieces(own, devices, between=()):
    if devices != 4:
        whole = lax.all_gather(own, "tensor", axis=0, tiled=True)
        return list(jnp.split(whole, devices, axis=0))
    half = own.shape[0] // 2
    from_x = tensor_permute(own, 1)
    from_y = tensor_permute(own, 2)
    lower, upper = after((from_y[:half], from_x[half:]), *between)
    lower = tensor_permute(lower, 1)
    upper = tensor_permute(upper, 2)
    return [own, from_x, from_y, jnp.concatenate([lower, upper], axis=0)]


def scatter_sum(terms):
    if len(terms) != 4:
        stacked = jnp.concatenate([term.astype(bf16) for term in terms], axis=0)
        return lax.psum_scatter(stacked, "tensor", scatter_dimension=0, tiled=True).astype(f32), (stacked,), (stacked,)
    own, over_x, over_y, across = terms
    half = own.shape[0] // 2
    across = across.astype(bf16)
    first = tensor_permute(across[:half], 1)
    second = tensor_permute(across[half:], 2)
    over_y = jnp.concatenate([over_y[:half] + first.astype(f32), over_y[half:]], axis=0)
    over_x = jnp.concatenate([over_x[:half], over_x[half:] + second.astype(f32)], axis=0)
    by_x = tensor_permute(over_x.astype(bf16), 1)
    by_y = tensor_permute(over_y.astype(bf16), 2)
    return own + by_x.astype(f32) + by_y.astype(f32), (first, second), (by_x, by_y)


def spread_sum_kernel(tensor_devices, devices, given_ref, sum_ref, landed_ref, send_sem, recv_sem):
    here = lax.axis_index("dp") * tensor_devices + lax.axis_index("tensor")

    def partner(k):
        other = lax.rem(here + k, devices)
        return other, (lax.div(other, tensor_devices), lax.rem(other, tensor_devices))

    def copy(k):
        other, device = partner(k)
        return pltpu.make_async_remote_copy(
            src_ref=given_ref.at[other],
            dst_ref=landed_ref.at[k],
            send_sem=send_sem.at[k],
            recv_sem=recv_sem.at[k],
            device_id=device,
            device_id_type=pl.DeviceIdType.MESH,
        )

    barrier = pltpu.get_barrier_semaphore()

    @pl.loop(1, devices)
    def _(k):
        pl.semaphore_signal(barrier, inc=1, device_id=partner(k)[1], device_id_type=pl.DeviceIdType.MESH)

    pl.semaphore_wait(barrier, devices - 1)

    @pl.loop(1, devices)
    def _(k):
        copy(k).start()

    sum_ref[...] = given_ref[here]

    @pl.loop(1, devices)
    def _(k):
        copy(k).wait()
        sum_ref[...] += landed_ref[k]


def spread_sum(vectors):
    dp, tensor = lax.axis_size("dp"), lax.axis_size("tensor")
    devices = dp * tensor
    part = vectors[0].shape[0] // devices
    given = jnp.stack([v.reshape(devices, part) for v in vectors], axis=1)
    given = jnp.pad(given, ((0, 0), (0, 8 - len(vectors)), (0, 128 - part)))
    total = pl.pallas_call(
        functools.partial(spread_sum_kernel, tensor, devices),
        out_shape=jax.ShapeDtypeStruct((8, 128), f32),
        in_specs=[pl.BlockSpec(memory_space=pltpu.VMEM)],
        out_specs=pl.BlockSpec(memory_space=pltpu.VMEM),
        scratch_shapes=[
            pltpu.VMEM((devices, 8, 128), f32),
            pltpu.SemaphoreType.DMA((devices,)),
            pltpu.SemaphoreType.DMA((devices,)),
        ],
        compiler_params=pltpu.CompilerParams(collective_id=1, has_side_effects=True),
        name="spread_sum",
    )(given)
    return [total[i, :part] for i in range(len(vectors))]


def normalize(values):
    average = jnp.mean(values, axis=-1, keepdims=True)
    centred = values - average
    variance = jnp.mean(centred * centred, axis=-1, keepdims=True)
    scale = lax.rsqrt(variance + norm_epsilon)
    return centred * scale, scale


def normalize_back(normed_grad, unit, scale, gain):
    g = normed_grad * gain
    mean_g = jnp.mean(g, axis=-1, keepdims=True)
    mean_gx = jnp.mean(g * unit, axis=-1, keepdims=True)
    return scale * (g - mean_g - unit * mean_gx)


def gelu_both(values):
    inner = 0.7978845608 * (values + 0.044715 * values * values * values)
    t = jnp.tanh(inner)
    slope = 0.7978845608 * (1.0 + 3.0 * 0.044715 * values * values)
    return 0.5 * values * (1.0 + t), 0.5 * (1.0 + t) + 0.5 * values * (1.0 - t * t) * slope


def turn(block, cosine, sine):
    a = block[:, : KEY // 2]
    b = block[:, KEY // 2 :]
    return jnp.concatenate([a * cosine - b * sine, b * cosine + a * sine], axis=1)


def turn_back(block, cosine, sine):
    a = block[:, : KEY // 2]
    b = block[:, KEY // 2 :]
    return jnp.concatenate([a * cosine + b * sine, b * cosine - a * sine], axis=1)


def head_parts(field_ref, angles, heads, head):
    cosine = angles[:, : KEY // 2]
    sine = angles[:, KEY // 2 :]
    query_at = head * KEY
    key_at = (heads + head) * KEY
    value_at = 2 * heads * KEY + head * VAL
    query = turn(field_ref[:, query_at : query_at + KEY].astype(f32), cosine, sine).astype(bf16)
    key = turn(field_ref[:, key_at : key_at + KEY].astype(f32), cosine, sine)
    key = (key * key_scale).astype(bf16)
    return query, key, field_ref[:, value_at : value_at + VAL]


def retention_forward(heads, which, field_ref, gate_ref, angle_ref, info_ref, row_ref, decay_ref, gated_ref, grouped_ref, scale_ref, past_ref, state_ref):
    @pl.when(pl.program_id(0) == 0)
    def _():
        state_ref[...] = jnp.zeros_like(state_ref)

    angles = angle_ref[...]
    info = info_ref[...]
    same = info[:, 0:1] == row_ref[0]
    scales = []
    for head in range(heads):
        query, key, value = head_parts(field_ref, angles, heads, head)
        columns = slice(head * VAL, (head + 1) * VAL)
        gate = gate_ref[:, columns].astype(f32)
        into = info[:, 1 + 2 * head : 2 + 2 * head]
        onward = info[:, 2 + 2 * head : 3 + 2 * head]
        state = state_ref[head]
        past_ref[0, head] = state.astype(bf16)
        scores = dot_nt(query, key)
        weights = (jnp.where(same, decay_ref[head], 0.0) * scores).astype(bf16)
        retained = dot_nn(weights, value) + into * dot_nn(query, state.astype(bf16))
        moved = (key.astype(f32) * onward).astype(bf16)
        state_ref[head] = into[CHUNK - 1 :, :] * state + dot_tn(moved, value)
        centred = retained - jnp.mean(retained, axis=-1, keepdims=True)
        scale = lax.rsqrt(jnp.mean(centred * centred, axis=-1, keepdims=True) + group_floor)
        grouped = centred * scale
        gated = gate / (1.0 + jnp.exp(-gate)) * grouped
        gated_ref[:, columns] = gated.astype(bf16)
        grouped_ref[:, columns] = grouped.astype(bf16)
        scales.append(scale)
    lane = lax.broadcasted_iota(jnp.int32, (CHUNK, 128), 1)
    spread = jnp.zeros((CHUNK, 128), f32)
    for head in range(heads):
        spread = jnp.where(lane == head, scales[head], spread)
    scale_ref[...] = spread


def retention_backward(heads, which, field_ref, gate_ref, angle_ref, info_ref, row_ref, decay_ref, grad_ref, grouped_ref, scale_ref, past_ref, back_ref, state_ref):
    @pl.when(pl.program_id(0) == 0)
    def _():
        state_ref[...] = jnp.zeros_like(state_ref)

    angles = angle_ref[...]
    cosine = angles[:, : KEY // 2]
    sine = angles[:, KEY // 2 :]
    info = info_ref[...]
    same = info[:, 0:1] == row_ref[0]
    for head in range(heads):
        query, key, value = head_parts(field_ref, angles, heads, head)
        columns = slice(head * VAL, (head + 1) * VAL)
        gate = gate_ref[:, columns].astype(f32)
        into = info[:, 1 + 2 * head : 2 + 2 * head]
        onward = info[:, 2 + 2 * head : 3 + 2 * head]
        grouped = grouped_ref[:, columns].astype(f32)
        scale = scale_ref[:, head : head + 1]
        c = grad_ref[:, columns].astype(f32) * (gate / (1.0 + jnp.exp(-gate)))
        mean_c = jnp.mean(c, axis=-1, keepdims=True)
        mean_cx = jnp.mean(c * grouped, axis=-1, keepdims=True)
        out_grad = (scale * (c - mean_c - grouped * mean_cx)).astype(bf16)
        state = state_ref[head]
        state_low = state.astype(bf16)
        past = past_ref[0, head]
        masked = jnp.where(same, decay_ref[head], 0.0)
        weights = (masked * dot_nt(query, key)).astype(bf16)
        score_grad = (masked * dot_nt(out_grad, value)).astype(bf16)
        value_grad = dot_tn(weights, out_grad) + onward * dot_nn(key, state_low)
        query_grad = dot_nn(score_grad, key) + into * dot_nt(out_grad, past)
        key_grad = dot_tn(score_grad, query) + onward * dot_nt(value, state_low)
        moved = (query.astype(f32) * into).astype(bf16)
        state_ref[head] = into[CHUNK - 1 :, :] * state + dot_tn(moved, out_grad)
        query_at = head * KEY
        key_at = (heads + head) * KEY
        value_at = 2 * heads * KEY + head * VAL
        back_ref[:, query_at : query_at + KEY] = turn_back(query_grad, cosine, sine).astype(bf16)
        back_ref[:, key_at : key_at + KEY] = (turn_back(key_grad, cosine, sine) * key_scale).astype(bf16)
        back_ref[:, value_at : value_at + VAL] = value_grad.astype(bf16)


def retention_tables(segment, heads, first_head):
    rows = segment.shape[0]
    chunks = rows // CHUNK
    index = jnp.arange(rows, dtype=jnp.int32)
    boundary = jnp.concatenate([jnp.ones((1,), jnp.int32), (segment[1:] != segment[:-1]).astype(jnp.int32)])
    position = index - lax.cummax(jnp.where(boundary > 0, index, 0), axis=0)
    half = KEY // 2
    frequency = jnp.exp(-jnp.log(10000.0) * jnp.arange(half, dtype=f32) / half)
    angles = position.astype(f32)[:, None] * frequency[None, :]
    angles = jnp.concatenate([jnp.cos(angles), jnp.sin(angles)], axis=1)
    head_ids = (first_head + jnp.arange(heads, dtype=jnp.int32)).astype(f32)
    log_decay = jnp.log1p(-jnp.exp2(-5.0 - head_ids))
    last = segment.reshape(chunks, CHUNK)[:, -1]
    before = jnp.concatenate([jnp.full((1,), -2, jnp.int32), last[:-1]])
    offset = (index % CHUNK).astype(f32)
    linked_in = (segment == jnp.repeat(before, CHUNK)) & (segment >= 0)
    linked_on = (segment == jnp.repeat(last, CHUNK)) & (segment >= 0)
    columns = [segment.astype(f32)]
    for head in range(heads):
        columns.append(jnp.where(linked_in, jnp.exp(log_decay[head] * (offset + 1.0)), 0.0))
        columns.append(jnp.where(linked_on, jnp.exp(log_decay[head] * (CHUNK - 1.0 - offset)), 0.0))
    info = jnp.stack(columns, axis=1)
    info = jnp.pad(info, ((0, 0), (0, 128 - info.shape[1])))
    keys = jnp.where(segment >= 0, segment, -7).astype(f32).reshape(chunks, 1, CHUNK)
    distance = (jnp.arange(CHUNK)[:, None] - jnp.arange(CHUNK)[None, :]).astype(f32)
    decay = jnp.where(distance >= 0, jnp.exp(log_decay[:, None, None] * jnp.maximum(distance, 0.0)), 0.0)
    return angles, info, keys, decay


def retention_call(backward, which, piece_rows, heads, field, gate, tables, extra):
    rows = field.shape[0]
    chunks = rows // CHUNK
    angles, info, keys, decay = tables
    per_piece = piece_rows // CHUNK

    def step(i):
        return chunks - 1 - i if backward else i

    def place(i, which_ref):
        c = step(i)
        return ((c // per_piece) ^ which_ref[0]) * per_piece + c % per_piece

    def placed(width):
        return pl.BlockSpec((CHUNK, width), lambda i, w: (place(i, w), 0))

    in_specs = [
        placed(heads * QKV),
        placed(heads * VAL),
        pl.BlockSpec((CHUNK, KEY), lambda i, w: (step(i), 0)),
        pl.BlockSpec((CHUNK, 128), lambda i, w: (step(i), 0)),
        pl.BlockSpec((1, 1, CHUNK), lambda i, w: (step(i), 0, 0)),
        pl.BlockSpec((heads, CHUNK, CHUNK), lambda i, w: (0, 0, 0)),
    ]
    past_spec = pl.BlockSpec((1, heads, KEY, VAL), lambda i, w: (step(i), 0, 0, 0))
    if backward:
        in_specs += [placed(heads * VAL), placed(heads * VAL), placed(128), past_spec]
        out_specs = placed(heads * QKV)
        out_shape = jax.ShapeDtypeStruct((rows, heads * QKV), bf16)
    else:
        out_specs = [placed(heads * VAL), placed(heads * VAL), placed(128), past_spec]
        out_shape = [
            jax.ShapeDtypeStruct((rows, heads * VAL), bf16),
            jax.ShapeDtypeStruct((rows, heads * VAL), bf16),
            jax.ShapeDtypeStruct((rows, 128), f32),
            jax.ShapeDtypeStruct((chunks, heads, KEY, VAL), bf16),
        ]
    products = 15 if backward else 7
    return pl.pallas_call(
        functools.partial(retention_backward if backward else retention_forward, heads),
        grid_spec=pltpu.PrefetchScalarGridSpec(
            num_scalar_prefetch=1,
            grid=(chunks,),
            in_specs=in_specs,
            out_specs=out_specs,
            scratch_shapes=[pltpu.VMEM((heads, KEY, VAL), f32)],
        ),
        out_shape=out_shape,
        compiler_params=pltpu.CompilerParams(
            dimension_semantics=("arbitrary",), vmem_limit_bytes=48 * 1024 * 1024
        ),
        cost_estimate=pl.CostEstimate(
            flops=products * chunks * heads * 2 * CHUNK * CHUNK * CHUNK,
            bytes_accessed=(5 if backward else 4) * rows * heads * (QKV + VAL),
            transcendentals=rows * heads * VAL,
        ),
        name="retention_backward" if backward else "retention_forward",
    )(which, field, gate, angles, info, keys, decay, *extra)


MESH = pl.DeviceIdType.MESH


def opening_kernel(
    heads, query_ref, key_ref, value_ref, gate_ref, out_ref, down_ref, token_ref, cot_ref, segment_ref, row_ref, rate_ref, gain_ref, bias_ref,
    w_qkv_ref, w_gate_ref, w_out_ref, normed_ref, cot_all_ref, field_ref, gate_raw_ref, gated_ref, grouped_ref, scale_ref, past_ref,
    angle_ref, info_ref, decay_ref, down_turned_ref,
    w_qkv, w_gate, w_out, tall, down_turned, normed, product, blocks, angles, info, decay, state, field_out, gate_out, gated_out, grouped_out,
    scale_out, past_out,
    local_sem, block_sem, out_sem, stage_sem, table_sem, up_send, up_recv, down_send, down_recv, core_send, core_recv,
    row_send, row_recv,
):
    dp = lax.axis_index("dp")
    tensor = lax.axis_index("tensor")
    z = lax.div(dp, 2)
    layers = 4
    depth = query_ref.shape[0]
    rows = token_ref.shape[0]
    half = rows // 2
    above = (dp + 2, tensor)
    below = (dp - 2, tensor)
    twin = (dp + 1 - 2 * lax.rem(dp, 2), tensor)
    over_x = (dp, tensor + 1 - 2 * lax.rem(tensor, 2))
    over_y = (dp, lax.rem(tensor + 2, 4))
    keys = heads * KEY
    values = heads * VAL

    def block_of(start, count):
        return pl.ds(pl.multiple_of(start, count), count)

    def start(copies):
        for copy in copies:
            copy.start()

    def wait(copies):
        for copy in copies:
            copy.wait()

    def remote(src, dst, send, recv, device):
        return pltpu.make_async_remote_copy(
            src_ref=src, dst_ref=dst, send_sem=send, recv_sem=recv, device_id=device, device_id_type=MESH
        )

    mine = block_of(dp * depth, depth)
    local = [
        pltpu.make_async_copy(src, dst, local_sem.at[i])
        for i, (src, dst) in enumerate((
            (query_ref, w_qkv.at[mine, pl.ds(0, keys)]),
            (key_ref, w_qkv.at[mine, pl.ds(keys, keys)]),
            (value_ref, w_qkv.at[mine, pl.ds(2 * keys, values)]),
            (gate_ref, w_gate.at[mine]),
            (out_ref, tall),
            (segment_ref, info),
        ))
    ]
    start(local)

    def token_block(i, slot):
        return pltpu.make_async_copy(token_ref.at[block_of(i * 64, 64)], blocks.at[slot], block_sem.at[slot])

    for i in range(4):
        token_block(i, i).start()
    own_cot = pltpu.make_async_copy(cot_ref, cot_all_ref.at[pl.ds(0, rows)], local_sem.at[6])
    own_cot.start()

    barrier = pltpu.get_barrier_semaphore()

    def greet(device):
        pl.semaphore_signal(barrier, inc=1, device_id=device, device_id_type=MESH)

    for device in (twin, over_x, over_y):
        greet(device)
    pl.when(z < layers - 1)(lambda: greet(above))
    pl.when(z > 0)(lambda: greet(below))
    pl.semaphore_wait(barrier, 3 + (z < layers - 1).astype(jnp.int32) + (z > 0).astype(jnp.int32))
    wait(local[:4])


    groups = ((w_qkv, w_gate), (w_out,))

    def shard_copies(g, shard, send_sem, recv_sem, index, device):
        place = block_of(shard * depth, depth)
        return [
            remote(ref.at[place], ref.at[place], send_sem.at[index, i + 2 * g], recv_sem.at[index, i + 2 * g], device)
            for i, ref in enumerate(groups[g])
        ]

    def rise(g, j):
        return shard_copies(g, dp - 2 * j, up_send, up_recv, j, above)

    def sink(g, j):
        return shard_copies(g, dp + 2 * j, down_send, down_recv, j, below)

    def to_twin(g, j):
        return shard_copies(g, dp + 2 * j, core_send, core_recv, j + 3, twin)

    def from_twin(g, j):
        return shard_copies(g, twin[0] + 2 * j, core_send, core_recv, j + 3, twin)

    def wait_recv(copies):
        for copy in copies:
            copy.wait_recv()

    def wait_send(copies):
        for copy in copies:
            copy.wait_send()

    def first_step(g):
        pl.when(z < layers - 1)(lambda: start(rise(g, 0)))
        pl.when(z > 0)(lambda: start(sink(g, 0)))
        start(to_twin(g, 0))

    def step(g, j):
        @pl.when(z - j >= 0)
        def _():
            wait_recv(shard_copies(g, dp - 2 * j, up_send, up_recv, j - 1, twin))
            if j < 3:
                pl.when(z < layers - 1)(lambda: start(rise(g, j)))
            start(to_twin(g, -j))

        @pl.when(z + j < layers)
        def _():
            wait_recv(shard_copies(g, dp + 2 * j, down_send, down_recv, j - 1, twin))
            if j < 3:
                pl.when(z > 0)(lambda: start(sink(g, j)))
            start(to_twin(g, j))

    def twin_step(g, j):
        for signed in sorted({-j, j}):
            @pl.when((z + signed >= 0) & (z + signed < layers))
            def _():
                wait_recv(from_twin(g, signed))

    def rows_of(r, first=0, count=rows):
        return pl.ds(r * rows + first, count)

    def row_copy(index, src, dst, device):
        return remote(src, dst, row_send.at[index], row_recv.at[index], device)

    piece = 64
    cot_early = [
        row_copy(8, cot_ref.at[pl.ds(0, piece)], cot_all_ref.at[rows_of(1, 0, piece)], over_x),
        row_copy(9, cot_ref.at[pl.ds(0, piece)], cot_all_ref.at[rows_of(2, 0, piece)], over_y),
    ]
    cot_over = [
        row_copy(4, cot_ref.at[pl.ds(piece, rows - piece)], cot_all_ref.at[rows_of(1, piece, rows - piece)], over_x),
        row_copy(5, cot_ref.at[pl.ds(piece, rows - piece)], cot_all_ref.at[rows_of(2, piece, rows - piece)], over_y),
    ]

    first_step(0)
    start(cot_early)

    @pl.loop(0, rows // 64)
    def _(i):
        slot = lax.rem(i, 4)
        token_block(i, slot).wait()
        plain, _ = normalize(blocks[slot].astype(f32))
        normed[block_of(i * 64, 64), :] = (plain * gain_ref[...] + bias_ref[...]).astype(bf16)

        @pl.when(i + 4 < rows // 64)
        def _():
            token_block(i + 4, slot).start()

    over = [
        row_copy(0, normed.at[rows_of(0)], normed.at[rows_of(1)], over_x),
        row_copy(1, normed.at[rows_of(0)], normed.at[rows_of(2)], over_y),
    ]
    onward = [
        row_copy(2, normed.at[rows_of(2, 0, half)], normed.at[rows_of(3, 0, half)], over_x),
        row_copy(3, normed.at[rows_of(1, half, half)], normed.at[rows_of(3, half, half)], over_y),
    ]
    cot_onward = [
        row_copy(6, cot_all_ref.at[rows_of(2, 0, half)], cot_all_ref.at[rows_of(3, 0, half)], over_x),
        row_copy(7, cot_all_ref.at[rows_of(1, half, half)], cot_all_ref.at[rows_of(3, half, half)], over_y),
    ]
    start(over)

    local[4].wait()
    w_out[mine, :] = tall[...].T
    down_load = pltpu.make_async_copy(down_ref, tall, local_sem.at[4])
    down_load.start()

    local[5].wait()
    half_key = KEY // 2
    lanes = lax.broadcasted_iota(jnp.int32, (CHUNK, half_key), 1).astype(f32)
    frequency = jnp.exp(lanes * (-9.210340371976184 / half_key))
    chunks = 4 * rows // CHUNK

    @pl.loop(0, chunks)
    def _(c):
        seat = block_of(c * CHUNK, CHUNK)
        own = info[seat, 0:1]
        ranked = jnp.where(own < 0, 3.0, own)
        before = jnp.zeros((CHUNK, 1), f32)
        for other in range(chunks):
            seen = row_ref[other]
            seen = jnp.where(seen < 0, 3.0, seen)
            before = before + jnp.sum((seen < ranked).astype(f32), axis=1, keepdims=True)
        index = lax.broadcasted_iota(jnp.int32, (CHUNK, 1), 0) + c * CHUNK
        turned = (index.astype(f32) - before) * frequency
        angles[seat, 0:half_key] = jnp.cos(turned)
        angles[seat, half_key:KEY] = jnp.sin(turned)

    distance = lax.broadcasted_iota(jnp.int32, (CHUNK, CHUNK), 0) - lax.broadcasted_iota(jnp.int32, (CHUNK, CHUNK), 1)
    span = jnp.maximum(distance, 0).astype(f32)
    for head in range(heads):
        decay[head] = jnp.where(distance >= 0, jnp.exp(rate_ref[head : head + 1, 0:1] * span), 0.0)
    down_load.wait()
    down_turned[...] = tall[...].T
    table_outs = [
        pltpu.make_async_copy(down_turned, down_turned_ref, table_sem.at[3]),
        pltpu.make_async_copy(angles, angle_ref, table_sem.at[0]),
        pltpu.make_async_copy(decay, decay_ref, table_sem.at[1]),
    ]
    start(table_outs)


    at_end = (z == 0) | (z == 3)

    def seen_from_end(index):
        return jnp.where(z >= 2, 3 - index, index)

    order = [z, jnp.where(at_end, seen_from_end(1), seen_from_end(0)), seen_from_end(2), seen_from_end(3)]

    def project(r, s):
        deep = block_of(order[s] * 2 * depth, 2 * depth)

        @pl.loop(0, (2 * keys + values) // 512)
        def _(j):
            tile = block_of(j * 512, 512)
            more = dot_nn(normed[rows_of(r), deep], w_qkv[deep, tile])
            product[rows_of(r), tile] = more if s == 0 else product[rows_of(r), tile] + more

        @pl.loop(0, values // 512)
        def _(j):
            tile = block_of(j * 512, 512)
            more = dot_nn(normed[rows_of(r), deep], w_gate[deep, tile])
            place = block_of(2 * keys + values + j * 512, 512)
            product[rows_of(r), place] = more if s == 0 else product[rows_of(r), place] + more


    per_piece = rows // CHUNK

    def chunk_place(c):
        piece = lax.div(c, per_piece)
        low = lax.rem(lax.rem(piece, 2) + lax.rem(tensor, 2), 2)
        high = lax.rem(lax.div(piece, 2) + lax.div(tensor, 2), 2)
        return (2 * high + low) * per_piece + lax.rem(c, per_piece)

    def chunk_outs(c):
        place = block_of(chunk_place(c) * CHUNK, CHUNK)
        pairs = (
            (field_out, field_ref.at[place]),
            (gate_out, gate_raw_ref.at[place]),
            (gated_out, gated_ref.at[place]),
            (grouped_out, grouped_ref.at[place]),
            (scale_out, scale_ref.at[place]),
            (past_out, past_ref.at[c]),
        )
        return [pltpu.make_async_copy(src, dst, stage_sem.at[i]) for i, (src, dst) in enumerate(pairs)]

    def retention(between):
        state[...] = jnp.zeros_like(state)

        @pl.loop(0, chunks)
        def _(c):
            place = block_of(chunk_place(c) * CHUNK, CHUNK)
            seat = block_of(c * CHUNK, CHUNK)
            cosine = angles[seat, 0:half_key]
            sine = angles[seat, half_key:KEY]
            own = info[seat, 0:1]
            same = own == row_ref[c]
            entering = (own == row_ref[jnp.maximum(c - 1, 0)][:, CHUNK - 1 :]) & (c > 0)
            leaving = own == row_ref[c][:, CHUNK - 1 :]
            offset = lax.broadcasted_iota(jnp.int32, (CHUNK, 1), 0).astype(f32)
            lane = lax.broadcasted_iota(jnp.int32, (CHUNK, 128), 1)
            facts = jnp.where(lane == 0, own, 0.0)
            scales = jnp.zeros((CHUNK, 128), f32)

            @pl.when(c > 0)
            def _():
                wait(chunk_outs(c - 1))

            for head in range(heads):
                rate = rate_ref[head : head + 1, 0:1]
                into = jnp.where(entering, jnp.exp(rate * (offset + 1.0)), 0.0)
                onto = jnp.where(leaving, jnp.exp(rate * (CHUNK - 1.0 - offset)), 0.0)
                facts = jnp.where(lane == 1 + 2 * head, into, facts)
                facts = jnp.where(lane == 2 + 2 * head, onto, facts)
                query_raw = product[place, pl.ds(head * KEY, KEY)]
                key_raw = product[place, pl.ds(keys + head * KEY, KEY)]
                value = product[place, pl.ds(2 * keys + head * VAL, VAL)].astype(bf16)
                gate = product[place, pl.ds(2 * keys + values + head * VAL, VAL)]
                query_raw = query_raw.astype(bf16)
                key_raw = key_raw.astype(bf16)
                gate_low = gate.astype(bf16)
                field_out[:, pl.ds(head * KEY, KEY)] = query_raw
                field_out[:, pl.ds(keys + head * KEY, KEY)] = key_raw
                field_out[:, pl.ds(2 * keys + head * VAL, VAL)] = value
                gate_out[:, pl.ds(head * VAL, VAL)] = gate_low
                query = turn(query_raw.astype(f32), cosine, sine).astype(bf16)
                key = (turn(key_raw.astype(f32), cosine, sine) * key_scale).astype(bf16)
                memory = state[head]
                memory_low = memory.astype(bf16)
                past_out[head] = memory_low
                scores = dot_nt(query, key)
                weights = (jnp.where(same, decay[head], 0.0) * scores).astype(bf16)
                retained = dot_nn(weights, value) + into * dot_nn(query, memory_low)
                moved = (key.astype(f32) * onto).astype(bf16)
                state[head] = into[CHUNK - 1 :, :] * memory + dot_tn(moved, value)
                centred = retained - jnp.mean(retained, axis=-1, keepdims=True)
                scale = lax.rsqrt(jnp.mean(centred * centred, axis=-1, keepdims=True) + group_floor)
                grouped = centred * scale
                columns = pl.ds(head * VAL, VAL)
                gated_out[:, columns] = (gate / (1.0 + jnp.exp(-gate)) * grouped).astype(bf16)
                grouped_out[:, columns] = grouped.astype(bf16)
                scales = jnp.where(lane == head, scale, scales)
            info[seat, :] = facts
            scale_out[...] = scales
            start(chunk_outs(c))
            between(c)

        wait(chunk_outs(chunks - 1))


    twin_step(0, 0)
    project(0, 0)
    step(0, 1)
    twin_step(0, 1)
    project(0, 1)
    wait_recv(over)
    start(onward)
    start(cot_over)
    for r in (1, 2):
        for s in (0, 1):
            project(r, s)
    step(0, 2)
    first_step(1)
    twin_step(0, 2)
    for r in (0, 1, 2):
        project(r, 2)
    wait_recv(onward)
    normed_out = pltpu.make_async_copy(normed, normed_ref, local_sem.at[7])
    normed_out.start()
    for s in (0, 1, 2):
        project(3, s)
    step(0, 3)
    twin_step(0, 3)
    for r in range(4):
        project(r, 3)
    step(1, 1)
    w_outs = [
        pltpu.make_async_copy(w_qkv, w_qkv_ref, out_sem.at[0]),
        pltpu.make_async_copy(w_gate, w_gate_ref, out_sem.at[1]),
    ]
    start(w_outs)

    def between(c):
        @pl.when(c == 2)
        def _():
            wait_recv(cot_early + cot_over)
            start(cot_onward)

        @pl.when(c == 4)
        def _():
            step(1, 2)

    retention(between)
    info_out = pltpu.make_async_copy(info, info_ref, table_sem.at[2])
    info_out.start()
    step(1, 3)
    for j in range(4):
        twin_step(1, j)
    w_out_out = pltpu.make_async_copy(w_out, w_out_ref, out_sem.at[2])
    w_out_out.start()
    wait_recv(cot_onward)

    wait_send(over + onward + cot_early + cot_over + cot_onward)
    for g in range(2):
        for j in range(3):
            pl.when((z < layers - 1) & (z - j >= 0))(lambda: wait_send(rise(g, j)))
            pl.when((z > 0) & (z + j < layers))(lambda: wait_send(sink(g, j)))
        for j in range(-3, 4):
            pl.when((z + j >= 0) & (z + j < layers))(lambda: wait_send(to_twin(g, j)))
    wait(table_outs + w_outs + [normed_out, own_cot, info_out, w_out_out])


def opening_exchange(heads, shards, tokens, cotangent, segment, gain, bias):
    dp = lax.axis_size("dp")
    depth, keys = shards[0].shape
    values = shards[2].shape[1]
    unit = shards[4].shape[0]
    token_rows, width = tokens.shape
    rows = 4 * token_rows
    chunks = rows // CHUNK
    anywhere = pl.BlockSpec(memory_space=pl.ANY)
    in_vmem = pl.BlockSpec(memory_space=pltpu.VMEM)
    sem = pltpu.SemaphoreType.DMA
    vmem = pltpu.VMEM
    here = lax.axis_index("tensor") * heads
    head_ids = (here + jnp.arange(8, dtype=jnp.int32)).astype(f32)
    rates = jnp.broadcast_to(jnp.log1p(-jnp.exp2(-5.0 - head_ids))[:, None], (8, 128))
    wide_segment = jnp.broadcast_to(segment.astype(f32)[:, None], (rows, 128))
    row_segment = jnp.where(segment >= 0, segment, -7).astype(f32).reshape(chunks, 1, CHUNK)
    results = pl.pallas_call(
        functools.partial(opening_kernel, heads),
        out_shape=[
            jax.ShapeDtypeStruct((dp * depth, 2 * keys + values), bf16),
            jax.ShapeDtypeStruct((dp * depth, values), bf16),
            jax.ShapeDtypeStruct((dp * depth, unit), bf16),
            jax.ShapeDtypeStruct((rows, width), bf16),
            jax.ShapeDtypeStruct((rows, width), bf16),
            jax.ShapeDtypeStruct((rows, 2 * keys + values), bf16),
            jax.ShapeDtypeStruct((rows, values), bf16),
            jax.ShapeDtypeStruct((rows, values), bf16),
            jax.ShapeDtypeStruct((rows, values), bf16),
            jax.ShapeDtypeStruct((rows, 128), f32),
            jax.ShapeDtypeStruct((chunks, heads, KEY, VAL), bf16),
            jax.ShapeDtypeStruct((rows, KEY), f32),
            jax.ShapeDtypeStruct((rows, 128), f32),
            jax.ShapeDtypeStruct((heads, CHUNK, CHUNK), f32),
            jax.ShapeDtypeStruct((depth, unit), bf16),
        ],
        in_specs=[anywhere] * 9 + [in_vmem] * 4,
        out_specs=[anywhere] * 15,
        scratch_shapes=[
            vmem((dp * depth, 2 * keys + values), bf16),
            vmem((dp * depth, values), bf16),
            vmem((dp * depth, unit), bf16),
            vmem((unit, depth), bf16),
            vmem((depth, unit), bf16),
            vmem((rows, width), bf16),
            vmem((rows, 2 * keys + 2 * values), f32),
            vmem((4, 64, width), bf16),
            vmem((rows, KEY), f32),
            vmem((rows, 128), f32),
            vmem((heads, CHUNK, CHUNK), f32),
            vmem((heads, KEY, VAL), f32),
            vmem((CHUNK, 2 * keys + values), bf16),
            vmem((CHUNK, values), bf16),
            vmem((CHUNK, values), bf16),
            vmem((CHUNK, values), bf16),
            vmem((CHUNK, 128), f32),
            vmem((heads, KEY, VAL), bf16),
            sem((8,)), sem((4,)), sem((3,)), sem((6,)), sem((4,)),
            sem((3, 3)), sem((3, 3)), sem((3, 3)), sem((3, 3)), sem((7, 3)), sem((7, 3)), sem((10,)), sem((10,)),
        ],
        compiler_params=pltpu.CompilerParams(
            collective_id=2, has_side_effects=True, vmem_limit_bytes=63_400_000
        ),
        name="opening_exchange",
    )(*shards, tokens, cotangent, wide_segment, row_segment, rates, gain.reshape(1, width), bias.reshape(1, width))
    return results, row_segment


def middle_kernel(
    gated_ref, w_out_ref, up_ref, down_ref, cot_ref, token_ref, gain_ref, bias_ref,
    low_ref, plus_ref, feed_ref, up_grad_out, down_grad_out, late_ref,
    big, units, columns, staged, terms, half_in, full_in, mixed, plus, total,
    load_sem, column_sem, staged_sem, feed_sem, out_sem, up_send, up_recv, below_send, below_recv, core_send, core_recv,
    row_send, row_recv, half_send, half_recv, full_send, full_recv, half_free, full_free, big_free,
):
    dp = lax.axis_index("dp")
    tensor = lax.axis_index("tensor")
    z = lax.div(dp, 2)
    layers = 4
    rows = token_ref.shape[0]
    half = rows // 2
    width = token_ref.shape[1]
    unit = units.shape[2]
    depth = up_ref.shape[0]
    above = (dp + 2, tensor)
    below = (dp - 2, tensor)
    twin = (dp + 1 - 2 * lax.rem(dp, 2), tensor)
    over_x = (dp, tensor + 1 - 2 * lax.rem(tensor, 2))
    over_y = (dp, lax.rem(tensor + 2, 4))
    sides = (over_x, over_y)

    def block_of(start, count):
        return pl.ds(pl.multiple_of(start, count), count)

    def start(copies):
        for copy in copies:
            copy.start()

    def wait(copies):
        for copy in copies:
            copy.wait()

    def remote(src, dst, send, recv, device):
        return pltpu.make_async_remote_copy(
            src_ref=src, dst_ref=dst, send_sem=send, recv_sem=recv, device_id=device, device_id_type=MESH
        )

    mine = block_of(dp * depth, depth)
    shard_loads = [
        pltpu.make_async_copy(down_ref, units.at[3, mine], load_sem.at[0]),
        pltpu.make_async_copy(up_ref, units.at[2, mine], load_sem.at[1]),
    ]
    first_loads = [
        pltpu.make_async_copy(gated_ref, units.at[0], load_sem.at[2]),
        pltpu.make_async_copy(w_out_ref, units.at[1], load_sem.at[3]),
    ]
    token_load = pltpu.make_async_copy(token_ref, plus, load_sem.at[5])
    cot_load = pltpu.make_async_copy(cot_ref, big, load_sem.at[6])
    start(shard_loads)
    start(first_loads)
    token_load.start()
    cot_load.start()

    barrier = pltpu.get_barrier_semaphore()

    def greet(device):
        pl.semaphore_signal(barrier, inc=1, device_id=device, device_id_type=MESH)

    for device in (twin, over_x, over_y):
        greet(device)
    pl.when(z < layers - 1)(lambda: greet(above))
    pl.when(z > 0)(lambda: greet(below))
    pl.semaphore_wait(barrier, 3 + (z < layers - 1).astype(jnp.int32) + (z > 0).astype(jnp.int32))


    def shard_copy(a, shard, send_sem, recv_sem, index, device):
        place = block_of(shard * depth, depth)
        ref = units.at[3 - a, place]
        return remote(ref, ref, send_sem.at[a, index], recv_sem.at[a, index], device)

    def rise(a, j):
        return shard_copy(a, dp - 2 * j, up_send, up_recv, j, above)

    def sink(a, j):
        return shard_copy(a, dp + 2 * j, below_send, below_recv, j, below)

    def to_twin(a, j):
        return shard_copy(a, dp + 2 * j, core_send, core_recv, j + 3, twin)

    def from_twin(a, j):
        return shard_copy(a, twin[0] + 2 * j, core_send, core_recv, j + 3, twin)

    def first_step(a):
        shard_loads[a].wait()
        pl.when(z < layers - 1)(lambda: rise(a, 0).start())
        pl.when(z > 0)(lambda: sink(a, 0).start())
        to_twin(a, 0).start()

    def step(a, j):
        @pl.when(z - j >= 0)
        def _():
            shard_copy(a, dp - 2 * j, up_send, up_recv, j - 1, twin).wait_recv()
            if j < 3:
                pl.when(z < layers - 1)(lambda: rise(a, j).start())
            to_twin(a, -j).start()

        @pl.when(z + j < layers)
        def _():
            shard_copy(a, dp + 2 * j, below_send, below_recv, j - 1, twin).wait_recv()
            if j < 3:
                pl.when(z > 0)(lambda: sink(a, j).start())
            to_twin(a, j).start()

    def gathered(a):
        for j in range(-3, 4):
            @pl.when((z + j >= 0) & (z + j < layers))
            def _():
                from_twin(a, j).wait_recv()


    def rows_of(r, first=0, count=rows):
        return pl.ds(r * rows + first, count)

    halves = [
        remote(terms.at[2, pl.ds(0, half)], half_in.at[0], half_send.at[0], half_recv.at[0], over_x),
        remote(terms.at[2, pl.ds(half, half)], half_in.at[1], half_send.at[1], half_recv.at[1], over_y),
    ]

    def part_copy(index, term, first, device):
        place = pl.ds(first, half)
        return remote(
            terms.at[term, place], full_in.at[term, place], full_send.at[index], full_recv.at[index], device
        )

    plain_parts = [part_copy(0, 0, 0, over_x), part_copy(1, 1, half, over_y)]
    grown_parts = [part_copy(2, 0, half, over_x), part_copy(3, 1, 0, over_y)]
    fulls = plain_parts + grown_parts
    lower, upper = (0, half), (half, half)

    def row_copy(index, source, first, target, device):
        return remote(
            big.at[rows_of(source, *first)], big.at[rows_of(target, *first)],
            row_send.at[index], row_recv.at[index], device,
        )

    early = [row_copy(0, 0, lower, 1, over_x), row_copy(1, 0, upper, 2, over_y)]
    across = [row_copy(2, 2, upper, 3, over_x), row_copy(3, 1, lower, 3, over_y)]
    late = [row_copy(4, 0, upper, 1, over_x), row_copy(5, 0, lower, 2, over_y)]

    def send_halves(stage):
        for i, copy in enumerate(halves):
            if stage == 1:
                pl.semaphore_wait(half_free.at[i], 1)
            copy.start()

    def take_halves(stage):
        for copy in halves:
            copy.wait_recv()
        for term, first, slot in ((1, 0, 0), (0, half, 1)):
            @pl.loop(0, half // 64)
            def _(i):
                place = block_of(first + i * 64, 64)
                grown = terms[term, place].astype(f32) + half_in[slot, block_of(i * 64, 64)].astype(f32)
                terms[term, place] = grown.astype(bf16)

        for i, copy in enumerate(grown_parts):
            if stage == 0:
                pl.semaphore_signal(half_free.at[i], inc=1, device_id=sides[i], device_id_type=MESH)
            copy.start()

    def send_plain(stage, i):
        if stage == 1:
            pl.semaphore_wait(full_free.at[i], 1)
        plain_parts[i].start()

    def slot_of(r):
        return (3, 0, 1, 2)[r]

    def branch_term(r):
        @pl.loop(0, width // 256)
        def _(j):
            tile = block_of(j * 256, 256)
            terms[slot_of(r), :, tile] = dot_nt(units[0, rows_of(r)], units[1, tile]).astype(bf16)

    def feed_grads(r):
        @pl.loop(0, unit // 256)
        def _(j):
            tile = block_of(j * 256, 256)
            units[4, rows_of(r), tile] = dot_nn(big[rows_of(r)], units[3, :, tile]).astype(bf16)

    def feed(r):
        @pl.loop(0, unit // 256)
        def _(j):
            tile = block_of(j * 256, 256)
            value, slope = gelu_both(dot_nn(big[rows_of(r)], units[2, :, tile]))
            units[0, rows_of(r), tile] = value.astype(bf16)
            units[1, rows_of(r), tile] = (units[4, rows_of(r), tile].astype(f32) * slope).astype(bf16)

    def back_term(r):
        @pl.loop(0, width // 256)
        def _(j):
            tile = block_of(j * 256, 256)
            terms[slot_of(r), :, tile] = dot_nt(units[1, rows_of(r)], units[2, tile]).astype(bf16)


    first_step(0)
    wait(first_loads)
    branch_term(3)
    send_halves(0)
    step(0, 1)
    branch_term(1)
    send_plain(0, 0)
    branch_term(2)
    send_plain(0, 1)
    step(0, 2)
    first_step(1)
    take_halves(0)
    branch_term(0)
    step(0, 3)
    cot_load.wait()
    gathered(0)
    step(1, 1)
    feed_grads(0)
    feed_grads(1)
    step(1, 2)
    feed_grads(2)
    feed_grads(3)
    for side in sides:
        pl.semaphore_signal(big_free, inc=1, device_id=side, device_id_type=MESH)
    step(1, 3)
    gathered(1)
    token_load.wait()
    pl.semaphore_wait(big_free, 2)
    for copy in fulls:
        copy.wait_recv()

    def second_norm(i):
        place = block_of(i * 64, 64)
        value = plus[place].astype(f32) + terms[3, place].astype(f32)
        value = value + full_in[0, place].astype(f32) + full_in[1, place].astype(f32)
        mixed[place] = value
        plain, _ = normalize(value)
        big[place] = (plain * gain_ref[...] + bias_ref[...]).astype(bf16)

    pl.loop(0, half // 64)(second_norm)
    early[0].start()
    pl.loop(half // 64, rows // 64)(second_norm)
    early[1].start()
    for i, side in enumerate(sides):
        pl.semaphore_signal(full_free.at[i], inc=1, device_id=side, device_id_type=MESH)
    feed(0)
    for copy in halves + fulls:
        copy.wait_send()
    back_term(0)
    for copy in early:
        copy.wait_recv()
    start(across)
    start(late)

    def cot_columns(t):
        return pltpu.make_async_copy(cot_ref.at[:, pl.ds(t * 512, 512)], columns.at[t % 2], column_sem.at[t])

    cot_columns(0).start()
    cot_columns(1).start()
    for copy in across:
        copy.wait_recv()
    feed(3)
    back_term(3)
    send_halves(1)
    for copy in late:
        copy.wait_recv()
    feed(1)
    back_term(1)
    send_plain(1, 0)
    feed(2)
    back_term(2)
    send_plain(1, 1)
    take_halves(1)

    def staged_out(out, t, slot):
        return pltpu.make_async_copy(staged.at[slot], out.at[pl.ds(t * 512, 512)], staged_sem.at[slot])

    def weight_grad(out, t, left_of, right):
        for j in range(unit // 256):
            tile = pl.ds(j * 256, 256)
            product = None
            for place in (pl.ds(0, 2 * rows), pl.ds(2 * rows, 2 * rows)):
                more = dot_tn(left_of(place), units[right, place, tile])
                product = more if product is None else product + more
            staged[t % 2, :, tile] = product.astype(bf16)
        staged_out(out, t, t % 2).start()

    for t in range(4):
        cot_columns(t).wait()
        if t >= 2:
            staged_out(down_grad_out, t - 2, t % 2).wait()
        weight_grad(down_grad_out, t, lambda place: columns[t % 2, place], 0)
        if t < 2:
            cot_columns(t + 2).start()
    for t in range(4):
        if t < 2:
            staged_out(down_grad_out, t + 2, t % 2).wait()
        else:
            staged_out(up_grad_out, t - 2, t % 2).wait()
        weight_grad(up_grad_out, t, lambda place: big[place, pl.ds(t * 512, 512)], 1)

    def feed_out(t):
        return pltpu.make_async_copy(columns.at[t % 2], feed_ref.at[:, pl.ds(t * 512, 512)], feed_sem.at[t % 2])

    for t in range(4):
        if t >= 2:
            feed_out(t - 2).wait()

        @pl.loop(0, 4)
        def _(r):
            place = block_of(r * rows, rows)
            columns[t % 2, place] = dot_nt(units[0, place], units[3, pl.ds(t * 512, 512)]).astype(bf16)

        feed_out(t).start()

        @pl.loop(0, rows // 64)
        def _(i):
            place = block_of(i * 64, 64)
            tile = pl.ds(t * 512, 512)
            plus[place, tile] = (mixed[place, tile] + columns[t % 2, place].astype(f32)).astype(bf16)

    plus_out = pltpu.make_async_copy(plus, plus_ref, out_sem.at[0])
    plus_out.start()
    for copy in halves:
        copy.wait_send()
    cot_own = pltpu.make_async_copy(cot_ref.at[pl.ds(0, rows)], terms.at[2], load_sem.at[7])
    cot_own.start()
    total[...] = jnp.zeros_like(total)
    cot_own.wait()
    for copy in fulls:
        copy.wait_recv()

    @pl.loop(0, rows // 64)
    def _(i):
        place = block_of(i * 64, 64)
        grad = terms[3, place].astype(f32) + full_in[0, place].astype(f32) + full_in[1, place].astype(f32)
        plain, scale = normalize(mixed[place])
        back = terms[2, place].astype(f32) + normalize_back(grad, plain, scale, gain_ref[...])
        full_in[0, place] = back.astype(bf16)
        total[0:1, :] += jnp.sum(grad * plain, axis=0, keepdims=True)
        total[1:2, :] += jnp.sum(grad, axis=0, keepdims=True)

    low_out = pltpu.make_async_copy(full_in.at[0], low_ref, out_sem.at[1])
    low_out.start()
    late_ref[...] = total[...]

    for t in (2, 3):
        staged_out(up_grad_out, t, t % 2).wait()
        feed_out(t).wait()
    for copy in fulls + early + across + late:
        copy.wait_send()
    for a in range(2):
        for j in range(3):
            pl.when((z < layers - 1) & (z - j >= 0))(lambda: rise(a, j).wait_send())
            pl.when((z > 0) & (z + j < layers))(lambda: sink(a, j).wait_send())
        for j in range(-3, 4):
            pl.when((z + j >= 0) & (z + j < layers))(lambda: to_twin(a, j).wait_send())
    plus_out.wait()
    low_out.wait()


def middle_exchange(gated, w_out, up_shard, down_shard, cot_all, tokens, gain, bias):
    token_rows, width = tokens.shape
    rows = 4 * token_rows
    unit = gated.shape[1]
    anywhere = pl.BlockSpec(memory_space=pl.ANY)
    in_vmem = pl.BlockSpec(memory_space=pltpu.VMEM)
    sem = pltpu.SemaphoreType.DMA
    regular = pltpu.SemaphoreType.REGULAR
    vmem = pltpu.VMEM
    return pl.pallas_call(
        middle_kernel,
        out_shape=[
            jax.ShapeDtypeStruct((token_rows, width), bf16),
            jax.ShapeDtypeStruct((token_rows, width), bf16),
            jax.ShapeDtypeStruct((rows, width), bf16),
            jax.ShapeDtypeStruct((width, unit), bf16),
            jax.ShapeDtypeStruct((width, unit), bf16),
            jax.ShapeDtypeStruct((2, width), f32),
        ],
        in_specs=[anywhere] * 6 + [in_vmem] * 2,
        out_specs=[anywhere] * 5 + [in_vmem],
        scratch_shapes=[
            vmem((rows, width), bf16),
            vmem((5, rows, unit), bf16),
            vmem((2, rows, 512), bf16),
            vmem((2, 512, unit), bf16),
            vmem((4, token_rows, width), bf16),
            vmem((2, token_rows // 2, width), bf16),
            vmem((2, token_rows, width), bf16),
            vmem((token_rows, width), f32),
            vmem((token_rows, width), bf16),
            vmem((2, width), f32),
            sem((8,)), sem((4,)), sem((2,)), sem((2,)), sem((2,)),
            sem((2, 3)), sem((2, 3)), sem((2, 3)), sem((2, 3)), sem((2, 7)), sem((2, 7)),
            sem((6,)), sem((6,)), sem((2,)), sem((2,)), sem((4,)), sem((4,)),
            regular((2,)), regular((2,)), regular,
        ],
        compiler_params=pltpu.CompilerParams(
            collective_id=4, has_side_effects=True, vmem_limit_bytes=63_400_000
        ),
        name="middle_exchange",
    )(gated, w_out, up_shard, down_shard, cot_all, tokens, gain.reshape(1, width), bias.reshape(1, width))


def closing_kernel(
    heads,
    normed1_ref, up_ref, down_ref, feed_ref, w_out_ref, w_qkv_ref, w_gate_ref,
    gate_ref, grouped_ref, gated_ref, scale_ref, field_ref, past_ref, angle_ref, info_ref,
    low_ref, token_ref, row_ref, decay_ref, gain_ref, late_ref,
    result_ref, grad_ref, query_out, key_out, value_out, gate_out, out_out, up_out, down_out, sums_ref,
    big, units, columns, terms, half_in, full_in, products, twin_in, line_in,
    state_ref, past_in, scale_in, angle_in, info_in, given, landed, total,
    unit_sem, column_sem, chunk_sem, out_sem, mixed_sem, over_send, over_recv, onward_send, onward_recv,
    half_send, half_recv, full_send, full_recv, twin_send, twin_recv, line_send, line_recv, sum_send, sum_recv,
    twin_free, line_free, half_free, full_free,
):
    dp = lax.axis_index("dp")
    tensor = lax.axis_index("tensor")
    z = lax.div(dp, 2)
    core = lax.rem(dp, 2)
    rows = token_ref.shape[0]
    half = rows // 2
    width = token_ref.shape[1]
    unit = units.shape[2]
    depth = columns.shape[2] // 2
    at_end = (z == 0) | (z == 3)
    upper = z >= 2
    twin = (dp + 1 - 2 * core, tensor)
    over_x = (dp, tensor + 1 - 2 * lax.rem(tensor, 2))
    over_y = (dp, lax.rem(tensor + 2, 4))
    here = dp * 4 + tensor
    peers = 32
    last = 5

    def layer(index):
        return (2 * index + core, tensor)

    def seen(index):
        return jnp.where(upper, 3 - index, index)

    end = layer(seen(0))
    near = layer(seen(1))
    opposite = layer(seen(2))
    targets = [seen(3), seen(2), jnp.where(at_end, seen(1), seen(0)), z]

    def remote(src, dst, send, recv, device):
        return pltpu.make_async_remote_copy(
            src_ref=src, dst_ref=dst, send_sem=send, recv_sem=recv, device_id=device, device_id_type=MESH
        )

    def block_of(start, count):
        return pl.ds(pl.multiple_of(start, count), count)


    def whole(index, ref, sem):
        return [pltpu.make_async_copy(ref, units.at[index], unit_sem.at[sem])]

    def part(index, ref, start, sem):
        return [pltpu.make_async_copy(ref.at[:, pl.ds(start, unit)], units.at[index], unit_sem.at[sem])]

    def start(copies):
        for copy in copies:
            copy.start()

    def wait(copies):
        for copy in copies:
            copy.wait()

    out_load = whole(3, w_out_ref, 4)
    feed_load = [
        pltpu.make_async_copy(feed_ref.at[pl.ds((i + 1) * rows, rows)], terms.at[i], unit_sem.at[i]) for i in range(3)
    ]
    gated_load = whole(2, gated_ref, 6)
    w_gate_load = whole(3, w_gate_ref, 7)
    w_value_load = part(2, w_qkv_ref, unit, 8)
    w_key_load = part(1, w_qkv_ref, 0, 9)

    def wait_recv(copies):
        for copy in copies:
            copy.wait_recv()

    def wait_send(copies):
        for copy in copies:
            copy.wait_send()


    sources = [up_ref, down_ref, normed1_ref, None, normed1_ref, normed1_ref]

    def given_copy(r, k):
        place = block_of(targets[k] * 2 * depth, 2 * depth)
        return pltpu.make_async_copy(sources[r].at[place], products.at[r, k], column_sem.at[4 * r + k])

    def column_copy(r, k):
        place = block_of(targets[k] * 2 * depth, 2 * depth)
        return pltpu.make_async_copy(sources[r].at[:, place], columns.at[k % 2], column_sem.at[k])

    def prefetch(r):
        column_copy(r, 0).start()
        column_copy(r, 1).start()

    mine = block_of(core * depth, depth)
    theirs = block_of((1 - core) * depth, depth)

    def to_twin(r, k):
        return remote(
            products.at[r % 2, k, theirs], twin_in.at[k % 2], twin_send.at[r % 2, k], twin_recv.at[k % 2], twin
        )

    def along(r, k, slot, device):
        return remote(
            products.at[r % 2, k, mine], line_in.at[slot], line_send.at[r % 2, k], line_recv.at[slot], device
        )

    def send_to_twin(r, k):
        if r >= 1 or k >= 2:
            pl.semaphore_wait(twin_free.at[k % 2], 1)
        to_twin(r, k).start()

    def multiply(r, k):
        to_twin(r - 2, k).wait_send()
        if k < 3:
            along(r - 2, k, 0, end).wait_send()
        else:
            wait(outputs(r - 2))
        if sources[r] is not None:
            column_copy(r, k).wait()

        @pl.loop(0, unit // 512)
        def _(j):
            tile = block_of(j * 512, 512)
            product = None
            for place in (pl.ds(0, 2 * rows), pl.ds(2 * rows, 2 * rows)):
                if r < 4:
                    right = units[(None, None, 0, 2)[r], place, tile]
                else:
                    right = big[place, block_of((r - 4) * unit + j * 512, 512)]
                if sources[r] is None:
                    left = big[place, block_of(targets[k] * 2 * depth, 2 * depth)]
                else:
                    left = columns[k % 2, place]
                more = dot_tn(left, right)
                product = more if product is None else product + more
            products[r % 2, k, :, tile] = product.astype(bf16)

        if sources[r] is not None and k + 2 < 4:
            column_copy(r, k + 2).start()
        elif r == 4:
            column_copy(5, k - 2).start()
        send_to_twin(r, k)

    def add_to_mine(r, k, others):
        @pl.loop(0, depth // 64)
        def _(i):
            inner = block_of(core * depth + i * 64, 64)
            value = products[r % 2, k, inner].astype(f32)
            for ref, index in others:
                value = value + ref[index, block_of(i * 64, 64)].astype(f32)
            products[r % 2, k, inner] = value.astype(bf16)

    def settle(r, k):
        to_twin(r, k).wait_recv()
        add_to_mine(r, k, [(twin_in, k % 2)])
        if r < last or k < 2:
            pl.semaphore_signal(twin_free.at[k % 2], inc=1, device_id=twin, device_id_type=MESH)

    def push(r, k):
        @pl.when(at_end)
        def _():
            if r >= 1:
                pl.semaphore_wait(line_free.at[k], 1)
            along(r, k, k, near).start()

    def line_wait(slot):
        along(0, 0, slot, end).wait_recv()

    def used(device, index):
        pl.semaphore_signal(line_free.at[index], inc=1, device_id=device, device_id_type=MESH)

    def pass_on(r, which):
        arrived, sender, slot, device = ((0, end, 3, opposite), (1, end, 4, opposite), (3, opposite, 0, end))[which]

        @pl.when(jnp.logical_not(at_end))
        def _():
            line_wait(arrived)
            add_to_mine(r, which, [(line_in, arrived)])
            if r < last:
                used(sender, (0, 1, 0)[which])
            if r >= 1:
                pl.semaphore_wait(line_free.at[which], 1)
            along(r, which, slot, device).start()

    def outputs(r):
        keys = heads * KEY
        slot = products.at[r % 2, 3]
        if r == 4:
            return [
                pltpu.make_async_copy(slot.at[mine, pl.ds(0, keys)], query_out, out_sem.at[0, 0]),
                pltpu.make_async_copy(slot.at[mine, pl.ds(keys, keys)], key_out, out_sem.at[0, 1]),
            ]
        out = (up_out, down_out, gate_out, out_out, None, value_out)[r]
        return [pltpu.make_async_copy(slot.at[mine], out, out_sem.at[r % 2, 0])]

    def finish(r):
        @pl.when(at_end)
        def _():
            line_wait(0)
            add_to_mine(r, 3, [(line_in, 0)])
            if r < last:
                used(near, 2)

        @pl.when(jnp.logical_not(at_end))
        def _():
            line_wait(2)
            line_wait(4)
            add_to_mine(r, 3, [(line_in, 2), (line_in, 4)])
            if r < last:
                used(end, 2)
                used(opposite, 1)

        start(outputs(r))


    def rows_of(r, first=0, count=rows):
        return pl.ds(r * rows + first, count)

    over = [
        remote(big.at[rows_of(0)], big.at[rows_of(1)], over_send.at[0], over_recv.at[0], over_x),
        remote(big.at[rows_of(0)], big.at[rows_of(2)], over_send.at[1], over_recv.at[1], over_y),
    ]
    onward = [
        remote(big.at[rows_of(2, 0, half)], big.at[rows_of(3, 0, half)], onward_send.at[0], onward_recv.at[0], over_x),
        remote(big.at[rows_of(1, half, half)], big.at[rows_of(3, half, half)], onward_send.at[1], onward_recv.at[1], over_y),
    ]
    halves = [
        remote(terms.at[2, pl.ds(0, half)], half_in.at[0], half_send.at[0], half_recv.at[0], over_x),
        remote(terms.at[2, pl.ds(half, half)], half_in.at[1], half_send.at[1], half_recv.at[1], over_y),
    ]

    def part_copy(index, term, first, device):
        place = pl.ds(first, half)
        return remote(
            terms.at[term, place], full_in.at[term, place], full_send.at[index], full_recv.at[index], device
        )

    plain_parts = [part_copy(0, 0, 0, over_x), part_copy(1, 1, half, over_y)]
    grown_parts = [part_copy(2, 0, half, over_x), part_copy(3, 1, 0, over_y)]
    fulls = plain_parts + grown_parts
    sides = (over_x, over_y)

    def send_halves(stage):
        for i, copy in enumerate(halves):
            if stage == 1:
                pl.semaphore_wait(half_free.at[i], 1)
            copy.start()

    def take_halves(stage):
        for copy in halves:
            copy.wait_recv()
        for term, first, slot in ((1, 0, 0), (0, half, 1)):
            @pl.loop(0, half // 64)
            def _(i):
                place = block_of(first + i * 64, 64)
                grown = terms[term, place].astype(f32) + half_in[slot, block_of(i * 64, 64)].astype(f32)
                terms[term, place] = grown.astype(bf16)

        for i, copy in enumerate(grown_parts):
            if stage == 0:
                pl.semaphore_signal(half_free.at[i], inc=1, device_id=sides[i], device_id_type=MESH)
            copy.start()

    def send_plain(stage, i):
        if stage == 1:
            pl.semaphore_wait(full_free.at[i], 1)
        plain_parts[i].start()

    def project(r):
        slot = (2, 0, 1, 2)[r]

        @pl.loop(0, width // 512)
        def _(j):
            tile = block_of(j * 512, 512)
            term = dot_nt(big[rows_of(r), pl.ds(0, unit)], units[1, tile])
            term = term + dot_nt(big[rows_of(r), pl.ds(unit, unit)], units[2, tile])
            term = term + dot_nt(units[0, rows_of(r)], units[3, tile])
            terms[slot, :, tile] = term.astype(bf16)


    def gate_copies(r):
        return [
            pltpu.make_async_copy(
                ref.at[rows_of(r), pl.ds(h * VAL, VAL)],
                columns.at[r % 2, pl.ds((2 * i + h) * rows, rows)],
                chunk_sem.at[r % 2, 2 * i + h],
            )
            for i, ref in enumerate((gate_ref, grouped_ref))
            for h in range(heads)
        ] + [pltpu.make_async_copy(scale_ref.at[rows_of(r)], scale_in.at[r % 2], chunk_sem.at[r % 2, 2 * heads])]

    def gate_back(r):
        wait(gate_copies(r))
        for head in range(heads):
            tile = pl.ds(head * VAL, VAL)

            @pl.loop(0, rows // CHUNK)
            def _(i):
                place = block_of(r * rows + i * CHUNK, CHUNK)
                grad = dot_nn(big[place], units[3, :, tile])
                raw = columns[r % 2, block_of(head * rows + i * CHUNK, CHUNK)].astype(f32)
                grouped = columns[r % 2, block_of((heads + head) * rows + i * CHUNK, CHUNK)].astype(f32)
                sigmoid = 1.0 / (1.0 + jnp.exp(-raw))
                units[0, place, tile] = (grad * grouped * (sigmoid * (1.0 + raw * (1.0 - sigmoid)))).astype(bf16)
                c = grad * (raw * sigmoid)
                mean_c = jnp.mean(c, axis=-1, keepdims=True)
                mean_cx = jnp.mean(c * grouped, axis=-1, keepdims=True)
                scale = scale_in[r % 2, block_of(i * CHUNK, CHUNK), head : head + 1]
                units[1, place, tile] = (scale * (c - mean_c - grouped * mean_cx)).astype(bf16)

    chunks = 4 * rows // CHUNK
    per_piece = rows // CHUNK

    def chunk_place(c):
        piece = lax.div(c, per_piece)
        low = lax.rem(lax.rem(piece, 2) + lax.rem(tensor, 2), 2)
        high = lax.rem(lax.div(piece, 2) + lax.div(tensor, 2), 2)
        return (2 * high + low) * per_piece + lax.rem(c, per_piece)

    def chunk_copies(c, slot):
        place = block_of(chunk_place(c) * CHUNK, CHUNK)
        seat = block_of(c * CHUNK, CHUNK)
        keys = heads * KEY
        pieces = [
            (field_ref.at[place, pl.ds(0, keys)], columns.at[slot, pl.ds(0, CHUNK)]),
            (field_ref.at[place, pl.ds(keys, keys)], columns.at[slot, pl.ds(CHUNK, CHUNK)]),
        ]
        for h in range(heads):
            pieces.append((field_ref.at[place, pl.ds(2 * keys + h * VAL, VAL)], columns.at[slot, pl.ds((2 + h) * CHUNK, CHUNK)]))
        pieces += [
            (past_ref.at[c], past_in.at[slot]),
            (angle_ref.at[seat], angle_in.at[slot]),
            (info_ref.at[seat], info_in.at[slot]),
        ]
        return [pltpu.make_async_copy(src, dst, chunk_sem.at[slot, i]) for i, (src, dst) in enumerate(pieces)]

    def retention_steps(between):
        @pl.loop(0, chunks)
        def _(step):
            c = chunks - 1 - step
            slot = lax.rem(step, 2)
            wait(chunk_copies(c, slot))

            @pl.when(step + 1 < chunks)
            def _():
                start(chunk_copies(c - 1, 1 - slot))

            place = block_of(chunk_place(c) * CHUNK, CHUNK)
            angles = angle_in[slot]
            cosine = angles[:, : KEY // 2]
            sine = angles[:, KEY // 2 :]
            info = info_in[slot]
            same = info[:, 0:1] == row_ref[c]

            for head in range(heads):
                at = pl.ds(head * KEY, KEY)
                query = turn(columns[slot, pl.ds(0, CHUNK), at].astype(f32), cosine, sine).astype(bf16)
                key = turn(columns[slot, pl.ds(CHUNK, CHUNK), at].astype(f32), cosine, sine)
                key = (key * key_scale).astype(bf16)
                value = columns[slot, pl.ds((2 + head) * CHUNK, CHUNK)]
                into = info[:, 1 + 2 * head : 2 + 2 * head]
                onto = info[:, 2 + 2 * head : 3 + 2 * head]
                past = past_in[slot, head]
                out_grad = units[1, place, pl.ds(head * VAL, VAL)]
                state = state_ref[head]
                state_low = state.astype(bf16)
                masked = jnp.where(same, decay_ref[head], 0.0)
                weights = (masked * dot_nt(query, key)).astype(bf16)
                score_grad = (masked * dot_nt(out_grad, value)).astype(bf16)
                value_grad = dot_tn(weights, out_grad) + onto * dot_nn(key, state_low)
                query_grad = dot_nn(score_grad, key) + into * dot_nt(out_grad, past)
                key_grad = dot_tn(score_grad, query) + onto * dot_nt(value, state_low)
                moved = (query.astype(f32) * into).astype(bf16)
                state_ref[head] = into[CHUNK - 1 :, :] * state + dot_tn(moved, out_grad)
                big[place, pl.ds(head * KEY, KEY)] = turn_back(query_grad, cosine, sine).astype(bf16)
                big[place, pl.ds((heads + head) * KEY, KEY)] = (turn_back(key_grad, cosine, sine) * key_scale).astype(bf16)
                big[place, pl.ds(2 * heads * KEY + head * VAL, VAL)] = value_grad.astype(bf16)

            between(step)


    own_load = pltpu.make_async_copy(low_ref, big.at[rows_of(0)], mixed_sem.at[0])
    own_load.start()
    for r in range(2):
        for k in range(4):
            given_copy(r, k).start()
    start(out_load)
    start(gated_load)
    start(gate_copies(0))
    start(gate_copies(1))
    start(feed_load)

    barrier = pltpu.get_barrier_semaphore()

    def partner(k):
        other = lax.rem(here + k, peers)
        return other, (lax.div(other, 4), lax.rem(other, 4))

    @pl.loop(1, peers)
    def _(k):
        pl.semaphore_signal(barrier, inc=1, device_id=partner(k)[1], device_id_type=MESH)

    pl.semaphore_wait(barrier, peers - 1)

    own_load.wait()
    start(over)
    for k in range(4):
        given_copy(0, k).wait()
        send_to_twin(0, k)
        if k > 0:
            settle(0, k - 1)
            push(0, k - 1)
    for k in range(4):
        given_copy(1, k).wait()
        send_to_twin(1, k)
        settle(*((1, k - 1) if k > 0 else (0, 3)))
    wait(out_load)
    pass_on(0, 0)
    pass_on(0, 1)
    push(1, 0)
    gate_back(0)
    start(gate_copies(2))
    push(1, 1)
    wait_recv(over)
    start(onward)
    gate_back(1)
    start(gate_copies(3))
    settle(1, 3)
    gate_back(2)
    pass_on(0, 2)
    pass_on(1, 0)
    finish(0)
    pass_on(1, 1)
    push(1, 2)
    wait_recv(onward)
    wait(feed_load)
    send_halves(0)
    send_plain(0, 0)
    send_plain(0, 1)
    gate_back(3)
    prefetch(2)
    start(w_gate_load)
    multiply(2, 0)
    pass_on(1, 2)
    settle(2, 0)
    push(2, 0)
    multiply(2, 1)
    multiply(2, 2)
    settle(2, 1)
    multiply(2, 3)
    start(chunk_copies(chunks - 1, 0))
    settle(2, 2)
    finish(1)
    push(2, 1)
    wait(gated_load)
    multiply(3, 0)
    pass_on(2, 0)
    settle(2, 3)
    multiply(3, 1)
    settle(3, 0)
    multiply(3, 2)
    push(2, 2)
    settle(3, 1)
    multiply(3, 3)
    start(w_value_load)
    wait_send(over + onward)
    state_ref[...] = jnp.zeros_like(state_ref)

    def between(step):
        @pl.when(step == 0)
        def _():
            push(3, 0)

        @pl.when(step == 1)
        def _():
            pass_on(2, 1)

        @pl.when(step == 4)
        def _():
            take_halves(0)

        @pl.when(step == 5)
        def _():
            settle(3, 2)
            pass_on(2, 2)
            push(3, 1)

    retention_steps(between)
    start(w_key_load)
    prefetch(4)
    wait_send(halves)
    wait(w_gate_load + w_value_load + w_key_load)
    project(3)
    pass_on(3, 0)
    settle(3, 3)
    send_halves(1)
    push(3, 2)
    finish(2)
    multiply(4, 0)
    settle(4, 0)
    multiply(4, 1)
    pass_on(3, 1)
    push(4, 0)
    wait_recv(fulls)
    result_copy = pltpu.make_async_copy(full_in, result_ref, mixed_sem.at[1])
    result_copy.start()
    result_copy.wait()
    for i, side in enumerate(sides):
        pl.semaphore_signal(full_free.at[i], inc=1, device_id=side, device_id_type=MESH)
    wait_send(fulls)
    project(1)
    send_plain(1, 0)
    pass_on(3, 2)
    settle(4, 1)
    multiply(4, 2)
    push(4, 1)
    project(2)
    send_plain(1, 1)
    settle(4, 2)
    push(4, 2)
    multiply(4, 3)
    pass_on(4, 0)
    finish(3)
    multiply(5, 0)
    settle(4, 3)
    multiply(5, 1)
    settle(5, 0)
    pass_on(4, 1)
    settle(5, 1)
    push(5, 0)
    pass_on(4, 2)
    multiply(5, 2)
    take_halves(1)
    multiply(5, 3)
    pass_on(5, 0)
    push(5, 1)
    finish(4)
    wait_send(halves)
    project(0)
    settle(5, 2)
    push(5, 2)
    pass_on(5, 1)
    pass_on(5, 2)
    for copy in fulls:
        copy.wait_recv()
        copy.wait_send()
    last_loads = [
        pltpu.make_async_copy(token_ref, terms.at[0], mixed_sem.at[2]),
        pltpu.make_async_copy(low_ref, terms.at[1], mixed_sem.at[0]),
    ]
    start(last_loads)
    total[...] = jnp.zeros_like(total)
    wait(last_loads)

    @pl.loop(0, rows // 64)
    def _(i):
        place = block_of(i * 64, 64)
        normed_grad = terms[2, place].astype(f32) + full_in[0, place].astype(f32) + full_in[1, place].astype(f32)
        plain, scale = normalize(terms[0, place].astype(f32))
        grad = terms[1, place].astype(f32) + normalize_back(normed_grad, plain, scale, gain_ref[...])
        full_in[0, place] = grad.astype(bf16)
        total[0:1, :] += jnp.sum(normed_grad * plain, axis=0, keepdims=True)
        total[1:2, :] += jnp.sum(normed_grad, axis=0, keepdims=True)

    grad_copy = pltpu.make_async_copy(full_in.at[0], grad_ref, mixed_sem.at[3])
    grad_copy.start()

    total[2:4, :] = late_ref[...]
    for k in range(peers // 2):
        given[k] = total[:, k * 128 : (k + 1) * 128]

    def sum_copy(k):
        other, device = partner(k)
        return remote(given.at[lax.div(other, 2)], landed.at[k], sum_send.at[k], sum_recv.at[k], device)

    @pl.loop(1, peers)
    def _(k):
        sum_copy(k).start()

    sums_ref[...] = given[lax.div(here, 2)]

    @pl.loop(1, peers)
    def _(k):
        sum_copy(k).wait()
        sums_ref[...] += landed[k]

    settle(5, 3)
    finish(5)

    for r in (4, 5):
        for k in range(4):
            to_twin(r, k).wait_send()
            if k < 3:
                along(r, k, 0, end).wait_send()
    wait(outputs(4) + outputs(5))
    grad_copy.wait()


def cast_kernel(plus_ref, parts_ref, *refs):
    count = len(refs) // 2
    total = plus_ref[...].astype(f32) + parts_ref[0].astype(f32) + parts_ref[1].astype(f32)
    refs[count][...] = total.astype(bf16)
    for i, (source, target) in enumerate(zip(refs[:count], refs[count + 1 :])):
        value = source[...].astype(target.dtype)
        target[...] = value.T if i >= count - 2 else value


def cast_all(plus, parts, arrays):
    steps = 2

    def slab(rows, width):
        return pl.BlockSpec((rows // steps, width), lambda j: (j, 0))

    rows, width = plus.shape
    in_specs = [slab(rows, width), pl.BlockSpec((2, rows // steps, width), lambda j: (0, j, 0))]
    out_specs, shapes = [slab(rows, width)], [jax.ShapeDtypeStruct(plus.shape, bf16)]
    for i, v in enumerate(arrays):
        rows, width = v.shape
        in_specs.append(slab(rows, width))
        if i >= len(arrays) - 2:
            out_specs.append(pl.BlockSpec((width, rows // steps), lambda j: (0, j)))
            shapes.append(jax.ShapeDtypeStruct((width, rows), f32))
        else:
            out_specs.append(slab(rows, width))
            shapes.append(jax.ShapeDtypeStruct((rows, width), bf16 if i == 0 else f32))
    return pl.pallas_call(
        cast_kernel,
        grid=(steps,),
        in_specs=in_specs,
        out_specs=out_specs,
        out_shape=shapes,
        compiler_params=pltpu.CompilerParams(vmem_limit_bytes=60 * 1024 * 1024),
        name="last_casts",
    )(plus, parts, *arrays)


def closing_exchange(heads, operands, small):
    token_rows, width = operands[-1].shape
    rows = 4 * token_rows
    depth = width // 8
    keys, values = heads * KEY, heads * VAL
    unit = operands[1].shape[1]
    anywhere = pl.BlockSpec(memory_space=pl.ANY)
    in_vmem = pl.BlockSpec(memory_space=pltpu.VMEM)
    sem = pltpu.SemaphoreType.DMA
    regular = pltpu.SemaphoreType.REGULAR
    vmem = pltpu.VMEM
    return pl.pallas_call(
        functools.partial(closing_kernel, heads),
        out_shape=[
            jax.ShapeDtypeStruct((2, token_rows, width), bf16),
            jax.ShapeDtypeStruct((token_rows, width), bf16),
            jax.ShapeDtypeStruct((depth, keys), bf16),
            jax.ShapeDtypeStruct((depth, keys), bf16),
            jax.ShapeDtypeStruct((depth, values), bf16),
            jax.ShapeDtypeStruct((depth, values), bf16),
            jax.ShapeDtypeStruct((depth, unit), bf16),
            jax.ShapeDtypeStruct((depth, unit), bf16),
            jax.ShapeDtypeStruct((depth, unit), bf16),
            jax.ShapeDtypeStruct((8, 128), f32),
        ],
        in_specs=[anywhere] * len(operands) + [in_vmem] * len(small),
        out_specs=[anywhere] * 9 + [in_vmem],
        scratch_shapes=[
            vmem((rows, width), bf16),
            vmem((4, rows, unit), bf16),
            vmem((2, rows, 2 * depth), bf16),
            vmem((3, token_rows, width), bf16),
            vmem((2, token_rows // 2, width), bf16),
            vmem((2, token_rows, width), bf16),
            vmem((2, 4, 2 * depth, unit), bf16),
            vmem((2, depth, unit), bf16),
            vmem((5, depth, unit), bf16),
            vmem((heads, KEY, VAL), f32),
            vmem((2, heads, KEY, VAL), bf16),
            vmem((2, token_rows, 128), f32),
            vmem((2, CHUNK, KEY), f32),
            vmem((2, CHUNK, 128), f32),
            vmem((16, 8, 128), f32),
            vmem((32, 8, 128), f32),
            vmem((8, width), f32),
            sem((10,)), sem((8,)), sem((2, 12)), sem((2, 2)), sem((4,)),
            sem((2,)), sem((2,)), sem((2,)), sem((2,)),
            sem((2,)), sem((2,)), sem((4,)), sem((4,)),
            sem((2, 4)), sem((2,)), sem((2, 3)), sem((5,)), sem((32,)), sem((32,)),
            regular((2,)), regular((3,)), regular((2,)), regular((2,)),
        ],
        compiler_params=pltpu.CompilerParams(
            collective_id=3, has_side_effects=True, vmem_limit_bytes=63_400_000
        ),
        name="closing_exchange",
    )(*operands, *small)


def body(tokens, cotangent, segment, first_gain, first_bias, query_weight, key_weight, value_weight, gate_weight, out_weight, second_gain, second_bias, up_weight, down_weight):
    devices = lax.axis_size("tensor")
    rows = tokens.shape[0]
    heads = query_weight.shape[1] // KEY
    here = lax.axis_index("tensor")
    which = (here if devices == 4 else jnp.zeros_like(here)).astype(jnp.int32).reshape(1)

    def per_piece(values):
        return [values[i * rows : (i + 1) * rows] for i in range(devices)]

    if devices == 4 and lax.axis_size("dp") == 8:
        shards = (query_weight, key_weight, value_weight, gate_weight, out_weight, down_weight)
        opened, keys = opening_exchange(heads, shards, tokens, cotangent, segment, first_gain, first_bias)
        w_qkv, w_gate, w_out, normed1_all, cot_all, field, gate, gated, grouped, group_scale, past = opened[:11]
        angles, info, decay, down_shard = opened[11:]
        mixed_low, plus, feed_terms, up_weight_grad, down_weight_grad, late = middle_exchange(
            gated, w_out, up_weight, down_shard, cot_all, tokens, second_gain, second_bias
        )
        parts, input_grad, query_sum, key_sum, value_sum, gate_sum, out_sum, up_sum, down_sum, sums = closing_exchange(
            heads,
            (
                normed1_all, up_weight_grad, down_weight_grad, feed_terms, w_out, w_qkv, w_gate,
                gate, grouped, gated, group_scale, field, past, angles, info,
                mixed_low, tokens,
            ),
            (keys, decay, first_gain.reshape(1, -1), late),
        )
        part = first_gain.shape[0] // 32
        sums = lax.dynamic_slice_in_dim(sums, (here % 2) * part, part, 1)
        norm_sums = [sums[0], sums[1], sums[2], sums[3]]
        result, input_grad, query_sum, key_sum, value_sum, gate_sum, up_sum, out_sum, down_sum = cast_all(
            plus, parts, (input_grad, query_sum, key_sum, value_sum, gate_sum, up_sum, out_sum, down_sum)
        )
    else:
        w_qkv = lax.all_gather(
            jnp.concatenate([query_weight, key_weight, value_weight], axis=1), "dp", axis=0, tiled=True
        )
        w_gate = lax.all_gather(gate_weight, "dp", axis=0, tiled=True)
        w_out = lax.all_gather(out_weight, "dp", axis=1, tiled=True)
        token_rows = tokens.astype(f32)
        unit1, scale1 = normalize(token_rows)
        normed1_all = jnp.concatenate(
            gather_pieces((unit1 * first_gain + first_bias).astype(bf16), devices), axis=0
        )
        cot_all = jnp.concatenate(gather_pieces(cotangent, devices), axis=0)
        tables = retention_tables(segment, heads, here * heads)
        field = dot_nn(normed1_all, w_qkv).astype(bf16)
        gate = dot_nn(normed1_all, w_gate).astype(bf16)
        gated, grouped, group_scale, past = retention_call(False, which, rows, heads, field, gate, tables, ())
        w_down = lax.all_gather(after(down_weight, w_out), "dp", axis=1, tiled=True)
        w_up = lax.all_gather(after(up_weight, w_down), "dp", axis=0, tiled=True)
        branch, begun, _ = scatter_sum([dot_nn(piece, w_out) for piece in per_piece(gated)])

        mixed = token_rows + branch
        unit2, scale2 = normalize(mixed)
        normed2 = (unit2 * second_gain + second_bias).astype(bf16)
        hidden_grads = per_piece(dot_nt(cot_all, after(w_down, normed2)).astype(bf16))

        def feed(piece, hidden_grad):
            value, slope = gelu_both(dot_nn(piece, w_up))
            return after((value.astype(bf16), (hidden_grad.astype(f32) * slope).astype(bf16)))

        fed_own = feed(normed2, hidden_grads[0])
        normed2_pieces = gather_pieces(normed2, devices, fed_own)
        fed = [fed_own] + [feed(piece, grad) for piece, grad in zip(normed2_pieces[1:-1], hidden_grads[1:-1])]
        fed.append(feed(after(normed2_pieces[-1], *fed), hidden_grads[-1]))
        hidden = [f[0] for f in fed]
        up_grad = [f[1] for f in fed]
        terms = [dot_nt(piece, w_up) for piece in up_grad]
        normed2_grad, _, _ = scatter_sum(terms)
        mixed_grad = cotangent.astype(f32) + normalize_back(normed2_grad, unit2, scale2, second_gain)
        gain2_grad = jnp.sum(normed2_grad * unit2, axis=0)
        bias2_grad = jnp.sum(normed2_grad, axis=0)
        mixed_low = mixed_grad.astype(bf16)
        hidden_all = jnp.concatenate(after(hidden, *terms), axis=0)
        normed2_all = jnp.concatenate(after(normed2_pieces, *terms), axis=0)
        up_grad_all = jnp.concatenate(after(up_grad, *terms), axis=0)
        feed_terms = dot_nn(hidden_all, w_down).astype(bf16)
        own_term = feed_terms[:rows].astype(f32)
        up_weight_grad = dot_tn(normed2_all, up_grad_all).astype(bf16)
        down_weight_grad = dot_tn(cot_all, hidden_all).astype(bf16)

        def summed(gradient, dimension):
            return lax.psum_scatter(
                gradient.astype(bf16), "dp", scatter_dimension=dimension, tiled=True
            ).astype(f32)

        up_sum = summed(up_weight_grad, 0)
        down_sum = summed(down_weight_grad, 0).T
        mixed_all = jnp.concatenate(gather_pieces(mixed_low, devices), axis=0)
        ffn, _, _ = scatter_sum([term.astype(f32) for term in per_piece(feed_terms)])
        result = (mixed + ffn).astype(bf16)
        gated_grad = dot_nt(mixed_all, w_out)
        raw = gate.astype(f32)
        sigmoid = 1.0 / (1.0 + jnp.exp(-raw))
        gate_grad = (gated_grad * grouped.astype(f32) * (sigmoid * (1.0 + raw * (1.0 - sigmoid)))).astype(bf16)
        back = retention_call(
            True, which, rows, heads, field, gate, tables, (gated_grad.astype(bf16), grouped, group_scale, past)
        )
        gate_sum = summed(dot_tn(normed1_all, gate_grad), 0)
        out_sum = summed(dot_tn(gated, mixed_all), 1)
        qkv_sum = summed(dot_tn(normed1_all, back), 0)
        keys_end = heads * KEY
        query_sum = qkv_sum[:, :keys_end]
        key_sum = qkv_sum[:, keys_end : 2 * keys_end]
        value_sum = qkv_sum[:, 2 * keys_end :]
        terms = [
            dot_nt(first, w_qkv) + dot_nt(second, w_gate) for first, second in zip(per_piece(back), per_piece(gate_grad))
        ]
        normed1_grad, _, _ = scatter_sum(terms)
        input_grad = (mixed_grad + normalize_back(normed1_grad, unit1, scale1, first_gain)).astype(bf16)
        gain1_grad = jnp.sum(normed1_grad * unit1, axis=0)
        bias1_grad = jnp.sum(normed1_grad, axis=0)
        norm_sums = spread_sum([gain1_grad, bias1_grad, gain2_grad, bias2_grad])
    return (
        result,
        input_grad,
        norm_sums[0],
        norm_sums[1],
        query_sum,
        key_sum,
        value_sum,
        gate_sum,
        out_sum,
        norm_sums[2],
        norm_sums[3],
        up_sum,
        down_sum,
    )


def solution(mesh):
    rows = P(("dp", "tensor"), None)
    vector = P(("dp", "tensor"))
    into = P("dp", "tensor")
    back = P("tensor", "dp")
    return jax.shard_map(
        body,
        mesh=mesh,
        in_specs=(rows, rows, P("dp"), P(), P(), into, into, into, into, back, P(), P(), into, back),
        out_specs=(rows, rows, vector, vector, into, into, into, into, back, vector, vector, into, back),
        check_vma=False,
    )
```

```python
import functools

import jax
import jax.numpy as jnp
from jax import lax
from jax.experimental import pallas as pl
from jax.experimental.pallas import tpu as pltpu
from jax.sharding import PartitionSpec as P

KEY = 256
VAL = 512
CHUNK = 256
QKV = 2 * KEY + VAL

norm_epsilon = 1e-05
group_floor = 0.5
key_scale = KEY ** (-0.5)

f32 = jnp.float32
bf16 = jnp.bfloat16


def dot_nn(left, right):
    return lax.dot_general(left, right, (((1,), (0,)), ((), ())), preferred_element_type=f32)


def dot_nt(left, right):
    return lax.dot_general(left, right, (((1,), (1,)), ((), ())), preferred_element_type=f32)


def dot_tn(left, right):
    return lax.dot_general(left, right, (((0,), (0,)), ((), ())), preferred_element_type=f32)


def tensor_permute(values, bit):
    pairs = [(i, i ^ bit) for i in range(4)]
    return lax.ppermute(values, "tensor", pairs)


def after(values, *tokens):
    return lax.optimization_barrier((values, tokens))[0]


def gather_pieces(own, devices, between=()):
    if devices != 4:
        whole = lax.all_gather(own, "tensor", axis=0, tiled=True)
        return list(jnp.split(whole, devices, axis=0))
    half = own.shape[0] // 2
    from_x = tensor_permute(own, 1)
    from_y = tensor_permute(own, 2)
    lower, upper = after((from_y[:half], from_x[half:]), *between)
    lower = tensor_permute(lower, 1)
    upper = tensor_permute(upper, 2)
    return [own, from_x, from_y, jnp.concatenate([lower, upper], axis=0)]


def scatter_sum(terms):
    if len(terms) != 4:
        stacked = jnp.concatenate([term.astype(bf16) for term in terms], axis=0)
        return lax.psum_scatter(stacked, "tensor", scatter_dimension=0, tiled=True).astype(f32), (stacked,), (stacked,)
    own, over_x, over_y, across = terms
    half = own.shape[0] // 2
    across = across.astype(bf16)
    first = tensor_permute(across[:half], 1)
    second = tensor_permute(across[half:], 2)
    over_y = jnp.concatenate([over_y[:half] + first.astype(f32), over_y[half:]], axis=0)
    over_x = jnp.concatenate([over_x[:half], over_x[half:] + second.astype(f32)], axis=0)
    by_x = tensor_permute(over_x.astype(bf16), 1)
    by_y = tensor_permute(over_y.astype(bf16), 2)
    return own + by_x.astype(f32) + by_y.astype(f32), (first, second), (by_x, by_y)


def spread_sum_kernel(tensor_devices, devices, given_ref, sum_ref, landed_ref, send_sem, recv_sem):
    here = lax.axis_index("dp") * tensor_devices + lax.axis_index("tensor")

    def partner(k):
        other = lax.rem(here + k, devices)
        return other, (lax.div(other, tensor_devices), lax.rem(other, tensor_devices))

    def copy(k):
        other, device = partner(k)
        return pltpu.make_async_remote_copy(
            src_ref=given_ref.at[other],
            dst_ref=landed_ref.at[k],
            send_sem=send_sem.at[k],
            recv_sem=recv_sem.at[k],
            device_id=device,
            device_id_type=pl.DeviceIdType.MESH,
        )

    barrier = pltpu.get_barrier_semaphore()

    @pl.loop(1, devices)
    def _(k):
        pl.semaphore_signal(barrier, inc=1, device_id=partner(k)[1], device_id_type=pl.DeviceIdType.MESH)

    pl.semaphore_wait(barrier, devices - 1)

    @pl.loop(1, devices)
    def _(k):
        copy(k).start()

    sum_ref[...] = given_ref[here]

    @pl.loop(1, devices)
    def _(k):
        copy(k).wait()
        sum_ref[...] += landed_ref[k]


def spread_sum(vectors):
    dp, tensor = lax.axis_size("dp"), lax.axis_size("tensor")
    devices = dp * tensor
    part = vectors[0].shape[0] // devices
    given = jnp.stack([v.reshape(devices, part) for v in vectors], axis=1)
    given = jnp.pad(given, ((0, 0), (0, 8 - len(vectors)), (0, 128 - part)))
    total = pl.pallas_call(
        functools.partial(spread_sum_kernel, tensor, devices),
        out_shape=jax.ShapeDtypeStruct((8, 128), f32),
        in_specs=[pl.BlockSpec(memory_space=pltpu.VMEM)],
        out_specs=pl.BlockSpec(memory_space=pltpu.VMEM),
        scratch_shapes=[
            pltpu.VMEM((devices, 8, 128), f32),
            pltpu.SemaphoreType.DMA((devices,)),
            pltpu.SemaphoreType.DMA((devices,)),
        ],
        compiler_params=pltpu.CompilerParams(collective_id=1, has_side_effects=True),
        name="spread_sum",
    )(given)
    return [total[i, :part] for i in range(len(vectors))]


def normalize(values):
    average = jnp.mean(values, axis=-1, keepdims=True)
    centred = values - average
    variance = jnp.mean(centred * centred, axis=-1, keepdims=True)
    scale = lax.rsqrt(variance + norm_epsilon)
    return centred * scale, scale


def normalize_back(normed_grad, unit, scale, gain):
    g = normed_grad * gain
    mean_g = jnp.mean(g, axis=-1, keepdims=True)
    mean_gx = jnp.mean(g * unit, axis=-1, keepdims=True)
    return scale * (g - mean_g - unit * mean_gx)


def gelu_both(values):
    inner = 0.7978845608 * (values + 0.044715 * values * values * values)
    t = jnp.tanh(inner)
    slope = 0.7978845608 * (1.0 + 3.0 * 0.044715 * values * values)
    return 0.5 * values * (1.0 + t), 0.5 * (1.0 + t) + 0.5 * values * (1.0 - t * t) * slope


def turn(block, cosine, sine):
    a = block[:, : KEY // 2]
    b = block[:, KEY // 2 :]
    return jnp.concatenate([a * cosine - b * sine, b * cosine + a * sine], axis=1)


def turn_back(block, cosine, sine):
    a = block[:, : KEY // 2]
    b = block[:, KEY // 2 :]
    return jnp.concatenate([a * cosine + b * sine, b * cosine - a * sine], axis=1)


def head_parts(field_ref, angles, heads, head):
    cosine = angles[:, : KEY // 2]
    sine = angles[:, KEY // 2 :]
    query_at = head * KEY
    key_at = (heads + head) * KEY
    value_at = 2 * heads * KEY + head * VAL
    query = turn(field_ref[:, query_at : query_at + KEY].astype(f32), cosine, sine).astype(bf16)
    key = turn(field_ref[:, key_at : key_at + KEY].astype(f32), cosine, sine)
    key = (key * key_scale).astype(bf16)
    return query, key, field_ref[:, value_at : value_at + VAL]


def retention_forward(heads, which, field_ref, gate_ref, angle_ref, info_ref, row_ref, decay_ref, gated_ref, grouped_ref, scale_ref, past_ref, state_ref):
    @pl.when(pl.program_id(0) == 0)
    def _():
        state_ref[...] = jnp.zeros_like(state_ref)

    angles = angle_ref[...]
    info = info_ref[...]
    same = info[:, 0:1] == row_ref[0]
    scales = []
    for head in range(heads):
        query, key, value = head_parts(field_ref, angles, heads, head)
        columns = slice(head * VAL, (head + 1) * VAL)
        gate = gate_ref[:, columns].astype(f32)
        into = info[:, 1 + 2 * head : 2 + 2 * head]
        onward = info[:, 2 + 2 * head : 3 + 2 * head]
        state = state_ref[head]
        past_ref[0, head] = state.astype(bf16)
        scores = dot_nt(query, key)
        weights = (jnp.where(same, decay_ref[head], 0.0) * scores).astype(bf16)
        retained = dot_nn(weights, value) + into * dot_nn(query, state.astype(bf16))
        moved = (key.astype(f32) * onward).astype(bf16)
        state_ref[head] = into[CHUNK - 1 :, :] * state + dot_tn(moved, value)
        centred = retained - jnp.mean(retained, axis=-1, keepdims=True)
        scale = lax.rsqrt(jnp.mean(centred * centred, axis=-1, keepdims=True) + group_floor)
        grouped = centred * scale
        gated = gate / (1.0 + jnp.exp(-gate)) * grouped
        gated_ref[:, columns] = gated.astype(bf16)
        grouped_ref[:, columns] = grouped.astype(bf16)
        scales.append(scale)
    lane = lax.broadcasted_iota(jnp.int32, (CHUNK, 128), 1)
    spread = jnp.zeros((CHUNK, 128), f32)
    for head in range(heads):
        spread = jnp.where(lane == head, scales[head], spread)
    scale_ref[...] = spread


def retention_backward(heads, which, field_ref, gate_ref, angle_ref, info_ref, row_ref, decay_ref, grad_ref, grouped_ref, scale_ref, past_ref, back_ref, state_ref):
    @pl.when(pl.program_id(0) == 0)
    def _():
        state_ref[...] = jnp.zeros_like(state_ref)

    angles = angle_ref[...]
    cosine = angles[:, : KEY // 2]
    sine = angles[:, KEY // 2 :]
    info = info_ref[...]
    same = info[:, 0:1] == row_ref[0]
    for head in range(heads):
        query, key, value = head_parts(field_ref, angles, heads, head)
        columns = slice(head * VAL, (head + 1) * VAL)
        gate = gate_ref[:, columns].astype(f32)
        into = info[:, 1 + 2 * head : 2 + 2 * head]
        onward = info[:, 2 + 2 * head : 3 + 2 * head]
        grouped = grouped_ref[:, columns].astype(f32)
        scale = scale_ref[:, head : head + 1]
        c = grad_ref[:, columns].astype(f32) * (gate / (1.0 + jnp.exp(-gate)))
        mean_c = jnp.mean(c, axis=-1, keepdims=True)
        mean_cx = jnp.mean(c * grouped, axis=-1, keepdims=True)
        out_grad = (scale * (c - mean_c - grouped * mean_cx)).astype(bf16)
        state = state_ref[head]
        state_low = state.astype(bf16)
        past = past_ref[0, head]
        masked = jnp.where(same, decay_ref[head], 0.0)
        weights = (masked * dot_nt(query, key)).astype(bf16)
        score_grad = (masked * dot_nt(out_grad, value)).astype(bf16)
        value_grad = dot_tn(weights, out_grad) + onward * dot_nn(key, state_low)
        query_grad = dot_nn(score_grad, key) + into * dot_nt(out_grad, past)
        key_grad = dot_tn(score_grad, query) + onward * dot_nt(value, state_low)
        moved = (query.astype(f32) * into).astype(bf16)
        state_ref[head] = into[CHUNK - 1 :, :] * state + dot_tn(moved, out_grad)
        query_at = head * KEY
        key_at = (heads + head) * KEY
        value_at = 2 * heads * KEY + head * VAL
        back_ref[:, query_at : query_at + KEY] = turn_back(query_grad, cosine, sine).astype(bf16)
        back_ref[:, key_at : key_at + KEY] = (turn_back(key_grad, cosine, sine) * key_scale).astype(bf16)
        back_ref[:, value_at : value_at + VAL] = value_grad.astype(bf16)


def retention_tables(segment, heads, first_head):
    rows = segment.shape[0]
    chunks = rows // CHUNK
    index = jnp.arange(rows, dtype=jnp.int32)
    boundary = jnp.concatenate([jnp.ones((1,), jnp.int32), (segment[1:] != segment[:-1]).astype(jnp.int32)])
    position = index - lax.cummax(jnp.where(boundary > 0, index, 0), axis=0)
    half = KEY // 2
    frequency = jnp.exp(-jnp.log(10000.0) * jnp.arange(half, dtype=f32) / half)
    angles = position.astype(f32)[:, None] * frequency[None, :]
    angles = jnp.concatenate([jnp.cos(angles), jnp.sin(angles)], axis=1)
    head_ids = (first_head + jnp.arange(heads, dtype=jnp.int32)).astype(f32)
    log_decay = jnp.log1p(-jnp.exp2(-5.0 - head_ids))
    last = segment.reshape(chunks, CHUNK)[:, -1]
    before = jnp.concatenate([jnp.full((1,), -2, jnp.int32), last[:-1]])
    offset = (index % CHUNK).astype(f32)
    linked_in = (segment == jnp.repeat(before, CHUNK)) & (segment >= 0)
    linked_on = (segment == jnp.repeat(last, CHUNK)) & (segment >= 0)
    columns = [segment.astype(f32)]
    for head in range(heads):
        columns.append(jnp.where(linked_in, jnp.exp(log_decay[head] * (offset + 1.0)), 0.0))
        columns.append(jnp.where(linked_on, jnp.exp(log_decay[head] * (CHUNK - 1.0 - offset)), 0.0))
    info = jnp.stack(columns, axis=1)
    info = jnp.pad(info, ((0, 0), (0, 128 - info.shape[1])))
    keys = jnp.where(segment >= 0, segment, -7).astype(f32).reshape(chunks, 1, CHUNK)
    distance = (jnp.arange(CHUNK)[:, None] - jnp.arange(CHUNK)[None, :]).astype(f32)
    decay = jnp.where(distance >= 0, jnp.exp(log_decay[:, None, None] * jnp.maximum(distance, 0.0)), 0.0)
    return angles, info, keys, decay


def retention_call(backward, which, piece_rows, heads, field, gate, tables, extra):
    rows = field.shape[0]
    chunks = rows // CHUNK
    angles, info, keys, decay = tables
    per_piece = piece_rows // CHUNK

    def step(i):
        return chunks - 1 - i if backward else i

    def place(i, which_ref):
        c = step(i)
        return ((c // per_piece) ^ which_ref[0]) * per_piece + c % per_piece

    def placed(width):
        return pl.BlockSpec((CHUNK, width), lambda i, w: (place(i, w), 0))

    in_specs = [
        placed(heads * QKV),
        placed(heads * VAL),
        pl.BlockSpec((CHUNK, KEY), lambda i, w: (step(i), 0)),
        pl.BlockSpec((CHUNK, 128), lambda i, w: (step(i), 0)),
        pl.BlockSpec((1, 1, CHUNK), lambda i, w: (step(i), 0, 0)),
        pl.BlockSpec((heads, CHUNK, CHUNK), lambda i, w: (0, 0, 0)),
    ]
    past_spec = pl.BlockSpec((1, heads, KEY, VAL), lambda i, w: (step(i), 0, 0, 0))
    if backward:
        in_specs += [placed(heads * VAL), placed(heads * VAL), placed(128), past_spec]
        out_specs = placed(heads * QKV)
        out_shape = jax.ShapeDtypeStruct((rows, heads * QKV), bf16)
    else:
        out_specs = [placed(heads * VAL), placed(heads * VAL), placed(128), past_spec]
        out_shape = [
            jax.ShapeDtypeStruct((rows, heads * VAL), bf16),
            jax.ShapeDtypeStruct((rows, heads * VAL), bf16),
            jax.ShapeDtypeStruct((rows, 128), f32),
            jax.ShapeDtypeStruct((chunks, heads, KEY, VAL), bf16),
        ]
    products = 15 if backward else 7
    return pl.pallas_call(
        functools.partial(retention_backward if backward else retention_forward, heads),
        grid_spec=pltpu.PrefetchScalarGridSpec(
            num_scalar_prefetch=1,
            grid=(chunks,),
            in_specs=in_specs,
            out_specs=out_specs,
            scratch_shapes=[pltpu.VMEM((heads, KEY, VAL), f32)],
        ),
        out_shape=out_shape,
        compiler_params=pltpu.CompilerParams(
            dimension_semantics=("arbitrary",), vmem_limit_bytes=48 * 1024 * 1024
        ),
        cost_estimate=pl.CostEstimate(
            flops=products * chunks * heads * 2 * CHUNK * CHUNK * CHUNK,
            bytes_accessed=(5 if backward else 4) * rows * heads * (QKV + VAL),
            transcendentals=rows * heads * VAL,
        ),
        name="retention_backward" if backward else "retention_forward",
    )(which, field, gate, angles, info, keys, decay, *extra)


MESH = pl.DeviceIdType.MESH


def opening_kernel(
    heads, query_ref, key_ref, value_ref, gate_ref, out_ref, down_ref, token_ref, cot_ref, row_ref, rate_ref, gain_ref, bias_ref,
    w_qkv_ref, w_gate_ref, w_out_ref, normed_ref, cot_all_ref, field_ref, gate_raw_ref, gated_ref, grouped_ref, scale_ref, past_ref,
    angle_ref, info_ref, decay_ref, down_turned_ref,
    w_qkv, w_gate, w_out, tall, normed, product, angles, info, decay, state, field_out, gate_out, gated_out, grouped_out,
    scale_out, past_out,
    local_sem, token_sem, out_sem, stage_sem, table_sem, up_send, up_recv, down_send, down_recv, core_send, core_recv,
    row_send, row_recv,
):
    dp = lax.axis_index("dp")
    tensor = lax.axis_index("tensor")
    z = lax.div(dp, 2)
    layers = 4
    depth = query_ref.shape[0]
    rows, width = token_ref.shape
    half = rows // 2
    above = (dp + 2, tensor)
    below = (dp - 2, tensor)
    twin = (dp + 1 - 2 * lax.rem(dp, 2), tensor)
    over_x = (dp, tensor + 1 - 2 * lax.rem(tensor, 2))
    over_y = (dp, lax.rem(tensor + 2, 4))
    keys = heads * KEY
    values = heads * VAL

    def block_of(start, count):
        return pl.ds(pl.multiple_of(start, count), count)

    def start(copies):
        for copy in copies:
            copy.start()

    def wait(copies):
        for copy in copies:
            copy.wait()

    def remote(src, dst, send, recv, device):
        return pltpu.make_async_remote_copy(
            src_ref=src, dst_ref=dst, send_sem=send, recv_sem=recv, device_id=device, device_id_type=MESH
        )

    mine = block_of(dp * depth, depth)
    local = [
        pltpu.make_async_copy(src, dst, local_sem.at[i])
        for i, (src, dst) in enumerate((
            (query_ref, w_qkv.at[mine, pl.ds(0, keys)]),
            (key_ref, w_qkv.at[mine, pl.ds(keys, keys)]),
            (value_ref, w_qkv.at[mine, pl.ds(2 * keys, values)]),
            (gate_ref, w_gate.at[mine]),
            (out_ref, tall),
        ))
    ]
    start(local)

    half_width = width // 2
    token_loads = [
        pltpu.make_async_copy(token_ref.at[pl.ds(0, half)], field_out, token_sem.at[0]),
        pltpu.make_async_copy(token_ref.at[pl.ds(half, half), pl.ds(0, half_width)], gated_out, token_sem.at[1]),
        pltpu.make_async_copy(token_ref.at[pl.ds(half, half), pl.ds(half_width, half_width)], grouped_out, token_sem.at[2]),
    ]
    start(token_loads)
    own_cot = pltpu.make_async_copy(cot_ref, cot_all_ref.at[pl.ds(0, rows)], local_sem.at[6])
    own_cot.start()

    barrier = pltpu.get_barrier_semaphore()

    def greet(device):
        pl.semaphore_signal(barrier, inc=1, device_id=device, device_id_type=MESH)

    for device in (twin, over_x, over_y):
        greet(device)
    pl.when(z < layers - 1)(lambda: greet(above))
    pl.when(z > 0)(lambda: greet(below))
    pl.semaphore_wait(barrier, 3 + (z < layers - 1).astype(jnp.int32) + (z > 0).astype(jnp.int32))
    wait(local[:4])


    groups = ((w_qkv, w_gate), (w_out,))

    def shard_copies(g, shard, send_sem, recv_sem, index, device):
        place = block_of(shard * depth, depth)
        return [
            remote(ref.at[place], ref.at[place], send_sem.at[index, i + 2 * g], recv_sem.at[index, i + 2 * g], device)
            for i, ref in enumerate(groups[g])
        ]

    def rise(g, j):
        return shard_copies(g, dp - 2 * j, up_send, up_recv, j, above)

    def sink(g, j):
        return shard_copies(g, dp + 2 * j, down_send, down_recv, j, below)

    def to_twin(g, j):
        return shard_copies(g, dp + 2 * j, core_send, core_recv, j + 3, twin)

    def from_twin(g, j):
        return shard_copies(g, twin[0] + 2 * j, core_send, core_recv, j + 3, twin)

    def wait_recv(copies):
        for copy in copies:
            copy.wait_recv()

    def wait_send(copies):
        for copy in copies:
            copy.wait_send()

    def first_step(g):
        pl.when(z < layers - 1)(lambda: start(rise(g, 0)))
        pl.when(z > 0)(lambda: start(sink(g, 0)))
        start(to_twin(g, 0))

    def step(g, j):
        @pl.when(z - j >= 0)
        def _():
            wait_recv(shard_copies(g, dp - 2 * j, up_send, up_recv, j - 1, twin))
            if j < 3:
                pl.when(z < layers - 1)(lambda: start(rise(g, j)))
            start(to_twin(g, -j))

        @pl.when(z + j < layers)
        def _():
            wait_recv(shard_copies(g, dp + 2 * j, down_send, down_recv, j - 1, twin))
            if j < 3:
                pl.when(z > 0)(lambda: start(sink(g, j)))
            start(to_twin(g, j))

    def when_end(wanted, work):
        pl.when(((z == 0) | (z == 3)) == wanted)(work)

    def twin_step(g, j):
        for signed in sorted({-j, j}):
            @pl.when((z + signed >= 0) & (z + signed < layers))
            def _():
                wait_recv(from_twin(g, signed))

    def rows_of(r, first=0, count=rows):
        return pl.ds(r * rows + first, count)

    def row_copy(index, src, dst, device):
        return remote(src, dst, row_send.at[index], row_recv.at[index], device)

    piece = 64
    cot_early = [
        row_copy(8, cot_ref.at[pl.ds(0, piece)], cot_all_ref.at[rows_of(1, 0, piece)], over_x),
        row_copy(9, cot_ref.at[pl.ds(0, piece)], cot_all_ref.at[rows_of(2, 0, piece)], over_y),
    ]
    cot_over = [
        row_copy(4, cot_ref.at[pl.ds(piece, rows - piece)], cot_all_ref.at[rows_of(1, piece, rows - piece)], over_x),
        row_copy(5, cot_ref.at[pl.ds(piece, rows - piece)], cot_all_ref.at[rows_of(2, piece, rows - piece)], over_y),
    ]

    first_step(0)
    start(cot_early)

    wait(token_loads)

    @pl.loop(0, half // 64)
    def _(i):
        place = block_of(i * 64, 64)
        plain, _ = normalize(field_out[place].astype(f32))
        normed[place] = (plain * gain_ref[...] + bias_ref[...]).astype(bf16)

    @pl.loop(0, half // 64)
    def _(i):
        place = block_of(i * 64, 64)
        both = jnp.concatenate([gated_out[place], grouped_out[place]], axis=1)
        plain, _ = normalize(both.astype(f32))
        normed[block_of(half + i * 64, 64)] = (plain * gain_ref[...] + bias_ref[...]).astype(bf16)

    over = [
        row_copy(0, normed.at[rows_of(0)], normed.at[rows_of(1)], over_x),
        row_copy(1, normed.at[rows_of(0)], normed.at[rows_of(2)], over_y),
    ]
    onward = [
        row_copy(2, normed.at[rows_of(2, 0, half)], normed.at[rows_of(3, 0, half)], over_x),
        row_copy(3, normed.at[rows_of(1, half, half)], normed.at[rows_of(3, half, half)], over_y),
    ]
    cot_onward = [
        row_copy(6, cot_all_ref.at[rows_of(2, 0, half)], cot_all_ref.at[rows_of(3, 0, half)], over_x),
        row_copy(7, cot_all_ref.at[rows_of(1, half, half)], cot_all_ref.at[rows_of(3, half, half)], over_y),
    ]
    start(over)

    local[4].wait()
    w_out[mine, :] = tall[...].T
    down_load = pltpu.make_async_copy(down_ref, tall, local_sem.at[4])
    down_load.start()

    half_key = KEY // 2
    lanes = lax.broadcasted_iota(jnp.int32, (CHUNK, half_key), 1).astype(f32)
    frequency = jnp.exp(lanes * (-9.210340371976184 / half_key))
    chunks = 4 * rows // CHUNK

    @pl.loop(0, chunks)
    def _(c):
        seat = block_of(c * CHUNK, CHUNK)
        diagonal = lax.broadcasted_iota(jnp.int32, (CHUNK, CHUNK), 0) == lax.broadcasted_iota(jnp.int32, (CHUNK, CHUNK), 1)
        own = jnp.sum(jnp.where(diagonal, jnp.maximum(row_ref[c], -1.0), 0.0), axis=1, keepdims=True)
        info[seat, :] = jnp.broadcast_to(own, (CHUNK, 128))
        ranked = jnp.where(own < 0, 3.0, own)
        before = jnp.zeros((CHUNK, 1), f32)
        for other in range(chunks):
            seen = row_ref[other]
            seen = jnp.where(seen < 0, 3.0, seen)
            before = before + jnp.sum((seen < ranked).astype(f32), axis=1, keepdims=True)
        index = lax.broadcasted_iota(jnp.int32, (CHUNK, 1), 0) + c * CHUNK
        turned = (index.astype(f32) - before) * frequency
        angles[seat, 0:half_key] = jnp.cos(turned)
        angles[seat, half_key:KEY] = jnp.sin(turned)

    distance = lax.broadcasted_iota(jnp.int32, (CHUNK, CHUNK), 0) - lax.broadcasted_iota(jnp.int32, (CHUNK, CHUNK), 1)
    span = jnp.maximum(distance, 0).astype(f32)
    for head in range(heads):
        decay[head] = jnp.where(distance >= 0, jnp.exp(rate_ref[head : head + 1, 0:1] * span), 0.0)
    down_load.wait()
    gate_out[...] = tall[...].T
    table_outs = [
        pltpu.make_async_copy(gate_out, down_turned_ref, table_sem.at[3]),
        pltpu.make_async_copy(angles, angle_ref, table_sem.at[0]),
        pltpu.make_async_copy(decay, decay_ref, table_sem.at[1]),
    ]
    start(table_outs)


    at_end = (z == 0) | (z == 3)

    def seen_from_end(index):
        return jnp.where(z >= 2, 3 - index, index)

    order = [z, jnp.where(at_end, seen_from_end(1), seen_from_end(0)), seen_from_end(2), seen_from_end(3)]

    def project(r, s):
        deep = block_of(order[s] * 2 * depth, 2 * depth)

        @pl.loop(0, (2 * keys + values) // 512)
        def _(j):
            tile = block_of(j * 512, 512)
            more = dot_nn(normed[rows_of(r), deep], w_qkv[deep, tile])
            product[rows_of(r), tile] = more if s == 0 else product[rows_of(r), tile] + more

        @pl.loop(0, values // 512)
        def _(j):
            tile = block_of(j * 512, 512)
            more = dot_nn(normed[rows_of(r), deep], w_gate[deep, tile])
            place = block_of(2 * keys + values + j * 512, 512)
            product[rows_of(r), place] = more if s == 0 else product[rows_of(r), place] + more


    per_piece = rows // CHUNK

    def chunk_place(c):
        piece = lax.div(c, per_piece)
        low = lax.rem(lax.rem(piece, 2) + lax.rem(tensor, 2), 2)
        high = lax.rem(lax.div(piece, 2) + lax.div(tensor, 2), 2)
        return (2 * high + low) * per_piece + lax.rem(c, per_piece)

    def chunk_outs(c):
        place = block_of(chunk_place(c) * CHUNK, CHUNK)
        pairs = (
            (field_out, field_ref.at[place]),
            (gate_out, gate_raw_ref.at[place]),
            (gated_out, gated_ref.at[place]),
            (grouped_out, grouped_ref.at[place]),
            (scale_out, scale_ref.at[place]),
            (past_out, past_ref.at[c]),
        )
        return [pltpu.make_async_copy(src, dst, stage_sem.at[i]) for i, (src, dst) in enumerate(pairs)]

    def retention(between):
        state[...] = jnp.zeros_like(state)

        @pl.loop(0, chunks)
        def _(c):
            place = block_of(chunk_place(c) * CHUNK, CHUNK)
            seat = block_of(c * CHUNK, CHUNK)
            cosine = angles[seat, 0:half_key]
            sine = angles[seat, half_key:KEY]
            own = info[seat, 0:1]
            same = own == row_ref[c]
            entering = (own == row_ref[jnp.maximum(c - 1, 0)][:, CHUNK - 1 :]) & (c > 0)
            leaving = own == row_ref[c][:, CHUNK - 1 :]
            offset = lax.broadcasted_iota(jnp.int32, (CHUNK, 1), 0).astype(f32)
            lane = lax.broadcasted_iota(jnp.int32, (CHUNK, 128), 1)
            facts = jnp.where(lane == 0, own, 0.0)
            scales = jnp.zeros((CHUNK, 128), f32)

            for head in range(heads):
                rate = rate_ref[head : head + 1, 0:1]
                into = jnp.where(entering, jnp.exp(rate * (offset + 1.0)), 0.0)
                onto = jnp.where(leaving, jnp.exp(rate * (CHUNK - 1.0 - offset)), 0.0)
                facts = jnp.where(lane == 1 + 2 * head, into, facts)
                facts = jnp.where(lane == 2 + 2 * head, onto, facts)
                query_raw = product[place, pl.ds(head * KEY, KEY)]
                key_raw = product[place, pl.ds(keys + head * KEY, KEY)]
                value = product[place, pl.ds(2 * keys + head * VAL, VAL)].astype(bf16)
                gate = product[place, pl.ds(2 * keys + values + head * VAL, VAL)]
                query_raw = query_raw.astype(bf16)
                key_raw = key_raw.astype(bf16)
                query = turn(query_raw.astype(f32), cosine, sine).astype(bf16)
                key = (turn(key_raw.astype(f32), cosine, sine) * key_scale).astype(bf16)
                memory = state[head]
                memory_low = memory.astype(bf16)
                scores = dot_nt(query, key)
                weights = (jnp.where(same, decay[head], 0.0) * scores).astype(bf16)
                retained = dot_nn(weights, value) + into * dot_nn(query, memory_low)
                moved = (key.astype(f32) * onto).astype(bf16)
                state[head] = into[CHUNK - 1 :, :] * memory + dot_tn(moved, value)
                centred = retained - jnp.mean(retained, axis=-1, keepdims=True)
                scale = lax.rsqrt(jnp.mean(centred * centred, axis=-1, keepdims=True) + group_floor)
                grouped = centred * scale
                columns = pl.ds(head * VAL, VAL)
                if head == 0:
                    @pl.when(c > 0)
                    def _():
                        wait(chunk_outs(c - 1))

                field_out[:, pl.ds(head * KEY, KEY)] = query_raw
                field_out[:, pl.ds(keys + head * KEY, KEY)] = key_raw
                field_out[:, pl.ds(2 * keys + head * VAL, VAL)] = value
                gate_out[:, columns] = gate.astype(bf16)
                past_out[head] = memory_low
                gated_out[:, columns] = (gate / (1.0 + jnp.exp(-gate)) * grouped).astype(bf16)
                grouped_out[:, columns] = grouped.astype(bf16)
                scales = jnp.where(lane == head, scale, scales)
            info[seat, :] = facts
            scale_out[...] = scales
            start(chunk_outs(c))
            between(c)

        wait(chunk_outs(chunks - 1))


    twin_step(0, 0)
    project(0, 0)
    step(0, 1)
    twin_step(0, 1)
    project(0, 1)
    wait_recv(over)
    start(onward)
    start(cot_over)
    for r in (1, 2):
        for s in (0, 1):
            project(r, s)
    step(0, 2)
    first_step(1)
    twin_step(0, 2)
    for r in (0, 1, 2):
        project(r, 2)
    wait_recv(onward)
    normed_out = pltpu.make_async_copy(normed, normed_ref, local_sem.at[7])
    normed_out.start()
    for s in (0, 1, 2):
        project(3, s)
    when_end(False, lambda: step(1, 1))
    step(0, 3)
    twin_step(0, 3)
    w_outs = [
        pltpu.make_async_copy(w_qkv, w_qkv_ref, out_sem.at[0]),
        pltpu.make_async_copy(w_gate, w_gate_ref, out_sem.at[1]),
    ]
    start(w_outs)
    project(0, 3)
    project(1, 3)
    when_end(False, lambda: step(1, 2))
    wait_recv(cot_early + cot_over)
    start(cot_onward)
    project(2, 3)
    project(3, 3)

    def between(c):
        @pl.when((c == 1) & at_end)
        def _():
            step(1, 1)

        @pl.when((c == 4) & at_end)
        def _():
            step(1, 2)

    wait(table_outs)
    retention(between)
    info_out = pltpu.make_async_copy(info, info_ref, table_sem.at[2])
    info_out.start()
    step(1, 3)
    for j in range(4):
        twin_step(1, j)
    w_out_out = pltpu.make_async_copy(w_out, w_out_ref, out_sem.at[2])
    w_out_out.start()
    wait_recv(cot_onward)

    wait_send(over + onward + cot_early + cot_over + cot_onward)
    for g in range(2):
        for j in range(3):
            pl.when((z < layers - 1) & (z - j >= 0))(lambda: wait_send(rise(g, j)))
            pl.when((z > 0) & (z + j < layers))(lambda: wait_send(sink(g, j)))
        for j in range(-3, 4):
            pl.when((z + j >= 0) & (z + j < layers))(lambda: wait_send(to_twin(g, j)))
    wait(w_outs + [normed_out, own_cot, info_out, w_out_out])


def opening_exchange(heads, shards, tokens, cotangent, segment, gain, bias):
    dp = lax.axis_size("dp")
    depth, keys = shards[0].shape
    values = shards[2].shape[1]
    unit = shards[4].shape[0]
    token_rows, width = tokens.shape
    rows = 4 * token_rows
    chunks = rows // CHUNK
    anywhere = pl.BlockSpec(memory_space=pl.ANY)
    in_vmem = pl.BlockSpec(memory_space=pltpu.VMEM)
    sem = pltpu.SemaphoreType.DMA
    vmem = pltpu.VMEM
    here = lax.axis_index("tensor") * heads
    head_ids = (here + jnp.arange(8, dtype=jnp.int32)).astype(f32)
    rates = jnp.broadcast_to(jnp.log1p(-jnp.exp2(-5.0 - head_ids))[:, None], (8, 128))
    row_segment = jnp.where(segment >= 0, segment, -7).astype(f32).reshape(chunks, 1, CHUNK)
    results = pl.pallas_call(
        functools.partial(opening_kernel, heads),
        out_shape=[
            jax.ShapeDtypeStruct((dp * depth, 2 * keys + values), bf16),
            jax.ShapeDtypeStruct((dp * depth, values), bf16),
            jax.ShapeDtypeStruct((dp * depth, unit), bf16),
            jax.ShapeDtypeStruct((rows, width), bf16),
            jax.ShapeDtypeStruct((rows, width), bf16),
            jax.ShapeDtypeStruct((rows, 2 * keys + values), bf16),
            jax.ShapeDtypeStruct((rows, values), bf16),
            jax.ShapeDtypeStruct((rows, values), bf16),
            jax.ShapeDtypeStruct((rows, values), bf16),
            jax.ShapeDtypeStruct((rows, 128), f32),
            jax.ShapeDtypeStruct((chunks, heads, KEY, VAL), bf16),
            jax.ShapeDtypeStruct((rows, KEY), f32),
            jax.ShapeDtypeStruct((rows, 128), f32),
            jax.ShapeDtypeStruct((heads, CHUNK, CHUNK), f32),
            jax.ShapeDtypeStruct((depth, unit), bf16),
        ],
        in_specs=[anywhere] * 8 + [in_vmem] * 4,
        out_specs=[anywhere] * 15,
        scratch_shapes=[
            vmem((dp * depth, 2 * keys + values), bf16),
            vmem((dp * depth, values), bf16),
            vmem((dp * depth, unit), bf16),
            vmem((unit, depth), bf16),
            vmem((rows, width), bf16),
            vmem((rows, 2 * keys + 2 * values), f32),
            vmem((rows, KEY), f32),
            vmem((rows, 128), f32),
            vmem((heads, CHUNK, CHUNK), f32),
            vmem((heads, KEY, VAL), f32),
            vmem((CHUNK, 2 * keys + values), bf16),
            vmem((CHUNK, values), bf16),
            vmem((CHUNK, values), bf16),
            vmem((CHUNK, values), bf16),
            vmem((CHUNK, 128), f32),
            vmem((heads, KEY, VAL), bf16),
            sem((8,)), sem((3,)), sem((3,)), sem((6,)), sem((4,)),
            sem((3, 3)), sem((3, 3)), sem((3, 3)), sem((3, 3)), sem((7, 3)), sem((7, 3)), sem((10,)), sem((10,)),
        ],
        compiler_params=pltpu.CompilerParams(
            collective_id=2, has_side_effects=True, vmem_limit_bytes=63_400_000
        ),
        name="opening_exchange",
    )(*shards, tokens, cotangent, row_segment, rates, gain.reshape(1, width), bias.reshape(1, width))
    return results, row_segment


def middle_kernel(
    gated_ref, w_out_ref, up_ref, down_ref, cot_ref, token_ref, gain_ref, bias_ref,
    low_ref, plus_ref, feed_ref, up_grad_out, down_grad_out, late_ref,
    big, units, columns, staged, terms, half_in, full_in, mixed, plus, total,
    load_sem, column_sem, staged_sem, feed_sem, out_sem, up_send, up_recv, below_send, below_recv, core_send, core_recv,
    row_send, row_recv, half_send, half_recv, full_send, full_recv, half_free, full_free, big_free,
):
    dp = lax.axis_index("dp")
    tensor = lax.axis_index("tensor")
    z = lax.div(dp, 2)
    layers = 4
    rows = token_ref.shape[0]
    half = rows // 2
    width = token_ref.shape[1]
    unit = units.shape[2]
    depth = up_ref.shape[0]
    above = (dp + 2, tensor)
    below = (dp - 2, tensor)
    twin = (dp + 1 - 2 * lax.rem(dp, 2), tensor)
    over_x = (dp, tensor + 1 - 2 * lax.rem(tensor, 2))
    over_y = (dp, lax.rem(tensor + 2, 4))
    sides = (over_x, over_y)

    def block_of(start, count):
        return pl.ds(pl.multiple_of(start, count), count)

    def start(copies):
        for copy in copies:
            copy.start()

    def wait(copies):
        for copy in copies:
            copy.wait()

    def remote(src, dst, send, recv, device):
        return pltpu.make_async_remote_copy(
            src_ref=src, dst_ref=dst, send_sem=send, recv_sem=recv, device_id=device, device_id_type=MESH
        )

    mine = block_of(dp * depth, depth)
    shard_loads = [
        pltpu.make_async_copy(down_ref, units.at[3, mine], load_sem.at[0]),
        pltpu.make_async_copy(up_ref, units.at[2, mine], load_sem.at[1]),
    ]
    first_loads = [
        pltpu.make_async_copy(gated_ref, units.at[0], load_sem.at[2]),
        pltpu.make_async_copy(w_out_ref, units.at[1], load_sem.at[3]),
    ]
    token_load = pltpu.make_async_copy(token_ref, plus, load_sem.at[5])
    cot_load = pltpu.make_async_copy(cot_ref, big, load_sem.at[6])
    start(shard_loads)
    start(first_loads)
    token_load.start()
    cot_load.start()

    barrier = pltpu.get_barrier_semaphore()

    def greet(device):
        pl.semaphore_signal(barrier, inc=1, device_id=device, device_id_type=MESH)

    for device in (twin, over_x, over_y):
        greet(device)
    pl.when(z < layers - 1)(lambda: greet(above))
    pl.when(z > 0)(lambda: greet(below))
    pl.semaphore_wait(barrier, 3 + (z < layers - 1).astype(jnp.int32) + (z > 0).astype(jnp.int32))


    def shard_copy(a, shard, send_sem, recv_sem, index, device):
        place = block_of(shard * depth, depth)
        ref = units.at[3 - a, place]
        return remote(ref, ref, send_sem.at[a, index], recv_sem.at[a, index], device)

    def rise(a, j):
        return shard_copy(a, dp - 2 * j, up_send, up_recv, j, above)

    def sink(a, j):
        return shard_copy(a, dp + 2 * j, below_send, below_recv, j, below)

    def to_twin(a, j):
        return shard_copy(a, dp + 2 * j, core_send, core_recv, j + 3, twin)

    def from_twin(a, j):
        return shard_copy(a, twin[0] + 2 * j, core_send, core_recv, j + 3, twin)

    def first_step(a):
        shard_loads[a].wait()
        pl.when(z < layers - 1)(lambda: rise(a, 0).start())
        pl.when(z > 0)(lambda: sink(a, 0).start())
        to_twin(a, 0).start()

    def step(a, j):
        @pl.when(z - j >= 0)
        def _():
            shard_copy(a, dp - 2 * j, up_send, up_recv, j - 1, twin).wait_recv()
            if j < 3:
                pl.when(z < layers - 1)(lambda: rise(a, j).start())
            to_twin(a, -j).start()

        @pl.when(z + j < layers)
        def _():
            shard_copy(a, dp + 2 * j, below_send, below_recv, j - 1, twin).wait_recv()
            if j < 3:
                pl.when(z > 0)(lambda: sink(a, j).start())
            to_twin(a, j).start()

    def gathered(a):
        for j in range(-3, 4):
            @pl.when((z + j >= 0) & (z + j < layers))
            def _():
                from_twin(a, j).wait_recv()


    def rows_of(r, first=0, count=rows):
        return pl.ds(r * rows + first, count)

    halves = [
        remote(terms.at[2, pl.ds(0, half)], half_in.at[0], half_send.at[0], half_recv.at[0], over_x),
        remote(terms.at[2, pl.ds(half, half)], half_in.at[1], half_send.at[1], half_recv.at[1], over_y),
    ]

    def part_copy(index, term, first, device):
        place = pl.ds(first, half)
        return remote(
            terms.at[term, place], full_in.at[term, place], full_send.at[index], full_recv.at[index], device
        )

    plain_parts = [part_copy(0, 0, 0, over_x), part_copy(1, 1, half, over_y)]
    grown_parts = [part_copy(2, 0, half, over_x), part_copy(3, 1, 0, over_y)]
    fulls = plain_parts + grown_parts
    lower, upper = (0, half), (half, half)

    def row_copy(index, source, first, target, device):
        return remote(
            big.at[rows_of(source, *first)], big.at[rows_of(target, *first)],
            row_send.at[index], row_recv.at[index], device,
        )

    early = [row_copy(0, 0, lower, 1, over_x), row_copy(1, 0, upper, 2, over_y)]
    across = [row_copy(2, 2, upper, 3, over_x), row_copy(3, 1, lower, 3, over_y)]
    late = [row_copy(4, 0, upper, 1, over_x), row_copy(5, 0, lower, 2, over_y)]

    def send_halves(stage):
        for i, copy in enumerate(halves):
            if stage == 1:
                pl.semaphore_wait(half_free.at[i], 1)
            copy.start()

    def take_halves(stage):
        for copy in halves:
            copy.wait_recv()
        for term, first, slot in ((1, 0, 0), (0, half, 1)):
            @pl.loop(0, half // 64)
            def _(i):
                place = block_of(first + i * 64, 64)
                grown = terms[term, place].astype(f32) + half_in[slot, block_of(i * 64, 64)].astype(f32)
                terms[term, place] = grown.astype(bf16)

        for i, copy in enumerate(grown_parts):
            if stage == 0:
                pl.semaphore_signal(half_free.at[i], inc=1, device_id=sides[i], device_id_type=MESH)
            copy.start()

    def send_plain(stage, i):
        if stage == 1:
            pl.semaphore_wait(full_free.at[i], 1)
        plain_parts[i].start()

    def slot_of(r):
        return (3, 0, 1, 2)[r]

    def branch_term(r):
        @pl.loop(0, width // 256)
        def _(j):
            tile = block_of(j * 256, 256)
            terms[slot_of(r), :, tile] = dot_nt(units[0, rows_of(r)], units[1, tile]).astype(bf16)

    def feed_grads(r):
        @pl.loop(0, unit // 256)
        def _(j):
            tile = block_of(j * 256, 256)
            units[4, rows_of(r), tile] = dot_nn(big[rows_of(r)], units[3, :, tile]).astype(bf16)

    def feed(r):
        @pl.loop(0, unit // 256)
        def _(j):
            tile = block_of(j * 256, 256)
            value, slope = gelu_both(dot_nn(big[rows_of(r)], units[2, :, tile]))
            units[0, rows_of(r), tile] = value.astype(bf16)
            units[1, rows_of(r), tile] = (units[4, rows_of(r), tile].astype(f32) * slope).astype(bf16)

    def back_term(r):
        @pl.loop(0, width // 256)
        def _(j):
            tile = block_of(j * 256, 256)
            terms[slot_of(r), :, tile] = dot_nt(units[1, rows_of(r)], units[2, tile]).astype(bf16)


    first_step(0)
    wait(first_loads)
    branch_term(3)
    send_halves(0)
    step(0, 1)
    branch_term(1)
    send_plain(0, 0)
    branch_term(2)
    send_plain(0, 1)
    step(0, 2)
    first_step(1)
    take_halves(0)
    branch_term(0)
    step(0, 3)
    cot_load.wait()
    gathered(0)
    step(1, 1)
    feed_grads(0)
    feed_grads(1)
    step(1, 2)
    feed_grads(2)
    feed_grads(3)
    for side in sides:
        pl.semaphore_signal(big_free, inc=1, device_id=side, device_id_type=MESH)
    step(1, 3)
    gathered(1)
    token_load.wait()
    pl.semaphore_wait(big_free, 2)
    for copy in fulls:
        copy.wait_recv()

    def second_norm(i):
        place = block_of(i * 64, 64)
        value = plus[place].astype(f32) + terms[3, place].astype(f32)
        value = value + full_in[0, place].astype(f32) + full_in[1, place].astype(f32)
        mixed[place] = value
        plain, _ = normalize(value)
        big[place] = (plain * gain_ref[...] + bias_ref[...]).astype(bf16)

    pl.loop(0, half // 64)(second_norm)
    early[0].start()
    pl.loop(half // 64, rows // 64)(second_norm)
    early[1].start()
    for i, side in enumerate(sides):
        pl.semaphore_signal(full_free.at[i], inc=1, device_id=side, device_id_type=MESH)
    feed(0)
    for copy in halves + fulls:
        copy.wait_send()
    back_term(0)
    for copy in early:
        copy.wait_recv()
    start(across)
    start(late)

    def cot_columns(t):
        return pltpu.make_async_copy(cot_ref.at[:, pl.ds(t * 512, 512)], columns.at[t % 2], column_sem.at[t])

    cot_columns(0).start()
    cot_columns(1).start()
    for copy in across:
        copy.wait_recv()
    feed(3)
    back_term(3)
    send_halves(1)
    for copy in late:
        copy.wait_recv()
    feed(1)
    back_term(1)
    send_plain(1, 0)
    feed(2)
    back_term(2)
    send_plain(1, 1)
    take_halves(1)

    def staged_out(out, t, slot):
        return pltpu.make_async_copy(staged.at[slot], out.at[pl.ds(t * 512, 512)], staged_sem.at[slot])

    def weight_grad(out, t, left_of, right):
        for j in range(unit // 256):
            tile = pl.ds(j * 256, 256)
            product = None
            for place in (pl.ds(0, 2 * rows), pl.ds(2 * rows, 2 * rows)):
                more = dot_tn(left_of(place), units[right, place, tile])
                product = more if product is None else product + more
            staged[t % 2, :, tile] = product.astype(bf16)
        staged_out(out, t, t % 2).start()

    for t in range(4):
        cot_columns(t).wait()
        if t >= 2:
            staged_out(down_grad_out, t - 2, t % 2).wait()
        weight_grad(down_grad_out, t, lambda place: columns[t % 2, place], 0)
        if t < 2:
            cot_columns(t + 2).start()
    for t in range(4):
        if t < 2:
            staged_out(down_grad_out, t + 2, t % 2).wait()
        else:
            staged_out(up_grad_out, t - 2, t % 2).wait()
        weight_grad(up_grad_out, t, lambda place: big[place, pl.ds(t * 512, 512)], 1)

    def feed_out(t):
        return pltpu.make_async_copy(columns.at[t % 2], feed_ref.at[:, pl.ds(t * 512, 512)], feed_sem.at[t % 2])

    for t in range(4):
        if t >= 2:
            feed_out(t - 2).wait()

        @pl.loop(0, 4)
        def _(r):
            place = block_of(r * rows, rows)
            columns[t % 2, place] = dot_nt(units[0, place], units[3, pl.ds(t * 512, 512)]).astype(bf16)

        feed_out(t).start()

        @pl.loop(0, rows // 64)
        def _(i):
            place = block_of(i * 64, 64)
            tile = pl.ds(t * 512, 512)
            plus[place, tile] = (mixed[place, tile] + columns[t % 2, place].astype(f32)).astype(bf16)

    plus_out = pltpu.make_async_copy(plus, plus_ref, out_sem.at[0])
    plus_out.start()
    for copy in halves:
        copy.wait_send()
    cot_own = pltpu.make_async_copy(cot_ref.at[pl.ds(0, rows)], terms.at[2], load_sem.at[7])
    cot_own.start()
    total[...] = jnp.zeros_like(total)
    cot_own.wait()
    for copy in fulls:
        copy.wait_recv()

    @pl.loop(0, rows // 64)
    def _(i):
        place = block_of(i * 64, 64)
        grad = terms[3, place].astype(f32) + full_in[0, place].astype(f32) + full_in[1, place].astype(f32)
        plain, scale = normalize(mixed[place])
        back = terms[2, place].astype(f32) + normalize_back(grad, plain, scale, gain_ref[...])
        full_in[0, place] = back.astype(bf16)
        total[0:1, :] += jnp.sum(grad * plain, axis=0, keepdims=True)
        total[1:2, :] += jnp.sum(grad, axis=0, keepdims=True)

    low_out = pltpu.make_async_copy(full_in.at[0], low_ref, out_sem.at[1])
    low_out.start()
    late_ref[...] = total[...]

    for t in (2, 3):
        staged_out(up_grad_out, t, t % 2).wait()
        feed_out(t).wait()
    for copy in fulls + early + across + late:
        copy.wait_send()
    for a in range(2):
        for j in range(3):
            pl.when((z < layers - 1) & (z - j >= 0))(lambda: rise(a, j).wait_send())
            pl.when((z > 0) & (z + j < layers))(lambda: sink(a, j).wait_send())
        for j in range(-3, 4):
            pl.when((z + j >= 0) & (z + j < layers))(lambda: to_twin(a, j).wait_send())
    plus_out.wait()
    low_out.wait()


def middle_exchange(gated, w_out, up_shard, down_shard, cot_all, tokens, gain, bias):
    token_rows, width = tokens.shape
    rows = 4 * token_rows
    unit = gated.shape[1]
    anywhere = pl.BlockSpec(memory_space=pl.ANY)
    in_vmem = pl.BlockSpec(memory_space=pltpu.VMEM)
    sem = pltpu.SemaphoreType.DMA
    regular = pltpu.SemaphoreType.REGULAR
    vmem = pltpu.VMEM
    return pl.pallas_call(
        middle_kernel,
        out_shape=[
            jax.ShapeDtypeStruct((token_rows, width), bf16),
            jax.ShapeDtypeStruct((token_rows, width), bf16),
            jax.ShapeDtypeStruct((rows, width), bf16),
            jax.ShapeDtypeStruct((width, unit), bf16),
            jax.ShapeDtypeStruct((width, unit), bf16),
            jax.ShapeDtypeStruct((2, width), f32),
        ],
        in_specs=[anywhere] * 6 + [in_vmem] * 2,
        out_specs=[anywhere] * 5 + [in_vmem],
        scratch_shapes=[
            vmem((rows, width), bf16),
            vmem((5, rows, unit), bf16),
            vmem((2, rows, 512), bf16),
            vmem((2, 512, unit), bf16),
            vmem((4, token_rows, width), bf16),
            vmem((2, token_rows // 2, width), bf16),
            vmem((2, token_rows, width), bf16),
            vmem((token_rows, width), f32),
            vmem((token_rows, width), bf16),
            vmem((2, width), f32),
            sem((8,)), sem((4,)), sem((2,)), sem((2,)), sem((2,)),
            sem((2, 3)), sem((2, 3)), sem((2, 3)), sem((2, 3)), sem((2, 7)), sem((2, 7)),
            sem((6,)), sem((6,)), sem((2,)), sem((2,)), sem((4,)), sem((4,)),
            regular((2,)), regular((2,)), regular,
        ],
        compiler_params=pltpu.CompilerParams(
            collective_id=4, has_side_effects=True, vmem_limit_bytes=63_400_000
        ),
        name="middle_exchange",
    )(gated, w_out, up_shard, down_shard, cot_all, tokens, gain.reshape(1, width), bias.reshape(1, width))


def closing_kernel(
    heads,
    normed1_ref, up_ref, down_ref, feed_ref, w_out_ref, w_qkv_ref, w_gate_ref,
    gate_ref, grouped_ref, gated_ref, scale_ref, field_ref, past_ref, angle_ref, info_ref,
    low_ref, token_ref, row_ref, decay_ref, gain_ref, late_ref,
    result_ref, grad_ref, query_out, key_out, value_out, gate_out, out_out, up_out, down_out, sums_ref,
    big, units, columns, terms, half_in, full_in, products, twin_in, line_in,
    state_ref, past_in, scale_in, angle_in, info_in, given, landed, total,
    unit_sem, column_sem, chunk_sem, out_sem, mixed_sem, over_send, over_recv, onward_send, onward_recv,
    half_send, half_recv, full_send, full_recv, twin_send, twin_recv, line_send, line_recv, sum_send, sum_recv,
    twin_free, line_free, half_free, full_free,
):
    dp = lax.axis_index("dp")
    tensor = lax.axis_index("tensor")
    z = lax.div(dp, 2)
    core = lax.rem(dp, 2)
    rows = token_ref.shape[0]
    half = rows // 2
    width = token_ref.shape[1]
    unit = units.shape[2]
    depth = columns.shape[2] // 2
    at_end = (z == 0) | (z == 3)
    upper = z >= 2
    twin = (dp + 1 - 2 * core, tensor)
    over_x = (dp, tensor + 1 - 2 * lax.rem(tensor, 2))
    over_y = (dp, lax.rem(tensor + 2, 4))
    here = dp * 4 + tensor
    peers = 32
    last = 5

    def layer(index):
        return (2 * index + core, tensor)

    def seen(index):
        return jnp.where(upper, 3 - index, index)

    end = layer(seen(0))
    near = layer(seen(1))
    opposite = layer(seen(2))
    targets = [seen(3), seen(2), jnp.where(at_end, seen(1), seen(0)), z]

    def remote(src, dst, send, recv, device):
        return pltpu.make_async_remote_copy(
            src_ref=src, dst_ref=dst, send_sem=send, recv_sem=recv, device_id=device, device_id_type=MESH
        )

    def block_of(start, count):
        return pl.ds(pl.multiple_of(start, count), count)


    def whole(index, ref, sem):
        return [pltpu.make_async_copy(ref, units.at[index], unit_sem.at[sem])]

    def part(index, ref, start, sem):
        return [pltpu.make_async_copy(ref.at[:, pl.ds(start, unit)], units.at[index], unit_sem.at[sem])]

    def start(copies):
        for copy in copies:
            copy.start()

    def wait(copies):
        for copy in copies:
            copy.wait()

    out_load = whole(3, w_out_ref, 4)
    feed_load = [
        pltpu.make_async_copy(feed_ref.at[pl.ds((i + 1) * rows, rows)], terms.at[i], unit_sem.at[i]) for i in range(3)
    ]
    gated_load = whole(2, gated_ref, 6)
    w_gate_load = whole(3, w_gate_ref, 7)
    w_value_load = part(2, w_qkv_ref, unit, 8)
    w_key_load = part(1, w_qkv_ref, 0, 9)

    def wait_recv(copies):
        for copy in copies:
            copy.wait_recv()

    def wait_send(copies):
        for copy in copies:
            copy.wait_send()


    sources = [up_ref, down_ref, normed1_ref, None, normed1_ref, normed1_ref]

    def given_copy(r, k):
        place = block_of(targets[k] * 2 * depth, 2 * depth)
        return pltpu.make_async_copy(sources[r].at[place], products.at[r, k], column_sem.at[4 * r + k])

    def column_copy(r, k):
        place = block_of(targets[k] * 2 * depth, 2 * depth)
        return pltpu.make_async_copy(sources[r].at[:, place], columns.at[k % 2], column_sem.at[k])

    def prefetch(r):
        column_copy(r, 0).start()
        column_copy(r, 1).start()

    mine = block_of(core * depth, depth)
    theirs = block_of((1 - core) * depth, depth)

    def to_twin(r, k):
        return remote(
            products.at[r % 2, k, theirs], twin_in.at[k % 2], twin_send.at[r % 2, k], twin_recv.at[k % 2], twin
        )

    def along(r, k, slot, device):
        return remote(
            products.at[r % 2, k, mine], line_in.at[slot], line_send.at[r % 2, k], line_recv.at[slot], device
        )

    def send_to_twin(r, k):
        if r >= 1 or k >= 2:
            pl.semaphore_wait(twin_free.at[k % 2], 1)
        to_twin(r, k).start()

    def multiply(r, k):
        to_twin(r - 2, k).wait_send()
        if k < 3:
            along(r - 2, k, 0, end).wait_send()
        else:
            wait(outputs(r - 2))
        if sources[r] is not None:
            column_copy(r, k).wait()

        @pl.loop(0, unit // 512)
        def _(j):
            tile = block_of(j * 512, 512)
            product = None
            for place in (pl.ds(0, 2 * rows), pl.ds(2 * rows, 2 * rows)):
                if r < 4:
                    right = units[(None, None, 0, 2)[r], place, tile]
                else:
                    right = big[place, block_of((r - 4) * unit + j * 512, 512)]
                if sources[r] is None:
                    left = big[place, block_of(targets[k] * 2 * depth, 2 * depth)]
                else:
                    left = columns[k % 2, place]
                more = dot_tn(left, right)
                product = more if product is None else product + more
            products[r % 2, k, :, tile] = product.astype(bf16)

        if sources[r] is not None and k + 2 < 4:
            column_copy(r, k + 2).start()
        elif r == 4:
            column_copy(5, k - 2).start()
        send_to_twin(r, k)

    def add_to_mine(r, k, others):
        @pl.loop(0, depth // 64)
        def _(i):
            inner = block_of(core * depth + i * 64, 64)
            value = products[r % 2, k, inner].astype(f32)
            for ref, index in others:
                value = value + ref[index, block_of(i * 64, 64)].astype(f32)
            products[r % 2, k, inner] = value.astype(bf16)

    def settle(r, k):
        to_twin(r, k).wait_recv()
        add_to_mine(r, k, [(twin_in, k % 2)])
        if r < last or k < 2:
            pl.semaphore_signal(twin_free.at[k % 2], inc=1, device_id=twin, device_id_type=MESH)

    def push(r, k):
        @pl.when(at_end)
        def _():
            if r >= 1:
                pl.semaphore_wait(line_free.at[k], 1)
            along(r, k, k, near).start()

    def line_wait(slot):
        along(0, 0, slot, end).wait_recv()

    def used(device, index):
        pl.semaphore_signal(line_free.at[index], inc=1, device_id=device, device_id_type=MESH)

    def pass_on(r, which):
        arrived, sender, slot, device = ((0, end, 3, opposite), (1, end, 4, opposite), (3, opposite, 0, end))[which]

        @pl.when(jnp.logical_not(at_end))
        def _():
            line_wait(arrived)
            add_to_mine(r, which, [(line_in, arrived)])
            if r < last:
                used(sender, (0, 1, 0)[which])
            if r >= 1:
                pl.semaphore_wait(line_free.at[which], 1)
            along(r, which, slot, device).start()

    def outputs(r):
        keys = heads * KEY
        slot = products.at[r % 2, 3]
        if r == 4:
            return [
                pltpu.make_async_copy(slot.at[mine, pl.ds(0, keys)], query_out, out_sem.at[0, 0]),
                pltpu.make_async_copy(slot.at[mine, pl.ds(keys, keys)], key_out, out_sem.at[0, 1]),
            ]
        out = (up_out, down_out, gate_out, out_out, None, value_out)[r]
        return [pltpu.make_async_copy(slot.at[mine], out, out_sem.at[r % 2, 0])]

    def finish(r):
        @pl.when(at_end)
        def _():
            line_wait(0)
            add_to_mine(r, 3, [(line_in, 0)])
            if r < last:
                used(near, 2)

        @pl.when(jnp.logical_not(at_end))
        def _():
            line_wait(2)
            line_wait(4)
            add_to_mine(r, 3, [(line_in, 2), (line_in, 4)])
            if r < last:
                used(end, 2)
                used(opposite, 1)

        start(outputs(r))


    def rows_of(r, first=0, count=rows):
        return pl.ds(r * rows + first, count)

    over = [
        remote(big.at[rows_of(0)], big.at[rows_of(1)], over_send.at[0], over_recv.at[0], over_x),
        remote(big.at[rows_of(0)], big.at[rows_of(2)], over_send.at[1], over_recv.at[1], over_y),
    ]
    onward = [
        remote(big.at[rows_of(2, 0, half)], big.at[rows_of(3, 0, half)], onward_send.at[0], onward_recv.at[0], over_x),
        remote(big.at[rows_of(1, half, half)], big.at[rows_of(3, half, half)], onward_send.at[1], onward_recv.at[1], over_y),
    ]
    halves = [
        remote(terms.at[2, pl.ds(0, half)], half_in.at[0], half_send.at[0], half_recv.at[0], over_x),
        remote(terms.at[2, pl.ds(half, half)], half_in.at[1], half_send.at[1], half_recv.at[1], over_y),
    ]

    def part_copy(index, term, first, device):
        place = pl.ds(first, half)
        return remote(
            terms.at[term, place], full_in.at[term, place], full_send.at[index], full_recv.at[index], device
        )

    plain_parts = [part_copy(0, 0, 0, over_x), part_copy(1, 1, half, over_y)]
    grown_parts = [part_copy(2, 0, half, over_x), part_copy(3, 1, 0, over_y)]
    fulls = plain_parts + grown_parts
    sides = (over_x, over_y)

    def send_halves(stage):
        for i, copy in enumerate(halves):
            if stage == 1:
                pl.semaphore_wait(half_free.at[i], 1)
            copy.start()

    def take_halves(stage):
        for copy in halves:
            copy.wait_recv()
        for term, first, slot in ((1, 0, 0), (0, half, 1)):
            @pl.loop(0, half // 64)
            def _(i):
                place = block_of(first + i * 64, 64)
                grown = terms[term, place].astype(f32) + half_in[slot, block_of(i * 64, 64)].astype(f32)
                terms[term, place] = grown.astype(bf16)

        for i, copy in enumerate(grown_parts):
            if stage == 0:
                pl.semaphore_signal(half_free.at[i], inc=1, device_id=sides[i], device_id_type=MESH)
            copy.start()

    def send_plain(stage, i):
        if stage == 1:
            pl.semaphore_wait(full_free.at[i], 1)
        plain_parts[i].start()

    def project(r):
        slot = (2, 0, 1, 2)[r]

        @pl.loop(0, width // 512)
        def _(j):
            tile = block_of(j * 512, 512)
            term = dot_nt(big[rows_of(r), pl.ds(0, unit)], units[1, tile])
            term = term + dot_nt(big[rows_of(r), pl.ds(unit, unit)], units[2, tile])
            term = term + dot_nt(units[0, rows_of(r)], units[3, tile])
            terms[slot, :, tile] = term.astype(bf16)


    def gate_copies(r):
        return [
            pltpu.make_async_copy(
                ref.at[rows_of(r), pl.ds(h * VAL, VAL)],
                columns.at[r % 2, pl.ds((2 * i + h) * rows, rows)],
                chunk_sem.at[r % 2, 2 * i + h],
            )
            for i, ref in enumerate((gate_ref, grouped_ref))
            for h in range(heads)
        ] + [pltpu.make_async_copy(scale_ref.at[rows_of(r)], scale_in.at[r % 2], chunk_sem.at[r % 2, 2 * heads])]

    def gate_back(r):
        wait(gate_copies(r))
        for head in range(heads):
            tile = pl.ds(head * VAL, VAL)

            @pl.loop(0, rows // CHUNK)
            def _(i):
                place = block_of(r * rows + i * CHUNK, CHUNK)
                grad = dot_nn(big[place], units[3, :, tile])
                raw = columns[r % 2, block_of(head * rows + i * CHUNK, CHUNK)].astype(f32)
                grouped = columns[r % 2, block_of((heads + head) * rows + i * CHUNK, CHUNK)].astype(f32)
                sigmoid = 1.0 / (1.0 + jnp.exp(-raw))
                units[0, place, tile] = (grad * grouped * (sigmoid * (1.0 + raw * (1.0 - sigmoid)))).astype(bf16)
                c = grad * (raw * sigmoid)
                mean_c = jnp.mean(c, axis=-1, keepdims=True)
                mean_cx = jnp.mean(c * grouped, axis=-1, keepdims=True)
                scale = scale_in[r % 2, block_of(i * CHUNK, CHUNK), head : head + 1]
                units[1, place, tile] = (scale * (c - mean_c - grouped * mean_cx)).astype(bf16)

    chunks = 4 * rows // CHUNK
    per_piece = rows // CHUNK

    def chunk_place(c):
        piece = lax.div(c, per_piece)
        low = lax.rem(lax.rem(piece, 2) + lax.rem(tensor, 2), 2)
        high = lax.rem(lax.div(piece, 2) + lax.div(tensor, 2), 2)
        return (2 * high + low) * per_piece + lax.rem(c, per_piece)

    def chunk_copies(c, slot):
        place = block_of(chunk_place(c) * CHUNK, CHUNK)
        seat = block_of(c * CHUNK, CHUNK)
        keys = heads * KEY
        pieces = [
            (field_ref.at[place, pl.ds(0, keys)], columns.at[slot, pl.ds(0, CHUNK)]),
            (field_ref.at[place, pl.ds(keys, keys)], columns.at[slot, pl.ds(CHUNK, CHUNK)]),
        ]
        for h in range(heads):
            pieces.append((field_ref.at[place, pl.ds(2 * keys + h * VAL, VAL)], columns.at[slot, pl.ds((2 + h) * CHUNK, CHUNK)]))
        pieces += [
            (past_ref.at[c], past_in.at[slot]),
            (angle_ref.at[seat], angle_in.at[slot]),
            (info_ref.at[seat], info_in.at[slot]),
        ]
        return [pltpu.make_async_copy(src, dst, chunk_sem.at[slot, i]) for i, (src, dst) in enumerate(pieces)]

    def retention_steps(between):
        @pl.loop(0, chunks)
        def _(step):
            c = chunks - 1 - step
            slot = lax.rem(step, 2)
            wait(chunk_copies(c, slot))

            @pl.when(step + 1 < chunks)
            def _():
                start(chunk_copies(c - 1, 1 - slot))

            place = block_of(chunk_place(c) * CHUNK, CHUNK)
            angles = angle_in[slot]
            cosine = angles[:, : KEY // 2]
            sine = angles[:, KEY // 2 :]
            info = info_in[slot]
            same = info[:, 0:1] == row_ref[c]

            for head in range(heads):
                at = pl.ds(head * KEY, KEY)
                query = turn(columns[slot, pl.ds(0, CHUNK), at].astype(f32), cosine, sine).astype(bf16)
                key = turn(columns[slot, pl.ds(CHUNK, CHUNK), at].astype(f32), cosine, sine)
                key = (key * key_scale).astype(bf16)
                value = columns[slot, pl.ds((2 + head) * CHUNK, CHUNK)]
                into = info[:, 1 + 2 * head : 2 + 2 * head]
                onto = info[:, 2 + 2 * head : 3 + 2 * head]
                past = past_in[slot, head]
                out_grad = units[1, place, pl.ds(head * VAL, VAL)]
                state = state_ref[head]
                state_low = state.astype(bf16)
                masked = jnp.where(same, decay_ref[head], 0.0)
                weights = (masked * dot_nt(query, key)).astype(bf16)
                score_grad = (masked * dot_nt(out_grad, value)).astype(bf16)
                value_grad = dot_tn(weights, out_grad) + onto * dot_nn(key, state_low)
                query_grad = dot_nn(score_grad, key) + into * dot_nt(out_grad, past)
                key_grad = dot_tn(score_grad, query) + onto * dot_nt(value, state_low)
                moved = (query.astype(f32) * into).astype(bf16)
                state_ref[head] = into[CHUNK - 1 :, :] * state + dot_tn(moved, out_grad)
                big[place, pl.ds(head * KEY, KEY)] = turn_back(query_grad, cosine, sine).astype(bf16)
                big[place, pl.ds((heads + head) * KEY, KEY)] = (turn_back(key_grad, cosine, sine) * key_scale).astype(bf16)
                big[place, pl.ds(2 * heads * KEY + head * VAL, VAL)] = value_grad.astype(bf16)

            between(step)


    own_load = pltpu.make_async_copy(low_ref, big.at[rows_of(0)], mixed_sem.at[0])
    own_load.start()
    for r in range(2):
        for k in range(4):
            given_copy(r, k).start()
    start(out_load)
    start(gated_load)
    start(gate_copies(0))
    start(gate_copies(1))
    start(feed_load)

    barrier = pltpu.get_barrier_semaphore()

    def partner(k):
        other = lax.rem(here + k, peers)
        return other, (lax.div(other, 4), lax.rem(other, 4))

    @pl.loop(1, peers)
    def _(k):
        pl.semaphore_signal(barrier, inc=1, device_id=partner(k)[1], device_id_type=MESH)

    pl.semaphore_wait(barrier, peers - 1)

    own_load.wait()
    start(over)
    for k in range(4):
        given_copy(0, k).wait()
        send_to_twin(0, k)
        if k > 0:
            settle(0, k - 1)
            push(0, k - 1)
    for k in range(4):
        given_copy(1, k).wait()
        send_to_twin(1, k)
        settle(*((1, k - 1) if k > 0 else (0, 3)))
    wait(out_load)
    pass_on(0, 0)
    pass_on(0, 1)
    push(1, 0)
    gate_back(0)
    start(gate_copies(2))
    push(1, 1)
    wait_recv(over)
    start(onward)
    gate_back(1)
    start(gate_copies(3))
    settle(1, 3)
    gate_back(2)
    pass_on(0, 2)
    pass_on(1, 0)
    finish(0)
    pass_on(1, 1)
    push(1, 2)
    wait_recv(onward)
    wait(feed_load)
    send_halves(0)
    send_plain(0, 0)
    send_plain(0, 1)
    gate_back(3)
    prefetch(2)
    start(w_gate_load)
    multiply(2, 0)
    pass_on(1, 2)
    settle(2, 0)
    push(2, 0)
    multiply(2, 1)
    multiply(2, 2)
    settle(2, 1)
    multiply(2, 3)
    start(chunk_copies(chunks - 1, 0))
    settle(2, 2)
    finish(1)
    push(2, 1)
    wait(gated_load)
    multiply(3, 0)
    pass_on(2, 0)
    settle(2, 3)
    multiply(3, 1)
    settle(3, 0)
    multiply(3, 2)
    push(2, 2)
    settle(3, 1)
    multiply(3, 3)
    start(w_value_load)
    wait_send(over + onward)
    state_ref[...] = jnp.zeros_like(state_ref)

    def between(step):
        @pl.when(step == 0)
        def _():
            push(3, 0)

        @pl.when(step == 1)
        def _():
            pass_on(2, 1)

        @pl.when(step == 4)
        def _():
            take_halves(0)

        @pl.when(step == 5)
        def _():
            settle(3, 2)
            pass_on(2, 2)
            push(3, 1)

    retention_steps(between)
    start(w_key_load)
    prefetch(4)
    wait_send(halves)
    wait(w_gate_load + w_value_load + w_key_load)
    project(3)
    pass_on(3, 0)
    settle(3, 3)
    send_halves(1)
    push(3, 2)
    finish(2)
    multiply(4, 0)
    settle(4, 0)
    multiply(4, 1)
    pass_on(3, 1)
    push(4, 0)
    wait_recv(fulls)
    result_copy = pltpu.make_async_copy(full_in, result_ref, mixed_sem.at[1])
    result_copy.start()
    result_copy.wait()
    for i, side in enumerate(sides):
        pl.semaphore_signal(full_free.at[i], inc=1, device_id=side, device_id_type=MESH)
    wait_send(fulls)
    project(1)
    send_plain(1, 0)
    pass_on(3, 2)
    settle(4, 1)
    multiply(4, 2)
    push(4, 1)
    project(2)
    send_plain(1, 1)
    settle(4, 2)
    push(4, 2)
    multiply(4, 3)
    pass_on(4, 0)
    finish(3)
    multiply(5, 0)
    settle(4, 3)
    multiply(5, 1)
    settle(5, 0)
    pass_on(4, 1)
    settle(5, 1)
    push(5, 0)
    pass_on(4, 2)
    multiply(5, 2)
    take_halves(1)
    multiply(5, 3)
    pass_on(5, 0)
    push(5, 1)
    finish(4)
    wait_send(halves)
    project(0)
    settle(5, 2)
    push(5, 2)
    pass_on(5, 1)
    pass_on(5, 2)
    for copy in fulls:
        copy.wait_recv()
        copy.wait_send()
    last_loads = [
        pltpu.make_async_copy(token_ref, terms.at[0], mixed_sem.at[2]),
        pltpu.make_async_copy(low_ref, terms.at[1], mixed_sem.at[0]),
    ]
    start(last_loads)
    total[...] = jnp.zeros_like(total)
    wait(last_loads)

    @pl.loop(0, rows // 64)
    def _(i):
        place = block_of(i * 64, 64)
        normed_grad = terms[2, place].astype(f32) + full_in[0, place].astype(f32) + full_in[1, place].astype(f32)
        plain, scale = normalize(terms[0, place].astype(f32))
        grad = terms[1, place].astype(f32) + normalize_back(normed_grad, plain, scale, gain_ref[...])
        full_in[0, place] = grad.astype(bf16)
        total[0:1, :] += jnp.sum(normed_grad * plain, axis=0, keepdims=True)
        total[1:2, :] += jnp.sum(normed_grad, axis=0, keepdims=True)

    grad_copy = pltpu.make_async_copy(full_in.at[0], grad_ref, mixed_sem.at[3])
    grad_copy.start()

    total[2:4, :] = late_ref[...]
    for k in range(peers // 2):
        given[k] = total[:, k * 128 : (k + 1) * 128]

    def sum_copy(k):
        other, device = partner(k)
        return remote(given.at[lax.div(other, 2)], landed.at[k], sum_send.at[k], sum_recv.at[k], device)

    @pl.loop(1, peers)
    def _(k):
        sum_copy(k).start()

    sums_ref[...] = given[lax.div(here, 2)]

    @pl.loop(1, peers)
    def _(k):
        sum_copy(k).wait()
        sums_ref[...] += landed[k]

    settle(5, 3)
    finish(5)

    for r in (4, 5):
        for k in range(4):
            to_twin(r, k).wait_send()
            if k < 3:
                along(r, k, 0, end).wait_send()
    wait(outputs(4) + outputs(5))
    grad_copy.wait()


def cast_kernel(plus_ref, parts_ref, *refs):
    count = len(refs) // 2
    total = plus_ref[...].astype(f32) + parts_ref[0].astype(f32) + parts_ref[1].astype(f32)
    refs[count][...] = total.astype(bf16)
    for i, (source, target) in enumerate(zip(refs[:count], refs[count + 1 :])):
        value = source[...].astype(target.dtype)
        target[...] = value.T if i >= count - 2 else value


def cast_all(plus, parts, arrays):
    steps = 4

    def slab(rows, width):
        return pl.BlockSpec((rows // steps, width), lambda j: (j, 0))

    rows, width = plus.shape
    in_specs = [slab(rows, width), pl.BlockSpec((2, rows // steps, width), lambda j: (0, j, 0))]
    out_specs, shapes = [slab(rows, width)], [jax.ShapeDtypeStruct(plus.shape, bf16)]
    for i, v in enumerate(arrays):
        rows, width = v.shape
        if i >= len(arrays) - 2:
            in_specs.append(pl.BlockSpec((rows, width // steps), lambda j: (0, j)))
            out_specs.append(pl.BlockSpec((width // steps, rows), lambda j: (j, 0)))
            shapes.append(jax.ShapeDtypeStruct((width, rows), f32))
        else:
            in_specs.append(slab(rows, width))
            out_specs.append(slab(rows, width))
            shapes.append(jax.ShapeDtypeStruct((rows, width), bf16 if i == 0 else f32))
    return pl.pallas_call(
        cast_kernel,
        grid=(steps,),
        in_specs=in_specs,
        out_specs=out_specs,
        out_shape=shapes,
        compiler_params=pltpu.CompilerParams(vmem_limit_bytes=60 * 1024 * 1024),
        name="last_casts",
    )(plus, parts, *arrays)


def closing_exchange(heads, operands, small):
    token_rows, width = operands[-1].shape
    rows = 4 * token_rows
    depth = width // 8
    keys, values = heads * KEY, heads * VAL
    unit = operands[1].shape[1]
    anywhere = pl.BlockSpec(memory_space=pl.ANY)
    in_vmem = pl.BlockSpec(memory_space=pltpu.VMEM)
    sem = pltpu.SemaphoreType.DMA
    regular = pltpu.SemaphoreType.REGULAR
    vmem = pltpu.VMEM
    return pl.pallas_call(
        functools.partial(closing_kernel, heads),
        out_shape=[
            jax.ShapeDtypeStruct((2, token_rows, width), bf16),
            jax.ShapeDtypeStruct((token_rows, width), bf16),
            jax.ShapeDtypeStruct((depth, keys), bf16),
            jax.ShapeDtypeStruct((depth, keys), bf16),
            jax.ShapeDtypeStruct((depth, values), bf16),
            jax.ShapeDtypeStruct((depth, values), bf16),
            jax.ShapeDtypeStruct((depth, unit), bf16),
            jax.ShapeDtypeStruct((depth, unit), bf16),
            jax.ShapeDtypeStruct((depth, unit), bf16),
            jax.ShapeDtypeStruct((8, 128), f32),
        ],
        in_specs=[anywhere] * len(operands) + [in_vmem] * len(small),
        out_specs=[anywhere] * 9 + [in_vmem],
        scratch_shapes=[
            vmem((rows, width), bf16),
            vmem((4, rows, unit), bf16),
            vmem((2, rows, 2 * depth), bf16),
            vmem((3, token_rows, width), bf16),
            vmem((2, token_rows // 2, width), bf16),
            vmem((2, token_rows, width), bf16),
            vmem((2, 4, 2 * depth, unit), bf16),
            vmem((2, depth, unit), bf16),
            vmem((5, depth, unit), bf16),
            vmem((heads, KEY, VAL), f32),
            vmem((2, heads, KEY, VAL), bf16),
            vmem((2, token_rows, 128), f32),
            vmem((2, CHUNK, KEY), f32),
            vmem((2, CHUNK, 128), f32),
            vmem((16, 8, 128), f32),
            vmem((32, 8, 128), f32),
            vmem((8, width), f32),
            sem((10,)), sem((8,)), sem((2, 12)), sem((2, 2)), sem((4,)),
            sem((2,)), sem((2,)), sem((2,)), sem((2,)),
            sem((2,)), sem((2,)), sem((4,)), sem((4,)),
            sem((2, 4)), sem((2,)), sem((2, 3)), sem((5,)), sem((32,)), sem((32,)),
            regular((2,)), regular((3,)), regular((2,)), regular((2,)),
        ],
        compiler_params=pltpu.CompilerParams(
            collective_id=3, has_side_effects=True, vmem_limit_bytes=63_400_000
        ),
        name="closing_exchange",
    )(*operands, *small)


def body(tokens, cotangent, segment, first_gain, first_bias, query_weight, key_weight, value_weight, gate_weight, out_weight, second_gain, second_bias, up_weight, down_weight):
    devices = lax.axis_size("tensor")
    rows = tokens.shape[0]
    heads = query_weight.shape[1] // KEY
    here = lax.axis_index("tensor")
    which = (here if devices == 4 else jnp.zeros_like(here)).astype(jnp.int32).reshape(1)

    def per_piece(values):
        return [values[i * rows : (i + 1) * rows] for i in range(devices)]

    if devices == 4 and lax.axis_size("dp") == 8:
        shards = (query_weight, key_weight, value_weight, gate_weight, out_weight, down_weight)
        opened, keys = opening_exchange(heads, shards, tokens, cotangent, segment, first_gain, first_bias)
        w_qkv, w_gate, w_out, normed1_all, cot_all, field, gate, gated, grouped, group_scale, past = opened[:11]
        angles, info, decay, down_shard = opened[11:]
        mixed_low, plus, feed_terms, up_weight_grad, down_weight_grad, late = middle_exchange(
            gated, w_out, up_weight, down_shard, cot_all, tokens, second_gain, second_bias
        )
        parts, input_grad, query_sum, key_sum, value_sum, gate_sum, out_sum, up_sum, down_sum, sums = closing_exchange(
            heads,
            (
                normed1_all, up_weight_grad, down_weight_grad, feed_terms, w_out, w_qkv, w_gate,
                gate, grouped, gated, group_scale, field, past, angles, info,
                mixed_low, tokens,
            ),
            (keys, decay, first_gain.reshape(1, -1), late),
        )
        part = first_gain.shape[0] // 32
        sums = lax.dynamic_slice_in_dim(sums, (here % 2) * part, part, 1)
        norm_sums = [sums[0], sums[1], sums[2], sums[3]]
        result, input_grad, query_sum, key_sum, value_sum, gate_sum, up_sum, out_sum, down_sum = cast_all(
            plus, parts, (input_grad, query_sum, key_sum, value_sum, gate_sum, up_sum, out_sum, down_sum)
        )
    else:
        w_qkv = lax.all_gather(
            jnp.concatenate([query_weight, key_weight, value_weight], axis=1), "dp", axis=0, tiled=True
        )
        w_gate = lax.all_gather(gate_weight, "dp", axis=0, tiled=True)
        w_out = lax.all_gather(out_weight, "dp", axis=1, tiled=True)
        token_rows = tokens.astype(f32)
        unit1, scale1 = normalize(token_rows)
        normed1_all = jnp.concatenate(
            gather_pieces((unit1 * first_gain + first_bias).astype(bf16), devices), axis=0
        )
        cot_all = jnp.concatenate(gather_pieces(cotangent, devices), axis=0)
        tables = retention_tables(segment, heads, here * heads)
        field = dot_nn(normed1_all, w_qkv).astype(bf16)
        gate = dot_nn(normed1_all, w_gate).astype(bf16)
        gated, grouped, group_scale, past = retention_call(False, which, rows, heads, field, gate, tables, ())
        w_down = lax.all_gather(after(down_weight, w_out), "dp", axis=1, tiled=True)
        w_up = lax.all_gather(after(up_weight, w_down), "dp", axis=0, tiled=True)
        branch, begun, _ = scatter_sum([dot_nn(piece, w_out) for piece in per_piece(gated)])

        mixed = token_rows + branch
        unit2, scale2 = normalize(mixed)
        normed2 = (unit2 * second_gain + second_bias).astype(bf16)
        hidden_grads = per_piece(dot_nt(cot_all, after(w_down, normed2)).astype(bf16))

        def feed(piece, hidden_grad):
            value, slope = gelu_both(dot_nn(piece, w_up))
            return after((value.astype(bf16), (hidden_grad.astype(f32) * slope).astype(bf16)))

        fed_own = feed(normed2, hidden_grads[0])
        normed2_pieces = gather_pieces(normed2, devices, fed_own)
        fed = [fed_own] + [feed(piece, grad) for piece, grad in zip(normed2_pieces[1:-1], hidden_grads[1:-1])]
        fed.append(feed(after(normed2_pieces[-1], *fed), hidden_grads[-1]))
        hidden = [f[0] for f in fed]
        up_grad = [f[1] for f in fed]
        terms = [dot_nt(piece, w_up) for piece in up_grad]
        normed2_grad, _, _ = scatter_sum(terms)
        mixed_grad = cotangent.astype(f32) + normalize_back(normed2_grad, unit2, scale2, second_gain)
        gain2_grad = jnp.sum(normed2_grad * unit2, axis=0)
        bias2_grad = jnp.sum(normed2_grad, axis=0)
        mixed_low = mixed_grad.astype(bf16)
        hidden_all = jnp.concatenate(after(hidden, *terms), axis=0)
        normed2_all = jnp.concatenate(after(normed2_pieces, *terms), axis=0)
        up_grad_all = jnp.concatenate(after(up_grad, *terms), axis=0)
        feed_terms = dot_nn(hidden_all, w_down).astype(bf16)
        own_term = feed_terms[:rows].astype(f32)
        up_weight_grad = dot_tn(normed2_all, up_grad_all).astype(bf16)
        down_weight_grad = dot_tn(cot_all, hidden_all).astype(bf16)

        def summed(gradient, dimension):
            return lax.psum_scatter(
                gradient.astype(bf16), "dp", scatter_dimension=dimension, tiled=True
            ).astype(f32)

        up_sum = summed(up_weight_grad, 0)
        down_sum = summed(down_weight_grad, 0).T
        mixed_all = jnp.concatenate(gather_pieces(mixed_low, devices), axis=0)
        ffn, _, _ = scatter_sum([term.astype(f32) for term in per_piece(feed_terms)])
        result = (mixed + ffn).astype(bf16)
        gated_grad = dot_nt(mixed_all, w_out)
        raw = gate.astype(f32)
        sigmoid = 1.0 / (1.0 + jnp.exp(-raw))
        gate_grad = (gated_grad * grouped.astype(f32) * (sigmoid * (1.0 + raw * (1.0 - sigmoid)))).astype(bf16)
        back = retention_call(
            True, which, rows, heads, field, gate, tables, (gated_grad.astype(bf16), grouped, group_scale, past)
        )
        gate_sum = summed(dot_tn(normed1_all, gate_grad), 0)
        out_sum = summed(dot_tn(gated, mixed_all), 1)
        qkv_sum = summed(dot_tn(normed1_all, back), 0)
        keys_end = heads * KEY
        query_sum = qkv_sum[:, :keys_end]
        key_sum = qkv_sum[:, keys_end : 2 * keys_end]
        value_sum = qkv_sum[:, 2 * keys_end :]
        terms = [
            dot_nt(first, w_qkv) + dot_nt(second, w_gate) for first, second in zip(per_piece(back), per_piece(gate_grad))
        ]
        normed1_grad, _, _ = scatter_sum(terms)
        input_grad = (mixed_grad + normalize_back(normed1_grad, unit1, scale1, first_gain)).astype(bf16)
        gain1_grad = jnp.sum(normed1_grad * unit1, axis=0)
        bias1_grad = jnp.sum(normed1_grad, axis=0)
        norm_sums = spread_sum([gain1_grad, bias1_grad, gain2_grad, bias2_grad])
    return (
        result,
        input_grad,
        norm_sums[0],
        norm_sums[1],
        query_sum,
        key_sum,
        value_sum,
        gate_sum,
        out_sum,
        norm_sums[2],
        norm_sums[3],
        up_sum,
        down_sum,
    )


def solution(mesh):
    rows = P(("dp", "tensor"), None)
    vector = P(("dp", "tensor"))
    into = P("dp", "tensor")
    back = P("tensor", "dp")
    return jax.shard_map(
        body,
        mesh=mesh,
        in_specs=(rows, rows, P("dp"), P(), P(), into, into, into, into, back, P(), P(), into, back),
        out_specs=(rows, rows, vector, vector, into, into, into, into, back, vector, vector, into, back),
        check_vma=False,
    )
```

```python
import functools

import jax
import jax.numpy as jnp
from jax import lax
from jax.experimental import pallas as pl
from jax.experimental.pallas import tpu as pltpu
from jax.sharding import PartitionSpec as P

KEY = 256
VAL = 512
CHUNK = 256
QKV = 2 * KEY + VAL

norm_epsilon = 1e-05
group_floor = 0.5
key_scale = KEY ** (-0.5)

f32 = jnp.float32
bf16 = jnp.bfloat16


def dot_nn(left, right):
    return lax.dot_general(left, right, (((1,), (0,)), ((), ())), preferred_element_type=f32)


def dot_nt(left, right):
    return lax.dot_general(left, right, (((1,), (1,)), ((), ())), preferred_element_type=f32)


def dot_tn(left, right):
    return lax.dot_general(left, right, (((0,), (0,)), ((), ())), preferred_element_type=f32)


def tensor_permute(values, bit):
    pairs = [(i, i ^ bit) for i in range(4)]
    return lax.ppermute(values, "tensor", pairs)


def after(values, *tokens):
    return lax.optimization_barrier((values, tokens))[0]


def gather_pieces(own, devices, between=()):
    if devices != 4:
        whole = lax.all_gather(own, "tensor", axis=0, tiled=True)
        return list(jnp.split(whole, devices, axis=0))
    half = own.shape[0] // 2
    from_x = tensor_permute(own, 1)
    from_y = tensor_permute(own, 2)
    lower, upper = after((from_y[:half], from_x[half:]), *between)
    lower = tensor_permute(lower, 1)
    upper = tensor_permute(upper, 2)
    return [own, from_x, from_y, jnp.concatenate([lower, upper], axis=0)]


def scatter_sum(terms):
    if len(terms) != 4:
        stacked = jnp.concatenate([term.astype(bf16) for term in terms], axis=0)
        return lax.psum_scatter(stacked, "tensor", scatter_dimension=0, tiled=True).astype(f32), (stacked,), (stacked,)
    own, over_x, over_y, across = terms
    half = own.shape[0] // 2
    across = across.astype(bf16)
    first = tensor_permute(across[:half], 1)
    second = tensor_permute(across[half:], 2)
    over_y = jnp.concatenate([over_y[:half] + first.astype(f32), over_y[half:]], axis=0)
    over_x = jnp.concatenate([over_x[:half], over_x[half:] + second.astype(f32)], axis=0)
    by_x = tensor_permute(over_x.astype(bf16), 1)
    by_y = tensor_permute(over_y.astype(bf16), 2)
    return own + by_x.astype(f32) + by_y.astype(f32), (first, second), (by_x, by_y)


def spread_sum_kernel(tensor_devices, devices, given_ref, sum_ref, landed_ref, send_sem, recv_sem):
    here = lax.axis_index("dp") * tensor_devices + lax.axis_index("tensor")

    def partner(k):
        other = lax.rem(here + k, devices)
        return other, (lax.div(other, tensor_devices), lax.rem(other, tensor_devices))

    def copy(k):
        other, device = partner(k)
        return pltpu.make_async_remote_copy(
            src_ref=given_ref.at[other],
            dst_ref=landed_ref.at[k],
            send_sem=send_sem.at[k],
            recv_sem=recv_sem.at[k],
            device_id=device,
            device_id_type=pl.DeviceIdType.MESH,
        )

    barrier = pltpu.get_barrier_semaphore()

    @pl.loop(1, devices)
    def _(k):
        pl.semaphore_signal(barrier, inc=1, device_id=partner(k)[1], device_id_type=pl.DeviceIdType.MESH)

    pl.semaphore_wait(barrier, devices - 1)

    @pl.loop(1, devices)
    def _(k):
        copy(k).start()

    sum_ref[...] = given_ref[here]

    @pl.loop(1, devices)
    def _(k):
        copy(k).wait()
        sum_ref[...] += landed_ref[k]


def spread_sum(vectors):
    dp, tensor = lax.axis_size("dp"), lax.axis_size("tensor")
    devices = dp * tensor
    part = vectors[0].shape[0] // devices
    given = jnp.stack([v.reshape(devices, part) for v in vectors], axis=1)
    given = jnp.pad(given, ((0, 0), (0, 8 - len(vectors)), (0, 128 - part)))
    total = pl.pallas_call(
        functools.partial(spread_sum_kernel, tensor, devices),
        out_shape=jax.ShapeDtypeStruct((8, 128), f32),
        in_specs=[pl.BlockSpec(memory_space=pltpu.VMEM)],
        out_specs=pl.BlockSpec(memory_space=pltpu.VMEM),
        scratch_shapes=[
            pltpu.VMEM((devices, 8, 128), f32),
            pltpu.SemaphoreType.DMA((devices,)),
            pltpu.SemaphoreType.DMA((devices,)),
        ],
        compiler_params=pltpu.CompilerParams(collective_id=1, has_side_effects=True),
        name="spread_sum",
    )(given)
    return [total[i, :part] for i in range(len(vectors))]


def normalize(values):
    average = jnp.mean(values, axis=-1, keepdims=True)
    centred = values - average
    variance = jnp.mean(centred * centred, axis=-1, keepdims=True)
    scale = lax.rsqrt(variance + norm_epsilon)
    return centred * scale, scale


def normalize_back(normed_grad, unit, scale, gain):
    g = normed_grad * gain
    mean_g = jnp.mean(g, axis=-1, keepdims=True)
    mean_gx = jnp.mean(g * unit, axis=-1, keepdims=True)
    return scale * (g - mean_g - unit * mean_gx)


def gelu_both(values):
    inner = 0.7978845608 * (values + 0.044715 * values * values * values)
    t = jnp.tanh(inner)
    slope = 0.7978845608 * (1.0 + 3.0 * 0.044715 * values * values)
    return 0.5 * values * (1.0 + t), 0.5 * (1.0 + t) + 0.5 * values * (1.0 - t * t) * slope


def turn(block, cosine, sine):
    a = block[:, : KEY // 2]
    b = block[:, KEY // 2 :]
    return jnp.concatenate([a * cosine - b * sine, b * cosine + a * sine], axis=1)


def turn_back(block, cosine, sine):
    a = block[:, : KEY // 2]
    b = block[:, KEY // 2 :]
    return jnp.concatenate([a * cosine + b * sine, b * cosine - a * sine], axis=1)


def head_parts(field_ref, angles, heads, head):
    cosine = angles[:, : KEY // 2]
    sine = angles[:, KEY // 2 :]
    query_at = head * KEY
    key_at = (heads + head) * KEY
    value_at = 2 * heads * KEY + head * VAL
    query = turn(field_ref[:, query_at : query_at + KEY].astype(f32), cosine, sine).astype(bf16)
    key = turn(field_ref[:, key_at : key_at + KEY].astype(f32), cosine, sine)
    key = (key * key_scale).astype(bf16)
    return query, key, field_ref[:, value_at : value_at + VAL]


def retention_forward(heads, which, field_ref, gate_ref, angle_ref, info_ref, row_ref, decay_ref, gated_ref, grouped_ref, scale_ref, past_ref, state_ref):
    @pl.when(pl.program_id(0) == 0)
    def _():
        state_ref[...] = jnp.zeros_like(state_ref)

    angles = angle_ref[...]
    info = info_ref[...]
    same = info[:, 0:1] == row_ref[0]
    scales = []
    for head in range(heads):
        query, key, value = head_parts(field_ref, angles, heads, head)
        columns = slice(head * VAL, (head + 1) * VAL)
        gate = gate_ref[:, columns].astype(f32)
        into = info[:, 1 + 2 * head : 2 + 2 * head]
        onward = info[:, 2 + 2 * head : 3 + 2 * head]
        state = state_ref[head]
        past_ref[0, head] = state.astype(bf16)
        scores = dot_nt(query, key)
        weights = (jnp.where(same, decay_ref[head], 0.0) * scores).astype(bf16)
        retained = dot_nn(weights, value) + into * dot_nn(query, state.astype(bf16))
        moved = (key.astype(f32) * onward).astype(bf16)
        state_ref[head] = into[CHUNK - 1 :, :] * state + dot_tn(moved, value)
        centred = retained - jnp.mean(retained, axis=-1, keepdims=True)
        scale = lax.rsqrt(jnp.mean(centred * centred, axis=-1, keepdims=True) + group_floor)
        grouped = centred * scale
        gated = gate / (1.0 + jnp.exp(-gate)) * grouped
        gated_ref[:, columns] = gated.astype(bf16)
        grouped_ref[:, columns] = grouped.astype(bf16)
        scales.append(scale)
    lane = lax.broadcasted_iota(jnp.int32, (CHUNK, 128), 1)
    spread = jnp.zeros((CHUNK, 128), f32)
    for head in range(heads):
        spread = jnp.where(lane == head, scales[head], spread)
    scale_ref[...] = spread


def retention_backward(heads, which, field_ref, gate_ref, angle_ref, info_ref, row_ref, decay_ref, grad_ref, grouped_ref, scale_ref, past_ref, back_ref, state_ref):
    @pl.when(pl.program_id(0) == 0)
    def _():
        state_ref[...] = jnp.zeros_like(state_ref)

    angles = angle_ref[...]
    cosine = angles[:, : KEY // 2]
    sine = angles[:, KEY // 2 :]
    info = info_ref[...]
    same = info[:, 0:1] == row_ref[0]
    for head in range(heads):
        query, key, value = head_parts(field_ref, angles, heads, head)
        columns = slice(head * VAL, (head + 1) * VAL)
        gate = gate_ref[:, columns].astype(f32)
        into = info[:, 1 + 2 * head : 2 + 2 * head]
        onward = info[:, 2 + 2 * head : 3 + 2 * head]
        grouped = grouped_ref[:, columns].astype(f32)
        scale = scale_ref[:, head : head + 1]
        c = grad_ref[:, columns].astype(f32) * (gate / (1.0 + jnp.exp(-gate)))
        mean_c = jnp.mean(c, axis=-1, keepdims=True)
        mean_cx = jnp.mean(c * grouped, axis=-1, keepdims=True)
        out_grad = (scale * (c - mean_c - grouped * mean_cx)).astype(bf16)
        state = state_ref[head]
        state_low = state.astype(bf16)
        past = past_ref[0, head]
        masked = jnp.where(same, decay_ref[head], 0.0)
        weights = (masked * dot_nt(query, key)).astype(bf16)
        score_grad = (masked * dot_nt(out_grad, value)).astype(bf16)
        value_grad = dot_tn(weights, out_grad) + onward * dot_nn(key, state_low)
        query_grad = dot_nn(score_grad, key) + into * dot_nt(out_grad, past)
        key_grad = dot_tn(score_grad, query) + onward * dot_nt(value, state_low)
        moved = (query.astype(f32) * into).astype(bf16)
        state_ref[head] = into[CHUNK - 1 :, :] * state + dot_tn(moved, out_grad)
        query_at = head * KEY
        key_at = (heads + head) * KEY
        value_at = 2 * heads * KEY + head * VAL
        back_ref[:, query_at : query_at + KEY] = turn_back(query_grad, cosine, sine).astype(bf16)
        back_ref[:, key_at : key_at + KEY] = (turn_back(key_grad, cosine, sine) * key_scale).astype(bf16)
        back_ref[:, value_at : value_at + VAL] = value_grad.astype(bf16)


def retention_tables(segment, heads, first_head):
    rows = segment.shape[0]
    chunks = rows // CHUNK
    index = jnp.arange(rows, dtype=jnp.int32)
    boundary = jnp.concatenate([jnp.ones((1,), jnp.int32), (segment[1:] != segment[:-1]).astype(jnp.int32)])
    position = index - lax.cummax(jnp.where(boundary > 0, index, 0), axis=0)
    half = KEY // 2
    frequency = jnp.exp(-jnp.log(10000.0) * jnp.arange(half, dtype=f32) / half)
    angles = position.astype(f32)[:, None] * frequency[None, :]
    angles = jnp.concatenate([jnp.cos(angles), jnp.sin(angles)], axis=1)
    head_ids = (first_head + jnp.arange(heads, dtype=jnp.int32)).astype(f32)
    log_decay = jnp.log1p(-jnp.exp2(-5.0 - head_ids))
    last = segment.reshape(chunks, CHUNK)[:, -1]
    before = jnp.concatenate([jnp.full((1,), -2, jnp.int32), last[:-1]])
    offset = (index % CHUNK).astype(f32)
    linked_in = (segment == jnp.repeat(before, CHUNK)) & (segment >= 0)
    linked_on = (segment == jnp.repeat(last, CHUNK)) & (segment >= 0)
    columns = [segment.astype(f32)]
    for head in range(heads):
        columns.append(jnp.where(linked_in, jnp.exp(log_decay[head] * (offset + 1.0)), 0.0))
        columns.append(jnp.where(linked_on, jnp.exp(log_decay[head] * (CHUNK - 1.0 - offset)), 0.0))
    info = jnp.stack(columns, axis=1)
    info = jnp.pad(info, ((0, 0), (0, 128 - info.shape[1])))
    keys = jnp.where(segment >= 0, segment, -7).astype(f32).reshape(chunks, 1, CHUNK)
    distance = (jnp.arange(CHUNK)[:, None] - jnp.arange(CHUNK)[None, :]).astype(f32)
    decay = jnp.where(distance >= 0, jnp.exp(log_decay[:, None, None] * jnp.maximum(distance, 0.0)), 0.0)
    return angles, info, keys, decay


def retention_call(backward, which, piece_rows, heads, field, gate, tables, extra):
    rows = field.shape[0]
    chunks = rows // CHUNK
    angles, info, keys, decay = tables
    per_piece = piece_rows // CHUNK

    def step(i):
        return chunks - 1 - i if backward else i

    def place(i, which_ref):
        c = step(i)
        return ((c // per_piece) ^ which_ref[0]) * per_piece + c % per_piece

    def placed(width):
        return pl.BlockSpec((CHUNK, width), lambda i, w: (place(i, w), 0))

    in_specs = [
        placed(heads * QKV),
        placed(heads * VAL),
        pl.BlockSpec((CHUNK, KEY), lambda i, w: (step(i), 0)),
        pl.BlockSpec((CHUNK, 128), lambda i, w: (step(i), 0)),
        pl.BlockSpec((1, 1, CHUNK), lambda i, w: (step(i), 0, 0)),
        pl.BlockSpec((heads, CHUNK, CHUNK), lambda i, w: (0, 0, 0)),
    ]
    past_spec = pl.BlockSpec((1, heads, KEY, VAL), lambda i, w: (step(i), 0, 0, 0))
    if backward:
        in_specs += [placed(heads * VAL), placed(heads * VAL), placed(128), past_spec]
        out_specs = placed(heads * QKV)
        out_shape = jax.ShapeDtypeStruct((rows, heads * QKV), bf16)
    else:
        out_specs = [placed(heads * VAL), placed(heads * VAL), placed(128), past_spec]
        out_shape = [
            jax.ShapeDtypeStruct((rows, heads * VAL), bf16),
            jax.ShapeDtypeStruct((rows, heads * VAL), bf16),
            jax.ShapeDtypeStruct((rows, 128), f32),
            jax.ShapeDtypeStruct((chunks, heads, KEY, VAL), bf16),
        ]
    products = 15 if backward else 7
    return pl.pallas_call(
        functools.partial(retention_backward if backward else retention_forward, heads),
        grid_spec=pltpu.PrefetchScalarGridSpec(
            num_scalar_prefetch=1,
            grid=(chunks,),
            in_specs=in_specs,
            out_specs=out_specs,
            scratch_shapes=[pltpu.VMEM((heads, KEY, VAL), f32)],
        ),
        out_shape=out_shape,
        compiler_params=pltpu.CompilerParams(
            dimension_semantics=("arbitrary",), vmem_limit_bytes=48 * 1024 * 1024
        ),
        cost_estimate=pl.CostEstimate(
            flops=products * chunks * heads * 2 * CHUNK * CHUNK * CHUNK,
            bytes_accessed=(5 if backward else 4) * rows * heads * (QKV + VAL),
            transcendentals=rows * heads * VAL,
        ),
        name="retention_backward" if backward else "retention_forward",
    )(which, field, gate, angles, info, keys, decay, *extra)


MESH = pl.DeviceIdType.MESH


def opening_kernel(
    heads, query_ref, key_ref, value_ref, gate_ref, out_ref, down_ref, token_ref, cot_ref, row_ref, rate_ref, gain_ref, bias_ref,
    w_qkv_ref, w_gate_ref, w_out_ref, normed_ref, cot_all_ref, field_ref, gate_raw_ref, gated_ref, grouped_ref, scale_ref, past_ref,
    angle_ref, info_ref, decay_ref, down_turned_ref,
    w_qkv, w_gate, w_out, tall, normed, product, angles, info, decay, state, field_out, gate_out, gated_out, grouped_out,
    scale_out, past_out,
    local_sem, token_sem, out_sem, stage_sem, table_sem, up_send, up_recv, down_send, down_recv, core_send, core_recv,
    row_send, row_recv,
):
    dp = lax.axis_index("dp")
    tensor = lax.axis_index("tensor")
    z = lax.div(dp, 2)
    layers = 4
    depth = query_ref.shape[0]
    rows, width = token_ref.shape
    half = rows // 2
    above = (dp + 2, tensor)
    below = (dp - 2, tensor)
    twin = (dp + 1 - 2 * lax.rem(dp, 2), tensor)
    over_x = (dp, tensor + 1 - 2 * lax.rem(tensor, 2))
    over_y = (dp, lax.rem(tensor + 2, 4))
    keys = heads * KEY
    values = heads * VAL

    def block_of(start, count):
        return pl.ds(pl.multiple_of(start, count), count)

    def start(copies):
        for copy in copies:
            copy.start()

    def wait(copies):
        for copy in copies:
            copy.wait()

    def remote(src, dst, send, recv, device):
        return pltpu.make_async_remote_copy(
            src_ref=src, dst_ref=dst, send_sem=send, recv_sem=recv, device_id=device, device_id_type=MESH
        )

    mine = block_of(dp * depth, depth)
    local = [
        pltpu.make_async_copy(src, dst, local_sem.at[i])
        for i, (src, dst) in enumerate((
            (query_ref, w_qkv.at[mine, pl.ds(0, keys)]),
            (key_ref, w_qkv.at[mine, pl.ds(keys, keys)]),
            (value_ref, w_qkv.at[mine, pl.ds(2 * keys, values)]),
            (gate_ref, w_gate.at[mine]),
            (out_ref, tall),
        ))
    ]
    start(local)

    half_width = width // 2
    token_loads = [
        pltpu.make_async_copy(token_ref.at[pl.ds(0, half)], field_out, token_sem.at[0]),
        pltpu.make_async_copy(token_ref.at[pl.ds(half, half), pl.ds(0, half_width)], gated_out, token_sem.at[1]),
        pltpu.make_async_copy(token_ref.at[pl.ds(half, half), pl.ds(half_width, half_width)], grouped_out, token_sem.at[2]),
    ]
    start(token_loads)
    own_cot = pltpu.make_async_copy(cot_ref, cot_all_ref.at[pl.ds(0, rows)], local_sem.at[6])
    own_cot.start()

    barrier = pltpu.get_barrier_semaphore()

    def greet(device):
        pl.semaphore_signal(barrier, inc=1, device_id=device, device_id_type=MESH)

    for device in (twin, over_x, over_y):
        greet(device)
    pl.when(z < layers - 1)(lambda: greet(above))
    pl.when(z > 0)(lambda: greet(below))
    pl.semaphore_wait(barrier, 3 + (z < layers - 1).astype(jnp.int32) + (z > 0).astype(jnp.int32))
    wait(local[:4])


    groups = ((w_qkv, w_gate), (w_out,))

    def shard_copies(g, shard, send_sem, recv_sem, index, device):
        place = block_of(shard * depth, depth)
        return [
            remote(ref.at[place], ref.at[place], send_sem.at[index, i + 2 * g], recv_sem.at[index, i + 2 * g], device)
            for i, ref in enumerate(groups[g])
        ]

    def rise(g, j):
        return shard_copies(g, dp - 2 * j, up_send, up_recv, j, above)

    def sink(g, j):
        return shard_copies(g, dp + 2 * j, down_send, down_recv, j, below)

    def to_twin(g, j):
        return shard_copies(g, dp + 2 * j, core_send, core_recv, j + 3, twin)

    def from_twin(g, j):
        return shard_copies(g, twin[0] + 2 * j, core_send, core_recv, j + 3, twin)

    def wait_recv(copies):
        for copy in copies:
            copy.wait_recv()

    def wait_send(copies):
        for copy in copies:
            copy.wait_send()

    def first_step(g):
        pl.when(z < layers - 1)(lambda: start(rise(g, 0)))
        pl.when(z > 0)(lambda: start(sink(g, 0)))
        start(to_twin(g, 0))

    def step(g, j):
        @pl.when(z - j >= 0)
        def _():
            wait_recv(shard_copies(g, dp - 2 * j, up_send, up_recv, j - 1, twin))
            if j < 3:
                pl.when(z < layers - 1)(lambda: start(rise(g, j)))
            start(to_twin(g, -j))

        @pl.when(z + j < layers)
        def _():
            wait_recv(shard_copies(g, dp + 2 * j, down_send, down_recv, j - 1, twin))
            if j < 3:
                pl.when(z > 0)(lambda: start(sink(g, j)))
            start(to_twin(g, j))

    def when_end(wanted, work):
        pl.when(((z == 0) | (z == 3)) == wanted)(work)

    def twin_step(g, j):
        for signed in sorted({-j, j}):
            @pl.when((z + signed >= 0) & (z + signed < layers))
            def _():
                wait_recv(from_twin(g, signed))

    def rows_of(r, first=0, count=rows):
        return pl.ds(r * rows + first, count)

    def row_copy(index, src, dst, device):
        return remote(src, dst, row_send.at[index], row_recv.at[index], device)

    piece = 64
    cot_early = [
        row_copy(8, cot_ref.at[pl.ds(0, piece)], cot_all_ref.at[rows_of(1, 0, piece)], over_x),
        row_copy(9, cot_ref.at[pl.ds(0, piece)], cot_all_ref.at[rows_of(2, 0, piece)], over_y),
    ]
    cot_over = [
        row_copy(4, cot_ref.at[pl.ds(piece, rows - piece)], cot_all_ref.at[rows_of(1, piece, rows - piece)], over_x),
        row_copy(5, cot_ref.at[pl.ds(piece, rows - piece)], cot_all_ref.at[rows_of(2, piece, rows - piece)], over_y),
    ]

    first_step(0)
    start(cot_early)

    wait(token_loads)

    @pl.loop(0, half // 64)
    def _(i):
        place = block_of(i * 64, 64)
        plain, _ = normalize(field_out[place].astype(f32))
        normed[place] = (plain * gain_ref[...] + bias_ref[...]).astype(bf16)

    @pl.loop(0, half // 64)
    def _(i):
        place = block_of(i * 64, 64)
        both = jnp.concatenate([gated_out[place], grouped_out[place]], axis=1)
        plain, _ = normalize(both.astype(f32))
        normed[block_of(half + i * 64, 64)] = (plain * gain_ref[...] + bias_ref[...]).astype(bf16)

    over = [
        row_copy(0, normed.at[rows_of(0)], normed.at[rows_of(1)], over_x),
        row_copy(1, normed.at[rows_of(0)], normed.at[rows_of(2)], over_y),
    ]
    onward = [
        row_copy(2, normed.at[rows_of(2, 0, half)], normed.at[rows_of(3, 0, half)], over_x),
        row_copy(3, normed.at[rows_of(1, half, half)], normed.at[rows_of(3, half, half)], over_y),
    ]
    cot_onward = [
        row_copy(6, cot_all_ref.at[rows_of(2, 0, half)], cot_all_ref.at[rows_of(3, 0, half)], over_x),
        row_copy(7, cot_all_ref.at[rows_of(1, half, half)], cot_all_ref.at[rows_of(3, half, half)], over_y),
    ]
    start(over)

    local[4].wait()
    w_out[mine, :] = tall[...].T
    down_load = pltpu.make_async_copy(down_ref, tall, local_sem.at[4])
    down_load.start()

    half_key = KEY // 2
    lanes = lax.broadcasted_iota(jnp.int32, (CHUNK, half_key), 1).astype(f32)
    frequency = jnp.exp(lanes * (-9.210340371976184 / half_key))
    chunks = 4 * rows // CHUNK

    @pl.loop(0, chunks)
    def _(c):
        seat = block_of(c * CHUNK, CHUNK)
        diagonal = lax.broadcasted_iota(jnp.int32, (CHUNK, CHUNK), 0) == lax.broadcasted_iota(jnp.int32, (CHUNK, CHUNK), 1)
        own = jnp.sum(jnp.where(diagonal, jnp.maximum(row_ref[c], -1.0), 0.0), axis=1, keepdims=True)
        info[seat, :] = jnp.broadcast_to(own, (CHUNK, 128))
        ranked = jnp.where(own < 0, 3.0, own)
        before = jnp.zeros((CHUNK, 1), f32)
        for other in range(chunks):
            seen = row_ref[other]
            seen = jnp.where(seen < 0, 3.0, seen)
            before = before + jnp.sum((seen < ranked).astype(f32), axis=1, keepdims=True)
        index = lax.broadcasted_iota(jnp.int32, (CHUNK, 1), 0) + c * CHUNK
        turned = (index.astype(f32) - before) * frequency
        angles[seat, 0:half_key] = jnp.cos(turned)
        angles[seat, half_key:KEY] = jnp.sin(turned)

    distance = lax.broadcasted_iota(jnp.int32, (CHUNK, CHUNK), 0) - lax.broadcasted_iota(jnp.int32, (CHUNK, CHUNK), 1)
    span = jnp.maximum(distance, 0).astype(f32)
    for head in range(heads):
        decay[head] = jnp.where(distance >= 0, jnp.exp(rate_ref[head : head + 1, 0:1] * span), 0.0)
    down_load.wait()
    gate_out[...] = tall[...].T
    table_outs = [
        pltpu.make_async_copy(gate_out, down_turned_ref, table_sem.at[3]),
        pltpu.make_async_copy(angles, angle_ref, table_sem.at[0]),
        pltpu.make_async_copy(decay, decay_ref, table_sem.at[1]),
    ]
    start(table_outs)


    at_end = (z == 0) | (z == 3)

    def seen_from_end(index):
        return jnp.where(z >= 2, 3 - index, index)

    order = [z, jnp.where(at_end, seen_from_end(1), seen_from_end(0)), seen_from_end(2), seen_from_end(3)]

    def project(r, s):
        deep = block_of(order[s] * 2 * depth, 2 * depth)

        @pl.loop(0, (2 * keys + values) // 512)
        def _(j):
            tile = block_of(j * 512, 512)
            more = dot_nn(normed[rows_of(r), deep], w_qkv[deep, tile])
            product[rows_of(r), tile] = more if s == 0 else product[rows_of(r), tile] + more

        @pl.loop(0, values // 512)
        def _(j):
            tile = block_of(j * 512, 512)
            more = dot_nn(normed[rows_of(r), deep], w_gate[deep, tile])
            place = block_of(2 * keys + values + j * 512, 512)
            product[rows_of(r), place] = more if s == 0 else product[rows_of(r), place] + more


    per_piece = rows // CHUNK

    def chunk_place(c):
        piece = lax.div(c, per_piece)
        low = lax.rem(lax.rem(piece, 2) + lax.rem(tensor, 2), 2)
        high = lax.rem(lax.div(piece, 2) + lax.div(tensor, 2), 2)
        return (2 * high + low) * per_piece + lax.rem(c, per_piece)

    def chunk_outs(c):
        place = block_of(chunk_place(c) * CHUNK, CHUNK)
        pairs = (
            (field_out, field_ref.at[place]),
            (gate_out, gate_raw_ref.at[place]),
            (gated_out, gated_ref.at[place]),
            (grouped_out, grouped_ref.at[place]),
            (scale_out, scale_ref.at[place]),
            (past_out, past_ref.at[c]),
        )
        return [pltpu.make_async_copy(src, dst, stage_sem.at[i]) for i, (src, dst) in enumerate(pairs)]

    def retention(between):
        state[...] = jnp.zeros_like(state)

        @pl.loop(0, chunks)
        def _(c):
            place = block_of(chunk_place(c) * CHUNK, CHUNK)
            seat = block_of(c * CHUNK, CHUNK)
            cosine = angles[seat, 0:half_key]
            sine = angles[seat, half_key:KEY]
            own = info[seat, 0:1]
            same = own == row_ref[c]
            entering = (own == row_ref[jnp.maximum(c - 1, 0)][:, CHUNK - 1 :]) & (c > 0)
            leaving = own == row_ref[c][:, CHUNK - 1 :]
            offset = lax.broadcasted_iota(jnp.int32, (CHUNK, 1), 0).astype(f32)
            lane = lax.broadcasted_iota(jnp.int32, (CHUNK, 128), 1)
            facts = jnp.where(lane == 0, own, 0.0)
            scales = jnp.zeros((CHUNK, 128), f32)

            for head in range(heads):
                rate = rate_ref[head : head + 1, 0:1]
                into = jnp.where(entering, jnp.exp(rate * (offset + 1.0)), 0.0)
                onto = jnp.where(leaving, jnp.exp(rate * (CHUNK - 1.0 - offset)), 0.0)
                facts = jnp.where(lane == 1 + 2 * head, into, facts)
                facts = jnp.where(lane == 2 + 2 * head, onto, facts)
                query_raw = product[place, pl.ds(head * KEY, KEY)]
                key_raw = product[place, pl.ds(keys + head * KEY, KEY)]
                value = product[place, pl.ds(2 * keys + head * VAL, VAL)].astype(bf16)
                gate = product[place, pl.ds(2 * keys + values + head * VAL, VAL)]
                query_raw = query_raw.astype(bf16)
                key_raw = key_raw.astype(bf16)
                query = turn(query_raw.astype(f32), cosine, sine).astype(bf16)
                key = (turn(key_raw.astype(f32), cosine, sine) * key_scale).astype(bf16)
                memory = state[head]
                memory_low = memory.astype(bf16)
                scores = dot_nt(query, key)
                weights = (jnp.where(same, decay[head], 0.0) * scores).astype(bf16)
                retained = dot_nn(weights, value) + into * dot_nn(query, memory_low)
                moved = (key.astype(f32) * onto).astype(bf16)
                state[head] = into[CHUNK - 1 :, :] * memory + dot_tn(moved, value)
                centred = retained - jnp.mean(retained, axis=-1, keepdims=True)
                scale = lax.rsqrt(jnp.mean(centred * centred, axis=-1, keepdims=True) + group_floor)
                grouped = centred * scale
                columns = pl.ds(head * VAL, VAL)
                if head == 0:
                    @pl.when(c > 0)
                    def _():
                        wait(chunk_outs(c - 1))

                field_out[:, pl.ds(head * KEY, KEY)] = query_raw
                field_out[:, pl.ds(keys + head * KEY, KEY)] = key_raw
                field_out[:, pl.ds(2 * keys + head * VAL, VAL)] = value
                gate_out[:, columns] = gate.astype(bf16)
                past_out[head] = memory_low
                gated_out[:, columns] = (gate / (1.0 + jnp.exp(-gate)) * grouped).astype(bf16)
                grouped_out[:, columns] = grouped.astype(bf16)
                scales = jnp.where(lane == head, scale, scales)
            info[seat, :] = facts
            scale_out[...] = scales
            start(chunk_outs(c))
            between(c)

        wait(chunk_outs(chunks - 1))


    twin_step(0, 0)
    project(0, 0)
    step(0, 1)
    twin_step(0, 1)
    project(0, 1)
    wait_recv(over)
    start(onward)
    start(cot_over)
    for r in (1, 2):
        for s in (0, 1):
            project(r, s)
    step(0, 2)
    first_step(1)
    twin_step(0, 2)
    for r in (0, 1, 2):
        project(r, 2)
    wait_recv(onward)
    normed_out = pltpu.make_async_copy(normed, normed_ref, local_sem.at[7])
    normed_out.start()
    for s in (0, 1, 2):
        project(3, s)
    when_end(False, lambda: step(1, 1))
    step(0, 3)
    twin_step(0, 3)
    w_outs = [
        pltpu.make_async_copy(w_qkv, w_qkv_ref, out_sem.at[0]),
        pltpu.make_async_copy(w_gate, w_gate_ref, out_sem.at[1]),
    ]
    start(w_outs)
    project(0, 3)
    project(1, 3)
    when_end(False, lambda: step(1, 2))
    wait_recv(cot_early + cot_over)
    start(cot_onward)
    project(2, 3)
    project(3, 3)

    def between(c):
        @pl.when((c == 1) & at_end)
        def _():
            step(1, 1)

        @pl.when((c == 4) & at_end)
        def _():
            step(1, 2)

    wait(table_outs)
    retention(between)
    info_out = pltpu.make_async_copy(info, info_ref, table_sem.at[2])
    info_out.start()
    step(1, 3)
    for j in range(4):
        twin_step(1, j)
    w_out_out = pltpu.make_async_copy(w_out, w_out_ref, out_sem.at[2])
    w_out_out.start()
    wait_recv(cot_onward)

    wait_send(over + onward + cot_early + cot_over + cot_onward)
    for g in range(2):
        for j in range(3):
            pl.when((z < layers - 1) & (z - j >= 0))(lambda: wait_send(rise(g, j)))
            pl.when((z > 0) & (z + j < layers))(lambda: wait_send(sink(g, j)))
        for j in range(-3, 4):
            pl.when((z + j >= 0) & (z + j < layers))(lambda: wait_send(to_twin(g, j)))
    wait(w_outs + [normed_out, own_cot, info_out, w_out_out])


def opening_exchange(heads, shards, tokens, cotangent, segment, gain, bias):
    dp = lax.axis_size("dp")
    depth, keys = shards[0].shape
    values = shards[2].shape[1]
    unit = shards[4].shape[0]
    token_rows, width = tokens.shape
    rows = 4 * token_rows
    chunks = rows // CHUNK
    anywhere = pl.BlockSpec(memory_space=pl.ANY)
    in_vmem = pl.BlockSpec(memory_space=pltpu.VMEM)
    sem = pltpu.SemaphoreType.DMA
    vmem = pltpu.VMEM
    here = lax.axis_index("tensor") * heads
    head_ids = (here + jnp.arange(8, dtype=jnp.int32)).astype(f32)
    rates = jnp.broadcast_to(jnp.log1p(-jnp.exp2(-5.0 - head_ids))[:, None], (8, 128))
    row_segment = jnp.where(segment >= 0, segment, -7).astype(f32).reshape(chunks, 1, CHUNK)
    results = pl.pallas_call(
        functools.partial(opening_kernel, heads),
        out_shape=[
            jax.ShapeDtypeStruct((dp * depth, 2 * keys + values), bf16),
            jax.ShapeDtypeStruct((dp * depth, values), bf16),
            jax.ShapeDtypeStruct((dp * depth, unit), bf16),
            jax.ShapeDtypeStruct((rows, width), bf16),
            jax.ShapeDtypeStruct((rows, width), bf16),
            jax.ShapeDtypeStruct((rows, 2 * keys + values), bf16),
            jax.ShapeDtypeStruct((rows, values), bf16),
            jax.ShapeDtypeStruct((rows, values), bf16),
            jax.ShapeDtypeStruct((rows, values), bf16),
            jax.ShapeDtypeStruct((rows, 128), f32),
            jax.ShapeDtypeStruct((chunks, heads, KEY, VAL), bf16),
            jax.ShapeDtypeStruct((rows, KEY), f32),
            jax.ShapeDtypeStruct((rows, 128), f32),
            jax.ShapeDtypeStruct((heads, CHUNK, CHUNK), f32),
            jax.ShapeDtypeStruct((depth, unit), bf16),
        ],
        in_specs=[anywhere] * 8 + [in_vmem] * 4,
        out_specs=[anywhere] * 15,
        scratch_shapes=[
            vmem((dp * depth, 2 * keys + values), bf16),
            vmem((dp * depth, values), bf16),
            vmem((dp * depth, unit), bf16),
            vmem((unit, depth), bf16),
            vmem((rows, width), bf16),
            vmem((rows, 2 * keys + 2 * values), f32),
            vmem((rows, KEY), f32),
            vmem((rows, 128), f32),
            vmem((heads, CHUNK, CHUNK), f32),
            vmem((heads, KEY, VAL), f32),
            vmem((CHUNK, 2 * keys + values), bf16),
            vmem((CHUNK, values), bf16),
            vmem((CHUNK, values), bf16),
            vmem((CHUNK, values), bf16),
            vmem((CHUNK, 128), f32),
            vmem((heads, KEY, VAL), bf16),
            sem((8,)), sem((3,)), sem((3,)), sem((6,)), sem((4,)),
            sem((3, 3)), sem((3, 3)), sem((3, 3)), sem((3, 3)), sem((7, 3)), sem((7, 3)), sem((10,)), sem((10,)),
        ],
        compiler_params=pltpu.CompilerParams(
            collective_id=2, has_side_effects=True, vmem_limit_bytes=63_400_000
        ),
        name="opening_exchange",
    )(*shards, tokens, cotangent, row_segment, rates, gain.reshape(1, width), bias.reshape(1, width))
    return results, row_segment


def middle_kernel(
    gated_ref, w_out_ref, up_ref, down_ref, cot_ref, token_ref, gain_ref, bias_ref,
    low_ref, plus_ref, feed_ref, up_grad_out, down_grad_out, late_ref,
    big, units, columns, staged, terms, half_in, full_in, mixed, plus, total,
    load_sem, column_sem, staged_sem, feed_sem, out_sem, up_send, up_recv, below_send, below_recv, core_send, core_recv,
    row_send, row_recv, half_send, half_recv, full_send, full_recv, half_free, full_free, big_free,
):
    dp = lax.axis_index("dp")
    tensor = lax.axis_index("tensor")
    z = lax.div(dp, 2)
    layers = 4
    rows = token_ref.shape[0]
    half = rows // 2
    width = token_ref.shape[1]
    unit = units.shape[2]
    depth = up_ref.shape[0]
    above = (dp + 2, tensor)
    below = (dp - 2, tensor)
    twin = (dp + 1 - 2 * lax.rem(dp, 2), tensor)
    over_x = (dp, tensor + 1 - 2 * lax.rem(tensor, 2))
    over_y = (dp, lax.rem(tensor + 2, 4))
    sides = (over_x, over_y)

    def block_of(start, count):
        return pl.ds(pl.multiple_of(start, count), count)

    def start(copies):
        for copy in copies:
            copy.start()

    def wait(copies):
        for copy in copies:
            copy.wait()

    def remote(src, dst, send, recv, device):
        return pltpu.make_async_remote_copy(
            src_ref=src, dst_ref=dst, send_sem=send, recv_sem=recv, device_id=device, device_id_type=MESH
        )

    mine = block_of(dp * depth, depth)
    shard_loads = [
        pltpu.make_async_copy(down_ref, units.at[3, mine], load_sem.at[0]),
        pltpu.make_async_copy(up_ref, units.at[2, mine], load_sem.at[1]),
    ]
    first_loads = [
        pltpu.make_async_copy(gated_ref, units.at[0], load_sem.at[2]),
        pltpu.make_async_copy(w_out_ref, units.at[1], load_sem.at[3]),
    ]
    token_load = pltpu.make_async_copy(token_ref, plus, load_sem.at[5])
    cot_load = pltpu.make_async_copy(cot_ref, big, load_sem.at[6])
    start(shard_loads)
    start(first_loads)
    token_load.start()
    cot_load.start()

    barrier = pltpu.get_barrier_semaphore()

    def greet(device):
        pl.semaphore_signal(barrier, inc=1, device_id=device, device_id_type=MESH)

    for device in (twin, over_x, over_y):
        greet(device)
    pl.when(z < layers - 1)(lambda: greet(above))
    pl.when(z > 0)(lambda: greet(below))
    pl.semaphore_wait(barrier, 3 + (z < layers - 1).astype(jnp.int32) + (z > 0).astype(jnp.int32))


    def shard_copy(a, shard, send_sem, recv_sem, index, device):
        place = block_of(shard * depth, depth)
        ref = units.at[3 - a, place]
        return remote(ref, ref, send_sem.at[a, index], recv_sem.at[a, index], device)

    def rise(a, j):
        return shard_copy(a, dp - 2 * j, up_send, up_recv, j, above)

    def sink(a, j):
        return shard_copy(a, dp + 2 * j, below_send, below_recv, j, below)

    def to_twin(a, j):
        return shard_copy(a, dp + 2 * j, core_send, core_recv, j + 3, twin)

    def from_twin(a, j):
        return shard_copy(a, twin[0] + 2 * j, core_send, core_recv, j + 3, twin)

    def first_step(a):
        shard_loads[a].wait()
        pl.when(z < layers - 1)(lambda: rise(a, 0).start())
        pl.when(z > 0)(lambda: sink(a, 0).start())
        to_twin(a, 0).start()

    def step(a, j):
        @pl.when(z - j >= 0)
        def _():
            shard_copy(a, dp - 2 * j, up_send, up_recv, j - 1, twin).wait_recv()
            if j < 3:
                pl.when(z < layers - 1)(lambda: rise(a, j).start())
            to_twin(a, -j).start()

        @pl.when(z + j < layers)
        def _():
            shard_copy(a, dp + 2 * j, below_send, below_recv, j - 1, twin).wait_recv()
            if j < 3:
                pl.when(z > 0)(lambda: sink(a, j).start())
            to_twin(a, j).start()

    def gathered(a):
        for j in range(-3, 4):
            @pl.when((z + j >= 0) & (z + j < layers))
            def _():
                from_twin(a, j).wait_recv()


    def rows_of(r, first=0, count=rows):
        return pl.ds(r * rows + first, count)

    halves = [
        remote(terms.at[2, pl.ds(0, half)], half_in.at[0], half_send.at[0], half_recv.at[0], over_x),
        remote(terms.at[2, pl.ds(half, half)], half_in.at[1], half_send.at[1], half_recv.at[1], over_y),
    ]

    def part_copy(index, term, first, device, count=half):
        place = pl.ds(first, count)
        return remote(
            terms.at[term, place], full_in.at[term, place], full_send.at[index], full_recv.at[index], device
        )

    plain_parts = [part_copy(0, 0, 0, over_x), part_copy(1, 1, half, over_y)]
    quarter = half // 2
    grown_parts = [
        part_copy(2, 0, half, over_x, quarter),
        part_copy(3, 1, 0, over_y, quarter),
        part_copy(4, 0, half + quarter, over_x, quarter),
        part_copy(5, 1, quarter, over_y, quarter),
    ]
    fulls = plain_parts + grown_parts
    lower, upper = (0, half), (half, half)

    def row_copy(index, source, first, target, device):
        return remote(
            big.at[rows_of(source, *first)], big.at[rows_of(target, *first)],
            row_send.at[index], row_recv.at[index], device,
        )

    early = [row_copy(0, 0, lower, 1, over_x), row_copy(1, 0, upper, 2, over_y)]
    across = [row_copy(2, 2, upper, 3, over_x), row_copy(3, 1, lower, 3, over_y)]
    late = [row_copy(4, 0, upper, 1, over_x), row_copy(5, 0, lower, 2, over_y)]

    def send_halves(stage):
        for i, copy in enumerate(halves):
            if stage == 1:
                pl.semaphore_wait(half_free.at[i], 1)
            copy.start()

    def take_halves(stage):
        for copy in halves:
            copy.wait_recv()
        for term, first, slot in ((1, 0, 0), (0, half, 1)):
            @pl.loop(0, half // 64)
            def _(i):
                place = block_of(first + i * 64, 64)
                grown = terms[term, place].astype(f32) + half_in[slot, block_of(i * 64, 64)].astype(f32)
                terms[term, place] = grown.astype(bf16)

        for i, copy in enumerate(grown_parts):
            if stage == 0 and i < 2:
                pl.semaphore_signal(half_free.at[i], inc=1, device_id=sides[i], device_id_type=MESH)
            copy.start()

    def send_plain(stage, i):
        if stage == 1:
            pl.semaphore_wait(full_free.at[i], 1)
        plain_parts[i].start()

    def slot_of(r):
        return (3, 0, 1, 2)[r]

    def branch_term(r):
        @pl.loop(0, width // 256)
        def _(j):
            tile = block_of(j * 256, 256)
            terms[slot_of(r), :, tile] = dot_nt(units[0, rows_of(r)], units[1, tile]).astype(bf16)

    def feed_grads(r):
        @pl.loop(0, unit // 256)
        def _(j):
            tile = block_of(j * 256, 256)
            units[4, rows_of(r), tile] = dot_nn(big[rows_of(r)], units[3, :, tile]).astype(bf16)

    def feed(r):
        @pl.loop(0, unit // 256)
        def _(j):
            tile = block_of(j * 256, 256)
            value, slope = gelu_both(dot_nn(big[rows_of(r)], units[2, :, tile]))
            units[0, rows_of(r), tile] = value.astype(bf16)
            units[1, rows_of(r), tile] = (units[4, rows_of(r), tile].astype(f32) * slope).astype(bf16)

    def back_term(r):
        @pl.loop(0, width // 256)
        def _(j):
            tile = block_of(j * 256, 256)
            terms[slot_of(r), :, tile] = dot_nt(units[1, rows_of(r)], units[2, tile]).astype(bf16)


    first_step(0)
    wait(first_loads)
    branch_term(3)
    send_halves(0)
    step(0, 1)
    branch_term(1)
    send_plain(0, 0)
    branch_term(2)
    send_plain(0, 1)
    step(0, 2)
    first_step(1)
    take_halves(0)
    branch_term(0)
    step(0, 3)
    cot_load.wait()
    gathered(0)
    step(1, 1)
    feed_grads(0)
    feed_grads(1)
    step(1, 2)
    feed_grads(2)
    feed_grads(3)
    for side in sides:
        pl.semaphore_signal(big_free, inc=1, device_id=side, device_id_type=MESH)
    step(1, 3)
    gathered(1)
    token_load.wait()
    pl.semaphore_wait(big_free, 2)

    def second_norm(i):
        place = block_of(i * 64, 64)
        value = plus[place].astype(f32) + terms[3, place].astype(f32)
        value = value + full_in[0, place].astype(f32) + full_in[1, place].astype(f32)
        mixed[place] = value
        plain, _ = normalize(value)
        big[place] = (plain * gain_ref[...] + bias_ref[...]).astype(bf16)

    for copy in plain_parts + grown_parts[:2]:
        copy.wait_recv()
    pl.loop(0, quarter // 64)(second_norm)
    pl.loop(half // 64, (half + quarter) // 64)(second_norm)
    for copy in grown_parts[2:]:
        copy.wait_recv()
    pl.loop(quarter // 64, half // 64)(second_norm)
    early[0].start()
    pl.loop((half + quarter) // 64, rows // 64)(second_norm)
    early[1].start()
    for i, side in enumerate(sides):
        pl.semaphore_signal(full_free.at[i], inc=1, device_id=side, device_id_type=MESH)
    feed(0)
    for copy in halves + fulls:
        copy.wait_send()
    back_term(0)
    for copy in early:
        copy.wait_recv()
    start(across)
    start(late)

    def cot_columns(t):
        return pltpu.make_async_copy(cot_ref.at[:, pl.ds(t * 512, 512)], columns.at[t % 2], column_sem.at[t])

    cot_columns(0).start()
    cot_columns(1).start()
    for copy in across:
        copy.wait_recv()
    feed(3)
    back_term(3)
    send_halves(1)
    for copy in late:
        copy.wait_recv()
    feed(1)
    back_term(1)
    send_plain(1, 0)
    feed(2)
    back_term(2)
    send_plain(1, 1)
    take_halves(1)

    def staged_out(out, t, slot):
        return pltpu.make_async_copy(staged.at[slot], out.at[pl.ds(t * 512, 512)], staged_sem.at[slot])

    def weight_grad(out, t, left_of, right):
        for j in range(unit // 256):
            tile = pl.ds(j * 256, 256)
            product = None
            for place in (pl.ds(0, 2 * rows), pl.ds(2 * rows, 2 * rows)):
                more = dot_tn(left_of(place), units[right, place, tile])
                product = more if product is None else product + more
            staged[t % 2, :, tile] = product.astype(bf16)
        staged_out(out, t, t % 2).start()

    for t in range(4):
        cot_columns(t).wait()
        if t >= 2:
            staged_out(down_grad_out, t - 2, t % 2).wait()
        weight_grad(down_grad_out, t, lambda place: columns[t % 2, place], 0)
        if t < 2:
            cot_columns(t + 2).start()
    for t in range(4):
        if t < 2:
            staged_out(down_grad_out, t + 2, t % 2).wait()
        else:
            staged_out(up_grad_out, t - 2, t % 2).wait()
        weight_grad(up_grad_out, t, lambda place: big[place, pl.ds(t * 512, 512)], 1)

    def feed_out(t):
        return pltpu.make_async_copy(columns.at[t % 2], feed_ref.at[:, pl.ds(t * 512, 512)], feed_sem.at[t % 2])

    for t in range(4):
        if t >= 2:
            feed_out(t - 2).wait()

        @pl.loop(0, 4)
        def _(r):
            place = block_of(r * rows, rows)
            columns[t % 2, place] = dot_nt(units[0, place], units[3, pl.ds(t * 512, 512)]).astype(bf16)

        feed_out(t).start()

        @pl.loop(0, rows // 64)
        def _(i):
            place = block_of(i * 64, 64)
            tile = pl.ds(t * 512, 512)
            plus[place, tile] = (mixed[place, tile] + columns[t % 2, place].astype(f32)).astype(bf16)

    plus_out = pltpu.make_async_copy(plus, plus_ref, out_sem.at[0])
    plus_out.start()
    for copy in halves:
        copy.wait_send()
    cot_own = pltpu.make_async_copy(cot_ref.at[pl.ds(0, rows)], terms.at[2], load_sem.at[7])
    cot_own.start()
    total[...] = jnp.zeros_like(total)
    cot_own.wait()

    def second_norm_back(i):
        place = block_of(i * 64, 64)
        grad = terms[3, place].astype(f32) + full_in[0, place].astype(f32) + full_in[1, place].astype(f32)
        plain, scale = normalize(mixed[place])
        back = terms[2, place].astype(f32) + normalize_back(grad, plain, scale, gain_ref[...])
        full_in[0, place] = back.astype(bf16)
        total[0:1, :] += jnp.sum(grad * plain, axis=0, keepdims=True)
        total[1:2, :] += jnp.sum(grad, axis=0, keepdims=True)

    for copy in plain_parts + grown_parts[:2]:
        copy.wait_recv()
    pl.loop(0, quarter // 64)(second_norm_back)
    pl.loop(half // 64, (half + quarter) // 64)(second_norm_back)
    for copy in grown_parts[2:]:
        copy.wait_recv()
    pl.loop(quarter // 64, half // 64)(second_norm_back)
    pl.loop((half + quarter) // 64, rows // 64)(second_norm_back)
    low_out = pltpu.make_async_copy(full_in.at[0], low_ref, out_sem.at[1])
    low_out.start()
    late_ref[...] = total[...]

    for t in (2, 3):
        staged_out(up_grad_out, t, t % 2).wait()
        feed_out(t).wait()
    for copy in fulls + early + across + late:
        copy.wait_send()
    for a in range(2):
        for j in range(3):
            pl.when((z < layers - 1) & (z - j >= 0))(lambda: rise(a, j).wait_send())
            pl.when((z > 0) & (z + j < layers))(lambda: sink(a, j).wait_send())
        for j in range(-3, 4):
            pl.when((z + j >= 0) & (z + j < layers))(lambda: to_twin(a, j).wait_send())
    plus_out.wait()
    low_out.wait()


def middle_exchange(gated, w_out, up_shard, down_shard, cot_all, tokens, gain, bias):
    token_rows, width = tokens.shape
    rows = 4 * token_rows
    unit = gated.shape[1]
    anywhere = pl.BlockSpec(memory_space=pl.ANY)
    in_vmem = pl.BlockSpec(memory_space=pltpu.VMEM)
    sem = pltpu.SemaphoreType.DMA
    regular = pltpu.SemaphoreType.REGULAR
    vmem = pltpu.VMEM
    return pl.pallas_call(
        middle_kernel,
        out_shape=[
            jax.ShapeDtypeStruct((token_rows, width), bf16),
            jax.ShapeDtypeStruct((token_rows, width), bf16),
            jax.ShapeDtypeStruct((rows, width), bf16),
            jax.ShapeDtypeStruct((width, unit), bf16),
            jax.ShapeDtypeStruct((width, unit), bf16),
            jax.ShapeDtypeStruct((2, width), f32),
        ],
        in_specs=[anywhere] * 6 + [in_vmem] * 2,
        out_specs=[anywhere] * 5 + [in_vmem],
        scratch_shapes=[
            vmem((rows, width), bf16),
            vmem((5, rows, unit), bf16),
            vmem((2, rows, 512), bf16),
            vmem((2, 512, unit), bf16),
            vmem((4, token_rows, width), bf16),
            vmem((2, token_rows // 2, width), bf16),
            vmem((2, token_rows, width), bf16),
            vmem((token_rows, width), f32),
            vmem((token_rows, width), bf16),
            vmem((2, width), f32),
            sem((8,)), sem((4,)), sem((2,)), sem((2,)), sem((2,)),
            sem((2, 3)), sem((2, 3)), sem((2, 3)), sem((2, 3)), sem((2, 7)), sem((2, 7)),
            sem((6,)), sem((6,)), sem((2,)), sem((2,)), sem((6,)), sem((6,)),
            regular((2,)), regular((2,)), regular,
        ],
        compiler_params=pltpu.CompilerParams(
            collective_id=4, has_side_effects=True, vmem_limit_bytes=63_400_000
        ),
        name="middle_exchange",
    )(gated, w_out, up_shard, down_shard, cot_all, tokens, gain.reshape(1, width), bias.reshape(1, width))


def closing_kernel(
    heads,
    normed1_ref, up_ref, down_ref, feed_ref, w_out_ref, w_qkv_ref, w_gate_ref,
    gate_ref, grouped_ref, gated_ref, scale_ref, field_ref, past_ref, angle_ref, info_ref,
    low_ref, token_ref, row_ref, decay_ref, gain_ref, late_ref,
    result_ref, grad_ref, query_out, key_out, value_out, gate_out, out_out, up_out, down_out, sums_ref,
    big, units, columns, terms, half_in, full_in, products, twin_in, line_in,
    state_ref, past_in, scale_in, angle_in, info_in, given, landed, total,
    unit_sem, column_sem, chunk_sem, out_sem, mixed_sem, over_send, over_recv, onward_send, onward_recv,
    half_send, half_recv, full_send, full_recv, twin_send, twin_recv, line_send, line_recv, sum_send, sum_recv,
    twin_free, line_free, half_free, full_free,
):
    dp = lax.axis_index("dp")
    tensor = lax.axis_index("tensor")
    z = lax.div(dp, 2)
    core = lax.rem(dp, 2)
    rows = token_ref.shape[0]
    half = rows // 2
    width = token_ref.shape[1]
    unit = units.shape[2]
    depth = columns.shape[2] // 2
    at_end = (z == 0) | (z == 3)
    upper = z >= 2
    twin = (dp + 1 - 2 * core, tensor)
    over_x = (dp, tensor + 1 - 2 * lax.rem(tensor, 2))
    over_y = (dp, lax.rem(tensor + 2, 4))
    here = dp * 4 + tensor
    peers = 32
    last = 5

    def layer(index):
        return (2 * index + core, tensor)

    def seen(index):
        return jnp.where(upper, 3 - index, index)

    end = layer(seen(0))
    near = layer(seen(1))
    opposite = layer(seen(2))
    targets = [seen(3), seen(2), jnp.where(at_end, seen(1), seen(0)), z]

    def remote(src, dst, send, recv, device):
        return pltpu.make_async_remote_copy(
            src_ref=src, dst_ref=dst, send_sem=send, recv_sem=recv, device_id=device, device_id_type=MESH
        )

    def block_of(start, count):
        return pl.ds(pl.multiple_of(start, count), count)


    def whole(index, ref, sem):
        return [pltpu.make_async_copy(ref, units.at[index], unit_sem.at[sem])]

    def part(index, ref, start, sem):
        return [pltpu.make_async_copy(ref.at[:, pl.ds(start, unit)], units.at[index], unit_sem.at[sem])]

    def start(copies):
        for copy in copies:
            copy.start()

    def wait(copies):
        for copy in copies:
            copy.wait()

    out_load = whole(3, w_out_ref, 4)
    feed_load = [
        pltpu.make_async_copy(feed_ref.at[pl.ds((i + 1) * rows, rows)], terms.at[i], unit_sem.at[i]) for i in range(3)
    ]
    gated_load = whole(2, gated_ref, 6)
    w_gate_load = whole(3, w_gate_ref, 7)
    w_value_load = part(2, w_qkv_ref, unit, 8)
    w_key_load = part(1, w_qkv_ref, 0, 9)

    def wait_recv(copies):
        for copy in copies:
            copy.wait_recv()

    def wait_send(copies):
        for copy in copies:
            copy.wait_send()


    sources = [up_ref, down_ref, None, normed1_ref, normed1_ref, normed1_ref]

    def given_copy(r, k):
        place = block_of(targets[k] * 2 * depth, 2 * depth)
        return pltpu.make_async_copy(sources[r].at[place], products.at[r, k], column_sem.at[4 * r + k])

    def column_copy(r, k):
        place = block_of(targets[k] * 2 * depth, 2 * depth)
        return pltpu.make_async_copy(sources[r].at[:, place], columns.at[k % 2], column_sem.at[k])

    def prefetch(r):
        column_copy(r, 0).start()
        column_copy(r, 1).start()

    mine = block_of(core * depth, depth)
    theirs = block_of((1 - core) * depth, depth)

    def to_twin(r, k):
        return remote(
            products.at[r % 2, k, theirs], twin_in.at[k % 2], twin_send.at[r % 2, k], twin_recv.at[k % 2], twin
        )

    def along(r, k, slot, device):
        return remote(
            products.at[r % 2, k, mine], line_in.at[slot], line_send.at[r % 2, k], line_recv.at[slot], device
        )

    def send_to_twin(r, k):
        if r >= 1 or k >= 2:
            pl.semaphore_wait(twin_free.at[k % 2], 1)
        to_twin(r, k).start()

    def multiply(r, k):
        to_twin(r - 2, k).wait_send()
        if k < 3:
            along(r - 2, k, 0, end).wait_send()
        else:
            wait(outputs(r - 2))
        if sources[r] is not None:
            column_copy(r, k).wait()

        @pl.loop(0, unit // 512)
        def _(j):
            tile = block_of(j * 512, 512)
            product = None
            for place in (pl.ds(0, 2 * rows), pl.ds(2 * rows, 2 * rows)):
                if r < 4:
                    right = units[(None, None, 2, 0)[r], place, tile]
                else:
                    right = big[place, block_of((r - 4) * unit + j * 512, 512)]
                if sources[r] is None:
                    left = big[place, block_of(targets[k] * 2 * depth, 2 * depth)]
                else:
                    left = columns[k % 2, place]
                more = dot_tn(left, right)
                product = more if product is None else product + more
            products[r % 2, k, :, tile] = product.astype(bf16)

        if sources[r] is not None and k + 2 < 4:
            column_copy(r, k + 2).start()
        elif r == 4:
            column_copy(5, k - 2).start()
        send_to_twin(r, k)

    def add_to_mine(r, k, others):
        @pl.loop(0, depth // 64)
        def _(i):
            inner = block_of(core * depth + i * 64, 64)
            value = products[r % 2, k, inner].astype(f32)
            for ref, index in others:
                value = value + ref[index, block_of(i * 64, 64)].astype(f32)
            products[r % 2, k, inner] = value.astype(bf16)

    def settle(r, k):
        to_twin(r, k).wait_recv()
        add_to_mine(r, k, [(twin_in, k % 2)])
        if r < last or k < 2:
            pl.semaphore_signal(twin_free.at[k % 2], inc=1, device_id=twin, device_id_type=MESH)

    def push(r, k):
        @pl.when(at_end)
        def _():
            if r >= 1:
                pl.semaphore_wait(line_free.at[k], 1)
            along(r, k, k, near).start()

    def line_wait(slot):
        along(0, 0, slot, end).wait_recv()

    def used(device, index):
        pl.semaphore_signal(line_free.at[index], inc=1, device_id=device, device_id_type=MESH)

    def pass_on(r, which):
        arrived, sender, slot, device = ((0, end, 3, opposite), (1, end, 4, opposite), (3, opposite, 0, end))[which]

        @pl.when(jnp.logical_not(at_end))
        def _():
            line_wait(arrived)
            add_to_mine(r, which, [(line_in, arrived)])
            if r < last:
                used(sender, (0, 1, 0)[which])
            if r >= 1:
                pl.semaphore_wait(line_free.at[which], 1)
            along(r, which, slot, device).start()

    def outputs(r):
        keys = heads * KEY
        slot = products.at[r % 2, 3]
        if r == 4:
            return [
                pltpu.make_async_copy(slot.at[mine, pl.ds(0, keys)], query_out, out_sem.at[0, 0]),
                pltpu.make_async_copy(slot.at[mine, pl.ds(keys, keys)], key_out, out_sem.at[0, 1]),
            ]
        out = (up_out, down_out, out_out, gate_out, None, value_out)[r]
        return [pltpu.make_async_copy(slot.at[mine], out, out_sem.at[r % 2, 0])]

    def finish(r):
        @pl.when(at_end)
        def _():
            line_wait(0)
            add_to_mine(r, 3, [(line_in, 0)])
            if r < last:
                used(near, 2)

        @pl.when(jnp.logical_not(at_end))
        def _():
            line_wait(2)
            line_wait(4)
            add_to_mine(r, 3, [(line_in, 2), (line_in, 4)])
            if r < last:
                used(end, 2)
                used(opposite, 1)

        start(outputs(r))


    def rows_of(r, first=0, count=rows):
        return pl.ds(r * rows + first, count)

    over = [
        remote(big.at[rows_of(0)], big.at[rows_of(1)], over_send.at[0], over_recv.at[0], over_x),
        remote(big.at[rows_of(0)], big.at[rows_of(2)], over_send.at[1], over_recv.at[1], over_y),
    ]
    onward = [
        remote(big.at[rows_of(2, 0, half)], big.at[rows_of(3, 0, half)], onward_send.at[0], onward_recv.at[0], over_x),
        remote(big.at[rows_of(1, half, half)], big.at[rows_of(3, half, half)], onward_send.at[1], onward_recv.at[1], over_y),
    ]
    halves = [
        remote(terms.at[2, pl.ds(0, half)], half_in.at[0], half_send.at[0], half_recv.at[0], over_x),
        remote(terms.at[2, pl.ds(half, half)], half_in.at[1], half_send.at[1], half_recv.at[1], over_y),
    ]

    def part_copy(index, term, first, device, count=half):
        place = pl.ds(first, count)
        return remote(
            terms.at[term, place], full_in.at[term, place], full_send.at[index], full_recv.at[index], device
        )

    plain_parts = [part_copy(0, 0, 0, over_x), part_copy(1, 1, half, over_y)]
    quarter = half // 2
    grown_parts = [
        part_copy(2, 0, half, over_x, quarter),
        part_copy(3, 1, 0, over_y, quarter),
        part_copy(4, 0, half + quarter, over_x, quarter),
        part_copy(5, 1, quarter, over_y, quarter),
    ]
    fulls = plain_parts + grown_parts
    sides = (over_x, over_y)

    def send_halves(stage):
        for i, copy in enumerate(halves):
            if stage == 1:
                pl.semaphore_wait(half_free.at[i], 1)
            copy.start()

    def take_halves(stage):
        for copy in halves:
            copy.wait_recv()
        for term, first, slot in ((1, 0, 0), (0, half, 1)):
            @pl.loop(0, half // 64)
            def _(i):
                place = block_of(first + i * 64, 64)
                grown = terms[term, place].astype(f32) + half_in[slot, block_of(i * 64, 64)].astype(f32)
                terms[term, place] = grown.astype(bf16)

        for i, copy in enumerate(grown_parts):
            if stage == 0 and i < 2:
                pl.semaphore_signal(half_free.at[i], inc=1, device_id=sides[i], device_id_type=MESH)
            copy.start()

    def send_plain(stage, i):
        if stage == 1:
            pl.semaphore_wait(full_free.at[i], 1)
        plain_parts[i].start()

    def project(r):
        slot = (2, 0, 1, 2)[r]

        @pl.loop(0, width // 512)
        def _(j):
            tile = block_of(j * 512, 512)
            term = dot_nt(big[rows_of(r), pl.ds(0, unit)], units[1, tile])
            term = term + dot_nt(big[rows_of(r), pl.ds(unit, unit)], units[2, tile])
            term = term + dot_nt(units[0, rows_of(r)], units[3, tile])
            terms[slot, :, tile] = term.astype(bf16)


    def gate_copies(r):
        return [
            pltpu.make_async_copy(
                ref.at[rows_of(r), pl.ds(h * VAL, VAL)],
                columns.at[r % 2, pl.ds((2 * i + h) * rows, rows)],
                chunk_sem.at[r % 2, 2 * i + h],
            )
            for i, ref in enumerate((gate_ref, grouped_ref))
            for h in range(heads)
        ] + [pltpu.make_async_copy(scale_ref.at[rows_of(r)], scale_in.at[r % 2], chunk_sem.at[r % 2, 2 * heads])]

    def gate_back(r):
        wait(gate_copies(r))
        for head in range(heads):
            tile = pl.ds(head * VAL, VAL)

            @pl.loop(0, rows // CHUNK)
            def _(i):
                place = block_of(r * rows + i * CHUNK, CHUNK)
                grad = dot_nn(big[place], units[3, :, tile])
                raw = columns[r % 2, block_of(head * rows + i * CHUNK, CHUNK)].astype(f32)
                grouped = columns[r % 2, block_of((heads + head) * rows + i * CHUNK, CHUNK)].astype(f32)
                sigmoid = 1.0 / (1.0 + jnp.exp(-raw))
                units[0, place, tile] = (grad * grouped * (sigmoid * (1.0 + raw * (1.0 - sigmoid)))).astype(bf16)
                c = grad * (raw * sigmoid)
                mean_c = jnp.mean(c, axis=-1, keepdims=True)
                mean_cx = jnp.mean(c * grouped, axis=-1, keepdims=True)
                scale = scale_in[r % 2, block_of(i * CHUNK, CHUNK), head : head + 1]
                units[1, place, tile] = (scale * (c - mean_c - grouped * mean_cx)).astype(bf16)

    chunks = 4 * rows // CHUNK
    per_piece = rows // CHUNK

    def chunk_place(c):
        piece = lax.div(c, per_piece)
        low = lax.rem(lax.rem(piece, 2) + lax.rem(tensor, 2), 2)
        high = lax.rem(lax.div(piece, 2) + lax.div(tensor, 2), 2)
        return (2 * high + low) * per_piece + lax.rem(c, per_piece)

    def chunk_copies(c, slot):
        place = block_of(chunk_place(c) * CHUNK, CHUNK)
        seat = block_of(c * CHUNK, CHUNK)
        keys = heads * KEY
        pieces = [
            (field_ref.at[place, pl.ds(0, keys)], columns.at[slot, pl.ds(0, CHUNK)]),
            (field_ref.at[place, pl.ds(keys, keys)], columns.at[slot, pl.ds(CHUNK, CHUNK)]),
        ]
        for h in range(heads):
            pieces.append((field_ref.at[place, pl.ds(2 * keys + h * VAL, VAL)], columns.at[slot, pl.ds((2 + h) * CHUNK, CHUNK)]))
        pieces += [
            (past_ref.at[c], past_in.at[slot]),
            (angle_ref.at[seat], angle_in.at[slot]),
            (info_ref.at[seat], info_in.at[slot]),
        ]
        return [pltpu.make_async_copy(src, dst, chunk_sem.at[slot, i]) for i, (src, dst) in enumerate(pieces)]

    def retention_steps(between):
        @pl.loop(0, chunks)
        def _(step):
            c = chunks - 1 - step
            slot = lax.rem(step, 2)
            wait(chunk_copies(c, slot))

            @pl.when(step + 1 < chunks)
            def _():
                start(chunk_copies(c - 1, 1 - slot))

            place = block_of(chunk_place(c) * CHUNK, CHUNK)
            angles = angle_in[slot]
            cosine = angles[:, : KEY // 2]
            sine = angles[:, KEY // 2 :]
            info = info_in[slot]
            same = info[:, 0:1] == row_ref[c]

            for head in range(heads):
                at = pl.ds(head * KEY, KEY)
                query = turn(columns[slot, pl.ds(0, CHUNK), at].astype(f32), cosine, sine).astype(bf16)
                key = turn(columns[slot, pl.ds(CHUNK, CHUNK), at].astype(f32), cosine, sine)
                key = (key * key_scale).astype(bf16)
                value = columns[slot, pl.ds((2 + head) * CHUNK, CHUNK)]
                into = info[:, 1 + 2 * head : 2 + 2 * head]
                onto = info[:, 2 + 2 * head : 3 + 2 * head]
                past = past_in[slot, head]
                out_grad = units[1, place, pl.ds(head * VAL, VAL)]
                state = state_ref[head]
                state_low = state.astype(bf16)
                masked = jnp.where(same, decay_ref[head], 0.0)
                weights = (masked * dot_nt(query, key)).astype(bf16)
                score_grad = (masked * dot_nt(out_grad, value)).astype(bf16)
                value_grad = dot_tn(weights, out_grad) + onto * dot_nn(key, state_low)
                query_grad = dot_nn(score_grad, key) + into * dot_nt(out_grad, past)
                key_grad = dot_tn(score_grad, query) + onto * dot_nt(value, state_low)
                moved = (query.astype(f32) * into).astype(bf16)
                state_ref[head] = into[CHUNK - 1 :, :] * state + dot_tn(moved, out_grad)
                big[place, pl.ds(head * KEY, KEY)] = turn_back(query_grad, cosine, sine).astype(bf16)
                big[place, pl.ds((heads + head) * KEY, KEY)] = (turn_back(key_grad, cosine, sine) * key_scale).astype(bf16)
                big[place, pl.ds(2 * heads * KEY + head * VAL, VAL)] = value_grad.astype(bf16)

            between(step)

    blocks = width // columns.shape[2]
    last_loads = [
        pltpu.make_async_copy(
            ref.at[:, pl.ds(q * columns.shape[2], columns.shape[2])], columns.at[i, rows_of(q)], chunk_sem.at[i, q]
        )
        for i, ref in enumerate((token_ref, low_ref))
        for q in range(blocks)
    ]

    def laid_out(slot, i):
        return jnp.concatenate([columns[slot, block_of(q * rows + i * 64, 64)] for q in range(blocks)], axis=1)


    own_load = pltpu.make_async_copy(low_ref, big.at[rows_of(0)], mixed_sem.at[0])
    own_load.start()
    for r in range(2):
        for k in range(4):
            given_copy(r, k).start()
    start(out_load)
    start(gated_load)
    start(gate_copies(0))
    start(gate_copies(1))
    start(feed_load)

    barrier = pltpu.get_barrier_semaphore()

    def partner(k):
        other = lax.rem(here + k, peers)
        return other, (lax.div(other, 4), lax.rem(other, 4))

    @pl.loop(1, peers)
    def _(k):
        pl.semaphore_signal(barrier, inc=1, device_id=partner(k)[1], device_id_type=MESH)

    pl.semaphore_wait(barrier, peers - 1)

    own_load.wait()
    start(over)
    for k in range(4):
        given_copy(0, k).wait()
        send_to_twin(0, k)
        if k > 0:
            settle(0, k - 1)
            push(0, k - 1)
    for k in range(4):
        given_copy(1, k).wait()
        send_to_twin(1, k)
        settle(*((1, k - 1) if k > 0 else (0, 3)))
    wait(out_load)
    settle(1, 3)
    pass_on(0, 0)
    push(1, 0)
    gate_back(0)
    start(gate_copies(2))
    wait_recv(over)
    start(onward)
    pass_on(0, 1)
    gate_back(1)
    start(gate_copies(3))
    push(1, 1)
    gate_back(2)
    pass_on(0, 2)
    pass_on(1, 0)
    push(1, 2)
    finish(0)
    wait_recv(onward)
    wait(feed_load)
    send_halves(0)
    send_plain(0, 0)
    send_plain(0, 1)
    wait(gated_load)
    multiply(2, 0)
    multiply(2, 1)
    pass_on(1, 2)
    settle(2, 0)
    push(2, 0)
    pass_on(1, 1)
    gate_back(3)
    prefetch(3)
    start(w_gate_load)
    settle(2, 1)
    multiply(2, 2)
    multiply(2, 3)
    start(w_value_load)
    settle(2, 2)
    push(2, 1)
    multiply(3, 0)
    finish(1)
    push(2, 2)
    settle(2, 3)
    multiply(3, 1)
    take_halves(0)
    settle(3, 0)
    pass_on(2, 0)
    multiply(3, 2)
    settle(3, 1)
    multiply(3, 3)
    start(chunk_copies(chunks - 1, 0))
    push(3, 0)
    wait_send(over + onward)
    state_ref[...] = jnp.zeros_like(state_ref)

    def between(step):
        @pl.when(step == 1)
        def _():
            pass_on(2, 2)
            pass_on(2, 1)
            settle(3, 2)

        @pl.when(step == 2)
        def _():
            push(3, 1)

    retention_steps(between)
    start(w_key_load)
    prefetch(4)
    settle(3, 3)
    multiply(4, 0)
    push(3, 2)
    pass_on(3, 0)
    finish(2)
    multiply(4, 1)
    wait_send(halves)
    wait(w_gate_load + w_value_load + w_key_load)
    project(3)
    send_halves(1)
    wait_recv(fulls)
    result_copy = pltpu.make_async_copy(full_in, result_ref, mixed_sem.at[1])
    result_copy.start()
    result_copy.wait()
    for i, side in enumerate(sides):
        pl.semaphore_signal(full_free.at[i], inc=1, device_id=side, device_id_type=MESH)
    wait_send(fulls)
    pass_on(3, 1)
    settle(4, 0)
    push(4, 0)
    pass_on(3, 2)
    multiply(4, 2)
    settle(4, 1)
    project(2)
    push(4, 1)
    settle(4, 2)
    project(1)
    pass_on(4, 0)
    send_plain(1, 0)
    send_plain(1, 1)
    multiply(4, 3)
    finish(3)
    push(4, 2)
    pass_on(4, 2)
    pass_on(4, 1)
    take_halves(1)
    settle(4, 3)
    multiply(5, 0)
    multiply(5, 1)
    settle(5, 0)
    push(5, 0)
    multiply(5, 2)
    settle(5, 1)
    settle(5, 2)
    finish(4)
    pass_on(5, 0)
    push(5, 1)
    multiply(5, 3)
    start(last_loads)
    wait_send(halves)
    project(0)
    pass_on(5, 1)
    pass_on(5, 2)
    push(5, 2)
    settle(5, 3)
    total[...] = jnp.zeros_like(total)
    wait(last_loads)

    def first_norm_back(i):
        place = block_of(i * 64, 64)
        normed_grad = terms[2, place].astype(f32) + full_in[0, place].astype(f32) + full_in[1, place].astype(f32)
        plain, scale = normalize(laid_out(0, i).astype(f32))
        grad = laid_out(1, i).astype(f32) + normalize_back(normed_grad, plain, scale, gain_ref[...])
        full_in[0, place] = grad.astype(bf16)
        total[0:1, :] += jnp.sum(normed_grad * plain, axis=0, keepdims=True)
        total[1:2, :] += jnp.sum(normed_grad, axis=0, keepdims=True)

    wait_recv(plain_parts + grown_parts[:2])
    pl.loop(0, quarter // 64)(first_norm_back)
    pl.loop(half // 64, (half + quarter) // 64)(first_norm_back)
    wait_recv(grown_parts[2:])
    pl.loop(quarter // 64, half // 64)(first_norm_back)
    pl.loop((half + quarter) // 64, rows // 64)(first_norm_back)
    grad_copy = pltpu.make_async_copy(full_in.at[0], grad_ref, mixed_sem.at[3])
    grad_copy.start()

    total[2:4, :] = late_ref[...]
    for k in range(peers // 2):
        given[k] = total[:, k * 128 : (k + 1) * 128]

    def sum_copy(k):
        other, device = partner(k)
        return remote(given.at[lax.div(other, 2)], landed.at[k], sum_send.at[k], sum_recv.at[k], device)

    @pl.loop(1, peers)
    def _(k):
        sum_copy(k).start()

    sums_ref[...] = given[lax.div(here, 2)]

    @pl.loop(1, peers)
    def _(k):
        sum_copy(k).wait()
        sums_ref[...] += landed[k]

    finish(5)

    wait_send(fulls)
    for r in (4, 5):
        for k in range(4):
            to_twin(r, k).wait_send()
            if k < 3:
                along(r, k, 0, end).wait_send()
    wait(outputs(4) + outputs(5))
    grad_copy.wait()


def cast_kernel(plus_ref, parts_ref, *refs):
    count = len(refs) // 2
    total = plus_ref[...].astype(f32) + parts_ref[0].astype(f32) + parts_ref[1].astype(f32)
    refs[count][...] = total.astype(bf16)
    for i, (source, target) in enumerate(zip(refs[:count], refs[count + 1 :])):
        value = source[...].astype(target.dtype)
        target[...] = value.T if i >= count - 2 else value


def cast_all(plus, parts, arrays):
    steps = 4

    def slab(rows, width):
        return pl.BlockSpec((rows // steps, width), lambda j: (j, 0))

    rows, width = plus.shape
    in_specs = [slab(rows, width), pl.BlockSpec((2, rows // steps, width), lambda j: (0, j, 0))]
    out_specs, shapes = [slab(rows, width)], [jax.ShapeDtypeStruct(plus.shape, bf16)]
    for i, v in enumerate(arrays):
        rows, width = v.shape
        if i >= len(arrays) - 2:
            in_specs.append(pl.BlockSpec((rows, width // steps), lambda j: (0, j)))
            out_specs.append(pl.BlockSpec((width // steps, rows), lambda j: (j, 0)))
            shapes.append(jax.ShapeDtypeStruct((width, rows), f32))
        else:
            in_specs.append(slab(rows, width))
            out_specs.append(slab(rows, width))
            shapes.append(jax.ShapeDtypeStruct((rows, width), bf16 if i == 0 else f32))
    return pl.pallas_call(
        cast_kernel,
        grid=(steps,),
        in_specs=in_specs,
        out_specs=out_specs,
        out_shape=shapes,
        compiler_params=pltpu.CompilerParams(vmem_limit_bytes=60 * 1024 * 1024),
        name="last_casts",
    )(plus, parts, *arrays)


def closing_exchange(heads, operands, small):
    token_rows, width = operands[-1].shape
    rows = 4 * token_rows
    depth = width // 8
    keys, values = heads * KEY, heads * VAL
    unit = operands[1].shape[1]
    anywhere = pl.BlockSpec(memory_space=pl.ANY)
    in_vmem = pl.BlockSpec(memory_space=pltpu.VMEM)
    sem = pltpu.SemaphoreType.DMA
    regular = pltpu.SemaphoreType.REGULAR
    vmem = pltpu.VMEM
    return pl.pallas_call(
        functools.partial(closing_kernel, heads),
        out_shape=[
            jax.ShapeDtypeStruct((2, token_rows, width), bf16),
            jax.ShapeDtypeStruct((token_rows, width), bf16),
            jax.ShapeDtypeStruct((depth, keys), bf16),
            jax.ShapeDtypeStruct((depth, keys), bf16),
            jax.ShapeDtypeStruct((depth, values), bf16),
            jax.ShapeDtypeStruct((depth, values), bf16),
            jax.ShapeDtypeStruct((depth, unit), bf16),
            jax.ShapeDtypeStruct((depth, unit), bf16),
            jax.ShapeDtypeStruct((depth, unit), bf16),
            jax.ShapeDtypeStruct((8, 128), f32),
        ],
        in_specs=[anywhere] * len(operands) + [in_vmem] * len(small),
        out_specs=[anywhere] * 9 + [in_vmem],
        scratch_shapes=[
            vmem((rows, width), bf16),
            vmem((4, rows, unit), bf16),
            vmem((2, rows, 2 * depth), bf16),
            vmem((3, token_rows, width), bf16),
            vmem((2, token_rows // 2, width), bf16),
            vmem((2, token_rows, width), bf16),
            vmem((2, 4, 2 * depth, unit), bf16),
            vmem((2, depth, unit), bf16),
            vmem((5, depth, unit), bf16),
            vmem((heads, KEY, VAL), f32),
            vmem((2, heads, KEY, VAL), bf16),
            vmem((2, token_rows, 128), f32),
            vmem((2, CHUNK, KEY), f32),
            vmem((2, CHUNK, 128), f32),
            vmem((16, 8, 128), f32),
            vmem((32, 8, 128), f32),
            vmem((8, width), f32),
            sem((10,)), sem((8,)), sem((2, 12)), sem((2, 2)), sem((4,)),
            sem((2,)), sem((2,)), sem((2,)), sem((2,)),
            sem((2,)), sem((2,)), sem((6,)), sem((6,)),
            sem((2, 4)), sem((2,)), sem((2, 3)), sem((5,)), sem((32,)), sem((32,)),
            regular((2,)), regular((3,)), regular((2,)), regular((2,)),
        ],
        compiler_params=pltpu.CompilerParams(
            collective_id=3, has_side_effects=True, vmem_limit_bytes=63_400_000
        ),
        name="closing_exchange",
    )(*operands, *small)


def body(tokens, cotangent, segment, first_gain, first_bias, query_weight, key_weight, value_weight, gate_weight, out_weight, second_gain, second_bias, up_weight, down_weight):
    devices = lax.axis_size("tensor")
    rows = tokens.shape[0]
    heads = query_weight.shape[1] // KEY
    here = lax.axis_index("tensor")
    which = (here if devices == 4 else jnp.zeros_like(here)).astype(jnp.int32).reshape(1)

    def per_piece(values):
        return [values[i * rows : (i + 1) * rows] for i in range(devices)]

    if devices == 4 and lax.axis_size("dp") == 8:
        shards = (query_weight, key_weight, value_weight, gate_weight, out_weight, down_weight)
        opened, keys = opening_exchange(heads, shards, tokens, cotangent, segment, first_gain, first_bias)
        w_qkv, w_gate, w_out, normed1_all, cot_all, field, gate, gated, grouped, group_scale, past = opened[:11]
        angles, info, decay, down_shard = opened[11:]
        mixed_low, plus, feed_terms, up_weight_grad, down_weight_grad, late = middle_exchange(
            gated, w_out, up_weight, down_shard, cot_all, tokens, second_gain, second_bias
        )
        parts, input_grad, query_sum, key_sum, value_sum, gate_sum, out_sum, up_sum, down_sum, sums = closing_exchange(
            heads,
            (
                normed1_all, up_weight_grad, down_weight_grad, feed_terms, w_out, w_qkv, w_gate,
                gate, grouped, gated, group_scale, field, past, angles, info,
                mixed_low, tokens,
            ),
            (keys, decay, first_gain.reshape(1, -1), late),
        )
        part = first_gain.shape[0] // 32
        sums = lax.dynamic_slice_in_dim(sums, (here % 2) * part, part, 1)
        norm_sums = [sums[0], sums[1], sums[2], sums[3]]
        result, input_grad, query_sum, key_sum, value_sum, gate_sum, up_sum, out_sum, down_sum = cast_all(
            plus, parts, (input_grad, query_sum, key_sum, value_sum, gate_sum, up_sum, out_sum, down_sum)
        )
    else:
        w_qkv = lax.all_gather(
            jnp.concatenate([query_weight, key_weight, value_weight], axis=1), "dp", axis=0, tiled=True
        )
        w_gate = lax.all_gather(gate_weight, "dp", axis=0, tiled=True)
        w_out = lax.all_gather(out_weight, "dp", axis=1, tiled=True)
        token_rows = tokens.astype(f32)
        unit1, scale1 = normalize(token_rows)
        normed1_all = jnp.concatenate(
            gather_pieces((unit1 * first_gain + first_bias).astype(bf16), devices), axis=0
        )
        cot_all = jnp.concatenate(gather_pieces(cotangent, devices), axis=0)
        tables = retention_tables(segment, heads, here * heads)
        field = dot_nn(normed1_all, w_qkv).astype(bf16)
        gate = dot_nn(normed1_all, w_gate).astype(bf16)
        gated, grouped, group_scale, past = retention_call(False, which, rows, heads, field, gate, tables, ())
        w_down = lax.all_gather(after(down_weight, w_out), "dp", axis=1, tiled=True)
        w_up = lax.all_gather(after(up_weight, w_down), "dp", axis=0, tiled=True)
        branch, begun, _ = scatter_sum([dot_nn(piece, w_out) for piece in per_piece(gated)])

        mixed = token_rows + branch
        unit2, scale2 = normalize(mixed)
        normed2 = (unit2 * second_gain + second_bias).astype(bf16)
        hidden_grads = per_piece(dot_nt(cot_all, after(w_down, normed2)).astype(bf16))

        def feed(piece, hidden_grad):
            value, slope = gelu_both(dot_nn(piece, w_up))
            return after((value.astype(bf16), (hidden_grad.astype(f32) * slope).astype(bf16)))

        fed_own = feed(normed2, hidden_grads[0])
        normed2_pieces = gather_pieces(normed2, devices, fed_own)
        fed = [fed_own] + [feed(piece, grad) for piece, grad in zip(normed2_pieces[1:-1], hidden_grads[1:-1])]
        fed.append(feed(after(normed2_pieces[-1], *fed), hidden_grads[-1]))
        hidden = [f[0] for f in fed]
        up_grad = [f[1] for f in fed]
        terms = [dot_nt(piece, w_up) for piece in up_grad]
        normed2_grad, _, _ = scatter_sum(terms)
        mixed_grad = cotangent.astype(f32) + normalize_back(normed2_grad, unit2, scale2, second_gain)
        gain2_grad = jnp.sum(normed2_grad * unit2, axis=0)
        bias2_grad = jnp.sum(normed2_grad, axis=0)
        mixed_low = mixed_grad.astype(bf16)
        hidden_all = jnp.concatenate(after(hidden, *terms), axis=0)
        normed2_all = jnp.concatenate(after(normed2_pieces, *terms), axis=0)
        up_grad_all = jnp.concatenate(after(up_grad, *terms), axis=0)
        feed_terms = dot_nn(hidden_all, w_down).astype(bf16)
        own_term = feed_terms[:rows].astype(f32)
        up_weight_grad = dot_tn(normed2_all, up_grad_all).astype(bf16)
        down_weight_grad = dot_tn(cot_all, hidden_all).astype(bf16)

        def summed(gradient, dimension):
            return lax.psum_scatter(
                gradient.astype(bf16), "dp", scatter_dimension=dimension, tiled=True
            ).astype(f32)

        up_sum = summed(up_weight_grad, 0)
        down_sum = summed(down_weight_grad, 0).T
        mixed_all = jnp.concatenate(gather_pieces(mixed_low, devices), axis=0)
        ffn, _, _ = scatter_sum([term.astype(f32) for term in per_piece(feed_terms)])
        result = (mixed + ffn).astype(bf16)
        gated_grad = dot_nt(mixed_all, w_out)
        raw = gate.astype(f32)
        sigmoid = 1.0 / (1.0 + jnp.exp(-raw))
        gate_grad = (gated_grad * grouped.astype(f32) * (sigmoid * (1.0 + raw * (1.0 - sigmoid)))).astype(bf16)
        back = retention_call(
            True, which, rows, heads, field, gate, tables, (gated_grad.astype(bf16), grouped, group_scale, past)
        )
        gate_sum = summed(dot_tn(normed1_all, gate_grad), 0)
        out_sum = summed(dot_tn(gated, mixed_all), 1)
        qkv_sum = summed(dot_tn(normed1_all, back), 0)
        keys_end = heads * KEY
        query_sum = qkv_sum[:, :keys_end]
        key_sum = qkv_sum[:, keys_end : 2 * keys_end]
        value_sum = qkv_sum[:, 2 * keys_end :]
        terms = [
            dot_nt(first, w_qkv) + dot_nt(second, w_gate) for first, second in zip(per_piece(back), per_piece(gate_grad))
        ]
        normed1_grad, _, _ = scatter_sum(terms)
        input_grad = (mixed_grad + normalize_back(normed1_grad, unit1, scale1, first_gain)).astype(bf16)
        gain1_grad = jnp.sum(normed1_grad * unit1, axis=0)
        bias1_grad = jnp.sum(normed1_grad, axis=0)
        norm_sums = spread_sum([gain1_grad, bias1_grad, gain2_grad, bias2_grad])
    return (
        result,
        input_grad,
        norm_sums[0],
        norm_sums[1],
        query_sum,
        key_sum,
        value_sum,
        gate_sum,
        out_sum,
        norm_sums[2],
        norm_sums[3],
        up_sum,
        down_sum,
    )


def solution(mesh):
    rows = P(("dp", "tensor"), None)
    vector = P(("dp", "tensor"))
    into = P("dp", "tensor")
    back = P("tensor", "dp")
    return jax.shard_map(
        body,
        mesh=mesh,
        in_specs=(rows, rows, P("dp"), P(), P(), into, into, into, into, back, P(), P(), into, back),
        out_specs=(rows, rows, vector, vector, into, into, into, into, back, vector, vector, into, back),
        check_vma=False,
    )
```

```python
import functools

import jax
import jax.numpy as jnp
from jax import lax
from jax.experimental import pallas as pl
from jax.experimental.pallas import tpu as pltpu
from jax.sharding import PartitionSpec as P

KEY = 256
VAL = 512
CHUNK = 256
QKV = 2 * KEY + VAL

norm_epsilon = 1e-05
group_floor = 0.5
key_scale = KEY ** (-0.5)

f32 = jnp.float32
bf16 = jnp.bfloat16


def dot_nn(left, right):
    return lax.dot_general(left, right, (((1,), (0,)), ((), ())), preferred_element_type=f32)


def dot_nt(left, right):
    return lax.dot_general(left, right, (((1,), (1,)), ((), ())), preferred_element_type=f32)


def dot_tn(left, right):
    return lax.dot_general(left, right, (((0,), (0,)), ((), ())), preferred_element_type=f32)


def tensor_permute(values, bit):
    pairs = [(i, i ^ bit) for i in range(4)]
    return lax.ppermute(values, "tensor", pairs)


def after(values, *tokens):
    return lax.optimization_barrier((values, tokens))[0]


def gather_pieces(own, devices, between=()):
    if devices != 4:
        whole = lax.all_gather(own, "tensor", axis=0, tiled=True)
        return list(jnp.split(whole, devices, axis=0))
    half = own.shape[0] // 2
    from_x = tensor_permute(own, 1)
    from_y = tensor_permute(own, 2)
    lower, upper = after((from_y[:half], from_x[half:]), *between)
    lower = tensor_permute(lower, 1)
    upper = tensor_permute(upper, 2)
    return [own, from_x, from_y, jnp.concatenate([lower, upper], axis=0)]


def scatter_sum(terms):
    if len(terms) != 4:
        stacked = jnp.concatenate([term.astype(bf16) for term in terms], axis=0)
        return lax.psum_scatter(stacked, "tensor", scatter_dimension=0, tiled=True).astype(f32), (stacked,), (stacked,)
    own, over_x, over_y, across = terms
    half = own.shape[0] // 2
    across = across.astype(bf16)
    first = tensor_permute(across[:half], 1)
    second = tensor_permute(across[half:], 2)
    over_y = jnp.concatenate([over_y[:half] + first.astype(f32), over_y[half:]], axis=0)
    over_x = jnp.concatenate([over_x[:half], over_x[half:] + second.astype(f32)], axis=0)
    by_x = tensor_permute(over_x.astype(bf16), 1)
    by_y = tensor_permute(over_y.astype(bf16), 2)
    return own + by_x.astype(f32) + by_y.astype(f32), (first, second), (by_x, by_y)


def spread_sum_kernel(tensor_devices, devices, given_ref, sum_ref, landed_ref, send_sem, recv_sem):
    here = lax.axis_index("dp") * tensor_devices + lax.axis_index("tensor")

    def partner(k):
        other = lax.rem(here + k, devices)
        return other, (lax.div(other, tensor_devices), lax.rem(other, tensor_devices))

    def copy(k):
        other, device = partner(k)
        return pltpu.make_async_remote_copy(
            src_ref=given_ref.at[other],
            dst_ref=landed_ref.at[k],
            send_sem=send_sem.at[k],
            recv_sem=recv_sem.at[k],
            device_id=device,
            device_id_type=pl.DeviceIdType.MESH,
        )

    barrier = pltpu.get_barrier_semaphore()

    @pl.loop(1, devices)
    def _(k):
        pl.semaphore_signal(barrier, inc=1, device_id=partner(k)[1], device_id_type=pl.DeviceIdType.MESH)

    pl.semaphore_wait(barrier, devices - 1)

    @pl.loop(1, devices)
    def _(k):
        copy(k).start()

    sum_ref[...] = given_ref[here]

    @pl.loop(1, devices)
    def _(k):
        copy(k).wait()
        sum_ref[...] += landed_ref[k]


def spread_sum(vectors):
    dp, tensor = lax.axis_size("dp"), lax.axis_size("tensor")
    devices = dp * tensor
    part = vectors[0].shape[0] // devices
    given = jnp.stack([v.reshape(devices, part) for v in vectors], axis=1)
    given = jnp.pad(given, ((0, 0), (0, 8 - len(vectors)), (0, 128 - part)))
    total = pl.pallas_call(
        functools.partial(spread_sum_kernel, tensor, devices),
        out_shape=jax.ShapeDtypeStruct((8, 128), f32),
        in_specs=[pl.BlockSpec(memory_space=pltpu.VMEM)],
        out_specs=pl.BlockSpec(memory_space=pltpu.VMEM),
        scratch_shapes=[
            pltpu.VMEM((devices, 8, 128), f32),
            pltpu.SemaphoreType.DMA((devices,)),
            pltpu.SemaphoreType.DMA((devices,)),
        ],
        compiler_params=pltpu.CompilerParams(collective_id=1, has_side_effects=True),
        name="spread_sum",
    )(given)
    return [total[i, :part] for i in range(len(vectors))]


def normalize(values):
    average = jnp.mean(values, axis=-1, keepdims=True)
    centred = values - average
    variance = jnp.mean(centred * centred, axis=-1, keepdims=True)
    scale = lax.rsqrt(variance + norm_epsilon)
    return centred * scale, scale


def normalize_back(normed_grad, unit, scale, gain):
    g = normed_grad * gain
    mean_g = jnp.mean(g, axis=-1, keepdims=True)
    mean_gx = jnp.mean(g * unit, axis=-1, keepdims=True)
    return scale * (g - mean_g - unit * mean_gx)


def gelu_both(values):
    inner = 0.7978845608 * (values + 0.044715 * values * values * values)
    t = jnp.tanh(inner)
    slope = 0.7978845608 * (1.0 + 3.0 * 0.044715 * values * values)
    return 0.5 * values * (1.0 + t), 0.5 * (1.0 + t) + 0.5 * values * (1.0 - t * t) * slope


def turn(block, cosine, sine):
    a = block[:, : KEY // 2]
    b = block[:, KEY // 2 :]
    return jnp.concatenate([a * cosine - b * sine, b * cosine + a * sine], axis=1)


def turn_back(block, cosine, sine):
    a = block[:, : KEY // 2]
    b = block[:, KEY // 2 :]
    return jnp.concatenate([a * cosine + b * sine, b * cosine - a * sine], axis=1)


def head_parts(field_ref, angles, heads, head):
    cosine = angles[:, : KEY // 2]
    sine = angles[:, KEY // 2 :]
    query_at = head * KEY
    key_at = (heads + head) * KEY
    value_at = 2 * heads * KEY + head * VAL
    query = turn(field_ref[:, query_at : query_at + KEY].astype(f32), cosine, sine).astype(bf16)
    key = turn(field_ref[:, key_at : key_at + KEY].astype(f32), cosine, sine)
    key = (key * key_scale).astype(bf16)
    return query, key, field_ref[:, value_at : value_at + VAL]


def retention_forward(heads, which, field_ref, gate_ref, angle_ref, info_ref, row_ref, decay_ref, gated_ref, grouped_ref, scale_ref, past_ref, state_ref):
    @pl.when(pl.program_id(0) == 0)
    def _():
        state_ref[...] = jnp.zeros_like(state_ref)

    angles = angle_ref[...]
    info = info_ref[...]
    same = info[:, 0:1] == row_ref[0]
    scales = []
    for head in range(heads):
        query, key, value = head_parts(field_ref, angles, heads, head)
        columns = slice(head * VAL, (head + 1) * VAL)
        gate = gate_ref[:, columns].astype(f32)
        into = info[:, 1 + 2 * head : 2 + 2 * head]
        onward = info[:, 2 + 2 * head : 3 + 2 * head]
        state = state_ref[head]
        past_ref[0, head] = state.astype(bf16)
        scores = dot_nt(query, key)
        weights = (jnp.where(same, decay_ref[head], 0.0) * scores).astype(bf16)
        retained = dot_nn(weights, value) + into * dot_nn(query, state.astype(bf16))
        moved = (key.astype(f32) * onward).astype(bf16)
        state_ref[head] = into[CHUNK - 1 :, :] * state + dot_tn(moved, value)
        centred = retained - jnp.mean(retained, axis=-1, keepdims=True)
        scale = lax.rsqrt(jnp.mean(centred * centred, axis=-1, keepdims=True) + group_floor)
        grouped = centred * scale
        gated = gate / (1.0 + jnp.exp(-gate)) * grouped
        gated_ref[:, columns] = gated.astype(bf16)
        grouped_ref[:, columns] = grouped.astype(bf16)
        scales.append(scale)
    lane = lax.broadcasted_iota(jnp.int32, (CHUNK, 128), 1)
    spread = jnp.zeros((CHUNK, 128), f32)
    for head in range(heads):
        spread = jnp.where(lane == head, scales[head], spread)
    scale_ref[...] = spread


def retention_backward(heads, which, field_ref, gate_ref, angle_ref, info_ref, row_ref, decay_ref, grad_ref, grouped_ref, scale_ref, past_ref, back_ref, state_ref):
    @pl.when(pl.program_id(0) == 0)
    def _():
        state_ref[...] = jnp.zeros_like(state_ref)

    angles = angle_ref[...]
    cosine = angles[:, : KEY // 2]
    sine = angles[:, KEY // 2 :]
    info = info_ref[...]
    same = info[:, 0:1] == row_ref[0]
    for head in range(heads):
        query, key, value = head_parts(field_ref, angles, heads, head)
        columns = slice(head * VAL, (head + 1) * VAL)
        gate = gate_ref[:, columns].astype(f32)
        into = info[:, 1 + 2 * head : 2 + 2 * head]
        onward = info[:, 2 + 2 * head : 3 + 2 * head]
        grouped = grouped_ref[:, columns].astype(f32)
        scale = scale_ref[:, head : head + 1]
        c = grad_ref[:, columns].astype(f32) * (gate / (1.0 + jnp.exp(-gate)))
        mean_c = jnp.mean(c, axis=-1, keepdims=True)
        mean_cx = jnp.mean(c * grouped, axis=-1, keepdims=True)
        out_grad = (scale * (c - mean_c - grouped * mean_cx)).astype(bf16)
        state = state_ref[head]
        state_low = state.astype(bf16)
        past = past_ref[0, head]
        masked = jnp.where(same, decay_ref[head], 0.0)
        weights = (masked * dot_nt(query, key)).astype(bf16)
        score_grad = (masked * dot_nt(out_grad, value)).astype(bf16)
        value_grad = dot_tn(weights, out_grad) + onward * dot_nn(key, state_low)
        query_grad = dot_nn(score_grad, key) + into * dot_nt(out_grad, past)
        key_grad = dot_tn(score_grad, query) + onward * dot_nt(value, state_low)
        moved = (query.astype(f32) * into).astype(bf16)
        state_ref[head] = into[CHUNK - 1 :, :] * state + dot_tn(moved, out_grad)
        query_at = head * KEY
        key_at = (heads + head) * KEY
        value_at = 2 * heads * KEY + head * VAL
        back_ref[:, query_at : query_at + KEY] = turn_back(query_grad, cosine, sine).astype(bf16)
        back_ref[:, key_at : key_at + KEY] = (turn_back(key_grad, cosine, sine) * key_scale).astype(bf16)
        back_ref[:, value_at : value_at + VAL] = value_grad.astype(bf16)


def retention_tables(segment, heads, first_head):
    rows = segment.shape[0]
    chunks = rows // CHUNK
    index = jnp.arange(rows, dtype=jnp.int32)
    boundary = jnp.concatenate([jnp.ones((1,), jnp.int32), (segment[1:] != segment[:-1]).astype(jnp.int32)])
    position = index - lax.cummax(jnp.where(boundary > 0, index, 0), axis=0)
    half = KEY // 2
    frequency = jnp.exp(-jnp.log(10000.0) * jnp.arange(half, dtype=f32) / half)
    angles = position.astype(f32)[:, None] * frequency[None, :]
    angles = jnp.concatenate([jnp.cos(angles), jnp.sin(angles)], axis=1)
    head_ids = (first_head + jnp.arange(heads, dtype=jnp.int32)).astype(f32)
    log_decay = jnp.log1p(-jnp.exp2(-5.0 - head_ids))
    last = segment.reshape(chunks, CHUNK)[:, -1]
    before = jnp.concatenate([jnp.full((1,), -2, jnp.int32), last[:-1]])
    offset = (index % CHUNK).astype(f32)
    linked_in = (segment == jnp.repeat(before, CHUNK)) & (segment >= 0)
    linked_on = (segment == jnp.repeat(last, CHUNK)) & (segment >= 0)
    columns = [segment.astype(f32)]
    for head in range(heads):
        columns.append(jnp.where(linked_in, jnp.exp(log_decay[head] * (offset + 1.0)), 0.0))
        columns.append(jnp.where(linked_on, jnp.exp(log_decay[head] * (CHUNK - 1.0 - offset)), 0.0))
    info = jnp.stack(columns, axis=1)
    info = jnp.pad(info, ((0, 0), (0, 128 - info.shape[1])))
    keys = jnp.where(segment >= 0, segment, -7).astype(f32).reshape(chunks, 1, CHUNK)
    distance = (jnp.arange(CHUNK)[:, None] - jnp.arange(CHUNK)[None, :]).astype(f32)
    decay = jnp.where(distance >= 0, jnp.exp(log_decay[:, None, None] * jnp.maximum(distance, 0.0)), 0.0)
    return angles, info, keys, decay


def retention_call(backward, which, piece_rows, heads, field, gate, tables, extra):
    rows = field.shape[0]
    chunks = rows // CHUNK
    angles, info, keys, decay = tables
    per_piece = piece_rows // CHUNK

    def step(i):
        return chunks - 1 - i if backward else i

    def place(i, which_ref):
        c = step(i)
        return ((c // per_piece) ^ which_ref[0]) * per_piece + c % per_piece

    def placed(width):
        return pl.BlockSpec((CHUNK, width), lambda i, w: (place(i, w), 0))

    in_specs = [
        placed(heads * QKV),
        placed(heads * VAL),
        pl.BlockSpec((CHUNK, KEY), lambda i, w: (step(i), 0)),
        pl.BlockSpec((CHUNK, 128), lambda i, w: (step(i), 0)),
        pl.BlockSpec((1, 1, CHUNK), lambda i, w: (step(i), 0, 0)),
        pl.BlockSpec((heads, CHUNK, CHUNK), lambda i, w: (0, 0, 0)),
    ]
    past_spec = pl.BlockSpec((1, heads, KEY, VAL), lambda i, w: (step(i), 0, 0, 0))
    if backward:
        in_specs += [placed(heads * VAL), placed(heads * VAL), placed(128), past_spec]
        out_specs = placed(heads * QKV)
        out_shape = jax.ShapeDtypeStruct((rows, heads * QKV), bf16)
    else:
        out_specs = [placed(heads * VAL), placed(heads * VAL), placed(128), past_spec]
        out_shape = [
            jax.ShapeDtypeStruct((rows, heads * VAL), bf16),
            jax.ShapeDtypeStruct((rows, heads * VAL), bf16),
            jax.ShapeDtypeStruct((rows, 128), f32),
            jax.ShapeDtypeStruct((chunks, heads, KEY, VAL), bf16),
        ]
    products = 15 if backward else 7
    return pl.pallas_call(
        functools.partial(retention_backward if backward else retention_forward, heads),
        grid_spec=pltpu.PrefetchScalarGridSpec(
            num_scalar_prefetch=1,
            grid=(chunks,),
            in_specs=in_specs,
            out_specs=out_specs,
            scratch_shapes=[pltpu.VMEM((heads, KEY, VAL), f32)],
        ),
        out_shape=out_shape,
        compiler_params=pltpu.CompilerParams(
            dimension_semantics=("arbitrary",), vmem_limit_bytes=48 * 1024 * 1024
        ),
        cost_estimate=pl.CostEstimate(
            flops=products * chunks * heads * 2 * CHUNK * CHUNK * CHUNK,
            bytes_accessed=(5 if backward else 4) * rows * heads * (QKV + VAL),
            transcendentals=rows * heads * VAL,
        ),
        name="retention_backward" if backward else "retention_forward",
    )(which, field, gate, angles, info, keys, decay, *extra)


MESH = pl.DeviceIdType.MESH


def opening_kernel(
    heads, query_ref, key_ref, value_ref, gate_ref, out_ref, down_ref, token_ref, cot_ref, row_ref, rate_ref, gain_ref, bias_ref,
    w_qkv_ref, w_gate_ref, w_out_ref, normed_ref, cot_all_ref, field_ref, gate_raw_ref, gated_ref, grouped_ref, scale_ref, past_ref,
    angle_ref, info_ref, decay_ref, down_turned_ref,
    w_qkv, w_gate, w_out, tall, normed, product, angles, info, decay, state, field_out, gate_out, gated_out, grouped_out,
    scale_out, past_out,
    local_sem, token_sem, out_sem, stage_sem, table_sem, up_send, up_recv, down_send, down_recv, core_send, core_recv,
    row_send, row_recv,
):
    dp = lax.axis_index("dp")
    tensor = lax.axis_index("tensor")
    z = lax.div(dp, 2)
    layers = 4
    depth = query_ref.shape[0]
    rows, width = token_ref.shape
    half = rows // 2
    above = (dp + 2, tensor)
    below = (dp - 2, tensor)
    twin = (dp + 1 - 2 * lax.rem(dp, 2), tensor)
    over_x = (dp, tensor + 1 - 2 * lax.rem(tensor, 2))
    over_y = (dp, lax.rem(tensor + 2, 4))
    keys = heads * KEY
    values = heads * VAL

    def block_of(start, count):
        return pl.ds(pl.multiple_of(start, count), count)

    def start(copies):
        for copy in copies:
            copy.start()

    def wait(copies):
        for copy in copies:
            copy.wait()

    def remote(src, dst, send, recv, device):
        return pltpu.make_async_remote_copy(
            src_ref=src, dst_ref=dst, send_sem=send, recv_sem=recv, device_id=device, device_id_type=MESH
        )

    mine = block_of(dp * depth, depth)
    local = [
        pltpu.make_async_copy(src, dst, local_sem.at[i])
        for i, (src, dst) in enumerate((
            (query_ref, w_qkv.at[mine, pl.ds(0, keys)]),
            (key_ref, w_qkv.at[mine, pl.ds(keys, keys)]),
            (value_ref, w_qkv.at[mine, pl.ds(2 * keys, values)]),
            (gate_ref, w_gate.at[mine]),
            (out_ref, tall),
        ))
    ]
    start(local)

    half_width = width // 2
    token_loads = [
        pltpu.make_async_copy(token_ref.at[pl.ds(0, half)], field_out, token_sem.at[0]),
        pltpu.make_async_copy(token_ref.at[pl.ds(half, half), pl.ds(0, half_width)], gated_out, token_sem.at[1]),
        pltpu.make_async_copy(token_ref.at[pl.ds(half, half), pl.ds(half_width, half_width)], grouped_out, token_sem.at[2]),
    ]
    start(token_loads)
    own_cot = pltpu.make_async_copy(cot_ref, cot_all_ref.at[pl.ds(0, rows)], local_sem.at[6])
    own_cot.start()

    barrier = pltpu.get_barrier_semaphore()

    def greet(device):
        pl.semaphore_signal(barrier, inc=1, device_id=device, device_id_type=MESH)

    for device in (twin, over_x, over_y):
        greet(device)
    pl.when(z < layers - 1)(lambda: greet(above))
    pl.when(z > 0)(lambda: greet(below))
    pl.semaphore_wait(barrier, 3 + (z < layers - 1).astype(jnp.int32) + (z > 0).astype(jnp.int32))
    wait(local[:4])


    groups = ((w_qkv, w_gate), (w_out,))

    def shard_copies(g, shard, send_sem, recv_sem, index, device):
        place = block_of(shard * depth, depth)
        return [
            remote(ref.at[place], ref.at[place], send_sem.at[index, i + 2 * g], recv_sem.at[index, i + 2 * g], device)
            for i, ref in enumerate(groups[g])
        ]

    def rise(g, j):
        return shard_copies(g, dp - 2 * j, up_send, up_recv, j, above)

    def sink(g, j):
        return shard_copies(g, dp + 2 * j, down_send, down_recv, j, below)

    def to_twin(g, j):
        return shard_copies(g, dp + 2 * j, core_send, core_recv, j + 3, twin)

    def from_twin(g, j):
        return shard_copies(g, twin[0] + 2 * j, core_send, core_recv, j + 3, twin)

    def wait_recv(copies):
        for copy in copies:
            copy.wait_recv()

    def wait_send(copies):
        for copy in copies:
            copy.wait_send()

    def first_step(g):
        pl.when(z < layers - 1)(lambda: start(rise(g, 0)))
        pl.when(z > 0)(lambda: start(sink(g, 0)))
        start(to_twin(g, 0))

    def step(g, j):
        @pl.when(z - j >= 0)
        def _():
            wait_recv(shard_copies(g, dp - 2 * j, up_send, up_recv, j - 1, twin))
            if j < 3:
                pl.when(z < layers - 1)(lambda: start(rise(g, j)))
            start(to_twin(g, -j))

        @pl.when(z + j < layers)
        def _():
            wait_recv(shard_copies(g, dp + 2 * j, down_send, down_recv, j - 1, twin))
            if j < 3:
                pl.when(z > 0)(lambda: start(sink(g, j)))
            start(to_twin(g, j))

    def when_end(wanted, work):
        pl.when(((z == 0) | (z == 3)) == wanted)(work)

    def twin_step(g, j):
        for signed in sorted({-j, j}):
            @pl.when((z + signed >= 0) & (z + signed < layers))
            def _():
                wait_recv(from_twin(g, signed))

    def rows_of(r, first=0, count=rows):
        return pl.ds(r * rows + first, count)

    def row_copy(index, src, dst, device):
        return remote(src, dst, row_send.at[index], row_recv.at[index], device)

    piece = 64
    cot_early = [
        row_copy(8, cot_ref.at[pl.ds(0, piece)], cot_all_ref.at[rows_of(1, 0, piece)], over_x),
        row_copy(9, cot_ref.at[pl.ds(0, piece)], cot_all_ref.at[rows_of(2, 0, piece)], over_y),
    ]
    cot_over = [
        row_copy(4, cot_ref.at[pl.ds(piece, rows - piece)], cot_all_ref.at[rows_of(1, piece, rows - piece)], over_x),
        row_copy(5, cot_ref.at[pl.ds(piece, rows - piece)], cot_all_ref.at[rows_of(2, piece, rows - piece)], over_y),
    ]

    first_step(0)
    start(cot_early)

    wait(token_loads)

    @pl.loop(0, half // 64)
    def _(i):
        place = block_of(i * 64, 64)
        plain, _ = normalize(field_out[place].astype(f32))
        normed[place] = (plain * gain_ref[...] + bias_ref[...]).astype(bf16)

    @pl.loop(0, half // 64)
    def _(i):
        place = block_of(i * 64, 64)
        both = jnp.concatenate([gated_out[place], grouped_out[place]], axis=1)
        plain, _ = normalize(both.astype(f32))
        normed[block_of(half + i * 64, 64)] = (plain * gain_ref[...] + bias_ref[...]).astype(bf16)

    over = [
        row_copy(0, normed.at[rows_of(0)], normed.at[rows_of(1)], over_x),
        row_copy(1, normed.at[rows_of(0)], normed.at[rows_of(2)], over_y),
    ]
    onward = [
        row_copy(2, normed.at[rows_of(2, 0, half)], normed.at[rows_of(3, 0, half)], over_x),
        row_copy(3, normed.at[rows_of(1, half, half)], normed.at[rows_of(3, half, half)], over_y),
    ]
    cot_onward = [
        row_copy(6, cot_all_ref.at[rows_of(2, 0, half)], cot_all_ref.at[rows_of(3, 0, half)], over_x),
        row_copy(7, cot_all_ref.at[rows_of(1, half, half)], cot_all_ref.at[rows_of(3, half, half)], over_y),
    ]
    start(over)

    local[4].wait()
    w_out[mine, :] = tall[...].T
    down_load = pltpu.make_async_copy(down_ref, tall, local_sem.at[4])
    down_load.start()

    half_key = KEY // 2
    lanes = lax.broadcasted_iota(jnp.int32, (CHUNK, half_key), 1).astype(f32)
    frequency = jnp.exp(lanes * (-9.210340371976184 / half_key))
    chunks = 4 * rows // CHUNK

    @pl.loop(0, chunks)
    def _(c):
        seat = block_of(c * CHUNK, CHUNK)
        diagonal = lax.broadcasted_iota(jnp.int32, (CHUNK, CHUNK), 0) == lax.broadcasted_iota(jnp.int32, (CHUNK, CHUNK), 1)
        own = jnp.sum(jnp.where(diagonal, jnp.maximum(row_ref[c], -1.0), 0.0), axis=1, keepdims=True)
        info[seat, :] = jnp.broadcast_to(own, (CHUNK, 128))
        ranked = jnp.where(own < 0, 3.0, own)
        before = jnp.zeros((CHUNK, 1), f32)
        for other in range(chunks):
            seen = row_ref[other]
            seen = jnp.where(seen < 0, 3.0, seen)
            before = before + jnp.sum((seen < ranked).astype(f32), axis=1, keepdims=True)
        index = lax.broadcasted_iota(jnp.int32, (CHUNK, 1), 0) + c * CHUNK
        turned = (index.astype(f32) - before) * frequency
        angles[seat, 0:half_key] = jnp.cos(turned)
        angles[seat, half_key:KEY] = jnp.sin(turned)

    distance = lax.broadcasted_iota(jnp.int32, (CHUNK, CHUNK), 0) - lax.broadcasted_iota(jnp.int32, (CHUNK, CHUNK), 1)
    span = jnp.maximum(distance, 0).astype(f32)
    for head in range(heads):
        decay[head] = jnp.where(distance >= 0, jnp.exp(rate_ref[head : head + 1, 0:1] * span), 0.0)
    down_load.wait()
    gate_out[...] = tall[...].T
    table_outs = [
        pltpu.make_async_copy(gate_out, down_turned_ref, table_sem.at[3]),
        pltpu.make_async_copy(angles, angle_ref, table_sem.at[0]),
        pltpu.make_async_copy(decay, decay_ref, table_sem.at[1]),
    ]
    start(table_outs)


    at_end = (z == 0) | (z == 3)

    def seen_from_end(index):
        return jnp.where(z >= 2, 3 - index, index)

    order = [z, jnp.where(at_end, seen_from_end(1), seen_from_end(0)), seen_from_end(2), seen_from_end(3)]

    def project(r, s):
        deep = block_of(order[s] * 2 * depth, 2 * depth)

        @pl.loop(0, (2 * keys + values) // 512)
        def _(j):
            tile = block_of(j * 512, 512)
            more = dot_nn(normed[rows_of(r), deep], w_qkv[deep, tile])
            product[rows_of(r), tile] = more if s == 0 else product[rows_of(r), tile] + more

        @pl.loop(0, values // 512)
        def _(j):
            tile = block_of(j * 512, 512)
            more = dot_nn(normed[rows_of(r), deep], w_gate[deep, tile])
            place = block_of(2 * keys + values + j * 512, 512)
            product[rows_of(r), place] = more if s == 0 else product[rows_of(r), place] + more


    per_piece = rows // CHUNK

    def chunk_place(c):
        piece = lax.div(c, per_piece)
        low = lax.rem(lax.rem(piece, 2) + lax.rem(tensor, 2), 2)
        high = lax.rem(lax.div(piece, 2) + lax.div(tensor, 2), 2)
        return (2 * high + low) * per_piece + lax.rem(c, per_piece)

    def chunk_outs(c):
        place = block_of(chunk_place(c) * CHUNK, CHUNK)
        pairs = (
            (field_out, field_ref.at[place]),
            (gate_out, gate_raw_ref.at[place]),
            (gated_out, gated_ref.at[place]),
            (grouped_out, grouped_ref.at[place]),
            (scale_out, scale_ref.at[place]),
            (past_out, past_ref.at[c]),
        )
        return [pltpu.make_async_copy(src, dst, stage_sem.at[i]) for i, (src, dst) in enumerate(pairs)]

    def retention(between):
        state[...] = jnp.zeros_like(state)

        @pl.loop(0, chunks)
        def _(c):
            place = block_of(chunk_place(c) * CHUNK, CHUNK)
            seat = block_of(c * CHUNK, CHUNK)
            cosine = angles[seat, 0:half_key]
            sine = angles[seat, half_key:KEY]
            own = info[seat, 0:1]
            same = own == row_ref[c]
            entering = (own == row_ref[jnp.maximum(c - 1, 0)][:, CHUNK - 1 :]) & (c > 0)
            leaving = own == row_ref[c][:, CHUNK - 1 :]
            offset = lax.broadcasted_iota(jnp.int32, (CHUNK, 1), 0).astype(f32)
            lane = lax.broadcasted_iota(jnp.int32, (CHUNK, 128), 1)
            facts = jnp.where(lane == 0, own, 0.0)
            scales = jnp.zeros((CHUNK, 128), f32)

            for head in range(heads):
                rate = rate_ref[head : head + 1, 0:1]
                into = jnp.where(entering, jnp.exp(rate * (offset + 1.0)), 0.0)
                onto = jnp.where(leaving, jnp.exp(rate * (CHUNK - 1.0 - offset)), 0.0)
                facts = jnp.where(lane == 1 + 2 * head, into, facts)
                facts = jnp.where(lane == 2 + 2 * head, onto, facts)
                query_raw = product[place, pl.ds(head * KEY, KEY)]
                key_raw = product[place, pl.ds(keys + head * KEY, KEY)]
                value = product[place, pl.ds(2 * keys + head * VAL, VAL)].astype(bf16)
                gate = product[place, pl.ds(2 * keys + values + head * VAL, VAL)]
                query_raw = query_raw.astype(bf16)
                key_raw = key_raw.astype(bf16)
                query = turn(query_raw.astype(f32), cosine, sine).astype(bf16)
                key = (turn(key_raw.astype(f32), cosine, sine) * key_scale).astype(bf16)
                memory = state[head]
                memory_low = memory.astype(bf16)
                scores = dot_nt(query, key)
                weights = (jnp.where(same, decay[head], 0.0) * scores).astype(bf16)
                retained = dot_nn(weights, value) + into * dot_nn(query, memory_low)
                moved = (key.astype(f32) * onto).astype(bf16)
                state[head] = into[CHUNK - 1 :, :] * memory + dot_tn(moved, value)
                centred = retained - jnp.mean(retained, axis=-1, keepdims=True)
                scale = lax.rsqrt(jnp.mean(centred * centred, axis=-1, keepdims=True) + group_floor)
                grouped = centred * scale
                columns = pl.ds(head * VAL, VAL)
                if head == 0:
                    @pl.when(c > 0)
                    def _():
                        wait(chunk_outs(c - 1))

                field_out[:, pl.ds(head * KEY, KEY)] = query_raw
                field_out[:, pl.ds(keys + head * KEY, KEY)] = key_raw
                field_out[:, pl.ds(2 * keys + head * VAL, VAL)] = value
                gate_out[:, columns] = gate.astype(bf16)
                past_out[head] = memory_low
                gated_out[:, columns] = (gate / (1.0 + jnp.exp(-gate)) * grouped).astype(bf16)
                grouped_out[:, columns] = grouped.astype(bf16)
                scales = jnp.where(lane == head, scale, scales)
            info[seat, :] = facts
            scale_out[...] = scales
            start(chunk_outs(c))
            between(c)

        wait(chunk_outs(chunks - 1))


    twin_step(0, 0)
    project(0, 0)
    step(0, 1)
    twin_step(0, 1)
    project(0, 1)
    wait_recv(over)
    start(onward)
    start(cot_over)
    for r in (1, 2):
        for s in (0, 1):
            project(r, s)
    step(0, 2)
    first_step(1)
    twin_step(0, 2)
    for r in (0, 1, 2):
        project(r, 2)
    wait_recv(onward)
    normed_out = pltpu.make_async_copy(normed, normed_ref, local_sem.at[7])
    normed_out.start()
    for s in (0, 1, 2):
        project(3, s)
    when_end(False, lambda: step(1, 1))
    step(0, 3)
    twin_step(0, 3)
    w_outs = [
        pltpu.make_async_copy(w_qkv, w_qkv_ref, out_sem.at[0]),
        pltpu.make_async_copy(w_gate, w_gate_ref, out_sem.at[1]),
    ]
    start(w_outs)
    project(0, 3)
    project(1, 3)
    when_end(False, lambda: step(1, 2))
    wait_recv(cot_early + cot_over)
    start(cot_onward)
    project(2, 3)
    project(3, 3)

    def between(c):
        @pl.when((c == 1) & at_end)
        def _():
            step(1, 1)

        @pl.when((c == 4) & at_end)
        def _():
            step(1, 2)

    wait(table_outs)
    retention(between)
    info_out = pltpu.make_async_copy(info, info_ref, table_sem.at[2])
    info_out.start()
    step(1, 3)
    for j in range(4):
        twin_step(1, j)
    w_out_out = pltpu.make_async_copy(w_out, w_out_ref, out_sem.at[2])
    w_out_out.start()
    wait_recv(cot_onward)

    wait_send(over + onward + cot_early + cot_over + cot_onward)
    for g in range(2):
        for j in range(3):
            pl.when((z < layers - 1) & (z - j >= 0))(lambda: wait_send(rise(g, j)))
            pl.when((z > 0) & (z + j < layers))(lambda: wait_send(sink(g, j)))
        for j in range(-3, 4):
            pl.when((z + j >= 0) & (z + j < layers))(lambda: wait_send(to_twin(g, j)))
    wait(w_outs + [normed_out, own_cot, info_out, w_out_out])


def opening_exchange(heads, shards, tokens, cotangent, segment, gain, bias):
    dp = lax.axis_size("dp")
    depth, keys = shards[0].shape
    values = shards[2].shape[1]
    unit = shards[4].shape[0]
    token_rows, width = tokens.shape
    rows = 4 * token_rows
    chunks = rows // CHUNK
    anywhere = pl.BlockSpec(memory_space=pl.ANY)
    in_vmem = pl.BlockSpec(memory_space=pltpu.VMEM)
    sem = pltpu.SemaphoreType.DMA
    vmem = pltpu.VMEM
    here = lax.axis_index("tensor") * heads
    head_ids = (here + jnp.arange(8, dtype=jnp.int32)).astype(f32)
    rates = jnp.broadcast_to(jnp.log1p(-jnp.exp2(-5.0 - head_ids))[:, None], (8, 128))
    row_segment = jnp.where(segment >= 0, segment, -7).astype(f32).reshape(chunks, 1, CHUNK)
    results = pl.pallas_call(
        functools.partial(opening_kernel, heads),
        out_shape=[
            jax.ShapeDtypeStruct((dp * depth, 2 * keys + values), bf16),
            jax.ShapeDtypeStruct((dp * depth, values), bf16),
            jax.ShapeDtypeStruct((dp * depth, unit), bf16),
            jax.ShapeDtypeStruct((rows, width), bf16),
            jax.ShapeDtypeStruct((rows, width), bf16),
            jax.ShapeDtypeStruct((rows, 2 * keys + values), bf16),
            jax.ShapeDtypeStruct((rows, values), bf16),
            jax.ShapeDtypeStruct((rows, values), bf16),
            jax.ShapeDtypeStruct((rows, values), bf16),
            jax.ShapeDtypeStruct((rows, 128), f32),
            jax.ShapeDtypeStruct((chunks, heads, KEY, VAL), bf16),
            jax.ShapeDtypeStruct((rows, KEY), f32),
            jax.ShapeDtypeStruct((rows, 128), f32),
            jax.ShapeDtypeStruct((heads, CHUNK, CHUNK), f32),
            jax.ShapeDtypeStruct((depth, unit), bf16),
        ],
        in_specs=[anywhere] * 8 + [in_vmem] * 4,
        out_specs=[anywhere] * 15,
        scratch_shapes=[
            vmem((dp * depth, 2 * keys + values), bf16),
            vmem((dp * depth, values), bf16),
            vmem((dp * depth, unit), bf16),
            vmem((unit, depth), bf16),
            vmem((rows, width), bf16),
            vmem((rows, 2 * keys + 2 * values), f32),
            vmem((rows, KEY), f32),
            vmem((rows, 128), f32),
            vmem((heads, CHUNK, CHUNK), f32),
            vmem((heads, KEY, VAL), f32),
            vmem((CHUNK, 2 * keys + values), bf16),
            vmem((CHUNK, values), bf16),
            vmem((CHUNK, values), bf16),
            vmem((CHUNK, values), bf16),
            vmem((CHUNK, 128), f32),
            vmem((heads, KEY, VAL), bf16),
            sem((8,)), sem((3,)), sem((3,)), sem((6,)), sem((4,)),
            sem((3, 3)), sem((3, 3)), sem((3, 3)), sem((3, 3)), sem((7, 3)), sem((7, 3)), sem((10,)), sem((10,)),
        ],
        compiler_params=pltpu.CompilerParams(
            collective_id=2, has_side_effects=True, vmem_limit_bytes=63_400_000
        ),
        name="opening_exchange",
    )(*shards, tokens, cotangent, row_segment, rates, gain.reshape(1, width), bias.reshape(1, width))
    return results, row_segment


def middle_kernel(
    gated_ref, w_out_ref, up_ref, down_ref, cot_ref, token_ref, gain_ref, bias_ref,
    low_ref, plus_ref, feed_ref, up_grad_out, down_grad_out, late_ref,
    big, units, columns, staged, terms, half_in, full_in, mixed, plus, total,
    load_sem, column_sem, staged_sem, feed_sem, out_sem, up_send, up_recv, below_send, below_recv, core_send, core_recv,
    row_send, row_recv, half_send, half_recv, full_send, full_recv, half_free, full_free, big_free,
):
    dp = lax.axis_index("dp")
    tensor = lax.axis_index("tensor")
    z = lax.div(dp, 2)
    layers = 4
    rows = token_ref.shape[0]
    half = rows // 2
    width = token_ref.shape[1]
    unit = units.shape[2]
    depth = up_ref.shape[0]
    above = (dp + 2, tensor)
    below = (dp - 2, tensor)
    twin = (dp + 1 - 2 * lax.rem(dp, 2), tensor)
    over_x = (dp, tensor + 1 - 2 * lax.rem(tensor, 2))
    over_y = (dp, lax.rem(tensor + 2, 4))
    sides = (over_x, over_y)

    def block_of(start, count):
        return pl.ds(pl.multiple_of(start, count), count)

    def start(copies):
        for copy in copies:
            copy.start()

    def wait(copies):
        for copy in copies:
            copy.wait()

    def remote(src, dst, send, recv, device):
        return pltpu.make_async_remote_copy(
            src_ref=src, dst_ref=dst, send_sem=send, recv_sem=recv, device_id=device, device_id_type=MESH
        )

    mine = block_of(dp * depth, depth)
    shard_loads = [
        pltpu.make_async_copy(down_ref, units.at[3, mine], load_sem.at[0]),
        pltpu.make_async_copy(up_ref, units.at[2, mine], load_sem.at[1]),
    ]
    first_loads = [pltpu.make_async_copy(w_out_ref, units.at[1], load_sem.at[3])] + [
        pltpu.make_async_copy(gated_ref.at[pl.ds(r * rows, rows)], units.at[0, pl.ds(r * rows, rows)], load_sem.at[8 + r])
        for r in (3, 1, 2, 0)
    ]
    token_load = pltpu.make_async_copy(token_ref, plus, load_sem.at[5])
    cot_load = pltpu.make_async_copy(cot_ref, big, load_sem.at[6])
    start(shard_loads)
    start(first_loads)
    token_load.start()
    cot_load.start()

    barrier = pltpu.get_barrier_semaphore()

    def greet(device):
        pl.semaphore_signal(barrier, inc=1, device_id=device, device_id_type=MESH)

    for device in (twin, over_x, over_y):
        greet(device)
    pl.when(z < layers - 1)(lambda: greet(above))
    pl.when(z > 0)(lambda: greet(below))
    pl.semaphore_wait(barrier, 3 + (z < layers - 1).astype(jnp.int32) + (z > 0).astype(jnp.int32))


    def shard_copy(a, shard, send_sem, recv_sem, index, device):
        place = block_of(shard * depth, depth)
        ref = units.at[3 - a, place]
        return remote(ref, ref, send_sem.at[a, index], recv_sem.at[a, index], device)

    def rise(a, j):
        return shard_copy(a, dp - 2 * j, up_send, up_recv, j, above)

    def sink(a, j):
        return shard_copy(a, dp + 2 * j, below_send, below_recv, j, below)

    def to_twin(a, j):
        return shard_copy(a, dp + 2 * j, core_send, core_recv, j + 3, twin)

    def from_twin(a, j):
        return shard_copy(a, twin[0] + 2 * j, core_send, core_recv, j + 3, twin)

    def first_step(a):
        shard_loads[a].wait()
        pl.when(z < layers - 1)(lambda: rise(a, 0).start())
        pl.when(z > 0)(lambda: sink(a, 0).start())
        to_twin(a, 0).start()

    def step(a, j):
        @pl.when(z - j >= 0)
        def _():
            shard_copy(a, dp - 2 * j, up_send, up_recv, j - 1, twin).wait_recv()
            if j < 3:
                pl.when(z < layers - 1)(lambda: rise(a, j).start())
            to_twin(a, -j).start()

        @pl.when(z + j < layers)
        def _():
            shard_copy(a, dp + 2 * j, below_send, below_recv, j - 1, twin).wait_recv()
            if j < 3:
                pl.when(z > 0)(lambda: sink(a, j).start())
            to_twin(a, j).start()

    def gathered(a):
        for j in range(-3, 4):
            @pl.when((z + j >= 0) & (z + j < layers))
            def _():
                from_twin(a, j).wait_recv()


    def rows_of(r, first=0, count=rows):
        return pl.ds(r * rows + first, count)

    halves = [
        remote(terms.at[2, pl.ds(0, half)], half_in.at[0], half_send.at[0], half_recv.at[0], over_x),
        remote(terms.at[2, pl.ds(half, half)], half_in.at[1], half_send.at[1], half_recv.at[1], over_y),
    ]

    def part_copy(index, term, first, device, count=half):
        place = pl.ds(first, count)
        return remote(
            terms.at[term, place], full_in.at[term, place], full_send.at[index], full_recv.at[index], device
        )

    plain_parts = [part_copy(0, 0, 0, over_x), part_copy(1, 1, half, over_y)]
    quarter = half // 2
    grown_parts = [
        part_copy(2, 0, half, over_x, quarter),
        part_copy(3, 1, 0, over_y, quarter),
        part_copy(4, 0, half + quarter, over_x, quarter),
        part_copy(5, 1, quarter, over_y, quarter),
    ]
    fulls = plain_parts + grown_parts
    lower, upper = (0, half), (half, half)

    def row_copy(index, source, first, target, device):
        return remote(
            big.at[rows_of(source, *first)], big.at[rows_of(target, *first)],
            row_send.at[index], row_recv.at[index], device,
        )

    early = [row_copy(0, 0, lower, 1, over_x), row_copy(1, 0, upper, 2, over_y)]
    across = [row_copy(2, 2, upper, 3, over_x), row_copy(3, 1, lower, 3, over_y)]
    late = [row_copy(4, 0, upper, 1, over_x), row_copy(5, 0, lower, 2, over_y)]

    def send_halves(stage):
        for i, copy in enumerate(halves):
            if stage == 1:
                pl.semaphore_wait(half_free.at[i], 1)
            copy.start()

    def take_halves(stage):
        for copy in halves:
            copy.wait_recv()
        for term, first, slot in ((1, 0, 0), (0, half, 1)):
            @pl.loop(0, half // 64)
            def _(i):
                place = block_of(first + i * 64, 64)
                grown = terms[term, place].astype(f32) + half_in[slot, block_of(i * 64, 64)].astype(f32)
                terms[term, place] = grown.astype(bf16)

        for i, copy in enumerate(grown_parts):
            if stage == 0 and i < 2:
                pl.semaphore_signal(half_free.at[i], inc=1, device_id=sides[i], device_id_type=MESH)
            copy.start()

    def send_plain(stage, i):
        if stage == 1:
            pl.semaphore_wait(full_free.at[i], 1)
        plain_parts[i].start()

    def slot_of(r):
        return (3, 0, 1, 2)[r]

    def branch_term(r):
        @pl.loop(0, width // 256)
        def _(j):
            tile = block_of(j * 256, 256)
            terms[slot_of(r), :, tile] = dot_nt(units[0, rows_of(r)], units[1, tile]).astype(bf16)

    def feed_grads(r):
        @pl.loop(0, unit // 256)
        def _(j):
            tile = block_of(j * 256, 256)
            units[4, rows_of(r), tile] = dot_nn(big[rows_of(r)], units[3, :, tile]).astype(bf16)

    def feed(r):
        @pl.loop(0, unit // 256)
        def _(j):
            tile = block_of(j * 256, 256)
            value, slope = gelu_both(dot_nn(big[rows_of(r)], units[2, :, tile]))
            units[0, rows_of(r), tile] = value.astype(bf16)
            units[1, rows_of(r), tile] = (units[4, rows_of(r), tile].astype(f32) * slope).astype(bf16)

    def back_term(r):
        @pl.loop(0, width // 256)
        def _(j):
            tile = block_of(j * 256, 256)
            terms[slot_of(r), :, tile] = dot_nt(units[1, rows_of(r)], units[2, tile]).astype(bf16)


    first_step(0)
    wait(first_loads[:2])
    branch_term(3)
    send_halves(0)
    wait(first_loads[2:])
    step(0, 1)
    branch_term(1)
    send_plain(0, 0)
    branch_term(2)
    send_plain(0, 1)
    step(0, 2)
    first_step(1)
    take_halves(0)
    branch_term(0)
    step(0, 3)
    cot_load.wait()
    gathered(0)
    step(1, 1)
    feed_grads(0)
    feed_grads(1)
    step(1, 2)
    feed_grads(2)
    feed_grads(3)
    for side in sides:
        pl.semaphore_signal(big_free, inc=1, device_id=side, device_id_type=MESH)
    step(1, 3)
    gathered(1)
    token_load.wait()
    pl.semaphore_wait(big_free, 2)

    def second_norm(i):
        place = block_of(i * 64, 64)
        value = plus[place].astype(f32) + terms[3, place].astype(f32)
        value = value + full_in[0, place].astype(f32) + full_in[1, place].astype(f32)
        mixed[place] = value
        plain, _ = normalize(value)
        big[place] = (plain * gain_ref[...] + bias_ref[...]).astype(bf16)

    for copy in plain_parts + grown_parts[:2]:
        copy.wait_recv()
    pl.loop(0, quarter // 64)(second_norm)
    pl.loop(half // 64, (half + quarter) // 64)(second_norm)
    for copy in grown_parts[2:]:
        copy.wait_recv()
    pl.loop(quarter // 64, half // 64)(second_norm)
    early[0].start()
    pl.loop((half + quarter) // 64, rows // 64)(second_norm)
    early[1].start()
    for i, side in enumerate(sides):
        pl.semaphore_signal(full_free.at[i], inc=1, device_id=side, device_id_type=MESH)
    feed(0)
    for copy in halves + fulls:
        copy.wait_send()
    back_term(0)
    for copy in early:
        copy.wait_recv()
    start(across)
    start(late)

    def cot_columns(t):
        return pltpu.make_async_copy(cot_ref.at[:, pl.ds(t * 512, 512)], columns.at[t % 2], column_sem.at[t])

    cot_columns(0).start()
    cot_columns(1).start()
    for copy in across:
        copy.wait_recv()
    feed(3)
    back_term(3)
    send_halves(1)
    for copy in late:
        copy.wait_recv()
    feed(1)
    back_term(1)
    send_plain(1, 0)
    feed(2)
    back_term(2)
    send_plain(1, 1)
    take_halves(1)

    def staged_out(out, t, slot):
        return pltpu.make_async_copy(staged.at[slot], out.at[pl.ds(t * 512, 512)], staged_sem.at[slot])

    def weight_grad(out, t, left_of, right):
        for j in range(unit // 256):
            tile = pl.ds(j * 256, 256)
            product = None
            for place in (pl.ds(0, 2 * rows), pl.ds(2 * rows, 2 * rows)):
                more = dot_tn(left_of(place), units[right, place, tile])
                product = more if product is None else product + more
            staged[t % 2, :, tile] = product.astype(bf16)
        staged_out(out, t, t % 2).start()

    for t in range(4):
        cot_columns(t).wait()
        if t >= 2:
            staged_out(down_grad_out, t - 2, t % 2).wait()
        weight_grad(down_grad_out, t, lambda place: columns[t % 2, place], 0)
        if t < 2:
            cot_columns(t + 2).start()
    for t in range(4):
        if t < 2:
            staged_out(down_grad_out, t + 2, t % 2).wait()
        else:
            staged_out(up_grad_out, t - 2, t % 2).wait()
        weight_grad(up_grad_out, t, lambda place: big[place, pl.ds(t * 512, 512)], 1)

    def feed_out(t):
        return pltpu.make_async_copy(columns.at[t % 2], feed_ref.at[:, pl.ds(t * 512, 512)], feed_sem.at[t % 2])

    for t in range(4):
        if t >= 2:
            feed_out(t - 2).wait()

        @pl.loop(0, 4)
        def _(r):
            place = block_of(r * rows, rows)
            columns[t % 2, place] = dot_nt(units[0, place], units[3, pl.ds(t * 512, 512)]).astype(bf16)

        feed_out(t).start()

        @pl.loop(0, rows // 64)
        def _(i):
            place = block_of(i * 64, 64)
            tile = pl.ds(t * 512, 512)
            plus[place, tile] = (mixed[place, tile] + columns[t % 2, place].astype(f32)).astype(bf16)

    plus_out = pltpu.make_async_copy(plus, plus_ref, out_sem.at[0])
    plus_out.start()
    for copy in halves:
        copy.wait_send()
    cot_own = pltpu.make_async_copy(cot_ref.at[pl.ds(0, rows)], terms.at[2], load_sem.at[7])
    cot_own.start()
    total[...] = jnp.zeros_like(total)
    cot_own.wait()

    def second_norm_back(i):
        place = block_of(i * 64, 64)
        grad = terms[3, place].astype(f32) + full_in[0, place].astype(f32) + full_in[1, place].astype(f32)
        plain, scale = normalize(mixed[place])
        back = terms[2, place].astype(f32) + normalize_back(grad, plain, scale, gain_ref[...])
        full_in[0, place] = back.astype(bf16)
        total[0:1, :] += jnp.sum(grad * plain, axis=0, keepdims=True)
        total[1:2, :] += jnp.sum(grad, axis=0, keepdims=True)

    for copy in plain_parts + grown_parts[:2]:
        copy.wait_recv()
    pl.loop(0, quarter // 64)(second_norm_back)
    pl.loop(half // 64, (half + quarter) // 64)(second_norm_back)
    for copy in grown_parts[2:]:
        copy.wait_recv()
    pl.loop(quarter // 64, half // 64)(second_norm_back)
    pl.loop((half + quarter) // 64, rows // 64)(second_norm_back)
    low_out = pltpu.make_async_copy(full_in.at[0], low_ref, out_sem.at[1])
    low_out.start()
    late_ref[...] = total[...]

    for t in (2, 3):
        staged_out(up_grad_out, t, t % 2).wait()
        feed_out(t).wait()
    for copy in fulls + early + across + late:
        copy.wait_send()
    for a in range(2):
        for j in range(3):
            pl.when((z < layers - 1) & (z - j >= 0))(lambda: rise(a, j).wait_send())
            pl.when((z > 0) & (z + j < layers))(lambda: sink(a, j).wait_send())
        for j in range(-3, 4):
            pl.when((z + j >= 0) & (z + j < layers))(lambda: to_twin(a, j).wait_send())
    plus_out.wait()
    low_out.wait()


def middle_exchange(gated, w_out, up_shard, down_shard, cot_all, tokens, gain, bias):
    token_rows, width = tokens.shape
    rows = 4 * token_rows
    unit = gated.shape[1]
    anywhere = pl.BlockSpec(memory_space=pl.ANY)
    in_vmem = pl.BlockSpec(memory_space=pltpu.VMEM)
    sem = pltpu.SemaphoreType.DMA
    regular = pltpu.SemaphoreType.REGULAR
    vmem = pltpu.VMEM
    return pl.pallas_call(
        middle_kernel,
        out_shape=[
            jax.ShapeDtypeStruct((token_rows, width), bf16),
            jax.ShapeDtypeStruct((token_rows, width), bf16),
            jax.ShapeDtypeStruct((rows, width), bf16),
            jax.ShapeDtypeStruct((width, unit), bf16),
            jax.ShapeDtypeStruct((width, unit), bf16),
            jax.ShapeDtypeStruct((2, width), f32),
        ],
        in_specs=[anywhere] * 6 + [in_vmem] * 2,
        out_specs=[anywhere] * 5 + [in_vmem],
        scratch_shapes=[
            vmem((rows, width), bf16),
            vmem((5, rows, unit), bf16),
            vmem((2, rows, 512), bf16),
            vmem((2, 512, unit), bf16),
            vmem((4, token_rows, width), bf16),
            vmem((2, token_rows // 2, width), bf16),
            vmem((2, token_rows, width), bf16),
            vmem((token_rows, width), f32),
            vmem((token_rows, width), bf16),
            vmem((2, width), f32),
            sem((12,)), sem((4,)), sem((2,)), sem((2,)), sem((2,)),
            sem((2, 3)), sem((2, 3)), sem((2, 3)), sem((2, 3)), sem((2, 7)), sem((2, 7)),
            sem((6,)), sem((6,)), sem((2,)), sem((2,)), sem((6,)), sem((6,)),
            regular((2,)), regular((2,)), regular,
        ],
        compiler_params=pltpu.CompilerParams(
            collective_id=4, has_side_effects=True, vmem_limit_bytes=63_400_000
        ),
        name="middle_exchange",
    )(gated, w_out, up_shard, down_shard, cot_all, tokens, gain.reshape(1, width), bias.reshape(1, width))


def closing_kernel(
    heads,
    normed1_ref, up_ref, down_ref, feed_ref, w_out_ref, w_qkv_ref, w_gate_ref,
    gate_ref, grouped_ref, gated_ref, scale_ref, field_ref, past_ref, angle_ref, info_ref,
    low_ref, token_ref, row_ref, decay_ref, gain_ref, late_ref,
    result_ref, grad_ref, query_out, key_out, value_out, gate_out, out_out, up_out, down_out, sums_ref,
    big, units, columns, terms, half_in, full_in, products, twin_in, line_in,
    state_ref, past_in, scale_in, angle_in, info_in, given, landed, total,
    unit_sem, column_sem, chunk_sem, out_sem, mixed_sem, over_send, over_recv, onward_send, onward_recv,
    half_send, half_recv, full_send, full_recv, twin_send, twin_recv, line_send, line_recv, sum_send, sum_recv,
    twin_free, line_free, half_free, full_free,
):
    dp = lax.axis_index("dp")
    tensor = lax.axis_index("tensor")
    z = lax.div(dp, 2)
    core = lax.rem(dp, 2)
    rows = token_ref.shape[0]
    half = rows // 2
    width = token_ref.shape[1]
    unit = units.shape[2]
    depth = columns.shape[2] // 2
    at_end = (z == 0) | (z == 3)
    upper = z >= 2
    twin = (dp + 1 - 2 * core, tensor)
    over_x = (dp, tensor + 1 - 2 * lax.rem(tensor, 2))
    over_y = (dp, lax.rem(tensor + 2, 4))
    here = dp * 4 + tensor
    peers = 32
    last = 5

    def layer(index):
        return (2 * index + core, tensor)

    def seen(index):
        return jnp.where(upper, 3 - index, index)

    end = layer(seen(0))
    near = layer(seen(1))
    opposite = layer(seen(2))
    targets = [seen(3), seen(2), jnp.where(at_end, seen(1), seen(0)), z]

    def remote(src, dst, send, recv, device):
        return pltpu.make_async_remote_copy(
            src_ref=src, dst_ref=dst, send_sem=send, recv_sem=recv, device_id=device, device_id_type=MESH
        )

    def block_of(start, count):
        return pl.ds(pl.multiple_of(start, count), count)


    def whole(index, ref, sem):
        return [pltpu.make_async_copy(ref, units.at[index], unit_sem.at[sem])]

    def part(index, ref, start, sem):
        return [pltpu.make_async_copy(ref.at[:, pl.ds(start, unit)], units.at[index], unit_sem.at[sem])]

    def start(copies):
        for copy in copies:
            copy.start()

    def wait(copies):
        for copy in copies:
            copy.wait()

    out_load = whole(3, w_out_ref, 4)
    feed_load = [
        pltpu.make_async_copy(feed_ref.at[pl.ds((i + 1) * rows, rows)], terms.at[i], unit_sem.at[i]) for i in range(3)
    ]
    gated_load = whole(2, gated_ref, 6)
    w_gate_load = whole(3, w_gate_ref, 7)
    w_value_load = part(2, w_qkv_ref, unit, 8)
    w_key_load = part(1, w_qkv_ref, 0, 9)

    def wait_recv(copies):
        for copy in copies:
            copy.wait_recv()

    def wait_send(copies):
        for copy in copies:
            copy.wait_send()


    sources = [up_ref, down_ref, None, normed1_ref, normed1_ref, normed1_ref]

    def given_copy(r, k):
        place = block_of(targets[k] * 2 * depth, 2 * depth)
        return pltpu.make_async_copy(sources[r].at[place], products.at[r, k], column_sem.at[4 * r + k])

    def column_copy(r, k):
        place = block_of(targets[k] * 2 * depth, 2 * depth)
        return pltpu.make_async_copy(sources[r].at[:, place], columns.at[k % 2], column_sem.at[k])

    def prefetch(r):
        column_copy(r, 0).start()
        column_copy(r, 1).start()

    mine = block_of(core * depth, depth)
    theirs = block_of((1 - core) * depth, depth)

    def to_twin(r, k):
        return remote(
            products.at[r % 2, k, theirs], twin_in.at[k % 2], twin_send.at[r % 2, k], twin_recv.at[k % 2], twin
        )

    def along(r, k, slot, device):
        return remote(
            products.at[r % 2, k, mine], line_in.at[slot], line_send.at[r % 2, k], line_recv.at[slot], device
        )

    def send_to_twin(r, k):
        if r >= 1 or k >= 2:
            pl.semaphore_wait(twin_free.at[k % 2], 1)
        to_twin(r, k).start()

    def multiply(r, k):
        to_twin(r - 2, k).wait_send()
        if k < 3:
            along(r - 2, k, 0, end).wait_send()
        else:
            wait(outputs(r - 2))
        if sources[r] is not None:
            column_copy(r, k).wait()

        @pl.loop(0, unit // 512)
        def _(j):
            tile = block_of(j * 512, 512)
            product = None
            for place in (pl.ds(0, 2 * rows), pl.ds(2 * rows, 2 * rows)):
                if r < 4:
                    right = units[(None, None, 2, 0)[r], place, tile]
                else:
                    right = big[place, block_of((r - 4) * unit + j * 512, 512)]
                if sources[r] is None:
                    left = big[place, block_of(targets[k] * 2 * depth, 2 * depth)]
                else:
                    left = columns[k % 2, place]
                more = dot_tn(left, right)
                product = more if product is None else product + more
            products[r % 2, k, :, tile] = product.astype(bf16)

        if sources[r] is not None and k + 2 < 4:
            column_copy(r, k + 2).start()
        elif r == 4:
            column_copy(5, k - 2).start()
        send_to_twin(r, k)

    def add_to_mine(r, k, others):
        @pl.loop(0, depth // 64)
        def _(i):
            inner = block_of(core * depth + i * 64, 64)
            value = products[r % 2, k, inner].astype(f32)
            for ref, index in others:
                value = value + ref[index, block_of(i * 64, 64)].astype(f32)
            products[r % 2, k, inner] = value.astype(bf16)

    def settle(r, k):
        to_twin(r, k).wait_recv()
        add_to_mine(r, k, [(twin_in, k % 2)])
        if r < last or k < 2:
            pl.semaphore_signal(twin_free.at[k % 2], inc=1, device_id=twin, device_id_type=MESH)

    def push(r, k):
        @pl.when(at_end)
        def _():
            if r >= 1:
                pl.semaphore_wait(line_free.at[k], 1)
            along(r, k, k, near).start()

    def line_wait(slot):
        along(0, 0, slot, end).wait_recv()

    def used(device, index):
        pl.semaphore_signal(line_free.at[index], inc=1, device_id=device, device_id_type=MESH)

    def pass_on(r, which):
        arrived, sender, slot, device = ((0, end, 3, opposite), (1, end, 4, opposite), (3, opposite, 0, end))[which]

        @pl.when(jnp.logical_not(at_end))
        def _():
            line_wait(arrived)
            add_to_mine(r, which, [(line_in, arrived)])
            if r < last:
                used(sender, (0, 1, 0)[which])
            if r >= 1:
                pl.semaphore_wait(line_free.at[which], 1)
            along(r, which, slot, device).start()

    def outputs(r):
        keys = heads * KEY
        slot = products.at[r % 2, 3]
        if r == 4:
            return [
                pltpu.make_async_copy(slot.at[mine, pl.ds(0, keys)], query_out, out_sem.at[0, 0]),
                pltpu.make_async_copy(slot.at[mine, pl.ds(keys, keys)], key_out, out_sem.at[0, 1]),
            ]
        out = (up_out, down_out, out_out, gate_out, None, value_out)[r]
        return [pltpu.make_async_copy(slot.at[mine], out, out_sem.at[r % 2, 0])]

    def finish(r):
        @pl.when(at_end)
        def _():
            line_wait(0)
            add_to_mine(r, 3, [(line_in, 0)])
            if r < last:
                used(near, 2)

        @pl.when(jnp.logical_not(at_end))
        def _():
            line_wait(2)
            line_wait(4)
            add_to_mine(r, 3, [(line_in, 2), (line_in, 4)])
            if r < last:
                used(end, 2)
                used(opposite, 1)

        start(outputs(r))


    def rows_of(r, first=0, count=rows):
        return pl.ds(r * rows + first, count)

    over = [
        remote(low_ref, big.at[rows_of(1)], over_send.at[0], over_recv.at[0], over_x),
        remote(low_ref, big.at[rows_of(2)], over_send.at[1], over_recv.at[1], over_y),
    ]
    onward = [
        remote(big.at[rows_of(2, 0, half)], big.at[rows_of(3, 0, half)], onward_send.at[0], onward_recv.at[0], over_x),
        remote(big.at[rows_of(1, half, half)], big.at[rows_of(3, half, half)], onward_send.at[1], onward_recv.at[1], over_y),
    ]
    halves = [
        remote(terms.at[2, pl.ds(0, half)], half_in.at[0], half_send.at[0], half_recv.at[0], over_x),
        remote(terms.at[2, pl.ds(half, half)], half_in.at[1], half_send.at[1], half_recv.at[1], over_y),
    ]

    def part_copy(index, term, first, device, count=half):
        place = pl.ds(first, count)
        return remote(
            terms.at[term, place], full_in.at[term, place], full_send.at[index], full_recv.at[index], device
        )

    plain_parts = [part_copy(0, 0, 0, over_x), part_copy(1, 1, half, over_y)]
    quarter = half // 2
    grown_parts = [
        part_copy(2, 0, half, over_x, quarter),
        part_copy(3, 1, 0, over_y, quarter),
        part_copy(4, 0, half + quarter, over_x, quarter),
        part_copy(5, 1, quarter, over_y, quarter),
    ]
    fulls = plain_parts + grown_parts
    sides = (over_x, over_y)

    def send_halves(stage):
        for i, copy in enumerate(halves):
            if stage == 1:
                pl.semaphore_wait(half_free.at[i], 1)
            copy.start()

    def take_halves(stage):
        for copy in halves:
            copy.wait_recv()
        for term, first, slot in ((1, 0, 0), (0, half, 1)):
            @pl.loop(0, half // 64)
            def _(i):
                place = block_of(first + i * 64, 64)
                grown = terms[term, place].astype(f32) + half_in[slot, block_of(i * 64, 64)].astype(f32)
                terms[term, place] = grown.astype(bf16)

        for i, copy in enumerate(grown_parts):
            if stage == 0 and i < 2:
                pl.semaphore_signal(half_free.at[i], inc=1, device_id=sides[i], device_id_type=MESH)
            copy.start()

    def send_plain(stage, i):
        if stage == 1:
            pl.semaphore_wait(full_free.at[i], 1)
        plain_parts[i].start()

    def project(r):
        slot = (2, 0, 1, 2)[r]

        @pl.loop(0, width // 512)
        def _(j):
            tile = block_of(j * 512, 512)
            term = dot_nt(big[rows_of(r), pl.ds(0, unit)], units[1, tile])
            term = term + dot_nt(big[rows_of(r), pl.ds(unit, unit)], units[2, tile])
            term = term + dot_nt(units[0, rows_of(r)], units[3, tile])
            terms[slot, :, tile] = term.astype(bf16)


    def gate_copies(r):
        return [
            pltpu.make_async_copy(
                ref.at[rows_of(r), pl.ds(h * VAL, VAL)],
                columns.at[r % 2, pl.ds((2 * i + h) * rows, rows)],
                chunk_sem.at[r % 2, 2 * i + h],
            )
            for i, ref in enumerate((gate_ref, grouped_ref))
            for h in range(heads)
        ] + [pltpu.make_async_copy(scale_ref.at[rows_of(r)], scale_in.at[r % 2], chunk_sem.at[r % 2, 2 * heads])]

    def gate_back(r):
        wait(gate_copies(r))
        for head in range(heads):
            tile = pl.ds(head * VAL, VAL)

            @pl.loop(0, rows // CHUNK)
            def _(i):
                place = block_of(r * rows + i * CHUNK, CHUNK)
                grad = dot_nn(big[place], units[3, :, tile])
                raw = columns[r % 2, block_of(head * rows + i * CHUNK, CHUNK)].astype(f32)
                grouped = columns[r % 2, block_of((heads + head) * rows + i * CHUNK, CHUNK)].astype(f32)
                sigmoid = 1.0 / (1.0 + jnp.exp(-raw))
                units[0, place, tile] = (grad * grouped * (sigmoid * (1.0 + raw * (1.0 - sigmoid)))).astype(bf16)
                c = grad * (raw * sigmoid)
                mean_c = jnp.mean(c, axis=-1, keepdims=True)
                mean_cx = jnp.mean(c * grouped, axis=-1, keepdims=True)
                scale = scale_in[r % 2, block_of(i * CHUNK, CHUNK), head : head + 1]
                units[1, place, tile] = (scale * (c - mean_c - grouped * mean_cx)).astype(bf16)

    chunks = 4 * rows // CHUNK
    per_piece = rows // CHUNK

    def chunk_place(c):
        piece = lax.div(c, per_piece)
        low = lax.rem(lax.rem(piece, 2) + lax.rem(tensor, 2), 2)
        high = lax.rem(lax.div(piece, 2) + lax.div(tensor, 2), 2)
        return (2 * high + low) * per_piece + lax.rem(c, per_piece)

    def chunk_copies(c, slot):
        place = block_of(chunk_place(c) * CHUNK, CHUNK)
        seat = block_of(c * CHUNK, CHUNK)
        keys = heads * KEY
        pieces = [
            (field_ref.at[place, pl.ds(0, keys)], columns.at[slot, pl.ds(0, CHUNK)]),
            (field_ref.at[place, pl.ds(keys, keys)], columns.at[slot, pl.ds(CHUNK, CHUNK)]),
        ]
        for h in range(heads):
            pieces.append((field_ref.at[place, pl.ds(2 * keys + h * VAL, VAL)], columns.at[slot, pl.ds((2 + h) * CHUNK, CHUNK)]))
        pieces += [
            (past_ref.at[c], past_in.at[slot]),
            (angle_ref.at[seat], angle_in.at[slot]),
            (info_ref.at[seat], info_in.at[slot]),
        ]
        return [pltpu.make_async_copy(src, dst, chunk_sem.at[slot, i]) for i, (src, dst) in enumerate(pieces)]

    def retention_steps(between):
        @pl.loop(0, chunks)
        def _(step):
            c = chunks - 1 - step
            slot = lax.rem(step, 2)
            wait(chunk_copies(c, slot))

            @pl.when(step + 1 < chunks)
            def _():
                start(chunk_copies(c - 1, 1 - slot))

            place = block_of(chunk_place(c) * CHUNK, CHUNK)
            angles = angle_in[slot]
            cosine = angles[:, : KEY // 2]
            sine = angles[:, KEY // 2 :]
            info = info_in[slot]
            same = info[:, 0:1] == row_ref[c]

            for head in range(heads):
                at = pl.ds(head * KEY, KEY)
                query = turn(columns[slot, pl.ds(0, CHUNK), at].astype(f32), cosine, sine).astype(bf16)
                key = turn(columns[slot, pl.ds(CHUNK, CHUNK), at].astype(f32), cosine, sine)
                key = (key * key_scale).astype(bf16)
                value = columns[slot, pl.ds((2 + head) * CHUNK, CHUNK)]
                into = info[:, 1 + 2 * head : 2 + 2 * head]
                onto = info[:, 2 + 2 * head : 3 + 2 * head]
                past = past_in[slot, head]
                out_grad = units[1, place, pl.ds(head * VAL, VAL)]
                state = state_ref[head]
                state_low = state.astype(bf16)
                masked = jnp.where(same, decay_ref[head], 0.0)
                weights = (masked * dot_nt(query, key)).astype(bf16)
                score_grad = (masked * dot_nt(out_grad, value)).astype(bf16)
                value_grad = dot_tn(weights, out_grad) + onto * dot_nn(key, state_low)
                query_grad = dot_nn(score_grad, key) + into * dot_nt(out_grad, past)
                key_grad = dot_tn(score_grad, query) + onto * dot_nt(value, state_low)
                moved = (query.astype(f32) * into).astype(bf16)
                state_ref[head] = into[CHUNK - 1 :, :] * state + dot_tn(moved, out_grad)
                big[place, pl.ds(head * KEY, KEY)] = turn_back(query_grad, cosine, sine).astype(bf16)
                big[place, pl.ds((heads + head) * KEY, KEY)] = (turn_back(key_grad, cosine, sine) * key_scale).astype(bf16)
                big[place, pl.ds(2 * heads * KEY + head * VAL, VAL)] = value_grad.astype(bf16)

            between(step)

    blocks = width // columns.shape[2]
    last_loads = [
        pltpu.make_async_copy(
            ref.at[:, pl.ds(q * columns.shape[2], columns.shape[2])], columns.at[i, rows_of(q)], chunk_sem.at[i, q]
        )
        for i, ref in enumerate((token_ref, low_ref))
        for q in range(blocks)
    ]

    def laid_out(slot, i):
        return jnp.concatenate([columns[slot, block_of(q * rows + i * 64, 64)] for q in range(blocks)], axis=1)


    own_load = pltpu.make_async_copy(low_ref, big.at[rows_of(0)], mixed_sem.at[0])
    own_load.start()
    for r in range(2):
        for k in range(4):
            given_copy(r, k).start()
    start(out_load)
    start(gated_load)
    start(gate_copies(0))
    start(gate_copies(1))
    start(feed_load)

    barrier = pltpu.get_barrier_semaphore()

    def partner(k):
        other = lax.rem(here + k, peers)
        return other, (lax.div(other, 4), lax.rem(other, 4))

    @pl.loop(1, peers)
    def _(k):
        pl.semaphore_signal(barrier, inc=1, device_id=partner(k)[1], device_id_type=MESH)

    pl.semaphore_wait(barrier, peers - 1)

    start(over)
    for k in range(4):
        given_copy(0, k).wait()
        send_to_twin(0, k)
        if k > 0:
            settle(0, k - 1)
            push(0, k - 1)
    for k in range(4):
        given_copy(1, k).wait()
        send_to_twin(1, k)
        settle(*((1, k - 1) if k > 0 else (0, 3)))
    wait(out_load)
    own_load.wait()
    settle(1, 3)
    pass_on(0, 0)
    push(1, 0)
    gate_back(0)
    start(gate_copies(2))
    wait_recv(over)
    start(onward)
    pass_on(0, 1)
    gate_back(1)
    start(gate_copies(3))
    push(1, 1)
    gate_back(2)
    pass_on(0, 2)
    pass_on(1, 0)
    push(1, 2)
    finish(0)
    wait_recv(onward)
    wait(feed_load)
    send_halves(0)
    send_plain(0, 0)
    send_plain(0, 1)
    wait(gated_load)
    multiply(2, 0)
    multiply(2, 1)
    pass_on(1, 2)
    settle(2, 0)
    push(2, 0)
    pass_on(1, 1)
    gate_back(3)
    prefetch(3)
    start(w_gate_load)
    settle(2, 1)
    multiply(2, 2)
    multiply(2, 3)
    start(w_value_load)
    settle(2, 2)
    push(2, 1)
    multiply(3, 0)
    finish(1)
    push(2, 2)
    settle(2, 3)
    multiply(3, 1)
    take_halves(0)
    settle(3, 0)
    pass_on(2, 0)
    multiply(3, 2)
    settle(3, 1)
    multiply(3, 3)
    start(chunk_copies(chunks - 1, 0))
    push(3, 0)
    wait_send(over + onward)
    state_ref[...] = jnp.zeros_like(state_ref)

    def between(step):
        @pl.when(step == 1)
        def _():
            pass_on(2, 2)
            pass_on(2, 1)
            settle(3, 2)

        @pl.when(step == 2)
        def _():
            push(3, 1)

    retention_steps(between)
    start(w_key_load)
    prefetch(4)
    settle(3, 3)
    multiply(4, 0)
    push(3, 2)
    pass_on(3, 0)
    finish(2)
    multiply(4, 1)
    wait_send(halves)
    wait(w_gate_load + w_value_load + w_key_load)
    project(3)
    send_halves(1)
    wait_recv(fulls)
    result_copy = pltpu.make_async_copy(full_in, result_ref, mixed_sem.at[1])
    result_copy.start()
    result_copy.wait()
    for i, side in enumerate(sides):
        pl.semaphore_signal(full_free.at[i], inc=1, device_id=side, device_id_type=MESH)
    wait_send(fulls)
    pass_on(3, 1)
    settle(4, 0)
    push(4, 0)
    pass_on(3, 2)
    multiply(4, 2)
    settle(4, 1)
    project(2)
    push(4, 1)
    settle(4, 2)
    project(1)
    pass_on(4, 0)
    send_plain(1, 0)
    send_plain(1, 1)
    multiply(4, 3)
    finish(3)
    push(4, 2)
    pass_on(4, 2)
    pass_on(4, 1)
    take_halves(1)
    settle(4, 3)
    multiply(5, 0)
    multiply(5, 1)
    settle(5, 0)
    push(5, 0)
    multiply(5, 2)
    settle(5, 1)
    settle(5, 2)
    finish(4)
    pass_on(5, 0)
    push(5, 1)
    multiply(5, 3)
    start(last_loads)
    wait_send(halves)
    project(0)
    pass_on(5, 1)
    pass_on(5, 2)
    push(5, 2)
    settle(5, 3)
    total[...] = jnp.zeros_like(total)
    wait(last_loads)

    def first_norm_back(i):
        place = block_of(i * 64, 64)
        normed_grad = terms[2, place].astype(f32) + full_in[0, place].astype(f32) + full_in[1, place].astype(f32)
        plain, scale = normalize(laid_out(0, i).astype(f32))
        grad = laid_out(1, i).astype(f32) + normalize_back(normed_grad, plain, scale, gain_ref[...])
        full_in[0, place] = grad.astype(bf16)
        total[0:1, :] += jnp.sum(normed_grad * plain, axis=0, keepdims=True)
        total[1:2, :] += jnp.sum(normed_grad, axis=0, keepdims=True)

    wait_recv(plain_parts + grown_parts[:2])
    pl.loop(0, quarter // 64)(first_norm_back)
    pl.loop(half // 64, (half + quarter) // 64)(first_norm_back)
    wait_recv(grown_parts[2:])
    pl.loop(quarter // 64, half // 64)(first_norm_back)
    pl.loop((half + quarter) // 64, rows // 64)(first_norm_back)
    grad_copy = pltpu.make_async_copy(full_in.at[0], grad_ref, mixed_sem.at[3])
    grad_copy.start()

    total[2:4, :] = late_ref[...]
    for k in range(peers // 2):
        given[k] = total[:, k * 128 : (k + 1) * 128]

    def sum_copy(k):
        other, device = partner(k)
        return remote(given.at[lax.div(other, 2)], landed.at[k], sum_send.at[k], sum_recv.at[k], device)

    @pl.loop(1, peers)
    def _(k):
        sum_copy(k).start()

    sums_ref[...] = given[lax.div(here, 2)]

    @pl.loop(1, peers)
    def _(k):
        sum_copy(k).wait()
        sums_ref[...] += landed[k]

    finish(5)

    wait_send(fulls)
    for r in (4, 5):
        for k in range(4):
            to_twin(r, k).wait_send()
            if k < 3:
                along(r, k, 0, end).wait_send()
    wait(outputs(4) + outputs(5))
    grad_copy.wait()


def cast_kernel(plus_ref, parts_ref, *refs):
    count = len(refs) // 2
    total = plus_ref[...].astype(f32) + parts_ref[0].astype(f32) + parts_ref[1].astype(f32)
    refs[count][...] = total.astype(bf16)
    for i, (source, target) in enumerate(zip(refs[:count], refs[count + 1 :])):
        value = source[...].astype(target.dtype)
        target[...] = value.T if i >= count - 2 else value


def cast_all(plus, parts, arrays):
    steps = 4

    def slab(rows, width):
        return pl.BlockSpec((rows // steps, width), lambda j: (j, 0))

    rows, width = plus.shape
    in_specs = [slab(rows, width), pl.BlockSpec((2, rows // steps, width), lambda j: (0, j, 0))]
    out_specs, shapes = [slab(rows, width)], [jax.ShapeDtypeStruct(plus.shape, bf16)]
    for i, v in enumerate(arrays):
        rows, width = v.shape
        if i >= len(arrays) - 2:
            in_specs.append(pl.BlockSpec((rows, width // steps), lambda j: (0, j)))
            out_specs.append(pl.BlockSpec((width // steps, rows), lambda j: (j, 0)))
            shapes.append(jax.ShapeDtypeStruct((width, rows), f32))
        else:
            in_specs.append(slab(rows, width))
            out_specs.append(slab(rows, width))
            shapes.append(jax.ShapeDtypeStruct((rows, width), bf16 if i == 0 else f32))
    return pl.pallas_call(
        cast_kernel,
        grid=(steps,),
        in_specs=in_specs,
        out_specs=out_specs,
        out_shape=shapes,
        compiler_params=pltpu.CompilerParams(vmem_limit_bytes=60 * 1024 * 1024),
        name="last_casts",
    )(plus, parts, *arrays)


def closing_exchange(heads, operands, small):
    token_rows, width = operands[-1].shape
    rows = 4 * token_rows
    depth = width // 8
    keys, values = heads * KEY, heads * VAL
    unit = operands[1].shape[1]
    anywhere = pl.BlockSpec(memory_space=pl.ANY)
    in_vmem = pl.BlockSpec(memory_space=pltpu.VMEM)
    sem = pltpu.SemaphoreType.DMA
    regular = pltpu.SemaphoreType.REGULAR
    vmem = pltpu.VMEM
    return pl.pallas_call(
        functools.partial(closing_kernel, heads),
        out_shape=[
            jax.ShapeDtypeStruct((2, token_rows, width), bf16),
            jax.ShapeDtypeStruct((token_rows, width), bf16),
            jax.ShapeDtypeStruct((depth, keys), bf16),
            jax.ShapeDtypeStruct((depth, keys), bf16),
            jax.ShapeDtypeStruct((depth, values), bf16),
            jax.ShapeDtypeStruct((depth, values), bf16),
            jax.ShapeDtypeStruct((depth, unit), bf16),
            jax.ShapeDtypeStruct((depth, unit), bf16),
            jax.ShapeDtypeStruct((depth, unit), bf16),
            jax.ShapeDtypeStruct((8, 128), f32),
        ],
        in_specs=[anywhere] * len(operands) + [in_vmem] * len(small),
        out_specs=[anywhere] * 9 + [in_vmem],
        scratch_shapes=[
            vmem((rows, width), bf16),
            vmem((4, rows, unit), bf16),
            vmem((2, rows, 2 * depth), bf16),
            vmem((3, token_rows, width), bf16),
            vmem((2, token_rows // 2, width), bf16),
            vmem((2, token_rows, width), bf16),
            vmem((2, 4, 2 * depth, unit), bf16),
            vmem((2, depth, unit), bf16),
            vmem((5, depth, unit), bf16),
            vmem((heads, KEY, VAL), f32),
            vmem((2, heads, KEY, VAL), bf16),
            vmem((2, token_rows, 128), f32),
            vmem((2, CHUNK, KEY), f32),
            vmem((2, CHUNK, 128), f32),
            vmem((16, 8, 128), f32),
            vmem((32, 8, 128), f32),
            vmem((8, width), f32),
            sem((10,)), sem((8,)), sem((2, 12)), sem((2, 2)), sem((4,)),
            sem((2,)), sem((2,)), sem((2,)), sem((2,)),
            sem((2,)), sem((2,)), sem((6,)), sem((6,)),
            sem((2, 4)), sem((2,)), sem((2, 3)), sem((5,)), sem((32,)), sem((32,)),
            regular((2,)), regular((3,)), regular((2,)), regular((2,)),
        ],
        compiler_params=pltpu.CompilerParams(
            collective_id=3, has_side_effects=True, vmem_limit_bytes=63_400_000
        ),
        name="closing_exchange",
    )(*operands, *small)


def body(tokens, cotangent, segment, first_gain, first_bias, query_weight, key_weight, value_weight, gate_weight, out_weight, second_gain, second_bias, up_weight, down_weight):
    devices = lax.axis_size("tensor")
    rows = tokens.shape[0]
    heads = query_weight.shape[1] // KEY
    here = lax.axis_index("tensor")
    which = (here if devices == 4 else jnp.zeros_like(here)).astype(jnp.int32).reshape(1)

    def per_piece(values):
        return [values[i * rows : (i + 1) * rows] for i in range(devices)]

    if devices == 4 and lax.axis_size("dp") == 8:
        shards = (query_weight, key_weight, value_weight, gate_weight, out_weight, down_weight)
        opened, keys = opening_exchange(heads, shards, tokens, cotangent, segment, first_gain, first_bias)
        w_qkv, w_gate, w_out, normed1_all, cot_all, field, gate, gated, grouped, group_scale, past = opened[:11]
        angles, info, decay, down_shard = opened[11:]
        mixed_low, plus, feed_terms, up_weight_grad, down_weight_grad, late = middle_exchange(
            gated, w_out, up_weight, down_shard, cot_all, tokens, second_gain, second_bias
        )
        parts, input_grad, query_sum, key_sum, value_sum, gate_sum, out_sum, up_sum, down_sum, sums = closing_exchange(
            heads,
            (
                normed1_all, up_weight_grad, down_weight_grad, feed_terms, w_out, w_qkv, w_gate,
                gate, grouped, gated, group_scale, field, past, angles, info,
                mixed_low, tokens,
            ),
            (keys, decay, first_gain.reshape(1, -1), late),
        )
        part = first_gain.shape[0] // 32
        sums = lax.dynamic_slice_in_dim(sums, (here % 2) * part, part, 1)
        norm_sums = [sums[0], sums[1], sums[2], sums[3]]
        result, input_grad, query_sum, key_sum, value_sum, gate_sum, up_sum, out_sum, down_sum = cast_all(
            plus, parts, (input_grad, query_sum, key_sum, value_sum, gate_sum, up_sum, out_sum, down_sum)
        )
    else:
        w_qkv = lax.all_gather(
            jnp.concatenate([query_weight, key_weight, value_weight], axis=1), "dp", axis=0, tiled=True
        )
        w_gate = lax.all_gather(gate_weight, "dp", axis=0, tiled=True)
        w_out = lax.all_gather(out_weight, "dp", axis=1, tiled=True)
        token_rows = tokens.astype(f32)
        unit1, scale1 = normalize(token_rows)
        normed1_all = jnp.concatenate(
            gather_pieces((unit1 * first_gain + first_bias).astype(bf16), devices), axis=0
        )
        cot_all = jnp.concatenate(gather_pieces(cotangent, devices), axis=0)
        tables = retention_tables(segment, heads, here * heads)
        field = dot_nn(normed1_all, w_qkv).astype(bf16)
        gate = dot_nn(normed1_all, w_gate).astype(bf16)
        gated, grouped, group_scale, past = retention_call(False, which, rows, heads, field, gate, tables, ())
        w_down = lax.all_gather(after(down_weight, w_out), "dp", axis=1, tiled=True)
        w_up = lax.all_gather(after(up_weight, w_down), "dp", axis=0, tiled=True)
        branch, begun, _ = scatter_sum([dot_nn(piece, w_out) for piece in per_piece(gated)])

        mixed = token_rows + branch
        unit2, scale2 = normalize(mixed)
        normed2 = (unit2 * second_gain + second_bias).astype(bf16)
        hidden_grads = per_piece(dot_nt(cot_all, after(w_down, normed2)).astype(bf16))

        def feed(piece, hidden_grad):
            value, slope = gelu_both(dot_nn(piece, w_up))
            return after((value.astype(bf16), (hidden_grad.astype(f32) * slope).astype(bf16)))

        fed_own = feed(normed2, hidden_grads[0])
        normed2_pieces = gather_pieces(normed2, devices, fed_own)
        fed = [fed_own] + [feed(piece, grad) for piece, grad in zip(normed2_pieces[1:-1], hidden_grads[1:-1])]
        fed.append(feed(after(normed2_pieces[-1], *fed), hidden_grads[-1]))
        hidden = [f[0] for f in fed]
        up_grad = [f[1] for f in fed]
        terms = [dot_nt(piece, w_up) for piece in up_grad]
        normed2_grad, _, _ = scatter_sum(terms)
        mixed_grad = cotangent.astype(f32) + normalize_back(normed2_grad, unit2, scale2, second_gain)
        gain2_grad = jnp.sum(normed2_grad * unit2, axis=0)
        bias2_grad = jnp.sum(normed2_grad, axis=0)
        mixed_low = mixed_grad.astype(bf16)
        hidden_all = jnp.concatenate(after(hidden, *terms), axis=0)
        normed2_all = jnp.concatenate(after(normed2_pieces, *terms), axis=0)
        up_grad_all = jnp.concatenate(after(up_grad, *terms), axis=0)
        feed_terms = dot_nn(hidden_all, w_down).astype(bf16)
        own_term = feed_terms[:rows].astype(f32)
        up_weight_grad = dot_tn(normed2_all, up_grad_all).astype(bf16)
        down_weight_grad = dot_tn(cot_all, hidden_all).astype(bf16)

        def summed(gradient, dimension):
            return lax.psum_scatter(
                gradient.astype(bf16), "dp", scatter_dimension=dimension, tiled=True
            ).astype(f32)

        up_sum = summed(up_weight_grad, 0)
        down_sum = summed(down_weight_grad, 0).T
        mixed_all = jnp.concatenate(gather_pieces(mixed_low, devices), axis=0)
        ffn, _, _ = scatter_sum([term.astype(f32) for term in per_piece(feed_terms)])
        result = (mixed + ffn).astype(bf16)
        gated_grad = dot_nt(mixed_all, w_out)
        raw = gate.astype(f32)
        sigmoid = 1.0 / (1.0 + jnp.exp(-raw))
        gate_grad = (gated_grad * grouped.astype(f32) * (sigmoid * (1.0 + raw * (1.0 - sigmoid)))).astype(bf16)
        back = retention_call(
            True, which, rows, heads, field, gate, tables, (gated_grad.astype(bf16), grouped, group_scale, past)
        )
        gate_sum = summed(dot_tn(normed1_all, gate_grad), 0)
        out_sum = summed(dot_tn(gated, mixed_all), 1)
        qkv_sum = summed(dot_tn(normed1_all, back), 0)
        keys_end = heads * KEY
        query_sum = qkv_sum[:, :keys_end]
        key_sum = qkv_sum[:, keys_end : 2 * keys_end]
        value_sum = qkv_sum[:, 2 * keys_end :]
        terms = [
            dot_nt(first, w_qkv) + dot_nt(second, w_gate) for first, second in zip(per_piece(back), per_piece(gate_grad))
        ]
        normed1_grad, _, _ = scatter_sum(terms)
        input_grad = (mixed_grad + normalize_back(normed1_grad, unit1, scale1, first_gain)).astype(bf16)
        gain1_grad = jnp.sum(normed1_grad * unit1, axis=0)
        bias1_grad = jnp.sum(normed1_grad, axis=0)
        norm_sums = spread_sum([gain1_grad, bias1_grad, gain2_grad, bias2_grad])
    return (
        result,
        input_grad,
        norm_sums[0],
        norm_sums[1],
        query_sum,
        key_sum,
        value_sum,
        gate_sum,
        out_sum,
        norm_sums[2],
        norm_sums[3],
        up_sum,
        down_sum,
    )


def solution(mesh):
    rows = P(("dp", "tensor"), None)
    vector = P(("dp", "tensor"))
    into = P("dp", "tensor")
    back = P("tensor", "dp")
    return jax.shard_map(
        body,
        mesh=mesh,
        in_specs=(rows, rows, P("dp"), P(), P(), into, into, into, into, back, P(), P(), into, back),
        out_specs=(rows, rows, vector, vector, into, into, into, into, back, vector, vector, into, back),
        check_vma=False,
    )
```

```python
import functools

import jax
import jax.numpy as jnp
from jax import lax
from jax.experimental import pallas as pl
from jax.experimental.pallas import tpu as pltpu
from jax.sharding import PartitionSpec as P

KEY = 256
VAL = 512
CHUNK = 256
QKV = 2 * KEY + VAL

norm_epsilon = 1e-05
group_floor = 0.5
key_scale = KEY ** (-0.5)

f32 = jnp.float32
bf16 = jnp.bfloat16


def dot_nn(left, right):
    return lax.dot_general(left, right, (((1,), (0,)), ((), ())), preferred_element_type=f32)


def dot_nt(left, right):
    return lax.dot_general(left, right, (((1,), (1,)), ((), ())), preferred_element_type=f32)


def dot_tn(left, right):
    return lax.dot_general(left, right, (((0,), (0,)), ((), ())), preferred_element_type=f32)


def tensor_permute(values, bit):
    pairs = [(i, i ^ bit) for i in range(4)]
    return lax.ppermute(values, "tensor", pairs)


def after(values, *tokens):
    return lax.optimization_barrier((values, tokens))[0]


def gather_pieces(own, devices, between=()):
    if devices != 4:
        whole = lax.all_gather(own, "tensor", axis=0, tiled=True)
        return list(jnp.split(whole, devices, axis=0))
    half = own.shape[0] // 2
    from_x = tensor_permute(own, 1)
    from_y = tensor_permute(own, 2)
    lower, upper = after((from_y[:half], from_x[half:]), *between)
    lower = tensor_permute(lower, 1)
    upper = tensor_permute(upper, 2)
    return [own, from_x, from_y, jnp.concatenate([lower, upper], axis=0)]


def scatter_sum(terms):
    if len(terms) != 4:
        stacked = jnp.concatenate([term.astype(bf16) for term in terms], axis=0)
        return lax.psum_scatter(stacked, "tensor", scatter_dimension=0, tiled=True).astype(f32), (stacked,), (stacked,)
    own, over_x, over_y, across = terms
    half = own.shape[0] // 2
    across = across.astype(bf16)
    first = tensor_permute(across[:half], 1)
    second = tensor_permute(across[half:], 2)
    over_y = jnp.concatenate([over_y[:half] + first.astype(f32), over_y[half:]], axis=0)
    over_x = jnp.concatenate([over_x[:half], over_x[half:] + second.astype(f32)], axis=0)
    by_x = tensor_permute(over_x.astype(bf16), 1)
    by_y = tensor_permute(over_y.astype(bf16), 2)
    return own + by_x.astype(f32) + by_y.astype(f32), (first, second), (by_x, by_y)


def spread_sum_kernel(tensor_devices, devices, given_ref, sum_ref, landed_ref, send_sem, recv_sem):
    here = lax.axis_index("dp") * tensor_devices + lax.axis_index("tensor")

    def partner(k):
        other = lax.rem(here + k, devices)
        return other, (lax.div(other, tensor_devices), lax.rem(other, tensor_devices))

    def copy(k):
        other, device = partner(k)
        return pltpu.make_async_remote_copy(
            src_ref=given_ref.at[other],
            dst_ref=landed_ref.at[k],
            send_sem=send_sem.at[k],
            recv_sem=recv_sem.at[k],
            device_id=device,
            device_id_type=pl.DeviceIdType.MESH,
        )

    barrier = pltpu.get_barrier_semaphore()

    @pl.loop(1, devices)
    def _(k):
        pl.semaphore_signal(barrier, inc=1, device_id=partner(k)[1], device_id_type=pl.DeviceIdType.MESH)

    pl.semaphore_wait(barrier, devices - 1)

    @pl.loop(1, devices)
    def _(k):
        copy(k).start()

    sum_ref[...] = given_ref[here]

    @pl.loop(1, devices)
    def _(k):
        copy(k).wait()
        sum_ref[...] += landed_ref[k]


def spread_sum(vectors):
    dp, tensor = lax.axis_size("dp"), lax.axis_size("tensor")
    devices = dp * tensor
    part = vectors[0].shape[0] // devices
    given = jnp.stack([v.reshape(devices, part) for v in vectors], axis=1)
    given = jnp.pad(given, ((0, 0), (0, 8 - len(vectors)), (0, 128 - part)))
    total = pl.pallas_call(
        functools.partial(spread_sum_kernel, tensor, devices),
        out_shape=jax.ShapeDtypeStruct((8, 128), f32),
        in_specs=[pl.BlockSpec(memory_space=pltpu.VMEM)],
        out_specs=pl.BlockSpec(memory_space=pltpu.VMEM),
        scratch_shapes=[
            pltpu.VMEM((devices, 8, 128), f32),
            pltpu.SemaphoreType.DMA((devices,)),
            pltpu.SemaphoreType.DMA((devices,)),
        ],
        compiler_params=pltpu.CompilerParams(collective_id=1, has_side_effects=True),
        name="spread_sum",
    )(given)
    return [total[i, :part] for i in range(len(vectors))]


def normalize(values):
    average = jnp.mean(values, axis=-1, keepdims=True)
    centred = values - average
    variance = jnp.mean(centred * centred, axis=-1, keepdims=True)
    scale = lax.rsqrt(variance + norm_epsilon)
    return centred * scale, scale


def normalize_back(normed_grad, unit, scale, gain):
    g = normed_grad * gain
    mean_g = jnp.mean(g, axis=-1, keepdims=True)
    mean_gx = jnp.mean(g * unit, axis=-1, keepdims=True)
    return scale * (g - mean_g - unit * mean_gx)


def gelu_both(values):
    inner = 0.7978845608 * (values + 0.044715 * values * values * values)
    t = jnp.tanh(inner)
    slope = 0.7978845608 * (1.0 + 3.0 * 0.044715 * values * values)
    return 0.5 * values * (1.0 + t), 0.5 * (1.0 + t) + 0.5 * values * (1.0 - t * t) * slope


def turn(block, cosine, sine):
    a = block[:, : KEY // 2]
    b = block[:, KEY // 2 :]
    return jnp.concatenate([a * cosine - b * sine, b * cosine + a * sine], axis=1)


def turn_back(block, cosine, sine):
    a = block[:, : KEY // 2]
    b = block[:, KEY // 2 :]
    return jnp.concatenate([a * cosine + b * sine, b * cosine - a * sine], axis=1)


def head_parts(field_ref, angles, heads, head):
    cosine = angles[:, : KEY // 2]
    sine = angles[:, KEY // 2 :]
    query_at = head * KEY
    key_at = (heads + head) * KEY
    value_at = 2 * heads * KEY + head * VAL
    query = turn(field_ref[:, query_at : query_at + KEY].astype(f32), cosine, sine).astype(bf16)
    key = turn(field_ref[:, key_at : key_at + KEY].astype(f32), cosine, sine)
    key = (key * key_scale).astype(bf16)
    return query, key, field_ref[:, value_at : value_at + VAL]


def retention_forward(heads, which, field_ref, gate_ref, angle_ref, info_ref, row_ref, decay_ref, gated_ref, grouped_ref, scale_ref, past_ref, state_ref):
    @pl.when(pl.program_id(0) == 0)
    def _():
        state_ref[...] = jnp.zeros_like(state_ref)

    angles = angle_ref[...]
    info = info_ref[...]
    same = info[:, 0:1] == row_ref[0]
    scales = []
    for head in range(heads):
        query, key, value = head_parts(field_ref, angles, heads, head)
        columns = slice(head * VAL, (head + 1) * VAL)
        gate = gate_ref[:, columns].astype(f32)
        into = info[:, 1 + 2 * head : 2 + 2 * head]
        onward = info[:, 2 + 2 * head : 3 + 2 * head]
        state = state_ref[head]
        past_ref[0, head] = state.astype(bf16)
        scores = dot_nt(query, key)
        weights = (jnp.where(same, decay_ref[head], 0.0) * scores).astype(bf16)
        retained = dot_nn(weights, value) + into * dot_nn(query, state.astype(bf16))
        moved = (key.astype(f32) * onward).astype(bf16)
        state_ref[head] = into[CHUNK - 1 :, :] * state + dot_tn(moved, value)
        centred = retained - jnp.mean(retained, axis=-1, keepdims=True)
        scale = lax.rsqrt(jnp.mean(centred * centred, axis=-1, keepdims=True) + group_floor)
        grouped = centred * scale
        gated = gate / (1.0 + jnp.exp(-gate)) * grouped
        gated_ref[:, columns] = gated.astype(bf16)
        grouped_ref[:, columns] = grouped.astype(bf16)
        scales.append(scale)
    lane = lax.broadcasted_iota(jnp.int32, (CHUNK, 128), 1)
    spread = jnp.zeros((CHUNK, 128), f32)
    for head in range(heads):
        spread = jnp.where(lane == head, scales[head], spread)
    scale_ref[...] = spread


def retention_backward(heads, which, field_ref, gate_ref, angle_ref, info_ref, row_ref, decay_ref, grad_ref, grouped_ref, scale_ref, past_ref, back_ref, state_ref):
    @pl.when(pl.program_id(0) == 0)
    def _():
        state_ref[...] = jnp.zeros_like(state_ref)

    angles = angle_ref[...]
    cosine = angles[:, : KEY // 2]
    sine = angles[:, KEY // 2 :]
    info = info_ref[...]
    same = info[:, 0:1] == row_ref[0]
    for head in range(heads):
        query, key, value = head_parts(field_ref, angles, heads, head)
        columns = slice(head * VAL, (head + 1) * VAL)
        gate = gate_ref[:, columns].astype(f32)
        into = info[:, 1 + 2 * head : 2 + 2 * head]
        onward = info[:, 2 + 2 * head : 3 + 2 * head]
        grouped = grouped_ref[:, columns].astype(f32)
        scale = scale_ref[:, head : head + 1]
        c = grad_ref[:, columns].astype(f32) * (gate / (1.0 + jnp.exp(-gate)))
        mean_c = jnp.mean(c, axis=-1, keepdims=True)
        mean_cx = jnp.mean(c * grouped, axis=-1, keepdims=True)
        out_grad = (scale * (c - mean_c - grouped * mean_cx)).astype(bf16)
        state = state_ref[head]
        state_low = state.astype(bf16)
        past = past_ref[0, head]
        masked = jnp.where(same, decay_ref[head], 0.0)
        weights = (masked * dot_nt(query, key)).astype(bf16)
        score_grad = (masked * dot_nt(out_grad, value)).astype(bf16)
        value_grad = dot_tn(weights, out_grad) + onward * dot_nn(key, state_low)
        query_grad = dot_nn(score_grad, key) + into * dot_nt(out_grad, past)
        key_grad = dot_tn(score_grad, query) + onward * dot_nt(value, state_low)
        moved = (query.astype(f32) * into).astype(bf16)
        state_ref[head] = into[CHUNK - 1 :, :] * state + dot_tn(moved, out_grad)
        query_at = head * KEY
        key_at = (heads + head) * KEY
        value_at = 2 * heads * KEY + head * VAL
        back_ref[:, query_at : query_at + KEY] = turn_back(query_grad, cosine, sine).astype(bf16)
        back_ref[:, key_at : key_at + KEY] = (turn_back(key_grad, cosine, sine) * key_scale).astype(bf16)
        back_ref[:, value_at : value_at + VAL] = value_grad.astype(bf16)


def retention_tables(segment, heads, first_head):
    rows = segment.shape[0]
    chunks = rows // CHUNK
    index = jnp.arange(rows, dtype=jnp.int32)
    boundary = jnp.concatenate([jnp.ones((1,), jnp.int32), (segment[1:] != segment[:-1]).astype(jnp.int32)])
    position = index - lax.cummax(jnp.where(boundary > 0, index, 0), axis=0)
    half = KEY // 2
    frequency = jnp.exp(-jnp.log(10000.0) * jnp.arange(half, dtype=f32) / half)
    angles = position.astype(f32)[:, None] * frequency[None, :]
    angles = jnp.concatenate([jnp.cos(angles), jnp.sin(angles)], axis=1)
    head_ids = (first_head + jnp.arange(heads, dtype=jnp.int32)).astype(f32)
    log_decay = jnp.log1p(-jnp.exp2(-5.0 - head_ids))
    last = segment.reshape(chunks, CHUNK)[:, -1]
    before = jnp.concatenate([jnp.full((1,), -2, jnp.int32), last[:-1]])
    offset = (index % CHUNK).astype(f32)
    linked_in = (segment == jnp.repeat(before, CHUNK)) & (segment >= 0)
    linked_on = (segment == jnp.repeat(last, CHUNK)) & (segment >= 0)
    columns = [segment.astype(f32)]
    for head in range(heads):
        columns.append(jnp.where(linked_in, jnp.exp(log_decay[head] * (offset + 1.0)), 0.0))
        columns.append(jnp.where(linked_on, jnp.exp(log_decay[head] * (CHUNK - 1.0 - offset)), 0.0))
    info = jnp.stack(columns, axis=1)
    info = jnp.pad(info, ((0, 0), (0, 128 - info.shape[1])))
    keys = jnp.where(segment >= 0, segment, -7).astype(f32).reshape(chunks, 1, CHUNK)
    distance = (jnp.arange(CHUNK)[:, None] - jnp.arange(CHUNK)[None, :]).astype(f32)
    decay = jnp.where(distance >= 0, jnp.exp(log_decay[:, None, None] * jnp.maximum(distance, 0.0)), 0.0)
    return angles, info, keys, decay


def retention_call(backward, which, piece_rows, heads, field, gate, tables, extra):
    rows = field.shape[0]
    chunks = rows // CHUNK
    angles, info, keys, decay = tables
    per_piece = piece_rows // CHUNK

    def step(i):
        return chunks - 1 - i if backward else i

    def place(i, which_ref):
        c = step(i)
        return ((c // per_piece) ^ which_ref[0]) * per_piece + c % per_piece

    def placed(width):
        return pl.BlockSpec((CHUNK, width), lambda i, w: (place(i, w), 0))

    in_specs = [
        placed(heads * QKV),
        placed(heads * VAL),
        pl.BlockSpec((CHUNK, KEY), lambda i, w: (step(i), 0)),
        pl.BlockSpec((CHUNK, 128), lambda i, w: (step(i), 0)),
        pl.BlockSpec((1, 1, CHUNK), lambda i, w: (step(i), 0, 0)),
        pl.BlockSpec((heads, CHUNK, CHUNK), lambda i, w: (0, 0, 0)),
    ]
    past_spec = pl.BlockSpec((1, heads, KEY, VAL), lambda i, w: (step(i), 0, 0, 0))
    if backward:
        in_specs += [placed(heads * VAL), placed(heads * VAL), placed(128), past_spec]
        out_specs = placed(heads * QKV)
        out_shape = jax.ShapeDtypeStruct((rows, heads * QKV), bf16)
    else:
        out_specs = [placed(heads * VAL), placed(heads * VAL), placed(128), past_spec]
        out_shape = [
            jax.ShapeDtypeStruct((rows, heads * VAL), bf16),
            jax.ShapeDtypeStruct((rows, heads * VAL), bf16),
            jax.ShapeDtypeStruct((rows, 128), f32),
            jax.ShapeDtypeStruct((chunks, heads, KEY, VAL), bf16),
        ]
    products = 15 if backward else 7
    return pl.pallas_call(
        functools.partial(retention_backward if backward else retention_forward, heads),
        grid_spec=pltpu.PrefetchScalarGridSpec(
            num_scalar_prefetch=1,
            grid=(chunks,),
            in_specs=in_specs,
            out_specs=out_specs,
            scratch_shapes=[pltpu.VMEM((heads, KEY, VAL), f32)],
        ),
        out_shape=out_shape,
        compiler_params=pltpu.CompilerParams(
            dimension_semantics=("arbitrary",), vmem_limit_bytes=48 * 1024 * 1024
        ),
        cost_estimate=pl.CostEstimate(
            flops=products * chunks * heads * 2 * CHUNK * CHUNK * CHUNK,
            bytes_accessed=(5 if backward else 4) * rows * heads * (QKV + VAL),
            transcendentals=rows * heads * VAL,
        ),
        name="retention_backward" if backward else "retention_forward",
    )(which, field, gate, angles, info, keys, decay, *extra)


MESH = pl.DeviceIdType.MESH


def opening_kernel(
    heads, query_ref, key_ref, value_ref, gate_ref, out_ref, down_ref, token_ref, cot_ref, row_ref, rate_ref, gain_ref, bias_ref,
    w_qkv_ref, w_gate_ref, w_out_ref, normed_ref, cot_all_ref, field_ref, gate_raw_ref, gated_ref, grouped_ref, scale_ref, past_ref,
    angle_ref, info_ref, decay_ref, down_turned_ref,
    w_qkv, w_gate, w_out, tall, normed, product, angles, info, decay, state, field_out, gate_out, gated_out, grouped_out,
    scale_out, past_out,
    local_sem, token_sem, out_sem, stage_sem, table_sem, up_send, up_recv, down_send, down_recv, core_send, core_recv,
    row_send, row_recv,
):
    dp = lax.axis_index("dp")
    tensor = lax.axis_index("tensor")
    z = lax.div(dp, 2)
    layers = 4
    depth = query_ref.shape[0]
    rows, width = token_ref.shape
    half = rows // 2
    above = (dp + 2, tensor)
    below = (dp - 2, tensor)
    twin = (dp + 1 - 2 * lax.rem(dp, 2), tensor)
    over_x = (dp, tensor + 1 - 2 * lax.rem(tensor, 2))
    over_y = (dp, lax.rem(tensor + 2, 4))
    keys = heads * KEY
    values = heads * VAL

    def block_of(start, count):
        return pl.ds(pl.multiple_of(start, count), count)

    def start(copies):
        for copy in copies:
            copy.start()

    def wait(copies):
        for copy in copies:
            copy.wait()

    def remote(src, dst, send, recv, device):
        return pltpu.make_async_remote_copy(
            src_ref=src, dst_ref=dst, send_sem=send, recv_sem=recv, device_id=device, device_id_type=MESH
        )

    mine = block_of(dp * depth, depth)
    local = [
        pltpu.make_async_copy(src, dst, local_sem.at[i])
        for i, (src, dst) in enumerate((
            (query_ref, w_qkv.at[mine, pl.ds(0, keys)]),
            (key_ref, w_qkv.at[mine, pl.ds(keys, keys)]),
            (value_ref, w_qkv.at[mine, pl.ds(2 * keys, values)]),
            (gate_ref, w_gate.at[mine]),
            (out_ref, tall),
        ))
    ]
    start(local)

    half_width = width // 2
    token_loads = [
        pltpu.make_async_copy(token_ref.at[pl.ds(0, half)], field_out, token_sem.at[0]),
        pltpu.make_async_copy(token_ref.at[pl.ds(half, half), pl.ds(0, half_width)], gated_out, token_sem.at[1]),
        pltpu.make_async_copy(token_ref.at[pl.ds(half, half), pl.ds(half_width, half_width)], grouped_out, token_sem.at[2]),
    ]
    start(token_loads)
    own_cot = pltpu.make_async_copy(cot_ref, cot_all_ref.at[pl.ds(0, rows)], local_sem.at[6])
    own_cot.start()

    barrier = pltpu.get_barrier_semaphore()

    def greet(device):
        pl.semaphore_signal(barrier, inc=1, device_id=device, device_id_type=MESH)

    for device in (twin, over_x, over_y):
        greet(device)
    pl.when(z < layers - 1)(lambda: greet(above))
    pl.when(z > 0)(lambda: greet(below))
    pl.semaphore_wait(barrier, 3 + (z < layers - 1).astype(jnp.int32) + (z > 0).astype(jnp.int32))
    wait(local[:4])


    groups = ((w_qkv, w_gate), (w_out,))

    def shard_copies(g, shard, send_sem, recv_sem, index, device):
        place = block_of(shard * depth, depth)
        return [
            remote(ref.at[place], ref.at[place], send_sem.at[index, i + 2 * g], recv_sem.at[index, i + 2 * g], device)
            for i, ref in enumerate(groups[g])
        ]

    def rise(g, j):
        return shard_copies(g, dp - 2 * j, up_send, up_recv, j, above)

    def sink(g, j):
        return shard_copies(g, dp + 2 * j, down_send, down_recv, j, below)

    def to_twin(g, j):
        return shard_copies(g, dp + 2 * j, core_send, core_recv, j + 3, twin)

    def from_twin(g, j):
        return shard_copies(g, twin[0] + 2 * j, core_send, core_recv, j + 3, twin)

    def wait_recv(copies):
        for copy in copies:
            copy.wait_recv()

    def wait_send(copies):
        for copy in copies:
            copy.wait_send()

    def first_step(g):
        pl.when(z < layers - 1)(lambda: start(rise(g, 0)))
        pl.when(z > 0)(lambda: start(sink(g, 0)))
        start(to_twin(g, 0))

    def step(g, j):
        @pl.when(z - j >= 0)
        def _():
            wait_recv(shard_copies(g, dp - 2 * j, up_send, up_recv, j - 1, twin))
            if j < 3:
                pl.when(z < layers - 1)(lambda: start(rise(g, j)))
            start(to_twin(g, -j))

        @pl.when(z + j < layers)
        def _():
            wait_recv(shard_copies(g, dp + 2 * j, down_send, down_recv, j - 1, twin))
            if j < 3:
                pl.when(z > 0)(lambda: start(sink(g, j)))
            start(to_twin(g, j))

    def when_end(wanted, work):
        pl.when(((z == 0) | (z == 3)) == wanted)(work)

    def twin_step(g, j):
        for signed in sorted({-j, j}):
            @pl.when((z + signed >= 0) & (z + signed < layers))
            def _():
                wait_recv(from_twin(g, signed))

    def rows_of(r, first=0, count=rows):
        return pl.ds(r * rows + first, count)

    def row_copy(index, src, dst, device):
        return remote(src, dst, row_send.at[index], row_recv.at[index], device)

    piece = 64
    cot_early = [
        row_copy(8, cot_ref.at[pl.ds(0, piece)], cot_all_ref.at[rows_of(1, 0, piece)], over_x),
        row_copy(9, cot_ref.at[pl.ds(0, piece)], cot_all_ref.at[rows_of(2, 0, piece)], over_y),
    ]
    cot_over = [
        row_copy(4, cot_ref.at[pl.ds(piece, rows - piece)], cot_all_ref.at[rows_of(1, piece, rows - piece)], over_x),
        row_copy(5, cot_ref.at[pl.ds(piece, rows - piece)], cot_all_ref.at[rows_of(2, piece, rows - piece)], over_y),
    ]

    first_step(0)
    start(cot_early)

    wait(token_loads)

    @pl.loop(0, half // 64)
    def _(i):
        place = block_of(i * 64, 64)
        plain, _ = normalize(field_out[place].astype(f32))
        normed[place] = (plain * gain_ref[...] + bias_ref[...]).astype(bf16)

    @pl.loop(0, half // 64)
    def _(i):
        place = block_of(i * 64, 64)
        both = jnp.concatenate([gated_out[place], grouped_out[place]], axis=1)
        plain, _ = normalize(both.astype(f32))
        normed[block_of(half + i * 64, 64)] = (plain * gain_ref[...] + bias_ref[...]).astype(bf16)

    over = [
        row_copy(0, normed.at[rows_of(0)], normed.at[rows_of(1)], over_x),
        row_copy(1, normed.at[rows_of(0)], normed.at[rows_of(2)], over_y),
    ]
    onward = [
        row_copy(2, normed.at[rows_of(2, 0, half)], normed.at[rows_of(3, 0, half)], over_x),
        row_copy(3, normed.at[rows_of(1, half, half)], normed.at[rows_of(3, half, half)], over_y),
    ]
    cot_onward = [
        row_copy(6, cot_all_ref.at[rows_of(2, 0, half)], cot_all_ref.at[rows_of(3, 0, half)], over_x),
        row_copy(7, cot_all_ref.at[rows_of(1, half, half)], cot_all_ref.at[rows_of(3, half, half)], over_y),
    ]
    start(over)

    local[4].wait()
    w_out[mine, :] = tall[...].T
    down_load = pltpu.make_async_copy(down_ref, tall, local_sem.at[4])
    down_load.start()

    half_key = KEY // 2
    lanes = lax.broadcasted_iota(jnp.int32, (CHUNK, half_key), 1).astype(f32)
    frequency = jnp.exp(lanes * (-9.210340371976184 / half_key))
    chunks = 4 * rows // CHUNK

    @pl.loop(0, chunks)
    def _(c):
        seat = block_of(c * CHUNK, CHUNK)
        diagonal = lax.broadcasted_iota(jnp.int32, (CHUNK, CHUNK), 0) == lax.broadcasted_iota(jnp.int32, (CHUNK, CHUNK), 1)
        own = jnp.sum(jnp.where(diagonal, jnp.maximum(row_ref[c], -1.0), 0.0), axis=1, keepdims=True)
        info[seat, :] = jnp.broadcast_to(own, (CHUNK, 128))
        ranked = jnp.where(own < 0, 3.0, own)
        before = jnp.zeros((CHUNK, 1), f32)
        for other in range(chunks):
            seen = row_ref[other]
            seen = jnp.where(seen < 0, 3.0, seen)
            before = before + jnp.sum((seen < ranked).astype(f32), axis=1, keepdims=True)
        index = lax.broadcasted_iota(jnp.int32, (CHUNK, 1), 0) + c * CHUNK
        turned = (index.astype(f32) - before) * frequency
        angles[seat, 0:half_key] = jnp.cos(turned)
        angles[seat, half_key:KEY] = jnp.sin(turned)

    distance = lax.broadcasted_iota(jnp.int32, (CHUNK, CHUNK), 0) - lax.broadcasted_iota(jnp.int32, (CHUNK, CHUNK), 1)
    span = jnp.maximum(distance, 0).astype(f32)
    for head in range(heads):
        decay[head] = jnp.where(distance >= 0, jnp.exp(rate_ref[head : head + 1, 0:1] * span), 0.0)
    down_load.wait()
    gate_out[...] = tall[...].T
    table_outs = [
        pltpu.make_async_copy(gate_out, down_turned_ref, table_sem.at[3]),
        pltpu.make_async_copy(angles, angle_ref, table_sem.at[0]),
        pltpu.make_async_copy(decay, decay_ref, table_sem.at[1]),
    ]
    start(table_outs)


    at_end = (z == 0) | (z == 3)

    def seen_from_end(index):
        return jnp.where(z >= 2, 3 - index, index)

    order = [z, jnp.where(at_end, seen_from_end(1), seen_from_end(0)), seen_from_end(2), seen_from_end(3)]

    def project(r, s):
        deep = block_of(order[s] * 2 * depth, 2 * depth)

        @pl.loop(0, (2 * keys + values) // 512)
        def _(j):
            tile = block_of(j * 512, 512)
            more = dot_nn(normed[rows_of(r), deep], w_qkv[deep, tile])
            product[rows_of(r), tile] = more if s == 0 else product[rows_of(r), tile] + more

        @pl.loop(0, values // 512)
        def _(j):
            tile = block_of(j * 512, 512)
            more = dot_nn(normed[rows_of(r), deep], w_gate[deep, tile])
            place = block_of(2 * keys + values + j * 512, 512)
            product[rows_of(r), place] = more if s == 0 else product[rows_of(r), place] + more


    per_piece = rows // CHUNK

    def chunk_place(c):
        piece = lax.div(c, per_piece)
        low = lax.rem(lax.rem(piece, 2) + lax.rem(tensor, 2), 2)
        high = lax.rem(lax.div(piece, 2) + lax.div(tensor, 2), 2)
        return (2 * high + low) * per_piece + lax.rem(c, per_piece)

    def chunk_outs(c):
        place = block_of(chunk_place(c) * CHUNK, CHUNK)
        pairs = (
            (field_out, field_ref.at[place]),
            (gate_out, gate_raw_ref.at[place]),
            (gated_out, gated_ref.at[place]),
            (grouped_out, grouped_ref.at[place]),
            (scale_out, scale_ref.at[place]),
            (past_out, past_ref.at[c]),
        )
        return [pltpu.make_async_copy(src, dst, stage_sem.at[i]) for i, (src, dst) in enumerate(pairs)]

    def retention(between):
        state[...] = jnp.zeros_like(state)

        @pl.loop(0, chunks)
        def _(c):
            place = block_of(chunk_place(c) * CHUNK, CHUNK)
            seat = block_of(c * CHUNK, CHUNK)
            cosine = angles[seat, 0:half_key]
            sine = angles[seat, half_key:KEY]
            own = info[seat, 0:1]
            same = own == row_ref[c]
            entering = (own == row_ref[jnp.maximum(c - 1, 0)][:, CHUNK - 1 :]) & (c > 0)
            leaving = own == row_ref[c][:, CHUNK - 1 :]
            offset = lax.broadcasted_iota(jnp.int32, (CHUNK, 1), 0).astype(f32)
            lane = lax.broadcasted_iota(jnp.int32, (CHUNK, 128), 1)
            facts = jnp.where(lane == 0, own, 0.0)
            scales = jnp.zeros((CHUNK, 128), f32)

            for head in range(heads):
                rate = rate_ref[head : head + 1, 0:1]
                into = jnp.where(entering, jnp.exp(rate * (offset + 1.0)), 0.0)
                onto = jnp.where(leaving, jnp.exp(rate * (CHUNK - 1.0 - offset)), 0.0)
                facts = jnp.where(lane == 1 + 2 * head, into, facts)
                facts = jnp.where(lane == 2 + 2 * head, onto, facts)
                query_raw = product[place, pl.ds(head * KEY, KEY)]
                key_raw = product[place, pl.ds(keys + head * KEY, KEY)]
                value = product[place, pl.ds(2 * keys + head * VAL, VAL)].astype(bf16)
                gate = product[place, pl.ds(2 * keys + values + head * VAL, VAL)]
                query_raw = query_raw.astype(bf16)
                key_raw = key_raw.astype(bf16)
                query = turn(query_raw.astype(f32), cosine, sine).astype(bf16)
                key = (turn(key_raw.astype(f32), cosine, sine) * key_scale).astype(bf16)
                memory = state[head]
                memory_low = memory.astype(bf16)
                scores = dot_nt(query, key)
                weights = (jnp.where(same, decay[head], 0.0) * scores).astype(bf16)
                retained = dot_nn(weights, value) + into * dot_nn(query, memory_low)
                moved = (key.astype(f32) * onto).astype(bf16)
                state[head] = into[CHUNK - 1 :, :] * memory + dot_tn(moved, value)
                centred = retained - jnp.mean(retained, axis=-1, keepdims=True)
                scale = lax.rsqrt(jnp.mean(centred * centred, axis=-1, keepdims=True) + group_floor)
                grouped = centred * scale
                columns = pl.ds(head * VAL, VAL)
                if head == 0:
                    @pl.when(c > 0)
                    def _():
                        wait(chunk_outs(c - 1))

                field_out[:, pl.ds(head * KEY, KEY)] = query_raw
                field_out[:, pl.ds(keys + head * KEY, KEY)] = key_raw
                field_out[:, pl.ds(2 * keys + head * VAL, VAL)] = value
                gate_out[:, columns] = gate.astype(bf16)
                past_out[head] = memory_low
                gated_out[:, columns] = (gate / (1.0 + jnp.exp(-gate)) * grouped).astype(bf16)
                grouped_out[:, columns] = grouped.astype(bf16)
                scales = jnp.where(lane == head, scale, scales)
            info[seat, :] = facts
            scale_out[...] = scales
            start(chunk_outs(c))
            between(c)

        wait(chunk_outs(chunks - 1))


    twin_step(0, 0)
    project(0, 0)
    step(0, 1)
    twin_step(0, 1)
    project(0, 1)
    wait_recv(over)
    start(onward)
    start(cot_over)
    for r in (1, 2):
        for s in (0, 1):
            project(r, s)
    step(0, 2)
    first_step(1)
    twin_step(0, 2)
    for r in (0, 1, 2):
        project(r, 2)
    wait_recv(onward)
    normed_out = pltpu.make_async_copy(normed, normed_ref, local_sem.at[7])
    normed_out.start()
    for s in (0, 1, 2):
        project(3, s)
    when_end(False, lambda: step(1, 1))
    step(0, 3)
    twin_step(0, 3)
    w_outs = [
        pltpu.make_async_copy(w_qkv, w_qkv_ref, out_sem.at[0]),
        pltpu.make_async_copy(w_gate, w_gate_ref, out_sem.at[1]),
    ]
    start(w_outs)
    project(0, 3)
    project(1, 3)
    def hand_on():
        wait_recv(cot_early + cot_over)
        start(cot_onward)

    when_end(False, lambda: step(1, 2))
    when_end(False, hand_on)
    project(2, 3)
    project(3, 3)
    when_end(True, hand_on)

    def between(c):
        @pl.when((c == 1) & at_end)
        def _():
            step(1, 1)

        @pl.when((c == 4) & at_end)
        def _():
            step(1, 2)

    wait(table_outs)
    retention(between)
    info_out = pltpu.make_async_copy(info, info_ref, table_sem.at[2])
    info_out.start()

    def layer_out(s):
        place = block_of(order[s] * 2 * depth, 2 * depth)
        return pltpu.make_async_copy(w_out.at[place], w_out_ref.at[place], out_sem.at[2 + s])

    for j in range(3):
        twin_step(1, j)
    for s in range(3):
        layer_out(s).start()
    step(1, 3)
    twin_step(1, 3)
    layer_out(3).start()
    wait_recv(cot_onward)

    wait_send(over + onward + cot_early + cot_over + cot_onward)
    for g in range(2):
        for j in range(3):
            pl.when((z < layers - 1) & (z - j >= 0))(lambda: wait_send(rise(g, j)))
            pl.when((z > 0) & (z + j < layers))(lambda: wait_send(sink(g, j)))
        for j in range(-3, 4):
            pl.when((z + j >= 0) & (z + j < layers))(lambda: wait_send(to_twin(g, j)))
    wait(w_outs + [normed_out, own_cot, info_out] + [layer_out(s) for s in range(4)])


def opening_exchange(heads, shards, tokens, cotangent, segment, gain, bias):
    dp = lax.axis_size("dp")
    depth, keys = shards[0].shape
    values = shards[2].shape[1]
    unit = shards[4].shape[0]
    token_rows, width = tokens.shape
    rows = 4 * token_rows
    chunks = rows // CHUNK
    anywhere = pl.BlockSpec(memory_space=pl.ANY)
    in_vmem = pl.BlockSpec(memory_space=pltpu.VMEM)
    sem = pltpu.SemaphoreType.DMA
    vmem = pltpu.VMEM
    here = lax.axis_index("tensor") * heads
    head_ids = (here + jnp.arange(8, dtype=jnp.int32)).astype(f32)
    rates = jnp.broadcast_to(jnp.log1p(-jnp.exp2(-5.0 - head_ids))[:, None], (8, 128))
    row_segment = jnp.where(segment >= 0, segment, -7).astype(f32).reshape(chunks, 1, CHUNK)
    results = pl.pallas_call(
        functools.partial(opening_kernel, heads),
        out_shape=[
            jax.ShapeDtypeStruct((dp * depth, 2 * keys + values), bf16),
            jax.ShapeDtypeStruct((dp * depth, values), bf16),
            jax.ShapeDtypeStruct((dp * depth, unit), bf16),
            jax.ShapeDtypeStruct((rows, width), bf16),
            jax.ShapeDtypeStruct((rows, width), bf16),
            jax.ShapeDtypeStruct((rows, 2 * keys + values), bf16),
            jax.ShapeDtypeStruct((rows, values), bf16),
            jax.ShapeDtypeStruct((rows, values), bf16),
            jax.ShapeDtypeStruct((rows, values), bf16),
            jax.ShapeDtypeStruct((rows, 128), f32),
            jax.ShapeDtypeStruct((chunks, heads, KEY, VAL), bf16),
            jax.ShapeDtypeStruct((rows, KEY), f32),
            jax.ShapeDtypeStruct((rows, 128), f32),
            jax.ShapeDtypeStruct((heads, CHUNK, CHUNK), f32),
            jax.ShapeDtypeStruct((depth, unit), bf16),
        ],
        in_specs=[anywhere] * 8 + [in_vmem] * 4,
        out_specs=[anywhere] * 15,
        scratch_shapes=[
            vmem((dp * depth, 2 * keys + values), bf16),
            vmem((dp * depth, values), bf16),
            vmem((dp * depth, unit), bf16),
            vmem((unit, depth), bf16),
            vmem((rows, width), bf16),
            vmem((rows, 2 * keys + 2 * values), f32),
            vmem((rows, KEY), f32),
            vmem((rows, 128), f32),
            vmem((heads, CHUNK, CHUNK), f32),
            vmem((heads, KEY, VAL), f32),
            vmem((CHUNK, 2 * keys + values), bf16),
            vmem((CHUNK, values), bf16),
            vmem((CHUNK, values), bf16),
            vmem((CHUNK, values), bf16),
            vmem((CHUNK, 128), f32),
            vmem((heads, KEY, VAL), bf16),
            sem((8,)), sem((3,)), sem((6,)), sem((6,)), sem((4,)),
            sem((3, 3)), sem((3, 3)), sem((3, 3)), sem((3, 3)), sem((7, 3)), sem((7, 3)), sem((10,)), sem((10,)),
        ],
        compiler_params=pltpu.CompilerParams(
            collective_id=2, has_side_effects=True, vmem_limit_bytes=63_400_000
        ),
        name="opening_exchange",
    )(*shards, tokens, cotangent, row_segment, rates, gain.reshape(1, width), bias.reshape(1, width))
    return results, row_segment


def middle_kernel(
    gated_ref, w_out_ref, up_ref, down_ref, cot_ref, token_ref, gain_ref, bias_ref,
    low_ref, plus_ref, feed_ref, up_grad_out, down_grad_out, late_ref,
    big, units, columns, staged, terms, half_in, full_in, mixed, plus, total,
    load_sem, column_sem, staged_sem, feed_sem, out_sem, up_send, up_recv, below_send, below_recv, core_send, core_recv,
    row_send, row_recv, half_send, half_recv, full_send, full_recv, half_free, full_free, big_free,
):
    dp = lax.axis_index("dp")
    tensor = lax.axis_index("tensor")
    z = lax.div(dp, 2)
    layers = 4
    rows = token_ref.shape[0]
    half = rows // 2
    width = token_ref.shape[1]
    unit = units.shape[2]
    depth = up_ref.shape[0]
    above = (dp + 2, tensor)
    below = (dp - 2, tensor)
    twin = (dp + 1 - 2 * lax.rem(dp, 2), tensor)
    over_x = (dp, tensor + 1 - 2 * lax.rem(tensor, 2))
    over_y = (dp, lax.rem(tensor + 2, 4))
    sides = (over_x, over_y)

    def block_of(start, count):
        return pl.ds(pl.multiple_of(start, count), count)

    def start(copies):
        for copy in copies:
            copy.start()

    def wait(copies):
        for copy in copies:
            copy.wait()

    def remote(src, dst, send, recv, device):
        return pltpu.make_async_remote_copy(
            src_ref=src, dst_ref=dst, send_sem=send, recv_sem=recv, device_id=device, device_id_type=MESH
        )

    mine = block_of(dp * depth, depth)
    shard_loads = [
        pltpu.make_async_copy(down_ref, units.at[3, mine], load_sem.at[0]),
        pltpu.make_async_copy(up_ref, units.at[2, mine], load_sem.at[1]),
    ]
    first_loads = [pltpu.make_async_copy(w_out_ref, units.at[1], load_sem.at[3])] + [
        pltpu.make_async_copy(gated_ref.at[pl.ds(r * rows, rows)], units.at[0, pl.ds(r * rows, rows)], load_sem.at[8 + r])
        for r in (3, 1, 2, 0)
    ]
    token_load = pltpu.make_async_copy(token_ref, plus, load_sem.at[5])
    cot_load = pltpu.make_async_copy(cot_ref, big, load_sem.at[6])
    start(shard_loads)
    start(first_loads)
    token_load.start()
    cot_load.start()

    barrier = pltpu.get_barrier_semaphore()

    def greet(device):
        pl.semaphore_signal(barrier, inc=1, device_id=device, device_id_type=MESH)

    for device in (twin, over_x, over_y):
        greet(device)
    pl.when(z < layers - 1)(lambda: greet(above))
    pl.when(z > 0)(lambda: greet(below))
    pl.semaphore_wait(barrier, 3 + (z < layers - 1).astype(jnp.int32) + (z > 0).astype(jnp.int32))


    def shard_copy(a, shard, send_sem, recv_sem, index, device):
        place = block_of(shard * depth, depth)
        ref = units.at[3 - a, place]
        return remote(ref, ref, send_sem.at[a, index], recv_sem.at[a, index], device)

    def rise(a, j):
        return shard_copy(a, dp - 2 * j, up_send, up_recv, j, above)

    def sink(a, j):
        return shard_copy(a, dp + 2 * j, below_send, below_recv, j, below)

    def to_twin(a, j):
        return shard_copy(a, dp + 2 * j, core_send, core_recv, j + 3, twin)

    def from_twin(a, j):
        return shard_copy(a, twin[0] + 2 * j, core_send, core_recv, j + 3, twin)

    def first_step(a):
        shard_loads[a].wait()
        pl.when(z < layers - 1)(lambda: rise(a, 0).start())
        pl.when(z > 0)(lambda: sink(a, 0).start())
        to_twin(a, 0).start()

    def step(a, j):
        @pl.when(z - j >= 0)
        def _():
            shard_copy(a, dp - 2 * j, up_send, up_recv, j - 1, twin).wait_recv()
            if j < 3:
                pl.when(z < layers - 1)(lambda: rise(a, j).start())
            to_twin(a, -j).start()

        @pl.when(z + j < layers)
        def _():
            shard_copy(a, dp + 2 * j, below_send, below_recv, j - 1, twin).wait_recv()
            if j < 3:
                pl.when(z > 0)(lambda: sink(a, j).start())
            to_twin(a, j).start()

    def gathered(a):
        for j in range(-3, 4):
            @pl.when((z + j >= 0) & (z + j < layers))
            def _():
                from_twin(a, j).wait_recv()


    def rows_of(r, first=0, count=rows):
        return pl.ds(r * rows + first, count)

    halves = [
        remote(terms.at[2, pl.ds(0, half)], half_in.at[0], half_send.at[0], half_recv.at[0], over_x),
        remote(terms.at[2, pl.ds(half, half)], half_in.at[1], half_send.at[1], half_recv.at[1], over_y),
    ]

    def part_copy(index, term, first, device, count=half):
        place = pl.ds(first, count)
        return remote(
            terms.at[term, place], full_in.at[term, place], full_send.at[index], full_recv.at[index], device
        )

    plain_parts = [part_copy(0, 0, 0, over_x), part_copy(1, 1, half, over_y)]
    quarter = half // 2
    grown_parts = [
        part_copy(2, 0, half, over_x, quarter),
        part_copy(3, 1, 0, over_y, quarter),
        part_copy(4, 0, half + quarter, over_x, quarter),
        part_copy(5, 1, quarter, over_y, quarter),
    ]
    fulls = plain_parts + grown_parts
    lower, upper = (0, half), (half, half)

    def row_copy(index, source, first, target, device):
        return remote(
            big.at[rows_of(source, *first)], big.at[rows_of(target, *first)],
            row_send.at[index], row_recv.at[index], device,
        )

    early = [row_copy(0, 0, lower, 1, over_x), row_copy(1, 0, upper, 2, over_y)]
    across = [row_copy(2, 2, upper, 3, over_x), row_copy(3, 1, lower, 3, over_y)]
    late = [row_copy(4, 0, upper, 1, over_x), row_copy(5, 0, lower, 2, over_y)]

    def send_halves(stage):
        for i, copy in enumerate(halves):
            if stage == 1:
                pl.semaphore_wait(half_free.at[i], 1)
            copy.start()

    def take_halves(stage):
        for copy in halves:
            copy.wait_recv()
        for term, first, slot in ((1, 0, 0), (0, half, 1)):
            @pl.loop(0, half // 64)
            def _(i):
                place = block_of(first + i * 64, 64)
                grown = terms[term, place].astype(f32) + half_in[slot, block_of(i * 64, 64)].astype(f32)
                terms[term, place] = grown.astype(bf16)

        for i, copy in enumerate(grown_parts):
            if stage == 0 and i < 2:
                pl.semaphore_signal(half_free.at[i], inc=1, device_id=sides[i], device_id_type=MESH)
            copy.start()

    def send_plain(stage, i):
        if stage == 1:
            pl.semaphore_wait(full_free.at[i], 1)
        plain_parts[i].start()

    def slot_of(r):
        return (3, 0, 1, 2)[r]

    def branch_term(r):
        @pl.loop(0, width // 256)
        def _(j):
            tile = block_of(j * 256, 256)
            terms[slot_of(r), :, tile] = dot_nt(units[0, rows_of(r)], units[1, tile]).astype(bf16)

    def feed_grads(r):
        @pl.loop(0, unit // 256)
        def _(j):
            tile = block_of(j * 256, 256)
            units[4, rows_of(r), tile] = dot_nn(big[rows_of(r)], units[3, :, tile]).astype(bf16)

    def feed(r):
        @pl.loop(0, unit // 256)
        def _(j):
            tile = block_of(j * 256, 256)
            value, slope = gelu_both(dot_nn(big[rows_of(r)], units[2, :, tile]))
            units[0, rows_of(r), tile] = value.astype(bf16)
            units[1, rows_of(r), tile] = (units[4, rows_of(r), tile].astype(f32) * slope).astype(bf16)

    def back_term(r):
        @pl.loop(0, width // 256)
        def _(j):
            tile = block_of(j * 256, 256)
            terms[slot_of(r), :, tile] = dot_nt(units[1, rows_of(r)], units[2, tile]).astype(bf16)


    first_step(0)
    wait(first_loads[:2])
    branch_term(3)
    send_halves(0)
    wait(first_loads[2:])
    step(0, 1)
    branch_term(1)
    send_plain(0, 0)
    branch_term(2)
    send_plain(0, 1)
    step(0, 2)
    first_step(1)
    take_halves(0)
    branch_term(0)
    step(0, 3)
    cot_load.wait()
    gathered(0)
    step(1, 1)
    feed_grads(0)
    feed_grads(1)
    step(1, 2)
    feed_grads(2)
    feed_grads(3)
    for side in sides:
        pl.semaphore_signal(big_free, inc=1, device_id=side, device_id_type=MESH)
    step(1, 3)
    gathered(1)
    token_load.wait()
    pl.semaphore_wait(big_free, 2)

    def second_norm(i):
        place = block_of(i * 64, 64)
        value = plus[place].astype(f32) + terms[3, place].astype(f32)
        value = value + full_in[0, place].astype(f32) + full_in[1, place].astype(f32)
        mixed[place] = value
        plain, _ = normalize(value)
        big[place] = (plain * gain_ref[...] + bias_ref[...]).astype(bf16)

    for copy in plain_parts + grown_parts[:2]:
        copy.wait_recv()
    pl.loop(0, quarter // 64)(second_norm)
    pl.loop(half // 64, (half + quarter) // 64)(second_norm)
    for copy in grown_parts[2:]:
        copy.wait_recv()
    pl.loop(quarter // 64, half // 64)(second_norm)
    early[0].start()
    pl.loop((half + quarter) // 64, rows // 64)(second_norm)
    early[1].start()
    for i, side in enumerate(sides):
        pl.semaphore_signal(full_free.at[i], inc=1, device_id=side, device_id_type=MESH)
    feed(0)
    for copy in halves + fulls:
        copy.wait_send()
    back_term(0)
    for copy in early:
        copy.wait_recv()
    start(across)
    start(late)

    def cot_columns(t):
        return pltpu.make_async_copy(cot_ref.at[:, pl.ds(t * 512, 512)], columns.at[t % 2], column_sem.at[t])

    cot_columns(0).start()
    cot_columns(1).start()
    for copy in across:
        copy.wait_recv()
    feed(3)
    back_term(3)
    send_halves(1)
    for copy in late:
        copy.wait_recv()
    feed(1)
    back_term(1)
    send_plain(1, 0)
    feed(2)
    back_term(2)
    send_plain(1, 1)
    take_halves(1)

    def staged_out(out, t, slot):
        return pltpu.make_async_copy(staged.at[slot], out.at[pl.ds(t * 512, 512)], staged_sem.at[slot])

    def weight_grad(out, t, left_of, right):
        for j in range(unit // 256):
            tile = pl.ds(j * 256, 256)
            product = None
            for place in (pl.ds(0, 2 * rows), pl.ds(2 * rows, 2 * rows)):
                more = dot_tn(left_of(place), units[right, place, tile])
                product = more if product is None else product + more
            staged[t % 2, :, tile] = product.astype(bf16)
        staged_out(out, t, t % 2).start()

    for t in range(4):
        cot_columns(t).wait()
        if t >= 2:
            staged_out(down_grad_out, t - 2, t % 2).wait()
        weight_grad(down_grad_out, t, lambda place: columns[t % 2, place], 0)
        if t < 2:
            cot_columns(t + 2).start()
    for t in range(4):
        if t < 2:
            staged_out(down_grad_out, t + 2, t % 2).wait()
        else:
            staged_out(up_grad_out, t - 2, t % 2).wait()
        weight_grad(up_grad_out, t, lambda place: big[place, pl.ds(t * 512, 512)], 1)

    def feed_out(t):
        return pltpu.make_async_copy(columns.at[t % 2], feed_ref.at[:, pl.ds(t * 512, 512)], feed_sem.at[t % 2])

    for t in range(4):
        if t >= 2:
            feed_out(t - 2).wait()

        @pl.loop(0, 4)
        def _(r):
            place = block_of(r * rows, rows)
            columns[t % 2, place] = dot_nt(units[0, place], units[3, pl.ds(t * 512, 512)]).astype(bf16)

        feed_out(t).start()

        @pl.loop(0, rows // 64)
        def _(i):
            place = block_of(i * 64, 64)
            tile = pl.ds(t * 512, 512)
            plus[place, tile] = (mixed[place, tile] + columns[t % 2, place].astype(f32)).astype(bf16)

    plus_out = pltpu.make_async_copy(plus, plus_ref, out_sem.at[0])
    plus_out.start()
    for copy in halves:
        copy.wait_send()
    cot_own = pltpu.make_async_copy(cot_ref.at[pl.ds(0, rows)], terms.at[2], load_sem.at[7])
    cot_own.start()
    total[...] = jnp.zeros_like(total)
    cot_own.wait()

    def second_norm_back(i):
        place = block_of(i * 64, 64)
        grad = terms[3, place].astype(f32) + full_in[0, place].astype(f32) + full_in[1, place].astype(f32)
        plain, scale = normalize(mixed[place])
        back = terms[2, place].astype(f32) + normalize_back(grad, plain, scale, gain_ref[...])
        full_in[0, place] = back.astype(bf16)
        total[0:1, :] += jnp.sum(grad * plain, axis=0, keepdims=True)
        total[1:2, :] += jnp.sum(grad, axis=0, keepdims=True)

    for copy in plain_parts + grown_parts[:2]:
        copy.wait_recv()
    pl.loop(0, quarter // 64)(second_norm_back)
    pl.loop(half // 64, (half + quarter) // 64)(second_norm_back)
    for copy in grown_parts[2:]:
        copy.wait_recv()
    pl.loop(quarter // 64, half // 64)(second_norm_back)
    pl.loop((half + quarter) // 64, rows // 64)(second_norm_back)
    low_out = pltpu.make_async_copy(full_in.at[0], low_ref, out_sem.at[1])
    low_out.start()
    late_ref[...] = total[...]

    for t in (2, 3):
        staged_out(up_grad_out, t, t % 2).wait()
        feed_out(t).wait()
    for copy in fulls + early + across + late:
        copy.wait_send()
    for a in range(2):
        for j in range(3):
            pl.when((z < layers - 1) & (z - j >= 0))(lambda: rise(a, j).wait_send())
            pl.when((z > 0) & (z + j < layers))(lambda: sink(a, j).wait_send())
        for j in range(-3, 4):
            pl.when((z + j >= 0) & (z + j < layers))(lambda: to_twin(a, j).wait_send())
    plus_out.wait()
    low_out.wait()


def middle_exchange(gated, w_out, up_shard, down_shard, cot_all, tokens, gain, bias):
    token_rows, width = tokens.shape
    rows = 4 * token_rows
    unit = gated.shape[1]
    anywhere = pl.BlockSpec(memory_space=pl.ANY)
    in_vmem = pl.BlockSpec(memory_space=pltpu.VMEM)
    sem = pltpu.SemaphoreType.DMA
    regular = pltpu.SemaphoreType.REGULAR
    vmem = pltpu.VMEM
    return pl.pallas_call(
        middle_kernel,
        out_shape=[
            jax.ShapeDtypeStruct((token_rows, width), bf16),
            jax.ShapeDtypeStruct((token_rows, width), bf16),
            jax.ShapeDtypeStruct((rows, width), bf16),
            jax.ShapeDtypeStruct((width, unit), bf16),
            jax.ShapeDtypeStruct((width, unit), bf16),
            jax.ShapeDtypeStruct((2, width), f32),
        ],
        in_specs=[anywhere] * 6 + [in_vmem] * 2,
        out_specs=[anywhere] * 5 + [in_vmem],
        scratch_shapes=[
            vmem((rows, width), bf16),
            vmem((5, rows, unit), bf16),
            vmem((2, rows, 512), bf16),
            vmem((2, 512, unit), bf16),
            vmem((4, token_rows, width), bf16),
            vmem((2, token_rows // 2, width), bf16),
            vmem((2, token_rows, width), bf16),
            vmem((token_rows, width), f32),
            vmem((token_rows, width), bf16),
            vmem((2, width), f32),
            sem((12,)), sem((4,)), sem((2,)), sem((2,)), sem((2,)),
            sem((2, 3)), sem((2, 3)), sem((2, 3)), sem((2, 3)), sem((2, 7)), sem((2, 7)),
            sem((6,)), sem((6,)), sem((2,)), sem((2,)), sem((6,)), sem((6,)),
            regular((2,)), regular((2,)), regular,
        ],
        compiler_params=pltpu.CompilerParams(
            collective_id=4, has_side_effects=True, vmem_limit_bytes=63_400_000
        ),
        name="middle_exchange",
    )(gated, w_out, up_shard, down_shard, cot_all, tokens, gain.reshape(1, width), bias.reshape(1, width))


def closing_kernel(
    heads,
    normed1_ref, up_ref, down_ref, feed_ref, w_out_ref, w_qkv_ref, w_gate_ref,
    gate_ref, grouped_ref, gated_ref, scale_ref, field_ref, past_ref, angle_ref, info_ref,
    low_ref, token_ref, row_ref, decay_ref, gain_ref, late_ref,
    result_ref, grad_ref, query_out, key_out, value_out, gate_out, out_out, up_out, down_out, sums_ref,
    big, units, columns, terms, half_in, full_in, products, twin_in, line_in,
    state_ref, past_in, scale_in, angle_in, info_in, given, landed, total,
    unit_sem, column_sem, chunk_sem, out_sem, mixed_sem, over_send, over_recv, onward_send, onward_recv,
    half_send, half_recv, full_send, full_recv, twin_send, twin_recv, line_send, line_recv, sum_send, sum_recv,
    twin_free, line_free, half_free, full_free,
):
    dp = lax.axis_index("dp")
    tensor = lax.axis_index("tensor")
    z = lax.div(dp, 2)
    core = lax.rem(dp, 2)
    rows = token_ref.shape[0]
    half = rows // 2
    width = token_ref.shape[1]
    unit = units.shape[2]
    depth = columns.shape[2] // 2
    at_end = (z == 0) | (z == 3)
    upper = z >= 2
    twin = (dp + 1 - 2 * core, tensor)
    over_x = (dp, tensor + 1 - 2 * lax.rem(tensor, 2))
    over_y = (dp, lax.rem(tensor + 2, 4))
    here = dp * 4 + tensor
    peers = 32
    last = 5

    def layer(index):
        return (2 * index + core, tensor)

    def seen(index):
        return jnp.where(upper, 3 - index, index)

    end = layer(seen(0))
    near = layer(seen(1))
    opposite = layer(seen(2))
    targets = [seen(3), seen(2), jnp.where(at_end, seen(1), seen(0)), z]

    def remote(src, dst, send, recv, device):
        return pltpu.make_async_remote_copy(
            src_ref=src, dst_ref=dst, send_sem=send, recv_sem=recv, device_id=device, device_id_type=MESH
        )

    def block_of(start, count):
        return pl.ds(pl.multiple_of(start, count), count)


    def whole(index, ref, sem):
        return [pltpu.make_async_copy(ref, units.at[index], unit_sem.at[sem])]

    def part(index, ref, start, sem):
        return [pltpu.make_async_copy(ref.at[:, pl.ds(start, unit)], units.at[index], unit_sem.at[sem])]

    def start(copies):
        for copy in copies:
            copy.start()

    def wait(copies):
        for copy in copies:
            copy.wait()

    out_load = whole(3, w_out_ref, 4)
    feed_load = [
        pltpu.make_async_copy(feed_ref.at[pl.ds((i + 1) * rows, rows)], terms.at[i], unit_sem.at[i]) for i in range(3)
    ]
    gated_load = whole(2, gated_ref, 6)
    w_gate_load = whole(3, w_gate_ref, 7)
    w_value_load = part(2, w_qkv_ref, unit, 8)
    w_key_load = part(1, w_qkv_ref, 0, 9)

    def wait_recv(copies):
        for copy in copies:
            copy.wait_recv()

    def wait_send(copies):
        for copy in copies:
            copy.wait_send()


    sources = [up_ref, down_ref, None, normed1_ref, normed1_ref, normed1_ref]

    def given_copy(r, k):
        place = block_of(targets[k] * 2 * depth, 2 * depth)
        return pltpu.make_async_copy(sources[r].at[place], products.at[r, k], column_sem.at[4 * r + k])

    def column_copy(r, k):
        place = block_of(targets[k] * 2 * depth, 2 * depth)
        return pltpu.make_async_copy(sources[r].at[:, place], columns.at[k % 2], column_sem.at[k])

    def prefetch(r):
        column_copy(r, 0).start()
        column_copy(r, 1).start()

    mine = block_of(core * depth, depth)
    theirs = block_of((1 - core) * depth, depth)

    def to_twin(r, k):
        return remote(
            products.at[r % 2, k, theirs], twin_in.at[k % 2], twin_send.at[r % 2, k], twin_recv.at[k % 2], twin
        )

    def along(r, k, slot, device):
        return remote(
            products.at[r % 2, k, mine], line_in.at[slot], line_send.at[r % 2, k], line_recv.at[slot], device
        )

    def send_to_twin(r, k):
        if r >= 1 or k >= 2:
            pl.semaphore_wait(twin_free.at[k % 2], 1)
        to_twin(r, k).start()

    def multiply(r, k):
        to_twin(r - 2, k).wait_send()
        if k < 3:
            along(r - 2, k, 0, end).wait_send()
        else:
            wait(outputs(r - 2))
        if sources[r] is not None:
            column_copy(r, k).wait()

        @pl.loop(0, unit // 512)
        def _(j):
            tile = block_of(j * 512, 512)
            product = None
            for place in (pl.ds(0, 2 * rows), pl.ds(2 * rows, 2 * rows)):
                if r < 4:
                    right = units[(None, None, 2, 0)[r], place, tile]
                else:
                    right = big[place, block_of((r - 4) * unit + j * 512, 512)]
                if sources[r] is None:
                    left = big[place, block_of(targets[k] * 2 * depth, 2 * depth)]
                else:
                    left = columns[k % 2, place]
                more = dot_tn(left, right)
                product = more if product is None else product + more
            products[r % 2, k, :, tile] = product.astype(bf16)

        if sources[r] is not None and k + 2 < 4:
            column_copy(r, k + 2).start()
        elif r == 4:
            column_copy(5, k - 2).start()
        send_to_twin(r, k)

    def add_to_mine(r, k, others):
        @pl.loop(0, depth // 64)
        def _(i):
            inner = block_of(core * depth + i * 64, 64)
            value = products[r % 2, k, inner].astype(f32)
            for ref, index in others:
                value = value + ref[index, block_of(i * 64, 64)].astype(f32)
            products[r % 2, k, inner] = value.astype(bf16)

    def settle(r, k):
        to_twin(r, k).wait_recv()
        add_to_mine(r, k, [(twin_in, k % 2)])
        if r < last or k < 2:
            pl.semaphore_signal(twin_free.at[k % 2], inc=1, device_id=twin, device_id_type=MESH)

    def push(r, k):
        @pl.when(at_end)
        def _():
            if r >= 1:
                pl.semaphore_wait(line_free.at[k], 1)
            along(r, k, k, near).start()

    def line_wait(slot):
        along(0, 0, slot, end).wait_recv()

    def used(device, index):
        pl.semaphore_signal(line_free.at[index], inc=1, device_id=device, device_id_type=MESH)

    def pass_on(r, which):
        arrived, sender, slot, device = ((0, end, 3, opposite), (1, end, 4, opposite), (3, opposite, 0, end))[which]

        @pl.when(jnp.logical_not(at_end))
        def _():
            line_wait(arrived)
            add_to_mine(r, which, [(line_in, arrived)])
            if r < last:
                used(sender, (0, 1, 0)[which])
            if r >= 1:
                pl.semaphore_wait(line_free.at[which], 1)
            along(r, which, slot, device).start()

    def outputs(r):
        keys = heads * KEY
        slot = products.at[r % 2, 3]
        if r == 4:
            return [
                pltpu.make_async_copy(slot.at[mine, pl.ds(0, keys)], query_out, out_sem.at[0, 0]),
                pltpu.make_async_copy(slot.at[mine, pl.ds(keys, keys)], key_out, out_sem.at[0, 1]),
            ]
        out = (up_out, down_out, out_out, gate_out, None, value_out)[r]
        return [pltpu.make_async_copy(slot.at[mine], out, out_sem.at[r % 2, 0])]

    def finish(r):
        @pl.when(at_end)
        def _():
            line_wait(0)
            add_to_mine(r, 3, [(line_in, 0)])
            if r < last:
                used(near, 2)

        @pl.when(jnp.logical_not(at_end))
        def _():
            line_wait(2)
            line_wait(4)
            add_to_mine(r, 3, [(line_in, 2), (line_in, 4)])
            if r < last:
                used(end, 2)
                used(opposite, 1)

        start(outputs(r))


    def rows_of(r, first=0, count=rows):
        return pl.ds(r * rows + first, count)

    over = [
        remote(low_ref, big.at[rows_of(1)], over_send.at[0], over_recv.at[0], over_x),
        remote(low_ref, big.at[rows_of(2)], over_send.at[1], over_recv.at[1], over_y),
    ]
    onward = [
        remote(big.at[rows_of(2, 0, half)], big.at[rows_of(3, 0, half)], onward_send.at[0], onward_recv.at[0], over_x),
        remote(big.at[rows_of(1, half, half)], big.at[rows_of(3, half, half)], onward_send.at[1], onward_recv.at[1], over_y),
    ]
    halves = [
        remote(terms.at[2, pl.ds(0, half)], half_in.at[0], half_send.at[0], half_recv.at[0], over_x),
        remote(terms.at[2, pl.ds(half, half)], half_in.at[1], half_send.at[1], half_recv.at[1], over_y),
    ]

    def part_copy(index, term, first, device, count=half):
        place = pl.ds(first, count)
        return remote(
            terms.at[term, place], full_in.at[term, place], full_send.at[index], full_recv.at[index], device
        )

    plain_parts = [part_copy(0, 0, 0, over_x), part_copy(1, 1, half, over_y)]
    quarter = half // 2
    grown_parts = [
        part_copy(2, 0, half, over_x, quarter),
        part_copy(3, 1, 0, over_y, quarter),
        part_copy(4, 0, half + quarter, over_x, quarter),
        part_copy(5, 1, quarter, over_y, quarter),
    ]
    fulls = plain_parts + grown_parts
    sides = (over_x, over_y)

    def send_halves(stage):
        for i, copy in enumerate(halves):
            if stage == 1:
                pl.semaphore_wait(half_free.at[i], 1)
            copy.start()

    def take_halves(stage):
        for copy in halves:
            copy.wait_recv()
        for term, first, slot in ((1, 0, 0), (0, half, 1)):
            @pl.loop(0, half // 64)
            def _(i):
                place = block_of(first + i * 64, 64)
                grown = terms[term, place].astype(f32) + half_in[slot, block_of(i * 64, 64)].astype(f32)
                terms[term, place] = grown.astype(bf16)

        for i, copy in enumerate(grown_parts):
            if stage == 0 and i < 2:
                pl.semaphore_signal(half_free.at[i], inc=1, device_id=sides[i], device_id_type=MESH)
            copy.start()

    def send_plain(stage, i):
        if stage == 1:
            pl.semaphore_wait(full_free.at[i], 1)
        plain_parts[i].start()

    def project(r):
        slot = (2, 0, 1, 2)[r]

        @pl.loop(0, width // 512)
        def _(j):
            tile = block_of(j * 512, 512)
            term = dot_nt(big[rows_of(r), pl.ds(0, unit)], units[1, tile])
            term = term + dot_nt(big[rows_of(r), pl.ds(unit, unit)], units[2, tile])
            term = term + dot_nt(units[0, rows_of(r)], units[3, tile])
            terms[slot, :, tile] = term.astype(bf16)


    def gate_copies(r):
        return [
            pltpu.make_async_copy(
                ref.at[rows_of(r), pl.ds(h * VAL, VAL)],
                columns.at[r % 2, pl.ds((2 * i + h) * rows, rows)],
                chunk_sem.at[r % 2, 2 * i + h],
            )
            for i, ref in enumerate((gate_ref, grouped_ref))
            for h in range(heads)
        ] + [pltpu.make_async_copy(scale_ref.at[rows_of(r)], scale_in.at[r % 2], chunk_sem.at[r % 2, 2 * heads])]

    def gate_back(r):
        wait(gate_copies(r))
        for head in range(heads):
            tile = pl.ds(head * VAL, VAL)

            @pl.loop(0, rows // CHUNK)
            def _(i):
                place = block_of(r * rows + i * CHUNK, CHUNK)
                grad = dot_nn(big[place], units[3, :, tile])
                raw = columns[r % 2, block_of(head * rows + i * CHUNK, CHUNK)].astype(f32)
                grouped = columns[r % 2, block_of((heads + head) * rows + i * CHUNK, CHUNK)].astype(f32)
                sigmoid = 1.0 / (1.0 + jnp.exp(-raw))
                units[0, place, tile] = (grad * grouped * (sigmoid * (1.0 + raw * (1.0 - sigmoid)))).astype(bf16)
                c = grad * (raw * sigmoid)
                mean_c = jnp.mean(c, axis=-1, keepdims=True)
                mean_cx = jnp.mean(c * grouped, axis=-1, keepdims=True)
                scale = scale_in[r % 2, block_of(i * CHUNK, CHUNK), head : head + 1]
                units[1, place, tile] = (scale * (c - mean_c - grouped * mean_cx)).astype(bf16)

    chunks = 4 * rows // CHUNK
    per_piece = rows // CHUNK

    def chunk_place(c):
        piece = lax.div(c, per_piece)
        low = lax.rem(lax.rem(piece, 2) + lax.rem(tensor, 2), 2)
        high = lax.rem(lax.div(piece, 2) + lax.div(tensor, 2), 2)
        return (2 * high + low) * per_piece + lax.rem(c, per_piece)

    def chunk_copies(c, slot):
        place = block_of(chunk_place(c) * CHUNK, CHUNK)
        seat = block_of(c * CHUNK, CHUNK)
        keys = heads * KEY
        pieces = [
            (field_ref.at[place, pl.ds(0, keys)], columns.at[slot, pl.ds(0, CHUNK)]),
            (field_ref.at[place, pl.ds(keys, keys)], columns.at[slot, pl.ds(CHUNK, CHUNK)]),
        ]
        for h in range(heads):
            pieces.append((field_ref.at[place, pl.ds(2 * keys + h * VAL, VAL)], columns.at[slot, pl.ds((2 + h) * CHUNK, CHUNK)]))
        pieces += [
            (past_ref.at[c], past_in.at[slot]),
            (angle_ref.at[seat], angle_in.at[slot]),
            (info_ref.at[seat], info_in.at[slot]),
        ]
        return [pltpu.make_async_copy(src, dst, chunk_sem.at[slot, i]) for i, (src, dst) in enumerate(pieces)]

    def retention_steps(between):
        @pl.loop(0, chunks)
        def _(step):
            c = chunks - 1 - step
            slot = lax.rem(step, 2)
            wait(chunk_copies(c, slot))

            @pl.when(step + 1 < chunks)
            def _():
                start(chunk_copies(c - 1, 1 - slot))

            place = block_of(chunk_place(c) * CHUNK, CHUNK)
            angles = angle_in[slot]
            cosine = angles[:, : KEY // 2]
            sine = angles[:, KEY // 2 :]
            info = info_in[slot]
            same = info[:, 0:1] == row_ref[c]

            for head in range(heads):
                at = pl.ds(head * KEY, KEY)
                query = turn(columns[slot, pl.ds(0, CHUNK), at].astype(f32), cosine, sine).astype(bf16)
                key = turn(columns[slot, pl.ds(CHUNK, CHUNK), at].astype(f32), cosine, sine)
                key = (key * key_scale).astype(bf16)
                value = columns[slot, pl.ds((2 + head) * CHUNK, CHUNK)]
                into = info[:, 1 + 2 * head : 2 + 2 * head]
                onto = info[:, 2 + 2 * head : 3 + 2 * head]
                past = past_in[slot, head]
                out_grad = units[1, place, pl.ds(head * VAL, VAL)]
                state = state_ref[head]
                state_low = state.astype(bf16)
                masked = jnp.where(same, decay_ref[head], 0.0)
                weights = (masked * dot_nt(query, key)).astype(bf16)
                score_grad = (masked * dot_nt(out_grad, value)).astype(bf16)
                value_grad = dot_tn(weights, out_grad) + onto * dot_nn(key, state_low)
                query_grad = dot_nn(score_grad, key) + into * dot_nt(out_grad, past)
                key_grad = dot_tn(score_grad, query) + onto * dot_nt(value, state_low)
                moved = (query.astype(f32) * into).astype(bf16)
                state_ref[head] = into[CHUNK - 1 :, :] * state + dot_tn(moved, out_grad)
                big[place, pl.ds(head * KEY, KEY)] = turn_back(query_grad, cosine, sine).astype(bf16)
                big[place, pl.ds((heads + head) * KEY, KEY)] = (turn_back(key_grad, cosine, sine) * key_scale).astype(bf16)
                big[place, pl.ds(2 * heads * KEY + head * VAL, VAL)] = value_grad.astype(bf16)

            between(step)

    blocks = width // columns.shape[2]
    last_loads = [
        pltpu.make_async_copy(
            ref.at[:, pl.ds(q * columns.shape[2], columns.shape[2])], columns.at[i, rows_of(q)], chunk_sem.at[i, q]
        )
        for i, ref in enumerate((token_ref, low_ref))
        for q in range(blocks)
    ]

    def laid_out(slot, i):
        return jnp.concatenate([columns[slot, block_of(q * rows + i * 64, 64)] for q in range(blocks)], axis=1)


    own_load = pltpu.make_async_copy(low_ref, big.at[rows_of(0)], mixed_sem.at[0])
    own_load.start()
    for r in range(2):
        for k in range(4):
            given_copy(r, k).start()
    start(out_load)
    start(gated_load)
    start(gate_copies(0))
    start(gate_copies(1))
    start(feed_load)

    barrier = pltpu.get_barrier_semaphore()

    def partner(k):
        other = lax.rem(here + k, peers)
        return other, (lax.div(other, 4), lax.rem(other, 4))

    @pl.loop(1, peers)
    def _(k):
        pl.semaphore_signal(barrier, inc=1, device_id=partner(k)[1], device_id_type=MESH)

    pl.semaphore_wait(barrier, peers - 1)

    start(over)
    for k in range(4):
        given_copy(0, k).wait()
        send_to_twin(0, k)
        if k > 0:
            settle(0, k - 1)
            push(0, k - 1)
    for k in range(4):
        given_copy(1, k).wait()
        send_to_twin(1, k)
        settle(*((1, k - 1) if k > 0 else (0, 3)))
    wait(out_load)
    own_load.wait()
    settle(1, 3)
    pass_on(0, 0)
    push(1, 0)
    gate_back(0)
    start(gate_copies(2))
    wait_recv(over)
    start(onward)
    pass_on(0, 1)
    gate_back(1)
    start(gate_copies(3))
    push(1, 1)
    gate_back(2)
    pass_on(0, 2)
    pass_on(1, 0)
    push(1, 2)
    finish(0)
    wait_recv(onward)
    wait(feed_load)
    send_halves(0)
    send_plain(0, 0)
    send_plain(0, 1)
    wait(gated_load)
    multiply(2, 0)
    multiply(2, 1)
    pass_on(1, 2)
    settle(2, 0)
    push(2, 0)
    pass_on(1, 1)
    gate_back(3)
    prefetch(3)
    start(w_gate_load)
    settle(2, 1)
    multiply(2, 2)
    multiply(2, 3)
    start(w_value_load)
    settle(2, 2)
    push(2, 1)
    multiply(3, 0)
    finish(1)
    push(2, 2)
    settle(2, 3)
    multiply(3, 1)
    take_halves(0)
    settle(3, 0)
    pass_on(2, 0)
    multiply(3, 2)
    settle(3, 1)
    multiply(3, 3)
    start(chunk_copies(chunks - 1, 0))
    push(3, 0)
    wait_send(over + onward)
    state_ref[...] = jnp.zeros_like(state_ref)

    def between(step):
        @pl.when(step == 1)
        def _():
            pass_on(2, 2)
            pass_on(2, 1)
            settle(3, 2)

        @pl.when(step == 2)
        def _():
            push(3, 1)

    retention_steps(between)
    start(w_key_load)
    prefetch(4)
    settle(3, 3)
    multiply(4, 0)
    push(3, 2)
    pass_on(3, 0)
    finish(2)
    multiply(4, 1)
    wait_send(halves)
    wait(w_gate_load + w_value_load + w_key_load)
    project(3)
    send_halves(1)
    wait_recv(fulls)
    result_copy = pltpu.make_async_copy(full_in, result_ref, mixed_sem.at[1])
    result_copy.start()
    result_copy.wait()
    for i, side in enumerate(sides):
        pl.semaphore_signal(full_free.at[i], inc=1, device_id=side, device_id_type=MESH)
    wait_send(fulls)
    pass_on(3, 1)
    settle(4, 0)
    push(4, 0)
    pass_on(3, 2)
    multiply(4, 2)
    settle(4, 1)
    project(2)
    push(4, 1)
    settle(4, 2)
    project(1)
    pass_on(4, 0)
    send_plain(1, 0)
    send_plain(1, 1)
    multiply(4, 3)
    finish(3)
    push(4, 2)
    pass_on(4, 2)
    pass_on(4, 1)
    take_halves(1)
    settle(4, 3)
    multiply(5, 0)
    multiply(5, 1)
    settle(5, 0)
    push(5, 0)
    multiply(5, 2)
    settle(5, 1)
    settle(5, 2)
    finish(4)
    pass_on(5, 0)
    push(5, 1)
    multiply(5, 3)
    start(last_loads)
    wait_send(halves)
    project(0)
    pass_on(5, 1)
    pass_on(5, 2)
    push(5, 2)
    settle(5, 3)
    total[...] = jnp.zeros_like(total)
    wait(last_loads)

    def first_norm_back(i):
        place = block_of(i * 64, 64)
        normed_grad = terms[2, place].astype(f32) + full_in[0, place].astype(f32) + full_in[1, place].astype(f32)
        plain, scale = normalize(laid_out(0, i).astype(f32))
        grad = laid_out(1, i).astype(f32) + normalize_back(normed_grad, plain, scale, gain_ref[...])
        full_in[0, place] = grad.astype(bf16)
        total[0:1, :] += jnp.sum(normed_grad * plain, axis=0, keepdims=True)
        total[1:2, :] += jnp.sum(normed_grad, axis=0, keepdims=True)

    wait_recv(plain_parts + grown_parts[:2])
    pl.loop(0, quarter // 64)(first_norm_back)
    pl.loop(half // 64, (half + quarter) // 64)(first_norm_back)
    wait_recv(grown_parts[2:])
    pl.loop(quarter // 64, half // 64)(first_norm_back)
    pl.loop((half + quarter) // 64, rows // 64)(first_norm_back)
    grad_copy = pltpu.make_async_copy(full_in.at[0], grad_ref, mixed_sem.at[3])
    grad_copy.start()

    total[2:4, :] = late_ref[...]
    for k in range(peers // 2):
        given[k] = total[:, k * 128 : (k + 1) * 128]

    def sum_copy(k):
        other, device = partner(k)
        return remote(given.at[lax.div(other, 2)], landed.at[k], sum_send.at[k], sum_recv.at[k], device)

    @pl.loop(1, peers)
    def _(k):
        sum_copy(k).start()

    sums_ref[...] = given[lax.div(here, 2)]

    @pl.loop(1, peers)
    def _(k):
        sum_copy(k).wait()
        sums_ref[...] += landed[k]

    finish(5)

    wait_send(fulls)
    for r in (4, 5):
        for k in range(4):
            to_twin(r, k).wait_send()
            if k < 3:
                along(r, k, 0, end).wait_send()
    wait(outputs(4) + outputs(5))
    grad_copy.wait()


def cast_kernel(plus_ref, parts_ref, *refs):
    count = len(refs) // 2
    total = plus_ref[...].astype(f32) + parts_ref[0].astype(f32) + parts_ref[1].astype(f32)
    refs[count][...] = total.astype(bf16)
    for i, (source, target) in enumerate(zip(refs[:count], refs[count + 1 :])):
        value = source[...].astype(target.dtype)
        target[...] = value.T if i >= count - 2 else value


def cast_all(plus, parts, arrays):
    steps = 4

    def slab(rows, width):
        return pl.BlockSpec((rows // steps, width), lambda j: (j, 0))

    rows, width = plus.shape
    in_specs = [slab(rows, width), pl.BlockSpec((2, rows // steps, width), lambda j: (0, j, 0))]
    out_specs, shapes = [slab(rows, width)], [jax.ShapeDtypeStruct(plus.shape, bf16)]
    for i, v in enumerate(arrays):
        rows, width = v.shape
        if i >= len(arrays) - 2:
            in_specs.append(pl.BlockSpec((rows, width // steps), lambda j: (0, j)))
            out_specs.append(pl.BlockSpec((width // steps, rows), lambda j: (j, 0)))
            shapes.append(jax.ShapeDtypeStruct((width, rows), f32))
        else:
            in_specs.append(slab(rows, width))
            out_specs.append(slab(rows, width))
            shapes.append(jax.ShapeDtypeStruct((rows, width), bf16 if i == 0 else f32))
    return pl.pallas_call(
        cast_kernel,
        grid=(steps,),
        in_specs=in_specs,
        out_specs=out_specs,
        out_shape=shapes,
        compiler_params=pltpu.CompilerParams(vmem_limit_bytes=60 * 1024 * 1024),
        name="last_casts",
    )(plus, parts, *arrays)


def closing_exchange(heads, operands, small):
    token_rows, width = operands[-1].shape
    rows = 4 * token_rows
    depth = width // 8
    keys, values = heads * KEY, heads * VAL
    unit = operands[1].shape[1]
    anywhere = pl.BlockSpec(memory_space=pl.ANY)
    in_vmem = pl.BlockSpec(memory_space=pltpu.VMEM)
    sem = pltpu.SemaphoreType.DMA
    regular = pltpu.SemaphoreType.REGULAR
    vmem = pltpu.VMEM
    return pl.pallas_call(
        functools.partial(closing_kernel, heads),
        out_shape=[
            jax.ShapeDtypeStruct((2, token_rows, width), bf16),
            jax.ShapeDtypeStruct((token_rows, width), bf16),
            jax.ShapeDtypeStruct((depth, keys), bf16),
            jax.ShapeDtypeStruct((depth, keys), bf16),
            jax.ShapeDtypeStruct((depth, values), bf16),
            jax.ShapeDtypeStruct((depth, values), bf16),
            jax.ShapeDtypeStruct((depth, unit), bf16),
            jax.ShapeDtypeStruct((depth, unit), bf16),
            jax.ShapeDtypeStruct((depth, unit), bf16),
            jax.ShapeDtypeStruct((8, 128), f32),
        ],
        in_specs=[anywhere] * len(operands) + [in_vmem] * len(small),
        out_specs=[anywhere] * 9 + [in_vmem],
        scratch_shapes=[
            vmem((rows, width), bf16),
            vmem((4, rows, unit), bf16),
            vmem((2, rows, 2 * depth), bf16),
            vmem((3, token_rows, width), bf16),
            vmem((2, token_rows // 2, width), bf16),
            vmem((2, token_rows, width), bf16),
            vmem((2, 4, 2 * depth, unit), bf16),
            vmem((2, depth, unit), bf16),
            vmem((5, depth, unit), bf16),
            vmem((heads, KEY, VAL), f32),
            vmem((2, heads, KEY, VAL), bf16),
            vmem((2, token_rows, 128), f32),
            vmem((2, CHUNK, KEY), f32),
            vmem((2, CHUNK, 128), f32),
            vmem((16, 8, 128), f32),
            vmem((32, 8, 128), f32),
            vmem((8, width), f32),
            sem((10,)), sem((8,)), sem((2, 12)), sem((2, 2)), sem((4,)),
            sem((2,)), sem((2,)), sem((2,)), sem((2,)),
            sem((2,)), sem((2,)), sem((6,)), sem((6,)),
            sem((2, 4)), sem((2,)), sem((2, 3)), sem((5,)), sem((32,)), sem((32,)),
            regular((2,)), regular((3,)), regular((2,)), regular((2,)),
        ],
        compiler_params=pltpu.CompilerParams(
            collective_id=3, has_side_effects=True, vmem_limit_bytes=63_400_000
        ),
        name="closing_exchange",
    )(*operands, *small)


def body(tokens, cotangent, segment, first_gain, first_bias, query_weight, key_weight, value_weight, gate_weight, out_weight, second_gain, second_bias, up_weight, down_weight):
    devices = lax.axis_size("tensor")
    rows = tokens.shape[0]
    heads = query_weight.shape[1] // KEY
    here = lax.axis_index("tensor")
    which = (here if devices == 4 else jnp.zeros_like(here)).astype(jnp.int32).reshape(1)

    def per_piece(values):
        return [values[i * rows : (i + 1) * rows] for i in range(devices)]

    if devices == 4 and lax.axis_size("dp") == 8:
        shards = (query_weight, key_weight, value_weight, gate_weight, out_weight, down_weight)
        opened, keys = opening_exchange(heads, shards, tokens, cotangent, segment, first_gain, first_bias)
        w_qkv, w_gate, w_out, normed1_all, cot_all, field, gate, gated, grouped, group_scale, past = opened[:11]
        angles, info, decay, down_shard = opened[11:]
        mixed_low, plus, feed_terms, up_weight_grad, down_weight_grad, late = middle_exchange(
            gated, w_out, up_weight, down_shard, cot_all, tokens, second_gain, second_bias
        )
        parts, input_grad, query_sum, key_sum, value_sum, gate_sum, out_sum, up_sum, down_sum, sums = closing_exchange(
            heads,
            (
                normed1_all, up_weight_grad, down_weight_grad, feed_terms, w_out, w_qkv, w_gate,
                gate, grouped, gated, group_scale, field, past, angles, info,
                mixed_low, tokens,
            ),
            (keys, decay, first_gain.reshape(1, -1), late),
        )
        part = first_gain.shape[0] // 32
        sums = lax.dynamic_slice_in_dim(sums, (here % 2) * part, part, 1)
        norm_sums = [sums[0], sums[1], sums[2], sums[3]]
        result, input_grad, query_sum, key_sum, value_sum, gate_sum, up_sum, out_sum, down_sum = cast_all(
            plus, parts, (input_grad, query_sum, key_sum, value_sum, gate_sum, up_sum, out_sum, down_sum)
        )
    else:
        w_qkv = lax.all_gather(
            jnp.concatenate([query_weight, key_weight, value_weight], axis=1), "dp", axis=0, tiled=True
        )
        w_gate = lax.all_gather(gate_weight, "dp", axis=0, tiled=True)
        w_out = lax.all_gather(out_weight, "dp", axis=1, tiled=True)
        token_rows = tokens.astype(f32)
        unit1, scale1 = normalize(token_rows)
        normed1_all = jnp.concatenate(
            gather_pieces((unit1 * first_gain + first_bias).astype(bf16), devices), axis=0
        )
        cot_all = jnp.concatenate(gather_pieces(cotangent, devices), axis=0)
        tables = retention_tables(segment, heads, here * heads)
        field = dot_nn(normed1_all, w_qkv).astype(bf16)
        gate = dot_nn(normed1_all, w_gate).astype(bf16)
        gated, grouped, group_scale, past = retention_call(False, which, rows, heads, field, gate, tables, ())
        w_down = lax.all_gather(after(down_weight, w_out), "dp", axis=1, tiled=True)
        w_up = lax.all_gather(after(up_weight, w_down), "dp", axis=0, tiled=True)
        branch, begun, _ = scatter_sum([dot_nn(piece, w_out) for piece in per_piece(gated)])

        mixed = token_rows + branch
        unit2, scale2 = normalize(mixed)
        normed2 = (unit2 * second_gain + second_bias).astype(bf16)
        hidden_grads = per_piece(dot_nt(cot_all, after(w_down, normed2)).astype(bf16))

        def feed(piece, hidden_grad):
            value, slope = gelu_both(dot_nn(piece, w_up))
            return after((value.astype(bf16), (hidden_grad.astype(f32) * slope).astype(bf16)))

        fed_own = feed(normed2, hidden_grads[0])
        normed2_pieces = gather_pieces(normed2, devices, fed_own)
        fed = [fed_own] + [feed(piece, grad) for piece, grad in zip(normed2_pieces[1:-1], hidden_grads[1:-1])]
        fed.append(feed(after(normed2_pieces[-1], *fed), hidden_grads[-1]))
        hidden = [f[0] for f in fed]
        up_grad = [f[1] for f in fed]
        terms = [dot_nt(piece, w_up) for piece in up_grad]
        normed2_grad, _, _ = scatter_sum(terms)
        mixed_grad = cotangent.astype(f32) + normalize_back(normed2_grad, unit2, scale2, second_gain)
        gain2_grad = jnp.sum(normed2_grad * unit2, axis=0)
        bias2_grad = jnp.sum(normed2_grad, axis=0)
        mixed_low = mixed_grad.astype(bf16)
        hidden_all = jnp.concatenate(after(hidden, *terms), axis=0)
        normed2_all = jnp.concatenate(after(normed2_pieces, *terms), axis=0)
        up_grad_all = jnp.concatenate(after(up_grad, *terms), axis=0)
        feed_terms = dot_nn(hidden_all, w_down).astype(bf16)
        own_term = feed_terms[:rows].astype(f32)
        up_weight_grad = dot_tn(normed2_all, up_grad_all).astype(bf16)
        down_weight_grad = dot_tn(cot_all, hidden_all).astype(bf16)

        def summed(gradient, dimension):
            return lax.psum_scatter(
                gradient.astype(bf16), "dp", scatter_dimension=dimension, tiled=True
            ).astype(f32)

        up_sum = summed(up_weight_grad, 0)
        down_sum = summed(down_weight_grad, 0).T
        mixed_all = jnp.concatenate(gather_pieces(mixed_low, devices), axis=0)
        ffn, _, _ = scatter_sum([term.astype(f32) for term in per_piece(feed_terms)])
        result = (mixed + ffn).astype(bf16)
        gated_grad = dot_nt(mixed_all, w_out)
        raw = gate.astype(f32)
        sigmoid = 1.0 / (1.0 + jnp.exp(-raw))
        gate_grad = (gated_grad * grouped.astype(f32) * (sigmoid * (1.0 + raw * (1.0 - sigmoid)))).astype(bf16)
        back = retention_call(
            True, which, rows, heads, field, gate, tables, (gated_grad.astype(bf16), grouped, group_scale, past)
        )
        gate_sum = summed(dot_tn(normed1_all, gate_grad), 0)
        out_sum = summed(dot_tn(gated, mixed_all), 1)
        qkv_sum = summed(dot_tn(normed1_all, back), 0)
        keys_end = heads * KEY
        query_sum = qkv_sum[:, :keys_end]
        key_sum = qkv_sum[:, keys_end : 2 * keys_end]
        value_sum = qkv_sum[:, 2 * keys_end :]
        terms = [
            dot_nt(first, w_qkv) + dot_nt(second, w_gate) for first, second in zip(per_piece(back), per_piece(gate_grad))
        ]
        normed1_grad, _, _ = scatter_sum(terms)
        input_grad = (mixed_grad + normalize_back(normed1_grad, unit1, scale1, first_gain)).astype(bf16)
        gain1_grad = jnp.sum(normed1_grad * unit1, axis=0)
        bias1_grad = jnp.sum(normed1_grad, axis=0)
        norm_sums = spread_sum([gain1_grad, bias1_grad, gain2_grad, bias2_grad])
    return (
        result,
        input_grad,
        norm_sums[0],
        norm_sums[1],
        query_sum,
        key_sum,
        value_sum,
        gate_sum,
        out_sum,
        norm_sums[2],
        norm_sums[3],
        up_sum,
        down_sum,
    )


def solution(mesh):
    rows = P(("dp", "tensor"), None)
    vector = P(("dp", "tensor"))
    into = P("dp", "tensor")
    back = P("tensor", "dp")
    return jax.shard_map(
        body,
        mesh=mesh,
        in_specs=(rows, rows, P("dp"), P(), P(), into, into, into, into, back, P(), P(), into, back),
        out_specs=(rows, rows, vector, vector, into, into, into, into, back, vector, vector, into, back),
        check_vma=False,
    )
```
